32 devices in a mesh: img: 4 (over z), row: 4 (over y, x), col: 2 (over core).
Axes of the slice: x: 2, y: 2, z: 4, core: 2. Of those that a mesh axis runs over, the one named last changes fastest.
Arguments:
- feature_in: bfloat16 [8, 64, 64, 2048], P('img', 'row', 'col'), may hold values from -6 to 6
- orientation: int32 [8], P('img'), may hold values from 0 to 1
- offset_base: int32 [8, 64, 64, 18], P('img', 'row', 'col'), may hold values from -4 to 4
- w_reduce_a: bfloat16 [2048, 512], replicated, may hold values from -0.125 to 0.125
- w_offset_a: bfloat16 [4608, 18], replicated, may hold values from -0.25 to 0.25
- w_deform_a: bfloat16 [4608, 512], replicated, may hold values from -0.09375 to 0.09375
- w_expand_a: bfloat16 [512, 2048], replicated, may hold values from -0.25 to 0.25
- scale_a: float32 [3072], replicated, may hold values from 0.5 to 1.5
- shift_a: float32 [3072], replicated, may hold values from -1.5 to 1.5
- w_reduce_b: bfloat16 [2048, 512], replicated, may hold values from -0.125 to 0.125
- w_conv_b: bfloat16 [4608, 512], replicated, may hold values from -0.09375 to 0.09375
- w_expand_b: bfloat16 [512, 2048], replicated, may hold values from -0.25 to 0.25
- scale_b: float32 [3072], replicated, may hold values from 0.5 to 1.5
- shift_b: float32 [3072], replicated, may hold values from -1.5 to 1.5
- cotangent: bfloat16 [8, 64, 64, 2048], P('img', 'row', 'col'), may hold values from -6 to 6
Outputs:
- feature_out: bfloat16 [8, 64, 64, 2048], P('img', 'row', 'col')
- grad_in: bfloat16 [8, 64, 64, 2048], P('img', 'row', 'col')
- grad_reduce_a: float32 [2048, 512], P('img')
- grad_offset_a: float32 [4608, 18], P('img')
- grad_deform_a: float32 [4608, 512], P('img')
- grad_expand_a: float32 [512, 2048], P('img')
- grad_scale_a: float32 [3072], replicated
- grad_shift_a: float32 [3072], replicated
- batch_mean_a: float32 [3072], replicated
- batch_var_a: float32 [3072], replicated
- grad_reduce_b: float32 [2048, 512], P('img')
- grad_conv_b: float32 [4608, 512], P('img')
- grad_expand_b: float32 [512, 2048], P('img')
- grad_scale_b: float32 [3072], replicated
- grad_shift_b: float32 [3072], replicated
- batch_mean_b: float32 [3072], replicated
- batch_var_b: float32 [3072], replicated
The draws below stay inside these ranges and needn't reach their ends.
Inputs may be any that keep to these rules, and one draw needn't show every extreme that they name: `orientation`: 0 marks an image of 44 rows by 64 columns, 1 one of 64 rows by 44 columns; either fills the top-left of a 64 x 64 canvas and the rest of the canvas is ignored. `offset_base`: channel 2k displaces tap k's rows, channel 2k + 1 its columns.
All inputs are finite; a program needn't handle non-finite values.
Results may differ from the reference program's by a relative error of at most 0.025.
Values may be sent and summed in bfloat16 or wider, within the bound.
A program may use at most 320 MiB of HBM per device.

```python
import jax
import jax.numpy as jnp
from jax import lax

C = 2048
M = 512
LONG = 64
SHORT = 44
BOUND = 4
IMAGES = 8


def touch_ends(array, stream_key, smallest, largest):
    longest = array.shape.index(max(array.shape))
    spots = []
    for shift in (0, 1):
        where = [jax.random.randint(jax.random.fold_in(stream_key, axis), (), 0, length) for axis, length in enumerate(array.shape)]
        where[longest] = (where[longest] + shift) % array.shape[longest]
        spots.append(tuple(where))
    return array.at[spots[0]].set(smallest).at[spots[1]].set(largest)


def steps_of(own_key, dims, split, least, high):
    loudness = 1.0
    for axis_at, shards_of in split:
        steps = jax.random.uniform(jax.random.fold_in(jax.random.fold_in(own_key, 6), axis_at), (shards_of,), jnp.float32, least / len(split), high / len(split))
        loudness = loudness * jnp.repeat(jnp.exp(steps), dims[axis_at] // shards_of).reshape((-1,) + (1,) * (len(dims) - 1 - axis_at))
    return loudness


def normal_values(stream_key, extent, scale, limit, split=(), kind=jnp.bfloat16):
    array = scale * jax.random.normal(stream_key, extent, jnp.float32)
    if split:
        array = array * steps_of(stream_key, extent, split, -0.22, 0.18)
    return jnp.clip(array, -limit, limit).astype(kind)


def setup_inputs(seed: int = 0) -> dict:
    key_list = jax.random.split(jax.random.key(seed), 16)
    return {
        "feature_in": normal_values(key_list[0], (IMAGES, LONG, LONG, C), 1.0, 6.0, ((0, 4), (1, 4), (2, 2))),
        "orientation": touch_ends(jax.random.randint(key_list[1], (IMAGES,), 0, 2), jax.random.fold_in(key_list[1], 1), 0, 1).astype(jnp.int32),
        "offset_base": touch_ends(jax.random.randint(key_list[2], (IMAGES, LONG, LONG, 18), -BOUND, BOUND + 1), jax.random.fold_in(key_list[2], 1), -BOUND, BOUND).astype(jnp.int32),
        "w_reduce_a": normal_values(key_list[3], (C, M), C ** -0.5, 0.125),
        "w_offset_a": normal_values(key_list[4], (9 * M, 18), M ** -0.5, 0.25),
        "w_deform_a": normal_values(key_list[5], (9 * M, M), (9 * M) ** -0.5, 0.09375),
        "w_expand_a": normal_values(key_list[6], (M, C), M ** -0.5, 0.25),
        "scale_a": jnp.clip(1.0 + 0.1 * jax.random.normal(key_list[7], (2 * M + C,), jnp.float32), 0.5, 1.5),
        "shift_a": normal_values(key_list[8], (2 * M + C,), 0.3, 1.5, (), jnp.float32),
        "w_reduce_b": normal_values(key_list[9], (C, M), C ** -0.5, 0.125),
        "w_conv_b": normal_values(key_list[10], (9 * M, M), (9 * M) ** -0.5, 0.09375),
        "w_expand_b": normal_values(key_list[11], (M, C), M ** -0.5, 0.25),
        "scale_b": jnp.clip(1.0 + 0.1 * jax.random.normal(key_list[12], (2 * M + C,), jnp.float32), 0.5, 1.5),
        "shift_b": normal_values(key_list[13], (2 * M + C,), 0.3, 1.5, (), jnp.float32),
        "cotangent": normal_values(key_list[14], (IMAGES, LONG, LONG, C), 1.0, 6.0, ((0, 4), (1, 4), (2, 2))),
    }


EPSILON = 1e-05
HIGHEST = lax.Precision.HIGHEST

@jax.custom_vjp
def low(v):
    return lax.optimization_barrier(v.astype(jnp.bfloat16)).astype(jnp.float32)

@jax.custom_vjp
def low_back(v):
    return v

def low_keep(v):
    return (low(v), None)

def low_pass(kept, grad):
    return (grad,)

def back_keep(v):
    return (v, None)

def back_low(kept, grad):
    return (low(grad),)
low.defvjp(low_keep, low_pass)
low_back.defvjp(back_keep, back_low)

def inside_mask(orientation):
    row_ids = jnp.arange(LONG, dtype=jnp.int32)[:, None]
    col_ids = jnp.arange(LONG, dtype=jnp.int32)[None, :]
    landscape = jnp.broadcast_to(row_ids < SHORT, (LONG, LONG))
    portrait = jnp.broadcast_to(col_ids < SHORT, (LONG, LONG))
    chosen = jnp.where(orientation[:, None, None] == 0, landscape[None], portrait[None])
    return chosen.astype(jnp.float32)

def project(values, weights):
    return jnp.einsum('nhwc,cd->nhwd', values, weights, precision=HIGHEST)

def gelu_exact(values):
    return jax.nn.gelu(values, approximate=False)

def batch_norm(pre_norm, inside, norm_gain, norm_shift, pixel_count):
    weight_map = inside[..., None]
    batch_mean = lax.optimization_barrier(jnp.sum(pre_norm * weight_map, axis=(0, 1, 2))) / pixel_count
    centered = pre_norm - batch_mean
    spread = lax.optimization_barrier(jnp.sum(centered * centered * weight_map, axis=(0, 1, 2))) / pixel_count
    return (centered * lax.rsqrt(spread + EPSILON) * norm_gain + norm_shift, batch_mean, spread)

def make_tap_conv(kernel_tap):

    def tap_conv(hidden, weight_rows):
        padded = jnp.pad(hidden, ((0, 0), (2, 2), (2, 2), (0, 0)))
        step_row = 2 + 2 * (kernel_tap // 3 - 1)
        step_col = 2 + 2 * (kernel_tap % 3 - 1)
        shifted = padded[:, step_row:step_row + LONG, step_col:step_col + LONG, :]
        return project(shifted, weight_rows)
    return jax.checkpoint(tap_conv)

def dilated_conv(hidden, weights):
    width = hidden.shape[-1]
    total = None
    for kernel_tap in range(9):
        term = make_tap_conv(kernel_tap)(hidden, weights[kernel_tap * width:(kernel_tap + 1) * width])
        total = term if total is None else total + term
    return total

def make_tap_sample(kernel_tap, offset_base):

    def tap_sample(hidden, fraction, weight_rows):
        reach_cells = BOUND + 3
        side_cells = LONG + 2 * reach_cells
        images = hidden.shape[0]
        padded = jnp.pad(hidden, ((0, 0), (reach_cells, reach_cells), (reach_cells, reach_cells), (0, 0)))
        padded = padded.reshape(images, side_cells * side_cells, M)
        image_ids = jnp.arange(images, dtype=jnp.int32)[:, None]
        row_ids = jnp.arange(LONG, dtype=jnp.int32).reshape(1, LONG, 1)
        col_ids = jnp.arange(LONG, dtype=jnp.int32).reshape(1, 1, LONG)
        upper = row_ids + 2 * (kernel_tap // 3 - 1) + reach_cells + offset_base[..., 2 * kernel_tap]
        leftmost = col_ids + 2 * (kernel_tap % 3 - 1) + reach_cells + offset_base[..., 2 * kernel_tap + 1]
        frac_row = fraction[..., 2 * kernel_tap]
        frac_col = fraction[..., 2 * kernel_tap + 1]
        summed = jnp.zeros(hidden.shape, hidden.dtype)
        for row_step, row_weight in ((0, 1.0 - frac_row), (1, frac_row)):
            for col_step, col_weight in ((0, 1.0 - frac_col), (1, frac_col)):
                flat_index = ((upper + row_step) * side_cells + leftmost + col_step).reshape(images, LONG * LONG)
                flat_index = flat_index.astype(jnp.int32)
                picked = padded[image_ids, flat_index].reshape(hidden.shape)
                summed = summed + low(row_weight * col_weight)[..., None] * picked
        sample = low(low_back(summed))
        return project(sample, weight_rows)
    return jax.checkpoint(tap_sample)

def deform_conv(hidden, fraction, offset_base, weights):
    total = None
    for kernel_tap in range(9):
        term = make_tap_sample(kernel_tap, offset_base)(hidden, fraction, weights[kernel_tap * M:(kernel_tap + 1) * M])
        total = term if total is None else total + term
    return total

def make_block_a(inside, offset_base, pixel_count):

    def block_a(block_in, w_reduce_a, w_offset_a, w_deform_a, w_expand_a, scale_a, shift_a):
        keep = inside[..., None]
        first_cut = M
        second_cut = 2 * M
        reduced = low_back(project(block_in, low(w_reduce_a)))
        normed_one, mean_one, spread_one = batch_norm(reduced, inside, scale_a[:first_cut], shift_a[:first_cut], pixel_count)
        hidden = low(gelu_exact(normed_one) * keep)
        offsets = low_back(dilated_conv(hidden, low(w_offset_a)))
        fraction = jax.nn.sigmoid(offsets)
        deformed = low_back(deform_conv(hidden, fraction, offset_base, low(w_deform_a)))
        normed_two, mean_two, spread_two = batch_norm(deformed, inside, scale_a[first_cut:second_cut], shift_a[first_cut:second_cut], pixel_count)
        hidden_two = low(gelu_exact(normed_two) * keep)
        expanded = low_back(project(hidden_two, low(w_expand_a)))
        normed_three, mean_three, spread_three = batch_norm(expanded, inside, scale_a[second_cut:], shift_a[second_cut:], pixel_count)
        middle = low(gelu_exact(normed_three + block_in) * keep)
        return (middle, jnp.concatenate([mean_one, mean_two, mean_three]), jnp.concatenate([spread_one, spread_two, spread_three]))
    return jax.checkpoint(block_a)

def make_block_b(inside, pixel_count):

    def block_b(middle, w_reduce_b, w_conv_b, w_expand_b, scale_b, shift_b):
        keep = inside[..., None]
        first_cut = M
        second_cut = 2 * M
        reduced_b = low_back(project(middle, low(w_reduce_b)))
        normed_b1, mean_b1, spread_b1 = batch_norm(reduced_b, inside, scale_b[:first_cut], shift_b[:first_cut], pixel_count)
        hidden_b = low(gelu_exact(normed_b1) * keep)
        conv_out = low_back(dilated_conv(hidden_b, low(w_conv_b)))
        normed_b2, mean_b2, spread_b2 = batch_norm(conv_out, inside, scale_b[first_cut:second_cut], shift_b[first_cut:second_cut], pixel_count)
        hidden_b2 = low(gelu_exact(normed_b2) * keep)
        expanded_b = low_back(project(hidden_b2, low(w_expand_b)))
        normed_b3, mean_b3, spread_b3 = batch_norm(expanded_b, inside, scale_b[second_cut:], shift_b[second_cut:], pixel_count)
        result = gelu_exact(normed_b3 + middle) * keep
        return (result, jnp.concatenate([mean_b1, mean_b2, mean_b3]), jnp.concatenate([spread_b1, spread_b2, spread_b3]))
    return jax.checkpoint(block_b)

def forward(feature, w_reduce_a, w_offset_a, w_deform_a, w_expand_a, scale_a, shift_a, w_reduce_b, w_conv_b, w_expand_b, scale_b, shift_b, inside, offset_base):
    pixel_count = IMAGES * LONG * SHORT * 1.0
    block_in = low(feature * inside[..., None])
    middle, mean_first, spread_first = make_block_a(inside, offset_base, pixel_count)(block_in, w_reduce_a, w_offset_a, w_deform_a, w_expand_a, scale_a, shift_a)
    result, mean_second, spread_second = make_block_b(inside, pixel_count)(middle, w_reduce_b, w_conv_b, w_expand_b, scale_b, shift_b)
    return (result, (mean_first, spread_first, mean_second, spread_second))

def reference(feature_in, orientation, offset_base, w_reduce_a, w_offset_a, w_deform_a, w_expand_a, scale_a, shift_a, w_reduce_b, w_conv_b, w_expand_b, scale_b, shift_b, cotangent):
    inside = inside_mask(orientation)
    primals = tuple((member.astype(jnp.float32) for member in (feature_in, w_reduce_a, w_offset_a, w_deform_a, w_expand_a, scale_a, shift_a, w_reduce_b, w_conv_b, w_expand_b, scale_b, shift_b)))

    def closed(*values):
        return forward(*values, inside, offset_base)
    result, pullback, stats = jax.vjp(closed, *primals, has_aux=True)
    grads = pullback(cotangent.astype(jnp.float32))
    pixel_count = IMAGES * LONG * SHORT * 1.0
    unbias = pixel_count / (pixel_count - 1.0)
    batch_mean_a = stats[0]
    batch_var_a = stats[1] * unbias
    batch_mean_b = stats[2]
    batch_var_b = stats[3] * unbias
    return (result.astype(jnp.bfloat16), grads[0].astype(jnp.bfloat16), grads[1], grads[2], grads[3], grads[4], grads[5], grads[6], batch_mean_a, batch_var_a, grads[7], grads[8], grads[9], grads[10], grads[11], batch_mean_b, batch_var_b)
```

```python
import functools

import jax
import jax.numpy as jnp
import numpy as np
from jax import lax
from jax.experimental import pallas as pl
from jax.experimental.pallas import tpu as pltpu
from jax.sharding import PartitionSpec as P

LONG = 64
SHORT = 44
BOUND = 4
EPSILON = 1e-05
MESH = pl.DeviceIdType.MESH
VMEM = pl.BlockSpec(memory_space=pltpu.VMEM)
VMEM_LIMIT = 60 * 1024 * 1024
F32 = jnp.float32
BF16 = jnp.bfloat16
REACH = BOUND + 3
PAD = 8
HALF = 16
CID = {"stats512": 0, "sums512": 1, "stats2048": 2, "sums2048": 3, "halo_a": 4, "halo_b": 5, "spill": 6}


def gelu_exact(values):
    return jax.nn.gelu(values, approximate=False)


def gelu_back(values, upstream):
    return jax.vjp(gelu_exact, values)[1](upstream)[0]


def group_of(axes):
    sizes = [lax.axis_size(a) for a in axes]
    total = int(np.prod(sizes))
    place = lax.axis_index(axes[0])
    for axis, size in zip(axes[1:], sizes[1:]):
        place = place * size + lax.axis_index(axis)

    def device(step):
        spot = lax.rem(place + step, total)
        coords = {}
        for axis, size in zip(reversed(axes), reversed(sizes)):
            coords[axis] = lax.rem(spot, size)
            spot = spot // size
        return coords

    return place, total, device


PLANE = ("row", "col")
LINE = ("img",)


def entry_barrier(groups):
    barrier = pltpu.get_barrier_semaphore()
    count = 0
    for axes in groups:
        _, total, device = group_of(axes)
        for step in range(1, total):
            pl.semaphore_signal(barrier, inc=1, device_id=device(step), device_id_type=MESH)
        count += total - 1
    pl.semaphore_wait(barrier, count)


def gather_start(axes, slots, send_sem, recv_sem):
    _, total, device = group_of(axes)
    for step in range(1, total):
        pltpu.make_async_remote_copy(
            src_ref=slots.at[0],
            dst_ref=slots.at[step],
            send_sem=send_sem,
            recv_sem=recv_sem,
            device_id=device(step),
            device_id_type=MESH,
        ).start()


def gather_wait(axes, slots, sem):
    _, total, _ = group_of(axes)
    others = slots.at[pl.ds(1, total - 1)]
    pltpu.make_async_copy(others, others, sem).wait()


def in_order(axes, slots):
    place, total, _ = group_of(axes)
    return [slots[lax.rem(place - spot + total, total)] for spot in range(total)]


def sums_kernel(x_ref, o_ref, slots1, slots2, send_sems, recv_sems):
    entry_barrier((PLANE, LINE))
    slots1[0] = x_ref[...]
    gather_start(PLANE, slots1, send_sems.at[0], recv_sems.at[0])
    gather_wait(PLANE, slots1, recv_sems.at[0])
    slots2[0] = functools.reduce(lambda a, b: a + b, in_order(PLANE, slots1))
    gather_start(LINE, slots2, send_sems.at[1], recv_sems.at[1])
    gather_wait(LINE, slots2, recv_sems.at[1])
    o_ref[...] = functools.reduce(lambda a, b: a + b, in_order(LINE, slots2))
    gather_wait(PLANE, slots1, send_sems.at[0])
    gather_wait(LINE, slots2, send_sems.at[1])


def stats_kernel(plane_count, x_ref, count_ref, o_ref, slots1, slots2, send_sems, recv_sems):
    entry_barrier((PLANE, LINE))
    half = x_ref.shape[0] // 2
    total_count = plane_count * lax.axis_size("img")
    slots1[0] = x_ref[...]
    gather_start(PLANE, slots1, send_sems.at[0], recv_sems.at[0])
    gather_wait(PLANE, slots1, recv_sems.at[0])
    parts = in_order(PLANE, slots1)
    total = functools.reduce(lambda a, b: a + b, [p[:half] for p in parts])
    center = total / plane_count
    spread = functools.reduce(lambda a, b: a + b, [p[half:] for p in parts])
    for spot, part in enumerate(parts):
        count = count_ref[spot : spot + 1, :]
        away = part[:half] / jnp.maximum(count, 1.0) - center
        spread = spread + count * (away * away)
    slots2[0, :half] = total
    slots2[0, half:] = spread
    gather_start(LINE, slots2, send_sems.at[1], recv_sems.at[1])
    gather_wait(LINE, slots2, recv_sems.at[1])
    parts = in_order(LINE, slots2)
    center = functools.reduce(lambda a, b: a + b, [p[:half] for p in parts]) / total_count
    spread = functools.reduce(lambda a, b: a + b, [p[half:] for p in parts])
    for part in parts:
        away = part[:half] / plane_count - center
        spread = spread + plane_count * (away * away)
    o_ref[:half] = center
    o_ref[half:] = spread / total_count
    gather_wait(PLANE, slots1, send_sems.at[0])
    gather_wait(LINE, slots2, send_sems.at[1])


def exchange(kernel, name, rows, operands):
    scratch = []
    for axes in (PLANE, LINE):
        total = int(np.prod([lax.axis_size(a) for a in axes]))
        scratch.append(pltpu.VMEM((total, rows, 128), F32))
    scratch += [pltpu.SemaphoreType.DMA((2,)), pltpu.SemaphoreType.DMA((2,))]
    return pl.pallas_call(
        kernel,
        out_shape=jax.ShapeDtypeStruct((rows, 128), F32),
        in_specs=[VMEM] * len(operands),
        out_specs=VMEM,
        scratch_shapes=scratch,
        compiler_params=pltpu.CompilerParams(collective_id=CID[name], has_side_effects=True),
        name=name,
    )(*operands)


def sums_over_devices(first, second):
    width = first.shape[0]
    both = jnp.concatenate([first, second]).reshape(-1, 128)
    out = exchange(sums_kernel, f"sums{width}", both.shape[0], (both,)).reshape(2, width)
    return out[0], out[1]


def stats_over_devices(total, spread, counts, plane_count):
    width = total.shape[0]
    both = jnp.concatenate([total, spread]).reshape(-1, 128)
    kernel = functools.partial(stats_kernel, plane_count)
    out = exchange(kernel, f"stats{width}", both.shape[0], (both, counts)).reshape(2, width)
    return out[0], out[1]


def halo_peers():
    row, rows, col = lax.axis_index("row"), lax.axis_size("row"), lax.axis_index("col")
    return row, rows, col, {"col": 1 - col}, {"row": row - 1}, {"row": row + 1}


def halo_barrier():
    row, rows, _, pair, above, below = halo_peers()
    barrier = pltpu.get_barrier_semaphore()
    pl.semaphore_signal(barrier, inc=1, device_id=pair, device_id_type=MESH)

    @pl.when(row > 0)
    def _():
        pl.semaphore_signal(barrier, inc=1, device_id=above, device_id_type=MESH)

    @pl.when(row < rows - 1)
    def _():
        pl.semaphore_signal(barrier, inc=1, device_id=below, device_id_type=MESH)

    count = 1 + (row > 0).astype(jnp.int32) + (row < rows - 1).astype(jnp.int32)
    pl.semaphore_wait(barrier, count)


def halo_kernel(pad, reach, h_ref, o_ref, send_sems, recv_sems):
    row, rows, col, pair, above, below = halo_peers()
    tile_rows, tile_cols = h_ref.shape[1], h_ref.shape[2]
    off = pl.multiple_of(HALF * col, HALF)
    spot = pl.multiple_of(2 * HALF * col, HALF)
    own = pl.ds(off, tile_cols)
    mid = pl.ds(HALF, HALF)
    upper = pl.ds(pad - reach, reach)
    lower = pl.ds(pad + tile_rows, reach)
    zero_row = jnp.zeros((h_ref.shape[0],) + o_ref.shape[2:], o_ref.dtype)

    def blank(at):
        for k in range(at.start, at.stop):
            o_ref[:, k] = zero_row

    blank(slice(0, pad - reach))
    blank(slice(pad + tile_rows + reach, 2 * pad + tile_rows))

    @pl.when(row == 0)
    def _():
        blank(slice(pad - reach, pad))

    @pl.when(row == rows - 1)
    def _():
        blank(slice(pad + tile_rows, pad + tile_rows + reach))

    halo_barrier()

    def copy(src, dst, k, device):
        return pltpu.make_async_remote_copy(
            src_ref=src,
            dst_ref=dst,
            send_sem=send_sems.at[k],
            recv_sem=recv_sems.at[k],
            device_id=device,
            device_id_type=MESH,
        )

    to_pair = copy(
        h_ref.at[:, :, pl.ds(pl.multiple_of(HALF * (1 - col), HALF), HALF)],
        o_ref.at[:, pl.ds(pad, tile_rows), pl.ds(spot, HALF)],
        0,
        pair,
    )
    up = copy(h_ref.at[:, pl.ds(0, reach)], o_ref.at[:, lower, own], 1, above)
    down = copy(h_ref.at[:, pl.ds(tile_rows - reach, reach)], o_ref.at[:, upper, own], 2, below)
    from_below = copy(o_ref.at[:, lower, mid], o_ref.at[:, lower, pl.ds(spot, HALF)], 3, pair)
    from_above = copy(o_ref.at[:, upper, mid], o_ref.at[:, upper, pl.ds(spot, HALF)], 4, pair)

    @pl.when(row > 0)
    def _():
        up.start()

    @pl.when(row < rows - 1)
    def _():
        down.start()

    to_pair.start()
    for n in range(h_ref.shape[0]):
        o_ref[n, pl.ds(pad, tile_rows), own, :] = h_ref[n]

    @pl.when(row < rows - 1)
    def _():
        up.wait_recv()
        from_below.start()

    @pl.when(row > 0)
    def _():
        down.wait_recv()
        from_above.start()

    to_pair.wait()

    @pl.when(row < rows - 1)
    def _():
        down.wait_send()
        from_below.wait()

    @pl.when(row > 0)
    def _():
        up.wait_send()
        from_above.wait()


def with_halo(tile, pad, reach, name):
    images, rows, cols, width = tile.shape
    return pl.pallas_call(
        functools.partial(halo_kernel, pad, reach),
        out_shape=jax.ShapeDtypeStruct((images, rows + 2 * pad, cols + HALF, width), tile.dtype),
        in_specs=[VMEM],
        out_specs=VMEM,
        scratch_shapes=[pltpu.SemaphoreType.DMA((5,)), pltpu.SemaphoreType.DMA((5,))],
        compiler_params=pltpu.CompilerParams(
            collective_id=CID[name], has_side_effects=True, vmem_limit_bytes=VMEM_LIMIT
        ),
        name=name,
    )(tile)


def spill_kernel(s_ref, o_ref, side_out, side_in, up_out, down_out, up_in, down_in, send_sems, recv_sems):
    row, rows, col, pair, above, below = halo_peers()
    images, tile_rows, tile_cols, width = o_ref.shape
    off = pl.multiple_of(HALF * col, HALF)
    own = pl.ds(off, tile_cols)
    away = pl.ds(pl.multiple_of(2 * HALF * (1 - col), HALF), HALF)
    near = pl.ds(pl.multiple_of(HALF * (1 - col), HALF), HALF)
    all_rows = s_ref.shape[1]

    def cast_side(k, carry):
        for n in range(images):
            side_out[n, k] = s_ref[n, k, away, :].astype(BF16)
        return carry

    lax.fori_loop(0, all_rows, cast_side, 0)
    halo_barrier()

    def copy(src, dst, k, device):
        return pltpu.make_async_remote_copy(
            src_ref=src,
            dst_ref=dst,
            send_sem=send_sems.at[k],
            recv_sem=recv_sems.at[k],
            device_id=device,
            device_id_type=MESH,
        )

    side = copy(side_out, side_in, 0, pair)
    up = copy(up_out, down_in, 1, above)
    down = copy(down_out, up_in, 2, below)
    side.start()
    side.wait_recv()

    def edge(buffer, first):
        for k in range(REACH):
            for n in range(images):
                wide = s_ref[n, first + k, own, :]
                buffer[n, k] = wide.astype(BF16)
                part = s_ref[n, first + k, pl.ds(HALF, HALF), :]
                buffer[n, k, near, :] = (part + side_in[n, first + k].astype(F32)).astype(BF16)

    @pl.when(row > 0)
    def _():
        edge(up_out, PAD - REACH)
        up.start()

    @pl.when(row < rows - 1)
    def _():
        edge(down_out, PAD + tile_rows)
        down.start()

    def fill(k, carry):
        for n in range(images):
            o_ref[n, k] = s_ref[n, PAD + k, own, :]
            part = s_ref[n, PAD + k, pl.ds(HALF, HALF), :]
            o_ref[n, k, near, :] = part + side_in[n, PAD + k].astype(F32)
        return carry

    lax.fori_loop(0, tile_rows, fill, 0)

    @pl.when(row > 0)
    def _():
        down.wait_recv()
        for k in range(REACH):
            for n in range(images):
                o_ref[n, k] = o_ref[n, k] + up_in[n, k].astype(F32)
        up.wait_send()

    @pl.when(row < rows - 1)
    def _():
        up.wait_recv()
        for k in range(REACH):
            for n in range(images):
                at = tile_rows - REACH + k
                o_ref[n, at] = o_ref[n, at] + down_in[n, k].astype(F32)
        down.wait_send()

    side.wait_send()


def spill_home(spill):
    images, rows, cols, width = spill.shape
    strip = pltpu.VMEM((images, REACH, cols - HALF, width), BF16)
    side = pltpu.VMEM((images, rows, HALF, width), BF16)
    return pl.pallas_call(
        spill_kernel,
        out_shape=jax.ShapeDtypeStruct((images, rows - 2 * PAD, cols - HALF, width), F32),
        in_specs=[VMEM],
        out_specs=VMEM,
        scratch_shapes=[
            side,
            side,
            strip,
            strip,
            strip,
            strip,
            pltpu.SemaphoreType.DMA((3,)),
            pltpu.SemaphoreType.DMA((3,)),
        ],
        compiler_params=pltpu.CompilerParams(
            collective_id=CID["spill"], has_side_effects=True, vmem_limit_bytes=VMEM_LIMIT
        ),
        name="spill",
    )(spill)


BLOCK_ROWS = 8
SPAN = 17
WINDOW = 3 * BLOCK_ROWS


def tap_span(group, cols):
    first = 2 + 2 * group
    start = first * cols // 128 * 128
    stop = -(-(first + SPAN) * cols // 128) * 128
    return first, start, stop


def tap_weights(tap, block, cols, up_ref, left_ref, fr_ref, fc_ref):
    pixels = up_ref.shape[-1]
    up = up_ref[0, tap : tap + 1, :] - block * BLOCK_ROWS
    left = left_ref[0, tap : tap + 1, :]
    fr = fr_ref[0, tap : tap + 1, :]
    fc = fc_ref[0, tap : tap + 1, :]

    def pair(size, at, frac):
        ids = lax.broadcasted_iota(jnp.int32, (size, pixels), 0)
        first, second = ids == at, ids == at + 1
        value = jnp.where(first, 1.0 - frac, jnp.where(second, frac, 0.0))
        slope = jnp.where(second, 1.0, jnp.where(first, -1.0, 0.0))
        return value, slope

    return pair(WINDOW, up, fr) + pair(cols, left, fc)


def write_table(table, lane, row_w, col_w, group, cols):
    first, start, stop = tap_span(group, cols)
    pixels = row_w.shape[1]
    low = start // cols
    high = -(-stop // cols)
    for r in range(low, min(high, WINDOW)):
        table[r * cols : (r + 1) * cols, lane : lane + pixels] = (
            row_w[r : r + 1, :] * col_w
        ).astype(BF16)


def sample_kernel(rim_ref, w_ref, up_ref, left_ref, fr_ref, fc_ref, s_ref, d_ref, table):
    block = pl.program_id(1)
    width = rim_ref.shape[1]
    cols = table.shape[0] // WINDOW
    base = block * (BLOCK_ROWS * cols)
    for tap in range(9):
        row_w, _, col_w, _ = tap_weights(tap, block, cols, up_ref, left_ref, fr_ref, fc_ref)
        write_table(table, 0, row_w, col_w, tap // 3, cols)
        _, start, stop = tap_span(tap // 3, cols)
        cells = pl.ds(pl.multiple_of(base + start, 128), stop - start)
        value = jnp.dot(rim_ref[0, :, cells], table[start:stop, :], preferred_element_type=F32)
        s_ref[tap * width : (tap + 1) * width, :] = value.astype(BF16)
    d_ref[...] = jnp.dot(w_ref[...], s_ref[...], preferred_element_type=F32)


def sample_forward(rim_t, w_t, up, left, fr, fc, cols):
    images, width, cells = rim_t.shape
    pixels = up.shape[-1]
    blocks = 2
    step = pixels // blocks
    tap_spec = pl.BlockSpec((1, 9, step), lambda i, b: (i, 0, b))
    return pl.pallas_call(
        sample_kernel,
        grid=(images, blocks),
        out_shape=(
            jax.ShapeDtypeStruct((9 * width, images * pixels), BF16),
            jax.ShapeDtypeStruct((width, images * pixels), F32),
        ),
        in_specs=[
            pl.BlockSpec((1, width, cells), lambda i, b: (i, 0, 0)),
            pl.BlockSpec((width, 9 * width), lambda i, b: (0, 0)),
            tap_spec,
            tap_spec,
            tap_spec,
            tap_spec,
        ],
        out_specs=(
            pl.BlockSpec((9 * width, step), lambda i, b: (0, i * blocks + b)),
            pl.BlockSpec((width, step), lambda i, b: (0, i * blocks + b)),
        ),
        scratch_shapes=[pltpu.VMEM((WINDOW * cols, step), BF16)],
        compiler_params=pltpu.CompilerParams(vmem_limit_bytes=VMEM_LIMIT),
        name="sample",
    )(rim_t, w_t, up, left, fr, fc)


def unsample_kernel(
    rim_ref, g_ref, w_ref, up_ref, left_ref, fr_ref, fc_ref, spill_ref, gr_ref, gc_ref, table, grads
):
    block = pl.program_id(1)
    width = rim_ref.shape[2]
    cols = table.shape[0] // WINDOW
    pixels = up_ref.shape[-1]
    base = block * (BLOCK_ROWS * cols)

    @pl.when(block == 0)
    def _():
        spill_ref[...] = jnp.zeros_like(spill_ref)

    for group in range(3):
        first, start, stop = tap_span(group, cols)
        cells = pl.ds(pl.multiple_of(base + start, 128), stop - start)
        for j in range(3):
            tap = 3 * group + j
            lanes = slice(j * pixels, (j + 1) * pixels)
            row_w, row_s, col_w, col_s = tap_weights(
                tap, block, cols, up_ref, left_ref, fr_ref, fc_ref
            )
            write_table(table, j * pixels, row_w, col_w, group, cols)
            grad = jnp.dot(
                w_ref[tap * width : (tap + 1) * width, :], g_ref[...], preferred_element_type=F32
            ).astype(BF16)
            grads[:, lanes] = grad
            scores = jnp.dot(rim_ref[0, cells, :], grad, preferred_element_type=F32)
            by_value = jnp.zeros((cols, pixels), F32)
            by_slope = jnp.zeros((cols, pixels), F32)
            for r in range(first, first + SPAN):
                line = scores[r * cols - start : (r + 1) * cols - start]
                by_value = by_value + line * row_w[r : r + 1, :]
                by_slope = by_slope + line * row_s[r : r + 1, :]
            gr_ref[0, tap : tap + 1, :] = jnp.sum(by_slope * col_w, axis=0, keepdims=True)
            gc_ref[0, tap : tap + 1, :] = jnp.sum(by_value * col_s, axis=0, keepdims=True)
        spill_ref[0, cells, :] += lax.dot_general(
            table[start:stop, :], grads[...], (((1,), (1,)), ((), ())), preferred_element_type=F32
        )


def sample_backward(rim, grad_t, w, up, left, fr, fc, cols):
    images, cells, width = rim.shape
    pixels = up.shape[-1]
    blocks = 2
    step = pixels // blocks
    tap_spec = pl.BlockSpec((1, 9, step), lambda i, b: (i, 0, b))
    map_spec = pl.BlockSpec((1, cells, width), lambda i, b: (i, 0, 0))
    return pl.pallas_call(
        unsample_kernel,
        grid=(images, blocks),
        out_shape=(
            jax.ShapeDtypeStruct(rim.shape, F32),
            jax.ShapeDtypeStruct(up.shape, F32),
            jax.ShapeDtypeStruct(up.shape, F32),
        ),
        in_specs=[
            map_spec,
            pl.BlockSpec((width, step), lambda i, b: (0, i * blocks + b)),
            pl.BlockSpec((9 * width, width), lambda i, b: (0, 0)),
            tap_spec,
            tap_spec,
            tap_spec,
            tap_spec,
        ],
        out_specs=(map_spec, tap_spec, tap_spec),
        scratch_shapes=[
            pltpu.VMEM((WINDOW * cols, 3 * step), BF16),
            pltpu.VMEM((width, 3 * step), BF16),
        ],
        compiler_params=pltpu.CompilerParams(vmem_limit_bytes=VMEM_LIMIT),
        name="unsample",
    )(rim, grad_t, w, up, left, fr, fc)


def build_shifted(rim_ref, shifted):
    images, rows, cols, width = rim_ref.shape
    col = lax.axis_index("col")
    tile = cols - HALF

    def fill(first):
        def one_row(k, carry):
            for n in range(images):
                line = rim_ref[n, k].astype(F32)
                none = jnp.zeros((2, width), F32)
                for d in range(3):
                    at = first + 2 * (d - 1)
                    if at < 0:
                        part = jnp.concatenate([none, line[: tile - 2]], axis=0)
                    elif at + tile > cols:
                        part = jnp.concatenate([line[at:], none], axis=0)
                    else:
                        part = line[at : at + tile]
                    shifted[n, k, :, d * width : (d + 1) * width] = part.astype(BF16)
            return carry

        lax.fori_loop(0, rows, one_row, 0)

    @pl.when(col == 0)
    def _():
        fill(0)

    @pl.when(col == 1)
    def _():
        fill(HALF)


def conv_kernel(rim_ref, w_ref, o_ref, shifted):
    images, rows, cols, width = rim_ref.shape
    build_shifted(rim_ref, shifted)
    tile_rows = rows - 4
    pixels = tile_rows * (cols - HALF)
    for n in range(images):
        total = None
        for i in range(3):
            taps = shifted[n, 2 * i : 2 * i + tile_rows].reshape(pixels, 3 * width)
            term = jnp.dot(
                taps, w_ref[3 * i * width : 3 * (i + 1) * width, :], preferred_element_type=F32
            )
            total = term if total is None else total + term
        o_ref[n * pixels : (n + 1) * pixels, :] = total


def conv_forward(rim, w):
    images, rows, cols, width = rim.shape
    pixels = images * (rows - 4) * (cols - HALF)
    return pl.pallas_call(
        conv_kernel,
        out_shape=jax.ShapeDtypeStruct((pixels, width), F32),
        in_specs=[VMEM, VMEM],
        out_specs=VMEM,
        scratch_shapes=[pltpu.VMEM((images, rows, cols - HALF, 3 * width), BF16)],
        compiler_params=pltpu.CompilerParams(vmem_limit_bytes=VMEM_LIMIT),
        name="conv",
    )(rim, w)


def unconv_kernel(rim_ref, back_ref, w_ref, g_ref, o_ref, gw_ref, shifted):
    images, rows, cols, width = rim_ref.shape
    tile_rows = rows - 4
    pixels = tile_rows * (cols - HALF)
    build_shifted(rim_ref, shifted)
    for i in range(3):
        total = None
        for n in range(images):
            taps = shifted[n, 2 * i : 2 * i + tile_rows].reshape(pixels, 3 * width)
            term = lax.dot_general(
                g_ref[n * pixels : (n + 1) * pixels, :],
                taps,
                (((0,), (0,)), ((), ())),
                preferred_element_type=F32,
            )
            total = term if total is None else total + term
        gw_ref[:, 3 * i * width : 3 * (i + 1) * width] = total.astype(BF16)
    build_shifted(back_ref, shifted)
    for n in range(images):
        total = None
        for tap in range(9):
            i, d = 2 - tap // 3, 2 - tap % 3
            grads = shifted[n, 2 * i : 2 * i + tile_rows, :, d * width : (d + 1) * width]
            term = lax.dot_general(
                grads.reshape(pixels, width),
                w_ref[tap * width : (tap + 1) * width, :],
                (((1,), (1,)), ((), ())),
                preferred_element_type=F32,
            )
            total = term if total is None else total + term
        o_ref[n * pixels : (n + 1) * pixels, :] = total


def conv_backward(rim, back_rim, w, grad):
    images, rows, cols, width = rim.shape
    return pl.pallas_call(
        unconv_kernel,
        out_shape=(
            jax.ShapeDtypeStruct(grad.shape, F32),
            jax.ShapeDtypeStruct((width, 9 * width), BF16),
        ),
        in_specs=[VMEM] * 4,
        out_specs=(VMEM, VMEM),
        scratch_shapes=[pltpu.VMEM((images, rows, cols - HALF, 3 * width), BF16)],
        compiler_params=pltpu.CompilerParams(vmem_limit_bytes=VMEM_LIMIT),
        name="unconv",
    )(rim, back_rim, w, grad)


def local_stats(values, weight_col, count):
    total = jnp.sum(values * weight_col, axis=0)
    away = values - total / jnp.maximum(count, 1.0)
    return total, jnp.sum(away * away * weight_col, axis=0)


def norm_forward(pre_norm, weight_col, norm_gain, norm_shift, counts):
    own_count, all_counts, plane_count = counts
    total, spread = local_stats(pre_norm, weight_col, own_count)
    batch_mean, spread = stats_over_devices(total, spread, all_counts, plane_count)
    inv_std = lax.rsqrt(spread + EPSILON)
    unit_value = (pre_norm - batch_mean) * inv_std
    return (unit_value * norm_gain + norm_shift, unit_value, inv_std, batch_mean, spread)


def norm_backward(grad_normed, unit_value, inv_std, norm_gain, weight_col, pixel_count):
    sum_grad, sum_unit = sums_over_devices(
        jnp.sum(grad_normed, axis=0), jnp.sum(grad_normed * unit_value, axis=0)
    )
    grad_pre = (
        norm_gain
        * inv_std
        * (grad_normed - (sum_grad + unit_value * sum_unit) / pixel_count)
        * weight_col
    )
    return (grad_pre.astype(BF16), sum_unit, sum_grad)


def inside_counts(orientation, tile_rows, tile_cols):
    rows, cols = lax.axis_size("row"), lax.axis_size("col")
    tall = np.clip(SHORT - np.arange(rows) * tile_rows, 0, tile_rows)[:, None] * tile_cols
    wide = np.clip(SHORT - np.arange(cols) * tile_cols, 0, tile_cols)[None, :] * tile_rows
    tall = jnp.asarray(np.broadcast_to(tall, (rows, cols)).reshape(-1), F32)
    wide = jnp.asarray(np.broadcast_to(wide, (rows, cols)).reshape(-1), F32)
    flat = (orientation == 0).astype(F32)[:, None]
    each = jnp.sum(flat * tall + (1.0 - flat) * wide, axis=0)
    place = lax.axis_index("row") * cols + lax.axis_index("col")
    own = lax.dynamic_index_in_dim(each, place, keepdims=False)
    return own, jnp.broadcast_to(each[:, None], (rows * cols, 128))


def body(
    feature_in,
    orientation,
    offset_base,
    w_reduce_a,
    w_offset_a,
    w_deform_a,
    w_expand_a,
    scale_a,
    shift_a,
    w_reduce_b,
    w_conv_b,
    w_expand_b,
    scale_b,
    shift_b,
    cotangent,
):
    images, tile_rows, tile_cols, channels = feature_in.shape
    inner_width = w_reduce_a.shape[1]
    second_cut = 2 * inner_width
    tile_pixels = tile_rows * tile_cols
    win_cols = tile_cols + HALF
    win_rows = tile_rows + 2 * PAD
    plane_count = 1.0 * images * LONG * SHORT
    pixel_count = plane_count * lax.axis_size("img")
    unbias = pixel_count / (pixel_count - 1.0)
    col_at = lax.axis_index("col")
    row_ids = lax.axis_index("row") * tile_rows + jnp.arange(tile_rows, dtype=jnp.int32)
    col_ids = col_at * tile_cols + jnp.arange(tile_cols, dtype=jnp.int32)
    landscape = jnp.broadcast_to((row_ids < SHORT)[:, None], (tile_rows, tile_cols))
    portrait = jnp.broadcast_to((col_ids < SHORT)[None, :], (tile_rows, tile_cols))
    inside = jnp.where(orientation[:, None, None] == 0, landscape[None], portrait[None]).astype(F32)
    weight_col = inside.reshape(-1, 1)
    pixels = weight_col.shape[0]
    own_count, all_counts = inside_counts(orientation, tile_rows, tile_cols)
    counts = (own_count, all_counts, plane_count)
    block_in = (
        (feature_in.astype(F32) * inside[..., None]).astype(BF16).reshape(pixels, channels)
    )
    reduced_a = jnp.dot(block_in, w_reduce_a, preferred_element_type=F32)
    normed_a1, unit_a1, inv_a1, mean_a1, spread_a1 = norm_forward(
        reduced_a, weight_col, scale_a[:inner_width], shift_a[:inner_width], counts
    )
    hidden_a = (gelu_exact(normed_a1) * weight_col).astype(BF16)
    rim_a = with_halo(
        hidden_a.reshape(images, tile_rows, tile_cols, inner_width), PAD, REACH, "halo_a"
    )
    rim_flat = rim_a.reshape(images, -1, inner_width)
    own_at = HALF * col_at
    w_off = w_offset_a.reshape(9, inner_width, 18).transpose(1, 0, 2).reshape(inner_width, 162)
    spread_taps = jnp.dot(
        rim_flat.reshape(-1, inner_width), w_off, preferred_element_type=F32
    ).reshape(images, win_rows, win_cols, 162)
    spread_taps = jnp.pad(spread_taps, ((0, 0), (0, 0), (2, 2), (0, 0)))
    spread_taps = lax.dynamic_slice_in_dim(spread_taps, own_at, tile_cols + 4, axis=2)
    offsets = 0.0
    for tap in range(9):
        i, j = 2 * (tap // 3), 2 * (tap % 3)
        offsets = offsets + spread_taps[
            :, PAD - 2 + i : PAD - 2 + i + tile_rows, j : j + tile_cols, 18 * tap : 18 * tap + 18
        ]
    fraction = jax.nn.sigmoid(offsets).reshape(images, tile_pixels, 18).transpose(0, 2, 1)
    frac_row, frac_col = fraction[:, 0::2], fraction[:, 1::2]
    base = offset_base.reshape(images, tile_pixels, 18).transpose(0, 2, 1)
    cell = np.arange(tile_pixels)
    tap_row = np.array([2 * (tap // 3 - 1) for tap in range(9)])[:, None]
    tap_col = np.array([2 * (tap % 3 - 1) for tap in range(9)])[:, None]
    upper = base[:, 0::2] + jnp.asarray(cell // tile_cols + PAD + tap_row, jnp.int32)
    left = base[:, 1::2] + jnp.asarray(cell % tile_cols + tap_col, jnp.int32) + own_at
    samples, deformed = sample_forward(
        rim_flat.transpose(0, 2, 1), w_deform_a.T, upper, left, frac_row, frac_col, win_cols
    )
    deformed = deformed.T
    normed_a2, unit_a2, inv_a2, mean_a2, spread_a2 = norm_forward(
        deformed,
        weight_col,
        scale_a[inner_width:second_cut],
        shift_a[inner_width:second_cut],
        counts,
    )
    hidden2_a = (gelu_exact(normed_a2) * weight_col).astype(BF16)
    expanded_a = jnp.dot(hidden2_a, w_expand_a, preferred_element_type=F32)
    normed_a3, unit_a3, inv_a3, mean_a3, spread_a3 = norm_forward(
        expanded_a, weight_col, scale_a[second_cut:], shift_a[second_cut:], counts
    )
    pre_a = normed_a3 + block_in.astype(F32)
    middle = (gelu_exact(pre_a) * weight_col).astype(BF16)
    reduced_b = jnp.dot(middle, w_reduce_b, preferred_element_type=F32)
    normed_b1, unit_b1, inv_b1, mean_b1, spread_b1 = norm_forward(
        reduced_b, weight_col, scale_b[:inner_width], shift_b[:inner_width], counts
    )
    hidden_b = (gelu_exact(normed_b1) * weight_col).astype(BF16)
    tile_shape = (images, tile_rows, tile_cols, inner_width)
    rim_b = with_halo(hidden_b.reshape(tile_shape), 2, 2, "halo_b")
    conv_out = conv_forward(rim_b, w_conv_b)
    normed_b2, unit_b2, inv_b2, mean_b2, spread_b2 = norm_forward(
        conv_out,
        weight_col,
        scale_b[inner_width:second_cut],
        shift_b[inner_width:second_cut],
        counts,
    )
    hidden2_b = (gelu_exact(normed_b2) * weight_col).astype(BF16)
    expanded_b = jnp.dot(hidden2_b, w_expand_b, preferred_element_type=F32)
    normed_b3, unit_b3, inv_b3, mean_b3, spread_b3 = norm_forward(
        expanded_b, weight_col, scale_b[second_cut:], shift_b[second_cut:], counts
    )
    pre_b = normed_b3 + middle.astype(F32)
    feature_out = (gelu_exact(pre_b) * weight_col).astype(BF16).reshape(feature_in.shape)
    upstream = cotangent.astype(F32).reshape(pixels, channels) * weight_col
    grad_pre_b = gelu_back(pre_b, upstream)
    grad_expand_out, gain_b3, bias_b3 = norm_backward(
        grad_pre_b, unit_b3, inv_b3, scale_b[second_cut:], weight_col, pixel_count
    )
    gw_expand_b = jnp.einsum("pm,pc->mc", hidden2_b, grad_expand_out, preferred_element_type=F32)
    grad_hidden2_b = jnp.einsum(
        "pc,mc->pm", grad_expand_out, w_expand_b, preferred_element_type=F32
    )
    grad_normed_b2 = gelu_back(normed_b2, grad_hidden2_b * weight_col)
    grad_conv_out, gain_b2, bias_b2 = norm_backward(
        grad_normed_b2, unit_b2, inv_b2, scale_b[inner_width:second_cut], weight_col, pixel_count
    )
    back_rim = with_halo(grad_conv_out.reshape(tile_shape), 2, 2, "halo_b")
    grad_hidden_b, gw_conv_b = conv_backward(rim_b, back_rim, w_conv_b, grad_conv_out)
    grad_normed_b1 = gelu_back(normed_b1, grad_hidden_b * weight_col)
    grad_reduce_out, gain_b1, bias_b1 = norm_backward(
        grad_normed_b1, unit_b1, inv_b1, scale_b[:inner_width], weight_col, pixel_count
    )
    gw_reduce_b = jnp.einsum("pc,pm->cm", middle, grad_reduce_out, preferred_element_type=F32)
    grad_middle = grad_pre_b + jnp.einsum(
        "pm,cm->pc", grad_reduce_out, w_reduce_b, preferred_element_type=F32
    )
    grad_pre_a = gelu_back(pre_a, grad_middle * weight_col)
    grad_expand_a, gain_a3, bias_a3 = norm_backward(
        grad_pre_a, unit_a3, inv_a3, scale_a[second_cut:], weight_col, pixel_count
    )
    gw_expand_a = jnp.einsum("pm,pc->mc", hidden2_a, grad_expand_a, preferred_element_type=F32)
    grad_hidden2_a = jnp.einsum("pc,mc->pm", grad_expand_a, w_expand_a, preferred_element_type=F32)
    grad_normed_a2 = gelu_back(normed_a2, grad_hidden2_a * weight_col)
    grad_deformed, gain_a2, bias_a2 = norm_backward(
        grad_normed_a2, unit_a2, inv_a2, scale_a[inner_width:second_cut], weight_col, pixel_count
    )
    gw_deform_a = jnp.dot(samples, grad_deformed, preferred_element_type=F32)
    spill, grad_row, grad_col = sample_backward(
        rim_flat, grad_deformed.T, w_deform_a, upper, left, frac_row, frac_col, win_cols
    )
    grad_fraction = jnp.stack([grad_row, grad_col], axis=2).reshape(images, 18, tile_pixels)
    grad_offsets = (grad_fraction * fraction * (1.0 - fraction)).astype(BF16)
    grad_offsets = grad_offsets.transpose(0, 2, 1).reshape(images, tile_rows, tile_cols, 18)
    placed = jnp.zeros((images, tile_rows, win_cols + 4, 18), BF16)
    placed = lax.dynamic_update_slice(placed, grad_offsets, (0, 0, own_at + 2, 0))
    on_cells = []
    for tap in range(9):
        i, j = 2 * (tap // 3 - 1), 2 * (tap % 3 - 1)
        moved = placed[:, :, 2 - j : 2 - j + win_cols]
        on_cells.append(jnp.pad(moved, ((0, 0), (PAD + i, PAD - i), (0, 0), (0, 0))))
    on_cells = jnp.concatenate(on_cells, axis=-1).reshape(-1, 162)
    gw_offset_a = jnp.einsum(
        "qm,qo->mo", rim_flat.reshape(-1, inner_width), on_cells, preferred_element_type=F32
    )
    gw_offset_a = gw_offset_a.reshape(inner_width, 9, 18).transpose(1, 0, 2).reshape(-1, 18)
    spill = spill.reshape(-1, inner_width) + jnp.einsum(
        "qo,mo->qm", on_cells, w_off, preferred_element_type=F32
    )
    grad_hidden_a = spill_home(spill.reshape(rim_a.shape)).reshape(pixels, inner_width)
    grad_normed_a1 = gelu_back(normed_a1, grad_hidden_a * weight_col)
    grad_reduce_a, gain_a1, bias_a1 = norm_backward(
        grad_normed_a1, unit_a1, inv_a1, scale_a[:inner_width], weight_col, pixel_count
    )
    gw_reduce_a = jnp.einsum("pc,pm->cm", block_in, grad_reduce_a, preferred_element_type=F32)
    grad_block_in = grad_pre_a + jnp.einsum(
        "pm,cm->pc", grad_reduce_a, w_reduce_a, preferred_element_type=F32
    )
    grad_in = (grad_block_in * weight_col).astype(BF16).reshape(feature_in.shape)

    def over_devices(grad, dim):
        part = lax.psum_scatter(grad.astype(BF16), "img", scatter_dimension=dim, tiled=True)
        return lax.psum(part, ("row", "col"))

    gw_expand_b = over_devices(gw_expand_b, 0).astype(F32)
    gw_conv_b = over_devices(gw_conv_b, 1).T.astype(F32)
    gw_reduce_b = over_devices(gw_reduce_b, 0).astype(F32)
    gw_expand_a = over_devices(gw_expand_a, 0).astype(F32)
    gw_deform_a = over_devices(gw_deform_a, 0).astype(F32)
    gw_offset_a = over_devices(gw_offset_a, 0).astype(F32)
    gw_reduce_a = over_devices(gw_reduce_a, 0).astype(F32)
    return (
        feature_out,
        grad_in,
        gw_reduce_a,
        gw_offset_a,
        gw_deform_a,
        gw_expand_a,
        jnp.concatenate([gain_a1, gain_a2, gain_a3]),
        jnp.concatenate([bias_a1, bias_a2, bias_a3]),
        jnp.concatenate([mean_a1, mean_a2, mean_a3]),
        jnp.concatenate([spread_a1, spread_a2, spread_a3]) * unbias,
        gw_reduce_b,
        gw_conv_b,
        gw_expand_b,
        jnp.concatenate([gain_b1, gain_b2, gain_b3]),
        jnp.concatenate([bias_b1, bias_b2, bias_b3]),
        jnp.concatenate([mean_b1, mean_b2, mean_b3]),
        jnp.concatenate([spread_b1, spread_b2, spread_b3]) * unbias,
    )


def solution(mesh):
    tiles = P("img", "row", "col", None)
    in_specs = (tiles, P("img"), tiles) + (P(),) * 11 + (tiles,)
    shares = P("img", None)
    out_specs = (tiles, tiles) + (shares,) * 4 + (P(),) * 4 + (shares,) * 3 + (P(),) * 4
    return jax.shard_map(body, mesh=mesh, in_specs=in_specs, out_specs=out_specs, check_vma=False)
```

```python
import functools

import jax
import jax.numpy as jnp
import numpy as np
from jax import lax
from jax.experimental import pallas as pl
from jax.experimental.pallas import tpu as pltpu
from jax.sharding import PartitionSpec as P

LONG = 64
SHORT = 44
BOUND = 4
EPSILON = 1e-05
MESH = pl.DeviceIdType.MESH
VMEM = pl.BlockSpec(memory_space=pltpu.VMEM)
VMEM_LIMIT = 60 * 1024 * 1024
F32 = jnp.float32
BF16 = jnp.bfloat16
REACH = BOUND + 3
PAD = 8
HALF = 16
CID = {"stats512": 0, "sums512": 1, "stats2048": 2, "sums2048": 3, "halo_a": 4, "halo_b": 5, "spill": 6, "reduce": 7}


def gelu_exact(values):
    return jax.nn.gelu(values, approximate=False)


def gelu_back(values, upstream):
    return jax.vjp(gelu_exact, values)[1](upstream)[0]


def group_of(axes):
    sizes = [lax.axis_size(a) for a in axes]
    total = int(np.prod(sizes))
    place = lax.axis_index(axes[0])
    for axis, size in zip(axes[1:], sizes[1:]):
        place = place * size + lax.axis_index(axis)

    def device(step):
        spot = lax.rem(place + step, total)
        coords = {}
        for axis, size in zip(reversed(axes), reversed(sizes)):
            coords[axis] = lax.rem(spot, size)
            spot = spot // size
        return coords

    return place, total, device


PLANE = ("row", "col")
LINE = ("img",)


def entry_barrier(groups):
    barrier = pltpu.get_barrier_semaphore()
    count = 0
    for axes in groups:
        _, total, device = group_of(axes)
        for step in range(1, total):
            pl.semaphore_signal(barrier, inc=1, device_id=device(step), device_id_type=MESH)
        count += total - 1
    pl.semaphore_wait(barrier, count)


def gather_start(axes, slots, send_sem, recv_sem):
    _, total, device = group_of(axes)
    for step in range(1, total):
        pltpu.make_async_remote_copy(
            src_ref=slots.at[0],
            dst_ref=slots.at[step],
            send_sem=send_sem,
            recv_sem=recv_sem,
            device_id=device(step),
            device_id_type=MESH,
        ).start()


def gather_wait(axes, slots, sem):
    _, total, _ = group_of(axes)
    others = slots.at[pl.ds(1, total - 1)]
    pltpu.make_async_copy(others, others, sem).wait()


def in_order(axes, slots):
    place, total, _ = group_of(axes)
    return [slots[lax.rem(place - spot + total, total)] for spot in range(total)]


def sums_kernel(x_ref, o_ref, slots1, slots2, send_sems, recv_sems):
    entry_barrier((PLANE, LINE))
    slots1[0] = x_ref[...]
    gather_start(PLANE, slots1, send_sems.at[0], recv_sems.at[0])
    gather_wait(PLANE, slots1, recv_sems.at[0])
    slots2[0] = functools.reduce(lambda a, b: a + b, in_order(PLANE, slots1))
    gather_start(LINE, slots2, send_sems.at[1], recv_sems.at[1])
    gather_wait(LINE, slots2, recv_sems.at[1])
    o_ref[...] = functools.reduce(lambda a, b: a + b, in_order(LINE, slots2))
    gather_wait(PLANE, slots1, send_sems.at[0])
    gather_wait(LINE, slots2, send_sems.at[1])


def stats_kernel(plane_count, x_ref, count_ref, o_ref, slots1, slots2, send_sems, recv_sems):
    entry_barrier((PLANE, LINE))
    half = x_ref.shape[0] // 2
    total_count = plane_count * lax.axis_size("img")
    slots1[0] = x_ref[...]
    gather_start(PLANE, slots1, send_sems.at[0], recv_sems.at[0])
    gather_wait(PLANE, slots1, recv_sems.at[0])
    parts = in_order(PLANE, slots1)
    total = functools.reduce(lambda a, b: a + b, [p[:half] for p in parts])
    center = total / plane_count
    spread = functools.reduce(lambda a, b: a + b, [p[half:] for p in parts])
    for spot, part in enumerate(parts):
        count = count_ref[spot : spot + 1, :]
        away = part[:half] / jnp.maximum(count, 1.0) - center
        spread = spread + count * (away * away)
    slots2[0, :half] = total
    slots2[0, half:] = spread
    gather_start(LINE, slots2, send_sems.at[1], recv_sems.at[1])
    gather_wait(LINE, slots2, recv_sems.at[1])
    parts = in_order(LINE, slots2)
    center = functools.reduce(lambda a, b: a + b, [p[:half] for p in parts]) / total_count
    spread = functools.reduce(lambda a, b: a + b, [p[half:] for p in parts])
    for part in parts:
        away = part[:half] / plane_count - center
        spread = spread + plane_count * (away * away)
    o_ref[:half] = center
    o_ref[half:] = spread / total_count
    gather_wait(PLANE, slots1, send_sems.at[0])
    gather_wait(LINE, slots2, send_sems.at[1])


def exchange(kernel, name, rows, operands):
    scratch = []
    for axes in (PLANE, LINE):
        total = int(np.prod([lax.axis_size(a) for a in axes]))
        scratch.append(pltpu.VMEM((total, rows, 128), F32))
    scratch += [pltpu.SemaphoreType.DMA((2,)), pltpu.SemaphoreType.DMA((2,))]
    return pl.pallas_call(
        kernel,
        out_shape=jax.ShapeDtypeStruct((rows, 128), F32),
        in_specs=[VMEM] * len(operands),
        out_specs=VMEM,
        scratch_shapes=scratch,
        compiler_params=pltpu.CompilerParams(collective_id=CID[name], has_side_effects=True),
        name=name,
    )(*operands)


def sums_over_devices(first, second):
    width = first.shape[0]
    both = jnp.concatenate([first, second]).reshape(-1, 128)
    out = exchange(sums_kernel, f"sums{width}", both.shape[0], (both,)).reshape(2, width)
    return out[0], out[1]


def stats_over_devices(total, spread, counts, plane_count):
    width = total.shape[0]
    both = jnp.concatenate([total, spread]).reshape(-1, 128)
    kernel = functools.partial(stats_kernel, plane_count)
    out = exchange(kernel, f"stats{width}", both.shape[0], (both, counts)).reshape(2, width)
    return out[0], out[1]


def halo_peers():
    row, rows, col = lax.axis_index("row"), lax.axis_size("row"), lax.axis_index("col")
    return row, rows, col, {"col": 1 - col}, {"row": row - 1}, {"row": row + 1}


def halo_barrier():
    row, rows, _, pair, above, below = halo_peers()
    barrier = pltpu.get_barrier_semaphore()
    pl.semaphore_signal(barrier, inc=1, device_id=pair, device_id_type=MESH)

    @pl.when(row > 0)
    def _():
        pl.semaphore_signal(barrier, inc=1, device_id=above, device_id_type=MESH)

    @pl.when(row < rows - 1)
    def _():
        pl.semaphore_signal(barrier, inc=1, device_id=below, device_id_type=MESH)

    count = 1 + (row > 0).astype(jnp.int32) + (row < rows - 1).astype(jnp.int32)
    pl.semaphore_wait(barrier, count)


def halo_kernel(pad, reach, h_ref, o_ref, send_sems, recv_sems):
    row, rows, col, pair, above, below = halo_peers()
    tile_rows, tile_cols = h_ref.shape[1], h_ref.shape[2]
    off = pl.multiple_of(HALF * col, HALF)
    spot = pl.multiple_of(2 * HALF * col, HALF)
    own = pl.ds(off, tile_cols)
    mid = pl.ds(HALF, HALF)
    upper = pl.ds(pad - reach, reach)
    lower = pl.ds(pad + tile_rows, reach)
    zero_row = jnp.zeros((h_ref.shape[0],) + o_ref.shape[2:], o_ref.dtype)

    def blank(at):
        for k in range(at.start, at.stop):
            o_ref[:, k] = zero_row

    blank(slice(0, pad - reach))
    blank(slice(pad + tile_rows + reach, 2 * pad + tile_rows))

    @pl.when(row == 0)
    def _():
        blank(slice(pad - reach, pad))

    @pl.when(row == rows - 1)
    def _():
        blank(slice(pad + tile_rows, pad + tile_rows + reach))

    halo_barrier()

    def copy(src, dst, k, device):
        return pltpu.make_async_remote_copy(
            src_ref=src,
            dst_ref=dst,
            send_sem=send_sems.at[k],
            recv_sem=recv_sems.at[k],
            device_id=device,
            device_id_type=MESH,
        )

    to_pair = copy(
        h_ref.at[:, :, pl.ds(pl.multiple_of(HALF * (1 - col), HALF), HALF)],
        o_ref.at[:, pl.ds(pad, tile_rows), pl.ds(spot, HALF)],
        0,
        pair,
    )
    up = copy(h_ref.at[:, pl.ds(0, reach)], o_ref.at[:, lower, own], 1, above)
    down = copy(h_ref.at[:, pl.ds(tile_rows - reach, reach)], o_ref.at[:, upper, own], 2, below)
    from_below = copy(o_ref.at[:, lower, mid], o_ref.at[:, lower, pl.ds(spot, HALF)], 3, pair)
    from_above = copy(o_ref.at[:, upper, mid], o_ref.at[:, upper, pl.ds(spot, HALF)], 4, pair)

    @pl.when(row > 0)
    def _():
        up.start()

    @pl.when(row < rows - 1)
    def _():
        down.start()

    to_pair.start()
    for n in range(h_ref.shape[0]):
        o_ref[n, pl.ds(pad, tile_rows), own, :] = h_ref[n]

    @pl.when(row < rows - 1)
    def _():
        up.wait_recv()
        from_below.start()

    @pl.when(row > 0)
    def _():
        down.wait_recv()
        from_above.start()

    to_pair.wait()

    @pl.when(row < rows - 1)
    def _():
        down.wait_send()
        from_below.wait()

    @pl.when(row > 0)
    def _():
        up.wait_send()
        from_above.wait()


def with_halo(tile, pad, reach, name):
    images, rows, cols, width = tile.shape
    return pl.pallas_call(
        functools.partial(halo_kernel, pad, reach),
        out_shape=jax.ShapeDtypeStruct((images, rows + 2 * pad, cols + HALF, width), tile.dtype),
        in_specs=[VMEM],
        out_specs=VMEM,
        scratch_shapes=[pltpu.SemaphoreType.DMA((5,)), pltpu.SemaphoreType.DMA((5,))],
        compiler_params=pltpu.CompilerParams(
            collective_id=CID[name], has_side_effects=True, vmem_limit_bytes=VMEM_LIMIT
        ),
        name=name,
    )(tile)


def spill_kernel(s_ref, o_ref, side_out, side_in, up_out, down_out, up_in, down_in, send_sems, recv_sems):
    row, rows, col, pair, above, below = halo_peers()
    images, tile_rows, tile_cols, width = o_ref.shape
    off = pl.multiple_of(HALF * col, HALF)
    own = pl.ds(off, tile_cols)
    away = pl.ds(pl.multiple_of(2 * HALF * (1 - col), HALF), HALF)
    near = pl.ds(pl.multiple_of(HALF * (1 - col), HALF), HALF)
    all_rows = s_ref.shape[1]

    def cast_side(k, carry):
        for n in range(images):
            side_out[n, k] = s_ref[n, k, away, :].astype(BF16)
        return carry

    lax.fori_loop(0, all_rows, cast_side, 0)
    halo_barrier()

    def copy(src, dst, k, device):
        return pltpu.make_async_remote_copy(
            src_ref=src,
            dst_ref=dst,
            send_sem=send_sems.at[k],
            recv_sem=recv_sems.at[k],
            device_id=device,
            device_id_type=MESH,
        )

    side = copy(side_out, side_in, 0, pair)
    up = copy(up_out, down_in, 1, above)
    down = copy(down_out, up_in, 2, below)
    side.start()
    side.wait_recv()

    def edge(buffer, first):
        for k in range(REACH):
            for n in range(images):
                wide = s_ref[n, first + k, own, :]
                buffer[n, k] = wide.astype(BF16)
                part = s_ref[n, first + k, pl.ds(HALF, HALF), :]
                buffer[n, k, near, :] = (part + side_in[n, first + k].astype(F32)).astype(BF16)

    @pl.when(row > 0)
    def _():
        edge(up_out, PAD - REACH)
        up.start()

    @pl.when(row < rows - 1)
    def _():
        edge(down_out, PAD + tile_rows)
        down.start()

    def fill(k, carry):
        for n in range(images):
            o_ref[n, k] = s_ref[n, PAD + k, own, :]
            part = s_ref[n, PAD + k, pl.ds(HALF, HALF), :]
            o_ref[n, k, near, :] = part + side_in[n, PAD + k].astype(F32)
        return carry

    lax.fori_loop(0, tile_rows, fill, 0)

    @pl.when(row > 0)
    def _():
        down.wait_recv()
        for k in range(REACH):
            for n in range(images):
                o_ref[n, k] = o_ref[n, k] + up_in[n, k].astype(F32)
        up.wait_send()

    @pl.when(row < rows - 1)
    def _():
        up.wait_recv()
        for k in range(REACH):
            for n in range(images):
                at = tile_rows - REACH + k
                o_ref[n, at] = o_ref[n, at] + down_in[n, k].astype(F32)
        down.wait_send()

    side.wait_send()


def spill_home(spill):
    images, rows, cols, width = spill.shape
    strip = pltpu.VMEM((images, REACH, cols - HALF, width), BF16)
    side = pltpu.VMEM((images, rows, HALF, width), BF16)
    return pl.pallas_call(
        spill_kernel,
        out_shape=jax.ShapeDtypeStruct((images, rows - 2 * PAD, cols - HALF, width), F32),
        in_specs=[VMEM],
        out_specs=VMEM,
        scratch_shapes=[
            side,
            side,
            strip,
            strip,
            strip,
            strip,
            pltpu.SemaphoreType.DMA((3,)),
            pltpu.SemaphoreType.DMA((3,)),
        ],
        compiler_params=pltpu.CompilerParams(
            collective_id=CID["spill"], has_side_effects=True, vmem_limit_bytes=VMEM_LIMIT
        ),
        name="spill",
    )(spill)


BLOCK_ROWS = 8
SPAN = 17
WINDOW = 3 * BLOCK_ROWS


def tap_span(group, cols):
    first = 2 + 2 * group
    start = first * cols // 128 * 128
    stop = -(-(first + SPAN) * cols // 128) * 128
    return first, start, stop


def tap_weights(tap, block, cols, up_ref, left_ref, fr_ref, fc_ref):
    pixels = up_ref.shape[-1]
    up = up_ref[0, tap : tap + 1, :] - block * BLOCK_ROWS
    left = left_ref[0, tap : tap + 1, :]
    fr = fr_ref[0, tap : tap + 1, :]
    fc = fc_ref[0, tap : tap + 1, :]

    def pair(size, at, frac):
        ids = lax.broadcasted_iota(jnp.int32, (size, pixels), 0)
        first, second = ids == at, ids == at + 1
        value = jnp.where(first, 1.0 - frac, jnp.where(second, frac, 0.0))
        slope = jnp.where(second, 1.0, jnp.where(first, -1.0, 0.0))
        return value, slope

    return pair(WINDOW, up, fr) + pair(cols, left, fc)


def write_table(table, lane, row_w, col_w, group, cols):
    first, start, stop = tap_span(group, cols)
    pixels = row_w.shape[1]
    low = start // cols
    high = -(-stop // cols)
    for r in range(low, min(high, WINDOW)):
        table[r * cols : (r + 1) * cols, lane : lane + pixels] = (
            row_w[r : r + 1, :] * col_w
        ).astype(BF16)


def sample_kernel(rim_ref, w_ref, up_ref, left_ref, fr_ref, fc_ref, s_ref, d_ref, table):
    block = pl.program_id(1)
    width = rim_ref.shape[1]
    cols = table.shape[0] // WINDOW
    base = block * (BLOCK_ROWS * cols)
    for tap in range(9):
        row_w, _, col_w, _ = tap_weights(tap, block, cols, up_ref, left_ref, fr_ref, fc_ref)
        write_table(table, 0, row_w, col_w, tap // 3, cols)
        _, start, stop = tap_span(tap // 3, cols)
        cells = pl.ds(pl.multiple_of(base + start, 128), stop - start)
        value = jnp.dot(rim_ref[0, :, cells], table[start:stop, :], preferred_element_type=F32)
        s_ref[tap * width : (tap + 1) * width, :] = value.astype(BF16)
    d_ref[...] = jnp.dot(w_ref[...], s_ref[...], preferred_element_type=F32)


def sample_forward(rim_t, w_t, up, left, fr, fc, cols):
    images, width, cells = rim_t.shape
    pixels = up.shape[-1]
    blocks = 2
    step = pixels // blocks
    tap_spec = pl.BlockSpec((1, 9, step), lambda i, b: (i, 0, b))
    return pl.pallas_call(
        sample_kernel,
        grid=(images, blocks),
        out_shape=(
            jax.ShapeDtypeStruct((9 * width, images * pixels), BF16),
            jax.ShapeDtypeStruct((width, images * pixels), F32),
        ),
        in_specs=[
            pl.BlockSpec((1, width, cells), lambda i, b: (i, 0, 0)),
            pl.BlockSpec((width, 9 * width), lambda i, b: (0, 0)),
            tap_spec,
            tap_spec,
            tap_spec,
            tap_spec,
        ],
        out_specs=(
            pl.BlockSpec((9 * width, step), lambda i, b: (0, i * blocks + b)),
            pl.BlockSpec((width, step), lambda i, b: (0, i * blocks + b)),
        ),
        scratch_shapes=[pltpu.VMEM((WINDOW * cols, step), BF16)],
        compiler_params=pltpu.CompilerParams(vmem_limit_bytes=VMEM_LIMIT),
        name="sample",
    )(rim_t, w_t, up, left, fr, fc)


def unsample_kernel(
    rim_ref, g_ref, w_ref, up_ref, left_ref, fr_ref, fc_ref, spill_ref, gr_ref, gc_ref, table, grads
):
    block = pl.program_id(1)
    width = rim_ref.shape[2]
    cols = table.shape[0] // WINDOW
    pixels = up_ref.shape[-1]
    base = block * (BLOCK_ROWS * cols)

    @pl.when(block == 0)
    def _():
        spill_ref[...] = jnp.zeros_like(spill_ref)

    for group in range(3):
        first, start, stop = tap_span(group, cols)
        cells = pl.ds(pl.multiple_of(base + start, 128), stop - start)
        for j in range(3):
            tap = 3 * group + j
            lanes = slice(j * pixels, (j + 1) * pixels)
            row_w, row_s, col_w, col_s = tap_weights(
                tap, block, cols, up_ref, left_ref, fr_ref, fc_ref
            )
            write_table(table, j * pixels, row_w, col_w, group, cols)
            grad = jnp.dot(
                w_ref[tap * width : (tap + 1) * width, :], g_ref[...], preferred_element_type=F32
            ).astype(BF16)
            grads[:, lanes] = grad
            scores = jnp.dot(rim_ref[0, cells, :], grad, preferred_element_type=F32)
            by_value = jnp.zeros((cols, pixels), F32)
            by_slope = jnp.zeros((cols, pixels), F32)
            for r in range(first, first + SPAN):
                line = scores[r * cols - start : (r + 1) * cols - start]
                by_value = by_value + line * row_w[r : r + 1, :]
                by_slope = by_slope + line * row_s[r : r + 1, :]
            gr_ref[0, tap : tap + 1, :] = jnp.sum(by_slope * col_w, axis=0, keepdims=True)
            gc_ref[0, tap : tap + 1, :] = jnp.sum(by_value * col_s, axis=0, keepdims=True)
        spill_ref[0, cells, :] += lax.dot_general(
            table[start:stop, :], grads[...], (((1,), (1,)), ((), ())), preferred_element_type=F32
        )


def sample_backward(rim, grad_t, w, up, left, fr, fc, cols):
    images, cells, width = rim.shape
    pixels = up.shape[-1]
    blocks = 2
    step = pixels // blocks
    tap_spec = pl.BlockSpec((1, 9, step), lambda i, b: (i, 0, b))
    map_spec = pl.BlockSpec((1, cells, width), lambda i, b: (i, 0, 0))
    return pl.pallas_call(
        unsample_kernel,
        grid=(images, blocks),
        out_shape=(
            jax.ShapeDtypeStruct(rim.shape, F32),
            jax.ShapeDtypeStruct(up.shape, F32),
            jax.ShapeDtypeStruct(up.shape, F32),
        ),
        in_specs=[
            map_spec,
            pl.BlockSpec((width, step), lambda i, b: (0, i * blocks + b)),
            pl.BlockSpec((9 * width, width), lambda i, b: (0, 0)),
            tap_spec,
            tap_spec,
            tap_spec,
            tap_spec,
        ],
        out_specs=(map_spec, tap_spec, tap_spec),
        scratch_shapes=[
            pltpu.VMEM((WINDOW * cols, 3 * step), BF16),
            pltpu.VMEM((width, 3 * step), BF16),
        ],
        compiler_params=pltpu.CompilerParams(vmem_limit_bytes=VMEM_LIMIT),
        name="unsample",
    )(rim, grad_t, w, up, left, fr, fc)


def build_shifted(rim_ref, shifted):
    images, rows, cols, width = rim_ref.shape
    col = lax.axis_index("col")
    tile = cols - HALF

    def fill(first):
        def one_row(k, carry):
            for n in range(images):
                line = rim_ref[n, k].astype(F32)
                none = jnp.zeros((2, width), F32)
                for d in range(3):
                    at = first + 2 * (d - 1)
                    if at < 0:
                        part = jnp.concatenate([none, line[: tile - 2]], axis=0)
                    elif at + tile > cols:
                        part = jnp.concatenate([line[at:], none], axis=0)
                    else:
                        part = line[at : at + tile]
                    shifted[n, k, :, d * width : (d + 1) * width] = part.astype(BF16)
            return carry

        lax.fori_loop(0, rows, one_row, 0)

    @pl.when(col == 0)
    def _():
        fill(0)

    @pl.when(col == 1)
    def _():
        fill(HALF)


def conv_kernel(rim_ref, w_ref, o_ref, shifted):
    images, rows, cols, width = rim_ref.shape
    build_shifted(rim_ref, shifted)
    tile_rows = rows - 4
    pixels = tile_rows * (cols - HALF)
    for n in range(images):
        total = None
        for i in range(3):
            taps = shifted[n, 2 * i : 2 * i + tile_rows].reshape(pixels, 3 * width)
            term = jnp.dot(
                taps, w_ref[3 * i * width : 3 * (i + 1) * width, :], preferred_element_type=F32
            )
            total = term if total is None else total + term
        o_ref[n * pixels : (n + 1) * pixels, :] = total


def conv_forward(rim, w):
    images, rows, cols, width = rim.shape
    pixels = images * (rows - 4) * (cols - HALF)
    return pl.pallas_call(
        conv_kernel,
        out_shape=jax.ShapeDtypeStruct((pixels, width), F32),
        in_specs=[VMEM, VMEM],
        out_specs=VMEM,
        scratch_shapes=[pltpu.VMEM((images, rows, cols - HALF, 3 * width), BF16)],
        compiler_params=pltpu.CompilerParams(vmem_limit_bytes=VMEM_LIMIT),
        name="conv",
    )(rim, w)


def unconv_kernel(rim_ref, back_ref, w_ref, g_ref, o_ref, gw_ref, shifted):
    images, rows, cols, width = rim_ref.shape
    tile_rows = rows - 4
    pixels = tile_rows * (cols - HALF)
    build_shifted(rim_ref, shifted)
    for i in range(3):
        total = None
        for n in range(images):
            taps = shifted[n, 2 * i : 2 * i + tile_rows].reshape(pixels, 3 * width)
            term = lax.dot_general(
                g_ref[n * pixels : (n + 1) * pixels, :],
                taps,
                (((0,), (0,)), ((), ())),
                preferred_element_type=F32,
            )
            total = term if total is None else total + term
        gw_ref[:, 3 * i * width : 3 * (i + 1) * width] = total.astype(BF16)
    build_shifted(back_ref, shifted)
    for n in range(images):
        total = None
        for tap in range(9):
            i, d = 2 - tap // 3, 2 - tap % 3
            grads = shifted[n, 2 * i : 2 * i + tile_rows, :, d * width : (d + 1) * width]
            term = lax.dot_general(
                grads.reshape(pixels, width),
                w_ref[tap * width : (tap + 1) * width, :],
                (((1,), (1,)), ((), ())),
                preferred_element_type=F32,
            )
            total = term if total is None else total + term
        o_ref[n * pixels : (n + 1) * pixels, :] = total


def conv_backward(rim, back_rim, w, grad):
    images, rows, cols, width = rim.shape
    return pl.pallas_call(
        unconv_kernel,
        out_shape=(
            jax.ShapeDtypeStruct(grad.shape, F32),
            jax.ShapeDtypeStruct((width, 9 * width), BF16),
        ),
        in_specs=[VMEM] * 4,
        out_specs=(VMEM, VMEM),
        scratch_shapes=[pltpu.VMEM((images, rows, cols - HALF, 3 * width), BF16)],
        compiler_params=pltpu.CompilerParams(vmem_limit_bytes=VMEM_LIMIT),
        name="unconv",
    )(rim, back_rim, w, grad)


class Reduction:
    count = 7

    def __init__(self, index, src, out, bufs, send_sems, recv_sems):
        self.src, self.out, self.bufs = src, out, bufs
        self.send, self.recv = send_sems.at[index], recv_sems.at[index]
        self.order = (0, 1) if index % 2 == 0 else (1, 0)
        self.img, self.row, self.col = (lax.axis_index(a) for a in ("img", "row", "col"))
        self.images = src.shape[0]
        self.bits = (lax.rem(self.row, 2), self.row // 2)

    @staticmethod
    def scratch(shape):
        images, _, rows, width = shape
        return [
            pltpu.VMEM((images, 4, rows, width), BF16),
            pltpu.VMEM((images, 2, rows, width), BF16),
            pltpu.VMEM((images, rows, width), BF16),
            pltpu.VMEM((images, rows, width), BF16),
        ]

    def copy(self, src, dst, k, device):
        return pltpu.make_async_remote_copy(
            src_ref=src,
            dst_ref=dst,
            send_sem=self.send.at[k],
            recv_sem=self.recv.at[k],
            device_id=device,
            device_id_type=MESH,
        )

    def neighbour(self, bit):
        here = self.bits[bit]
        return {"row": self.row + (1 - 2 * here) * (1 + bit)}

    def wait(self, ref, k):
        pltpu.make_async_copy(ref, ref, self.recv.at[k]).wait()

    def wait_sent(self, ref, k):
        pltpu.make_async_copy(ref, ref, self.send.at[k]).wait()

    def step(self, k):
        images, (half, quarter, eighth, line) = self.images, self.bufs
        mine = 4 * self.col
        first, second = self.order
        a, b = self.bits[first], self.bits[second]
        if k == 0:
            other = pl.ds(4 * (1 - self.col), 4)
            self.copy(self.src.at[:, other], half, 0, {"col": 1 - self.col}).start()
        elif k == 1:
            self.wait(half, 0)

            def add(i, carry):
                for s in range(4):
                    own = self.src[i, mine + s].astype(F32)
                    half[i, s] = (own + half[i, s].astype(F32)).astype(BF16)
                return carry

            lax.fori_loop(0, images, add, 0)
            for i in range(2):
                spot = self.piece(1 - a, i)
                self.copy(half.at[:, spot], quarter.at[:, i], 1, self.neighbour(first)).start()
        elif k == 2:
            self.wait(quarter, 1)

            def add(i, carry):
                for s in range(2):
                    own = half[i, self.piece(a, s)].astype(F32)
                    quarter[i, s] = (own + quarter[i, s].astype(F32)).astype(BF16)
                return carry

            lax.fori_loop(0, images, add, 0)
            self.copy(quarter.at[:, 1 - b], eighth, 2, self.neighbour(second)).start()
        elif k == 3:
            self.wait(eighth, 2)

            def add(i, carry):
                own = quarter[i, b].astype(F32)
                eighth[i] = (own + eighth[i].astype(F32)).astype(BF16)
                return carry

            lax.fori_loop(0, images, add, 0)
            for j in range(1, images):
                there = lax.rem(self.img + j, images)
                self.copy(eighth.at[there], line.at[j], 3, {"img": there}).start()
        elif k == 4:
            arrived = line.at[pl.ds(1, images - 1)]
            self.wait(arrived, 3)
            total = eighth[self.img].astype(F32)
            for j in range(1, images):
                total = total + line[j].astype(F32)
            self.out[mine + self.row] = total.astype(BF16)
            for j in range(1, 4):
                there = lax.rem(self.row + j, 4)
                spot = self.out.at[mine + self.row]
                self.copy(spot, spot, 4, {"row": there}).start()
        elif k == 5:
            three = self.out.at[pl.ds(0, 3)]
            self.wait(three, 4)
            four = self.out.at[pl.ds(mine, 4)]
            self.copy(four, four, 5, {"col": 1 - self.col}).start()
        elif k == 6:
            four = self.out.at[pl.ds(0, 4)]
            self.wait(four, 5)
            self.wait_sent(half, 0)
            self.wait_sent(quarter, 1)
            self.wait_sent(eighth, 2)
            self.wait_sent(line.at[pl.ds(1, images - 1)], 3)
            self.wait_sent(self.out.at[pl.ds(0, 3)], 4)
            self.wait_sent(four, 5)

    def piece(self, bit_value, free):
        if self.order[0] == 0:
            return bit_value + 2 * free
        return 2 * bit_value + free


def reduction_peers():
    row, col, img = lax.axis_index("row"), lax.axis_index("col"), lax.axis_index("img")
    images = lax.axis_size("img")
    peers = [{"col": 1 - col}]
    peers += [{"row": lax.rem(row + j, 4)} for j in range(1, 4)]
    peers += [{"img": lax.rem(img + j, images)} for j in range(1, images)]
    return peers


def reduce_kernel(count, *refs):
    srcs, outs, rest = refs[:count], refs[count : 2 * count], refs[2 * count :]
    send_sems, recv_sems = rest[4 * count :]
    barrier = pltpu.get_barrier_semaphore()
    peers = reduction_peers()
    for peer in peers:
        pl.semaphore_signal(barrier, inc=1, device_id=peer, device_id_type=MESH)
    pl.semaphore_wait(barrier, len(peers))
    parts = [
        Reduction(t, srcs[t], outs[t], rest[4 * t : 4 * t + 4], send_sems, recv_sems)
        for t in range(count)
    ]
    for now in range(Reduction.count + count - 1):
        for t in range(count):
            if 0 <= now - t < Reduction.count:
                parts[t].step(now - t)


def reduce_all(grads):
    count = len(grads)
    scratch = []
    for grad in grads:
        scratch += Reduction.scratch(grad.shape)
    scratch += [pltpu.SemaphoreType.DMA((count, 6)), pltpu.SemaphoreType.DMA((count, 6))]
    return pl.pallas_call(
        functools.partial(reduce_kernel, count),
        out_shape=[jax.ShapeDtypeStruct(g.shape[1:], BF16) for g in grads],
        in_specs=[VMEM] * count,
        out_specs=[VMEM] * count,
        scratch_shapes=scratch,
        compiler_params=pltpu.CompilerParams(
            collective_id=CID["reduce"], has_side_effects=True, vmem_limit_bytes=VMEM_LIMIT
        ),
        name="reduce",
    )(*grads)


def local_stats(values, weight_col, count):
    total = jnp.sum(values * weight_col, axis=0)
    away = values - total / jnp.maximum(count, 1.0)
    return total, jnp.sum(away * away * weight_col, axis=0)


def norm_forward(pre_norm, weight_col, norm_gain, norm_shift, counts):
    own_count, all_counts, plane_count = counts
    total, spread = local_stats(pre_norm, weight_col, own_count)
    batch_mean, spread = stats_over_devices(total, spread, all_counts, plane_count)
    inv_std = lax.rsqrt(spread + EPSILON)
    unit_value = (pre_norm - batch_mean) * inv_std
    return (unit_value * norm_gain + norm_shift, unit_value, inv_std, batch_mean, spread)


def norm_backward(grad_normed, unit_value, inv_std, norm_gain, weight_col, pixel_count):
    sum_grad, sum_unit = sums_over_devices(
        jnp.sum(grad_normed, axis=0), jnp.sum(grad_normed * unit_value, axis=0)
    )
    grad_pre = (
        norm_gain
        * inv_std
        * (grad_normed - (sum_grad + unit_value * sum_unit) / pixel_count)
        * weight_col
    )
    return (grad_pre.astype(BF16), sum_unit, sum_grad)


def inside_counts(orientation, tile_rows, tile_cols):
    rows, cols = lax.axis_size("row"), lax.axis_size("col")
    tall = np.clip(SHORT - np.arange(rows) * tile_rows, 0, tile_rows)[:, None] * tile_cols
    wide = np.clip(SHORT - np.arange(cols) * tile_cols, 0, tile_cols)[None, :] * tile_rows
    tall = jnp.asarray(np.broadcast_to(tall, (rows, cols)).reshape(-1), F32)
    wide = jnp.asarray(np.broadcast_to(wide, (rows, cols)).reshape(-1), F32)
    flat = (orientation == 0).astype(F32)[:, None]
    each = jnp.sum(flat * tall + (1.0 - flat) * wide, axis=0)
    place = lax.axis_index("row") * cols + lax.axis_index("col")
    own = lax.dynamic_index_in_dim(each, place, keepdims=False)
    return own, jnp.broadcast_to(each[:, None], (rows * cols, 128))


def body(
    feature_in,
    orientation,
    offset_base,
    w_reduce_a,
    w_offset_a,
    w_deform_a,
    w_expand_a,
    scale_a,
    shift_a,
    w_reduce_b,
    w_conv_b,
    w_expand_b,
    scale_b,
    shift_b,
    cotangent,
):
    images, tile_rows, tile_cols, channels = feature_in.shape
    inner_width = w_reduce_a.shape[1]
    second_cut = 2 * inner_width
    tile_pixels = tile_rows * tile_cols
    win_cols = tile_cols + HALF
    win_rows = tile_rows + 2 * PAD
    plane_count = 1.0 * images * LONG * SHORT
    pixel_count = plane_count * lax.axis_size("img")
    unbias = pixel_count / (pixel_count - 1.0)
    col_at = lax.axis_index("col")
    row_ids = lax.axis_index("row") * tile_rows + jnp.arange(tile_rows, dtype=jnp.int32)
    col_ids = col_at * tile_cols + jnp.arange(tile_cols, dtype=jnp.int32)
    landscape = jnp.broadcast_to((row_ids < SHORT)[:, None], (tile_rows, tile_cols))
    portrait = jnp.broadcast_to((col_ids < SHORT)[None, :], (tile_rows, tile_cols))
    inside = jnp.where(orientation[:, None, None] == 0, landscape[None], portrait[None]).astype(F32)
    weight_col = inside.reshape(-1, 1)
    pixels = weight_col.shape[0]
    own_count, all_counts = inside_counts(orientation, tile_rows, tile_cols)
    counts = (own_count, all_counts, plane_count)
    block_in = (
        (feature_in.astype(F32) * inside[..., None]).astype(BF16).reshape(pixels, channels)
    )
    reduced_a = jnp.dot(block_in, w_reduce_a, preferred_element_type=F32)
    normed_a1, unit_a1, inv_a1, mean_a1, spread_a1 = norm_forward(
        reduced_a, weight_col, scale_a[:inner_width], shift_a[:inner_width], counts
    )
    hidden_a = (gelu_exact(normed_a1) * weight_col).astype(BF16)
    rim_a = with_halo(
        hidden_a.reshape(images, tile_rows, tile_cols, inner_width), PAD, REACH, "halo_a"
    )
    rim_flat = rim_a.reshape(images, -1, inner_width)
    own_at = HALF * col_at
    w_off = w_offset_a.reshape(9, inner_width, 18).transpose(1, 0, 2).reshape(inner_width, 162)
    spread_taps = jnp.dot(
        rim_flat.reshape(-1, inner_width), w_off, preferred_element_type=F32
    ).reshape(images, win_rows, win_cols, 162)
    spread_taps = jnp.pad(spread_taps, ((0, 0), (0, 0), (2, 2), (0, 0)))
    spread_taps = lax.dynamic_slice_in_dim(spread_taps, own_at, tile_cols + 4, axis=2)
    offsets = 0.0
    for tap in range(9):
        i, j = 2 * (tap // 3), 2 * (tap % 3)
        offsets = offsets + spread_taps[
            :, PAD - 2 + i : PAD - 2 + i + tile_rows, j : j + tile_cols, 18 * tap : 18 * tap + 18
        ]
    fraction = jax.nn.sigmoid(offsets).reshape(images, tile_pixels, 18).transpose(0, 2, 1)
    frac_row, frac_col = fraction[:, 0::2], fraction[:, 1::2]
    base = offset_base.reshape(images, tile_pixels, 18).transpose(0, 2, 1)
    cell = np.arange(tile_pixels)
    tap_row = np.array([2 * (tap // 3 - 1) for tap in range(9)])[:, None]
    tap_col = np.array([2 * (tap % 3 - 1) for tap in range(9)])[:, None]
    upper = base[:, 0::2] + jnp.asarray(cell // tile_cols + PAD + tap_row, jnp.int32)
    left = base[:, 1::2] + jnp.asarray(cell % tile_cols + tap_col, jnp.int32) + own_at
    samples, deformed = sample_forward(
        rim_flat.transpose(0, 2, 1), w_deform_a.T, upper, left, frac_row, frac_col, win_cols
    )
    deformed = deformed.T
    normed_a2, unit_a2, inv_a2, mean_a2, spread_a2 = norm_forward(
        deformed,
        weight_col,
        scale_a[inner_width:second_cut],
        shift_a[inner_width:second_cut],
        counts,
    )
    hidden2_a = (gelu_exact(normed_a2) * weight_col).astype(BF16)
    expanded_a = jnp.dot(hidden2_a, w_expand_a, preferred_element_type=F32)
    normed_a3, unit_a3, inv_a3, mean_a3, spread_a3 = norm_forward(
        expanded_a, weight_col, scale_a[second_cut:], shift_a[second_cut:], counts
    )
    pre_a = normed_a3 + block_in.astype(F32)
    middle = (gelu_exact(pre_a) * weight_col).astype(BF16)
    reduced_b = jnp.dot(middle, w_reduce_b, preferred_element_type=F32)
    normed_b1, unit_b1, inv_b1, mean_b1, spread_b1 = norm_forward(
        reduced_b, weight_col, scale_b[:inner_width], shift_b[:inner_width], counts
    )
    hidden_b = (gelu_exact(normed_b1) * weight_col).astype(BF16)
    tile_shape = (images, tile_rows, tile_cols, inner_width)
    rim_b = with_halo(hidden_b.reshape(tile_shape), 2, 2, "halo_b")
    conv_out = conv_forward(rim_b, w_conv_b)
    normed_b2, unit_b2, inv_b2, mean_b2, spread_b2 = norm_forward(
        conv_out,
        weight_col,
        scale_b[inner_width:second_cut],
        shift_b[inner_width:second_cut],
        counts,
    )
    hidden2_b = (gelu_exact(normed_b2) * weight_col).astype(BF16)
    expanded_b = jnp.dot(hidden2_b, w_expand_b, preferred_element_type=F32)
    normed_b3, unit_b3, inv_b3, mean_b3, spread_b3 = norm_forward(
        expanded_b, weight_col, scale_b[second_cut:], shift_b[second_cut:], counts
    )
    pre_b = normed_b3 + middle.astype(F32)
    feature_out = (gelu_exact(pre_b) * weight_col).astype(BF16).reshape(feature_in.shape)
    upstream = cotangent.astype(F32).reshape(pixels, channels) * weight_col
    grad_pre_b = gelu_back(pre_b, upstream)
    grad_expand_out, gain_b3, bias_b3 = norm_backward(
        grad_pre_b, unit_b3, inv_b3, scale_b[second_cut:], weight_col, pixel_count
    )
    gw_expand_b = jnp.einsum("pm,pc->mc", hidden2_b, grad_expand_out, preferred_element_type=F32)
    grad_hidden2_b = jnp.einsum(
        "pc,mc->pm", grad_expand_out, w_expand_b, preferred_element_type=F32
    )
    grad_normed_b2 = gelu_back(normed_b2, grad_hidden2_b * weight_col)
    grad_conv_out, gain_b2, bias_b2 = norm_backward(
        grad_normed_b2, unit_b2, inv_b2, scale_b[inner_width:second_cut], weight_col, pixel_count
    )
    back_rim = with_halo(grad_conv_out.reshape(tile_shape), 2, 2, "halo_b")
    grad_hidden_b, gw_conv_b = conv_backward(rim_b, back_rim, w_conv_b, grad_conv_out)
    grad_normed_b1 = gelu_back(normed_b1, grad_hidden_b * weight_col)
    grad_reduce_out, gain_b1, bias_b1 = norm_backward(
        grad_normed_b1, unit_b1, inv_b1, scale_b[:inner_width], weight_col, pixel_count
    )
    gw_reduce_b = jnp.einsum("pc,pm->cm", middle, grad_reduce_out, preferred_element_type=F32)
    grad_middle = grad_pre_b + jnp.einsum(
        "pm,cm->pc", grad_reduce_out, w_reduce_b, preferred_element_type=F32
    )
    grad_pre_a = gelu_back(pre_a, grad_middle * weight_col)
    grad_expand_a, gain_a3, bias_a3 = norm_backward(
        grad_pre_a, unit_a3, inv_a3, scale_a[second_cut:], weight_col, pixel_count
    )
    gw_expand_a = jnp.einsum("pm,pc->mc", hidden2_a, grad_expand_a, preferred_element_type=F32)
    grad_hidden2_a = jnp.einsum("pc,mc->pm", grad_expand_a, w_expand_a, preferred_element_type=F32)
    grad_normed_a2 = gelu_back(normed_a2, grad_hidden2_a * weight_col)
    grad_deformed, gain_a2, bias_a2 = norm_backward(
        grad_normed_a2, unit_a2, inv_a2, scale_a[inner_width:second_cut], weight_col, pixel_count
    )
    gw_deform_a = jnp.dot(samples, grad_deformed, preferred_element_type=F32)
    spill, grad_row, grad_col = sample_backward(
        rim_flat, grad_deformed.T, w_deform_a, upper, left, frac_row, frac_col, win_cols
    )
    grad_fraction = jnp.stack([grad_row, grad_col], axis=2).reshape(images, 18, tile_pixels)
    grad_offsets = (grad_fraction * fraction * (1.0 - fraction)).astype(BF16)
    grad_offsets = grad_offsets.transpose(0, 2, 1).reshape(images, tile_rows, tile_cols, 18)
    placed = jnp.zeros((images, tile_rows, win_cols + 4, 18), BF16)
    placed = lax.dynamic_update_slice(placed, grad_offsets, (0, 0, own_at + 2, 0))
    on_cells = []
    for tap in range(9):
        i, j = 2 * (tap // 3 - 1), 2 * (tap % 3 - 1)
        moved = placed[:, :, 2 - j : 2 - j + win_cols]
        on_cells.append(jnp.pad(moved, ((0, 0), (PAD + i, PAD - i), (0, 0), (0, 0))))
    on_cells = jnp.concatenate(on_cells, axis=-1).reshape(-1, 162)
    gw_offset_a = jnp.einsum(
        "qm,qo->mo", rim_flat.reshape(-1, inner_width), on_cells, preferred_element_type=F32
    )
    gw_offset_a = gw_offset_a.reshape(inner_width, 9, 18).transpose(1, 0, 2).reshape(-1, 18)
    spill = spill.reshape(-1, inner_width) + jnp.einsum(
        "qo,mo->qm", on_cells, w_off, preferred_element_type=F32
    )
    grad_hidden_a = spill_home(spill.reshape(rim_a.shape)).reshape(pixels, inner_width)
    grad_normed_a1 = gelu_back(normed_a1, grad_hidden_a * weight_col)
    grad_reduce_a, gain_a1, bias_a1 = norm_backward(
        grad_normed_a1, unit_a1, inv_a1, scale_a[:inner_width], weight_col, pixel_count
    )
    gw_reduce_a = jnp.einsum("pc,pm->cm", block_in, grad_reduce_a, preferred_element_type=F32)
    grad_block_in = grad_pre_a + jnp.einsum(
        "pm,cm->pc", grad_reduce_a, w_reduce_a, preferred_element_type=F32
    )
    grad_in = (grad_block_in * weight_col).astype(BF16).reshape(feature_in.shape)

    images_axis = lax.axis_size("img")
    grads = [gw_expand_b, gw_conv_b, gw_reduce_b, gw_expand_a, gw_deform_a, gw_offset_a, gw_reduce_a]
    if gw_expand_b.shape[0] % (images_axis * 8 * 16) == 0:
        gw_offset = jnp.pad(gw_offset_a, ((0, 0), (0, 128 - 18)))
        grads[5] = gw_offset
        cut = 9 * inner_width // images_axis
        shaped = []
        for k, grad in enumerate(grads):
            grad = grad.astype(BF16)
            if k == 1:
                grad = jnp.stack([grad[:, cut * i : cut * (i + 1)] for i in range(images_axis)])
                shaped.append(grad.reshape(images_axis, 8, -1, cut))
            else:
                shaped.append(grad.reshape(images_axis, 8, -1, grad.shape[-1]))
        grads = [g.reshape(-1, g.shape[-1]) for g in reduce_all(shaped)]
        grads[1] = grads[1].T
        grads[5] = grads[5][:, :18]
    else:

        def over_devices(grad, dim):
            part = lax.psum_scatter(grad.astype(BF16), "img", scatter_dimension=dim, tiled=True)
            return lax.psum(part, ("row", "col"))

        grads = [over_devices(g, 1 if k == 1 else 0) for k, g in enumerate(grads)]
        grads[1] = grads[1].T
    gw_expand_b, gw_conv_b, gw_reduce_b, gw_expand_a, gw_deform_a, gw_offset_a, gw_reduce_a = (
        g.astype(F32) for g in grads
    )
    return (
        feature_out,
        grad_in,
        gw_reduce_a,
        gw_offset_a,
        gw_deform_a,
        gw_expand_a,
        jnp.concatenate([gain_a1, gain_a2, gain_a3]),
        jnp.concatenate([bias_a1, bias_a2, bias_a3]),
        jnp.concatenate([mean_a1, mean_a2, mean_a3]),
        jnp.concatenate([spread_a1, spread_a2, spread_a3]) * unbias,
        gw_reduce_b,
        gw_conv_b,
        gw_expand_b,
        jnp.concatenate([gain_b1, gain_b2, gain_b3]),
        jnp.concatenate([bias_b1, bias_b2, bias_b3]),
        jnp.concatenate([mean_b1, mean_b2, mean_b3]),
        jnp.concatenate([spread_b1, spread_b2, spread_b3]) * unbias,
    )


def solution(mesh):
    tiles = P("img", "row", "col", None)
    in_specs = (tiles, P("img"), tiles) + (P(),) * 11 + (tiles,)
    shares = P("img", None)
    out_specs = (tiles, tiles) + (shares,) * 4 + (P(),) * 4 + (shares,) * 3 + (P(),) * 4
    return jax.shard_map(body, mesh=mesh, in_specs=in_specs, out_specs=out_specs, check_vma=False)
```

```python
import functools
import types

import jax
import jax.numpy as jnp
import numpy as np
from jax import lax
from jax.experimental import pallas as pl
from jax.experimental.pallas import tpu as pltpu
from jax.sharding import PartitionSpec as P

LONG = 64
SHORT = 44
BOUND = 4
EPSILON = 1e-05
IMG, ROW, COL = "img", "row", "col"
MESH = pl.DeviceIdType.MESH
VMEM = pl.BlockSpec(memory_space=pltpu.VMEM)
VMEM_LIMIT = 60 * 1024 * 1024
F32 = jnp.float32
BF16 = jnp.bfloat16
REACH = BOUND + 3
PAD = 8
HALF = 16
STATS_CID, HALO_CID, FORWARD_A_CID, FORWARD_B_CID = 0, 1, 2, 3
BACKWARD_B_CID, BACKWARD_A_CID, BACKWARD_S_CID, LAST_CID = 4, 5, 6, 7


def gelu_exact(values):
    return jax.nn.gelu(values, approximate=False)


def group_of(axes):
    sizes = [lax.axis_size(a) for a in axes]
    total = int(np.prod(sizes))
    place = lax.axis_index(axes[0])
    for axis, size in zip(axes[1:], sizes[1:]):
        place = place * size + lax.axis_index(axis)

    def device(step):
        spot = lax.rem(place + step, total)
        coords = {}
        for axis, size in zip(reversed(axes), reversed(sizes)):
            coords[axis] = lax.rem(spot, size)
            spot = spot // size
        return coords

    return place, total, device


PLANE = (ROW, COL)
LINE = (IMG,)


def entry_barrier(groups):
    barrier = pltpu.get_barrier_semaphore()
    count = 0
    for axes in groups:
        _, total, device = group_of(axes)
        for step in range(1, total):
            pl.semaphore_signal(barrier, inc=1, device_id=device(step), device_id_type=MESH)
        count += total - 1
    pl.semaphore_wait(barrier, count)


def gather_start(axes, slots, send_sem, recv_sem):
    _, total, device = group_of(axes)
    for step in range(1, total):
        pltpu.make_async_remote_copy(
            src_ref=slots.at[0],
            dst_ref=slots.at[step],
            send_sem=send_sem,
            recv_sem=recv_sem,
            device_id=device(step),
            device_id_type=MESH,
        ).start()


def gather_wait(axes, slots, sem):
    _, total, _ = group_of(axes)
    others = slots.at[pl.ds(1, total - 1)]
    pltpu.make_async_copy(others, others, sem).wait()


def in_order(axes, slots):
    place, total, _ = group_of(axes)
    return [slots[lax.rem(place - spot + total, total)] for spot in range(total)]


def stats_kernel(plane_count, x_ref, count_ref, o_ref, slots1, slots2, send_sems, recv_sems):
    entry_barrier((PLANE, LINE))
    half = x_ref.shape[0] // 2
    total_count = plane_count * lax.axis_size(IMG)
    slots1[0] = x_ref[...]
    gather_start(PLANE, slots1, send_sems.at[0], recv_sems.at[0])
    gather_wait(PLANE, slots1, recv_sems.at[0])
    parts = in_order(PLANE, slots1)
    total = functools.reduce(lambda a, b: a + b, [p[:half] for p in parts])
    center = total / plane_count
    spread = functools.reduce(lambda a, b: a + b, [p[half:] for p in parts])
    for spot, part in enumerate(parts):
        count = count_ref[spot : spot + 1, :]
        away = part[:half] / jnp.maximum(count, 1.0) - center
        spread = spread + count * (away * away)
    slots2[0, :half] = total
    slots2[0, half:] = spread
    gather_start(LINE, slots2, send_sems.at[1], recv_sems.at[1])
    gather_wait(LINE, slots2, recv_sems.at[1])
    parts = in_order(LINE, slots2)
    center = functools.reduce(lambda a, b: a + b, [p[:half] for p in parts]) / total_count
    spread = functools.reduce(lambda a, b: a + b, [p[half:] for p in parts])
    for part in parts:
        away = part[:half] / plane_count - center
        spread = spread + plane_count * (away * away)
    o_ref[:half] = center
    o_ref[half:] = spread / total_count
    gather_wait(PLANE, slots1, send_sems.at[0])
    gather_wait(LINE, slots2, send_sems.at[1])


def stats_over_devices(total, spread, counts, plane_count):
    width = total.shape[0]
    both = jnp.concatenate([total, spread]).reshape(-1, 128)
    rows = both.shape[0]
    scratch = []
    for axes in (PLANE, LINE):
        size = int(np.prod([lax.axis_size(a) for a in axes]))
        scratch.append(pltpu.VMEM((size, rows, 128), F32))
    scratch += [pltpu.SemaphoreType.DMA((2,)), pltpu.SemaphoreType.DMA((2,))]
    out = pl.pallas_call(
        functools.partial(stats_kernel, plane_count),
        out_shape=jax.ShapeDtypeStruct((rows, 128), F32),
        in_specs=[VMEM, VMEM],
        out_specs=VMEM,
        scratch_shapes=scratch,
        compiler_params=pltpu.CompilerParams(collective_id=STATS_CID, has_side_effects=True),
    )(both, counts)
    out = out.reshape(2, width)
    return out[0], out[1]


def halo_peers():
    row, rows, col = lax.axis_index(ROW), lax.axis_size(ROW), lax.axis_index(COL)
    return row, rows, col, {COL: 1 - col}, {ROW: row - 1}, {ROW: row + 1}


def halo_barrier():
    row, rows, _, pair, above, below = halo_peers()
    barrier = pltpu.get_barrier_semaphore()
    pl.semaphore_signal(barrier, inc=1, device_id=pair, device_id_type=MESH)

    @pl.when(row > 0)
    def _():
        pl.semaphore_signal(barrier, inc=1, device_id=above, device_id_type=MESH)

    @pl.when(row < rows - 1)
    def _():
        pl.semaphore_signal(barrier, inc=1, device_id=below, device_id_type=MESH)

    count = 1 + (row > 0).astype(jnp.int32) + (row < rows - 1).astype(jnp.int32)
    pl.semaphore_wait(barrier, count)


def halo_kernel(pad, reach, h_ref, o_ref, send_sems, recv_sems):
    row, rows, col, pair, above, below = halo_peers()
    tile_rows, tile_cols = h_ref.shape[1], h_ref.shape[2]
    off = pl.multiple_of(HALF * col, HALF)
    spot = pl.multiple_of(2 * HALF * col, HALF)
    own = pl.ds(off, tile_cols)
    mid = pl.ds(HALF, HALF)
    upper = pl.ds(pad - reach, reach)
    lower = pl.ds(pad + tile_rows, reach)
    zero_row = jnp.zeros((h_ref.shape[0],) + o_ref.shape[2:], o_ref.dtype)

    def blank(at):
        for k in range(at.start, at.stop):
            o_ref[:, k] = zero_row

    blank(slice(0, pad - reach))
    blank(slice(pad + tile_rows + reach, 2 * pad + tile_rows))

    @pl.when(row == 0)
    def _():
        blank(slice(pad - reach, pad))

    @pl.when(row == rows - 1)
    def _():
        blank(slice(pad + tile_rows, pad + tile_rows + reach))

    halo_barrier()

    def copy(src, dst, k, device):
        return pltpu.make_async_remote_copy(
            src_ref=src,
            dst_ref=dst,
            send_sem=send_sems.at[k],
            recv_sem=recv_sems.at[k],
            device_id=device,
            device_id_type=MESH,
        )

    to_pair = copy(
        h_ref.at[:, :, pl.ds(pl.multiple_of(HALF * (1 - col), HALF), HALF)],
        o_ref.at[:, pl.ds(pad, tile_rows), pl.ds(spot, HALF)],
        0,
        pair,
    )
    up = copy(h_ref.at[:, pl.ds(0, reach)], o_ref.at[:, lower, own], 1, above)
    down = copy(h_ref.at[:, pl.ds(tile_rows - reach, reach)], o_ref.at[:, upper, own], 2, below)
    from_below = copy(o_ref.at[:, lower, mid], o_ref.at[:, lower, pl.ds(spot, HALF)], 3, pair)
    from_above = copy(o_ref.at[:, upper, mid], o_ref.at[:, upper, pl.ds(spot, HALF)], 4, pair)

    @pl.when(row > 0)
    def _():
        up.start()

    @pl.when(row < rows - 1)
    def _():
        down.start()

    to_pair.start()
    for n in range(h_ref.shape[0]):
        o_ref[n, pl.ds(pad, tile_rows), own, :] = h_ref[n]

    @pl.when(row < rows - 1)
    def _():
        up.wait_recv()
        from_below.start()

    @pl.when(row > 0)
    def _():
        down.wait_recv()
        from_above.start()

    to_pair.wait()

    @pl.when(row < rows - 1)
    def _():
        down.wait_send()
        from_below.wait()

    @pl.when(row > 0)
    def _():
        up.wait_send()
        from_above.wait()


def with_halo(tile, pad, reach):
    images, rows, cols, width = tile.shape
    return pl.pallas_call(
        functools.partial(halo_kernel, pad, reach),
        out_shape=jax.ShapeDtypeStruct((images, rows + 2 * pad, cols + HALF, width), tile.dtype),
        in_specs=[VMEM],
        out_specs=VMEM,
        scratch_shapes=[pltpu.SemaphoreType.DMA((5,)), pltpu.SemaphoreType.DMA((5,))],
        compiler_params=pltpu.CompilerParams(
            collective_id=HALO_CID, has_side_effects=True, vmem_limit_bytes=VMEM_LIMIT
        ),
    )(tile)


BLOCK_ROWS = 8
SPAN = 17
WINDOW = 3 * BLOCK_ROWS


def tap_span(group, cols):
    first = 2 + 2 * group
    start = first * cols // 128 * 128
    stop = -(-(first + SPAN) * cols // 128) * 128
    return first, start, stop


def tap_weights(tap, block, cols, up_ref, left_ref, fr_ref, fc_ref, image=0, lanes=slice(None)):
    up, left, fr, fc = (
        ref[image, tap : tap + 1, lanes] for ref in (up_ref, left_ref, fr_ref, fc_ref)
    )
    up = up - block * BLOCK_ROWS
    pixels = up.shape[1]

    def pair(size, at, frac):
        ids = lax.broadcasted_iota(jnp.int32, (size, pixels), 0)
        first, second = ids == at, ids == at + 1
        value = jnp.where(first, 1.0 - frac, jnp.where(second, frac, 0.0))
        slope = jnp.where(second, 1.0, jnp.where(first, -1.0, 0.0))
        return value, slope

    return pair(WINDOW, up, fr) + pair(cols, left, fc)


def write_table(table, lane, row_w, col_w, group, cols):
    first, start, stop = tap_span(group, cols)
    pixels = row_w.shape[1]
    low = start // cols
    high = -(-stop // cols)
    for r in range(low, min(high, WINDOW)):
        table[r * cols : (r + 1) * cols, lane : lane + pixels] = (
            row_w[r : r + 1, :] * col_w
        ).astype(BF16)


def sample_kernel(rim_ref, w_ref, up_ref, left_ref, fr_ref, fc_ref, s_ref, d_ref, table):
    block = pl.program_id(1)
    width = rim_ref.shape[1]
    cols = table.shape[0] // WINDOW
    base = block * (BLOCK_ROWS * cols)
    for tap in range(9):
        row_w, _, col_w, _ = tap_weights(tap, block, cols, up_ref, left_ref, fr_ref, fc_ref)
        write_table(table, 0, row_w, col_w, tap // 3, cols)
        _, start, stop = tap_span(tap // 3, cols)
        cells = pl.ds(pl.multiple_of(base + start, 128), stop - start)
        value = jnp.dot(rim_ref[0, :, cells], table[start:stop, :], preferred_element_type=F32)
        s_ref[tap * width : (tap + 1) * width, :] = value.astype(BF16)
    d_ref[...] = jnp.dot(w_ref[...], s_ref[...], preferred_element_type=F32)


def sample_forward(rim_t, w_t, up, left, fr, fc, cols):
    images, width, cells = rim_t.shape
    pixels = up.shape[-1]
    blocks = 2
    step = pixels // blocks
    tap_spec = pl.BlockSpec((1, 16, step), lambda i, b: (i, 0, b))
    return pl.pallas_call(
        sample_kernel,
        grid=(images, blocks),
        out_shape=(
            jax.ShapeDtypeStruct((9 * width, images * pixels), BF16),
            jax.ShapeDtypeStruct((width, images * pixels), F32),
        ),
        in_specs=[
            pl.BlockSpec((1, width, cells), lambda i, b: (i, 0, 0)),
            pl.BlockSpec((width, 9 * width), lambda i, b: (0, 0)),
            tap_spec,
            tap_spec,
            tap_spec,
            tap_spec,
        ],
        out_specs=(
            pl.BlockSpec((9 * width, step), lambda i, b: (0, i * blocks + b)),
            pl.BlockSpec((width, step), lambda i, b: (0, i * blocks + b)),
        ),
        scratch_shapes=[pltpu.VMEM((WINDOW * cols, step), BF16)],
        compiler_params=pltpu.CompilerParams(vmem_limit_bytes=VMEM_LIMIT),
    )(rim_t, w_t, up, left, fr, fc)


def build_shifted(rim_ref, shifted):
    images, rows, cols, width = rim_ref.shape
    col = lax.axis_index(COL)
    tile = cols - HALF

    def fill(first):
        def one_row(k, carry):
            for n in range(images):
                line = rim_ref[n, k].astype(F32)
                none = jnp.zeros((2, width), F32)
                for d in range(3):
                    at = first + 2 * (d - 1)
                    if at < 0:
                        part = jnp.concatenate([none, line[: tile - 2]], axis=0)
                    elif at + tile > cols:
                        part = jnp.concatenate([line[at:], none], axis=0)
                    else:
                        part = line[at : at + tile]
                    shifted[n, k, :, d * width : (d + 1) * width] = part.astype(BF16)
            return carry

        lax.fori_loop(0, rows, one_row, 0)

    @pl.when(col == 0)
    def _():
        fill(0)

    @pl.when(col == 1)
    def _():
        fill(HALF)


def conv_product(shifted, w_ref, o_ref):
    images, rows, cols, width3 = shifted.shape
    tile_rows = rows - 4
    pixels = tile_rows * cols
    for n in range(images):
        total = None
        for i in range(3):
            taps = shifted[n, 2 * i : 2 * i + tile_rows].reshape(pixels, width3)
            term = jnp.dot(taps, w_ref[i * width3 : (i + 1) * width3, :], preferred_element_type=F32)
            total = term if total is None else total + term
        o_ref[n * pixels : (n + 1) * pixels, :] = total


def conv_weight_product(turned, shifted, gw_ref, i):
    images, rows, cols, width3 = shifted.shape
    tile_rows = rows - 4
    pixels = tile_rows * cols
    total = None
    for n in range(images):
        taps = shifted[n, 2 * i : 2 * i + tile_rows].reshape(pixels, width3)
        term = jnp.dot(turned[:, n * pixels : (n + 1) * pixels], taps, preferred_element_type=F32)
        total = term if total is None else total + term
    put_lanes(gw_ref, i * width3, total)


def unconv_product(shifted, w_ref, o_ref):
    images, rows, cols, width3 = shifted.shape
    width = width3 // 3
    tile_rows = rows - 4
    pixels = tile_rows * cols
    for n in range(images):
        total = None
        for tap in range(9):
            i, d = 2 - tap // 3, 2 - tap % 3
            grads = shifted[n, 2 * i : 2 * i + tile_rows, :, d * width : (d + 1) * width]
            term = lax.dot_general(
                grads.reshape(pixels, width),
                w_ref[tap * width : (tap + 1) * width, :],
                (((1,), (1,)), ((), ())),
                preferred_element_type=F32,
            )
            total = term if total is None else total + term
        o_ref[n * pixels : (n + 1) * pixels, :] = total


def halves(width):
    first = -(-width // 256) * 128
    return ((0, first), (first, width - first)) if first < width else ((0, width),)


def remote(src, dst, send, recv, device):
    return pltpu.make_async_remote_copy(
        src_ref=src, dst_ref=dst, send_sem=send, recv_sem=recv, device_id=device, device_id_type=MESH
    )


def arrival(ref, sem):
    return pltpu.make_async_copy(ref, ref, sem)


class Plane:
    @staticmethod
    def scratch(shape):
        images, _, rows, width = shape
        count = len(halves(width))
        return [
            pltpu.VMEM((images, 4, rows, width), BF16),
            pltpu.VMEM((images, 2, rows, width), BF16),
            pltpu.SemaphoreType.DMA((count, 3)),
            pltpu.SemaphoreType.DMA((count, 3)),
        ]

    def __init__(self, src, eighth, refs, part):
        half, quarter, send, recv = refs
        lanes = pl.ds(*halves(src.shape[-1])[part])
        self.src, self.half, self.quarter = (
            ref.at[:, :, :, lanes] for ref in (src, half, quarter)
        )
        self.eighth = eighth.at[:, :, lanes]
        self.images = src.shape[0]
        self.send, self.recv = [send.at[part, k] for k in range(3)], [recv.at[part, k] for k in range(3)]
        self.x_first = part == 0
        row, col = lax.axis_index(ROW), lax.axis_index(COL)
        bits = (lax.rem(row, 2), row // 2)
        peers = ({ROW: row + 1 - 2 * bits[0]}, {ROW: row + 2 - 4 * bits[1]})
        order = (0, 1) if self.x_first else (1, 0)
        self.a, self.b = (bits[k] for k in order)
        self.first, self.second = (peers[k] for k in order)
        self.mine, self.pair, self.other = 4 * col, {COL: 1 - col}, 4 * (1 - col)

    def spot(self, bit, free):
        return bit + 2 * free if self.x_first else 2 * bit + free

    def steps(self):
        return [self.to_pair, self.to_first, self.to_second, self.done]

    def to_pair(self):
        src = self.src.at[:, pl.ds(self.other, 4)]
        remote(src, self.half, self.send[0], self.recv[0], self.pair).start()

    def to_first(self):
        arrival(self.half, self.recv[0]).wait()

        def add(i, carry):
            for s in range(4):
                own = self.src[i, self.mine + s].astype(F32)
                self.half[i, s] = (own + self.half[i, s].astype(F32)).astype(BF16)
            return carry

        lax.fori_loop(0, self.images, add, 0)
        for k in range(2):
            src = self.half.at[:, self.spot(1 - self.a, k)]
            remote(src, self.quarter.at[:, k], self.send[1], self.recv[1], self.first).start()

    def to_second(self):
        arrival(self.quarter, self.recv[1]).wait()

        def add(i, carry):
            for k in range(2):
                own = self.half[i, self.spot(self.a, k)].astype(F32)
                self.quarter[i, k] = (own + self.quarter[i, k].astype(F32)).astype(BF16)
            return carry

        lax.fori_loop(0, self.images, add, 0)
        src = self.quarter.at[:, 1 - self.b]
        remote(src, self.eighth, self.send[2], self.recv[2], self.second).start()

    def done(self):
        arrival(self.eighth, self.recv[2]).wait()

        def add(i, carry):
            own = self.quarter[i, self.b].astype(F32)
            self.eighth[i] = (own + self.eighth[i].astype(F32)).astype(BF16)
            return carry

        lax.fori_loop(0, self.images, add, 0)
        arrival(self.half, self.send[0]).wait()
        arrival(self.quarter, self.send[1]).wait()
        arrival(self.eighth, self.send[2]).wait()


class Line:
    @staticmethod
    def scratch(shape):
        images, rows, width = shape
        count = len(halves(width))
        return [
            pltpu.VMEM(shape, BF16),
            pltpu.SemaphoreType.DMA((count, 3)),
            pltpu.SemaphoreType.DMA((count, 3)),
        ]

    def __init__(self, eighth, out, refs, part):
        line, send, recv = refs
        lanes = pl.ds(*halves(eighth.shape[-1])[part])
        self.eighth, self.line, self.out = (ref.at[:, :, lanes] for ref in (eighth, line, out))
        self.images = eighth.shape[0]
        self.send, self.recv = [send.at[part, k] for k in range(3)], [recv.at[part, k] for k in range(3)]
        self.img, self.row, col = (lax.axis_index(a) for a in (IMG, ROW, COL))
        self.mine, self.pair = 4 * col, {COL: 1 - col}

    def steps(self):
        return [self.to_line, self.to_rows, self.to_pair, self.done]

    def arrived(self):
        return self.line.at[pl.ds(1, self.images - 1)]

    def to_line(self):
        for j in range(1, self.images):
            there = lax.rem(self.img + j, self.images)
            src = self.eighth.at[there]
            remote(src, self.line.at[j], self.send[0], self.recv[0], {IMG: there}).start()

    def to_rows(self):
        arrival(self.arrived(), self.recv[0]).wait()
        total = self.eighth[self.img].astype(F32)
        for j in range(1, self.images):
            total = total + self.line[j].astype(F32)
        spot = self.out.at[self.mine + self.row]
        self.out[self.mine + self.row] = total.astype(BF16)
        for j in range(1, 4):
            there = lax.rem(self.row + j, 4)
            remote(spot, spot, self.send[1], self.recv[1], {ROW: there}).start()

    def to_pair(self):
        arrival(self.out.at[pl.ds(0, 3)], self.recv[1]).wait()
        four = self.out.at[pl.ds(self.mine, 4)]
        remote(four, four, self.send[2], self.recv[2], self.pair).start()

    def done(self):
        arrival(self.out.at[pl.ds(0, 4)], self.recv[2]).wait()
        arrival(self.arrived(), self.send[0]).wait()
        arrival(self.out.at[pl.ds(0, 3)], self.send[1]).wait()
        arrival(self.out.at[pl.ds(0, 4)], self.send[2]).wait()


class SmallSum:
    @staticmethod
    def scratch(shape):
        sizes = [lax.axis_size(IMG), lax.axis_size(ROW) * lax.axis_size(COL)]
        return [pltpu.VMEM((size,) + shape[1:], BF16) for size in sizes] + [
            pltpu.SemaphoreType.DMA((2,)),
            pltpu.SemaphoreType.DMA((2,)),
        ]

    def __init__(self, src, out, refs):
        self.src, self.out = src, out
        self.slots1, self.slots2, self.send, self.recv = refs

    def steps(self):
        return [self.to_line, self.to_plane, self.done]

    def to_line(self):
        here, total, _ = group_of(LINE)
        self.slots1[0] = self.src[here]
        for j in range(1, total):
            there = lax.rem(here + j, total)
            remote(
                self.src.at[there], self.slots1.at[j], self.send.at[0], self.recv.at[0], {IMG: there}
            ).start()

    def to_plane(self):
        gather_wait(LINE, self.slots1, self.recv.at[0])
        total = added([p.astype(F32) for p in in_order(LINE, self.slots1)])
        self.slots2[0] = total.astype(BF16)
        gather_start(PLANE, self.slots2, self.send.at[1], self.recv.at[1])

    def done(self):
        gather_wait(PLANE, self.slots2, self.recv.at[1])
        self.out[...] = added([p.astype(F32) for p in in_order(PLANE, self.slots2)])
        gather_wait(LINE, self.slots1, self.send.at[0])
        gather_wait(PLANE, self.slots2, self.send.at[1])


class Jobs:
    def __init__(self):
        self.queue = []

    def add(self, *jobs):
        lists = [job.steps() for job in jobs]
        for k in range(max(len(steps) for steps in lists)):
            self.queue += [steps[k] for steps in lists if k < len(steps)]

    def tick(self, count=1):
        for _ in range(min(count, len(self.queue))):
            self.queue.pop(0)()

    def finish(self):
        self.tick(len(self.queue))


def plane_jobs(src, eighth, refs):
    return [Plane(src, eighth, refs, part) for part in range(len(halves(src.shape[-1])))]


def line_jobs(eighth, out, refs):
    return [Line(eighth, out, refs, part) for part in range(len(halves(out.shape[-1])))]


STEP = 32
PIECE = 256
CHUNK = 256


class Refs:
    def __init__(self):
        self.loads, self.stores = {}, {}

    def ready(self, *refs):
        for ref in refs:
            self.loads.pop(id(ref)).wait()

    def push(self, *refs):
        for ref in refs:
            self.stores[id(ref)].start()

    def flush(self):
        for copy in self.stores.values():
            copy.wait()


def fused(work, cid, ins, staged, outs, pushed, scratch):
    sizes = (len(ins), len(staged), len(outs), len(pushed))

    def kernel(*refs):
        r = Refs()
        refs = list(refs)

        def take(count):
            taken = refs[:count]
            del refs[:count]
            return taken

        in_refs, in_raw, out_refs, out_raw = (take(count) for count in sizes)
        for key, shape in scratch.items():
            setattr(r, key, take(len(shape)) if isinstance(shape, list) else take(1)[0])
        in_bufs, out_bufs = take(sizes[1]), take(sizes[3])
        in_sems, out_sems = take(2)
        for keys, named in ((ins, in_refs), (staged, in_bufs), (outs, out_refs), (pushed, out_bufs)):
            for key, ref in zip(keys, named):
                setattr(r, key, ref)
        for k, (raw, buf) in enumerate(zip(in_raw, in_bufs)):
            r.loads[id(buf)] = pltpu.make_async_copy(raw, buf, in_sems.at[k])
            r.loads[id(buf)].start()
        for k, (raw, buf) in enumerate(zip(out_raw, out_bufs)):
            r.stores[id(buf)] = pltpu.make_async_copy(buf, raw, out_sems.at[k])
        work(r)
        r.flush()

    flat = []
    for shape in scratch.values():
        flat += shape if isinstance(shape, list) else [shape]
    flat += [pltpu.VMEM(a.shape, a.dtype) for a in (*staged.values(), *pushed.values())]
    flat += [pltpu.SemaphoreType.DMA((max(count, 1),)) for count in (sizes[1], sizes[3])]
    anywhere = pl.BlockSpec(memory_space=pl.ANY)
    result = pl.pallas_call(
        kernel,
        out_shape=[*outs.values(), *pushed.values()],
        in_specs=[VMEM] * sizes[0] + [anywhere] * sizes[1],
        out_specs=[VMEM] * sizes[2] + [anywhere] * sizes[3],
        scratch_shapes=flat,
        compiler_params=pltpu.CompilerParams(
            collective_id=cid, has_side_effects=True, vmem_limit_bytes=VMEM_LIMIT
        ),
    )(*ins.values(), *staged.values())
    return types.SimpleNamespace(**dict(zip((*outs, *pushed), result)))


def signal_all():
    barrier = pltpu.get_barrier_semaphore()
    for axes in (PLANE, LINE):
        _, total, device = group_of(axes)
        for step in range(1, total):
            pl.semaphore_signal(barrier, inc=1, device_id=device(step), device_id_type=MESH)


def wait_all():
    count = sum(group_of(axes)[1] - 1 for axes in (PLANE, LINE))
    pl.semaphore_wait(pltpu.get_barrier_semaphore(), count)


def added(parts):
    return functools.reduce(lambda a, b: a + b, parts)


class Exchange:
    @staticmethod
    def scratch(width):
        rows = 2 * width // 128
        sizes = [int(np.prod([lax.axis_size(a) for a in axes])) for axes in (PLANE, LINE)]
        return [
            pltpu.VMEM((sizes[0], rows, 128), F32),
            pltpu.VMEM((sizes[1], rows, 128), F32),
            pltpu.VMEM((rows, 128), F32),
            pltpu.SemaphoreType.DMA((2,)),
            pltpu.SemaphoreType.DMA((2,)),
        ]

    def __init__(self, refs):
        self.slots1, self.slots2, self.out, self.send, self.recv = refs
        self.half = self.out.shape[0] // 2

    def put(self, first, second):
        for k in range(self.half):
            self.slots1[0, k : k + 1, :] = first[:, 128 * k : 128 * (k + 1)]
            self.slots1[0, self.half + k : self.half + k + 1, :] = second[:, 128 * k : 128 * (k + 1)]
        gather_start(PLANE, self.slots1, self.send.at[0], self.recv.at[0])

    def line(self):
        gather_start(LINE, self.slots2, self.send.at[1], self.recv.at[1])

    def middle_sums(self):
        gather_wait(PLANE, self.slots1, self.recv.at[0])
        self.slots2[0] = added(in_order(PLANE, self.slots1))
        self.line()

    def finish_sums(self):
        gather_wait(LINE, self.slots2, self.recv.at[1])
        self.out[...] = added(in_order(LINE, self.slots2))
        self.drain()

    def middle_stats(self, count_ref, plane_count):
        half = self.half
        gather_wait(PLANE, self.slots1, self.recv.at[0])
        parts = in_order(PLANE, self.slots1)
        total = added([p[:half] for p in parts])
        center = total / plane_count
        spread = added([p[half:] for p in parts])
        for spot, part in enumerate(parts):
            count = count_ref[spot : spot + 1, :]
            away = part[:half] / jnp.maximum(count, 1.0) - center
            spread = spread + count * (away * away)
        self.slots2[0, :half] = total
        self.slots2[0, half:] = spread
        self.line()

    def finish_stats(self, plane_count):
        half = self.half
        total_count = plane_count * lax.axis_size(IMG)
        gather_wait(LINE, self.slots2, self.recv.at[1])
        parts = in_order(LINE, self.slots2)
        center = added([p[:half] for p in parts]) / total_count
        spread = added([p[half:] for p in parts])
        for part in parts:
            away = part[:half] / plane_count - center
            spread = spread + plane_count * (away * away)
        self.out[:half] = center
        self.out[half:] = spread / total_count
        self.drain()

    def drain(self):
        gather_wait(PLANE, self.slots1, self.send.at[0])
        gather_wait(LINE, self.slots2, self.send.at[1])

    def rows(self):
        out = self.out[...]
        first = [out[k : k + 1] for k in range(self.half)]
        second = [out[self.half + k : self.half + k + 1] for k in range(self.half)]
        return jnp.concatenate(first, axis=1), jnp.concatenate(second, axis=1)


class Halo:
    scratch = [pltpu.SemaphoreType.DMA((5,)), pltpu.SemaphoreType.DMA((5,))]

    def __init__(self, pad, reach, tile, window, sems):
        self.row, self.rows, col, pair, above, below = halo_peers()
        self.pad, self.reach, self.tile, self.window = pad, reach, tile, window
        self.tile_rows, self.tile_cols = tile.shape[1], tile.shape[2]
        self.own = own = pl.ds(pl.multiple_of(HALF * col, HALF), self.tile_cols)
        spot = pl.ds(pl.multiple_of(2 * HALF * col, HALF), HALF)
        side = pl.ds(pl.multiple_of(HALF * (1 - col), HALF), HALF)
        mid = pl.ds(HALF, HALF)
        upper = pl.ds(pad - reach, reach)
        lower = pl.ds(pad + self.tile_rows, reach)
        send, recv = sems

        def copy(src, dst, k, device):
            return pltpu.make_async_remote_copy(
                src_ref=src,
                dst_ref=dst,
                send_sem=send.at[k],
                recv_sem=recv.at[k],
                device_id=device,
                device_id_type=MESH,
            )

        w = window
        self.to_pair = copy(
            tile.at[:, :, side], w.at[:, pl.ds(pad, self.tile_rows), spot], 0, pair
        )
        self.up = copy(tile.at[:, pl.ds(0, reach)], w.at[:, lower, own], 1, above)
        self.down = copy(
            tile.at[:, pl.ds(self.tile_rows - reach, reach)], w.at[:, upper, own], 2, below
        )
        self.from_below = copy(w.at[:, lower, mid], w.at[:, lower, spot], 3, pair)
        self.from_above = copy(w.at[:, upper, mid], w.at[:, upper, spot], 4, pair)

    def blank(self):
        window, pad, reach, tile_rows = self.window, self.pad, self.reach, self.tile_rows
        zero = jnp.zeros((window.shape[0],) + window.shape[2:], window.dtype)

        def fill(first, last):
            for k in range(first, last):
                window[:, k] = zero

        fill(0, pad - reach)
        fill(pad + tile_rows + reach, 2 * pad + tile_rows)

        @pl.when(self.row == 0)
        def _():
            fill(pad - reach, pad)

        @pl.when(self.row == self.rows - 1)
        def _():
            fill(pad + tile_rows, pad + tile_rows + reach)

    def start(self):
        @pl.when(self.row > 0)
        def _():
            self.up.start()

        @pl.when(self.row < self.rows - 1)
        def _():
            self.down.start()

        self.to_pair.start()
        for n in range(self.tile.shape[0]):
            self.window[n, pl.ds(self.pad, self.tile_rows), self.own, :] = self.tile[n]

    def middle(self):
        @pl.when(self.row < self.rows - 1)
        def _():
            self.up.wait_recv()
            self.from_below.start()

        @pl.when(self.row > 0)
        def _():
            self.down.wait_recv()
            self.from_above.start()

    def finish(self):
        self.to_pair.wait()

        @pl.when(self.row < self.rows - 1)
        def _():
            self.down.wait_send()
            self.from_below.wait()

        @pl.when(self.row > 0)
        def _():
            self.up.wait_send()
            self.from_above.wait()


def gauss(x):
    bell = jnp.exp(-0.5 * x * x)
    t = 1.0 / (1.0 + (0.3275911 * 0.7071067811865476) * jnp.abs(x))
    poly = 1.061405429 * t - 1.453152027
    poly = poly * t + 1.421413741
    poly = poly * t - 0.284496736
    poly = poly * t + 0.254829592
    tail = 0.5 * poly * t * bell
    return jnp.where(x < 0, tail, 1.0 - tail), bell * 0.3989422804014327


def wide(mask, width):
    return jnp.concatenate([mask] * (width // 128), axis=1)


def place(ref, i, lanes):
    if len(ref.shape) == 4:
        return (i // ref.shape[1], lax.rem(i, ref.shape[1]), slice(None), lanes)
    return (pl.ds(pl.multiple_of(i * STEP, STEP), STEP), lanes)


def by_rows(pixels, width, work, sums=0):
    pieces = [slice(l, l + PIECE) for l in range(0, width, PIECE)]

    def one(i, carry):
        out = []
        for k, lanes in enumerate(pieces):
            got = work(i, lanes)
            for j in range(sums):
                folded = jnp.sum(got[j].reshape(STEP // 8, 8, PIECE), axis=0)
                out.append(carry[k * sums + j] + folded)
        return tuple(out)

    start = tuple(jnp.zeros((8, PIECE), F32) for _ in range(sums * len(pieces)))
    final = lax.fori_loop(0, pixels // STEP, one, start)
    rows = []
    for j in range(sums):
        parts = [jnp.sum(final[k * sums + j], axis=0, keepdims=True) for k in range(len(pieces))]
        rows.append(jnp.concatenate(parts, axis=1))
    return rows


NORM_ROWS = 8


def norm_table(exchange, gain_ref, shift_ref, out_ref):
    mean, var = exchange.rows()
    inv = lax.rsqrt(var + EPSILON)
    out_ref[...] = jnp.zeros_like(out_ref)
    out_ref[0:1, :] = mean
    out_ref[1:2, :] = inv
    out_ref[2:3, :] = inv * gain_ref[...]
    out_ref[3:4, :] = shift_ref[...]
    out_ref[4:5, :] = var


def normed(u_ref, norm, i, lanes):
    away = u_ref[place(u_ref, i, lanes)].astype(F32) - norm[0:1, lanes]
    return away * norm[2:3, lanes] + norm[3:4, lanes], away


def activate(u_ref, norm, mask, h_ref, residual=None, slope=None, keep=None):
    def work(i, lanes):
        x, _ = normed(u_ref, norm, i, lanes)
        if residual is not None:
            x = x + residual[place(residual, i, lanes)].astype(F32)
        below, bell = gauss(x)
        m = wide(mask[place(mask, i, slice(None))], PIECE)
        h_ref[place(h_ref, i, lanes)] = (x * below * m).astype(BF16)
        if slope is not None:
            slope[place(slope, i, lanes)] = ((below + x * bell) * m).astype(BF16)
        if keep is not None:
            keep[place(keep, i, lanes)] = u_ref[place(u_ref, i, lanes)].astype(BF16)

    by_rows(mask.shape[0], norm.shape[1], work)


def device_stats(u_ref, mask, count):
    pixels, width = u_ref.shape

    def total_of(i, lanes):
        m = wide(mask[place(mask, i, slice(None))], PIECE)
        return (u_ref[place(u_ref, i, lanes)] * m,)

    (total,) = by_rows(pixels, width, total_of, 1)
    center = total / jnp.maximum(wide(count, width), 1.0)

    def spread_of(i, lanes):
        m = wide(mask[place(mask, i, slice(None))], PIECE)
        away = u_ref[place(u_ref, i, lanes)] - center[:, lanes]
        return (away * away * m,)

    (spread,) = by_rows(pixels, width, spread_of, 1)
    return total, spread


def product(a_ref, w_ref, o_ref, turned=False):
    dims = (((1,), (1 if turned else 0,)), ((), ()))

    def one(i, carry):
        rows = pl.ds(pl.multiple_of(i * CHUNK, CHUNK), CHUNK)
        o_ref[rows, :] = lax.dot_general(
            a_ref[rows, :], w_ref[...], dims, preferred_element_type=F32
        )
        return carry

    lax.fori_loop(0, a_ref.shape[0] // CHUNK, one, 0)


def turn(a_ref, t_ref):
    def one(i, carry):
        rows = pl.ds(pl.multiple_of(i * CHUNK, CHUNK), CHUNK)
        t_ref[:, rows] = a_ref[rows, :].T
        return carry

    lax.fori_loop(0, a_ref.shape[0] // CHUNK, one, 0)


def put_lanes(ref, first, value):
    width = ref.shape[-1]
    at, stop = first, first + value.shape[1]
    while at < stop:
        cut = at // width
        until = min(stop, (cut + 1) * width)
        part = value[:, at - first : until - first].astype(ref.dtype)
        lanes = slice(at - cut * width, until - cut * width)
        if len(ref.shape) == 4:
            ref[cut, :, :, lanes] = part.reshape(ref.shape[1:3] + part.shape[1:])
        else:
            ref[cut, :, lanes] = part
        at = until


def weight_product(t_ref, b_ref, gw_ref):
    channels = b_ref.shape[1]
    for first in range(0, channels, 512):
        value = jnp.dot(t_ref[...], b_ref[:, first : first + 512], preferred_element_type=F32)
        put_lanes(gw_ref, first, value)


def norm_back(e_ref, u_ref, norm, sums, pixel_count, mask, out_ref):
    sum_grad, sum_unit = (s * (1.0 / pixel_count) for s in sums)

    def work(i, lanes):
        away = u_ref[place(u_ref, i, lanes)].astype(F32) - norm[0:1, lanes]
        unit = away * norm[1:2, lanes]
        e = e_ref[place(e_ref, i, lanes)].astype(F32)
        m = wide(mask[place(mask, i, slice(None))], PIECE)
        grad = norm[2:3, lanes] * (e - sum_grad[:, lanes] - unit * sum_unit[:, lanes]) * m
        out_ref[place(out_ref, i, lanes)] = grad.astype(BF16)

    by_rows(mask.shape[0], norm.shape[1], work)


def gelu_grad(e_ref, u_ref, norm, mask):
    def work(i, lanes):
        x, away = normed(u_ref, norm, i, lanes)
        below, bell = gauss(x)
        m = wide(mask[place(mask, i, slice(None))], PIECE)
        e = e_ref[place(e_ref, i, lanes)] * (below + x * bell) * m
        e_ref[place(e_ref, i, lanes)] = e
        return e, e * (away * norm[1:2, lanes])

    return by_rows(mask.shape[0], norm.shape[1], work, 2)


def put_sums(exchange, out_ref):
    first, second = exchange.rows()
    out_ref[...] = jnp.zeros_like(out_ref)
    out_ref[0:1, :] = first
    out_ref[1:2, :] = second
    return first, second


def forward_a(plane_count, r):
    signal_all()
    ex3, ex1 = Exchange(r.ex3), Exchange(r.ex1)
    halo = Halo(2, 2, r.tile, r.rim_b, r.halo)
    halo.blank()
    r.ready(r.u_a2)
    activate(r.u_a2, r.norm_a2, r.mask, r.h2_a)
    r.push(r.h2_a)
    r.ready(r.w_expand)
    product(r.h2_a, r.w_expand, r.wide)
    count = r.counts[8:9, :]
    total, spread = device_stats(r.wide, r.mask, count)
    wait_all()
    ex3.put(total, spread)
    r.ready(r.feature, r.w_reduce)
    ex3.middle_stats(r.counts, plane_count)
    ex3.finish_stats(plane_count)
    norm_table(ex3, r.gain_a3, r.shift_a3, r.norm_a3)
    activate(r.wide, r.norm_a3, r.mask, r.middle, r.feature, r.slope_a, r.u_a3)
    r.push(r.middle, r.slope_a, r.u_a3)
    product(r.middle, r.w_reduce, r.u_b1)
    r.push(r.u_b1)
    total, spread = device_stats(r.u_b1, r.mask, count)
    ex1.put(total, spread)
    ex1.middle_stats(r.counts, plane_count)
    ex1.finish_stats(plane_count)
    norm_table(ex1, r.gain_b1, r.shift_b1, r.norm_b1)
    activate(r.u_b1, r.norm_b1, r.mask, r.tile)
    halo.start()
    halo.middle()
    halo.finish()
    r.push(r.rim_b)


def forward_b(plane_count, r):
    signal_all()
    ex2, ex3, ex4 = Exchange(r.ex2), Exchange(r.ex3), Exchange(r.ex4)
    count = r.counts[8:9, :]
    r.ready(r.rim_b)
    build_shifted(r.rim_b, r.shifted)
    r.ready(r.w_conv)
    conv_product(r.shifted, r.w_conv, r.u_b2)
    r.push(r.u_b2)
    total, spread = device_stats(r.u_b2, r.mask, count)
    wait_all()
    ex2.put(total, spread)
    ex2.middle_stats(r.counts, plane_count)
    ex2.finish_stats(plane_count)
    norm_table(ex2, r.gain_b2, r.shift_b2, r.norm_b2)
    activate(r.u_b2, r.norm_b2, r.mask, r.h2_b)
    r.push(r.h2_b)
    r.ready(r.w_expand)
    product(r.h2_b, r.w_expand, r.wide)
    total, spread = device_stats(r.wide, r.mask, count)
    ex3.put(total, spread)
    r.ready(r.middle, r.cotangent)
    ex3.middle_stats(r.counts, plane_count)
    ex3.finish_stats(plane_count)
    norm = r.norm_b3
    norm_table(ex3, r.gain_b3, r.shift_b3, norm)

    def work(i, lanes):
        x, away = normed(r.wide, norm, i, lanes)
        at = place(r.wide, i, lanes)
        r.u_b3[at] = r.wide[at].astype(BF16)
        x = x + r.middle[at].astype(F32)
        below, bell = gauss(x)
        m = wide(r.mask[place(r.mask, i, slice(None))], PIECE)
        r.feature_out[at] = (x * below * m).astype(BF16)
        e = (below + x * bell) * r.cotangent[at].astype(F32) * m
        r.e_b3[at] = e.astype(BF16)
        return e, e * (away * norm[1:2, lanes])

    sums = by_rows(r.wide.shape[0], r.wide.shape[1], work, 2)
    ex4.put(*sums)
    r.push(r.feature_out, r.e_b3, r.u_b3)
    ex4.middle_sums()
    ex4.finish_sums()
    put_sums(ex4, r.sums_b3)


def backward_b(pixel_count, r):
    signal_all()
    ex2, ex1 = Exchange(r.ex2), Exchange(r.ex1)
    halo = Halo(2, 2, r.tile, r.back_rim, r.halo)
    halo.blank()
    r.ready(r.e_b3, r.u_b3)
    sums = (r.sums_b3[0:1, :], r.sums_b3[1:2, :])
    norm_back(r.e_b3, r.u_b3, r.norm_b3, sums, pixel_count, r.mask, r.geo)
    r.ready(r.w_expand)
    product(r.geo, r.w_expand, r.grad, turned=True)
    r.ready(r.u_b2)
    sums = gelu_grad(r.grad, r.u_b2, r.norm_b2, r.mask)
    wait_all()
    ex2.put(*sums)
    r.ready(r.h2_b)
    turn(r.h2_b, r.turned)
    ex2.middle_sums()
    weight_product(r.turned, r.geo, r.gw_expand)
    r.push(r.gw_expand)
    ex2.finish_sums()
    sums = put_sums(ex2, r.sums_b2)
    norm_back(r.grad, r.u_b2, r.norm_b2, sums, pixel_count, r.mask, r.tile)
    halo.start()
    tile_rows, tile_cols, width = r.tile.shape[1:]
    pixels = tile_rows * tile_cols
    for n in range(r.tile.shape[0]):
        for k in range(0, tile_rows, 8):
            at = n * pixels + k * tile_cols
            block = r.tile[n, k : k + 8].reshape(8 * tile_cols, width)
            r.turned[:, at : at + 8 * tile_cols] = block.T
    r.ready(r.rim_b)
    build_shifted(r.rim_b, r.shifted)
    conv_weight_product(r.turned, r.shifted, r.gw_conv, 0)
    halo.middle()
    conv_weight_product(r.turned, r.shifted, r.gw_conv, 1)
    halo.finish()
    build_shifted(r.back_rim, r.back_shifted)
    r.ready(r.w_conv)
    unconv_product(r.back_shifted, r.w_conv, r.grad)
    r.ready(r.u_b1)
    sums = gelu_grad(r.grad, r.u_b1, r.norm_b1, r.mask)
    ex1.put(*sums)
    ex1.middle_sums()
    conv_weight_product(r.turned, r.shifted, r.gw_conv, 2)
    r.push(r.gw_conv)
    ex1.finish_sums()
    sums = put_sums(ex1, r.sums_b1)
    norm_back(r.grad, r.u_b1, r.norm_b1, sums, pixel_count, r.mask, r.gro_b)


def backward_a(pixel_count, direct, r):
    signal_all()
    ex3, ex2 = Exchange(r.ex3), Exchange(r.ex2)
    jobs = Jobs()
    wait_all()
    if direct:
        r.ready(r.src_conv_b, r.src_expand_b)
        jobs.add(
            *plane_jobs(r.src_conv_b, r.eighth_conv_b, r.plane_conv_b),
            *plane_jobs(r.src_expand_b, r.eighth_expand_b, r.plane_expand_b),
        )
    jobs.tick(4)
    r.ready(r.gro_b, r.w_reduce)
    product(r.gro_b, r.w_reduce, r.wide, turned=True)
    r.ready(r.e_b3, r.slope_a, r.u_a3)
    norm = r.norm_a3

    def work(i, lanes):
        at = place(r.wide, i, lanes)
        e = (r.wide[at] + r.e_b3[at].astype(F32)) * r.slope_a[at].astype(F32)
        r.e_a3[at] = e.astype(BF16)
        away = r.u_a3[at].astype(F32) - norm[0:1, lanes]
        return e, e * (away * norm[1:2, lanes])

    sums = by_rows(r.wide.shape[0], r.wide.shape[1], work, 2)
    ex3.put(*sums)
    jobs.tick(4)
    r.push(r.e_a3)
    turn(r.gro_b, r.turned)
    ex3.middle_sums()
    r.ready(r.middle)
    weight_product(r.turned, r.middle, r.gw_reduce)
    r.push(r.gw_reduce)
    ex3.finish_sums()
    sums = put_sums(ex3, r.sums_a3)
    norm_back(r.e_a3, r.u_a3, norm, sums, pixel_count, r.mask, r.e_b3)
    r.ready(r.w_expand)
    product(r.e_b3, r.w_expand, r.grad, turned=True)
    r.ready(r.u_a2)
    sums = gelu_grad(r.grad, r.u_a2, r.norm_a2, r.mask)
    ex2.put(*sums)
    r.ready(r.h2_a)
    turn(r.h2_a, r.turned)
    ex2.middle_sums()
    weight_product(r.turned, r.e_b3, r.gw_expand)
    r.push(r.gw_expand)
    jobs.tick(4)
    ex2.finish_sums()
    sums = put_sums(ex2, r.sums_a2)
    norm_back(r.grad, r.u_a2, r.norm_a2, sums, pixel_count, r.mask, r.gd)
    jobs.finish()
    if direct:
        r.push(r.eighth_conv_b, r.eighth_expand_b)


def unsample(r, plan):
    width = r.rim.shape[2]
    cols = r.table.shape[0] // WINDOW
    pixels = r.up.shape[2] // 2
    r.spill[...] = jnp.zeros_like(r.spill)
    r.grad_row[...] = jnp.zeros_like(r.grad_row)
    r.grad_col[...] = jnp.zeros_like(r.grad_col)

    def unit(step, carry):
        n, block = step // 2, lax.rem(step, 2)
        lanes = pl.ds(pl.multiple_of(block * pixels, pixels), pixels)
        base = block * (BLOCK_ROWS * cols)
        grad_in = r.turned[:, pl.ds(pl.multiple_of(step * pixels, pixels), pixels)]
        for group in range(3):
            first, start, stop = tap_span(group, cols)
            cells = pl.ds(pl.multiple_of(base + start, 128), stop - start)
            for j in range(3):
                tap = 3 * group + j
                spot = slice(j * pixels, (j + 1) * pixels)
                row_w, row_s, col_w, col_s = tap_weights(
                    tap, block, cols, r.up, r.left, r.fr, r.fc, n, lanes
                )
                write_table(r.table, j * pixels, row_w, col_w, group, cols)
                grad = jnp.dot(
                    r.w_deform[tap * width : (tap + 1) * width, :],
                    grad_in,
                    preferred_element_type=F32,
                ).astype(BF16)
                r.grads[:, spot] = grad
                scores = jnp.dot(r.rim[n, cells, :], grad, preferred_element_type=F32)
                by_value = jnp.zeros((cols, pixels), F32)
                by_slope = jnp.zeros((cols, pixels), F32)
                for k in range(first, first + SPAN):
                    line = scores[k * cols - start : (k + 1) * cols - start]
                    by_value = by_value + line * row_w[k : k + 1, :]
                    by_slope = by_slope + line * row_s[k : k + 1, :]
                r.grad_row[n, tap : tap + 1, lanes] = jnp.sum(
                    by_slope * col_w, axis=0, keepdims=True
                )
                r.grad_col[n, tap : tap + 1, lanes] = jnp.sum(
                    by_value * col_s, axis=0, keepdims=True
                )
            r.spill[n, cells, :] += lax.dot_general(
                r.table[start:stop, :],
                r.grads[...],
                (((1,), (1,)), ((), ())),
                preferred_element_type=F32,
            )
            for turn_at in range(4):
                if 3 * turn_at + group in plan:

                    @pl.when(step == turn_at)
                    def _(slot=3 * turn_at + group):
                        plan[slot]()

        return carry

    lax.fori_loop(0, 4, unit, 0)


def select_cells(r, cols):
    off = HALF * lax.axis_index(COL)
    cells = r.select.shape[1]

    def fill(i, carry):
        ids = lax.broadcasted_iota(jnp.int32, (STEP, cells), 1)
        pixel = lax.broadcasted_iota(jnp.int32, (STEP, cells), 0)
        hit = ids == pixel + (i + PAD) * cols + off
        r.select[pl.ds(pl.multiple_of(i * STEP, STEP), STEP), :] = jnp.where(hit, 1.0, 0.0).astype(
            BF16
        )
        return carry

    lax.fori_loop(0, r.select.shape[0] // STEP, fill, 0)


def unoffset(r):
    images, cells, width = r.rim.shape
    cols = r.table.shape[0] // WINDOW
    select_cells(r, cols)
    column = lax.rem(lax.broadcasted_iota(jnp.int32, (32, cells), 1), cols)
    for n in range(images):
        parts = []
        for grad, frac in ((r.grad_row, r.fr), (r.grad_col, r.fc)):
            f = frac[n]
            parts.append(grad[n] * f * (1.0 - f))
        go = jnp.concatenate(parts, axis=0).astype(BF16)
        on_tile = jnp.dot(go, r.select[...], preferred_element_type=F32)
        for tap in range(9):
            i, j = 2 * (tap // 3 - 1), 2 * (tap % 3 - 1)
            kept = on_tile
            if j < 0:
                kept = jnp.where(column >= -j, on_tile, 0.0)
            if j > 0:
                kept = jnp.where(column < cols - j, on_tile, 0.0)
            shift = (i * cols + j) % cells
            if shift:
                kept = pltpu.roll(kept, shift, axis=1)
            r.on_cells[32 * tap : 32 * tap + 32, :] = kept.astype(BF16)
        grad = jnp.dot(r.on_cells[...], r.rim[n], preferred_element_type=F32)
        if n == 0:
            r.gw_off_sum[...] = grad
        else:
            r.gw_off_sum[...] += grad
        for first in range(0, cells, 512):
            r.spill[n, first : first + 512, :] += lax.dot_general(
                r.on_cells[:, first : first + 512],
                r.w_off[...],
                (((0,), (0,)), ((), ())),
                preferred_element_type=F32,
            )
    for tap in range(9):
        put_lanes(r.gw_off, tap * width, r.gw_off_sum[32 * tap : 32 * tap + 32, :])


class Spill:
    @staticmethod
    def scratch(images, tile_rows, tile_cols, width):
        side = pltpu.VMEM((images, tile_rows + 2 * PAD, HALF, width), BF16)
        strip = pltpu.VMEM((images, REACH, tile_cols, width), BF16)
        sems = pltpu.SemaphoreType.DMA((3,))
        return [side, side, strip, strip, strip, strip, sems, sems]

    def __init__(self, spill, grad, cols, refs):
        self.spill, self.grad, self.cols = spill, grad, cols
        self.side_out, self.side_in, self.up_out, self.down_out, self.up_in, self.down_in = refs[:6]
        send, recv = refs[6:]
        self.row, self.rows, col, pair, above, below = halo_peers()
        self.images, self.all_rows = self.side_out.shape[:2]
        self.tile_rows, self.tile_cols = self.all_rows - 2 * PAD, self.up_out.shape[2]
        self.off, self.away, self.near = HALF * col, 2 * HALF * (1 - col), HALF * (1 - col)
        self.side = remote(self.side_out, self.side_in, send.at[0], recv.at[0], pair)
        self.up = remote(self.up_out, self.down_in, send.at[1], recv.at[1], above)
        self.down = remote(self.down_out, self.up_in, send.at[2], recv.at[2], below)

    def cells(self, k, first, count):
        return pl.ds(pl.multiple_of(k * self.cols + first, HALF), count)

    def start(self):
        def cast(k, carry):
            for n in range(self.images):
                self.side_out[n, k] = self.spill[n, self.cells(k, self.away, HALF), :].astype(BF16)
            return carry

        lax.fori_loop(0, self.all_rows, cast, 0)
        self.side.start()

    def edge(self, buffer, first):
        near = pl.ds(pl.multiple_of(self.near, HALF), HALF)

        def one(k, carry):
            for n in range(self.images):
                at = first + k
                buffer[n, k] = self.spill[n, self.cells(at, self.off, self.tile_cols), :].astype(BF16)
                part = self.spill[n, self.cells(at, HALF, HALF), :]
                buffer[n, k, near, :] = (part + self.side_in[n, at].astype(F32)).astype(BF16)
            return carry

        lax.fori_loop(0, REACH, one, 0)

    def middle(self):
        self.side.wait_recv()

        @pl.when(self.row > 0)
        def _():
            self.edge(self.up_out, PAD - REACH)
            self.up.start()

        @pl.when(self.row < self.rows - 1)
        def _():
            self.edge(self.down_out, PAD + self.tile_rows)
            self.down.start()

    def pixels(self, n, k, first, count):
        at = (n * self.tile_rows + k) * self.tile_cols + first
        return pl.ds(pl.multiple_of(at, HALF), count)

    def own(self):
        def fill(k, carry):
            for n in range(self.images):
                home = self.spill[n, self.cells(PAD + k, self.off, self.tile_cols), :]
                self.grad[self.pixels(n, k, 0, self.tile_cols), :] = home
                self.grad[self.pixels(n, k, self.near, HALF), :] += self.side_in[n, PAD + k].astype(F32)
            return carry

        lax.fori_loop(0, self.tile_rows, fill, 0)

    def finish(self):
        def arrive(buffer, first):
            def one(k, carry):
                for n in range(self.images):
                    at = self.pixels(n, first + k, 0, self.tile_cols)
                    self.grad[at, :] += buffer[n, k].astype(F32)
                return carry

            lax.fori_loop(0, REACH, one, 0)

        @pl.when(self.row > 0)
        def _():
            self.down.wait_recv()
            arrive(self.up_in, 0)
            self.up.wait_send()

        @pl.when(self.row < self.rows - 1)
        def _():
            self.up.wait_recv()
            arrive(self.down_in, self.tile_rows - REACH)
            self.down.wait_send()

        self.side.wait_send()


def backward_s(pixel_count, direct, r):
    signal_all()
    ex = Exchange(r.ex1)
    cols = r.table.shape[0] // WINDOW
    spill = Spill(r.spill, r.grad, cols, r.strips)
    wait_all()

    def nothing():
        pass

    first_jobs, second, third, plan = Jobs(), Jobs(), Jobs(), {}
    if direct:
        lines = Jobs()
        lines.add(
            *line_jobs(r.eighth_conv_b, r.sum_conv_b, r.line_conv_b),
            *line_jobs(r.eighth_expand_b, r.sum_expand_b, r.line_expand_b),
        )
        planes = Jobs()
        planes.add(
            *plane_jobs(r.src_reduce_b, r.eighth_reduce_b, r.plane_reduce_b),
            *plane_jobs(r.src_expand_a, r.eighth_expand_a, r.plane_expand_a),
        )
        deform = Jobs()
        deform.add(*plane_jobs(r.src_deform, r.eighth_deform, r.plane_deform))
        later = Jobs()
        later.add(
            *line_jobs(r.eighth_reduce_b, r.sum_reduce_b, r.line_reduce_b),
            *line_jobs(r.eighth_expand_a, r.sum_expand_a, r.line_expand_a),
        )
        r.ready(r.src_reduce_b, r.src_expand_a)
        planes.tick(4)
        r.ready(r.eighth_conv_b, r.eighth_expand_b)
        lines.tick(4)
        r.ready(r.src_deform)
        deform.tick(2)
        q1, q2, q3, q4 = planes.queue, lines.queue, deform.queue, later.queue
        slots = {
            2: q1[0:4],
            4: q3[0:2],
            7: q1[4:8] + q2[0:4],
            10: q1[8:12] + q4[0:4],
            11: q3[2:4] + q2[4:8],
        }

        def run(queue):
            def call():
                for step in queue:
                    step()

            return call

        plan = {slot: run(queue) for slot, queue in slots.items()}
        first_jobs.queue = q2[8:12]
        second.queue = q4[4:8]
        third.queue = q3[4:6] + q4[8:16]
    r.ready(r.gd, r.rim, r.w_deform)
    turn(r.gd, r.turned)
    unsample(r, plan)
    r.ready(r.w_off)
    unoffset(r)
    spill.start()
    r.push(r.gw_off)
    first_jobs.finish()
    spill.middle()
    spill.own()
    second.finish()
    r.ready(r.u_a1)
    spill.finish()
    sums = gelu_grad(r.grad, r.u_a1, r.norm_a1, r.mask)
    ex.put(*sums)
    third.tick(6)
    ex.middle_sums()
    ex.finish_sums()
    sums = put_sums(ex, r.sums_a1)
    norm_back(r.grad, r.u_a1, r.norm_a1, sums, pixel_count, r.mask, r.gr_a)
    third.finish()
    if direct:
        r.push(r.sum_conv_b, r.sum_expand_b, r.sum_reduce_b, r.sum_expand_a, r.eighth_deform)


def last(direct, r):
    signal_all()
    wait_all()
    jobs, plane = Jobs(), Jobs()
    if direct:
        r.ready(r.eighth_deform, r.gw_off)
        small = SmallSum(r.gw_off, r.sum_off, r.small)
        jobs.add(*line_jobs(r.eighth_deform, r.sum_deform, r.line_deform), small)
        jobs.tick(3)
    r.ready(r.gr_a, r.feature)
    turn(r.gr_a, r.turned)
    weight_product(r.turned, r.feature, r.gw_reduce)
    if direct:
        plane.add(*plane_jobs(r.gw_reduce, r.eighth_reduce_a, r.plane_reduce_a))
        plane.add(*line_jobs(r.eighth_reduce_a, r.sum_reduce_a, r.line_reduce_a))
    else:
        r.push(r.gw_reduce)
    plane.tick(2)
    r.ready(r.w_reduce, r.e_a3)

    def chunk(i, carry):
        rows = pl.ds(pl.multiple_of(i * CHUNK, CHUNK), CHUNK)
        for first in range(0, r.feature.shape[1], 512):
            lanes = slice(first, first + 512)
            grad = lax.dot_general(
                r.gr_a[rows, :],
                r.w_reduce[lanes, :],
                (((1,), (1,)), ((), ())),
                preferred_element_type=F32,
            )
            r.grad_in[rows, lanes] = (grad + r.e_a3[rows, lanes].astype(F32)).astype(BF16)
        return carry

    half = r.feature.shape[0] // CHUNK // 2
    lax.fori_loop(0, half, chunk, 0)
    plane.tick(2)
    lax.fori_loop(half, 2 * half, chunk, 0)
    r.push(r.grad_in)
    jobs.tick(3)
    plane.tick(2)
    jobs.tick(3)
    plane.tick(4)
    jobs.finish()
    plane.finish()
    if direct:
        r.push(r.sum_deform, r.sum_reduce_a)


def local_stats(values, weight_col, count):
    total = jnp.sum(values * weight_col, axis=0)
    away = values - total / jnp.maximum(count, 1.0)
    return total, jnp.sum(away * away * weight_col, axis=0)


def norm_forward(pre_norm, weight_col, norm_gain, norm_shift, counts):
    own_count, all_counts, plane_count = counts
    total, spread = local_stats(pre_norm, weight_col, own_count)
    batch_mean, spread = stats_over_devices(total, spread, all_counts, plane_count)
    inv_std = lax.rsqrt(spread + EPSILON)
    unit_value = (pre_norm - batch_mean) * inv_std
    return (unit_value * norm_gain + norm_shift, unit_value, inv_std, batch_mean, spread)


def inside_counts(orientation, tile_rows, tile_cols):
    rows, cols = lax.axis_size(ROW), lax.axis_size(COL)
    tall = np.clip(SHORT - np.arange(rows) * tile_rows, 0, tile_rows)[:, None] * tile_cols
    wide = np.clip(SHORT - np.arange(cols) * tile_cols, 0, tile_cols)[None, :] * tile_rows
    tall = jnp.asarray(np.broadcast_to(tall, (rows, cols)).reshape(-1), F32)
    wide = jnp.asarray(np.broadcast_to(wide, (rows, cols)).reshape(-1), F32)
    flat = (orientation == 0).astype(F32)[:, None]
    each = jnp.sum(flat * tall + (1.0 - flat) * wide, axis=0)
    place = lax.axis_index(ROW) * cols + lax.axis_index(COL)
    own = lax.dynamic_index_in_dim(each, place, keepdims=False)
    return own, jnp.broadcast_to(each[:, None], (rows * cols, 128))


def body(
    feature_in,
    orientation,
    offset_base,
    w_reduce_a,
    w_offset_a,
    w_deform_a,
    w_expand_a,
    scale_a,
    shift_a,
    w_reduce_b,
    w_conv_b,
    w_expand_b,
    scale_b,
    shift_b,
    cotangent,
):
    images, tile_rows, tile_cols, channels = feature_in.shape
    inner_width = w_reduce_a.shape[1]
    second_cut = 2 * inner_width
    tile_pixels = tile_rows * tile_cols
    win_cols = tile_cols + HALF
    win_rows = tile_rows + 2 * PAD
    plane_count = 1.0 * images * LONG * SHORT
    pixel_count = plane_count * lax.axis_size(IMG)
    unbias = pixel_count / (pixel_count - 1.0)
    col_at = lax.axis_index(COL)
    row_ids = lax.axis_index(ROW) * tile_rows + jnp.arange(tile_rows, dtype=jnp.int32)
    col_ids = col_at * tile_cols + jnp.arange(tile_cols, dtype=jnp.int32)
    landscape = jnp.broadcast_to((row_ids < SHORT)[:, None], (tile_rows, tile_cols))
    portrait = jnp.broadcast_to((col_ids < SHORT)[None, :], (tile_rows, tile_cols))
    inside = jnp.where(orientation[:, None, None] == 0, landscape[None], portrait[None]).astype(F32)
    weight_col = inside.reshape(-1, 1)
    pixels = weight_col.shape[0]
    own_count, all_counts = inside_counts(orientation, tile_rows, tile_cols)
    counts = (own_count, all_counts, plane_count)
    block_in = (
        (feature_in.astype(F32) * inside[..., None]).astype(BF16).reshape(pixels, channels)
    )
    reduced_a = jnp.dot(block_in, w_reduce_a, preferred_element_type=F32)
    normed_a1, unit_a1, inv_a1, mean_a1, spread_a1 = norm_forward(
        reduced_a, weight_col, scale_a[:inner_width], shift_a[:inner_width], counts
    )
    hidden_a = (gelu_exact(normed_a1) * weight_col).astype(BF16)
    rim_a = with_halo(
        hidden_a.reshape(images, tile_rows, tile_cols, inner_width), PAD, REACH
    )
    rim_flat = rim_a.reshape(images, -1, inner_width)
    own_at = HALF * col_at
    w_off = w_offset_a.reshape(9, inner_width, 18).transpose(1, 0, 2).reshape(inner_width, 162)
    spread_taps = jnp.dot(
        rim_flat.reshape(-1, inner_width), w_off, preferred_element_type=F32
    ).reshape(images, win_rows, win_cols, 162)
    spread_taps = jnp.pad(spread_taps, ((0, 0), (0, 0), (2, 2), (0, 0)))
    spread_taps = lax.dynamic_slice_in_dim(spread_taps, own_at, tile_cols + 4, axis=2)
    offsets = 0.0
    for tap in range(9):
        i, j = 2 * (tap // 3), 2 * (tap % 3)
        offsets = offsets + spread_taps[
            :, PAD - 2 + i : PAD - 2 + i + tile_rows, j : j + tile_cols, 18 * tap : 18 * tap + 18
        ]
    pad_taps = ((0, 0), (0, 16 - 9), (0, 0))
    fraction = jax.nn.sigmoid(offsets).reshape(images, tile_pixels, 18).transpose(0, 2, 1)
    frac_row, frac_col = (jnp.pad(fraction[:, k::2], pad_taps) for k in range(2))
    base = offset_base.reshape(images, tile_pixels, 18).transpose(0, 2, 1)
    cell = np.arange(tile_pixels)
    tap_row = np.array([2 * (tap // 3 - 1) for tap in range(9)])[:, None]
    tap_col = np.array([2 * (tap % 3 - 1) for tap in range(9)])[:, None]
    upper = base[:, 0::2] + jnp.asarray(cell // tile_cols + PAD + tap_row, jnp.int32)
    left = base[:, 1::2] + jnp.asarray(cell % tile_cols + tap_col, jnp.int32) + own_at
    upper, left = jnp.pad(upper, pad_taps), jnp.pad(left, pad_taps)
    samples, deformed = sample_forward(
        rim_flat.transpose(0, 2, 1), w_deform_a.T, upper, left, frac_row, frac_col, win_cols
    )
    deformed = deformed.T
    total, spread = local_stats(deformed, weight_col, own_count)
    mean_a2, spread_a2 = stats_over_devices(total, spread, all_counts, plane_count)
    one, two, three = slice(0, inner_width), slice(inner_width, second_cut), slice(second_cut, None)

    def norm_rows(mean, var, part):
        inv = lax.rsqrt(var + EPSILON)
        rows = jnp.stack([mean, inv, inv * scale_a[part], shift_a[part], var])
        return jnp.pad(rows, ((0, NORM_ROWS - 5), (0, 0)))

    norm_a1 = norm_rows(mean_a1, spread_a1, one)
    norm_a2 = norm_rows(mean_a2, spread_a2, two)
    mask = jnp.broadcast_to(weight_col, (pixels, 128))
    own_counts = jnp.broadcast_to(own_count, (8, 128))
    count_rows = jnp.concatenate([all_counts, own_counts], axis=0)

    def array(*shape, dtype=BF16):
        return jax.ShapeDtypeStruct(shape, dtype)

    def table(width):
        return array(NORM_ROWS, width, dtype=F32)

    small = (pixels, inner_width)
    big = (pixels, channels)
    window_b = (images, tile_rows + 4, win_cols, inner_width)
    shifted = pltpu.VMEM((images, tile_rows + 4, tile_cols, 3 * inner_width), BF16)
    tile = pltpu.VMEM((images, tile_rows, tile_cols, inner_width), BF16)
    turned = pltpu.VMEM((inner_width, pixels), BF16)
    images_axis = lax.axis_size(IMG)
    direct = inner_width % (images_axis * 8 * 16) == 0
    cuts = images_axis if direct else 1
    feature = feature_in.reshape(big)
    fwd_a = fused(
        functools.partial(forward_a, plane_count),
        FORWARD_A_CID,
        ins=dict(
            norm_a2=norm_a2,
            mask=mask,
            counts=count_rows,
            gain_a3=scale_a[None, three],
            shift_a3=shift_a[None, three],
            gain_b1=scale_b[None, one],
            shift_b1=shift_b[None, one],
        ),
        staged=dict(u_a2=deformed, w_expand=w_expand_a, feature=feature, w_reduce=w_reduce_b),
        outs=dict(norm_a3=table(channels), norm_b1=table(inner_width)),
        pushed=dict(
            h2_a=array(*small),
            middle=array(*big),
            slope_a=array(*big),
            u_a3=array(*big),
            u_b1=array(*small, dtype=F32),
            rim_b=array(*window_b),
        ),
        scratch=dict(
            ex3=Exchange.scratch(channels),
            ex1=Exchange.scratch(inner_width),
            halo=Halo.scratch,
            wide=pltpu.VMEM(big, F32),
            tile=tile,
        ),
    )
    fwd_b = fused(
        functools.partial(forward_b, plane_count),
        FORWARD_B_CID,
        ins=dict(
            mask=mask,
            counts=count_rows,
            gain_b2=scale_b[None, two],
            shift_b2=shift_b[None, two],
            gain_b3=scale_b[None, three],
            shift_b3=shift_b[None, three],
        ),
        staged=dict(
            rim_b=fwd_a.rim_b,
            w_conv=w_conv_b,
            w_expand=w_expand_b,
            middle=fwd_a.middle,
            cotangent=cotangent.reshape(big),
        ),
        outs=dict(norm_b2=table(inner_width), norm_b3=table(channels), sums_b3=table(channels)),
        pushed=dict(
            u_b2=array(*small, dtype=F32),
            h2_b=array(*small),
            u_b3=array(*big),
            feature_out=array(*big),
            e_b3=array(*big),
        ),
        scratch=dict(
            ex2=Exchange.scratch(inner_width),
            ex3=Exchange.scratch(channels),
            ex4=Exchange.scratch(channels),
            wide=pltpu.VMEM(big, F32),
            shifted=shifted,
        ),
    )
    bwd_b = fused(
        functools.partial(backward_b, pixel_count),
        BACKWARD_B_CID,
        ins=dict(
            mask=mask,
            norm_b3=fwd_b.norm_b3,
            sums_b3=fwd_b.sums_b3,
            norm_b2=fwd_b.norm_b2,
            norm_b1=fwd_a.norm_b1,
        ),
        staged=dict(
            e_b3=fwd_b.e_b3,
            u_b3=fwd_b.u_b3,
            w_expand=w_expand_b,
            u_b2=fwd_b.u_b2,
            h2_b=fwd_b.h2_b,
            rim_b=fwd_a.rim_b,
            w_conv=w_conv_b,
            u_b1=fwd_a.u_b1,
        ),
        outs=dict(gro_b=array(*small), sums_b2=table(inner_width), sums_b1=table(inner_width)),
        pushed=dict(
            gw_expand=array(1, inner_width, channels),
            gw_conv=array(cuts, inner_width, 9 * inner_width // cuts),
        ),
        scratch=dict(
            ex2=Exchange.scratch(inner_width),
            ex1=Exchange.scratch(inner_width),
            halo=Halo.scratch,
            geo=pltpu.VMEM(big, BF16),
            grad=pltpu.VMEM(small, F32),
            tile=tile,
            turned=turned,
            back_rim=pltpu.VMEM(window_b, BF16),
            shifted=shifted,
            back_shifted=shifted,
        ),
    )

    def eighths(grad):
        return grad.reshape(images_axis, 8, -1, grad.shape[-1])

    def eighth_of(src):
        return array(images_axis, *src.shape[2:])

    def sum_of(src):
        return array(*src.shape[1:])

    def vmem(struct):
        return pltpu.VMEM(struct.shape, struct.dtype)

    staged_a, pushed_a, scratch_a = {}, {}, {}
    if direct:
        conv_b, expand_b = eighths(bwd_b.gw_conv), eighths(bwd_b.gw_expand)
        staged_a = dict(src_conv_b=conv_b, src_expand_b=expand_b)
        pushed_a = dict(eighth_conv_b=eighth_of(conv_b), eighth_expand_b=eighth_of(expand_b))
        scratch_a = dict(
            plane_conv_b=Plane.scratch(conv_b.shape), plane_expand_b=Plane.scratch(expand_b.shape)
        )
    bwd_a = fused(
        functools.partial(backward_a, pixel_count, direct),
        BACKWARD_A_CID,
        ins=dict(mask=mask, norm_a3=fwd_a.norm_a3, norm_a2=norm_a2),
        staged=dict(
            **staged_a,
            gro_b=bwd_b.gro_b,
            w_reduce=w_reduce_b,
            e_b3=fwd_b.e_b3,
            slope_a=fwd_a.slope_a,
            u_a3=fwd_a.u_a3,
            middle=fwd_a.middle,
            w_expand=w_expand_a,
            u_a2=deformed,
            h2_a=fwd_a.h2_a,
        ),
        outs=dict(gd=array(*small), sums_a3=table(channels), sums_a2=table(inner_width)),
        pushed=dict(
            **pushed_a,
            gw_reduce=array(cuts, inner_width, channels // cuts),
            gw_expand=array(1, inner_width, channels),
            e_a3=array(*big),
        ),
        scratch=dict(
            **scratch_a,
            ex3=Exchange.scratch(channels),
            ex2=Exchange.scratch(inner_width),
            wide=pltpu.VMEM(big, F32),
            grad=pltpu.VMEM(small, F32),
            turned=turned,
        ),
    )
    feature_out = fwd_b.feature_out.reshape(feature_in.shape)
    gw_deform = jnp.dot(samples, bwd_a.gd, preferred_element_type=F32).astype(BF16)
    w_off_rows = w_offset_a.reshape(9, inner_width, 9, 2).transpose(0, 3, 2, 1)
    w_off_rows = jnp.pad(w_off_rows, ((0, 0), (0, 0), (0, 7), (0, 0))).reshape(288, inner_width)
    staged_s, pushed_s, scratch_s = {}, {}, {}
    if direct:
        reduce_b, expand_a = eighths(bwd_a.gw_reduce), eighths(bwd_a.gw_expand)
        deform = eighths(gw_deform)
        staged_s = dict(
            eighth_conv_b=bwd_a.eighth_conv_b,
            eighth_expand_b=bwd_a.eighth_expand_b,
            src_reduce_b=reduce_b,
            src_expand_a=expand_a,
            src_deform=deform,
        )
        pushed_s = dict(
            sum_conv_b=sum_of(conv_b),
            sum_expand_b=sum_of(expand_b),
            sum_reduce_b=sum_of(reduce_b),
            sum_expand_a=sum_of(expand_a),
            eighth_deform=eighth_of(deform),
        )
        scratch_s = dict(
            line_conv_b=Line.scratch(bwd_a.eighth_conv_b.shape),
            line_expand_b=Line.scratch(bwd_a.eighth_expand_b.shape),
            plane_reduce_b=Plane.scratch(reduce_b.shape),
            plane_expand_a=Plane.scratch(expand_a.shape),
            plane_deform=Plane.scratch(deform.shape),
            eighth_reduce_b=vmem(eighth_of(reduce_b)),
            eighth_expand_a=vmem(eighth_of(expand_a)),
            line_reduce_b=Line.scratch(eighth_of(reduce_b).shape),
            line_expand_a=Line.scratch(eighth_of(expand_a).shape),
        )
    cells = win_rows * win_cols
    taps_shape = (images, 16, tile_pixels)
    block = tile_pixels // 2
    bwd_s = fused(
        functools.partial(backward_s, pixel_count, direct),
        BACKWARD_S_CID,
        ins=dict(mask=mask, norm_a1=norm_a1, up=upper, left=left, fr=frac_row, fc=frac_col),
        staged=dict(
            **staged_s,
            gd=bwd_a.gd,
            rim=rim_flat,
            w_deform=w_deform_a,
            w_off=w_off_rows,
            u_a1=reduced_a,
        ),
        outs=dict(gr_a=array(*small), sums_a1=table(inner_width)),
        pushed=dict(**pushed_s, gw_off=array(cuts, 32, 9 * inner_width // cuts)),
        scratch=dict(
            **scratch_s,
            ex1=Exchange.scratch(inner_width),
            strips=Spill.scratch(images, tile_rows, tile_cols, inner_width),
            spill=pltpu.VMEM((images, cells, inner_width), F32),
            table=pltpu.VMEM((WINDOW * win_cols, 3 * block), BF16),
            grads=pltpu.VMEM((inner_width, 3 * block), BF16),
            turned=turned,
            grad_row=pltpu.VMEM(taps_shape, F32),
            grad_col=pltpu.VMEM(taps_shape, F32),
            select=pltpu.VMEM((tile_pixels, cells), BF16),
            on_cells=pltpu.VMEM((288, cells), BF16),
            gw_off_sum=pltpu.VMEM((288, inner_width), F32),
            grad=pltpu.VMEM(small, F32),
        ),
    )
    staged_l, pushed_l, scratch_l = {}, {}, {}
    if direct:
        reduce_a = array(images_axis, 8, inner_width // 8, channels // cuts)
        staged_l = dict(eighth_deform=bwd_s.eighth_deform, gw_off=bwd_s.gw_off)
        pushed_l = dict(sum_deform=sum_of(deform), sum_reduce_a=sum_of(reduce_a))
        scratch_l = dict(
            gw_reduce=vmem(reduce_a),
            small=SmallSum.scratch(bwd_s.gw_off.shape),
            line_deform=Line.scratch(bwd_s.eighth_deform.shape),
            plane_reduce_a=Plane.scratch(reduce_a.shape),
            eighth_reduce_a=vmem(eighth_of(reduce_a)),
            line_reduce_a=Line.scratch(eighth_of(reduce_a).shape),
        )
        outs_l = dict(sum_off=array(*bwd_s.gw_off.shape[1:], dtype=F32))
    else:
        pushed_l = dict(gw_reduce=array(cuts, inner_width, channels // cuts))
        outs_l = {}
    end = fused(
        functools.partial(last, direct),
        LAST_CID,
        ins={},
        staged=dict(
            **staged_l, gr_a=bwd_s.gr_a, feature=feature, w_reduce=w_reduce_a, e_a3=bwd_a.e_a3
        ),
        outs=outs_l,
        pushed=dict(**pushed_l, grad_in=array(*big)),
        scratch=dict(**scratch_l, turned=turned),
    )
    if direct:

        def rows_of(grad):
            return grad.reshape(-1, grad.shape[-1]).astype(F32)

        gw_expand_b, gw_expand_a = rows_of(bwd_s.sum_expand_b), rows_of(bwd_s.sum_expand_a)
        gw_conv_b, gw_reduce_b = rows_of(bwd_s.sum_conv_b).T, rows_of(bwd_s.sum_reduce_b).T
        gw_deform_a, gw_reduce_a = rows_of(end.sum_deform), rows_of(end.sum_reduce_a).T
        gw_off = end.sum_off
    else:

        def over_devices(grad, dim):
            part = lax.psum_scatter(grad, IMG, scatter_dimension=dim, tiled=True)
            return lax.psum(part, (ROW, COL)).astype(F32)

        gw_expand_b, gw_expand_a = (
            over_devices(g[0], 0) for g in (bwd_b.gw_expand, bwd_a.gw_expand)
        )
        gw_conv_b, gw_reduce_b, gw_reduce_a, gw_off_t = (
            over_devices(g[0], 1).T
            for g in (bwd_b.gw_conv, bwd_a.gw_reduce, end.gw_reduce, bwd_s.gw_off)
        )
        gw_deform_a = over_devices(gw_deform, 0)
        gw_off = gw_off_t.T
    gw_offset_a = gw_off.reshape(2, 16, -1)[:, :9].transpose(2, 1, 0).reshape(-1, 18)
    sums_a = [bwd_s.sums_a1, bwd_a.sums_a2, bwd_a.sums_a3]
    sums_b = [bwd_b.sums_b1, bwd_b.sums_b2, fwd_b.sums_b3]
    norms_a = [norm_a1, norm_a2, fwd_a.norm_a3]
    norms_b = [fwd_a.norm_b1, fwd_b.norm_b2, fwd_b.norm_b3]

    def join(tables, row):
        return jnp.concatenate([t[row] for t in tables])

    return (
        feature_out,
        end.grad_in.reshape(feature_in.shape),
        gw_reduce_a,
        gw_offset_a,
        gw_deform_a,
        gw_expand_a,
        join(sums_a, 1),
        join(sums_a, 0),
        join(norms_a, 0),
        join(norms_a, 4) * unbias,
        gw_reduce_b,
        gw_conv_b,
        gw_expand_b,
        join(sums_b, 1),
        join(sums_b, 0),
        join(norms_b, 0),
        join(norms_b, 4) * unbias,
    )


def solution(mesh):
    tiles = P(IMG, ROW, COL, None)
    in_specs = (tiles, P(IMG), tiles) + (P(),) * 11 + (tiles,)
    shares = P(IMG, None)
    out_specs = (tiles, tiles) + (shares,) * 4 + (P(),) * 4 + (shares,) * 3 + (P(),) * 4
    return jax.shard_map(body, mesh=mesh, in_specs=in_specs, out_specs=out_specs, check_vma=False)
```

```python
import functools
import types

import jax
import jax.numpy as jnp
import numpy as np
from jax import lax
from jax.experimental import pallas as pl
from jax.experimental.pallas import tpu as pltpu
from jax.sharding import PartitionSpec as P

LONG = 64
SHORT = 44
BOUND = 4
EPSILON = 1e-05
IMG, ROW, COL = "img", "row", "col"
MESH = pl.DeviceIdType.MESH
VMEM = pl.BlockSpec(memory_space=pltpu.VMEM)
VMEM_LIMIT = 60 * 1024 * 1024
F32 = jnp.float32
BF16 = jnp.bfloat16
REACH = BOUND + 3
PAD = 8
HALF = 16
FIRST_CID, SAMPLE_CID, FORWARD_A_CID, FORWARD_B_CID = 0, 1, 2, 3
BACKWARD_B_CID, BACKWARD_A_CID, BACKWARD_S_CID, LAST_CID = 4, 5, 6, 7


def group_of(axes):
    sizes = [lax.axis_size(a) for a in axes]
    total = int(np.prod(sizes))
    place = lax.axis_index(axes[0])
    for axis, size in zip(axes[1:], sizes[1:]):
        place = place * size + lax.axis_index(axis)

    def device(step):
        spot = lax.rem(place + step, total)
        coords = {}
        for axis, size in zip(reversed(axes), reversed(sizes)):
            coords[axis] = lax.rem(spot, size)
            spot = spot // size
        return coords

    return place, total, device


PLANE = (ROW, COL)
LINE = (IMG,)


def gather_start(axes, slots, send_sem, recv_sem):
    _, total, device = group_of(axes)
    for step in range(1, total):
        pltpu.make_async_remote_copy(
            src_ref=slots.at[0],
            dst_ref=slots.at[step],
            send_sem=send_sem,
            recv_sem=recv_sem,
            device_id=device(step),
            device_id_type=MESH,
        ).start()


def gather_wait(axes, slots, sem):
    _, total, _ = group_of(axes)
    others = slots.at[pl.ds(1, total - 1)]
    pltpu.make_async_copy(others, others, sem).wait()


def in_order(axes, slots):
    place, total, _ = group_of(axes)
    return [slots[lax.rem(place - spot + total, total)] for spot in range(total)]


def halo_peers():
    row, rows, col = lax.axis_index(ROW), lax.axis_size(ROW), lax.axis_index(COL)
    return row, rows, col, {COL: 1 - col}, {ROW: row - 1}, {ROW: row + 1}


BLOCK_ROWS = 8
SPAN = 17
WINDOW = 3 * BLOCK_ROWS


def tap_span(group, cols):
    first = 2 + 2 * group
    start = first * cols // 128 * 128
    stop = -(-(first + SPAN) * cols // 128) * 128
    return first, start, stop


def tap_weights(tap, block, cols, up_ref, left_ref, fr_ref, fc_ref, image=0, lanes=slice(None)):
    up, left, fr, fc = (
        ref[image, tap : tap + 1, lanes] for ref in (up_ref, left_ref, fr_ref, fc_ref)
    )
    up = up - block * BLOCK_ROWS
    pixels = up.shape[1]

    def pair(size, at, frac):
        ids = lax.broadcasted_iota(jnp.int32, (size, pixels), 0)
        first, second = ids == at, ids == at + 1
        value = jnp.where(first, 1.0 - frac, jnp.where(second, frac, 0.0))
        slope = jnp.where(second, 1.0, jnp.where(first, -1.0, 0.0))
        return value, slope

    return pair(WINDOW, up, fr) + pair(cols, left, fc)


def write_table(table, lane, row_w, col_w, group, cols):
    first, start, stop = tap_span(group, cols)
    pixels = row_w.shape[1]
    low = start // cols
    high = -(-stop // cols)
    for r in range(low, min(high, WINDOW)):
        table[r * cols : (r + 1) * cols, lane : lane + pixels] = (
            row_w[r : r + 1, :] * col_w
        ).astype(BF16)


def build_shifted(rim_ref, shifted):
    images, rows, cols, width = rim_ref.shape
    col = lax.axis_index(COL)
    tile = cols - HALF

    def fill(first):
        def one_row(k, carry):
            for n in range(images):
                line = rim_ref[n, k].astype(F32)
                none = jnp.zeros((2, width), F32)
                for d in range(3):
                    at = first + 2 * (d - 1)
                    if at < 0:
                        part = jnp.concatenate([none, line[: tile - 2]], axis=0)
                    elif at + tile > cols:
                        part = jnp.concatenate([line[at:], none], axis=0)
                    else:
                        part = line[at : at + tile]
                    shifted[n, k, :, d * width : (d + 1) * width] = part.astype(BF16)
            return carry

        lax.fori_loop(0, rows, one_row, 0)

    @pl.when(col == 0)
    def _():
        fill(0)

    @pl.when(col == 1)
    def _():
        fill(HALF)


def conv_product(shifted, w_ref, o_ref):
    images, rows, cols, width3 = shifted.shape
    tile_rows = rows - 4
    pixels = tile_rows * cols
    for n in range(images):
        total = None
        for i in range(3):
            taps = shifted[n, 2 * i : 2 * i + tile_rows].reshape(pixels, width3)
            term = jnp.dot(taps, w_ref[i * width3 : (i + 1) * width3, :], preferred_element_type=F32)
            total = term if total is None else total + term
        o_ref[n * pixels : (n + 1) * pixels, :] = total


def conv_weight_product(turned, shifted, gw_ref, i):
    images, rows, cols, width3 = shifted.shape
    tile_rows = rows - 4
    pixels = tile_rows * cols
    total = None
    for n in range(images):
        taps = shifted[n, 2 * i : 2 * i + tile_rows].reshape(pixels, width3)
        term = jnp.dot(turned[:, n * pixels : (n + 1) * pixels], taps, preferred_element_type=F32)
        total = term if total is None else total + term
    put_lanes(gw_ref, i * width3, total)


def unconv_product(shifted, w_ref, o_ref):
    images, rows, cols, width3 = shifted.shape
    width = width3 // 3
    tile_rows = rows - 4
    pixels = tile_rows * cols
    for n in range(images):
        total = None
        for tap in range(9):
            i, d = 2 - tap // 3, 2 - tap % 3
            grads = shifted[n, 2 * i : 2 * i + tile_rows, :, d * width : (d + 1) * width]
            term = lax.dot_general(
                grads.reshape(pixels, width),
                w_ref[tap * width : (tap + 1) * width, :],
                (((1,), (1,)), ((), ())),
                preferred_element_type=F32,
            )
            total = term if total is None else total + term
        o_ref[n * pixels : (n + 1) * pixels, :] = total


def halves(width):
    first = -(-width // 256) * 128
    return ((0, first), (first, width - first)) if first < width else ((0, width),)


def remote(src, dst, send, recv, device):
    return pltpu.make_async_remote_copy(
        src_ref=src, dst_ref=dst, send_sem=send, recv_sem=recv, device_id=device, device_id_type=MESH
    )


def arrival(ref, sem):
    return pltpu.make_async_copy(ref, ref, sem)


class Plane:
    @staticmethod
    def scratch(shape):
        images, _, rows, width = shape
        count = len(halves(width))
        return [
            pltpu.VMEM((images, 4, rows, width), BF16),
            pltpu.VMEM((images, 2, rows, width), BF16),
            pltpu.SemaphoreType.DMA((count, 3)),
            pltpu.SemaphoreType.DMA((count, 3)),
        ]

    def __init__(self, src, eighth, refs, part):
        half, quarter, send, recv = refs
        lanes = pl.ds(*halves(src.shape[-1])[part])
        self.src, self.half, self.quarter = (
            ref.at[:, :, :, lanes] for ref in (src, half, quarter)
        )
        self.eighth = eighth.at[:, :, lanes]
        self.images = src.shape[0]
        self.send, self.recv = [send.at[part, k] for k in range(3)], [recv.at[part, k] for k in range(3)]
        self.x_first = part == 0
        row, col = lax.axis_index(ROW), lax.axis_index(COL)
        bits = (lax.rem(row, 2), row // 2)
        peers = ({ROW: row + 1 - 2 * bits[0]}, {ROW: row + 2 - 4 * bits[1]})
        order = (0, 1) if self.x_first else (1, 0)
        self.a, self.b = (bits[k] for k in order)
        self.first, self.second = (peers[k] for k in order)
        self.mine, self.pair, self.other = 4 * col, {COL: 1 - col}, 4 * (1 - col)

    def spot(self, bit, free):
        return bit + 2 * free if self.x_first else 2 * bit + free

    def steps(self):
        return [self.to_pair, self.to_first, self.to_second, self.done]

    def to_pair(self):
        src = self.src.at[:, pl.ds(self.other, 4)]
        remote(src, self.half, self.send[0], self.recv[0], self.pair).start()

    def to_first(self):
        arrival(self.half, self.recv[0]).wait()

        def add(i, carry):
            for s in range(4):
                own = self.src[i, self.mine + s].astype(F32)
                self.half[i, s] = (own + self.half[i, s].astype(F32)).astype(BF16)
            return carry

        lax.fori_loop(0, self.images, add, 0)
        for k in range(2):
            src = self.half.at[:, self.spot(1 - self.a, k)]
            remote(src, self.quarter.at[:, k], self.send[1], self.recv[1], self.first).start()

    def to_second(self):
        arrival(self.quarter, self.recv[1]).wait()

        def add(i, carry):
            for k in range(2):
                own = self.half[i, self.spot(self.a, k)].astype(F32)
                self.quarter[i, k] = (own + self.quarter[i, k].astype(F32)).astype(BF16)
            return carry

        lax.fori_loop(0, self.images, add, 0)
        src = self.quarter.at[:, 1 - self.b]
        remote(src, self.eighth, self.send[2], self.recv[2], self.second).start()

    def done(self):
        arrival(self.eighth, self.recv[2]).wait()

        def add(i, carry):
            own = self.quarter[i, self.b].astype(F32)
            self.eighth[i] = (own + self.eighth[i].astype(F32)).astype(BF16)
            return carry

        lax.fori_loop(0, self.images, add, 0)
        arrival(self.half, self.send[0]).wait()
        arrival(self.quarter, self.send[1]).wait()
        arrival(self.eighth, self.send[2]).wait()


class Line:
    @staticmethod
    def scratch(shape):
        images, rows, width = shape
        count = len(halves(width))
        return [
            pltpu.VMEM(shape, BF16),
            pltpu.SemaphoreType.DMA((count, 3)),
            pltpu.SemaphoreType.DMA((count, 3)),
        ]

    def __init__(self, eighth, out, refs, part):
        line, send, recv = refs
        lanes = pl.ds(*halves(eighth.shape[-1])[part])
        self.eighth, self.line, self.out = (ref.at[:, :, lanes] for ref in (eighth, line, out))
        self.images = eighth.shape[0]
        self.send, self.recv = [send.at[part, k] for k in range(3)], [recv.at[part, k] for k in range(3)]
        self.img, self.row, col = (lax.axis_index(a) for a in (IMG, ROW, COL))
        self.mine, self.pair = 4 * col, {COL: 1 - col}

    def steps(self):
        return [self.to_line, self.to_rows, self.to_pair, self.done]

    def arrived(self):
        return self.line.at[pl.ds(1, self.images - 1)]

    def to_line(self):
        for j in range(1, self.images):
            there = lax.rem(self.img + j, self.images)
            src = self.eighth.at[there]
            remote(src, self.line.at[j], self.send[0], self.recv[0], {IMG: there}).start()

    def to_rows(self):
        arrival(self.arrived(), self.recv[0]).wait()
        total = self.eighth[self.img].astype(F32)
        for j in range(1, self.images):
            total = total + self.line[j].astype(F32)
        spot = self.out.at[self.mine + self.row]
        self.out[self.mine + self.row] = total.astype(BF16)
        for j in range(1, 4):
            there = lax.rem(self.row + j, 4)
            remote(spot, spot, self.send[1], self.recv[1], {ROW: there}).start()

    def to_pair(self):
        arrival(self.out.at[pl.ds(0, 3)], self.recv[1]).wait()
        four = self.out.at[pl.ds(self.mine, 4)]
        remote(four, four, self.send[2], self.recv[2], self.pair).start()

    def done(self):
        arrival(self.out.at[pl.ds(0, 4)], self.recv[2]).wait()
        arrival(self.arrived(), self.send[0]).wait()
        arrival(self.out.at[pl.ds(0, 3)], self.send[1]).wait()
        arrival(self.out.at[pl.ds(0, 4)], self.send[2]).wait()


class SmallSum:
    @staticmethod
    def scratch(shape):
        sizes = [lax.axis_size(IMG), lax.axis_size(ROW) * lax.axis_size(COL)]
        return [pltpu.VMEM((size,) + shape[1:], BF16) for size in sizes] + [
            pltpu.SemaphoreType.DMA((2,)),
            pltpu.SemaphoreType.DMA((2,)),
        ]

    def __init__(self, src, out, refs):
        self.src, self.out = src, out
        self.slots1, self.slots2, self.send, self.recv = refs

    def steps(self):
        return [self.to_line, self.to_plane, self.done]

    def to_line(self):
        here, total, _ = group_of(LINE)
        self.slots1[0] = self.src[here]
        for j in range(1, total):
            there = lax.rem(here + j, total)
            remote(
                self.src.at[there], self.slots1.at[j], self.send.at[0], self.recv.at[0], {IMG: there}
            ).start()

    def to_plane(self):
        gather_wait(LINE, self.slots1, self.recv.at[0])
        total = added([p.astype(F32) for p in in_order(LINE, self.slots1)])
        self.slots2[0] = total.astype(BF16)
        gather_start(PLANE, self.slots2, self.send.at[1], self.recv.at[1])

    def done(self):
        gather_wait(PLANE, self.slots2, self.recv.at[1])
        self.out[...] = added([p.astype(F32) for p in in_order(PLANE, self.slots2)])
        gather_wait(LINE, self.slots1, self.send.at[0])
        gather_wait(PLANE, self.slots2, self.send.at[1])


class Jobs:
    def __init__(self):
        self.queue = []

    def add(self, *jobs):
        lists = [job.steps() for job in jobs]
        for k in range(max(len(steps) for steps in lists)):
            self.queue += [steps[k] for steps in lists if k < len(steps)]

    def tick(self, count=1):
        for _ in range(min(count, len(self.queue))):
            self.queue.pop(0)()

    def finish(self):
        self.tick(len(self.queue))


def plane_jobs(src, eighth, refs):
    return [Plane(src, eighth, refs, part) for part in range(len(halves(src.shape[-1])))]


def line_jobs(eighth, out, refs):
    return [Line(eighth, out, refs, part) for part in range(len(halves(out.shape[-1])))]


STEP = 32
PIECE = 256
CHUNK = 256


class Refs:
    def __init__(self):
        self.loads, self.stores = {}, {}

    def ready(self, *refs):
        for ref in refs:
            self.loads.pop(id(ref)).wait()

    def push(self, *refs):
        for ref in refs:
            self.stores[id(ref)].start()

    def flush(self):
        for copy in self.stores.values():
            copy.wait()


def fused(work, cid, ins, staged, outs, pushed, scratch, smem={}):
    sizes = (len(ins), len(staged), len(outs), len(pushed))
    scalars = pl.BlockSpec(memory_space=pltpu.SMEM)

    def kernel(*refs):
        r = Refs()
        refs = list(refs)

        def take(count):
            taken = refs[:count]
            del refs[:count]
            return taken

        for key, ref in zip(smem, take(len(smem))):
            setattr(r, key, ref)
        in_refs, in_raw, out_refs, out_raw = (take(count) for count in sizes)
        for key, shape in scratch.items():
            setattr(r, key, take(len(shape)) if isinstance(shape, list) else take(1)[0])
        in_bufs, out_bufs = take(sizes[1]), take(sizes[3])
        in_sems, out_sems = take(2)
        for keys, named in ((ins, in_refs), (staged, in_bufs), (outs, out_refs), (pushed, out_bufs)):
            for key, ref in zip(keys, named):
                setattr(r, key, ref)
        for k, (raw, buf) in enumerate(zip(in_raw, in_bufs)):
            r.loads[id(buf)] = pltpu.make_async_copy(raw, buf, in_sems.at[k])
            r.loads[id(buf)].start()
        for k, (raw, buf) in enumerate(zip(out_raw, out_bufs)):
            r.stores[id(buf)] = pltpu.make_async_copy(buf, raw, out_sems.at[k])
        work(r)
        r.flush()

    flat = []
    for shape in scratch.values():
        flat += shape if isinstance(shape, list) else [shape]
    flat += [pltpu.VMEM(a.shape, a.dtype) for a in (*staged.values(), *pushed.values())]
    flat += [pltpu.SemaphoreType.DMA((max(count, 1),)) for count in (sizes[1], sizes[3])]
    anywhere = pl.BlockSpec(memory_space=pl.ANY)
    result = pl.pallas_call(
        kernel,
        out_shape=[*outs.values(), *pushed.values()],
        in_specs=[scalars] * len(smem) + [VMEM] * sizes[0] + [anywhere] * sizes[1],
        out_specs=[VMEM] * sizes[2] + [anywhere] * sizes[3],
        scratch_shapes=flat,
        compiler_params=pltpu.CompilerParams(
            collective_id=cid, has_side_effects=True, vmem_limit_bytes=VMEM_LIMIT
        ),
    )(*smem.values(), *ins.values(), *staged.values())
    return types.SimpleNamespace(**dict(zip((*outs, *pushed), result)))


def signal_all():
    barrier = pltpu.get_barrier_semaphore()
    for axes in (PLANE, LINE):
        _, total, device = group_of(axes)
        for step in range(1, total):
            pl.semaphore_signal(barrier, inc=1, device_id=device(step), device_id_type=MESH)


def wait_all():
    count = sum(group_of(axes)[1] - 1 for axes in (PLANE, LINE))
    pl.semaphore_wait(pltpu.get_barrier_semaphore(), count)


def added(parts):
    return functools.reduce(lambda a, b: a + b, parts)


class Exchange:
    @staticmethod
    def scratch(width):
        rows = 2 * width // 128
        sizes = [int(np.prod([lax.axis_size(a) for a in axes])) for axes in (PLANE, LINE)]
        return [
            pltpu.VMEM((sizes[0], rows, 128), F32),
            pltpu.VMEM((sizes[1], rows, 128), F32),
            pltpu.VMEM((rows, 128), F32),
            pltpu.SemaphoreType.DMA((2,)),
            pltpu.SemaphoreType.DMA((2,)),
        ]

    def __init__(self, refs):
        self.slots1, self.slots2, self.out, self.send, self.recv = refs
        self.half = self.out.shape[0] // 2

    def put(self, first, second):
        for k in range(self.half):
            self.slots1[0, k : k + 1, :] = first[:, 128 * k : 128 * (k + 1)]
            self.slots1[0, self.half + k : self.half + k + 1, :] = second[:, 128 * k : 128 * (k + 1)]
        gather_start(PLANE, self.slots1, self.send.at[0], self.recv.at[0])

    def line(self):
        gather_start(LINE, self.slots2, self.send.at[1], self.recv.at[1])

    def middle_sums(self):
        gather_wait(PLANE, self.slots1, self.recv.at[0])
        self.slots2[0] = added(in_order(PLANE, self.slots1))
        self.line()

    def finish_sums(self):
        gather_wait(LINE, self.slots2, self.recv.at[1])
        self.out[...] = added(in_order(LINE, self.slots2))
        self.drain()

    def middle_stats(self, count_ref, plane_count):
        half = self.half
        gather_wait(PLANE, self.slots1, self.recv.at[0])
        parts = in_order(PLANE, self.slots1)
        total = added([p[:half] for p in parts])
        center = total / plane_count
        spread = added([p[half:] for p in parts])
        for spot, part in enumerate(parts):
            count = count_ref[spot : spot + 1, :]
            away = part[:half] / jnp.maximum(count, 1.0) - center
            spread = spread + count * (away * away)
        self.slots2[0, :half] = total
        self.slots2[0, half:] = spread
        self.line()

    def finish_stats(self, plane_count):
        half = self.half
        total_count = plane_count * lax.axis_size(IMG)
        gather_wait(LINE, self.slots2, self.recv.at[1])
        parts = in_order(LINE, self.slots2)
        center = added([p[:half] for p in parts]) / total_count
        spread = added([p[half:] for p in parts])
        for part in parts:
            away = part[:half] / plane_count - center
            spread = spread + plane_count * (away * away)
        self.out[:half] = center
        self.out[half:] = spread / total_count
        self.drain()

    def drain(self):
        gather_wait(PLANE, self.slots1, self.send.at[0])
        gather_wait(LINE, self.slots2, self.send.at[1])

    def rows(self):
        out = self.out[...]
        first = [out[k : k + 1] for k in range(self.half)]
        second = [out[self.half + k : self.half + k + 1] for k in range(self.half)]
        return jnp.concatenate(first, axis=1), jnp.concatenate(second, axis=1)


class Halo:
    scratch = [pltpu.SemaphoreType.DMA((5,)), pltpu.SemaphoreType.DMA((5,))]

    def __init__(self, pad, reach, tile, window, sems):
        self.row, self.rows, col, pair, above, below = halo_peers()
        self.pad, self.reach, self.tile, self.window = pad, reach, tile, window
        self.tile_rows, self.tile_cols = tile.shape[1], tile.shape[2]
        self.own = own = pl.ds(pl.multiple_of(HALF * col, HALF), self.tile_cols)
        spot = pl.ds(pl.multiple_of(2 * HALF * col, HALF), HALF)
        side = pl.ds(pl.multiple_of(HALF * (1 - col), HALF), HALF)
        mid = pl.ds(HALF, HALF)
        upper = pl.ds(pad - reach, reach)
        lower = pl.ds(pad + self.tile_rows, reach)
        send, recv = sems

        def copy(src, dst, k, device):
            return pltpu.make_async_remote_copy(
                src_ref=src,
                dst_ref=dst,
                send_sem=send.at[k],
                recv_sem=recv.at[k],
                device_id=device,
                device_id_type=MESH,
            )

        w = window
        self.to_pair = copy(
            tile.at[:, :, side], w.at[:, pl.ds(pad, self.tile_rows), spot], 0, pair
        )
        self.up = copy(tile.at[:, pl.ds(0, reach)], w.at[:, lower, own], 1, above)
        self.down = copy(
            tile.at[:, pl.ds(self.tile_rows - reach, reach)], w.at[:, upper, own], 2, below
        )
        self.from_below = copy(w.at[:, lower, mid], w.at[:, lower, spot], 3, pair)
        self.from_above = copy(w.at[:, upper, mid], w.at[:, upper, spot], 4, pair)

    def blank(self):
        window, pad, reach, tile_rows = self.window, self.pad, self.reach, self.tile_rows
        zero = jnp.zeros((window.shape[0],) + window.shape[2:], window.dtype)

        def fill(first, last):
            for k in range(first, last):
                window[:, k] = zero

        fill(0, pad - reach)
        fill(pad + tile_rows + reach, 2 * pad + tile_rows)

        @pl.when(self.row == 0)
        def _():
            fill(pad - reach, pad)

        @pl.when(self.row == self.rows - 1)
        def _():
            fill(pad + tile_rows, pad + tile_rows + reach)

    def start(self):
        @pl.when(self.row > 0)
        def _():
            self.up.start()

        @pl.when(self.row < self.rows - 1)
        def _():
            self.down.start()

        self.to_pair.start()
        for n in range(self.tile.shape[0]):
            self.window[n, pl.ds(self.pad, self.tile_rows), self.own, :] = self.tile[n]

    def middle(self):
        @pl.when(self.row < self.rows - 1)
        def _():
            self.up.wait_recv()
            self.from_below.start()

        @pl.when(self.row > 0)
        def _():
            self.down.wait_recv()
            self.from_above.start()

    def finish(self):
        self.to_pair.wait()

        @pl.when(self.row < self.rows - 1)
        def _():
            self.down.wait_send()
            self.from_below.wait()

        @pl.when(self.row > 0)
        def _():
            self.up.wait_send()
            self.from_above.wait()


def gauss(x):
    bell = jnp.exp(-0.5 * x * x)
    t = 1.0 / (1.0 + (0.3275911 * 0.7071067811865476) * jnp.abs(x))
    poly = 1.061405429 * t - 1.453152027
    poly = poly * t + 1.421413741
    poly = poly * t - 0.284496736
    poly = poly * t + 0.254829592
    tail = 0.5 * poly * t * bell
    return jnp.where(x < 0, tail, 1.0 - tail), bell * 0.3989422804014327


def wide(mask, width):
    return jnp.concatenate([mask] * (width // 128), axis=1)


def place(ref, i, lanes):
    if len(ref.shape) == 4:
        return (i // ref.shape[1], lax.rem(i, ref.shape[1]), slice(None), lanes)
    return (pl.ds(pl.multiple_of(i * STEP, STEP), STEP), lanes)


def by_rows(pixels, width, work, sums=0):
    pieces = [slice(l, l + PIECE) for l in range(0, width, PIECE)]

    def one(i, carry):
        out = []
        for k, lanes in enumerate(pieces):
            got = work(i, lanes)
            for j in range(sums):
                folded = jnp.sum(got[j].reshape(STEP // 8, 8, PIECE), axis=0)
                out.append(carry[k * sums + j] + folded)
        return tuple(out)

    start = tuple(jnp.zeros((8, PIECE), F32) for _ in range(sums * len(pieces)))
    final = lax.fori_loop(0, pixels // STEP, one, start)
    rows = []
    for j in range(sums):
        parts = [jnp.sum(final[k * sums + j], axis=0, keepdims=True) for k in range(len(pieces))]
        rows.append(jnp.concatenate(parts, axis=1))
    return rows


NORM_ROWS = 8


def norm_table(exchange, gain_ref, shift_ref, out_ref, first):
    mean, var = exchange.rows()
    lanes = slice(first, first + mean.shape[1])
    inv = lax.rsqrt(var + EPSILON)
    out_ref[...] = jnp.zeros_like(out_ref)
    out_ref[0:1, :] = mean
    out_ref[1:2, :] = inv
    out_ref[2:3, :] = inv * gain_ref[:, lanes]
    out_ref[3:4, :] = shift_ref[:, lanes]
    out_ref[4:5, :] = var


def normed(u_ref, norm, i, lanes):
    away = u_ref[place(u_ref, i, lanes)].astype(F32) - norm[0:1, lanes]
    return away * norm[2:3, lanes] + norm[3:4, lanes], away


def activate(u_ref, norm, mask, h_ref, residual=None, slope=None, keep=None):
    def work(i, lanes):
        x, _ = normed(u_ref, norm, i, lanes)
        if residual is not None:
            x = x + residual[place(residual, i, lanes)].astype(F32)
        below, bell = gauss(x)
        m = wide(mask[place(mask, i, slice(None))], PIECE)
        h_ref[place(h_ref, i, lanes)] = (x * below * m).astype(BF16)
        if slope is not None:
            slope[place(slope, i, lanes)] = ((below + x * bell) * m).astype(BF16)
        if keep is not None:
            keep[place(keep, i, lanes)] = u_ref[place(u_ref, i, lanes)].astype(BF16)

    by_rows(mask.shape[0], norm.shape[1], work)


def device_stats(u_ref, mask, count):
    pixels, width = u_ref.shape

    def total_of(i, lanes):
        m = wide(mask[place(mask, i, slice(None))], PIECE)
        return (u_ref[place(u_ref, i, lanes)] * m,)

    (total,) = by_rows(pixels, width, total_of, 1)
    center = total / jnp.maximum(wide(count, width), 1.0)

    def spread_of(i, lanes):
        m = wide(mask[place(mask, i, slice(None))], PIECE)
        away = u_ref[place(u_ref, i, lanes)] - center[:, lanes]
        return (away * away * m,)

    (spread,) = by_rows(pixels, width, spread_of, 1)
    return total, spread


def product(a_ref, w_ref, o_ref, turned=False):
    dims = (((1,), (1 if turned else 0,)), ((), ()))

    def one(i, carry):
        rows = pl.ds(pl.multiple_of(i * CHUNK, CHUNK), CHUNK)
        o_ref[rows, :] = lax.dot_general(
            a_ref[rows, :], w_ref[...], dims, preferred_element_type=F32
        )
        return carry

    lax.fori_loop(0, a_ref.shape[0] // CHUNK, one, 0)


def turn(a_ref, t_ref):
    def one(i, carry):
        rows = pl.ds(pl.multiple_of(i * CHUNK, CHUNK), CHUNK)
        t_ref[:, rows] = a_ref[rows, :].T
        return carry

    lax.fori_loop(0, a_ref.shape[0] // CHUNK, one, 0)


def put_lanes(ref, first, value):
    width = ref.shape[-1]
    at, stop = first, first + value.shape[1]
    while at < stop:
        cut = at // width
        until = min(stop, (cut + 1) * width)
        part = value[:, at - first : until - first].astype(ref.dtype)
        lanes = slice(at - cut * width, until - cut * width)
        if len(ref.shape) == 4:
            ref[cut, :, :, lanes] = part.reshape(ref.shape[1:3] + part.shape[1:])
        else:
            ref[cut, :, lanes] = part
        at = until


def weight_product(t_ref, b_ref, gw_ref):
    channels = b_ref.shape[1]
    for first in range(0, channels, 512):
        value = jnp.dot(t_ref[...], b_ref[:, first : first + 512], preferred_element_type=F32)
        put_lanes(gw_ref, first, value)


def norm_back(e_ref, u_ref, norm, sums, pixel_count, mask, out_ref):
    sum_grad, sum_unit = (s * (1.0 / pixel_count) for s in sums)

    def work(i, lanes):
        away = u_ref[place(u_ref, i, lanes)].astype(F32) - norm[0:1, lanes]
        unit = away * norm[1:2, lanes]
        e = e_ref[place(e_ref, i, lanes)].astype(F32)
        m = wide(mask[place(mask, i, slice(None))], PIECE)
        grad = norm[2:3, lanes] * (e - sum_grad[:, lanes] - unit * sum_unit[:, lanes]) * m
        out_ref[place(out_ref, i, lanes)] = grad.astype(BF16)

    by_rows(mask.shape[0], norm.shape[1], work)


def gelu_grad(e_ref, u_ref, norm, mask):
    def work(i, lanes):
        x, away = normed(u_ref, norm, i, lanes)
        below, bell = gauss(x)
        m = wide(mask[place(mask, i, slice(None))], PIECE)
        e = e_ref[place(e_ref, i, lanes)] * (below + x * bell) * m
        e_ref[place(e_ref, i, lanes)] = e
        return e, e * (away * norm[1:2, lanes])

    return by_rows(mask.shape[0], norm.shape[1], work, 2)


def put_sums(exchange, out_ref):
    first, second = exchange.rows()
    out_ref[...] = jnp.zeros_like(out_ref)
    out_ref[0:1, :] = first
    out_ref[1:2, :] = second
    return first, second


def order_taps(rows, width):
    to = lax.broadcasted_iota(jnp.int32, (rows, width), 0)
    at = lax.broadcasted_iota(jnp.int32, (rows, width), 1)
    picked = jnp.where(to < 16, 2 * to, 2 * (to - 16) + 1)
    real = lax.rem(to, 16) < 9
    return jnp.where(jnp.logical_and(at == picked, real), 1.0, 0.0)


def make_mask(r, tile_cols):
    row, col = lax.axis_index(ROW), lax.axis_index(COL)
    rows, cols = lax.axis_size(ROW), lax.axis_size(COL)
    images = r.orientation.shape[0]
    tile_rows = r.mask.shape[0] // images // tile_cols
    tall = [r.orientation[n].astype(F32) for n in range(images)]
    for n in range(images):

        def fill(i, carry, n=n):
            column = lax.broadcasted_iota(jnp.int32, (tile_cols, 128), 0) + col * tile_cols
            portrait = jnp.where(column < SHORT, 1.0, 0.0)
            line = jnp.zeros((tile_cols, 128), jnp.int32) + (row * tile_rows + i)
            landscape = jnp.where(line < SHORT, 1.0, 0.0)
            at = (n * tile_rows + i) * tile_cols
            r.mask[pl.ds(pl.multiple_of(at, tile_cols), tile_cols), :] = (
                landscape * (1.0 - tall[n]) + portrait * tall[n]
            )
            return carry

        lax.fori_loop(0, tile_rows, fill, 0)

    def count(row, col):
        return (
            jnp.clip(SHORT - row * tile_rows, 0, tile_rows) * tile_cols,
            jnp.clip(SHORT - col * tile_cols, 0, tile_cols) * tile_rows,
        )

    def fill_count(at, row, col):
        flat, upright = (c.astype(F32) for c in count(row, col))
        total = added([flat * (1.0 - t) + upright * t for t in tall])
        r.counts[at : at + 1, :] = jnp.zeros((1, 128), F32) + total

    r.counts[...] = jnp.zeros_like(r.counts)
    for k in range(rows * cols):
        fill_count(k, jnp.int32(k // cols), jnp.int32(k % cols))
    fill_count(8, row, col)


def make_corners(r, cols):
    images, _, pixels = r.up.shape
    tile_cols = cols - HALF
    order = order_taps(32, r.base.shape[1]).astype(BF16)
    tap = lax.broadcasted_iota(jnp.int32, (16, pixels), 0)
    pixel = lax.broadcasted_iota(jnp.int32, (16, pixels), 1)
    up0 = pixel // tile_cols + PAD + 2 * (tap // 3 - 1)
    left0 = lax.rem(pixel, tile_cols) + HALF * lax.axis_index(COL) + 2 * (lax.rem(tap, 3) - 1)
    for n in range(images):
        base = r.base[n * pixels : (n + 1) * pixels, :].astype(F32).astype(BF16)
        moved = lax.dot_general(
            order, base, (((1,), (1,)), ((), ())), preferred_element_type=F32
        ).astype(jnp.int32)
        r.up[n] = moved[:16] + up0
        r.left[n] = moved[16:] + left0


def first(plane_count, r):
    signal_all()
    ex = Exchange(r.ex1)
    images, _, cols, width = r.rim.shape
    halo = Halo(PAD, REACH, r.tile, r.rim, r.halo)
    make_mask(r, cols - HALF)
    halo.blank()
    r.ready(r.feature, r.w_reduce)
    product(r.feature, r.w_reduce, r.u_a1)
    r.push(r.u_a1)
    total, spread = device_stats(r.u_a1, r.mask, r.counts[8:9, :])
    wait_all()
    ex.put(total, spread)
    make_corners(r, cols)
    ex.middle_stats(r.counts, plane_count)
    order = order_taps(32, r.w_offset.shape[1]).astype(BF16)
    for tap in range(9):
        rows = r.w_offset[tap * width : (tap + 1) * width, :]
        r.w_off[32 * tap : 32 * tap + 32, :] = lax.dot_general(
            order, rows, (((1,), (1,)), ((), ())), preferred_element_type=F32
        ).astype(BF16)
    ex.finish_stats(plane_count)
    norm_table(ex, r.scale, r.shift, r.norm_a1, 0)
    activate(r.u_a1, r.norm_a1, r.mask, r.tile)
    halo.start()
    select_cells(r, cols)
    r.push(r.select)
    halo.middle()
    r.ready(r.w_deform)
    turn(r.w_deform, r.w_turned)
    r.push(r.w_turned)
    halo.finish()
    r.push(r.rim)


def offset_fractions(r, cols):
    images, width, cells = r.rim_t.shape
    column = lax.rem(lax.broadcasted_iota(jnp.int32, (32, cells), 1), cols)
    for n in range(images):
        r.spread[...] = jnp.dot(r.w_off[...], r.rim_t[n], preferred_element_type=F32)
        total = None
        for tap in range(9):
            i, j = 2 * (tap // 3 - 1), 2 * (tap % 3 - 1)
            term = r.spread[32 * tap : 32 * tap + 32, :]
            shift = -(i * cols + j) % cells
            if shift:
                term = pltpu.roll(term, shift, axis=1)
            if j < 0:
                term = jnp.where(column >= -j, term, 0.0)
            if j > 0:
                term = jnp.where(column < cols - j, term, 0.0)
            total = term if total is None else total + term
        parts = []
        for _ in range(3):
            parts.append(total.astype(BF16))
            total = total - parts[-1].astype(F32)
        on_tile = lax.dot_general(
            jnp.concatenate(parts, axis=0),
            r.select[...],
            (((1,), (1,)), ((), ())),
            preferred_element_type=F32,
        )
        offsets = on_tile[:32] + on_tile[32:64] + on_tile[64:]
        fraction = 1.0 / (1.0 + jnp.exp(-offsets))
        r.fr[n] = fraction[:16]
        r.fc[n] = fraction[16:]


def sample(plane_count, r):
    signal_all()
    ex = Exchange(r.ex2)
    images, cells, width = r.rim.shape
    cols = r.table.shape[0] // WINDOW
    block = r.table.shape[1]
    r.ready(r.rim)
    for n in range(images):
        for at in range(0, cells, 512):
            r.rim_t[n, :, at : at + 512] = r.rim[n, at : at + 512, :].T
    r.ready(r.select, r.w_off)
    offset_fractions(r, cols)
    r.push(r.fr, r.fc)

    def unit(step, carry):
        n, b = step // 2, lax.rem(step, 2)
        lanes = pl.ds(pl.multiple_of(b * block, block), block)
        mine = pl.ds(pl.multiple_of(step * block, block), block)
        base = b * (BLOCK_ROWS * cols)
        for tap in range(9):
            row_w, _, col_w, _ = tap_weights(
                tap, b, cols, r.up, r.left, r.fr, r.fc, n, lanes
            )
            write_table(r.table, 0, row_w, col_w, tap // 3, cols)
            _, start, stop = tap_span(tap // 3, cols)
            at = pl.ds(pl.multiple_of(base + start, 128), stop - start)
            value = jnp.dot(r.rim_t[n, :, at], r.table[start:stop, :], preferred_element_type=F32)
            r.samples[tap * width : (tap + 1) * width, mine] = value.astype(BF16)
        deformed = jnp.dot(r.w_turned[...], r.samples[:, mine], preferred_element_type=F32)
        r.u_a2[mine, :] = deformed.T
        return carry

    r.ready(r.w_turned)
    lax.fori_loop(0, 2 * images, unit, 0)
    r.push(r.samples, r.u_a2)
    total, spread = device_stats(r.u_a2, r.mask, r.counts[8:9, :])
    wait_all()
    ex.put(total, spread)
    ex.middle_stats(r.counts, plane_count)
    ex.finish_stats(plane_count)
    norm_table(ex, r.scale, r.shift, r.norm_a2, width)


def finish_kernel(unbias, *refs):
    conv_b, reduce_b, reduce_a, expand_b, expand_a, deform, off = refs[:7]
    tables, outs = refs[7:19], refs[19:]
    for src, out in zip((conv_b, reduce_b, reduce_a), outs[:3]):
        eighth = src.shape[1]
        for s in range(0, 8, 2):
            rows = jnp.concatenate([src[s], src[s + 1]], axis=0).astype(F32)
            out[:, s * eighth : (s + 2) * eighth] = rows.T
    for src, out in zip((expand_b, expand_a, deform), outs[3:6]):
        rows = src.shape[1]
        for s in range(8):
            out[s * rows : (s + 1) * rows, :] = src[s].astype(F32)
    rest, total = off[...], None
    order = order_taps(32, 18).astype(BF16)
    for _ in range(3):
        part = rest.astype(BF16)
        rest = rest - part.astype(F32)
        term = lax.dot_general(part, order, (((0,), (0,)), ((), ())), preferred_element_type=F32)
        total = term if total is None else total + term
    outs[6][...] = total
    for k in range(4):
        group, which = tables[3 * k : 3 * k + 3], outs[7 + 2 * k : 9 + 2 * k]
        norms = k >= 2
        for out, row in zip(which, (0, 4) if norms else (1, 0)):
            at = 0
            for table in group:
                for first_lane in range(0, table.shape[1], 128):
                    value = table[row : row + 1, first_lane : first_lane + 128]
                    out[at : at + 1, :] = value * unbias if norms and row == 4 else value
                    at += 1


def forward_a(plane_count, r):
    signal_all()
    ex3, ex1 = Exchange(r.ex3), Exchange(r.ex1)
    halo = Halo(2, 2, r.tile, r.rim_b, r.halo)
    halo.blank()
    r.ready(r.u_a2)
    activate(r.u_a2, r.norm_a2, r.mask, r.h2_a)
    r.push(r.h2_a)
    r.ready(r.w_expand)
    product(r.h2_a, r.w_expand, r.wide)
    count = r.counts[8:9, :]
    total, spread = device_stats(r.wide, r.mask, count)
    wait_all()
    ex3.put(total, spread)
    r.ready(r.feature, r.w_reduce)
    ex3.middle_stats(r.counts, plane_count)
    ex3.finish_stats(plane_count)
    norm_table(ex3, r.scale_a, r.shift_a, r.norm_a3, 2 * r.h2_a.shape[1])
    activate(r.wide, r.norm_a3, r.mask, r.middle, r.feature, r.slope_a, r.u_a3)
    r.push(r.middle, r.slope_a, r.u_a3)
    product(r.middle, r.w_reduce, r.u_b1)
    r.push(r.u_b1)
    total, spread = device_stats(r.u_b1, r.mask, count)
    ex1.put(total, spread)
    ex1.middle_stats(r.counts, plane_count)
    ex1.finish_stats(plane_count)
    norm_table(ex1, r.scale_b, r.shift_b, r.norm_b1, 0)
    activate(r.u_b1, r.norm_b1, r.mask, r.tile)
    halo.start()
    halo.middle()
    halo.finish()
    r.push(r.rim_b)


def forward_b(plane_count, r):
    signal_all()
    ex2, ex3, ex4 = Exchange(r.ex2), Exchange(r.ex3), Exchange(r.ex4)
    count = r.counts[8:9, :]
    r.ready(r.rim_b)
    build_shifted(r.rim_b, r.shifted)
    r.ready(r.w_conv)
    conv_product(r.shifted, r.w_conv, r.u_b2)
    r.push(r.u_b2)
    total, spread = device_stats(r.u_b2, r.mask, count)
    wait_all()
    ex2.put(total, spread)
    ex2.middle_stats(r.counts, plane_count)
    ex2.finish_stats(plane_count)
    norm_table(ex2, r.scale, r.shift, r.norm_b2, r.h2_b.shape[1])
    activate(r.u_b2, r.norm_b2, r.mask, r.h2_b)
    r.push(r.h2_b)
    r.ready(r.w_expand)
    product(r.h2_b, r.w_expand, r.wide)
    total, spread = device_stats(r.wide, r.mask, count)
    ex3.put(total, spread)
    r.ready(r.middle, r.cotangent)
    ex3.middle_stats(r.counts, plane_count)
    ex3.finish_stats(plane_count)
    norm = r.norm_b3
    norm_table(ex3, r.scale, r.shift, norm, 2 * r.h2_b.shape[1])

    def work(i, lanes):
        x, away = normed(r.wide, norm, i, lanes)
        at = place(r.wide, i, lanes)
        r.u_b3[at] = r.wide[at].astype(BF16)
        x = x + r.middle[at].astype(F32)
        below, bell = gauss(x)
        m = wide(r.mask[place(r.mask, i, slice(None))], PIECE)
        r.feature_out[at] = (x * below * m).astype(BF16)
        e = (below + x * bell) * r.cotangent[at].astype(F32) * m
        r.e_b3[at] = e.astype(BF16)
        return e, e * (away * norm[1:2, lanes])

    sums = by_rows(r.wide.shape[0], r.wide.shape[1], work, 2)
    ex4.put(*sums)
    r.push(r.feature_out, r.e_b3, r.u_b3)
    ex4.middle_sums()
    ex4.finish_sums()
    put_sums(ex4, r.sums_b3)


def backward_b(pixel_count, r):
    signal_all()
    ex2, ex1 = Exchange(r.ex2), Exchange(r.ex1)
    halo = Halo(2, 2, r.tile, r.back_rim, r.halo)
    halo.blank()
    r.ready(r.e_b3, r.u_b3)
    sums = (r.sums_b3[0:1, :], r.sums_b3[1:2, :])
    norm_back(r.e_b3, r.u_b3, r.norm_b3, sums, pixel_count, r.mask, r.geo)
    r.ready(r.w_expand)
    product(r.geo, r.w_expand, r.grad, turned=True)
    r.ready(r.u_b2)
    sums = gelu_grad(r.grad, r.u_b2, r.norm_b2, r.mask)
    wait_all()
    ex2.put(*sums)
    r.ready(r.h2_b)
    turn(r.h2_b, r.turned)
    ex2.middle_sums()
    weight_product(r.turned, r.geo, r.gw_expand)
    r.push(r.gw_expand)
    ex2.finish_sums()
    sums = put_sums(ex2, r.sums_b2)
    norm_back(r.grad, r.u_b2, r.norm_b2, sums, pixel_count, r.mask, r.tile)
    halo.start()
    tile_rows, tile_cols, width = r.tile.shape[1:]
    pixels = tile_rows * tile_cols
    for n in range(r.tile.shape[0]):
        for k in range(0, tile_rows, 8):
            at = n * pixels + k * tile_cols
            block = r.tile[n, k : k + 8].reshape(8 * tile_cols, width)
            r.turned[:, at : at + 8 * tile_cols] = block.T
    r.ready(r.rim_b)
    build_shifted(r.rim_b, r.shifted)
    conv_weight_product(r.turned, r.shifted, r.gw_conv, 0)
    halo.middle()
    conv_weight_product(r.turned, r.shifted, r.gw_conv, 1)
    halo.finish()
    build_shifted(r.back_rim, r.back_shifted)
    r.ready(r.w_conv)
    unconv_product(r.back_shifted, r.w_conv, r.grad)
    r.ready(r.u_b1)
    sums = gelu_grad(r.grad, r.u_b1, r.norm_b1, r.mask)
    ex1.put(*sums)
    ex1.middle_sums()
    conv_weight_product(r.turned, r.shifted, r.gw_conv, 2)
    r.push(r.gw_conv)
    ex1.finish_sums()
    sums = put_sums(ex1, r.sums_b1)
    norm_back(r.grad, r.u_b1, r.norm_b1, sums, pixel_count, r.mask, r.gro_b)


def backward_a(pixel_count, direct, r):
    signal_all()
    ex3, ex2 = Exchange(r.ex3), Exchange(r.ex2)
    jobs = Jobs()
    wait_all()
    if direct:
        r.ready(r.src_conv_b, r.src_expand_b)
        jobs.add(
            *plane_jobs(r.src_conv_b, r.eighth_conv_b, r.plane_conv_b),
            *plane_jobs(r.src_expand_b, r.eighth_expand_b, r.plane_expand_b),
        )
    jobs.tick(4)
    r.ready(r.gro_b, r.w_reduce)
    product(r.gro_b, r.w_reduce, r.wide, turned=True)
    r.ready(r.e_b3, r.slope_a, r.u_a3)
    norm = r.norm_a3

    def work(i, lanes):
        at = place(r.wide, i, lanes)
        e = (r.wide[at] + r.e_b3[at].astype(F32)) * r.slope_a[at].astype(F32)
        r.e_a3[at] = e.astype(BF16)
        away = r.u_a3[at].astype(F32) - norm[0:1, lanes]
        return e, e * (away * norm[1:2, lanes])

    sums = by_rows(r.wide.shape[0], r.wide.shape[1], work, 2)
    ex3.put(*sums)
    jobs.tick(4)
    r.push(r.e_a3)
    turn(r.gro_b, r.turned)
    ex3.middle_sums()
    r.ready(r.middle)
    weight_product(r.turned, r.middle, r.gw_reduce)
    r.push(r.gw_reduce)
    ex3.finish_sums()
    sums = put_sums(ex3, r.sums_a3)
    norm_back(r.e_a3, r.u_a3, norm, sums, pixel_count, r.mask, r.e_b3)
    r.ready(r.w_expand)
    product(r.e_b3, r.w_expand, r.grad, turned=True)
    r.ready(r.u_a2)
    sums = gelu_grad(r.grad, r.u_a2, r.norm_a2, r.mask)
    ex2.put(*sums)
    r.ready(r.h2_a)
    turn(r.h2_a, r.turned)
    ex2.middle_sums()
    weight_product(r.turned, r.e_b3, r.gw_expand)
    r.push(r.gw_expand)
    jobs.tick(4)
    ex2.finish_sums()
    sums = put_sums(ex2, r.sums_a2)
    norm_back(r.grad, r.u_a2, r.norm_a2, sums, pixel_count, r.mask, r.gd)
    jobs.finish()
    if direct:
        r.push(r.eighth_conv_b, r.eighth_expand_b)


def unsample(r, plan):
    width = r.rim.shape[2]
    cols = r.table.shape[0] // WINDOW
    pixels = r.up.shape[2] // 2
    r.spill[...] = jnp.zeros_like(r.spill)
    r.grad_row[...] = jnp.zeros_like(r.grad_row)
    r.grad_col[...] = jnp.zeros_like(r.grad_col)

    def unit(step, carry):
        n, block = step // 2, lax.rem(step, 2)
        lanes = pl.ds(pl.multiple_of(block * pixels, pixels), pixels)
        base = block * (BLOCK_ROWS * cols)
        grad_in = r.turned[:, pl.ds(pl.multiple_of(step * pixels, pixels), pixels)]
        for group in range(3):
            first, start, stop = tap_span(group, cols)
            cells = pl.ds(pl.multiple_of(base + start, 128), stop - start)
            for j in range(3):
                tap = 3 * group + j
                spot = slice(j * pixels, (j + 1) * pixels)
                row_w, row_s, col_w, col_s = tap_weights(
                    tap, block, cols, r.up, r.left, r.fr, r.fc, n, lanes
                )
                write_table(r.table, j * pixels, row_w, col_w, group, cols)
                grad = jnp.dot(
                    r.w_deform[tap * width : (tap + 1) * width, :],
                    grad_in,
                    preferred_element_type=F32,
                ).astype(BF16)
                r.grads[:, spot] = grad
                scores = jnp.dot(r.rim[n, cells, :], grad, preferred_element_type=F32)
                by_value = jnp.zeros((cols, pixels), F32)
                by_slope = jnp.zeros((cols, pixels), F32)
                for k in range(first, first + SPAN):
                    line = scores[k * cols - start : (k + 1) * cols - start]
                    by_value = by_value + line * row_w[k : k + 1, :]
                    by_slope = by_slope + line * row_s[k : k + 1, :]
                r.grad_row[n, tap : tap + 1, lanes] = jnp.sum(
                    by_slope * col_w, axis=0, keepdims=True
                )
                r.grad_col[n, tap : tap + 1, lanes] = jnp.sum(
                    by_value * col_s, axis=0, keepdims=True
                )
            r.spill[n, cells, :] += lax.dot_general(
                r.table[start:stop, :],
                r.grads[...],
                (((1,), (1,)), ((), ())),
                preferred_element_type=F32,
            )
            for turn_at in range(4):
                if 3 * turn_at + group in plan:

                    @pl.when(step == turn_at)
                    def _(slot=3 * turn_at + group):
                        plan[slot]()

        return carry

    lax.fori_loop(0, 4, unit, 0)


def select_cells(r, cols):
    off = HALF * lax.axis_index(COL)
    cells = r.select.shape[1]

    def fill(i, carry):
        ids = lax.broadcasted_iota(jnp.int32, (STEP, cells), 1)
        pixel = lax.broadcasted_iota(jnp.int32, (STEP, cells), 0)
        hit = ids == pixel + (i + PAD) * cols + off
        r.select[pl.ds(pl.multiple_of(i * STEP, STEP), STEP), :] = jnp.where(hit, 1.0, 0.0).astype(
            BF16
        )
        return carry

    lax.fori_loop(0, r.select.shape[0] // STEP, fill, 0)


def unoffset(r):
    images, cells, width = r.rim.shape
    cols = r.table.shape[0] // WINDOW
    column = lax.rem(lax.broadcasted_iota(jnp.int32, (32, cells), 1), cols)
    for n in range(images):
        parts = []
        for grad, frac in ((r.grad_row, r.fr), (r.grad_col, r.fc)):
            f = frac[n]
            parts.append(grad[n] * f * (1.0 - f))
        go = jnp.concatenate(parts, axis=0).astype(BF16)
        on_tile = jnp.dot(go, r.select[...], preferred_element_type=F32)
        for tap in range(9):
            i, j = 2 * (tap // 3 - 1), 2 * (tap % 3 - 1)
            kept = on_tile
            if j < 0:
                kept = jnp.where(column >= -j, on_tile, 0.0)
            if j > 0:
                kept = jnp.where(column < cols - j, on_tile, 0.0)
            shift = (i * cols + j) % cells
            if shift:
                kept = pltpu.roll(kept, shift, axis=1)
            r.on_cells[32 * tap : 32 * tap + 32, :] = kept.astype(BF16)
        grad = jnp.dot(r.on_cells[...], r.rim[n], preferred_element_type=F32)
        if n == 0:
            r.gw_off_sum[...] = grad
        else:
            r.gw_off_sum[...] += grad
        for first in range(0, cells, 512):
            r.spill[n, first : first + 512, :] += lax.dot_general(
                r.on_cells[:, first : first + 512],
                r.w_off[...],
                (((0,), (0,)), ((), ())),
                preferred_element_type=F32,
            )
    for tap in range(9):
        put_lanes(r.gw_off, tap * width, r.gw_off_sum[32 * tap : 32 * tap + 32, :])


class Spill:
    @staticmethod
    def scratch(images, tile_rows, tile_cols, width):
        side = pltpu.VMEM((images, tile_rows + 2 * PAD, HALF, width), BF16)
        strip = pltpu.VMEM((images, REACH, tile_cols, width), BF16)
        sems = pltpu.SemaphoreType.DMA((3,))
        return [side, side, strip, strip, strip, strip, sems, sems]

    def __init__(self, spill, grad, cols, refs):
        self.spill, self.grad, self.cols = spill, grad, cols
        self.side_out, self.side_in, self.up_out, self.down_out, self.up_in, self.down_in = refs[:6]
        send, recv = refs[6:]
        self.row, self.rows, col, pair, above, below = halo_peers()
        self.images, self.all_rows = self.side_out.shape[:2]
        self.tile_rows, self.tile_cols = self.all_rows - 2 * PAD, self.up_out.shape[2]
        self.off, self.away, self.near = HALF * col, 2 * HALF * (1 - col), HALF * (1 - col)
        self.side = remote(self.side_out, self.side_in, send.at[0], recv.at[0], pair)
        self.up = remote(self.up_out, self.down_in, send.at[1], recv.at[1], above)
        self.down = remote(self.down_out, self.up_in, send.at[2], recv.at[2], below)

    def cells(self, k, first, count):
        return pl.ds(pl.multiple_of(k * self.cols + first, HALF), count)

    def start(self):
        def cast(k, carry):
            for n in range(self.images):
                self.side_out[n, k] = self.spill[n, self.cells(k, self.away, HALF), :].astype(BF16)
            return carry

        lax.fori_loop(0, self.all_rows, cast, 0)
        self.side.start()

    def edge(self, buffer, first):
        near = pl.ds(pl.multiple_of(self.near, HALF), HALF)

        def one(k, carry):
            for n in range(self.images):
                at = first + k
                buffer[n, k] = self.spill[n, self.cells(at, self.off, self.tile_cols), :].astype(BF16)
                part = self.spill[n, self.cells(at, HALF, HALF), :]
                buffer[n, k, near, :] = (part + self.side_in[n, at].astype(F32)).astype(BF16)
            return carry

        lax.fori_loop(0, REACH, one, 0)

    def middle(self):
        self.side.wait_recv()

        @pl.when(self.row > 0)
        def _():
            self.edge(self.up_out, PAD - REACH)
            self.up.start()

        @pl.when(self.row < self.rows - 1)
        def _():
            self.edge(self.down_out, PAD + self.tile_rows)
            self.down.start()

    def pixels(self, n, k, first, count):
        at = (n * self.tile_rows + k) * self.tile_cols + first
        return pl.ds(pl.multiple_of(at, HALF), count)

    def own(self):
        def fill(k, carry):
            for n in range(self.images):
                home = self.spill[n, self.cells(PAD + k, self.off, self.tile_cols), :]
                self.grad[self.pixels(n, k, 0, self.tile_cols), :] = home
                self.grad[self.pixels(n, k, self.near, HALF), :] += self.side_in[n, PAD + k].astype(F32)
            return carry

        lax.fori_loop(0, self.tile_rows, fill, 0)

    def finish(self):
        def arrive(buffer, first):
            def one(k, carry):
                for n in range(self.images):
                    at = self.pixels(n, first + k, 0, self.tile_cols)
                    self.grad[at, :] += buffer[n, k].astype(F32)
                return carry

            lax.fori_loop(0, REACH, one, 0)

        @pl.when(self.row > 0)
        def _():
            self.down.wait_recv()
            arrive(self.up_in, 0)
            self.up.wait_send()

        @pl.when(self.row < self.rows - 1)
        def _():
            self.up.wait_recv()
            arrive(self.down_in, self.tile_rows - REACH)
            self.down.wait_send()

        self.side.wait_send()


def backward_s(pixel_count, direct, r):
    signal_all()
    ex = Exchange(r.ex1)
    cols = r.table.shape[0] // WINDOW
    spill = Spill(r.spill, r.grad, cols, r.strips)
    wait_all()

    def nothing():
        pass

    first_jobs, second, third, plan = Jobs(), Jobs(), Jobs(), {}
    if direct:
        lines = Jobs()
        lines.add(
            *line_jobs(r.eighth_conv_b, r.sum_conv_b, r.line_conv_b),
            *line_jobs(r.eighth_expand_b, r.sum_expand_b, r.line_expand_b),
        )
        planes = Jobs()
        planes.add(
            *plane_jobs(r.src_reduce_b, r.eighth_reduce_b, r.plane_reduce_b),
            *plane_jobs(r.src_expand_a, r.eighth_expand_a, r.plane_expand_a),
        )
        deform = Jobs()
        deform.add(*plane_jobs(r.src_deform, r.eighth_deform, r.plane_deform))
        later = Jobs()
        later.add(
            *line_jobs(r.eighth_reduce_b, r.sum_reduce_b, r.line_reduce_b),
            *line_jobs(r.eighth_expand_a, r.sum_expand_a, r.line_expand_a),
        )
        r.ready(r.src_reduce_b, r.src_expand_a)
        planes.tick(4)
        r.ready(r.eighth_conv_b, r.eighth_expand_b)
        lines.tick(4)
        r.ready(r.src_deform)
        deform.tick(2)
        q1, q2, q3, q4 = planes.queue, lines.queue, deform.queue, later.queue
        slots = {
            2: q1[0:4],
            4: q3[0:2],
            7: q1[4:8] + q2[0:4],
            10: q1[8:12] + q4[0:4],
            11: q3[2:4] + q2[4:8],
        }

        def run(queue):
            def call():
                for step in queue:
                    step()

            return call

        plan = {slot: run(queue) for slot, queue in slots.items()}
        first_jobs.queue = q2[8:12]
        second.queue = q4[4:8]
        third.queue = q3[4:6] + q4[8:16]
    r.ready(r.gd, r.rim, r.w_deform)
    turn(r.gd, r.turned)
    unsample(r, plan)
    r.ready(r.w_off, r.select)
    unoffset(r)
    spill.start()
    r.push(r.gw_off)
    first_jobs.finish()
    spill.middle()
    spill.own()
    second.finish()
    r.ready(r.u_a1)
    spill.finish()
    sums = gelu_grad(r.grad, r.u_a1, r.norm_a1, r.mask)
    ex.put(*sums)
    third.tick(6)
    ex.middle_sums()
    ex.finish_sums()
    sums = put_sums(ex, r.sums_a1)
    norm_back(r.grad, r.u_a1, r.norm_a1, sums, pixel_count, r.mask, r.gr_a)
    third.finish()
    if direct:
        r.push(r.sum_conv_b, r.sum_expand_b, r.sum_reduce_b, r.sum_expand_a, r.eighth_deform)


def last(direct, r):
    signal_all()
    wait_all()
    jobs, plane = Jobs(), Jobs()
    if direct:
        r.ready(r.eighth_deform, r.gw_off)
        small = SmallSum(r.gw_off, r.sum_off, r.small)
        jobs.add(*line_jobs(r.eighth_deform, r.sum_deform, r.line_deform), small)
        jobs.tick(3)
    r.ready(r.gr_a, r.feature)
    turn(r.gr_a, r.turned)
    weight_product(r.turned, r.feature, r.gw_reduce)
    if direct:
        plane.add(*plane_jobs(r.gw_reduce, r.eighth_reduce_a, r.plane_reduce_a))
        plane.add(*line_jobs(r.eighth_reduce_a, r.sum_reduce_a, r.line_reduce_a))
    else:
        r.push(r.gw_reduce)
    plane.tick(2)
    r.ready(r.w_reduce, r.e_a3)

    def chunk(i, carry):
        rows = pl.ds(pl.multiple_of(i * CHUNK, CHUNK), CHUNK)
        for first in range(0, r.feature.shape[1], 512):
            lanes = slice(first, first + 512)
            grad = lax.dot_general(
                r.gr_a[rows, :],
                r.w_reduce[lanes, :],
                (((1,), (1,)), ((), ())),
                preferred_element_type=F32,
            )
            r.grad_in[rows, lanes] = (grad + r.e_a3[rows, lanes].astype(F32)).astype(BF16)
        return carry

    half = r.feature.shape[0] // CHUNK // 2
    lax.fori_loop(0, half, chunk, 0)
    plane.tick(2)
    lax.fori_loop(half, 2 * half, chunk, 0)
    r.push(r.grad_in)
    jobs.tick(3)
    plane.tick(2)
    jobs.tick(3)
    plane.tick(4)
    jobs.finish()
    plane.finish()
    if direct:
        r.push(r.sum_deform, r.sum_reduce_a)


def body(
    feature_in,
    orientation,
    offset_base,
    w_reduce_a,
    w_offset_a,
    w_deform_a,
    w_expand_a,
    scale_a,
    shift_a,
    w_reduce_b,
    w_conv_b,
    w_expand_b,
    scale_b,
    shift_b,
    cotangent,
):
    images, tile_rows, tile_cols, channels = feature_in.shape
    inner_width = w_reduce_a.shape[1]
    tile_pixels = tile_rows * tile_cols
    pixels = images * tile_pixels
    win_cols = tile_cols + HALF
    win_rows = tile_rows + 2 * PAD
    cells = win_rows * win_cols
    plane_count = 1.0 * images * LONG * SHORT
    pixel_count = plane_count * lax.axis_size(IMG)
    unbias = pixel_count / (pixel_count - 1.0)

    def array(*shape, dtype=BF16):
        return jax.ShapeDtypeStruct(shape, dtype)

    def table(width):
        return array(NORM_ROWS, width, dtype=F32)

    small = (pixels, inner_width)
    big = (pixels, channels)
    window_b = (images, tile_rows + 4, win_cols, inner_width)
    shifted = pltpu.VMEM((images, tile_rows + 4, tile_cols, 3 * inner_width), BF16)
    tile = pltpu.VMEM((images, tile_rows, tile_cols, inner_width), BF16)
    turned = pltpu.VMEM((inner_width, pixels), BF16)
    images_axis = lax.axis_size(IMG)
    direct = inner_width % (images_axis * 8 * 16) == 0
    cuts = images_axis if direct else 1
    feature = feature_in.reshape(big)
    scale_a, shift_a, scale_b, shift_b = (v[None] for v in (scale_a, shift_a, scale_b, shift_b))
    taps_shape = (images, 16, tile_pixels)
    start = fused(
        functools.partial(first, plane_count),
        FIRST_CID,
        ins=dict(
            base=offset_base.reshape(pixels, 18),
            w_offset=w_offset_a,
            scale=scale_a,
            shift=shift_a,
        ),
        smem=dict(orientation=orientation),
        staged=dict(feature=feature, w_reduce=w_reduce_a, w_deform=w_deform_a),
        outs=dict(
            mask=array(pixels, 128, dtype=F32),
            counts=array(16, 128, dtype=F32),
            up=array(*taps_shape, dtype=jnp.int32),
            left=array(*taps_shape, dtype=jnp.int32),
            w_off=array(288, inner_width),
            norm_a1=table(inner_width),
        ),
        pushed=dict(
            u_a1=array(*small, dtype=F32),
            rim=array(images, win_rows, win_cols, inner_width),
            select=array(tile_pixels, cells),
            w_turned=array(inner_width, 9 * inner_width),
        ),
        scratch=dict(ex1=Exchange.scratch(inner_width), halo=Halo.scratch, tile=tile),
    )
    mask, count_rows, norm_a1 = start.mask, start.counts, start.norm_a1
    rim_flat = start.rim.reshape(images, cells, inner_width)
    sampled = fused(
        functools.partial(sample, plane_count),
        SAMPLE_CID,
        ins=dict(
            mask=mask, counts=count_rows, up=start.up, left=start.left, scale=scale_a, shift=shift_a
        ),
        staged=dict(rim=rim_flat, select=start.select, w_off=start.w_off, w_turned=start.w_turned),
        outs=dict(norm_a2=table(inner_width)),
        pushed=dict(
            fr=array(*taps_shape, dtype=F32),
            fc=array(*taps_shape, dtype=F32),
            samples=array(9 * inner_width, pixels),
            u_a2=array(*small, dtype=F32),
        ),
        scratch=dict(
            ex2=Exchange.scratch(inner_width),
            rim_t=pltpu.VMEM((images, inner_width, cells), BF16),
            spread=pltpu.VMEM((288, cells), F32),
            table=pltpu.VMEM((WINDOW * win_cols, tile_pixels // 2), BF16),
        ),
    )
    norm_a2, deformed = sampled.norm_a2, sampled.u_a2
    fwd_a = fused(
        functools.partial(forward_a, plane_count),
        FORWARD_A_CID,
        ins=dict(
            norm_a2=norm_a2,
            mask=mask,
            counts=count_rows,
            scale_a=scale_a,
            shift_a=shift_a,
            scale_b=scale_b,
            shift_b=shift_b,
        ),
        staged=dict(u_a2=deformed, w_expand=w_expand_a, feature=feature, w_reduce=w_reduce_b),
        outs=dict(norm_a3=table(channels), norm_b1=table(inner_width)),
        pushed=dict(
            h2_a=array(*small),
            middle=array(*big),
            slope_a=array(*big),
            u_a3=array(*big),
            u_b1=array(*small, dtype=F32),
            rim_b=array(*window_b),
        ),
        scratch=dict(
            ex3=Exchange.scratch(channels),
            ex1=Exchange.scratch(inner_width),
            halo=Halo.scratch,
            wide=pltpu.VMEM(big, F32),
            tile=tile,
        ),
    )
    fwd_b = fused(
        functools.partial(forward_b, plane_count),
        FORWARD_B_CID,
        ins=dict(
            mask=mask,
            counts=count_rows,
            scale=scale_b,
            shift=shift_b,
        ),
        staged=dict(
            rim_b=fwd_a.rim_b,
            w_conv=w_conv_b,
            w_expand=w_expand_b,
            middle=fwd_a.middle,
            cotangent=cotangent.reshape(big),
        ),
        outs=dict(norm_b2=table(inner_width), norm_b3=table(channels), sums_b3=table(channels)),
        pushed=dict(
            u_b2=array(*small, dtype=F32),
            h2_b=array(*small),
            u_b3=array(*big),
            feature_out=array(*big),
            e_b3=array(*big),
        ),
        scratch=dict(
            ex2=Exchange.scratch(inner_width),
            ex3=Exchange.scratch(channels),
            ex4=Exchange.scratch(channels),
            wide=pltpu.VMEM(big, F32),
            shifted=shifted,
        ),
    )
    bwd_b = fused(
        functools.partial(backward_b, pixel_count),
        BACKWARD_B_CID,
        ins=dict(
            mask=mask,
            norm_b3=fwd_b.norm_b3,
            sums_b3=fwd_b.sums_b3,
            norm_b2=fwd_b.norm_b2,
            norm_b1=fwd_a.norm_b1,
        ),
        staged=dict(
            e_b3=fwd_b.e_b3,
            u_b3=fwd_b.u_b3,
            w_expand=w_expand_b,
            u_b2=fwd_b.u_b2,
            h2_b=fwd_b.h2_b,
            rim_b=fwd_a.rim_b,
            w_conv=w_conv_b,
            u_b1=fwd_a.u_b1,
        ),
        outs=dict(gro_b=array(*small), sums_b2=table(inner_width), sums_b1=table(inner_width)),
        pushed=dict(
            gw_expand=array(1, inner_width, channels),
            gw_conv=array(cuts, inner_width, 9 * inner_width // cuts),
        ),
        scratch=dict(
            ex2=Exchange.scratch(inner_width),
            ex1=Exchange.scratch(inner_width),
            halo=Halo.scratch,
            geo=pltpu.VMEM(big, BF16),
            grad=pltpu.VMEM(small, F32),
            tile=tile,
            turned=turned,
            back_rim=pltpu.VMEM(window_b, BF16),
            shifted=shifted,
            back_shifted=shifted,
        ),
    )

    def eighths(grad):
        return grad.reshape(images_axis, 8, -1, grad.shape[-1])

    def eighth_of(src):
        return array(images_axis, *src.shape[2:])

    def sum_of(src):
        return array(*src.shape[1:])

    def vmem(struct):
        return pltpu.VMEM(struct.shape, struct.dtype)

    staged_a, pushed_a, scratch_a = {}, {}, {}
    if direct:
        conv_b, expand_b = eighths(bwd_b.gw_conv), eighths(bwd_b.gw_expand)
        staged_a = dict(src_conv_b=conv_b, src_expand_b=expand_b)
        pushed_a = dict(eighth_conv_b=eighth_of(conv_b), eighth_expand_b=eighth_of(expand_b))
        scratch_a = dict(
            plane_conv_b=Plane.scratch(conv_b.shape), plane_expand_b=Plane.scratch(expand_b.shape)
        )
    bwd_a = fused(
        functools.partial(backward_a, pixel_count, direct),
        BACKWARD_A_CID,
        ins=dict(mask=mask, norm_a3=fwd_a.norm_a3, norm_a2=norm_a2),
        staged=dict(
            **staged_a,
            gro_b=bwd_b.gro_b,
            w_reduce=w_reduce_b,
            e_b3=fwd_b.e_b3,
            slope_a=fwd_a.slope_a,
            u_a3=fwd_a.u_a3,
            middle=fwd_a.middle,
            w_expand=w_expand_a,
            u_a2=deformed,
            h2_a=fwd_a.h2_a,
        ),
        outs=dict(gd=array(*small), sums_a3=table(channels), sums_a2=table(inner_width)),
        pushed=dict(
            **pushed_a,
            gw_reduce=array(cuts, inner_width, channels // cuts),
            gw_expand=array(1, inner_width, channels),
            e_a3=array(*big),
        ),
        scratch=dict(
            **scratch_a,
            ex3=Exchange.scratch(channels),
            ex2=Exchange.scratch(inner_width),
            wide=pltpu.VMEM(big, F32),
            grad=pltpu.VMEM(small, F32),
            turned=turned,
        ),
    )
    gw_deform = jnp.dot(sampled.samples, bwd_a.gd, preferred_element_type=F32).astype(BF16)
    staged_s, pushed_s, scratch_s = {}, {}, {}
    if direct:
        reduce_b, expand_a = eighths(bwd_a.gw_reduce), eighths(bwd_a.gw_expand)
        deform = eighths(gw_deform)
        staged_s = dict(
            eighth_conv_b=bwd_a.eighth_conv_b,
            eighth_expand_b=bwd_a.eighth_expand_b,
            src_reduce_b=reduce_b,
            src_expand_a=expand_a,
            src_deform=deform,
        )
        pushed_s = dict(
            sum_conv_b=sum_of(conv_b),
            sum_expand_b=sum_of(expand_b),
            sum_reduce_b=sum_of(reduce_b),
            sum_expand_a=sum_of(expand_a),
            eighth_deform=eighth_of(deform),
        )
        scratch_s = dict(
            line_conv_b=Line.scratch(bwd_a.eighth_conv_b.shape),
            line_expand_b=Line.scratch(bwd_a.eighth_expand_b.shape),
            plane_reduce_b=Plane.scratch(reduce_b.shape),
            plane_expand_a=Plane.scratch(expand_a.shape),
            plane_deform=Plane.scratch(deform.shape),
            eighth_reduce_b=vmem(eighth_of(reduce_b)),
            eighth_expand_a=vmem(eighth_of(expand_a)),
            line_reduce_b=Line.scratch(eighth_of(reduce_b).shape),
            line_expand_a=Line.scratch(eighth_of(expand_a).shape),
        )
    block = tile_pixels // 2
    bwd_s = fused(
        functools.partial(backward_s, pixel_count, direct),
        BACKWARD_S_CID,
        ins=dict(
            mask=mask,
            norm_a1=norm_a1,
            up=start.up,
            left=start.left,
            fr=sampled.fr,
            fc=sampled.fc,
        ),
        staged=dict(
            **staged_s,
            gd=bwd_a.gd,
            rim=rim_flat,
            w_deform=w_deform_a,
            w_off=start.w_off,
            select=start.select,
            u_a1=start.u_a1,
        ),
        outs=dict(gr_a=array(*small), sums_a1=table(inner_width)),
        pushed=dict(**pushed_s, gw_off=array(cuts, 32, 9 * inner_width // cuts)),
        scratch=dict(
            **scratch_s,
            ex1=Exchange.scratch(inner_width),
            strips=Spill.scratch(images, tile_rows, tile_cols, inner_width),
            spill=pltpu.VMEM((images, cells, inner_width), F32),
            table=pltpu.VMEM((WINDOW * win_cols, 3 * block), BF16),
            grads=pltpu.VMEM((inner_width, 3 * block), BF16),
            turned=turned,
            grad_row=pltpu.VMEM(taps_shape, F32),
            grad_col=pltpu.VMEM(taps_shape, F32),
            on_cells=pltpu.VMEM((288, cells), BF16),
            gw_off_sum=pltpu.VMEM((288, inner_width), F32),
            grad=pltpu.VMEM(small, F32),
        ),
    )
    staged_l, pushed_l, scratch_l = {}, {}, {}
    if direct:
        reduce_a = array(images_axis, 8, inner_width // 8, channels // cuts)
        staged_l = dict(eighth_deform=bwd_s.eighth_deform, gw_off=bwd_s.gw_off)
        pushed_l = dict(sum_deform=sum_of(deform), sum_reduce_a=sum_of(reduce_a))
        scratch_l = dict(
            gw_reduce=vmem(reduce_a),
            small=SmallSum.scratch(bwd_s.gw_off.shape),
            line_deform=Line.scratch(bwd_s.eighth_deform.shape),
            plane_reduce_a=Plane.scratch(reduce_a.shape),
            eighth_reduce_a=vmem(eighth_of(reduce_a)),
            line_reduce_a=Line.scratch(eighth_of(reduce_a).shape),
        )
        outs_l = dict(sum_off=array(*bwd_s.gw_off.shape[1:], dtype=F32))
    else:
        pushed_l = dict(gw_reduce=array(cuts, inner_width, channels // cuts))
        outs_l = {}
    end = fused(
        functools.partial(last, direct),
        LAST_CID,
        ins={},
        staged=dict(
            **staged_l, gr_a=bwd_s.gr_a, feature=feature, w_reduce=w_reduce_a, e_a3=bwd_a.e_a3
        ),
        outs=outs_l,
        pushed=dict(**pushed_l, grad_in=array(*big)),
        scratch=dict(**scratch_l, turned=turned),
    )
    sums_a = [bwd_s.sums_a1, bwd_a.sums_a2, bwd_a.sums_a3]
    sums_b = [bwd_b.sums_b1, bwd_b.sums_b2, fwd_b.sums_b3]
    norms_a = [norm_a1, norm_a2, fwd_a.norm_a3]
    norms_b = [fwd_a.norm_b1, fwd_b.norm_b2, fwd_b.norm_b3]
    if direct:
        sums = [
            bwd_s.sum_conv_b,
            bwd_s.sum_reduce_b,
            end.sum_reduce_a,
            bwd_s.sum_expand_b,
            bwd_s.sum_expand_a,
            end.sum_deform,
            end.sum_off,
        ]
    else:

        def over_devices(grad, dim):
            part = lax.psum_scatter(grad, IMG, scatter_dimension=dim, tiled=True)
            return lax.psum(part, (ROW, COL))

        turned_grads = (bwd_b.gw_conv, bwd_a.gw_reduce, end.gw_reduce)
        sums = [over_devices(g[0], 1) for g in turned_grads]
        sums += [over_devices(g[0], 0) for g in (bwd_b.gw_expand, bwd_a.gw_expand)]
        sums.append(over_devices(gw_deform, 0))
        sums = [g.reshape(8, -1, g.shape[1]) for g in sums]
        sums.append(over_devices(bwd_s.gw_off[0], 1).astype(F32))
    share = inner_width // images_axis
    long_share, wide_share = 9 * share, channels // images_axis
    shapes = [
        (long_share, inner_width),
        (wide_share, inner_width),
        (wide_share, inner_width),
        (share, channels),
        (share, channels),
        (long_share, inner_width),
        (long_share, 18),
    ]
    vectors = ((2 * inner_width + channels) // 128, 128)
    shapes += [vectors] * 8
    operands = sums + sums_a + sums_b + norms_a + norms_b
    results = pl.pallas_call(
        functools.partial(finish_kernel, unbias),
        out_shape=[array(*shape, dtype=F32) for shape in shapes],
        in_specs=[VMEM] * len(operands),
        out_specs=[VMEM] * len(shapes),
        compiler_params=pltpu.CompilerParams(vmem_limit_bytes=VMEM_LIMIT),
    )(*operands)
    conv_b, reduce_b, reduce_a, expand_b, expand_a, deform_a, offset_a = results[:7]
    scale_sums_a, shift_sums_a, scale_sums_b, shift_sums_b, mean_a, var_a, mean_b, var_b = (
        v.reshape(-1) for v in results[7:]
    )
    return (
        fwd_b.feature_out.reshape(feature_in.shape),
        end.grad_in.reshape(feature_in.shape),
        reduce_a,
        offset_a,
        deform_a,
        expand_a,
        scale_sums_a,
        shift_sums_a,
        mean_a,
        var_a,
        reduce_b,
        conv_b,
        expand_b,
        scale_sums_b,
        shift_sums_b,
        mean_b,
        var_b,
    )


def solution(mesh):
    tiles = P(IMG, ROW, COL, None)
    in_specs = (tiles, P(IMG), tiles) + (P(),) * 11 + (tiles,)
    shares = P(IMG, None)
    out_specs = (tiles, tiles) + (shares,) * 4 + (P(),) * 4 + (shares,) * 3 + (P(),) * 4
    return jax.shard_map(body, mesh=mesh, in_specs=in_specs, out_specs=out_specs, check_vma=False)
```

```python
import functools
import types

import jax
import jax.numpy as jnp
import numpy as np
from jax import lax
from jax.experimental import pallas as pl
from jax.experimental.pallas import tpu as pltpu
from jax.sharding import PartitionSpec as P

LONG = 64
SHORT = 44
BOUND = 4
EPSILON = 1e-05
IMG, ROW, COL = "img", "row", "col"
MESH = pl.DeviceIdType.MESH
VMEM = pl.BlockSpec(memory_space=pltpu.VMEM)
VMEM_LIMIT = 60 * 1024 * 1024
F32 = jnp.float32
BF16 = jnp.bfloat16
REACH = BOUND + 3
PAD = 8
HALF = 16
FIRST_CID, FORWARD_A_CID, FORWARD_B_CID = 0, 1, 2
BACKWARD_B_CID, BACKWARD_A_CID, BACKWARD_S_CID, LAST_CID = 3, 4, 5, 6


def group_of(axes):
    sizes = [lax.axis_size(a) for a in axes]
    total = int(np.prod(sizes))
    place = lax.axis_index(axes[0])
    for axis, size in zip(axes[1:], sizes[1:]):
        place = place * size + lax.axis_index(axis)

    def device(step):
        spot = lax.rem(place + step, total)
        coords = {}
        for axis, size in zip(reversed(axes), reversed(sizes)):
            coords[axis] = lax.rem(spot, size)
            spot = spot // size
        return coords

    return place, total, device


PLANE = (ROW, COL)
LINE = (IMG,)


def gather_start(axes, slots, send_sem, recv_sem):
    _, total, device = group_of(axes)
    for step in range(1, total):
        pltpu.make_async_remote_copy(
            src_ref=slots.at[0],
            dst_ref=slots.at[step],
            send_sem=send_sem,
            recv_sem=recv_sem,
            device_id=device(step),
            device_id_type=MESH,
        ).start()


def gather_wait(axes, slots, sem):
    _, total, _ = group_of(axes)
    others = slots.at[pl.ds(1, total - 1)]
    pltpu.make_async_copy(others, others, sem).wait()


def in_order(axes, slots):
    place, total, _ = group_of(axes)
    return [slots[lax.rem(place - spot + total, total)] for spot in range(total)]


def halo_peers():
    row, rows, col = lax.axis_index(ROW), lax.axis_size(ROW), lax.axis_index(COL)
    return row, rows, col, {COL: 1 - col}, {ROW: row - 1}, {ROW: row + 1}


BLOCK_ROWS = 8
SPAN = 17
WINDOW = 3 * BLOCK_ROWS


def tap_span(group, cols):
    first = 2 + 2 * group
    start = first * cols // 128 * 128
    stop = -(-(first + SPAN) * cols // 128) * 128
    return first, start, stop


def tap_weights(tap, block, cols, up_ref, left_ref, fr_ref, fc_ref, image=0, lanes=slice(None)):
    up, left, fr, fc = (
        ref[image, tap : tap + 1, lanes] for ref in (up_ref, left_ref, fr_ref, fc_ref)
    )
    up = up - block * BLOCK_ROWS
    pixels = up.shape[1]

    def pair(size, at, frac):
        ids = lax.broadcasted_iota(jnp.int32, (size, pixels), 0)
        first, second = ids == at, ids == at + 1
        value = jnp.where(first, 1.0 - frac, jnp.where(second, frac, 0.0))
        slope = jnp.where(second, 1.0, jnp.where(first, -1.0, 0.0))
        return value, slope

    return pair(WINDOW, up, fr) + pair(cols, left, fc)


def write_table(table, lane, row_w, col_w, group, cols):
    first, start, stop = tap_span(group, cols)
    pixels = row_w.shape[1]
    low = start // cols
    high = -(-stop // cols)
    for r in range(low, min(high, WINDOW)):
        table[r * cols : (r + 1) * cols, lane : lane + pixels] = (
            row_w[r : r + 1, :] * col_w
        ).astype(BF16)


def build_shifted(rim_ref, shifted):
    images, rows, cols, width = rim_ref.shape
    col = lax.axis_index(COL)
    tile = cols - HALF

    def fill(first):
        def one_row(k, carry):
            for n in range(images):
                line = rim_ref[n, k].astype(F32)
                none = jnp.zeros((2, width), F32)
                for d in range(3):
                    at = first + 2 * (d - 1)
                    if at < 0:
                        part = jnp.concatenate([none, line[: tile - 2]], axis=0)
                    elif at + tile > cols:
                        part = jnp.concatenate([line[at:], none], axis=0)
                    else:
                        part = line[at : at + tile]
                    shifted[n, k, :, d * width : (d + 1) * width] = part.astype(BF16)
            return carry

        lax.fori_loop(0, rows, one_row, 0)

    @pl.when(col == 0)
    def _():
        fill(0)

    @pl.when(col == 1)
    def _():
        fill(HALF)


def conv_product(shifted, w_ref, o_ref):
    images, rows, cols, width3 = shifted.shape
    tile_rows = rows - 4
    pixels = tile_rows * cols
    for n in range(images):
        total = None
        for i in range(3):
            taps = shifted[n, 2 * i : 2 * i + tile_rows].reshape(pixels, width3)
            term = jnp.dot(taps, w_ref[i * width3 : (i + 1) * width3, :], preferred_element_type=F32)
            total = term if total is None else total + term
        o_ref[n * pixels : (n + 1) * pixels, :] = total


def conv_weight_product(turned, shifted, gw_ref, i):
    images, rows, cols, width3 = shifted.shape
    tile_rows = rows - 4
    pixels = tile_rows * cols
    total = None
    for n in range(images):
        taps = shifted[n, 2 * i : 2 * i + tile_rows].reshape(pixels, width3)
        term = jnp.dot(turned[:, n * pixels : (n + 1) * pixels], taps, preferred_element_type=F32)
        total = term if total is None else total + term
    put_lanes(gw_ref, i * width3, total)


def unconv_product(shifted, w_ref, o_ref):
    images, rows, cols, width3 = shifted.shape
    width = width3 // 3
    tile_rows = rows - 4
    pixels = tile_rows * cols
    for n in range(images):
        total = None
        for tap in range(9):
            i, d = 2 - tap // 3, 2 - tap % 3
            grads = shifted[n, 2 * i : 2 * i + tile_rows, :, d * width : (d + 1) * width]
            term = lax.dot_general(
                grads.reshape(pixels, width),
                w_ref[tap * width : (tap + 1) * width, :],
                (((1,), (1,)), ((), ())),
                preferred_element_type=F32,
            )
            total = term if total is None else total + term
        o_ref[n * pixels : (n + 1) * pixels, :] = total


def halves(width):
    first = -(-width // 256) * 128
    return ((0, first), (first, width - first)) if first < width else ((0, width),)


def remote(src, dst, send, recv, device):
    return pltpu.make_async_remote_copy(
        src_ref=src, dst_ref=dst, send_sem=send, recv_sem=recv, device_id=device, device_id_type=MESH
    )


def arrival(ref, sem):
    return pltpu.make_async_copy(ref, ref, sem)


class Plane:
    @staticmethod
    def scratch(shape):
        images, _, rows, width = shape
        count = len(halves(width))
        return [
            pltpu.VMEM((images, 4, rows, width), BF16),
            pltpu.VMEM((images, 2, rows, width), BF16),
            pltpu.SemaphoreType.DMA((count, 3)),
            pltpu.SemaphoreType.DMA((count, 3)),
        ]

    def __init__(self, src, eighth, refs, part):
        half, quarter, send, recv = refs
        lanes = pl.ds(*halves(src.shape[-1])[part])
        self.src, self.half, self.quarter = (
            ref.at[:, :, :, lanes] for ref in (src, half, quarter)
        )
        self.eighth = eighth.at[:, :, lanes]
        self.images = src.shape[0]
        self.send, self.recv = [send.at[part, k] for k in range(3)], [recv.at[part, k] for k in range(3)]
        self.x_first = part == 0
        row, col = lax.axis_index(ROW), lax.axis_index(COL)
        bits = (lax.rem(row, 2), row // 2)
        peers = ({ROW: row + 1 - 2 * bits[0]}, {ROW: row + 2 - 4 * bits[1]})
        order = (0, 1) if self.x_first else (1, 0)
        self.a, self.b = (bits[k] for k in order)
        self.first, self.second = (peers[k] for k in order)
        self.mine, self.pair, self.other = 4 * col, {COL: 1 - col}, 4 * (1 - col)

    def spot(self, bit, free):
        return bit + 2 * free if self.x_first else 2 * bit + free

    def steps(self):
        return [self.to_pair, self.to_first, self.to_second, self.done]

    def to_pair(self):
        src = self.src.at[:, pl.ds(self.other, 4)]
        remote(src, self.half, self.send[0], self.recv[0], self.pair).start()

    def to_first(self):
        arrival(self.half, self.recv[0]).wait()

        def add(i, carry):
            for s in range(4):
                own = self.src[i, self.mine + s].astype(F32)
                self.half[i, s] = (own + self.half[i, s].astype(F32)).astype(BF16)
            return carry

        lax.fori_loop(0, self.images, add, 0)
        for k in range(2):
            src = self.half.at[:, self.spot(1 - self.a, k)]
            remote(src, self.quarter.at[:, k], self.send[1], self.recv[1], self.first).start()

    def to_second(self):
        arrival(self.quarter, self.recv[1]).wait()

        def add(i, carry):
            for k in range(2):
                own = self.half[i, self.spot(self.a, k)].astype(F32)
                self.quarter[i, k] = (own + self.quarter[i, k].astype(F32)).astype(BF16)
            return carry

        lax.fori_loop(0, self.images, add, 0)
        src = self.quarter.at[:, 1 - self.b]
        remote(src, self.eighth, self.send[2], self.recv[2], self.second).start()

    def done(self):
        arrival(self.eighth, self.recv[2]).wait()

        def add(i, carry):
            own = self.quarter[i, self.b].astype(F32)
            self.eighth[i] = (own + self.eighth[i].astype(F32)).astype(BF16)
            return carry

        lax.fori_loop(0, self.images, add, 0)
        arrival(self.half, self.send[0]).wait()
        arrival(self.quarter, self.send[1]).wait()
        arrival(self.eighth, self.send[2]).wait()


class Line:
    @staticmethod
    def scratch(shape):
        images, rows, width = shape
        count = len(halves(width))
        return [
            pltpu.VMEM(shape, BF16),
            pltpu.SemaphoreType.DMA((count, 3)),
            pltpu.SemaphoreType.DMA((count, 3)),
        ]

    def __init__(self, eighth, out, refs, part):
        line, send, recv = refs
        lanes = pl.ds(*halves(eighth.shape[-1])[part])
        self.eighth, self.line, self.out = (ref.at[:, :, lanes] for ref in (eighth, line, out))
        self.images = eighth.shape[0]
        self.send, self.recv = [send.at[part, k] for k in range(3)], [recv.at[part, k] for k in range(3)]
        self.img, self.row, col = (lax.axis_index(a) for a in (IMG, ROW, COL))
        self.mine, self.pair = 4 * col, {COL: 1 - col}

    def steps(self):
        return [self.to_line, self.to_rows, self.to_pair, self.done]

    def arrived(self):
        return self.line.at[pl.ds(1, self.images - 1)]

    def to_line(self):
        for j in range(1, self.images):
            there = lax.rem(self.img + j, self.images)
            src = self.eighth.at[there]
            remote(src, self.line.at[j], self.send[0], self.recv[0], {IMG: there}).start()

    def to_rows(self):
        arrival(self.arrived(), self.recv[0]).wait()
        total = self.eighth[self.img].astype(F32)
        for j in range(1, self.images):
            total = total + self.line[j].astype(F32)
        spot = self.out.at[self.mine + self.row]
        self.out[self.mine + self.row] = total.astype(BF16)
        for j in range(1, 4):
            there = lax.rem(self.row + j, 4)
            remote(spot, spot, self.send[1], self.recv[1], {ROW: there}).start()

    def to_pair(self):
        arrival(self.out.at[pl.ds(0, 3)], self.recv[1]).wait()
        four = self.out.at[pl.ds(self.mine, 4)]
        remote(four, four, self.send[2], self.recv[2], self.pair).start()

    def done(self):
        arrival(self.out.at[pl.ds(0, 4)], self.recv[2]).wait()
        arrival(self.arrived(), self.send[0]).wait()
        arrival(self.out.at[pl.ds(0, 3)], self.send[1]).wait()
        arrival(self.out.at[pl.ds(0, 4)], self.send[2]).wait()


class SmallSum:
    @staticmethod
    def scratch(shape):
        sizes = [lax.axis_size(IMG), lax.axis_size(ROW) * lax.axis_size(COL)]
        return [pltpu.VMEM((size,) + shape[1:], BF16) for size in sizes] + [
            pltpu.SemaphoreType.DMA((2,)),
            pltpu.SemaphoreType.DMA((2,)),
        ]

    def __init__(self, src, out, refs):
        self.src, self.out = src, out
        self.slots1, self.slots2, self.send, self.recv = refs

    def steps(self):
        return [self.to_line, self.to_plane, self.done]

    def to_line(self):
        here, total, _ = group_of(LINE)
        self.slots1[0] = self.src[here]
        for j in range(1, total):
            there = lax.rem(here + j, total)
            remote(
                self.src.at[there], self.slots1.at[j], self.send.at[0], self.recv.at[0], {IMG: there}
            ).start()

    def to_plane(self):
        gather_wait(LINE, self.slots1, self.recv.at[0])
        total = added([p.astype(F32) for p in in_order(LINE, self.slots1)])
        self.slots2[0] = total.astype(BF16)
        gather_start(PLANE, self.slots2, self.send.at[1], self.recv.at[1])

    def done(self):
        gather_wait(PLANE, self.slots2, self.recv.at[1])
        self.out[...] = added([p.astype(F32) for p in in_order(PLANE, self.slots2)])
        gather_wait(LINE, self.slots1, self.send.at[0])
        gather_wait(PLANE, self.slots2, self.send.at[1])


class Jobs:
    def __init__(self):
        self.queue = []

    def add(self, *jobs):
        lists = [job.steps() for job in jobs]
        for k in range(max(len(steps) for steps in lists)):
            self.queue += [steps[k] for steps in lists if k < len(steps)]

    def tick(self, count=1):
        for _ in range(min(count, len(self.queue))):
            self.queue.pop(0)()

    def finish(self):
        self.tick(len(self.queue))


def plane_jobs(src, eighth, refs):
    return [Plane(src, eighth, refs, part) for part in range(len(halves(src.shape[-1])))]


def line_jobs(eighth, out, refs):
    return [Line(eighth, out, refs, part) for part in range(len(halves(out.shape[-1])))]


STEP = 32
PIECE = 256
CHUNK = 256


class Refs:
    FLYING = 6 * 1024 * 1024

    def __init__(self):
        self.loads, self.stores, self.queue, self.flying = {}, {}, [], {}

    def load(self, ref, copy):
        self.loads[id(ref)] = copy
        self.queue.append((id(ref), int(np.prod(ref.shape)) * ref.dtype.itemsize))

    def start_loads(self, until=None):
        while self.queue:
            if until is None and sum(self.flying.values()) >= self.FLYING:
                return
            if until is not None and until in self.flying:
                return
            key, size = self.queue.pop(0)
            self.loads[key].start()
            self.flying[key] = size

    def ready(self, *refs):
        for ref in refs:
            self.start_loads(id(ref))
            self.loads.pop(id(ref)).wait()
            self.flying.pop(id(ref))
            self.start_loads()

    def push(self, *refs):
        for ref in refs:
            self.stores[id(ref)].start()

    def flush(self):
        for copy in self.stores.values():
            copy.wait()


def fused(work, cid, ins, staged, outs, pushed, scratch, smem={}, far={}):
    loaded, stored = {**ins, **staged}, {**outs, **pushed}
    sizes = (len(loaded), len(stored))

    def kernel(*refs):
        r = Refs()
        refs = list(refs)

        def take(count):
            taken = refs[:count]
            del refs[:count]
            return taken

        for key, ref in zip((*smem, *far), take(len(smem) + len(far))):
            setattr(r, key, ref)
        in_raw, out_raw = (take(count) for count in sizes)
        for key, shape in scratch.items():
            setattr(r, key, take(len(shape)) if isinstance(shape, list) else take(1)[0])
        in_bufs, out_bufs = (take(count) for count in sizes)
        in_sems, out_sems = take(2)
        for keys, bufs in ((loaded, in_bufs), (stored, out_bufs)):
            for key, buf in zip(keys, bufs):
                setattr(r, key, buf)
        for k, (raw, buf) in enumerate(zip(in_raw, in_bufs)):
            r.load(buf, pltpu.make_async_copy(raw, buf, in_sems.at[k]))
        for k, (raw, buf) in enumerate(zip(out_raw, out_bufs)):
            r.stores[id(buf)] = pltpu.make_async_copy(buf, raw, out_sems.at[k])
        r.start_loads()
        signal_all()
        r.ready(*in_bufs[: len(ins)])
        work(r)
        r.push(*out_bufs[: len(outs)])
        r.flush()

    flat = []
    for shape in scratch.values():
        flat += shape if isinstance(shape, list) else [shape]
    flat += [pltpu.VMEM(a.shape, a.dtype) for a in (*loaded.values(), *stored.values())]
    flat += [pltpu.SemaphoreType.DMA((count,)) for count in sizes]
    anywhere, scalars = pl.BlockSpec(memory_space=pl.ANY), pl.BlockSpec(memory_space=pltpu.SMEM)
    result = pl.pallas_call(
        kernel,
        out_shape=list(stored.values()),
        in_specs=[scalars] * len(smem) + [anywhere] * (len(far) + sizes[0]),
        out_specs=[anywhere] * sizes[1],
        scratch_shapes=flat,
        compiler_params=pltpu.CompilerParams(
            collective_id=cid, has_side_effects=True, vmem_limit_bytes=VMEM_LIMIT
        ),
    )(*smem.values(), *far.values(), *loaded.values())
    return types.SimpleNamespace(**dict(zip(stored, result)))


def signal_all():
    barrier = pltpu.get_barrier_semaphore()
    for axes in (PLANE, LINE):
        _, total, device = group_of(axes)
        for step in range(1, total):
            pl.semaphore_signal(barrier, inc=1, device_id=device(step), device_id_type=MESH)


def wait_all():
    count = sum(group_of(axes)[1] - 1 for axes in (PLANE, LINE))
    pl.semaphore_wait(pltpu.get_barrier_semaphore(), count)


def added(parts):
    return functools.reduce(lambda a, b: a + b, parts)


class Exchange:
    @staticmethod
    def scratch(width):
        rows = 2 * width // 128
        sizes = [int(np.prod([lax.axis_size(a) for a in axes])) for axes in (PLANE, LINE)]
        return [
            pltpu.VMEM((sizes[0], rows, 128), F32),
            pltpu.VMEM((sizes[1], rows, 128), F32),
            pltpu.VMEM((rows, 128), F32),
            pltpu.SemaphoreType.DMA((2,)),
            pltpu.SemaphoreType.DMA((2,)),
        ]

    def __init__(self, refs):
        self.slots1, self.slots2, self.out, self.send, self.recv = refs
        self.half = self.out.shape[0] // 2

    def put(self, first, second):
        for k in range(self.half):
            self.slots1[0, k : k + 1, :] = first[:, 128 * k : 128 * (k + 1)]
            self.slots1[0, self.half + k : self.half + k + 1, :] = second[:, 128 * k : 128 * (k + 1)]
        gather_start(PLANE, self.slots1, self.send.at[0], self.recv.at[0])

    def line(self):
        gather_start(LINE, self.slots2, self.send.at[1], self.recv.at[1])

    def middle_sums(self):
        gather_wait(PLANE, self.slots1, self.recv.at[0])
        self.slots2[0] = added(in_order(PLANE, self.slots1))
        self.line()

    def finish_sums(self):
        gather_wait(LINE, self.slots2, self.recv.at[1])
        self.out[...] = added(in_order(LINE, self.slots2))
        self.drain()

    def middle_stats(self, count_ref, plane_count):
        half = self.half
        gather_wait(PLANE, self.slots1, self.recv.at[0])
        parts = in_order(PLANE, self.slots1)
        total = added([p[:half] for p in parts])
        center = total / plane_count
        spread = added([p[half:] for p in parts])
        for spot, part in enumerate(parts):
            count = count_ref[spot : spot + 1, :]
            away = part[:half] / jnp.maximum(count, 1.0) - center
            spread = spread + count * (away * away)
        self.slots2[0, :half] = total
        self.slots2[0, half:] = spread
        self.line()

    def finish_stats(self, plane_count):
        half = self.half
        total_count = plane_count * lax.axis_size(IMG)
        gather_wait(LINE, self.slots2, self.recv.at[1])
        parts = in_order(LINE, self.slots2)
        center = added([p[:half] for p in parts]) / total_count
        spread = added([p[half:] for p in parts])
        for part in parts:
            away = part[:half] / plane_count - center
            spread = spread + plane_count * (away * away)
        self.out[:half] = center
        self.out[half:] = spread / total_count
        self.drain()

    def drain(self):
        gather_wait(PLANE, self.slots1, self.send.at[0])
        gather_wait(LINE, self.slots2, self.send.at[1])

    def rows(self):
        out = self.out[...]
        first = [out[k : k + 1] for k in range(self.half)]
        second = [out[self.half + k : self.half + k + 1] for k in range(self.half)]
        return jnp.concatenate(first, axis=1), jnp.concatenate(second, axis=1)


class Halo:
    scratch = [pltpu.SemaphoreType.DMA((5,)), pltpu.SemaphoreType.DMA((5,))]

    def __init__(self, pad, reach, tile, window, sems, image=None):
        if image is not None:
            tile, window = (ref.at[pl.ds(image, 1)] for ref in (tile, window))
        self.row, self.rows, col, pair, above, below = halo_peers()
        self.pad, self.reach, self.tile, self.window = pad, reach, tile, window
        self.tile_rows, self.tile_cols = tile.shape[1], tile.shape[2]
        self.own = own = pl.ds(pl.multiple_of(HALF * col, HALF), self.tile_cols)
        spot = pl.ds(pl.multiple_of(2 * HALF * col, HALF), HALF)
        side = pl.ds(pl.multiple_of(HALF * (1 - col), HALF), HALF)
        mid = pl.ds(HALF, HALF)
        upper = pl.ds(pad - reach, reach)
        lower = pl.ds(pad + self.tile_rows, reach)
        send, recv = sems

        def copy(src, dst, k, device):
            return pltpu.make_async_remote_copy(
                src_ref=src,
                dst_ref=dst,
                send_sem=send.at[k],
                recv_sem=recv.at[k],
                device_id=device,
                device_id_type=MESH,
            )

        w = window
        self.to_pair = copy(
            tile.at[:, :, side], w.at[:, pl.ds(pad, self.tile_rows), spot], 0, pair
        )
        self.up = copy(tile.at[:, pl.ds(0, reach)], w.at[:, lower, own], 1, above)
        self.down = copy(
            tile.at[:, pl.ds(self.tile_rows - reach, reach)], w.at[:, upper, own], 2, below
        )
        self.from_below = copy(w.at[:, lower, mid], w.at[:, lower, spot], 3, pair)
        self.from_above = copy(w.at[:, upper, mid], w.at[:, upper, spot], 4, pair)

    def blank(self):
        window, pad, reach, tile_rows = self.window, self.pad, self.reach, self.tile_rows
        zero = jnp.zeros((window.shape[0],) + window.shape[2:], window.dtype)

        def fill(first, last):
            for k in range(first, last):
                window[:, k] = zero

        fill(0, pad - reach)
        fill(pad + tile_rows + reach, 2 * pad + tile_rows)

        @pl.when(self.row == 0)
        def _():
            fill(pad - reach, pad)

        @pl.when(self.row == self.rows - 1)
        def _():
            fill(pad + tile_rows, pad + tile_rows + reach)

    def start(self):
        @pl.when(self.row > 0)
        def _():
            self.up.start()

        @pl.when(self.row < self.rows - 1)
        def _():
            self.down.start()

        self.to_pair.start()
        for n in range(self.tile.shape[0]):
            self.window[n, pl.ds(self.pad, self.tile_rows), self.own, :] = self.tile[n]

    def middle(self):
        @pl.when(self.row < self.rows - 1)
        def _():
            self.up.wait_recv()
            self.from_below.start()

        @pl.when(self.row > 0)
        def _():
            self.down.wait_recv()
            self.from_above.start()

    def finish(self):
        self.to_pair.wait()

        @pl.when(self.row < self.rows - 1)
        def _():
            self.down.wait_send()
            self.from_below.wait()

        @pl.when(self.row > 0)
        def _():
            self.up.wait_send()
            self.from_above.wait()


def gauss(x):
    bell = jnp.exp2(x * (x * -0.7213475204444817))
    d = 1.0 + (0.3275911 * 0.7071067811865476) * jnp.abs(x)
    t = pl.reciprocal(d, approx=True)
    t = t * (2.0 - d * t)
    poly = 0.5307027145 * t - 0.7265760135
    poly = poly * t + 0.7107068705
    poly = poly * t - 0.142248368
    poly = poly * t + 0.127414796
    tail = poly * (t * bell)
    return jnp.where(x < 0, tail, 1.0 - tail), bell * 0.3989422804014327


def wide(mask, width):
    return jnp.concatenate([mask] * (width // 128), axis=1)


def place(ref, i, lanes):
    if len(ref.shape) == 4:
        return (i // ref.shape[1], lax.rem(i, ref.shape[1]), slice(None), lanes)
    return (pl.ds(pl.multiple_of(i * STEP, STEP), STEP), lanes)


def by_rows(pixels, width, work, sums=0):
    pieces = [slice(l, l + PIECE) for l in range(0, width, PIECE)]

    def one(i, carry):
        out = []
        for k, lanes in enumerate(pieces):
            got = work(i, lanes)
            for j in range(sums):
                folded = jnp.sum(got[j].reshape(STEP // 8, 8, PIECE), axis=0)
                out.append(carry[k * sums + j] + folded)
        return tuple(out)

    start = tuple(jnp.zeros((8, PIECE), F32) for _ in range(sums * len(pieces)))
    final = lax.fori_loop(0, pixels // STEP, one, start)
    rows = []
    for j in range(sums):
        parts = [jnp.sum(final[k * sums + j], axis=0, keepdims=True) for k in range(len(pieces))]
        rows.append(jnp.concatenate(parts, axis=1))
    return rows


NORM_ROWS = 8


def norm_table(exchange, gain_ref, shift_ref, out_ref, first):
    mean, var = exchange.rows()
    lanes = slice(first, first + mean.shape[1])
    inv = lax.rsqrt(var + EPSILON)
    out_ref[...] = jnp.zeros_like(out_ref)
    out_ref[0:1, :] = mean
    out_ref[1:2, :] = inv
    out_ref[2:3, :] = inv * gain_ref[:, lanes]
    out_ref[3:4, :] = shift_ref[:, lanes]
    out_ref[4:5, :] = var


def normed(u_ref, norm, i, lanes):
    away = u_ref[place(u_ref, i, lanes)].astype(F32) - norm[0:1, lanes]
    return away * norm[2:3, lanes] + norm[3:4, lanes], away


def activate(u_ref, norm, mask, h_ref, residual=None, slope=None, keep=None):
    def work(i, lanes):
        x, _ = normed(u_ref, norm, i, lanes)
        if residual is not None:
            x = x + residual[place(residual, i, lanes)].astype(F32)
        below, bell = gauss(x)
        m = wide(mask[place(mask, i, slice(None))], PIECE)
        h_ref[place(h_ref, i, lanes)] = (x * below * m).astype(BF16)
        if slope is not None:
            slope[place(slope, i, lanes)] = ((below + x * bell) * m).astype(BF16)
        if keep is not None:
            keep[place(keep, i, lanes)] = u_ref[place(u_ref, i, lanes)].astype(BF16)

    by_rows(mask.shape[0], norm.shape[1], work)


def device_stats(u_ref, mask, count):
    pixels, width = u_ref.shape

    def total_of(i, lanes):
        m = wide(mask[place(mask, i, slice(None))], PIECE)
        return (u_ref[place(u_ref, i, lanes)] * m,)

    (total,) = by_rows(pixels, width, total_of, 1)
    center = total / jnp.maximum(wide(count, width), 1.0)

    def spread_of(i, lanes):
        m = wide(mask[place(mask, i, slice(None))], PIECE)
        away = u_ref[place(u_ref, i, lanes)] - center[:, lanes]
        return (away * away * m,)

    (spread,) = by_rows(pixels, width, spread_of, 1)
    return total, spread


def product(a_ref, w_ref, o_ref, turned=False):
    dims = (((1,), (1 if turned else 0,)), ((), ()))

    def one(i, carry):
        rows = pl.ds(pl.multiple_of(i * CHUNK, CHUNK), CHUNK)
        o_ref[rows, :] = lax.dot_general(
            a_ref[rows, :], w_ref[...], dims, preferred_element_type=F32
        )
        return carry

    lax.fori_loop(0, a_ref.shape[0] // CHUNK, one, 0)


def turn(a_ref, t_ref):
    def one(i, carry):
        rows = pl.ds(pl.multiple_of(i * CHUNK, CHUNK), CHUNK)
        t_ref[:, rows] = a_ref[rows, :].T
        return carry

    lax.fori_loop(0, a_ref.shape[0] // CHUNK, one, 0)


def put_lanes(ref, first, value):
    width = ref.shape[-1]
    at, stop = first, first + value.shape[1]
    while at < stop:
        cut = at // width
        until = min(stop, (cut + 1) * width)
        part = value[:, at - first : until - first].astype(ref.dtype)
        lanes = slice(at - cut * width, until - cut * width)
        if len(ref.shape) == 4:
            ref[cut, :, :, lanes] = part.reshape(ref.shape[1:3] + part.shape[1:])
        else:
            ref[cut, :, lanes] = part
        at = until


def weight_product(t_ref, b_ref, gw_ref):
    channels = b_ref.shape[1]
    for first in range(0, channels, 512):
        value = jnp.dot(t_ref[...], b_ref[:, first : first + 512], preferred_element_type=F32)
        if len(gw_ref.shape) == 4 and gw_ref.shape[-1] == channels:
            part = value.astype(gw_ref.dtype).reshape(gw_ref.shape[:3] + (512,))
            gw_ref[:, :, :, first : first + 512] = part
        else:
            put_lanes(gw_ref, first, value)


def put_rows(ref, first, value):
    if len(ref.shape) == 3:
        ref[0, first : first + value.shape[0], :] = value.astype(ref.dtype)
        return
    rows = ref.shape[2]
    at, stop = first, first + value.shape[0]
    while at < stop:
        eighth = at // rows
        until = min(stop, (eighth + 1) * rows)
        low, high = at - eighth * rows, until - eighth * rows
        part = value[at - first : until - first].astype(ref.dtype)
        ref[eighth // 8, eighth % 8, low:high, :] = part
        at = until


def norm_back(e_ref, u_ref, norm, sums, pixel_count, mask, out_ref):
    sum_grad, sum_unit = (s * (1.0 / pixel_count) for s in sums)

    def work(i, lanes):
        away = u_ref[place(u_ref, i, lanes)].astype(F32) - norm[0:1, lanes]
        unit = away * norm[1:2, lanes]
        e = e_ref[place(e_ref, i, lanes)].astype(F32)
        m = wide(mask[place(mask, i, slice(None))], PIECE)
        grad = norm[2:3, lanes] * (e - sum_grad[:, lanes] - unit * sum_unit[:, lanes]) * m
        out_ref[place(out_ref, i, lanes)] = grad.astype(BF16)

    by_rows(mask.shape[0], norm.shape[1], work)


def gelu_grad(e_ref, u_ref, norm, mask):
    def work(i, lanes):
        x, away = normed(u_ref, norm, i, lanes)
        below, bell = gauss(x)
        m = wide(mask[place(mask, i, slice(None))], PIECE)
        e = e_ref[place(e_ref, i, lanes)] * (below + x * bell) * m
        e_ref[place(e_ref, i, lanes)] = e
        return e, e * (away * norm[1:2, lanes])

    return by_rows(mask.shape[0], norm.shape[1], work, 2)


def put_sums(exchange, out_ref):
    first, second = exchange.rows()
    out_ref[...] = jnp.zeros_like(out_ref)
    out_ref[0:1, :] = first
    out_ref[1:2, :] = second
    return first, second


def order_taps(rows, width):
    to = lax.broadcasted_iota(jnp.int32, (rows, width), 0)
    at = lax.broadcasted_iota(jnp.int32, (rows, width), 1)
    picked = jnp.where(to < 16, 2 * to, 2 * (to - 16) + 1)
    real = lax.rem(to, 16) < 9
    return jnp.where(jnp.logical_and(at == picked, real), 1.0, 0.0)


def make_mask(r, tile_cols):
    row, col = lax.axis_index(ROW), lax.axis_index(COL)
    rows, cols = lax.axis_size(ROW), lax.axis_size(COL)
    images = r.orientation.shape[0]
    tile_rows = r.mask.shape[0] // images // tile_cols
    tall = [r.orientation[n].astype(F32) for n in range(images)]
    for n in range(images):

        def fill(i, carry, n=n):
            column = lax.broadcasted_iota(jnp.int32, (tile_cols, 128), 0) + col * tile_cols
            portrait = jnp.where(column < SHORT, 1.0, 0.0)
            line = jnp.zeros((tile_cols, 128), jnp.int32) + (row * tile_rows + i)
            landscape = jnp.where(line < SHORT, 1.0, 0.0)
            at = (n * tile_rows + i) * tile_cols
            r.mask[pl.ds(pl.multiple_of(at, tile_cols), tile_cols), :] = (
                landscape * (1.0 - tall[n]) + portrait * tall[n]
            )
            return carry

        lax.fori_loop(0, tile_rows, fill, 0)

    def count(row, col):
        return (
            jnp.clip(SHORT - row * tile_rows, 0, tile_rows) * tile_cols,
            jnp.clip(SHORT - col * tile_cols, 0, tile_cols) * tile_rows,
        )

    def fill_count(at, row, col):
        flat, upright = (c.astype(F32) for c in count(row, col))
        total = added([flat * (1.0 - t) + upright * t for t in tall])
        r.counts[at : at + 1, :] = jnp.zeros((1, 128), F32) + total

    r.counts[...] = jnp.zeros_like(r.counts)
    for k in range(rows * cols):
        fill_count(k, jnp.int32(k // cols), jnp.int32(k % cols))
    fill_count(8, row, col)


def make_corners(r, cols):
    images, _, pixels = r.up.shape
    tile_cols = cols - HALF
    order = order_taps(32, r.base.shape[1]).astype(BF16)
    tap = lax.broadcasted_iota(jnp.int32, (16, pixels), 0)
    pixel = lax.broadcasted_iota(jnp.int32, (16, pixels), 1)
    up0 = pixel // tile_cols + PAD + 2 * (tap // 3 - 1)
    left0 = lax.rem(pixel, tile_cols) + HALF * lax.axis_index(COL) + 2 * (lax.rem(tap, 3) - 1)
    for n in range(images):
        base = r.base[n * pixels : (n + 1) * pixels, :].astype(F32).astype(BF16)
        moved = lax.dot_general(
            order, base, (((1,), (1,)), ((), ())), preferred_element_type=F32
        ).astype(jnp.int32)
        r.up[n] = moved[:16] + up0
        r.left[n] = moved[16:] + left0


def first(plane_count, r):
    ex, ex2 = Exchange(r.ex1), Exchange(r.ex2)
    images, all_rows, cols, width = r.rim.shape
    halos = [Halo(PAD, REACH, r.tile, r.rim, r.halo[2 * n : 2 * n + 2], n) for n in range(images)]
    make_mask(r, cols - HALF)
    r.ready(r.feature, r.w_reduce)
    product(r.feature, r.w_reduce, r.u_a1)
    r.push(r.u_a1)
    total, spread = device_stats(r.u_a1, r.mask, r.counts[8:9, :])
    wait_all()
    ex.put(total, spread)
    make_corners(r, cols)
    ex.middle_stats(r.counts, plane_count)
    for halo in halos:
        halo.blank()
    order = order_taps(32, r.w_offset.shape[0]).astype(BF16)
    for tap in range(9):
        columns = r.w_offset[:, tap * width : (tap + 1) * width]
        r.w_off[32 * tap : 32 * tap + 32, :] = jnp.dot(
            order, columns, preferred_element_type=F32
        ).astype(BF16)
    ex.finish_stats(plane_count)
    norm_table(ex, r.scale, r.shift, r.norm_a1, 0)
    activate(r.u_a1, r.norm_a1, r.mask, r.tile)
    for halo in halos:
        halo.start()
    select_cells(r, cols)
    r.push(r.select)
    r.ready(r.w_deform)
    turn(r.w_deform, r.w_turned)
    for n, halo in enumerate(halos):
        if n == 0:
            halo.middle()
        halo.finish()
        for k in range(0, all_rows, 8):
            lines = r.rim[n, k : k + 8].reshape(8 * cols, width)
            r.rim_t[n, :, k * cols : (k + 8) * cols] = lines.T
        offset_fractions(r, cols, n)
        sample_units(r, cols, n, 0)
        if n + 1 < images:
            halos[n + 1].middle()
        sample_units(r, cols, n, 1)
    r.push(r.rim, r.fr, r.fc, r.samples, r.u_a2)
    total, spread = device_stats(r.u_a2, r.mask, r.counts[8:9, :])
    ex2.put(total, spread)
    ex2.middle_stats(r.counts, plane_count)
    ex2.finish_stats(plane_count)
    norm_table(ex2, r.scale, r.shift, r.norm_a2, width)


def offset_fractions(r, cols, n):
    _, width, cells = r.rim_t.shape
    column = lax.rem(lax.broadcasted_iota(jnp.int32, (32, cells), 1), cols)
    r.spread[...] = jnp.dot(r.w_off[...], r.rim_t[n], preferred_element_type=F32)
    total = None
    for tap in range(9):
        i, j = 2 * (tap // 3 - 1), 2 * (tap % 3 - 1)
        term = r.spread[32 * tap : 32 * tap + 32, :]
        shift = -(i * cols + j) % cells
        if shift:
            term = pltpu.roll(term, shift, axis=1)
        if j < 0:
            term = jnp.where(column >= -j, term, 0.0)
        if j > 0:
            term = jnp.where(column < cols - j, term, 0.0)
        total = term if total is None else total + term
    parts = []
    for _ in range(3):
        parts.append(total.astype(BF16))
        total = total - parts[-1].astype(F32)
    on_tile = lax.dot_general(
        jnp.concatenate(parts, axis=0),
        r.select[...],
        (((1,), (1,)), ((), ())),
        preferred_element_type=F32,
    )
    offsets = on_tile[:32] + on_tile[32:64] + on_tile[64:]
    fraction = 1.0 / (1.0 + jnp.exp(-offsets))
    r.fr[n] = fraction[:16]
    r.fc[n] = fraction[16:]


def sample_units(r, cols, n, b):
    block = r.table.shape[1]
    width = r.rim_t.shape[1]
    lanes = slice(b * block, (b + 1) * block)
    mine = slice((2 * n + b) * block, (2 * n + b + 1) * block)
    base = b * (BLOCK_ROWS * cols)
    for tap in range(9):
        row_w, _, col_w, _ = tap_weights(tap, b, cols, r.up, r.left, r.fr, r.fc, n, lanes)
        write_table(r.table, 0, row_w, col_w, tap // 3, cols)
        _, start, stop = tap_span(tap // 3, cols)
        cells = r.rim_t[n, :, base + start : base + stop]
        value = jnp.dot(cells, r.table[start:stop, :], preferred_element_type=F32)
        r.samples[tap * width : (tap + 1) * width, mine] = value.astype(BF16)
    deformed = jnp.dot(r.w_turned[...], r.samples[:, mine], preferred_element_type=F32)
    r.u_a2[mine, :] = deformed.T


def finish_kernel(unbias, *refs):
    conv_b, reduce_b, reduce_a, expand_b, expand_a, deform, off = refs[:7]
    tables, maps, outs, map_outs = refs[7:19], refs[19:21], refs[21:36], refs[36:38]
    bufs, sems = refs[38:40], refs[40]
    loads = [pltpu.make_async_copy(maps[k], bufs[k], sems.at[k]) for k in range(2)]
    stores = [pltpu.make_async_copy(bufs[k], map_outs[k], sems.at[2 + k]) for k in range(2)]
    for copy in loads:
        copy.start()
    for src, out in zip((conv_b, reduce_b, reduce_a), outs[:3]):
        eighth = src.shape[1]
        for s in range(0, 8, 2):
            rows = jnp.concatenate([src[s], src[s + 1]], axis=0).astype(F32)
            out[:, s * eighth : (s + 2) * eighth] = rows.T
    for load, store in zip(loads, stores):
        load.wait()
        store.start()
    for src, out in zip((expand_b, expand_a, deform), outs[3:6]):
        rows = src.shape[1]
        for s in range(8):
            out[s * rows : (s + 1) * rows, :] = src[s].astype(F32)
    rest, total = off[...], None
    order = order_taps(32, 18).astype(BF16)
    for _ in range(3):
        part = rest.astype(BF16)
        rest = rest - part.astype(F32)
        term = lax.dot_general(order, part, (((0,), (0,)), ((), ())), preferred_element_type=F32)
        total = term if total is None else total + term
    outs[6][...] = total
    for k in range(4):
        group, which = tables[3 * k : 3 * k + 3], outs[7 + 2 * k : 9 + 2 * k]
        norms = k >= 2
        for out, row in zip(which, (0, 4) if norms else (1, 0)):
            at = 0
            for table in group:
                for first_lane in range(0, table.shape[1], 128):
                    value = table[row : row + 1, first_lane : first_lane + 128]
                    out[at : at + 1, :] = value * unbias if norms and row == 4 else value
                    at += 1
    for copy in stores:
        copy.wait()


def forward_a(plane_count, r):
    ex3, ex1 = Exchange(r.ex3), Exchange(r.ex1)
    halo = Halo(2, 2, r.tile, r.rim_b, r.halo)
    halo.blank()
    r.ready(r.u_a2)
    activate(r.u_a2, r.norm_a2, r.mask, r.h2_a)
    r.push(r.h2_a)
    r.ready(r.w_expand)
    product(r.h2_a, r.w_expand, r.wide)
    count = r.counts[8:9, :]
    total, spread = device_stats(r.wide, r.mask, count)
    wait_all()
    ex3.put(total, spread)
    r.ready(r.feature, r.w_reduce)
    ex3.middle_stats(r.counts, plane_count)
    ex3.finish_stats(plane_count)
    norm_table(ex3, r.scale_a, r.shift_a, r.norm_a3, 2 * r.h2_a.shape[1])
    activate(r.wide, r.norm_a3, r.mask, r.middle, r.feature, r.slope_a, r.u_a3)
    r.push(r.middle, r.slope_a, r.u_a3)
    product(r.middle, r.w_reduce, r.u_b1)
    r.push(r.u_b1)
    total, spread = device_stats(r.u_b1, r.mask, count)
    ex1.put(total, spread)
    ex1.middle_stats(r.counts, plane_count)
    ex1.finish_stats(plane_count)
    norm_table(ex1, r.scale_b, r.shift_b, r.norm_b1, 0)
    activate(r.u_b1, r.norm_b1, r.mask, r.tile)
    halo.start()
    halo.middle()
    halo.finish()
    r.push(r.rim_b)


def forward_b(plane_count, r):
    ex2, ex3, ex4 = Exchange(r.ex2), Exchange(r.ex3), Exchange(r.ex4)
    count = r.counts[8:9, :]
    r.ready(r.rim_b)
    build_shifted(r.rim_b, r.shifted)
    r.ready(r.w_conv)
    conv_product(r.shifted, r.w_conv, r.u_b2)
    r.push(r.u_b2)
    total, spread = device_stats(r.u_b2, r.mask, count)
    wait_all()
    ex2.put(total, spread)
    ex2.middle_stats(r.counts, plane_count)
    ex2.finish_stats(plane_count)
    norm_table(ex2, r.scale, r.shift, r.norm_b2, r.h2_b.shape[1])
    activate(r.u_b2, r.norm_b2, r.mask, r.h2_b)
    r.push(r.h2_b)
    r.ready(r.w_expand)
    product(r.h2_b, r.w_expand, r.wide)
    total, spread = device_stats(r.wide, r.mask, count)
    ex3.put(total, spread)
    r.ready(r.middle, r.cotangent)
    ex3.middle_stats(r.counts, plane_count)
    ex3.finish_stats(plane_count)
    norm = r.norm_b3
    norm_table(ex3, r.scale, r.shift, norm, 2 * r.h2_b.shape[1])

    def work(i, lanes):
        x, away = normed(r.wide, norm, i, lanes)
        at = place(r.wide, i, lanes)
        r.u_b3[at] = r.wide[at].astype(BF16)
        x = x + r.middle[at].astype(F32)
        below, bell = gauss(x)
        m = wide(r.mask[place(r.mask, i, slice(None))], PIECE)
        r.feature_out[at] = (x * below * m).astype(BF16)
        e = (below + x * bell) * r.cotangent[at].astype(F32) * m
        r.e_b3[at] = e.astype(BF16)
        return e, e * (away * norm[1:2, lanes])

    sums = by_rows(r.wide.shape[0], r.wide.shape[1], work, 2)
    ex4.put(*sums)
    r.push(r.feature_out, r.e_b3, r.u_b3)
    ex4.middle_sums()
    ex4.finish_sums()
    put_sums(ex4, r.sums_b3)


def backward_b(pixel_count, direct, r):
    ex2, ex1 = Exchange(r.ex2), Exchange(r.ex1)
    halo = Halo(2, 2, r.tile, r.back_rim, r.halo)
    halo.blank()
    r.ready(r.e_b3, r.u_b3)
    sums = (r.sums_b3[0:1, :], r.sums_b3[1:2, :])
    norm_back(r.e_b3, r.u_b3, r.norm_b3, sums, pixel_count, r.mask, r.geo)
    r.ready(r.w_expand)
    product(r.geo, r.w_expand, r.grad, turned=True)
    r.ready(r.u_b2)
    sums = gelu_grad(r.grad, r.u_b2, r.norm_b2, r.mask)
    wait_all()
    ex2.put(*sums)
    r.ready(r.h2_b)
    turn(r.h2_b, r.turned)
    ex2.middle_sums()
    weight_product(r.turned, r.geo, r.gw_expand)
    jobs = Jobs()
    if direct:
        jobs.add(*plane_jobs(r.gw_expand, r.eighth_expand_b, r.plane_expand_b))
    else:
        r.push(r.gw_expand)
    jobs.tick(2)
    ex2.finish_sums()
    sums = put_sums(ex2, r.sums_b2)
    norm_back(r.grad, r.u_b2, r.norm_b2, sums, pixel_count, r.mask, r.tile)
    halo.start()
    tile_rows, tile_cols, width = r.tile.shape[1:]
    pixels = tile_rows * tile_cols
    for n in range(r.tile.shape[0]):
        for k in range(0, tile_rows, 8):
            at = n * pixels + k * tile_cols
            block = r.tile[n, k : k + 8].reshape(8 * tile_cols, width)
            r.turned[:, at : at + 8 * tile_cols] = block.T
    r.ready(r.rim_b)
    build_shifted(r.rim_b, r.shifted)
    conv_weight_product(r.turned, r.shifted, r.gw_conv, 0)
    halo.middle()
    jobs.tick(2)
    conv_weight_product(r.turned, r.shifted, r.gw_conv, 1)
    halo.finish()
    build_shifted(r.back_rim, r.back_shifted)
    r.ready(r.w_conv)
    unconv_product(r.back_shifted, r.w_conv, r.grad)
    r.ready(r.u_b1)
    sums = gelu_grad(r.grad, r.u_b1, r.norm_b1, r.mask)
    ex1.put(*sums)
    jobs.tick(2)
    ex1.middle_sums()
    conv_weight_product(r.turned, r.shifted, r.gw_conv, 2)
    r.push(r.gw_conv)
    jobs.finish()
    if direct:
        r.push(r.eighth_expand_b)
    ex1.finish_sums()
    sums = put_sums(ex1, r.sums_b1)
    norm_back(r.grad, r.u_b1, r.norm_b1, sums, pixel_count, r.mask, r.gro_b)


def backward_a(pixel_count, direct, r):
    ex3, ex2 = Exchange(r.ex3), Exchange(r.ex2)
    conv, line = Jobs(), Jobs()
    r.ready(r.gro_b, r.w_reduce)
    product(r.gro_b, r.w_reduce, r.wide, turned=True)
    wait_all()
    if direct:
        r.ready(r.src_conv_b, r.eighth_expand_b)
        conv.add(*plane_jobs(r.src_conv_b, r.eighth_conv_b, r.plane_conv_b))
        line.add(*line_jobs(r.eighth_expand_b, r.sum_expand_b, r.line_expand_b))
    conv.tick(2)
    line.tick(2)
    r.ready(r.e_b3, r.slope_a, r.u_a3)
    norm = r.norm_a3

    def work(i, lanes):
        at = place(r.wide, i, lanes)
        e = (r.wide[at] + r.e_b3[at].astype(F32)) * r.slope_a[at].astype(F32)
        r.e_a3[at] = e.astype(BF16)
        away = r.u_a3[at].astype(F32) - norm[0:1, lanes]
        return e, e * (away * norm[1:2, lanes])

    sums = by_rows(r.wide.shape[0], r.wide.shape[1], work, 2)
    ex3.put(*sums)
    conv.tick(2)
    r.push(r.e_a3)
    turn(r.gro_b, r.turned)
    ex3.middle_sums()
    r.ready(r.middle)
    weight_product(r.turned, r.middle, r.gw_reduce)
    r.push(r.gw_reduce)
    line.tick(2)
    ex3.finish_sums()
    sums = put_sums(ex3, r.sums_a3)
    norm_back(r.e_a3, r.u_a3, norm, sums, pixel_count, r.mask, r.e_b3)
    r.ready(r.w_expand)
    product(r.e_b3, r.w_expand, r.grad, turned=True)
    r.ready(r.u_a2)
    sums = gelu_grad(r.grad, r.u_a2, r.norm_a2, r.mask)
    ex2.put(*sums)
    conv.tick(2)
    line.tick(2)
    r.ready(r.h2_a)
    turn(r.h2_a, r.turned)
    ex2.middle_sums()
    weight_product(r.turned, r.e_b3, r.gw_expand)
    r.push(r.gw_expand)
    ex2.finish_sums()
    sums = put_sums(ex2, r.sums_a2)
    norm_back(r.grad, r.u_a2, r.norm_a2, sums, pixel_count, r.mask, r.gd)
    conv.finish()
    line.finish()
    if direct:
        r.push(r.eighth_conv_b, r.sum_expand_b)


def unsample(r, plan):
    width = r.rim.shape[2]
    cols = r.table.shape[0] // WINDOW
    pixels = r.up.shape[2] // 2
    r.spill[...] = jnp.zeros_like(r.spill)
    r.grad_row[...] = jnp.zeros_like(r.grad_row)
    r.grad_col[...] = jnp.zeros_like(r.grad_col)

    def unit(step, carry):
        n, block = step // 2, lax.rem(step, 2)
        lanes = pl.ds(pl.multiple_of(block * pixels, pixels), pixels)
        base = block * (BLOCK_ROWS * cols)
        grad_in = r.turned[:, pl.ds(pl.multiple_of(step * pixels, pixels), pixels)]
        for group in range(3):
            first, start, stop = tap_span(group, cols)
            cells = pl.ds(pl.multiple_of(base + start, 128), stop - start)
            for j in range(3):
                tap = 3 * group + j
                spot = slice(j * pixels, (j + 1) * pixels)
                row_w, row_s, col_w, col_s = tap_weights(
                    tap, block, cols, r.up, r.left, r.fr, r.fc, n, lanes
                )
                write_table(r.table, j * pixels, row_w, col_w, group, cols)
                grad = jnp.dot(
                    r.w_deform[tap * width : (tap + 1) * width, :],
                    grad_in,
                    preferred_element_type=F32,
                ).astype(BF16)
                r.grads[:, spot] = grad
                scores = jnp.dot(r.rim[n, cells, :], grad, preferred_element_type=F32)
                by_value = jnp.zeros((cols, pixels), F32)
                by_slope = jnp.zeros((cols, pixels), F32)
                for k in range(first, first + SPAN):
                    line = scores[k * cols - start : (k + 1) * cols - start]
                    by_value = by_value + line * row_w[k : k + 1, :]
                    by_slope = by_slope + line * row_s[k : k + 1, :]
                r.grad_row[n, tap : tap + 1, lanes] = jnp.sum(
                    by_slope * col_w, axis=0, keepdims=True
                )
                r.grad_col[n, tap : tap + 1, lanes] = jnp.sum(
                    by_value * col_s, axis=0, keepdims=True
                )
            r.spill[n, cells, :] += lax.dot_general(
                r.table[start:stop, :],
                r.grads[...],
                (((1,), (1,)), ((), ())),
                preferred_element_type=F32,
            )
            for turn_at in range(4):
                if 3 * turn_at + group in plan:

                    @pl.when(step == turn_at)
                    def _(slot=3 * turn_at + group):
                        plan[slot]()

        return carry

    lax.fori_loop(0, 4, unit, 0)


def select_cells(r, cols):
    off = HALF * lax.axis_index(COL)
    cells = r.select.shape[1]

    def fill(i, carry):
        ids = lax.broadcasted_iota(jnp.int32, (STEP, cells), 1)
        pixel = lax.broadcasted_iota(jnp.int32, (STEP, cells), 0)
        hit = ids == pixel + (i + PAD) * cols + off
        r.select[pl.ds(pl.multiple_of(i * STEP, STEP), STEP), :] = jnp.where(hit, 1.0, 0.0).astype(
            BF16
        )
        return carry

    lax.fori_loop(0, r.select.shape[0] // STEP, fill, 0)


def unoffset(r):
    images, cells, width = r.rim.shape
    cols = r.table.shape[0] // WINDOW
    column = lax.rem(lax.broadcasted_iota(jnp.int32, (32, cells), 1), cols)
    for n in range(images):
        parts = []
        for grad, frac in ((r.grad_row, r.fr), (r.grad_col, r.fc)):
            f = frac[n]
            parts.append(grad[n] * f * (1.0 - f))
        go = jnp.concatenate(parts, axis=0).astype(BF16)
        on_tile = jnp.dot(go, r.select[...], preferred_element_type=F32)
        for tap in range(9):
            i, j = 2 * (tap // 3 - 1), 2 * (tap % 3 - 1)
            kept = on_tile
            if j < 0:
                kept = jnp.where(column >= -j, on_tile, 0.0)
            if j > 0:
                kept = jnp.where(column < cols - j, on_tile, 0.0)
            shift = (i * cols + j) % cells
            if shift:
                kept = pltpu.roll(kept, shift, axis=1)
            r.on_cells[32 * tap : 32 * tap + 32, :] = kept.astype(BF16)
        grad = jnp.dot(r.on_cells[...], r.rim[n], preferred_element_type=F32)
        if n == 0:
            r.gw_off_sum[...] = grad
        else:
            r.gw_off_sum[...] += grad
        for first in range(0, cells, 512):
            r.spill[n, first : first + 512, :] += lax.dot_general(
                r.on_cells[:, first : first + 512],
                r.w_off[...],
                (((0,), (0,)), ((), ())),
                preferred_element_type=F32,
            )
    for tap in range(9):
        put_lanes(r.gw_off, tap * width, r.gw_off_sum[32 * tap : 32 * tap + 32, :])


class Spill:
    @staticmethod
    def scratch(images, tile_rows, tile_cols, width):
        side = pltpu.VMEM((images, tile_rows + 2 * PAD, HALF, width), BF16)
        strip = pltpu.VMEM((images, REACH, tile_cols, width), BF16)
        sems = pltpu.SemaphoreType.DMA((3,))
        return [side, side, strip, strip, strip, strip, sems, sems]

    def __init__(self, spill, grad, cols, refs):
        self.spill, self.grad, self.cols = spill, grad, cols
        self.side_out, self.side_in, self.up_out, self.down_out, self.up_in, self.down_in = refs[:6]
        send, recv = refs[6:]
        self.row, self.rows, col, pair, above, below = halo_peers()
        self.images, self.all_rows = self.side_out.shape[:2]
        self.tile_rows, self.tile_cols = self.all_rows - 2 * PAD, self.up_out.shape[2]
        self.off, self.away, self.near = HALF * col, 2 * HALF * (1 - col), HALF * (1 - col)
        self.side = remote(self.side_out, self.side_in, send.at[0], recv.at[0], pair)
        self.up = remote(self.up_out, self.down_in, send.at[1], recv.at[1], above)
        self.down = remote(self.down_out, self.up_in, send.at[2], recv.at[2], below)

    def cells(self, k, first, count):
        return pl.ds(pl.multiple_of(k * self.cols + first, HALF), count)

    def start(self):
        def cast(k, carry):
            for n in range(self.images):
                self.side_out[n, k] = self.spill[n, self.cells(k, self.away, HALF), :].astype(BF16)
            return carry

        lax.fori_loop(0, self.all_rows, cast, 0)
        self.side.start()

    def edge(self, buffer, first):
        near = pl.ds(pl.multiple_of(self.near, HALF), HALF)

        def one(k, carry):
            for n in range(self.images):
                at = first + k
                buffer[n, k] = self.spill[n, self.cells(at, self.off, self.tile_cols), :].astype(BF16)
                part = self.spill[n, self.cells(at, HALF, HALF), :]
                buffer[n, k, near, :] = (part + self.side_in[n, at].astype(F32)).astype(BF16)
            return carry

        lax.fori_loop(0, REACH, one, 0)

    def middle(self):
        self.side.wait_recv()

        @pl.when(self.row > 0)
        def _():
            self.edge(self.up_out, PAD - REACH)
            self.up.start()

        @pl.when(self.row < self.rows - 1)
        def _():
            self.edge(self.down_out, PAD + self.tile_rows)
            self.down.start()

    def pixels(self, n, k, first, count):
        at = (n * self.tile_rows + k) * self.tile_cols + first
        return pl.ds(pl.multiple_of(at, HALF), count)

    def own(self):
        def fill(k, carry):
            for n in range(self.images):
                home = self.spill[n, self.cells(PAD + k, self.off, self.tile_cols), :]
                self.grad[self.pixels(n, k, 0, self.tile_cols), :] = home
                self.grad[self.pixels(n, k, self.near, HALF), :] += self.side_in[n, PAD + k].astype(F32)
            return carry

        lax.fori_loop(0, self.tile_rows, fill, 0)

    def finish(self):
        def arrive(buffer, first):
            def one(k, carry):
                for n in range(self.images):
                    at = self.pixels(n, first + k, 0, self.tile_cols)
                    self.grad[at, :] += buffer[n, k].astype(F32)
                return carry

            lax.fori_loop(0, REACH, one, 0)

        @pl.when(self.row > 0)
        def _():
            self.down.wait_recv()
            arrive(self.up_in, 0)
            self.up.wait_send()

        @pl.when(self.row < self.rows - 1)
        def _():
            self.up.wait_recv()
            arrive(self.down_in, self.tile_rows - REACH)
            self.down.wait_send()

        self.side.wait_send()


def backward_s(pixel_count, direct, r):
    ex = Exchange(r.ex1)
    cols = r.table.shape[0] // WINDOW
    spill = Spill(r.spill, r.grad, cols, r.strips)

    mid, late, plan = Jobs(), Jobs(), {}
    r.ready(r.gd)
    deform_weight_product(r)
    wait_all()
    if direct:
        line, planes, deform = Jobs(), Jobs(), Jobs()
        line.add(*line_jobs(r.eighth_conv_b, r.sum_conv_b, r.line_conv_b))
        planes.add(
            *plane_jobs(r.src_reduce_b, r.eighth_reduce_b, r.plane_reduce_b),
            *plane_jobs(r.src_expand_a, r.eighth_expand_a, r.plane_expand_a),
        )
        deform.add(*plane_jobs(r.gw_deform, r.eighth_deform, r.plane_deform))
        r.ready(r.src_reduce_b, r.src_expand_a)
        planes.tick(4)
        r.ready(r.eighth_conv_b)
        line.tick(2)
        deform.tick(2)
        q1, q2, q3 = planes.queue, line.queue, deform.queue
        slots = {
            2: q1[0:4],
            5: q3[0:2],
            7: q1[4:8] + q2[0:2],
            10: q1[8:12] + q2[2:4],
            11: q3[2:4],
        }

        def run(queue):
            def call():
                for step in queue:
                    step()

            return call

        plan = {slot: run(queue) for slot, queue in slots.items()}
        mid.queue = q2[4:6]
        late.queue = q3[4:6]
    else:
        r.push(r.gw_deform)
    r.ready(r.w_deform, r.rim)
    turn(r.gd, r.turned)
    unsample(r, plan)
    r.ready(r.w_off, r.select)
    unoffset(r)
    spill.start()
    r.push(r.gw_off)
    mid.finish()
    spill.middle()
    spill.own()
    late.finish()
    if direct:
        r.push(r.sum_conv_b, r.eighth_reduce_b, r.eighth_expand_a, r.eighth_deform)
    r.ready(r.u_a1)
    spill.finish()
    sums = gelu_grad(r.grad, r.u_a1, r.norm_a1, r.mask)
    ex.put(*sums)
    ex.middle_sums()
    ex.finish_sums()
    sums = put_sums(ex, r.sums_a1)
    norm_back(r.grad, r.u_a1, r.norm_a1, sums, pixel_count, r.mask, r.gr_a)


def deform_weight_product(r):
    width = r.gd.shape[1]

    def load(tap):
        rows = pl.ds(tap * width, width)
        return pltpu.make_async_copy(
            r.samples.at[rows], r.sample_slots.at[tap % 2], r.sample_sems.at[tap % 2]
        )

    load(0).start()
    for tap in range(9):
        load(tap).wait()
        if tap < 8:
            load(tap + 1).start()
        value = jnp.dot(r.sample_slots[tap % 2], r.gd[...], preferred_element_type=F32)
        put_rows(r.gw_deform, tap * width, value)


def last(direct, r):
    jobs, plane = Jobs(), Jobs()
    r.ready(r.gr_a, r.feature)
    turn(r.gr_a, r.turned)
    weight_product(r.turned, r.feature, r.gw_reduce)
    wait_all()
    if direct:
        plane.add(*plane_jobs(r.gw_reduce, r.eighth_reduce_a, r.plane_reduce_a))
        plane.add(*line_jobs(r.eighth_reduce_a, r.sum_reduce_a, r.line_reduce_a))
    else:
        r.push(r.gw_reduce)
    plane.tick(2)
    if direct:
        r.ready(r.eighth_reduce_b, r.eighth_expand_a, r.eighth_deform, r.gw_off)
        jobs.add(
            *line_jobs(r.eighth_deform, r.sum_deform, r.line_deform),
            *line_jobs(r.eighth_reduce_b, r.sum_reduce_b, r.line_reduce_b),
            *line_jobs(r.eighth_expand_a, r.sum_expand_a, r.line_expand_a),
            SmallSum(r.gw_off, r.sum_off, r.small),
        )
    jobs.tick(7)
    r.ready(r.w_reduce, r.e_a3)

    def chunk(i, carry):
        rows = pl.ds(pl.multiple_of(i * CHUNK, CHUNK), CHUNK)
        for first in range(0, r.feature.shape[1], 512):
            lanes = slice(first, first + 512)
            grad = lax.dot_general(
                r.gr_a[rows, :],
                r.w_reduce[lanes, :],
                (((1,), (1,)), ((), ())),
                preferred_element_type=F32,
            )
            r.grad_in[rows, lanes] = (grad + r.e_a3[rows, lanes].astype(F32)).astype(BF16)
        return carry

    half = r.feature.shape[0] // CHUNK // 2
    lax.fori_loop(0, half, chunk, 0)
    plane.tick(2)
    lax.fori_loop(half, 2 * half, chunk, 0)
    r.push(r.grad_in)
    plane.tick(2)
    jobs.tick(7)
    plane.tick(4)
    jobs.tick(7)
    plane.tick(2)
    jobs.finish()
    if direct:
        r.push(r.sum_reduce_b, r.sum_expand_a, r.sum_deform)
    plane.finish()
    if direct:
        r.push(r.sum_reduce_a)


def body(
    feature_in,
    orientation,
    offset_base,
    w_reduce_a,
    w_offset_a,
    w_deform_a,
    w_expand_a,
    scale_a,
    shift_a,
    w_reduce_b,
    w_conv_b,
    w_expand_b,
    scale_b,
    shift_b,
    cotangent,
):
    images, tile_rows, tile_cols, channels = feature_in.shape
    inner_width = w_reduce_a.shape[1]
    tile_pixels = tile_rows * tile_cols
    pixels = images * tile_pixels
    win_cols = tile_cols + HALF
    win_rows = tile_rows + 2 * PAD
    cells = win_rows * win_cols
    plane_count = 1.0 * images * LONG * SHORT
    pixel_count = plane_count * lax.axis_size(IMG)
    unbias = pixel_count / (pixel_count - 1.0)

    def array(*shape, dtype=BF16):
        return jax.ShapeDtypeStruct(shape, dtype)

    def table(width):
        return array(NORM_ROWS, width, dtype=F32)

    small = (pixels, inner_width)
    big = (pixels, channels)
    window_b = (images, tile_rows + 4, win_cols, inner_width)
    shifted = pltpu.VMEM((images, tile_rows + 4, tile_cols, 3 * inner_width), BF16)
    tile = pltpu.VMEM((images, tile_rows, tile_cols, inner_width), BF16)
    turned = pltpu.VMEM((inner_width, pixels), BF16)
    images_axis = lax.axis_size(IMG)
    direct = inner_width % (images_axis * 8 * 16) == 0
    cuts = images_axis if direct else 1
    feature = feature_in.reshape(big)
    scale_a, shift_a, scale_b, shift_b = (v[None] for v in (scale_a, shift_a, scale_b, shift_b))
    taps_shape = (images, 16, tile_pixels)
    start = fused(
        functools.partial(first, plane_count),
        FIRST_CID,
        ins=dict(
            base=offset_base.reshape(pixels, 18),
            w_offset=w_offset_a.T,
            scale=scale_a,
            shift=shift_a,
        ),
        smem=dict(orientation=orientation),
        staged=dict(feature=feature, w_reduce=w_reduce_a, w_deform=w_deform_a),
        outs=dict(
            mask=array(pixels, 128, dtype=F32),
            counts=array(16, 128, dtype=F32),
            up=array(*taps_shape, dtype=jnp.int32),
            left=array(*taps_shape, dtype=jnp.int32),
            w_off=array(288, inner_width),
            norm_a1=table(inner_width),
            norm_a2=table(inner_width),
        ),
        pushed=dict(
            u_a1=array(*small, dtype=F32),
            rim=array(images, win_rows, win_cols, inner_width),
            select=array(tile_pixels, cells),
            fr=array(*taps_shape, dtype=F32),
            fc=array(*taps_shape, dtype=F32),
            samples=array(9 * inner_width, pixels),
            u_a2=array(*small, dtype=F32),
        ),
        scratch=dict(
            ex1=Exchange.scratch(inner_width),
            ex2=Exchange.scratch(inner_width),
            halo=Halo.scratch * images,
            tile=tile,
            w_turned=pltpu.VMEM((inner_width, 9 * inner_width), BF16),
            rim_t=pltpu.VMEM((images, inner_width, cells), BF16),
            spread=pltpu.VMEM((288, cells), F32),
            table=pltpu.VMEM((WINDOW * win_cols, tile_pixels // 2), BF16),
        ),
    )
    mask, count_rows, norm_a1 = start.mask, start.counts, start.norm_a1
    rim_flat = start.rim.reshape(images, cells, inner_width)
    norm_a2, deformed = start.norm_a2, start.u_a2
    fwd_a = fused(
        functools.partial(forward_a, plane_count),
        FORWARD_A_CID,
        ins=dict(
            norm_a2=norm_a2,
            mask=mask,
            counts=count_rows,
            scale_a=scale_a,
            shift_a=shift_a,
            scale_b=scale_b,
            shift_b=shift_b,
        ),
        staged=dict(u_a2=deformed, w_expand=w_expand_a, feature=feature, w_reduce=w_reduce_b),
        outs=dict(norm_a3=table(channels), norm_b1=table(inner_width)),
        pushed=dict(
            h2_a=array(*small),
            middle=array(*big),
            slope_a=array(*big),
            u_a3=array(*big),
            u_b1=array(*small, dtype=F32),
            rim_b=array(*window_b),
        ),
        scratch=dict(
            ex3=Exchange.scratch(channels),
            ex1=Exchange.scratch(inner_width),
            halo=Halo.scratch,
            wide=pltpu.VMEM(big, F32),
            tile=tile,
        ),
    )
    fwd_b = fused(
        functools.partial(forward_b, plane_count),
        FORWARD_B_CID,
        ins=dict(
            mask=mask,
            counts=count_rows,
            scale=scale_b,
            shift=shift_b,
        ),
        staged=dict(
            rim_b=fwd_a.rim_b,
            w_conv=w_conv_b,
            w_expand=w_expand_b,
            middle=fwd_a.middle,
            cotangent=cotangent.reshape(big),
        ),
        outs=dict(norm_b2=table(inner_width), norm_b3=table(channels), sums_b3=table(channels)),
        pushed=dict(
            u_b2=array(*small, dtype=F32),
            h2_b=array(*small),
            u_b3=array(*big),
            feature_out=array(*big),
            e_b3=array(*big),
        ),
        scratch=dict(
            ex2=Exchange.scratch(inner_width),
            ex3=Exchange.scratch(channels),
            ex4=Exchange.scratch(channels),
            wide=pltpu.VMEM(big, F32),
            shifted=shifted,
        ),
    )
    def eighths(grad):
        return grad.reshape(images_axis, 8, -1, grad.shape[-1])

    def eighth_of(src):
        return array(images_axis, *src.shape[2:])

    def sum_of(src):
        return array(*src.shape[1:])

    def vmem(struct):
        return pltpu.VMEM(struct.shape, struct.dtype)

    natural = array(1, inner_width, channels)
    pushed_b, scratch_b = dict(gw_expand=natural), {}
    if direct:
        expand_b = array(images_axis, 8, inner_width // images_axis // 8, channels)
        pushed_b = dict(eighth_expand_b=eighth_of(expand_b))
        scratch_b = dict(gw_expand=vmem(expand_b), plane_expand_b=Plane.scratch(expand_b.shape))
    bwd_b = fused(
        functools.partial(backward_b, pixel_count, direct),
        BACKWARD_B_CID,
        ins=dict(
            mask=mask,
            norm_b3=fwd_b.norm_b3,
            sums_b3=fwd_b.sums_b3,
            norm_b2=fwd_b.norm_b2,
            norm_b1=fwd_a.norm_b1,
        ),
        staged=dict(
            e_b3=fwd_b.e_b3,
            u_b3=fwd_b.u_b3,
            w_expand=w_expand_b,
            u_b2=fwd_b.u_b2,
            h2_b=fwd_b.h2_b,
            rim_b=fwd_a.rim_b,
            w_conv=w_conv_b,
            u_b1=fwd_a.u_b1,
        ),
        outs=dict(gro_b=array(*small), sums_b2=table(inner_width), sums_b1=table(inner_width)),
        pushed=dict(
            **pushed_b,
            gw_conv=array(cuts, inner_width, 9 * inner_width // cuts),
        ),
        scratch=dict(
            **scratch_b,
            ex2=Exchange.scratch(inner_width),
            ex1=Exchange.scratch(inner_width),
            halo=Halo.scratch,
            geo=pltpu.VMEM(big, BF16),
            grad=pltpu.VMEM(small, F32),
            tile=tile,
            turned=turned,
            back_rim=pltpu.VMEM(window_b, BF16),
            shifted=shifted,
            back_shifted=shifted,
        ),
    )

    staged_a, pushed_a, scratch_a = {}, {}, {}
    if direct:
        conv_b = eighths(bwd_b.gw_conv)
        staged_a = dict(src_conv_b=conv_b, eighth_expand_b=bwd_b.eighth_expand_b)
        pushed_a = dict(eighth_conv_b=eighth_of(conv_b), sum_expand_b=sum_of(expand_b))
        scratch_a = dict(
            plane_conv_b=Plane.scratch(conv_b.shape),
            line_expand_b=Line.scratch(bwd_b.eighth_expand_b.shape),
        )
    bwd_a = fused(
        functools.partial(backward_a, pixel_count, direct),
        BACKWARD_A_CID,
        ins=dict(mask=mask, norm_a3=fwd_a.norm_a3, norm_a2=norm_a2),
        staged=dict(
            gro_b=bwd_b.gro_b,
            w_reduce=w_reduce_b,
            **staged_a,
            e_b3=fwd_b.e_b3,
            slope_a=fwd_a.slope_a,
            u_a3=fwd_a.u_a3,
            middle=fwd_a.middle,
            w_expand=w_expand_a,
            u_a2=deformed,
            h2_a=fwd_a.h2_a,
        ),
        outs=dict(gd=array(*small), sums_a3=table(channels), sums_a2=table(inner_width)),
        pushed=dict(
            **pushed_a,
            gw_reduce=array(cuts, inner_width, channels // cuts),
            gw_expand=natural,
            e_a3=array(*big),
        ),
        scratch=dict(
            **scratch_a,
            ex3=Exchange.scratch(channels),
            ex2=Exchange.scratch(inner_width),
            wide=pltpu.VMEM(big, F32),
            grad=pltpu.VMEM(small, F32),
            turned=turned,
        ),
    )
    staged_s, scratch_s = {}, {}
    pushed_s = dict(gw_deform=array(1, 9 * inner_width, inner_width))
    if direct:
        reduce_b, expand_a = eighths(bwd_a.gw_reduce), eighths(bwd_a.gw_expand)
        deform = array(images_axis, 8, 9 * inner_width // images_axis // 8, inner_width)
        staged_s = dict(
            src_reduce_b=reduce_b,
            src_expand_a=expand_a,
            eighth_conv_b=bwd_a.eighth_conv_b,
        )
        pushed_s = dict(
            sum_conv_b=sum_of(conv_b),
            eighth_reduce_b=eighth_of(reduce_b),
            eighth_expand_a=eighth_of(expand_a),
            eighth_deform=eighth_of(deform),
        )
        scratch_s = dict(
            gw_deform=vmem(deform),
            line_conv_b=Line.scratch(bwd_a.eighth_conv_b.shape),
            plane_reduce_b=Plane.scratch(reduce_b.shape),
            plane_expand_a=Plane.scratch(expand_a.shape),
            plane_deform=Plane.scratch(deform.shape),
        )
    block = tile_pixels // 2
    bwd_s = fused(
        functools.partial(backward_s, pixel_count, direct),
        BACKWARD_S_CID,
        ins=dict(
            mask=mask,
            norm_a1=norm_a1,
            up=start.up,
            left=start.left,
            fr=start.fr,
            fc=start.fc,
        ),
        far=dict(samples=start.samples),
        staged=dict(
            gd=bwd_a.gd,
            **staged_s,
            w_deform=w_deform_a,
            rim=rim_flat,
            w_off=start.w_off,
            select=start.select,
            u_a1=start.u_a1,
        ),
        outs=dict(gr_a=array(*small), sums_a1=table(inner_width)),
        pushed=dict(**pushed_s, gw_off=array(cuts, 32, 9 * inner_width // cuts)),
        scratch=dict(
            **scratch_s,
            ex1=Exchange.scratch(inner_width),
            strips=Spill.scratch(images, tile_rows, tile_cols, inner_width),
            spill=pltpu.VMEM((images, cells, inner_width), F32),
            table=pltpu.VMEM((WINDOW * win_cols, 3 * block), BF16),
            grads=pltpu.VMEM((inner_width, 3 * block), BF16),
            turned=turned,
            grad_row=pltpu.VMEM(taps_shape, F32),
            grad_col=pltpu.VMEM(taps_shape, F32),
            on_cells=pltpu.VMEM((288, cells), BF16),
            gw_off_sum=pltpu.VMEM((288, inner_width), F32),
            sample_slots=pltpu.VMEM((2, inner_width, pixels), BF16),
            sample_sems=pltpu.SemaphoreType.DMA((2,)),
            grad=pltpu.VMEM(small, F32),
        ),
    )
    staged_l, pushed_l, scratch_l = {}, {}, {}
    if direct:
        reduce_a = array(images_axis, 8, inner_width // 8, channels // cuts)
        staged_l = dict(
            eighth_reduce_b=bwd_s.eighth_reduce_b,
            eighth_expand_a=bwd_s.eighth_expand_a,
            eighth_deform=bwd_s.eighth_deform,
            gw_off=bwd_s.gw_off,
        )
        pushed_l = dict(
            sum_reduce_b=sum_of(reduce_b),
            sum_expand_a=sum_of(expand_a),
            sum_deform=sum_of(deform),
            sum_reduce_a=sum_of(reduce_a),
        )
        scratch_l = dict(
            gw_reduce=vmem(reduce_a),
            small=SmallSum.scratch(bwd_s.gw_off.shape),
            line_reduce_b=Line.scratch(bwd_s.eighth_reduce_b.shape),
            line_expand_a=Line.scratch(bwd_s.eighth_expand_a.shape),
            line_deform=Line.scratch(bwd_s.eighth_deform.shape),
            plane_reduce_a=Plane.scratch(reduce_a.shape),
            eighth_reduce_a=vmem(eighth_of(reduce_a)),
            line_reduce_a=Line.scratch(eighth_of(reduce_a).shape),
        )
        outs_l = dict(sum_off=array(*bwd_s.gw_off.shape[1:], dtype=F32))
    else:
        pushed_l = dict(gw_reduce=array(cuts, inner_width, channels // cuts))
        outs_l = {}
    end = fused(
        functools.partial(last, direct),
        LAST_CID,
        ins={},
        staged=dict(
            gr_a=bwd_s.gr_a, feature=feature, **staged_l, w_reduce=w_reduce_a, e_a3=bwd_a.e_a3
        ),
        outs=outs_l,
        pushed=dict(**pushed_l, grad_in=array(*big)),
        scratch=dict(**scratch_l, turned=turned),
    )
    sums_a = [bwd_s.sums_a1, bwd_a.sums_a2, bwd_a.sums_a3]
    sums_b = [bwd_b.sums_b1, bwd_b.sums_b2, fwd_b.sums_b3]
    norms_a = [norm_a1, norm_a2, fwd_a.norm_a3]
    norms_b = [fwd_a.norm_b1, fwd_b.norm_b2, fwd_b.norm_b3]
    if direct:
        sums = [
            bwd_s.sum_conv_b,
            end.sum_reduce_b,
            end.sum_reduce_a,
            bwd_a.sum_expand_b,
            end.sum_expand_a,
            end.sum_deform,
            end.sum_off,
        ]
    else:

        def over_devices(grad, dim):
            part = lax.psum_scatter(grad, IMG, scatter_dimension=dim, tiled=True)
            return lax.psum(part, (ROW, COL))

        turned_grads = (bwd_b.gw_conv, bwd_a.gw_reduce, end.gw_reduce)
        sums = [over_devices(g[0], 1) for g in turned_grads]
        sums += [over_devices(g[0], 0) for g in (bwd_b.gw_expand, bwd_a.gw_expand)]
        sums.append(over_devices(bwd_s.gw_deform[0], 0))
        sums = [g.reshape(8, -1, g.shape[1]) for g in sums]
        sums.append(over_devices(bwd_s.gw_off[0], 1).astype(F32))
    share = inner_width // images_axis
    long_share, wide_share = 9 * share, channels // images_axis
    shapes = [
        (long_share, inner_width),
        (wide_share, inner_width),
        (wide_share, inner_width),
        (share, channels),
        (share, channels),
        (long_share, inner_width),
        (18, long_share),
    ]
    vectors = ((2 * inner_width + channels) // 128, 128)
    shapes += [vectors] * 8
    operands = sums + sums_a + sums_b + norms_a + norms_b
    results = pl.pallas_call(
        functools.partial(finish_kernel, unbias),
        out_shape=[array(*shape, dtype=F32) for shape in shapes] + [array(*big)] * 2,
        in_specs=[VMEM] * len(operands) + [pl.BlockSpec(memory_space=pl.ANY)] * 2,
        out_specs=[VMEM] * len(shapes) + [pl.BlockSpec(memory_space=pl.ANY)] * 2,
        scratch_shapes=[pltpu.VMEM(big, BF16)] * 2 + [pltpu.SemaphoreType.DMA((4,))],
        compiler_params=pltpu.CompilerParams(vmem_limit_bytes=VMEM_LIMIT),
    )(*operands, fwd_b.feature_out, end.grad_in)
    conv_b, reduce_b, reduce_a, expand_b, expand_a, deform_a, offset_a = results[:7]
    scale_sums_a, shift_sums_a, scale_sums_b, shift_sums_b, mean_a, var_a, mean_b, var_b = (
        v.reshape(-1) for v in results[7:15]
    )
    return (
        results[15].reshape(feature_in.shape),
        results[16].reshape(feature_in.shape),
        reduce_a,
        offset_a.T,
        deform_a,
        expand_a,
        scale_sums_a,
        shift_sums_a,
        mean_a,
        var_a,
        reduce_b,
        conv_b,
        expand_b,
        scale_sums_b,
        shift_sums_b,
        mean_b,
        var_b,
    )


def solution(mesh):
    tiles = P(IMG, ROW, COL, None)
    in_specs = (tiles, P(IMG), tiles) + (P(),) * 11 + (tiles,)
    shares = P(IMG, None)
    out_specs = (tiles, tiles) + (shares,) * 4 + (P(),) * 4 + (shares,) * 3 + (P(),) * 4
    return jax.shard_map(body, mesh=mesh, in_specs=in_specs, out_specs=out_specs, check_vma=False)
```

```python
import functools
import types

import jax
import jax.numpy as jnp
import numpy as np
from jax import lax
from jax.experimental import pallas as pl
from jax.experimental.pallas import tpu as pltpu
from jax.sharding import PartitionSpec as P

LONG = 64
SHORT = 44
BOUND = 4
EPSILON = 1e-05
IMG, ROW, COL = "img", "row", "col"
MESH = pl.DeviceIdType.MESH
VMEM = pl.BlockSpec(memory_space=pltpu.VMEM)
VMEM_LIMIT = 60 * 1024 * 1024
F32 = jnp.float32
BF16 = jnp.bfloat16
REACH = BOUND + 3
PAD = 8
HALF = 16
FIRST_CID, FORWARD_A_CID, FORWARD_B_CID = 0, 1, 2
BACKWARD_B_CID, BACKWARD_A_CID, BACKWARD_S_CID, LAST_CID = 3, 4, 5, 6


def group_of(axes):
    sizes = [lax.axis_size(a) for a in axes]
    total = int(np.prod(sizes))
    place = lax.axis_index(axes[0])
    for axis, size in zip(axes[1:], sizes[1:]):
        place = place * size + lax.axis_index(axis)

    def device(step):
        spot = lax.rem(place + step, total)
        coords = {}
        for axis, size in zip(reversed(axes), reversed(sizes)):
            coords[axis] = lax.rem(spot, size)
            spot = spot // size
        return coords

    return place, total, device


PLANE = (ROW, COL)
LINE = (IMG,)


def gather_start(axes, slots, send_sem, recv_sem):
    _, total, device = group_of(axes)
    for step in range(1, total):
        pltpu.make_async_remote_copy(
            src_ref=slots.at[0],
            dst_ref=slots.at[step],
            send_sem=send_sem,
            recv_sem=recv_sem,
            device_id=device(step),
            device_id_type=MESH,
        ).start()


def gather_wait(axes, slots, sem):
    _, total, _ = group_of(axes)
    others = slots.at[pl.ds(1, total - 1)]
    pltpu.make_async_copy(others, others, sem).wait()


def in_order(axes, slots):
    place, total, _ = group_of(axes)
    return [slots[lax.rem(place - spot + total, total)] for spot in range(total)]


def halo_peers():
    row, rows, col = lax.axis_index(ROW), lax.axis_size(ROW), lax.axis_index(COL)
    return row, rows, col, {COL: 1 - col}, {ROW: row - 1}, {ROW: row + 1}


BLOCK_ROWS = 8
SPAN = 17
WINDOW = 3 * BLOCK_ROWS


def tap_span(group, cols):
    first = 2 + 2 * group
    start = first * cols // 128 * 128
    stop = -(-(first + SPAN) * cols // 128) * 128
    return first, start, stop


def tap_weights(tap, block, cols, up_ref, left_ref, fr_ref, fc_ref, image=0, lanes=slice(None)):
    up, left, fr, fc = (
        ref[image, tap : tap + 1, lanes] for ref in (up_ref, left_ref, fr_ref, fc_ref)
    )
    up = up - block * BLOCK_ROWS
    pixels = up.shape[1]

    def pair(size, at, frac):
        ids = lax.broadcasted_iota(jnp.int32, (size, pixels), 0)
        first, second = ids == at, ids == at + 1
        value = jnp.where(first, 1.0 - frac, jnp.where(second, frac, 0.0))
        slope = jnp.where(second, 1.0, jnp.where(first, -1.0, 0.0))
        return value, slope

    return pair(WINDOW, up, fr) + pair(cols, left, fc)


def write_table(table, lane, row_w, col_w, group, cols):
    first, start, stop = tap_span(group, cols)
    pixels = row_w.shape[1]
    low = start // cols
    high = -(-stop // cols)
    for r in range(low, min(high, WINDOW)):
        table[r * cols : (r + 1) * cols, lane : lane + pixels] = (
            row_w[r : r + 1, :] * col_w
        ).astype(BF16)


def build_shifted(rim_ref, shifted):
    images, rows, cols, width = rim_ref.shape
    col = lax.axis_index(COL)
    tile = cols - HALF

    def fill(first):
        def one_row(k, carry):
            for n in range(images):
                line = rim_ref[n, k].astype(F32)
                none = jnp.zeros((2, width), F32)
                for d in range(3):
                    at = first + 2 * (d - 1)
                    if at < 0:
                        part = jnp.concatenate([none, line[: tile - 2]], axis=0)
                    elif at + tile > cols:
                        part = jnp.concatenate([line[at:], none], axis=0)
                    else:
                        part = line[at : at + tile]
                    shifted[n, k, :, d * width : (d + 1) * width] = part.astype(BF16)
            return carry

        lax.fori_loop(0, rows, one_row, 0)

    @pl.when(col == 0)
    def _():
        fill(0)

    @pl.when(col == 1)
    def _():
        fill(HALF)


def conv_product(shifted, w_ref, o_ref):
    images, rows, cols, width3 = shifted.shape
    tile_rows = rows - 4
    pixels = tile_rows * cols
    for n in range(images):
        total = None
        for i in range(3):
            taps = shifted[n, 2 * i : 2 * i + tile_rows].reshape(pixels, width3)
            term = jnp.dot(taps, w_ref[i * width3 : (i + 1) * width3, :], preferred_element_type=F32)
            total = term if total is None else total + term
        o_ref[n * pixels : (n + 1) * pixels, :] = total


def conv_weight_product(turned, shifted, gw_ref, i):
    images, rows, cols, width3 = shifted.shape
    tile_rows = rows - 4
    pixels = tile_rows * cols
    total = None
    for n in range(images):
        taps = shifted[n, 2 * i : 2 * i + tile_rows].reshape(pixels, width3)
        term = jnp.dot(turned[:, n * pixels : (n + 1) * pixels], taps, preferred_element_type=F32)
        total = term if total is None else total + term
    put_lanes(gw_ref, i * width3, total)


def unconv_product(shifted, w_ref, o_ref):
    images, rows, cols, width3 = shifted.shape
    width = width3 // 3
    tile_rows = rows - 4
    pixels = tile_rows * cols
    for n in range(images):
        total = None
        for tap in range(9):
            i, d = 2 - tap // 3, 2 - tap % 3
            grads = shifted[n, 2 * i : 2 * i + tile_rows, :, d * width : (d + 1) * width]
            term = lax.dot_general(
                grads.reshape(pixels, width),
                w_ref[tap * width : (tap + 1) * width, :],
                (((1,), (1,)), ((), ())),
                preferred_element_type=F32,
            )
            total = term if total is None else total + term
        o_ref[n * pixels : (n + 1) * pixels, :] = total


def halves(width):
    first = -(-width // 256) * 128
    return ((0, first), (first, width - first)) if first < width else ((0, width),)


def remote(src, dst, send, recv, device):
    return pltpu.make_async_remote_copy(
        src_ref=src, dst_ref=dst, send_sem=send, recv_sem=recv, device_id=device, device_id_type=MESH
    )


def arrival(ref, sem):
    return pltpu.make_async_copy(ref, ref, sem)


class Plane:
    @staticmethod
    def scratch(shape):
        images, _, rows, width = shape
        count = len(halves(width))
        return [
            pltpu.VMEM((images, 4, rows, width), BF16),
            pltpu.VMEM((images, 2, rows, width), BF16),
            pltpu.SemaphoreType.DMA((count, 3)),
            pltpu.SemaphoreType.DMA((count, 3)),
        ]

    def __init__(self, src, eighth, refs, part):
        half, quarter, send, recv = refs
        lanes = pl.ds(*halves(src.shape[-1])[part])
        self.src, self.half, self.quarter = (
            ref.at[:, :, :, lanes] for ref in (src, half, quarter)
        )
        self.eighth = eighth.at[:, :, lanes]
        self.images = src.shape[0]
        self.send, self.recv = [send.at[part, k] for k in range(3)], [recv.at[part, k] for k in range(3)]
        self.x_first = part == 0
        row, col = lax.axis_index(ROW), lax.axis_index(COL)
        bits = (lax.rem(row, 2), row // 2)
        peers = ({ROW: row + 1 - 2 * bits[0]}, {ROW: row + 2 - 4 * bits[1]})
        order = (0, 1) if self.x_first else (1, 0)
        self.a, self.b = (bits[k] for k in order)
        self.first, self.second = (peers[k] for k in order)
        self.mine, self.pair, self.other = 4 * col, {COL: 1 - col}, 4 * (1 - col)

    def spot(self, bit, free):
        return bit + 2 * free if self.x_first else 2 * bit + free

    def steps(self):
        return [self.to_pair, self.to_first, self.to_second, self.done]

    def to_pair(self):
        src = self.src.at[:, pl.ds(self.other, 4)]
        remote(src, self.half, self.send[0], self.recv[0], self.pair).start()

    def to_first(self):
        arrival(self.half, self.recv[0]).wait()

        def add(i, carry):
            for s in range(4):
                own = self.src[i, self.mine + s].astype(F32)
                self.half[i, s] = (own + self.half[i, s].astype(F32)).astype(BF16)
            return carry

        lax.fori_loop(0, self.images, add, 0)
        for k in range(2):
            src = self.half.at[:, self.spot(1 - self.a, k)]
            remote(src, self.quarter.at[:, k], self.send[1], self.recv[1], self.first).start()

    def to_second(self):
        arrival(self.quarter, self.recv[1]).wait()

        def add(i, carry):
            for k in range(2):
                own = self.half[i, self.spot(self.a, k)].astype(F32)
                self.quarter[i, k] = (own + self.quarter[i, k].astype(F32)).astype(BF16)
            return carry

        lax.fori_loop(0, self.images, add, 0)
        src = self.quarter.at[:, 1 - self.b]
        remote(src, self.eighth, self.send[2], self.recv[2], self.second).start()

    def done(self):
        arrival(self.eighth, self.recv[2]).wait()

        def add(i, carry):
            own = self.quarter[i, self.b].astype(F32)
            self.eighth[i] = (own + self.eighth[i].astype(F32)).astype(BF16)
            return carry

        lax.fori_loop(0, self.images, add, 0)
        arrival(self.half, self.send[0]).wait()
        arrival(self.quarter, self.send[1]).wait()
        arrival(self.eighth, self.send[2]).wait()


class LineSum:
    @staticmethod
    def scratch(shape):
        sems = pltpu.SemaphoreType.DMA((len(halves(shape[-1])),))
        return [pltpu.VMEM(shape, BF16), sems, sems]

    def __init__(self, eighth, own, refs, part):
        line, send, recv = refs
        lanes = pl.ds(*halves(eighth.shape[-1])[part])
        self.eighth, self.line, self.own = eighth.at[:, :, lanes], line.at[:, :, lanes], own.at[:, lanes]
        self.images, self.img = eighth.shape[0], lax.axis_index(IMG)
        self.send, self.recv = send.at[part], recv.at[part]

    def steps(self):
        return [self.to_line, self.done]

    def to_line(self):
        for j in range(1, self.images):
            there = lax.rem(self.img + j, self.images)
            src = self.eighth.at[there]
            remote(src, self.line.at[j], self.send, self.recv, {IMG: there}).start()

    def done(self):
        arrived = self.line.at[pl.ds(1, self.images - 1)]
        arrival(arrived, self.recv).wait()
        total = self.eighth[self.img].astype(F32)
        for j in range(1, self.images):
            total = total + self.line[j].astype(F32)
        self.own[...] = total.astype(BF16)
        arrival(arrived, self.send).wait()


class Gather:
    @staticmethod
    def scratch(shape):
        sems = pltpu.SemaphoreType.DMA((len(halves(shape[-1])), 2))
        return [sems, sems]

    def __init__(self, own, out, refs, part):
        send, recv = refs
        lanes = pl.ds(*halves(out.shape[-1])[part])
        self.own, self.out = own.at[:, lanes], out.at[:, :, lanes]
        self.send, self.recv = [send.at[part, k] for k in range(2)], [recv.at[part, k] for k in range(2)]
        self.row, col = lax.axis_index(ROW), lax.axis_index(COL)
        self.mine, self.pair = 4 * col, {COL: 1 - col}

    def steps(self):
        return [self.to_rows, self.to_pair, self.done]

    def to_rows(self):
        spot = self.out.at[self.mine + self.row]
        self.out[self.mine + self.row] = self.own[...]
        for j in range(1, 4):
            there = lax.rem(self.row + j, 4)
            remote(spot, spot, self.send[0], self.recv[0], {ROW: there}).start()

    def to_pair(self):
        arrival(self.out.at[pl.ds(0, 3)], self.recv[0]).wait()
        four = self.out.at[pl.ds(self.mine, 4)]
        remote(four, four, self.send[1], self.recv[1], self.pair).start()

    def done(self):
        four = self.out.at[pl.ds(0, 4)]
        arrival(four, self.recv[1]).wait()
        arrival(self.out.at[pl.ds(0, 3)], self.send[0]).wait()
        arrival(four, self.send[1]).wait()


class Line:
    @staticmethod
    def scratch(shape):
        return [pltpu.VMEM(shape[1:], BF16)] + LineSum.scratch(shape) + Gather.scratch(shape)

    def __init__(self, eighth, out, refs, part):
        own = refs[0]
        self.sum = LineSum(eighth, own, refs[1:4], part)
        self.gather = Gather(own, out, refs[4:], part)

    def steps(self):
        return [self.sum.to_line, self.to_rows, self.gather.to_pair, self.gather.done]

    def to_rows(self):
        self.sum.done()
        self.gather.to_rows()


class SmallSum:
    @staticmethod
    def scratch(shape):
        sizes = [lax.axis_size(IMG), lax.axis_size(ROW) * lax.axis_size(COL)]
        return [pltpu.VMEM((size,) + shape[1:], BF16) for size in sizes] + [
            pltpu.SemaphoreType.DMA((2,)),
            pltpu.SemaphoreType.DMA((2,)),
        ]

    def __init__(self, src, out, refs):
        self.src, self.out = src, out
        self.slots1, self.slots2, self.send, self.recv = refs

    def steps(self):
        return [self.to_line, self.to_plane, self.done]

    def to_line(self):
        here, total, _ = group_of(LINE)
        self.slots1[0] = self.src[here]
        for j in range(1, total):
            there = lax.rem(here + j, total)
            remote(
                self.src.at[there], self.slots1.at[j], self.send.at[0], self.recv.at[0], {IMG: there}
            ).start()

    def to_plane(self):
        gather_wait(LINE, self.slots1, self.recv.at[0])
        total = added([p.astype(F32) for p in in_order(LINE, self.slots1)])
        self.slots2[0] = total.astype(BF16)
        gather_start(PLANE, self.slots2, self.send.at[1], self.recv.at[1])

    def done(self):
        gather_wait(PLANE, self.slots2, self.recv.at[1])
        self.out[...] = added([p.astype(F32) for p in in_order(PLANE, self.slots2)])
        gather_wait(LINE, self.slots1, self.send.at[0])
        gather_wait(PLANE, self.slots2, self.send.at[1])


class Jobs:
    def __init__(self):
        self.queue = []

    def add(self, *jobs):
        lists = [job.steps() for job in jobs]
        for k in range(max(len(steps) for steps in lists)):
            self.queue += [steps[k] for steps in lists if k < len(steps)]

    def tick(self, count=1):
        for _ in range(min(count, len(self.queue))):
            self.queue.pop(0)()

    def finish(self):
        self.tick(len(self.queue))


def plane_jobs(src, eighth, refs):
    return [Plane(src, eighth, refs, part) for part in range(len(halves(src.shape[-1])))]


def part_jobs(kind, first, second, refs):
    return [kind(first, second, refs, part) for part in range(len(halves(first.shape[-1])))]


def line_jobs(eighth, out, refs):
    return [Line(eighth, out, refs, part) for part in range(len(halves(out.shape[-1])))]


STEP = 32
PIECE = 256
CHUNK = 256


class Refs:
    FLYING = 6 * 1024 * 1024

    def __init__(self):
        self.loads, self.stores, self.queue, self.flying = {}, {}, [], {}

    def load(self, ref, copy):
        self.loads[id(ref)] = copy
        self.queue.append((id(ref), int(np.prod(ref.shape)) * ref.dtype.itemsize))

    def start_loads(self, until=None):
        while self.queue:
            if until is None and sum(self.flying.values()) >= self.FLYING:
                return
            if until is not None and until in self.flying:
                return
            key, size = self.queue.pop(0)
            self.loads[key].start()
            self.flying[key] = size

    def ready(self, *refs):
        for ref in refs:
            self.start_loads(id(ref))
            self.loads.pop(id(ref)).wait()
            self.flying.pop(id(ref))
            self.start_loads()

    def push(self, *refs):
        for ref in refs:
            self.stores[id(ref)].start()

    def flush(self):
        for copy in self.stores.values():
            copy.wait()


def fused(work, cid, ins, staged, outs, pushed, scratch, smem={}, far={}):
    loaded, stored = {**ins, **staged}, {**outs, **pushed}
    sizes = (len(loaded), len(stored))

    def kernel(*refs):
        r = Refs()
        refs = list(refs)

        def take(count):
            taken = refs[:count]
            del refs[:count]
            return taken

        for key, ref in zip((*smem, *far), take(len(smem) + len(far))):
            setattr(r, key, ref)
        in_raw, out_raw = (take(count) for count in sizes)
        for key, shape in scratch.items():
            setattr(r, key, take(len(shape)) if isinstance(shape, list) else take(1)[0])
        in_bufs, out_bufs = (take(count) for count in sizes)
        in_sems, out_sems = take(2)
        for keys, bufs in ((loaded, in_bufs), (stored, out_bufs)):
            for key, buf in zip(keys, bufs):
                setattr(r, key, buf)
        for k, (raw, buf) in enumerate(zip(in_raw, in_bufs)):
            r.load(buf, pltpu.make_async_copy(raw, buf, in_sems.at[k]))
        for k, (raw, buf) in enumerate(zip(out_raw, out_bufs)):
            r.stores[id(buf)] = pltpu.make_async_copy(buf, raw, out_sems.at[k])
        r.start_loads()
        signal_all()
        r.ready(*in_bufs[: len(ins)])
        work(r)
        r.push(*out_bufs[: len(outs)])
        r.flush()

    flat = []
    for shape in scratch.values():
        flat += shape if isinstance(shape, list) else [shape]
    flat += [pltpu.VMEM(a.shape, a.dtype) for a in (*loaded.values(), *stored.values())]
    flat += [pltpu.SemaphoreType.DMA((count,)) for count in sizes]
    anywhere, scalars = pl.BlockSpec(memory_space=pl.ANY), pl.BlockSpec(memory_space=pltpu.SMEM)
    result = pl.pallas_call(
        kernel,
        out_shape=list(stored.values()),
        in_specs=[scalars] * len(smem) + [anywhere] * (len(far) + sizes[0]),
        out_specs=[anywhere] * sizes[1],
        scratch_shapes=flat,
        compiler_params=pltpu.CompilerParams(
            collective_id=cid, has_side_effects=True, vmem_limit_bytes=VMEM_LIMIT
        ),
    )(*smem.values(), *far.values(), *loaded.values())
    return types.SimpleNamespace(**dict(zip(stored, result)))


def signal_all():
    barrier = pltpu.get_barrier_semaphore()
    for axes in (PLANE, LINE):
        _, total, device = group_of(axes)
        for step in range(1, total):
            pl.semaphore_signal(barrier, inc=1, device_id=device(step), device_id_type=MESH)


def wait_all():
    count = sum(group_of(axes)[1] - 1 for axes in (PLANE, LINE))
    pl.semaphore_wait(pltpu.get_barrier_semaphore(), count)


def added(parts):
    return functools.reduce(lambda a, b: a + b, parts)


class Exchange:
    @staticmethod
    def scratch(width):
        rows = 2 * width // 128
        sizes = [int(np.prod([lax.axis_size(a) for a in axes])) for axes in (PLANE, LINE)]
        return [
            pltpu.VMEM((sizes[0], rows, 128), F32),
            pltpu.VMEM((sizes[1], rows, 128), F32),
            pltpu.VMEM((rows, 128), F32),
            pltpu.SemaphoreType.DMA((2,)),
            pltpu.SemaphoreType.DMA((2,)),
        ]

    def __init__(self, refs):
        self.slots1, self.slots2, self.out, self.send, self.recv = refs
        self.half = self.out.shape[0] // 2

    def put(self, first, second):
        for k in range(self.half):
            self.slots1[0, k : k + 1, :] = first[:, 128 * k : 128 * (k + 1)]
            self.slots1[0, self.half + k : self.half + k + 1, :] = second[:, 128 * k : 128 * (k + 1)]
        gather_start(PLANE, self.slots1, self.send.at[0], self.recv.at[0])

    def line(self):
        gather_start(LINE, self.slots2, self.send.at[1], self.recv.at[1])

    def middle_sums(self):
        gather_wait(PLANE, self.slots1, self.recv.at[0])
        self.slots2[0] = added(in_order(PLANE, self.slots1))
        self.line()

    def finish_sums(self):
        gather_wait(LINE, self.slots2, self.recv.at[1])
        self.out[...] = added(in_order(LINE, self.slots2))
        self.drain()

    def middle_stats(self, count_ref, plane_count):
        half = self.half
        gather_wait(PLANE, self.slots1, self.recv.at[0])
        parts = in_order(PLANE, self.slots1)
        total = added([p[:half] for p in parts])
        center = total / plane_count
        spread = added([p[half:] for p in parts])
        for spot, part in enumerate(parts):
            count = count_ref[spot : spot + 1, :]
            away = part[:half] / jnp.maximum(count, 1.0) - center
            spread = spread + count * (away * away)
        self.slots2[0, :half] = total
        self.slots2[0, half:] = spread
        self.line()

    def finish_stats(self, plane_count):
        half = self.half
        total_count = plane_count * lax.axis_size(IMG)
        gather_wait(LINE, self.slots2, self.recv.at[1])
        parts = in_order(LINE, self.slots2)
        center = added([p[:half] for p in parts]) / total_count
        spread = added([p[half:] for p in parts])
        for part in parts:
            away = part[:half] / plane_count - center
            spread = spread + plane_count * (away * away)
        self.out[:half] = center
        self.out[half:] = spread / total_count
        self.drain()

    def drain(self):
        gather_wait(PLANE, self.slots1, self.send.at[0])
        gather_wait(LINE, self.slots2, self.send.at[1])

    def rows(self):
        out = self.out[...]
        first = [out[k : k + 1] for k in range(self.half)]
        second = [out[self.half + k : self.half + k + 1] for k in range(self.half)]
        return jnp.concatenate(first, axis=1), jnp.concatenate(second, axis=1)


class Halo:
    scratch = [pltpu.SemaphoreType.DMA((5,)), pltpu.SemaphoreType.DMA((5,))]

    def __init__(self, pad, reach, tile, window, sems, image=None):
        if image is not None:
            tile, window = (ref.at[pl.ds(image, 1)] for ref in (tile, window))
        self.row, self.rows, col, pair, above, below = halo_peers()
        self.pad, self.reach, self.tile, self.window = pad, reach, tile, window
        self.tile_rows, self.tile_cols = tile.shape[1], tile.shape[2]
        self.own = own = pl.ds(pl.multiple_of(HALF * col, HALF), self.tile_cols)
        spot = pl.ds(pl.multiple_of(2 * HALF * col, HALF), HALF)
        side = pl.ds(pl.multiple_of(HALF * (1 - col), HALF), HALF)
        mid = pl.ds(HALF, HALF)
        upper = pl.ds(pad - reach, reach)
        lower = pl.ds(pad + self.tile_rows, reach)
        send, recv = sems

        def copy(src, dst, k, device):
            return pltpu.make_async_remote_copy(
                src_ref=src,
                dst_ref=dst,
                send_sem=send.at[k],
                recv_sem=recv.at[k],
                device_id=device,
                device_id_type=MESH,
            )

        w = window
        self.to_pair = copy(
            tile.at[:, :, side], w.at[:, pl.ds(pad, self.tile_rows), spot], 0, pair
        )
        self.up = copy(tile.at[:, pl.ds(0, reach)], w.at[:, lower, own], 1, above)
        self.down = copy(
            tile.at[:, pl.ds(self.tile_rows - reach, reach)], w.at[:, upper, own], 2, below
        )
        self.from_below = copy(w.at[:, lower, mid], w.at[:, lower, spot], 3, pair)
        self.from_above = copy(w.at[:, upper, mid], w.at[:, upper, spot], 4, pair)

    def blank(self):
        window, pad, reach, tile_rows = self.window, self.pad, self.reach, self.tile_rows
        zero = jnp.zeros((window.shape[0],) + window.shape[2:], window.dtype)

        def fill(first, last):
            for k in range(first, last):
                window[:, k] = zero

        fill(0, pad - reach)
        fill(pad + tile_rows + reach, 2 * pad + tile_rows)

        @pl.when(self.row == 0)
        def _():
            fill(pad - reach, pad)

        @pl.when(self.row == self.rows - 1)
        def _():
            fill(pad + tile_rows, pad + tile_rows + reach)

    def start(self):
        @pl.when(self.row > 0)
        def _():
            self.up.start()

        @pl.when(self.row < self.rows - 1)
        def _():
            self.down.start()

        self.to_pair.start()
        for n in range(self.tile.shape[0]):
            self.window[n, pl.ds(self.pad, self.tile_rows), self.own, :] = self.tile[n]

    def middle(self):
        @pl.when(self.row < self.rows - 1)
        def _():
            self.up.wait_recv()
            self.from_below.start()

        @pl.when(self.row > 0)
        def _():
            self.down.wait_recv()
            self.from_above.start()

    def finish(self):
        self.to_pair.wait()

        @pl.when(self.row < self.rows - 1)
        def _():
            self.down.wait_send()
            self.from_below.wait()

        @pl.when(self.row > 0)
        def _():
            self.up.wait_send()
            self.from_above.wait()


def gauss(x):
    bell = jnp.exp2(x * (x * -0.7213475204444817))
    d = 1.0 + (0.3275911 * 0.7071067811865476) * jnp.abs(x)
    t = pl.reciprocal(d, approx=True)
    t = t * (2.0 - d * t)
    poly = 0.5307027145 * t - 0.7265760135
    poly = poly * t + 0.7107068705
    poly = poly * t - 0.142248368
    poly = poly * t + 0.127414796
    tail = poly * (t * bell)
    return jnp.where(x < 0, tail, 1.0 - tail), bell * 0.3989422804014327


def wide(mask, width):
    return jnp.concatenate([mask] * (width // 128), axis=1)


def place(ref, i, lanes):
    if len(ref.shape) == 4:
        return (i // ref.shape[1], lax.rem(i, ref.shape[1]), slice(None), lanes)
    return (pl.ds(pl.multiple_of(i * STEP, STEP), STEP), lanes)


def by_rows(pixels, width, work, sums=0):
    pieces = [slice(l, l + PIECE) for l in range(0, width, PIECE)]

    def one(i, carry):
        out = []
        for k, lanes in enumerate(pieces):
            got = work(i, lanes)
            for j in range(sums):
                folded = jnp.sum(got[j].reshape(STEP // 8, 8, PIECE), axis=0)
                out.append(carry[k * sums + j] + folded)
        return tuple(out)

    start = tuple(jnp.zeros((8, PIECE), F32) for _ in range(sums * len(pieces)))
    final = lax.fori_loop(0, pixels // STEP, one, start)
    rows = []
    for j in range(sums):
        parts = [jnp.sum(final[k * sums + j], axis=0, keepdims=True) for k in range(len(pieces))]
        rows.append(jnp.concatenate(parts, axis=1))
    return rows


NORM_ROWS = 8


def norm_table(exchange, gain_ref, shift_ref, out_ref, first):
    mean, var = exchange.rows()
    lanes = slice(first, first + mean.shape[1])
    inv = lax.rsqrt(var + EPSILON)
    out_ref[...] = jnp.zeros_like(out_ref)
    out_ref[0:1, :] = mean
    out_ref[1:2, :] = inv
    out_ref[2:3, :] = inv * gain_ref[:, lanes]
    out_ref[3:4, :] = shift_ref[:, lanes]
    out_ref[4:5, :] = var


def normed(u_ref, norm, i, lanes):
    away = u_ref[place(u_ref, i, lanes)].astype(F32) - norm[0:1, lanes]
    return away * norm[2:3, lanes] + norm[3:4, lanes], away


def activate(u_ref, norm, mask, h_ref, residual=None, slope=None, keep=None):
    def work(i, lanes):
        x, _ = normed(u_ref, norm, i, lanes)
        if residual is not None:
            x = x + residual[place(residual, i, lanes)].astype(F32)
        below, bell = gauss(x)
        m = wide(mask[place(mask, i, slice(None))], PIECE)
        h_ref[place(h_ref, i, lanes)] = (x * below * m).astype(BF16)
        if slope is not None:
            slope[place(slope, i, lanes)] = ((below + x * bell) * m).astype(BF16)
        if keep is not None:
            keep[place(keep, i, lanes)] = u_ref[place(u_ref, i, lanes)].astype(BF16)

    by_rows(mask.shape[0], norm.shape[1], work)


def device_stats(u_ref, mask, count):
    pixels, width = u_ref.shape

    def total_of(i, lanes):
        m = wide(mask[place(mask, i, slice(None))], PIECE)
        return (u_ref[place(u_ref, i, lanes)] * m,)

    (total,) = by_rows(pixels, width, total_of, 1)
    center = total / jnp.maximum(wide(count, width), 1.0)

    def spread_of(i, lanes):
        m = wide(mask[place(mask, i, slice(None))], PIECE)
        away = u_ref[place(u_ref, i, lanes)] - center[:, lanes]
        return (away * away * m,)

    (spread,) = by_rows(pixels, width, spread_of, 1)
    return total, spread


def product(a_ref, w_ref, o_ref, turned=False):
    dims = (((1,), (1 if turned else 0,)), ((), ()))

    def one(i, carry):
        rows = pl.ds(pl.multiple_of(i * CHUNK, CHUNK), CHUNK)
        o_ref[rows, :] = lax.dot_general(
            a_ref[rows, :], w_ref[...], dims, preferred_element_type=F32
        )
        return carry

    lax.fori_loop(0, a_ref.shape[0] // CHUNK, one, 0)


def turn(a_ref, t_ref):
    def one(i, carry):
        rows = pl.ds(pl.multiple_of(i * CHUNK, CHUNK), CHUNK)
        t_ref[:, rows] = a_ref[rows, :].T
        return carry

    lax.fori_loop(0, a_ref.shape[0] // CHUNK, one, 0)


def put_lanes(ref, first, value):
    width = ref.shape[-1]
    at, stop = first, first + value.shape[1]
    while at < stop:
        cut = at // width
        until = min(stop, (cut + 1) * width)
        part = value[:, at - first : until - first].astype(ref.dtype)
        lanes = slice(at - cut * width, until - cut * width)
        if len(ref.shape) == 4:
            ref[cut, :, :, lanes] = part.reshape(ref.shape[1:3] + part.shape[1:])
        else:
            ref[cut, :, lanes] = part
        at = until


def weight_product(t_ref, b_ref, gw_ref):
    channels = b_ref.shape[1]
    for first in range(0, channels, 512):
        value = jnp.dot(t_ref[...], b_ref[:, first : first + 512], preferred_element_type=F32)
        if len(gw_ref.shape) == 4 and gw_ref.shape[-1] == channels:
            part = value.astype(gw_ref.dtype).reshape(gw_ref.shape[:3] + (512,))
            gw_ref[:, :, :, first : first + 512] = part
        else:
            put_lanes(gw_ref, first, value)


def put_rows(ref, first, value):
    if len(ref.shape) == 3:
        ref[0, first : first + value.shape[0], :] = value.astype(ref.dtype)
        return
    rows = ref.shape[2]
    at, stop = first, first + value.shape[0]
    while at < stop:
        eighth = at // rows
        until = min(stop, (eighth + 1) * rows)
        low, high = at - eighth * rows, until - eighth * rows
        part = value[at - first : until - first].astype(ref.dtype)
        ref[eighth // 8, eighth % 8, low:high, :] = part
        at = until


def norm_back(e_ref, u_ref, norm, sums, pixel_count, mask, out_ref):
    sum_grad, sum_unit = (s * (1.0 / pixel_count) for s in sums)

    def work(i, lanes):
        away = u_ref[place(u_ref, i, lanes)].astype(F32) - norm[0:1, lanes]
        unit = away * norm[1:2, lanes]
        e = e_ref[place(e_ref, i, lanes)].astype(F32)
        m = wide(mask[place(mask, i, slice(None))], PIECE)
        grad = norm[2:3, lanes] * (e - sum_grad[:, lanes] - unit * sum_unit[:, lanes]) * m
        out_ref[place(out_ref, i, lanes)] = grad.astype(BF16)

    by_rows(mask.shape[0], norm.shape[1], work)


def gelu_grad(e_ref, u_ref, norm, mask):
    def work(i, lanes):
        x, away = normed(u_ref, norm, i, lanes)
        below, bell = gauss(x)
        m = wide(mask[place(mask, i, slice(None))], PIECE)
        e = e_ref[place(e_ref, i, lanes)] * (below + x * bell) * m
        e_ref[place(e_ref, i, lanes)] = e
        return e, e * (away * norm[1:2, lanes])

    return by_rows(mask.shape[0], norm.shape[1], work, 2)


def put_sums(exchange, out_ref):
    first, second = exchange.rows()
    out_ref[...] = jnp.zeros_like(out_ref)
    out_ref[0:1, :] = first
    out_ref[1:2, :] = second
    return first, second


def order_taps(rows, width):
    to = lax.broadcasted_iota(jnp.int32, (rows, width), 0)
    at = lax.broadcasted_iota(jnp.int32, (rows, width), 1)
    picked = jnp.where(to < 16, 2 * to, 2 * (to - 16) + 1)
    real = lax.rem(to, 16) < 9
    return jnp.where(jnp.logical_and(at == picked, real), 1.0, 0.0)


def make_mask(r, tile_cols):
    row, col = lax.axis_index(ROW), lax.axis_index(COL)
    rows, cols = lax.axis_size(ROW), lax.axis_size(COL)
    images = r.orientation.shape[0]
    tile_rows = r.mask.shape[0] // images // tile_cols
    tall = [r.orientation[n].astype(F32) for n in range(images)]
    for n in range(images):

        def fill(i, carry, n=n):
            column = lax.broadcasted_iota(jnp.int32, (tile_cols, 128), 0) + col * tile_cols
            portrait = jnp.where(column < SHORT, 1.0, 0.0)
            line = jnp.zeros((tile_cols, 128), jnp.int32) + (row * tile_rows + i)
            landscape = jnp.where(line < SHORT, 1.0, 0.0)
            at = (n * tile_rows + i) * tile_cols
            r.mask[pl.ds(pl.multiple_of(at, tile_cols), tile_cols), :] = (
                landscape * (1.0 - tall[n]) + portrait * tall[n]
            )
            return carry

        lax.fori_loop(0, tile_rows, fill, 0)

    def count(row, col):
        return (
            jnp.clip(SHORT - row * tile_rows, 0, tile_rows) * tile_cols,
            jnp.clip(SHORT - col * tile_cols, 0, tile_cols) * tile_rows,
        )

    def fill_count(at, row, col):
        flat, upright = (c.astype(F32) for c in count(row, col))
        total = added([flat * (1.0 - t) + upright * t for t in tall])
        r.counts[at : at + 1, :] = jnp.zeros((1, 128), F32) + total

    r.counts[...] = jnp.zeros_like(r.counts)
    for k in range(rows * cols):
        fill_count(k, jnp.int32(k // cols), jnp.int32(k % cols))
    fill_count(8, row, col)


def make_corners(r, cols):
    images, _, pixels = r.up.shape
    tile_cols = cols - HALF
    order = order_taps(32, r.base.shape[1]).astype(BF16)
    tap = lax.broadcasted_iota(jnp.int32, (16, pixels), 0)
    pixel = lax.broadcasted_iota(jnp.int32, (16, pixels), 1)
    up0 = pixel // tile_cols + PAD + 2 * (tap // 3 - 1)
    left0 = lax.rem(pixel, tile_cols) + HALF * lax.axis_index(COL) + 2 * (lax.rem(tap, 3) - 1)
    for n in range(images):
        base = r.base[n * pixels : (n + 1) * pixels, :].astype(F32).astype(BF16)
        moved = lax.dot_general(
            order, base, (((1,), (1,)), ((), ())), preferred_element_type=F32
        ).astype(jnp.int32)
        r.up[n] = moved[:16] + up0
        r.left[n] = moved[16:] + left0


def first(plane_count, r):
    ex, ex2 = Exchange(r.ex1), Exchange(r.ex2)
    images, all_rows, cols, width = r.rim.shape
    halos = [Halo(PAD, REACH, r.tile, r.rim, r.halo[2 * n : 2 * n + 2], n) for n in range(images)]
    make_mask(r, cols - HALF)
    r.ready(r.feature, r.w_reduce)
    product(r.feature, r.w_reduce, r.u_a1)
    r.push(r.u_a1)
    total, spread = device_stats(r.u_a1, r.mask, r.counts[8:9, :])
    wait_all()
    ex.put(total, spread)
    make_corners(r, cols)
    ex.middle_stats(r.counts, plane_count)
    for halo in halos:
        halo.blank()
    order = order_taps(32, r.w_offset.shape[0]).astype(BF16)
    for tap in range(9):
        columns = r.w_offset[:, tap * width : (tap + 1) * width]
        r.w_off[32 * tap : 32 * tap + 32, :] = jnp.dot(
            order, columns, preferred_element_type=F32
        ).astype(BF16)
    ex.finish_stats(plane_count)
    norm_table(ex, r.scale, r.shift, r.norm_a1, 0)
    activate(r.u_a1, r.norm_a1, r.mask, r.tile)
    for halo in halos:
        halo.start()
    select_cells(r, cols)
    r.push(r.select)
    r.ready(r.w_deform)
    turn(r.w_deform, r.w_turned)
    for n, halo in enumerate(halos):
        if n == 0:
            halo.middle()
        halo.finish()
        for k in range(0, all_rows, 8):
            lines = r.rim[n, k : k + 8].reshape(8 * cols, width)
            r.rim_t[n, :, k * cols : (k + 8) * cols] = lines.T
        offset_fractions(r, cols, n)
        sample_units(r, cols, n, 0)
        if n + 1 < images:
            halos[n + 1].middle()
        sample_units(r, cols, n, 1)
    r.push(r.rim, r.fr, r.fc, r.samples, r.u_a2)
    total, spread = device_stats(r.u_a2, r.mask, r.counts[8:9, :])
    ex2.put(total, spread)
    ex2.middle_stats(r.counts, plane_count)
    ex2.finish_stats(plane_count)
    norm_table(ex2, r.scale, r.shift, r.norm_a2, width)


def offset_fractions(r, cols, n):
    _, width, cells = r.rim_t.shape
    column = lax.rem(lax.broadcasted_iota(jnp.int32, (32, cells), 1), cols)
    r.spread[...] = jnp.dot(r.w_off[...], r.rim_t[n], preferred_element_type=F32)
    total = None
    for tap in range(9):
        i, j = 2 * (tap // 3 - 1), 2 * (tap % 3 - 1)
        term = r.spread[32 * tap : 32 * tap + 32, :]
        shift = -(i * cols + j) % cells
        if shift:
            term = pltpu.roll(term, shift, axis=1)
        if j < 0:
            term = jnp.where(column >= -j, term, 0.0)
        if j > 0:
            term = jnp.where(column < cols - j, term, 0.0)
        total = term if total is None else total + term
    parts = []
    for _ in range(3):
        parts.append(total.astype(BF16))
        total = total - parts[-1].astype(F32)
    on_tile = lax.dot_general(
        jnp.concatenate(parts, axis=0),
        r.select[...],
        (((1,), (1,)), ((), ())),
        preferred_element_type=F32,
    )
    offsets = on_tile[:32] + on_tile[32:64] + on_tile[64:]
    fraction = 1.0 / (1.0 + jnp.exp(-offsets))
    r.fr[n] = fraction[:16]
    r.fc[n] = fraction[16:]


def sample_units(r, cols, n, b):
    block = r.table.shape[1]
    width = r.rim_t.shape[1]
    lanes = slice(b * block, (b + 1) * block)
    mine = slice((2 * n + b) * block, (2 * n + b + 1) * block)
    base = b * (BLOCK_ROWS * cols)
    for tap in range(9):
        row_w, _, col_w, _ = tap_weights(tap, b, cols, r.up, r.left, r.fr, r.fc, n, lanes)
        write_table(r.table, 0, row_w, col_w, tap // 3, cols)
        _, start, stop = tap_span(tap // 3, cols)
        cells = r.rim_t[n, :, base + start : base + stop]
        value = jnp.dot(cells, r.table[start:stop, :], preferred_element_type=F32)
        r.samples[tap * width : (tap + 1) * width, mine] = value.astype(BF16)
    deformed = jnp.dot(r.w_turned[...], r.samples[:, mine], preferred_element_type=F32)
    r.u_a2[mine, :] = deformed.T


def finish_kernel(unbias, count, *refs):
    ins, outs, rest = refs[:count], refs[count : count + 17], refs[count + 17 :]
    bufs, out_bufs, sems, out_sems = rest[:count], rest[count : count + 15], rest[-2], rest[-1]
    loads = [pltpu.make_async_copy(ins[k], bufs[k], sems.at[k]) for k in range(count)]
    stores = [pltpu.make_async_copy(out_bufs[k], outs[k], out_sems.at[k]) for k in range(15)]
    stores += [
        pltpu.make_async_copy(bufs[count - 2 + k], outs[15 + k], out_sems.at[15 + k]) for k in range(2)
    ]
    for load in loads:
        load.start()
    conv_b, reduce_b, reduce_a, expand_b, expand_a, deform, off = bufs[:7]
    tables = bufs[7:19]
    for load in loads[:7]:
        load.wait()
    for k, src in enumerate((expand_b, expand_a, deform)):
        rows = src.shape[1]
        for s in range(8):
            out_bufs[3 + k][s * rows : (s + 1) * rows, :] = src[s].astype(F32)
        stores[3 + k].start()
    for k, src in enumerate((conv_b, reduce_b, reduce_a)):
        eighth = src.shape[1]
        for s in range(0, 8, 2):
            rows = jnp.concatenate([src[s], src[s + 1]], axis=0).astype(F32)
            out_bufs[k][:, s * eighth : (s + 2) * eighth] = rows.T
        stores[k].start()
    for k in range(2):
        loads[count - 2 + k].wait()
        stores[15 + k].start()
    rest, total = off[...], None
    order = order_taps(32, 18).astype(BF16)
    for _ in range(3):
        part = rest.astype(BF16)
        rest = rest - part.astype(F32)
        term = lax.dot_general(order, part, (((0,), (0,)), ((), ())), preferred_element_type=F32)
        total = term if total is None else total + term
    out_bufs[6][...] = total
    for load in loads[7 : count - 2]:
        load.wait()
    for k in range(4):
        group, which = tables[3 * k : 3 * k + 3], out_bufs[7 + 2 * k : 9 + 2 * k]
        norms = k >= 2
        for out, row in zip(which, (0, 4) if norms else (1, 0)):
            at = 0
            for table in group:
                for first_lane in range(0, table.shape[1], 128):
                    value = table[row : row + 1, first_lane : first_lane + 128]
                    out[at : at + 1, :] = value * unbias if norms and row == 4 else value
                    at += 1
    for store in stores[6:15]:
        store.start()
    for store in stores:
        store.wait()


def forward_a(plane_count, r):
    ex3, ex1 = Exchange(r.ex3), Exchange(r.ex1)
    halo = Halo(2, 2, r.tile, r.rim_b, r.halo)
    halo.blank()
    r.ready(r.u_a2)
    activate(r.u_a2, r.norm_a2, r.mask, r.h2_a)
    r.push(r.h2_a)
    r.ready(r.w_expand)
    product(r.h2_a, r.w_expand, r.wide)
    count = r.counts[8:9, :]
    total, spread = device_stats(r.wide, r.mask, count)
    wait_all()
    ex3.put(total, spread)
    r.ready(r.feature, r.w_reduce)
    ex3.middle_stats(r.counts, plane_count)
    ex3.finish_stats(plane_count)
    norm_table(ex3, r.scale_a, r.shift_a, r.norm_a3, 2 * r.h2_a.shape[1])
    activate(r.wide, r.norm_a3, r.mask, r.middle, r.feature, r.slope_a, r.u_a3)
    r.push(r.middle, r.slope_a, r.u_a3)
    product(r.middle, r.w_reduce, r.u_b1)
    r.push(r.u_b1)
    total, spread = device_stats(r.u_b1, r.mask, count)
    ex1.put(total, spread)
    ex1.middle_stats(r.counts, plane_count)
    ex1.finish_stats(plane_count)
    norm_table(ex1, r.scale_b, r.shift_b, r.norm_b1, 0)
    activate(r.u_b1, r.norm_b1, r.mask, r.tile)
    halo.start()
    halo.middle()
    halo.finish()
    r.push(r.rim_b)


def forward_b(plane_count, r):
    ex2, ex3, ex4 = Exchange(r.ex2), Exchange(r.ex3), Exchange(r.ex4)
    count = r.counts[8:9, :]
    r.ready(r.rim_b)
    build_shifted(r.rim_b, r.shifted)
    r.ready(r.w_conv)
    conv_product(r.shifted, r.w_conv, r.u_b2)
    r.push(r.u_b2)
    total, spread = device_stats(r.u_b2, r.mask, count)
    wait_all()
    ex2.put(total, spread)
    ex2.middle_stats(r.counts, plane_count)
    ex2.finish_stats(plane_count)
    norm_table(ex2, r.scale, r.shift, r.norm_b2, r.h2_b.shape[1])
    activate(r.u_b2, r.norm_b2, r.mask, r.h2_b)
    r.push(r.h2_b)
    r.ready(r.w_expand)
    product(r.h2_b, r.w_expand, r.wide)
    total, spread = device_stats(r.wide, r.mask, count)
    ex3.put(total, spread)
    r.ready(r.middle, r.cotangent)
    ex3.middle_stats(r.counts, plane_count)
    ex3.finish_stats(plane_count)
    norm = r.norm_b3
    norm_table(ex3, r.scale, r.shift, norm, 2 * r.h2_b.shape[1])

    def work(i, lanes):
        x, away = normed(r.wide, norm, i, lanes)
        at = place(r.wide, i, lanes)
        r.u_b3[at] = r.wide[at].astype(BF16)
        x = x + r.middle[at].astype(F32)
        below, bell = gauss(x)
        m = wide(r.mask[place(r.mask, i, slice(None))], PIECE)
        r.feature_out[at] = (x * below * m).astype(BF16)
        e = (below + x * bell) * r.cotangent[at].astype(F32) * m
        r.e_b3[at] = e.astype(BF16)
        return e, e * (away * norm[1:2, lanes])

    sums = by_rows(r.wide.shape[0], r.wide.shape[1], work, 2)
    ex4.put(*sums)
    r.push(r.feature_out, r.e_b3, r.u_b3)
    ex4.middle_sums()
    ex4.finish_sums()
    put_sums(ex4, r.sums_b3)


def backward_b(pixel_count, direct, r):
    ex2, ex1 = Exchange(r.ex2), Exchange(r.ex1)
    halo = Halo(2, 2, r.tile, r.back_rim, r.halo)
    halo.blank()
    r.ready(r.e_b3, r.u_b3)
    sums = (r.sums_b3[0:1, :], r.sums_b3[1:2, :])
    norm_back(r.e_b3, r.u_b3, r.norm_b3, sums, pixel_count, r.mask, r.geo)
    r.ready(r.w_expand)
    product(r.geo, r.w_expand, r.grad, turned=True)
    r.ready(r.u_b2)
    sums = gelu_grad(r.grad, r.u_b2, r.norm_b2, r.mask)
    wait_all()
    ex2.put(*sums)
    r.ready(r.h2_b)
    turn(r.h2_b, r.turned)
    ex2.middle_sums()
    weight_product(r.turned, r.geo, r.gw_expand)
    jobs = Jobs()
    if direct:
        jobs.add(*plane_jobs(r.gw_expand, r.eighth_expand_b, r.plane_expand_b))
    else:
        r.push(r.gw_expand)
    jobs.tick(2)
    ex2.finish_sums()
    sums = put_sums(ex2, r.sums_b2)
    norm_back(r.grad, r.u_b2, r.norm_b2, sums, pixel_count, r.mask, r.tile)
    halo.start()
    tile_rows, tile_cols, width = r.tile.shape[1:]
    pixels = tile_rows * tile_cols
    for n in range(r.tile.shape[0]):
        for k in range(0, tile_rows, 8):
            at = n * pixels + k * tile_cols
            block = r.tile[n, k : k + 8].reshape(8 * tile_cols, width)
            r.turned[:, at : at + 8 * tile_cols] = block.T
    r.ready(r.rim_b)
    build_shifted(r.rim_b, r.shifted)
    conv_weight_product(r.turned, r.shifted, r.gw_conv, 0)
    halo.middle()
    jobs.tick(2)
    conv_weight_product(r.turned, r.shifted, r.gw_conv, 1)
    halo.finish()
    build_shifted(r.back_rim, r.back_shifted)
    r.ready(r.w_conv)
    unconv_product(r.back_shifted, r.w_conv, r.grad)
    r.ready(r.u_b1)
    sums = gelu_grad(r.grad, r.u_b1, r.norm_b1, r.mask)
    ex1.put(*sums)
    jobs.tick(2)
    ex1.middle_sums()
    conv_weight_product(r.turned, r.shifted, r.gw_conv, 2)
    r.push(r.gw_conv)
    jobs.finish()
    if direct:
        r.push(r.eighth_expand_b)
    ex1.finish_sums()
    sums = put_sums(ex1, r.sums_b1)
    norm_back(r.grad, r.u_b1, r.norm_b1, sums, pixel_count, r.mask, r.gro_b)


def backward_a(pixel_count, direct, r):
    ex3, ex2 = Exchange(r.ex3), Exchange(r.ex2)
    conv, line = Jobs(), Jobs()
    r.ready(r.gro_b, r.w_reduce)
    product(r.gro_b, r.w_reduce, r.wide, turned=True)
    wait_all()
    if direct:
        r.ready(r.src_conv_b, r.eighth_expand_b)
        conv.add(*plane_jobs(r.src_conv_b, r.eighth_conv_b, r.plane_conv_b))
        line.add(*line_jobs(r.eighth_expand_b, r.sum_expand_b, r.line_expand_b))
    conv.tick(2)
    line.tick(2)
    r.ready(r.e_b3, r.slope_a, r.u_a3)
    norm = r.norm_a3

    def work(i, lanes):
        at = place(r.wide, i, lanes)
        e = (r.wide[at] + r.e_b3[at].astype(F32)) * r.slope_a[at].astype(F32)
        r.e_a3[at] = e.astype(BF16)
        away = r.u_a3[at].astype(F32) - norm[0:1, lanes]
        return e, e * (away * norm[1:2, lanes])

    sums = by_rows(r.wide.shape[0], r.wide.shape[1], work, 2)
    ex3.put(*sums)
    conv.tick(2)
    r.push(r.e_a3)
    turn(r.gro_b, r.turned)
    ex3.middle_sums()
    r.ready(r.middle)
    weight_product(r.turned, r.middle, r.gw_reduce)
    r.push(r.gw_reduce)
    line.tick(2)
    ex3.finish_sums()
    sums = put_sums(ex3, r.sums_a3)
    norm_back(r.e_a3, r.u_a3, norm, sums, pixel_count, r.mask, r.e_b3)
    r.ready(r.w_expand)
    product(r.e_b3, r.w_expand, r.grad, turned=True)
    r.ready(r.u_a2)
    sums = gelu_grad(r.grad, r.u_a2, r.norm_a2, r.mask)
    ex2.put(*sums)
    conv.tick(2)
    line.tick(2)
    r.ready(r.h2_a)
    turn(r.h2_a, r.turned)
    ex2.middle_sums()
    weight_product(r.turned, r.e_b3, r.gw_expand)
    r.push(r.gw_expand)
    ex2.finish_sums()
    sums = put_sums(ex2, r.sums_a2)
    norm_back(r.grad, r.u_a2, r.norm_a2, sums, pixel_count, r.mask, r.gd)
    conv.finish()
    line.finish()
    if direct:
        r.push(r.eighth_conv_b, r.sum_expand_b)


def unsample(r, plan):
    width = r.rim.shape[2]
    cols = r.table.shape[0] // WINDOW
    pixels = r.up.shape[2] // 2
    r.spill[...] = jnp.zeros_like(r.spill)
    r.grad_row[...] = jnp.zeros_like(r.grad_row)
    r.grad_col[...] = jnp.zeros_like(r.grad_col)

    def unit(step, carry):
        n, block = step // 2, lax.rem(step, 2)
        lanes = pl.ds(pl.multiple_of(block * pixels, pixels), pixels)
        base = block * (BLOCK_ROWS * cols)
        grad_in = r.turned[:, pl.ds(pl.multiple_of(step * pixels, pixels), pixels)]
        for group in range(3):
            first, start, stop = tap_span(group, cols)
            cells = pl.ds(pl.multiple_of(base + start, 128), stop - start)
            for j in range(3):
                tap = 3 * group + j
                spot = slice(j * pixels, (j + 1) * pixels)
                row_w, row_s, col_w, col_s = tap_weights(
                    tap, block, cols, r.up, r.left, r.fr, r.fc, n, lanes
                )
                write_table(r.table, j * pixels, row_w, col_w, group, cols)
                grad = jnp.dot(
                    r.w_deform[tap * width : (tap + 1) * width, :],
                    grad_in,
                    preferred_element_type=F32,
                ).astype(BF16)
                r.grads[:, spot] = grad
                scores = jnp.dot(r.rim[n, cells, :], grad, preferred_element_type=F32)
                by_value = jnp.zeros((cols, pixels), F32)
                by_slope = jnp.zeros((cols, pixels), F32)
                for k in range(first, first + SPAN):
                    line = scores[k * cols - start : (k + 1) * cols - start]
                    by_value = by_value + line * row_w[k : k + 1, :]
                    by_slope = by_slope + line * row_s[k : k + 1, :]
                r.grad_row[n, tap : tap + 1, lanes] = jnp.sum(
                    by_slope * col_w, axis=0, keepdims=True
                )
                r.grad_col[n, tap : tap + 1, lanes] = jnp.sum(
                    by_value * col_s, axis=0, keepdims=True
                )
            r.spill[n, cells, :] += lax.dot_general(
                r.table[start:stop, :],
                r.grads[...],
                (((1,), (1,)), ((), ())),
                preferred_element_type=F32,
            )
            for turn_at in range(4):
                if 3 * turn_at + group in plan:

                    @pl.when(step == turn_at)
                    def _(slot=3 * turn_at + group):
                        plan[slot]()

        return carry

    lax.fori_loop(0, 4, unit, 0)


def select_cells(r, cols):
    off = HALF * lax.axis_index(COL)
    cells = r.select.shape[1]

    def fill(i, carry):
        ids = lax.broadcasted_iota(jnp.int32, (STEP, cells), 1)
        pixel = lax.broadcasted_iota(jnp.int32, (STEP, cells), 0)
        hit = ids == pixel + (i + PAD) * cols + off
        r.select[pl.ds(pl.multiple_of(i * STEP, STEP), STEP), :] = jnp.where(hit, 1.0, 0.0).astype(
            BF16
        )
        return carry

    lax.fori_loop(0, r.select.shape[0] // STEP, fill, 0)


def unoffset(r, n):
    images, cells, width = r.rim.shape
    cols = r.table.shape[0] // WINDOW
    column = lax.rem(lax.broadcasted_iota(jnp.int32, (32, cells), 1), cols)
    parts = []
    for grad, frac in ((r.grad_row, r.fr), (r.grad_col, r.fc)):
        f = frac[n]
        parts.append(grad[n] * f * (1.0 - f))
    go = jnp.concatenate(parts, axis=0).astype(BF16)
    on_tile = jnp.dot(go, r.select[...], preferred_element_type=F32)
    for tap in range(9):
        i, j = 2 * (tap // 3 - 1), 2 * (tap % 3 - 1)
        kept = on_tile
        if j < 0:
            kept = jnp.where(column >= -j, on_tile, 0.0)
        if j > 0:
            kept = jnp.where(column < cols - j, on_tile, 0.0)
        shift = (i * cols + j) % cells
        if shift:
            kept = pltpu.roll(kept, shift, axis=1)
        r.on_cells[32 * tap : 32 * tap + 32, :] = kept.astype(BF16)
    grad = jnp.dot(r.on_cells[...], r.rim[n], preferred_element_type=F32)
    if n == 0:
        r.gw_off_sum[...] = grad
    else:
        r.gw_off_sum[...] += grad
    for first in range(0, cells, 512):
        r.spill[n, first : first + 512, :] += lax.dot_general(
            r.on_cells[:, first : first + 512],
            r.w_off[...],
            (((0,), (0,)), ((), ())),
            preferred_element_type=F32,
        )
    if n == images - 1:
        for tap in range(9):
            put_lanes(r.gw_off, tap * width, r.gw_off_sum[32 * tap : 32 * tap + 32, :])


class Spill:
    @staticmethod
    def scratch(images, tile_rows, tile_cols, width):
        side = pltpu.VMEM((images, tile_rows + 2 * PAD, HALF, width), BF16)
        strip = pltpu.VMEM((images, REACH, tile_cols, width), BF16)
        sems = pltpu.SemaphoreType.DMA((3,))
        return [side, side, strip, strip, strip, strip, sems, sems]

    def __init__(self, spill, grad, cols, refs, image):
        self.spill, self.grad, self.cols = spill.at[pl.ds(image, 1)], grad, cols
        self.image = image
        self.side_out, self.side_in, self.up_out, self.down_out, self.up_in, self.down_in = refs[:6]
        send, recv = refs[6:]
        self.row, self.rows, col, pair, above, below = halo_peers()
        self.images, self.all_rows = self.side_out.shape[:2]
        self.tile_rows, self.tile_cols = self.all_rows - 2 * PAD, self.up_out.shape[2]
        self.off, self.away, self.near = HALF * col, 2 * HALF * (1 - col), HALF * (1 - col)
        self.side = remote(self.side_out, self.side_in, send.at[0], recv.at[0], pair)
        self.up = remote(self.up_out, self.down_in, send.at[1], recv.at[1], above)
        self.down = remote(self.down_out, self.up_in, send.at[2], recv.at[2], below)

    def cells(self, k, first, count):
        return pl.ds(pl.multiple_of(k * self.cols + first, HALF), count)

    def start(self):
        def cast(k, carry):
            for n in range(self.images):
                self.side_out[n, k] = self.spill[n, self.cells(k, self.away, HALF), :].astype(BF16)
            return carry

        lax.fori_loop(0, self.all_rows, cast, 0)
        self.side.start()

    def edge(self, buffer, first):
        near = pl.ds(pl.multiple_of(self.near, HALF), HALF)

        def one(k, carry):
            for n in range(self.images):
                at = first + k
                buffer[n, k] = self.spill[n, self.cells(at, self.off, self.tile_cols), :].astype(BF16)
                part = self.spill[n, self.cells(at, HALF, HALF), :]
                buffer[n, k, near, :] = (part + self.side_in[n, at].astype(F32)).astype(BF16)
            return carry

        lax.fori_loop(0, REACH, one, 0)

    def middle(self):
        self.side.wait_recv()

        @pl.when(self.row > 0)
        def _():
            self.edge(self.up_out, PAD - REACH)
            self.up.start()

        @pl.when(self.row < self.rows - 1)
        def _():
            self.edge(self.down_out, PAD + self.tile_rows)
            self.down.start()

    def pixels(self, n, k, first, count):
        at = ((self.image + n) * self.tile_rows + k) * self.tile_cols + first
        return pl.ds(pl.multiple_of(at, HALF), count)

    def own(self):
        def fill(k, carry):
            for n in range(self.images):
                home = self.spill[n, self.cells(PAD + k, self.off, self.tile_cols), :]
                self.grad[self.pixels(n, k, 0, self.tile_cols), :] = home
                self.grad[self.pixels(n, k, self.near, HALF), :] += self.side_in[n, PAD + k].astype(F32)
            return carry

        lax.fori_loop(0, self.tile_rows, fill, 0)

    def finish(self):
        def arrive(buffer, first):
            def one(k, carry):
                for n in range(self.images):
                    at = self.pixels(n, first + k, 0, self.tile_cols)
                    self.grad[at, :] += buffer[n, k].astype(F32)
                return carry

            lax.fori_loop(0, REACH, one, 0)

        @pl.when(self.row > 0)
        def _():
            self.down.wait_recv()
            arrive(self.up_in, 0)
            self.up.wait_send()

        @pl.when(self.row < self.rows - 1)
        def _():
            self.up.wait_recv()
            arrive(self.down_in, self.tile_rows - REACH)
            self.down.wait_send()

        self.side.wait_send()


def backward_s(pixel_count, direct, r):
    ex = Exchange(r.ex1)
    cols = r.table.shape[0] // WINDOW
    spills = [Spill(r.spill, r.grad, cols, r.strips[8 * n : 8 * n + 8], n) for n in range(2)]

    mid, late, end = Jobs(), Jobs(), Jobs()
    deform_weight_product(r)
    wait_all()
    if direct:
        line, planes, deform = Jobs(), Jobs(), Jobs()
        line.add(*line_jobs(r.eighth_conv_b, r.sum_conv_b, r.line_conv_b))
        planes.add(
            *plane_jobs(r.src_reduce_b, r.eighth_reduce_b, r.plane_reduce_b),
            *plane_jobs(r.src_expand_a, r.eighth_expand_a, r.plane_expand_a),
        )
        deform.add(*plane_jobs(r.gw_deform, r.eighth_deform, r.plane_deform))
        r.ready(r.src_reduce_b, r.src_expand_a)
        planes.tick(4)
        r.ready(r.eighth_conv_b)
        line.tick(2)
        deform.tick(2)
        sums = [
            part_jobs(LineSum, r.eighth_reduce_b, r.own_reduce_b, r.line_reduce_b),
            part_jobs(LineSum, r.eighth_expand_a, r.own_expand_a, r.line_expand_a),
            part_jobs(LineSum, r.eighth_deform, r.own_deform, r.line_deform),
        ]
        early, final = Jobs(), Jobs()
        early.add(*sums[0], *sums[1])
        final.add(*sums[2])
        q1, q2, q3, q4, q5 = planes.queue, line.queue, deform.queue, early.queue, final.queue
        slots = {
            2: q1[0:4],
            4: q3[0:2],
            6: q1[4:8] + q2[0:2],
            9: q1[8:12] + q4[0:4],
            10: q2[2:4],
            11: q3[2:4],
        }
        mid.queue = q2[4:6]
        late.queue = q3[4:6] + q5[0:2]
        end.queue = q4[4:8] + q5[2:4]
    else:
        slots = {}
        r.push(r.gw_deform)
    slots[5] = [functools.partial(unoffset, r, 0), spills[0].start] + slots.get(5, [])
    slots[8] = [spills[0].middle] + slots.get(8, [])

    def run(queue):
        def call():
            for step in queue:
                step()

        return call

    plan = {slot: run(queue) for slot, queue in slots.items()}
    r.ready(r.w_deform, r.rim, r.w_off, r.select)
    turn(r.gd, r.turned)
    unsample(r, plan)
    unoffset(r, 1)
    spills[1].start()
    r.push(r.gw_off)
    mid.finish()
    spills[1].middle()
    if direct:
        r.push(r.sum_conv_b)
    for spill in spills:
        spill.own()
    spills[0].finish()
    late.finish()
    r.ready(r.u_a1)
    spills[1].finish()
    sums = gelu_grad(r.grad, r.u_a1, r.norm_a1, r.mask)
    ex.put(*sums)
    ex.middle_sums()
    ex.finish_sums()
    sums = put_sums(ex, r.sums_a1)
    norm_back(r.grad, r.u_a1, r.norm_a1, sums, pixel_count, r.mask, r.gr_a)
    end.finish()
    if direct:
        r.push(r.own_reduce_b, r.own_expand_a, r.own_deform)


def deform_weight_product(r):
    width = r.gd.shape[1]
    slots = r.sample_slots.shape[0]

    def load(tap):
        rows, slot = pl.ds(tap * width, width), tap % slots
        return pltpu.make_async_copy(
            r.samples.at[rows], r.sample_slots.at[slot], r.sample_sems.at[slot]
        )

    for tap in range(slots):
        load(tap).start()
    r.ready(r.gd)
    for tap in range(9):
        load(tap).wait()
        value = jnp.dot(r.sample_slots[tap % slots], r.gd[...], preferred_element_type=F32)
        put_rows(r.gw_deform, tap * width, value)
        if tap + slots < 9:
            load(tap + slots).start()


def last(direct, r):
    jobs, plane = Jobs(), Jobs()
    r.ready(r.gr_a, r.feature)
    turn(r.gr_a, r.turned)
    weight_product(r.turned, r.feature, r.gw_reduce)
    wait_all()
    if direct:
        plane.add(*plane_jobs(r.gw_reduce, r.eighth_reduce_a, r.plane_reduce_a))
        plane.add(*line_jobs(r.eighth_reduce_a, r.sum_reduce_a, r.line_reduce_a))
    else:
        r.push(r.gw_reduce)
    plane.tick(2)
    if direct:
        r.ready(r.own_reduce_b, r.own_expand_a, r.own_deform, r.gw_off)
        jobs.add(
            SmallSum(r.gw_off, r.sum_off, r.small),
            *part_jobs(Gather, r.own_deform, r.sum_deform, r.gather_deform),
            *part_jobs(Gather, r.own_reduce_b, r.sum_reduce_b, r.gather_reduce_b),
            *part_jobs(Gather, r.own_expand_a, r.sum_expand_a, r.gather_expand_a),
        )
    jobs.tick(7)
    r.ready(r.w_reduce, r.e_a3)

    def chunk(i, carry):
        rows = pl.ds(pl.multiple_of(i * CHUNK, CHUNK), CHUNK)
        for first in range(0, r.feature.shape[1], 512):
            lanes = slice(first, first + 512)
            grad = lax.dot_general(
                r.gr_a[rows, :],
                r.w_reduce[lanes, :],
                (((1,), (1,)), ((), ())),
                preferred_element_type=F32,
            )
            r.grad_in[rows, lanes] = (grad + r.e_a3[rows, lanes].astype(F32)).astype(BF16)
        return carry

    half = r.feature.shape[0] // CHUNK // 2
    lax.fori_loop(0, half, chunk, 0)
    plane.tick(2)
    lax.fori_loop(half, 2 * half, chunk, 0)
    r.push(r.grad_in)
    plane.tick(2)
    jobs.tick(7)
    plane.tick(4)
    jobs.tick(7)
    plane.tick(2)
    jobs.finish()
    if direct:
        r.push(r.sum_reduce_b, r.sum_expand_a, r.sum_deform)
    plane.finish()
    if direct:
        r.push(r.sum_reduce_a)


def body(
    feature_in,
    orientation,
    offset_base,
    w_reduce_a,
    w_offset_a,
    w_deform_a,
    w_expand_a,
    scale_a,
    shift_a,
    w_reduce_b,
    w_conv_b,
    w_expand_b,
    scale_b,
    shift_b,
    cotangent,
):
    images, tile_rows, tile_cols, channels = feature_in.shape
    inner_width = w_reduce_a.shape[1]
    tile_pixels = tile_rows * tile_cols
    pixels = images * tile_pixels
    win_cols = tile_cols + HALF
    win_rows = tile_rows + 2 * PAD
    cells = win_rows * win_cols
    plane_count = 1.0 * images * LONG * SHORT
    pixel_count = plane_count * lax.axis_size(IMG)
    unbias = pixel_count / (pixel_count - 1.0)

    def array(*shape, dtype=BF16):
        return jax.ShapeDtypeStruct(shape, dtype)

    def table(width):
        return array(NORM_ROWS, width, dtype=F32)

    small = (pixels, inner_width)
    big = (pixels, channels)
    window_b = (images, tile_rows + 4, win_cols, inner_width)
    shifted = pltpu.VMEM((images, tile_rows + 4, tile_cols, 3 * inner_width), BF16)
    tile = pltpu.VMEM((images, tile_rows, tile_cols, inner_width), BF16)
    turned = pltpu.VMEM((inner_width, pixels), BF16)
    images_axis = lax.axis_size(IMG)
    direct = inner_width % (images_axis * 8 * 16) == 0
    cuts = images_axis if direct else 1
    feature = feature_in.reshape(big)
    scale_a, shift_a, scale_b, shift_b = (v[None] for v in (scale_a, shift_a, scale_b, shift_b))
    taps_shape = (images, 16, tile_pixels)
    start = fused(
        functools.partial(first, plane_count),
        FIRST_CID,
        ins=dict(
            base=offset_base.reshape(pixels, 18),
            w_offset=w_offset_a.T,
            scale=scale_a,
            shift=shift_a,
        ),
        smem=dict(orientation=orientation),
        staged=dict(feature=feature, w_reduce=w_reduce_a, w_deform=w_deform_a),
        outs=dict(
            mask=array(pixels, 128, dtype=F32),
            counts=array(16, 128, dtype=F32),
            up=array(*taps_shape, dtype=jnp.int32),
            left=array(*taps_shape, dtype=jnp.int32),
            w_off=array(288, inner_width),
            norm_a1=table(inner_width),
            norm_a2=table(inner_width),
        ),
        pushed=dict(
            u_a1=array(*small, dtype=F32),
            rim=array(images, win_rows, win_cols, inner_width),
            select=array(tile_pixels, cells),
            fr=array(*taps_shape, dtype=F32),
            fc=array(*taps_shape, dtype=F32),
            samples=array(9 * inner_width, pixels),
            u_a2=array(*small, dtype=F32),
        ),
        scratch=dict(
            ex1=Exchange.scratch(inner_width),
            ex2=Exchange.scratch(inner_width),
            halo=Halo.scratch * images,
            tile=tile,
            w_turned=pltpu.VMEM((inner_width, 9 * inner_width), BF16),
            rim_t=pltpu.VMEM((images, inner_width, cells), BF16),
            spread=pltpu.VMEM((288, cells), F32),
            table=pltpu.VMEM((WINDOW * win_cols, tile_pixels // 2), BF16),
        ),
    )
    mask, count_rows, norm_a1 = start.mask, start.counts, start.norm_a1
    rim_flat = start.rim.reshape(images, cells, inner_width)
    norm_a2, deformed = start.norm_a2, start.u_a2
    fwd_a = fused(
        functools.partial(forward_a, plane_count),
        FORWARD_A_CID,
        ins=dict(
            norm_a2=norm_a2,
            mask=mask,
            counts=count_rows,
            scale_a=scale_a,
            shift_a=shift_a,
            scale_b=scale_b,
            shift_b=shift_b,
        ),
        staged=dict(u_a2=deformed, w_expand=w_expand_a, feature=feature, w_reduce=w_reduce_b),
        outs=dict(norm_a3=table(channels), norm_b1=table(inner_width)),
        pushed=dict(
            h2_a=array(*small),
            middle=array(*big),
            slope_a=array(*big),
            u_a3=array(*big),
            u_b1=array(*small, dtype=F32),
            rim_b=array(*window_b),
        ),
        scratch=dict(
            ex3=Exchange.scratch(channels),
            ex1=Exchange.scratch(inner_width),
            halo=Halo.scratch,
            wide=pltpu.VMEM(big, F32),
            tile=tile,
        ),
    )
    fwd_b = fused(
        functools.partial(forward_b, plane_count),
        FORWARD_B_CID,
        ins=dict(
            mask=mask,
            counts=count_rows,
            scale=scale_b,
            shift=shift_b,
        ),
        staged=dict(
            rim_b=fwd_a.rim_b,
            w_conv=w_conv_b,
            w_expand=w_expand_b,
            middle=fwd_a.middle,
            cotangent=cotangent.reshape(big),
        ),
        outs=dict(norm_b2=table(inner_width), norm_b3=table(channels), sums_b3=table(channels)),
        pushed=dict(
            u_b2=array(*small, dtype=F32),
            h2_b=array(*small),
            u_b3=array(*big),
            feature_out=array(*big),
            e_b3=array(*big),
        ),
        scratch=dict(
            ex2=Exchange.scratch(inner_width),
            ex3=Exchange.scratch(channels),
            ex4=Exchange.scratch(channels),
            wide=pltpu.VMEM(big, F32),
            shifted=shifted,
        ),
    )
    def eighths(grad):
        return grad.reshape(images_axis, 8, -1, grad.shape[-1])

    def eighth_of(src):
        return array(images_axis, *src.shape[2:])

    def own_of(src):
        return array(*src.shape[2:])

    def sum_of(src):
        return array(*src.shape[1:])

    def vmem(struct):
        return pltpu.VMEM(struct.shape, struct.dtype)

    natural = array(1, inner_width, channels)
    pushed_b, scratch_b = dict(gw_expand=natural), {}
    if direct:
        expand_b = array(images_axis, 8, inner_width // images_axis // 8, channels)
        pushed_b = dict(eighth_expand_b=eighth_of(expand_b))
        scratch_b = dict(gw_expand=vmem(expand_b), plane_expand_b=Plane.scratch(expand_b.shape))
    bwd_b = fused(
        functools.partial(backward_b, pixel_count, direct),
        BACKWARD_B_CID,
        ins=dict(
            mask=mask,
            norm_b3=fwd_b.norm_b3,
            sums_b3=fwd_b.sums_b3,
            norm_b2=fwd_b.norm_b2,
            norm_b1=fwd_a.norm_b1,
        ),
        staged=dict(
            e_b3=fwd_b.e_b3,
            u_b3=fwd_b.u_b3,
            w_expand=w_expand_b,
            u_b2=fwd_b.u_b2,
            h2_b=fwd_b.h2_b,
            rim_b=fwd_a.rim_b,
            w_conv=w_conv_b,
            u_b1=fwd_a.u_b1,
        ),
        outs=dict(gro_b=array(*small), sums_b2=table(inner_width), sums_b1=table(inner_width)),
        pushed=dict(
            **pushed_b,
            gw_conv=array(cuts, inner_width, 9 * inner_width // cuts),
        ),
        scratch=dict(
            **scratch_b,
            ex2=Exchange.scratch(inner_width),
            ex1=Exchange.scratch(inner_width),
            halo=Halo.scratch,
            geo=pltpu.VMEM(big, BF16),
            grad=pltpu.VMEM(small, F32),
            tile=tile,
            turned=turned,
            back_rim=pltpu.VMEM(window_b, BF16),
            shifted=shifted,
            back_shifted=shifted,
        ),
    )

    staged_a, pushed_a, scratch_a = {}, {}, {}
    if direct:
        conv_b = eighths(bwd_b.gw_conv)
        staged_a = dict(src_conv_b=conv_b, eighth_expand_b=bwd_b.eighth_expand_b)
        pushed_a = dict(eighth_conv_b=eighth_of(conv_b), sum_expand_b=sum_of(expand_b))
        scratch_a = dict(
            plane_conv_b=Plane.scratch(conv_b.shape),
            line_expand_b=Line.scratch(bwd_b.eighth_expand_b.shape),
        )
    bwd_a = fused(
        functools.partial(backward_a, pixel_count, direct),
        BACKWARD_A_CID,
        ins=dict(mask=mask, norm_a3=fwd_a.norm_a3, norm_a2=norm_a2),
        staged=dict(
            gro_b=bwd_b.gro_b,
            w_reduce=w_reduce_b,
            **staged_a,
            e_b3=fwd_b.e_b3,
            slope_a=fwd_a.slope_a,
            u_a3=fwd_a.u_a3,
            middle=fwd_a.middle,
            w_expand=w_expand_a,
            u_a2=deformed,
            h2_a=fwd_a.h2_a,
        ),
        outs=dict(gd=array(*small), sums_a3=table(channels), sums_a2=table(inner_width)),
        pushed=dict(
            **pushed_a,
            gw_reduce=array(cuts, inner_width, channels // cuts),
            gw_expand=natural,
            e_a3=array(*big),
        ),
        scratch=dict(
            **scratch_a,
            ex3=Exchange.scratch(channels),
            ex2=Exchange.scratch(inner_width),
            wide=pltpu.VMEM(big, F32),
            grad=pltpu.VMEM(small, F32),
            turned=turned,
        ),
    )
    staged_s, scratch_s = {}, {}
    pushed_s = dict(gw_deform=array(1, 9 * inner_width, inner_width))
    if direct:
        reduce_b, expand_a = eighths(bwd_a.gw_reduce), eighths(bwd_a.gw_expand)
        deform = array(images_axis, 8, 9 * inner_width // images_axis // 8, inner_width)
        staged_s = dict(
            src_reduce_b=reduce_b,
            src_expand_a=expand_a,
            eighth_conv_b=bwd_a.eighth_conv_b,
        )
        pushed_s = dict(
            sum_conv_b=sum_of(conv_b),
            own_reduce_b=own_of(reduce_b),
            own_expand_a=own_of(expand_a),
            own_deform=own_of(deform),
        )
        scratch_s = dict(
            gw_deform=vmem(deform),
            line_conv_b=Line.scratch(bwd_a.eighth_conv_b.shape),
            plane_reduce_b=Plane.scratch(reduce_b.shape),
            plane_expand_a=Plane.scratch(expand_a.shape),
            plane_deform=Plane.scratch(deform.shape),
            eighth_reduce_b=vmem(eighth_of(reduce_b)),
            eighth_expand_a=vmem(eighth_of(expand_a)),
            eighth_deform=vmem(eighth_of(deform)),
            line_reduce_b=LineSum.scratch(eighth_of(reduce_b).shape),
            line_expand_a=LineSum.scratch(eighth_of(expand_a).shape),
            line_deform=LineSum.scratch(eighth_of(deform).shape),
        )
    block = tile_pixels // 2
    bwd_s = fused(
        functools.partial(backward_s, pixel_count, direct),
        BACKWARD_S_CID,
        ins=dict(
            mask=mask,
            norm_a1=norm_a1,
            up=start.up,
            left=start.left,
            fr=start.fr,
            fc=start.fc,
        ),
        far=dict(samples=start.samples),
        staged=dict(
            gd=bwd_a.gd,
            **staged_s,
            w_deform=w_deform_a,
            rim=rim_flat,
            w_off=start.w_off,
            select=start.select,
            u_a1=start.u_a1,
        ),
        outs=dict(gr_a=array(*small), sums_a1=table(inner_width)),
        pushed=dict(**pushed_s, gw_off=array(cuts, 32, 9 * inner_width // cuts)),
        scratch=dict(
            **scratch_s,
            ex1=Exchange.scratch(inner_width),
            strips=Spill.scratch(1, tile_rows, tile_cols, inner_width) * images,
            spill=pltpu.VMEM((images, cells, inner_width), F32),
            table=pltpu.VMEM((WINDOW * win_cols, 3 * block), BF16),
            grads=pltpu.VMEM((inner_width, 3 * block), BF16),
            turned=turned,
            grad_row=pltpu.VMEM(taps_shape, F32),
            grad_col=pltpu.VMEM(taps_shape, F32),
            on_cells=pltpu.VMEM((288, cells), BF16),
            gw_off_sum=pltpu.VMEM((288, inner_width), F32),
            sample_slots=pltpu.VMEM((3, inner_width, pixels), BF16),
            sample_sems=pltpu.SemaphoreType.DMA((3,)),
            grad=pltpu.VMEM(small, F32),
        ),
    )
    staged_l, pushed_l, scratch_l = {}, {}, {}
    if direct:
        reduce_a = array(images_axis, 8, inner_width // 8, channels // cuts)
        staged_l = dict(
            own_reduce_b=bwd_s.own_reduce_b,
            own_expand_a=bwd_s.own_expand_a,
            own_deform=bwd_s.own_deform,
            gw_off=bwd_s.gw_off,
        )
        pushed_l = dict(
            sum_reduce_b=sum_of(reduce_b),
            sum_expand_a=sum_of(expand_a),
            sum_deform=sum_of(deform),
            sum_reduce_a=sum_of(reduce_a),
        )
        scratch_l = dict(
            gw_reduce=vmem(reduce_a),
            small=SmallSum.scratch(bwd_s.gw_off.shape),
            gather_reduce_b=Gather.scratch(reduce_b.shape),
            gather_expand_a=Gather.scratch(expand_a.shape),
            gather_deform=Gather.scratch(deform.shape),
            plane_reduce_a=Plane.scratch(reduce_a.shape),
            eighth_reduce_a=vmem(eighth_of(reduce_a)),
            line_reduce_a=Line.scratch(eighth_of(reduce_a).shape),
        )
        outs_l = dict(sum_off=array(*bwd_s.gw_off.shape[1:], dtype=F32))
    else:
        pushed_l = dict(gw_reduce=array(cuts, inner_width, channels // cuts))
        outs_l = {}
    end = fused(
        functools.partial(last, direct),
        LAST_CID,
        ins={},
        staged=dict(
            gr_a=bwd_s.gr_a, feature=feature, **staged_l, w_reduce=w_reduce_a, e_a3=bwd_a.e_a3
        ),
        outs=outs_l,
        pushed=dict(**pushed_l, grad_in=array(*big)),
        scratch=dict(**scratch_l, turned=turned),
    )
    sums_a = [bwd_s.sums_a1, bwd_a.sums_a2, bwd_a.sums_a3]
    sums_b = [bwd_b.sums_b1, bwd_b.sums_b2, fwd_b.sums_b3]
    norms_a = [norm_a1, norm_a2, fwd_a.norm_a3]
    norms_b = [fwd_a.norm_b1, fwd_b.norm_b2, fwd_b.norm_b3]
    if direct:
        sums = [
            bwd_s.sum_conv_b,
            end.sum_reduce_b,
            end.sum_reduce_a,
            bwd_a.sum_expand_b,
            end.sum_expand_a,
            end.sum_deform,
            end.sum_off,
        ]
    else:

        def over_devices(grad, dim):
            part = lax.psum_scatter(grad, IMG, scatter_dimension=dim, tiled=True)
            return lax.psum(part, (ROW, COL))

        turned_grads = (bwd_b.gw_conv, bwd_a.gw_reduce, end.gw_reduce)
        sums = [over_devices(g[0], 1) for g in turned_grads]
        sums += [over_devices(g[0], 0) for g in (bwd_b.gw_expand, bwd_a.gw_expand)]
        sums.append(over_devices(bwd_s.gw_deform[0], 0))
        sums = [g.reshape(8, -1, g.shape[1]) for g in sums]
        sums.append(over_devices(bwd_s.gw_off[0], 1).astype(F32))
    share = inner_width // images_axis
    long_share, wide_share = 9 * share, channels // images_axis
    shapes = [
        (long_share, inner_width),
        (wide_share, inner_width),
        (wide_share, inner_width),
        (share, channels),
        (share, channels),
        (long_share, inner_width),
        (18, long_share),
    ]
    vectors = ((2 * inner_width + channels) // 128, 128)
    shapes += [vectors] * 8
    operands = sums + sums_a + sums_b + norms_a + norms_b + [fwd_b.feature_out, end.grad_in]
    results = [array(*shape, dtype=F32) for shape in shapes]
    anywhere = pl.BlockSpec(memory_space=pl.ANY)
    results = pl.pallas_call(
        functools.partial(finish_kernel, unbias, len(operands)),
        out_shape=results + [array(*big)] * 2,
        in_specs=[anywhere] * len(operands),
        out_specs=[anywhere] * (len(shapes) + 2),
        scratch_shapes=[vmem(v) for v in operands + results]
        + [pltpu.SemaphoreType.DMA((len(operands),)), pltpu.SemaphoreType.DMA((17,))],
        compiler_params=pltpu.CompilerParams(vmem_limit_bytes=VMEM_LIMIT),
    )(*operands)
    conv_b, reduce_b, reduce_a, expand_b, expand_a, deform_a, offset_a = results[:7]
    scale_sums_a, shift_sums_a, scale_sums_b, shift_sums_b, mean_a, var_a, mean_b, var_b = (
        v.reshape(-1) for v in results[7:15]
    )
    return (
        results[15].reshape(feature_in.shape),
        results[16].reshape(feature_in.shape),
        reduce_a,
        offset_a.T,
        deform_a,
        expand_a,
        scale_sums_a,
        shift_sums_a,
        mean_a,
        var_a,
        reduce_b,
        conv_b,
        expand_b,
        scale_sums_b,
        shift_sums_b,
        mean_b,
        var_b,
    )


def solution(mesh):
    tiles = P(IMG, ROW, COL, None)
    in_specs = (tiles, P(IMG), tiles) + (P(),) * 11 + (tiles,)
    shares = P(IMG, None)
    out_specs = (tiles, tiles) + (shares,) * 4 + (P(),) * 4 + (shares,) * 3 + (P(),) * 4
    return jax.shard_map(body, mesh=mesh, in_specs=in_specs, out_specs=out_specs, check_vma=False)
```

```python
import functools
import types

import jax
import jax.numpy as jnp
import numpy as np
from jax import lax
from jax.experimental import pallas as pl
from jax.experimental.pallas import tpu as pltpu
from jax.sharding import PartitionSpec as P

LONG = 64
SHORT = 44
BOUND = 4
EPSILON = 1e-05
IMG, ROW, COL = "img", "row", "col"
MESH = pl.DeviceIdType.MESH
VMEM = pl.BlockSpec(memory_space=pltpu.VMEM)
VMEM_LIMIT = 60 * 1024 * 1024
F32 = jnp.float32
BF16 = jnp.bfloat16
REACH = BOUND + 3
PAD = 8
HALF = 16
FIRST_CID, FORWARD_CID, BACKWARD_B_CID, BACKWARD_A_CID, BACKWARD_S_CID, LAST_CID = range(6)


def group_of(axes):
    sizes = [lax.axis_size(a) for a in axes]
    total = int(np.prod(sizes))
    place = lax.axis_index(axes[0])
    for axis, size in zip(axes[1:], sizes[1:]):
        place = place * size + lax.axis_index(axis)

    def device(step):
        spot = lax.rem(place + step, total)
        coords = {}
        for axis, size in zip(reversed(axes), reversed(sizes)):
            coords[axis] = lax.rem(spot, size)
            spot = spot // size
        return coords

    return place, total, device


PLANE = (ROW, COL)
LINE = (IMG,)


def gather_start(axes, slots, send_sem, recv_sem):
    _, total, device = group_of(axes)
    for step in range(1, total):
        pltpu.make_async_remote_copy(
            src_ref=slots.at[0],
            dst_ref=slots.at[step],
            send_sem=send_sem,
            recv_sem=recv_sem,
            device_id=device(step),
            device_id_type=MESH,
        ).start()


def gather_wait(axes, slots, sem):
    _, total, _ = group_of(axes)
    others = slots.at[pl.ds(1, total - 1)]
    pltpu.make_async_copy(others, others, sem).wait()


def in_order(axes, slots):
    place, total, _ = group_of(axes)
    return [slots[lax.rem(place - spot + total, total)] for spot in range(total)]


def halo_peers():
    row, rows, col = lax.axis_index(ROW), lax.axis_size(ROW), lax.axis_index(COL)
    return row, rows, col, {COL: 1 - col}, {ROW: row - 1}, {ROW: row + 1}


BLOCK_ROWS = 8
SPAN = 17
WINDOW = 3 * BLOCK_ROWS


def tap_span(group, cols):
    first = 2 + 2 * group
    start = first * cols // 128 * 128
    stop = -(-(first + SPAN) * cols // 128) * 128
    return first, start, stop


def tap_weights(tap, block, cols, up_ref, left_ref, fr_ref, fc_ref, image=0, lanes=slice(None)):
    up, left, fr, fc = (
        ref[image, tap : tap + 1, lanes] for ref in (up_ref, left_ref, fr_ref, fc_ref)
    )
    up = up - block * BLOCK_ROWS
    pixels = up.shape[1]

    def pair(size, at, frac):
        ids = lax.broadcasted_iota(jnp.int32, (size, pixels), 0)
        first, second = ids == at, ids == at + 1
        value = jnp.where(first, 1.0 - frac, jnp.where(second, frac, 0.0))
        slope = jnp.where(second, 1.0, jnp.where(first, -1.0, 0.0))
        return value, slope

    return pair(WINDOW, up, fr) + pair(cols, left, fc)


def write_table(table, lane, row_w, col_w, group, cols):
    first, start, stop = tap_span(group, cols)
    pixels = row_w.shape[1]
    low = start // cols
    high = -(-stop // cols)
    for r in range(low, min(high, WINDOW)):
        table[r * cols : (r + 1) * cols, lane : lane + pixels] = (
            row_w[r : r + 1, :] * col_w
        ).astype(BF16)


def build_shifted(rim_ref, shifted):
    images, rows, cols, width = rim_ref.shape
    col = lax.axis_index(COL)
    tile = cols - HALF

    def fill(first):
        def one_row(k, carry):
            for n in range(images):
                line = rim_ref[n, k].astype(F32)
                none = jnp.zeros((2, width), F32)
                for d in range(3):
                    at = first + 2 * (d - 1)
                    if at < 0:
                        part = jnp.concatenate([none, line[: tile - 2]], axis=0)
                    elif at + tile > cols:
                        part = jnp.concatenate([line[at:], none], axis=0)
                    else:
                        part = line[at : at + tile]
                    shifted[n, k, :, d * width : (d + 1) * width] = part.astype(BF16)
            return carry

        lax.fori_loop(0, rows, one_row, 0)

    @pl.when(col == 0)
    def _():
        fill(0)

    @pl.when(col == 1)
    def _():
        fill(HALF)


def conv_product(shifted, w_ref, o_ref):
    images, rows, cols, width3 = shifted.shape
    tile_rows = rows - 4
    pixels = tile_rows * cols
    for n in range(images):
        total = None
        for i in range(3):
            taps = shifted[n, 2 * i : 2 * i + tile_rows].reshape(pixels, width3)
            term = jnp.dot(taps, w_ref[i * width3 : (i + 1) * width3, :], preferred_element_type=F32)
            total = term if total is None else total + term
        o_ref[n * pixels : (n + 1) * pixels, :] = total


def conv_weight_product(turned, shifted, gw_ref, i):
    images, rows, cols, width3 = shifted.shape
    tile_rows = rows - 4
    pixels = tile_rows * cols
    total = None
    for n in range(images):
        taps = shifted[n, 2 * i : 2 * i + tile_rows].reshape(pixels, width3)
        term = jnp.dot(turned[:, n * pixels : (n + 1) * pixels], taps, preferred_element_type=F32)
        total = term if total is None else total + term
    put_lanes(gw_ref, i * width3, total)


def unconv_product(shifted, w_ref, o_ref):
    images, rows, cols, width3 = shifted.shape
    width = width3 // 3
    tile_rows = rows - 4
    pixels = tile_rows * cols
    for n in range(images):
        total = None
        for tap in range(9):
            i, d = 2 - tap // 3, 2 - tap % 3
            grads = shifted[n, 2 * i : 2 * i + tile_rows, :, d * width : (d + 1) * width]
            term = lax.dot_general(
                grads.reshape(pixels, width),
                w_ref[tap * width : (tap + 1) * width, :],
                (((1,), (1,)), ((), ())),
                preferred_element_type=F32,
            )
            total = term if total is None else total + term
        o_ref[n * pixels : (n + 1) * pixels, :] = total


def halves(width):
    first = -(-width // 256) * 128
    return ((0, first), (first, width - first)) if first < width else ((0, width),)


def remote(src, dst, send, recv, device):
    return pltpu.make_async_remote_copy(
        src_ref=src, dst_ref=dst, send_sem=send, recv_sem=recv, device_id=device, device_id_type=MESH
    )


def arrival(ref, sem):
    return pltpu.make_async_copy(ref, ref, sem)


class Plane:
    @staticmethod
    def scratch(shape):
        images, _, rows, width = shape
        count = len(halves(width))
        return [
            pltpu.VMEM((images, 4, rows, width), BF16),
            pltpu.VMEM((images, 2, rows, width), BF16),
            pltpu.SemaphoreType.DMA((count, 3)),
            pltpu.SemaphoreType.DMA((count, 3)),
        ]

    def __init__(self, src, eighth, refs, part):
        half, quarter, send, recv = refs
        lanes = pl.ds(*halves(src.shape[-1])[part])
        self.src, self.half, self.quarter = (
            ref.at[:, :, :, lanes] for ref in (src, half, quarter)
        )
        self.eighth = eighth.at[:, :, lanes]
        self.images = src.shape[0]
        self.send, self.recv = [send.at[part, k] for k in range(3)], [recv.at[part, k] for k in range(3)]
        self.x_first = part == 0
        row, col = lax.axis_index(ROW), lax.axis_index(COL)
        bits = (lax.rem(row, 2), row // 2)
        peers = ({ROW: row + 1 - 2 * bits[0]}, {ROW: row + 2 - 4 * bits[1]})
        order = (0, 1) if self.x_first else (1, 0)
        self.a, self.b = (bits[k] for k in order)
        self.first, self.second = (peers[k] for k in order)
        self.mine, self.pair, self.other = 4 * col, {COL: 1 - col}, 4 * (1 - col)

    def spot(self, bit, free):
        return bit + 2 * free if self.x_first else 2 * bit + free

    def steps(self):
        return [self.to_pair, self.to_first, self.to_second, self.done]

    def to_pair(self):
        src = self.src.at[:, pl.ds(self.other, 4)]
        remote(src, self.half, self.send[0], self.recv[0], self.pair).start()

    def to_first(self):
        arrival(self.half, self.recv[0]).wait()

        def add(i, carry):
            for s in range(4):
                own = self.src[i, self.mine + s].astype(F32)
                self.half[i, s] = (own + self.half[i, s].astype(F32)).astype(BF16)
            return carry

        lax.fori_loop(0, self.images, add, 0)
        for k in range(2):
            src = self.half.at[:, self.spot(1 - self.a, k)]
            remote(src, self.quarter.at[:, k], self.send[1], self.recv[1], self.first).start()

    def to_second(self):
        arrival(self.quarter, self.recv[1]).wait()

        def add(i, carry):
            for k in range(2):
                own = self.half[i, self.spot(self.a, k)].astype(F32)
                self.quarter[i, k] = (own + self.quarter[i, k].astype(F32)).astype(BF16)
            return carry

        lax.fori_loop(0, self.images, add, 0)
        src = self.quarter.at[:, 1 - self.b]
        remote(src, self.eighth, self.send[2], self.recv[2], self.second).start()

    def done(self):
        arrival(self.eighth, self.recv[2]).wait()

        def add(i, carry):
            own = self.quarter[i, self.b].astype(F32)
            self.eighth[i] = (own + self.eighth[i].astype(F32)).astype(BF16)
            return carry

        lax.fori_loop(0, self.images, add, 0)
        arrival(self.half, self.send[0]).wait()
        arrival(self.quarter, self.send[1]).wait()
        arrival(self.eighth, self.send[2]).wait()


class LineSum:
    @staticmethod
    def scratch(shape):
        sems = pltpu.SemaphoreType.DMA((len(halves(shape[-1])),))
        return [pltpu.VMEM(shape, BF16), sems, sems]

    def __init__(self, eighth, own, refs, part):
        line, send, recv = refs
        lanes = pl.ds(*halves(eighth.shape[-1])[part])
        self.eighth, self.line, self.own = eighth.at[:, :, lanes], line.at[:, :, lanes], own.at[:, lanes]
        self.images, self.img = eighth.shape[0], lax.axis_index(IMG)
        self.send, self.recv = send.at[part], recv.at[part]

    def steps(self):
        return [self.to_line, self.done]

    def to_line(self):
        for j in range(1, self.images):
            there = lax.rem(self.img + j, self.images)
            src = self.eighth.at[there]
            remote(src, self.line.at[j], self.send, self.recv, {IMG: there}).start()

    def done(self):
        arrived = self.line.at[pl.ds(1, self.images - 1)]
        arrival(arrived, self.recv).wait()
        total = self.eighth[self.img].astype(F32)
        for j in range(1, self.images):
            total = total + self.line[j].astype(F32)
        self.own[...] = total.astype(BF16)
        arrival(arrived, self.send).wait()


class Gather:
    @staticmethod
    def scratch(shape):
        sems = pltpu.SemaphoreType.DMA((len(halves(shape[-1])), 2))
        return [sems, sems]

    def __init__(self, own, out, refs, part):
        send, recv = refs
        lanes = pl.ds(*halves(out.shape[-1])[part])
        self.own, self.out = own.at[:, lanes], out.at[:, :, lanes]
        self.send, self.recv = [send.at[part, k] for k in range(2)], [recv.at[part, k] for k in range(2)]
        self.row, col = lax.axis_index(ROW), lax.axis_index(COL)
        self.mine, self.pair = 4 * col, {COL: 1 - col}

    def steps(self):
        return [self.to_rows, self.to_pair, self.done]

    def to_rows(self):
        spot = self.out.at[self.mine + self.row]
        self.out[self.mine + self.row] = self.own[...]
        for j in range(1, 4):
            there = lax.rem(self.row + j, 4)
            remote(spot, spot, self.send[0], self.recv[0], {ROW: there}).start()

    def to_pair(self):
        arrival(self.out.at[pl.ds(0, 3)], self.recv[0]).wait()
        four = self.out.at[pl.ds(self.mine, 4)]
        remote(four, four, self.send[1], self.recv[1], self.pair).start()

    def done(self):
        four = self.out.at[pl.ds(0, 4)]
        arrival(four, self.recv[1]).wait()
        arrival(self.out.at[pl.ds(0, 3)], self.send[0]).wait()
        arrival(four, self.send[1]).wait()


class Line:
    @staticmethod
    def scratch(shape):
        return [pltpu.VMEM(shape[1:], BF16)] + LineSum.scratch(shape) + Gather.scratch(shape)

    def __init__(self, eighth, out, refs, part):
        own = refs[0]
        self.sum = LineSum(eighth, own, refs[1:4], part)
        self.gather = Gather(own, out, refs[4:], part)

    def steps(self):
        return [self.sum.to_line, self.to_rows, self.gather.to_pair, self.gather.done]

    def to_rows(self):
        self.sum.done()
        self.gather.to_rows()


class SmallSum:
    @staticmethod
    def scratch(shape):
        sizes = [lax.axis_size(IMG), lax.axis_size(ROW) * lax.axis_size(COL)]
        return [pltpu.VMEM((size,) + shape[1:], BF16) for size in sizes] + [
            pltpu.SemaphoreType.DMA((2,)),
            pltpu.SemaphoreType.DMA((2,)),
        ]

    def __init__(self, src, out, refs):
        self.src, self.out = src, out
        self.slots1, self.slots2, self.send, self.recv = refs

    def steps(self):
        return [self.to_line, self.to_plane, self.done]

    def to_line(self):
        here, total, _ = group_of(LINE)
        self.slots1[0] = self.src[here]
        for j in range(1, total):
            there = lax.rem(here + j, total)
            remote(
                self.src.at[there], self.slots1.at[j], self.send.at[0], self.recv.at[0], {IMG: there}
            ).start()

    def to_plane(self):
        gather_wait(LINE, self.slots1, self.recv.at[0])
        total = added([p.astype(F32) for p in in_order(LINE, self.slots1)])
        self.slots2[0] = total.astype(BF16)
        gather_start(PLANE, self.slots2, self.send.at[1], self.recv.at[1])

    def done(self):
        gather_wait(PLANE, self.slots2, self.recv.at[1])
        self.out[...] = added([p.astype(F32) for p in in_order(PLANE, self.slots2)])
        gather_wait(LINE, self.slots1, self.send.at[0])
        gather_wait(PLANE, self.slots2, self.send.at[1])


class Jobs:
    def __init__(self):
        self.queue = []

    def add(self, *jobs):
        lists = [job.steps() for job in jobs]
        for k in range(max(len(steps) for steps in lists)):
            self.queue += [steps[k] for steps in lists if k < len(steps)]

    def tick(self, count=1):
        for _ in range(min(count, len(self.queue))):
            self.queue.pop(0)()

    def finish(self):
        self.tick(len(self.queue))


def plane_jobs(src, eighth, refs):
    return [Plane(src, eighth, refs, part) for part in range(len(halves(src.shape[-1])))]


def part_jobs(kind, first, second, refs):
    return [kind(first, second, refs, part) for part in range(len(halves(first.shape[-1])))]


def line_jobs(eighth, out, refs):
    return [Line(eighth, out, refs, part) for part in range(len(halves(out.shape[-1])))]


STEP = 32
PIECE = 256
CHUNK = 256


class Refs:
    FLYING = 6 * 1024 * 1024

    def __init__(self):
        self.loads, self.stores, self.queue, self.flying = {}, {}, [], {}

    def load(self, ref, copy):
        self.loads[id(ref)] = copy
        self.queue.append((id(ref), int(np.prod(ref.shape)) * ref.dtype.itemsize))

    def start_loads(self, until=None):
        while self.queue:
            if until is None and sum(self.flying.values()) >= self.FLYING:
                return
            if until is not None and until in self.flying:
                return
            key, size = self.queue.pop(0)
            self.loads[key].start()
            self.flying[key] = size

    def ready(self, *refs):
        for ref in refs:
            self.start_loads(id(ref))
            self.loads.pop(id(ref)).wait()
            self.flying.pop(id(ref))
            self.start_loads()

    def push(self, *refs):
        for ref in refs:
            self.stores[id(ref)].start()

    def pushed(self, *refs):
        for ref in refs:
            self.stores.pop(id(ref)).wait()

    def flush(self):
        for copy in self.stores.values():
            copy.wait()


def fused(work, cid, ins, staged, outs, pushed, scratch, smem={}, far={}, far_outs={}):
    loaded, stored = {**ins, **staged}, {**outs, **pushed}
    sizes = (len(loaded), len(stored))

    def kernel(*refs):
        r = Refs()
        refs = list(refs)

        def take(count):
            taken = refs[:count]
            del refs[:count]
            return taken

        for key, ref in zip((*smem, *far), take(len(smem) + len(far))):
            setattr(r, key, ref)
        in_raw, out_raw = (take(count) for count in sizes)
        for key, ref in zip(far_outs, take(len(far_outs))):
            setattr(r, key, ref)
        for key, shape in scratch.items():
            setattr(r, key, take(len(shape)) if isinstance(shape, list) else take(1)[0])
        in_bufs, out_bufs = (take(count) for count in sizes)
        in_sems, out_sems = take(2)
        for keys, bufs in ((loaded, in_bufs), (stored, out_bufs)):
            for key, buf in zip(keys, bufs):
                setattr(r, key, buf)
        for k, (raw, buf) in enumerate(zip(in_raw, in_bufs)):
            r.load(buf, pltpu.make_async_copy(raw, buf, in_sems.at[k]))
        for k, (raw, buf) in enumerate(zip(out_raw, out_bufs)):
            r.stores[id(buf)] = pltpu.make_async_copy(buf, raw, out_sems.at[k])
        r.start_loads()
        signal_all()
        r.ready(*in_bufs[: len(ins)])
        work(r)
        r.push(*out_bufs[: len(outs)])
        r.flush()

    flat = []
    for shape in scratch.values():
        flat += shape if isinstance(shape, list) else [shape]
    flat += [pltpu.VMEM(a.shape, a.dtype) for a in (*loaded.values(), *stored.values())]
    flat += [pltpu.SemaphoreType.DMA((count,)) for count in sizes]
    anywhere, scalars = pl.BlockSpec(memory_space=pl.ANY), pl.BlockSpec(memory_space=pltpu.SMEM)
    result = pl.pallas_call(
        kernel,
        out_shape=[*stored.values(), *far_outs.values()],
        in_specs=[scalars] * len(smem) + [anywhere] * (len(far) + sizes[0]),
        out_specs=[anywhere] * (sizes[1] + len(far_outs)),
        scratch_shapes=flat,
        compiler_params=pltpu.CompilerParams(
            collective_id=cid, has_side_effects=True, vmem_limit_bytes=VMEM_LIMIT
        ),
    )(*smem.values(), *far.values(), *loaded.values())
    return types.SimpleNamespace(**dict(zip((*stored, *far_outs), result)))


def signal_all():
    barrier = pltpu.get_barrier_semaphore()
    for axes in (PLANE, LINE):
        _, total, device = group_of(axes)
        for step in range(1, total):
            pl.semaphore_signal(barrier, inc=1, device_id=device(step), device_id_type=MESH)


def wait_all():
    count = sum(group_of(axes)[1] - 1 for axes in (PLANE, LINE))
    pl.semaphore_wait(pltpu.get_barrier_semaphore(), count)


def added(parts):
    return functools.reduce(lambda a, b: a + b, parts)


class Exchange:
    @staticmethod
    def scratch(width):
        rows = 2 * width // 128
        sizes = [int(np.prod([lax.axis_size(a) for a in axes])) for axes in (PLANE, LINE)]
        return [
            pltpu.VMEM((sizes[0], rows, 128), F32),
            pltpu.VMEM((sizes[1], rows, 128), F32),
            pltpu.VMEM((rows, 128), F32),
            pltpu.SemaphoreType.DMA((2,)),
            pltpu.SemaphoreType.DMA((2,)),
        ]

    def __init__(self, refs):
        self.slots1, self.slots2, self.out, self.send, self.recv = refs
        self.half = self.out.shape[0] // 2

    def put(self, first, second):
        for k in range(self.half):
            self.slots1[0, k : k + 1, :] = first[:, 128 * k : 128 * (k + 1)]
            self.slots1[0, self.half + k : self.half + k + 1, :] = second[:, 128 * k : 128 * (k + 1)]
        gather_start(PLANE, self.slots1, self.send.at[0], self.recv.at[0])

    def line(self):
        gather_start(LINE, self.slots2, self.send.at[1], self.recv.at[1])

    def middle_sums(self):
        gather_wait(PLANE, self.slots1, self.recv.at[0])
        self.slots2[0] = added(in_order(PLANE, self.slots1))
        self.line()

    def finish_sums(self):
        gather_wait(LINE, self.slots2, self.recv.at[1])
        self.out[...] = added(in_order(LINE, self.slots2))
        self.drain()

    def middle_stats(self, count_ref, plane_count):
        half = self.half
        gather_wait(PLANE, self.slots1, self.recv.at[0])
        parts = in_order(PLANE, self.slots1)
        total = added([p[:half] for p in parts])
        center = total / plane_count
        spread = added([p[half:] for p in parts])
        for spot, part in enumerate(parts):
            count = count_ref[spot : spot + 1, :]
            away = part[:half] / jnp.maximum(count, 1.0) - center
            spread = spread + count * (away * away)
        self.slots2[0, :half] = total
        self.slots2[0, half:] = spread
        self.line()

    def finish_stats(self, plane_count):
        half = self.half
        total_count = plane_count * lax.axis_size(IMG)
        gather_wait(LINE, self.slots2, self.recv.at[1])
        parts = in_order(LINE, self.slots2)
        center = added([p[:half] for p in parts]) / total_count
        spread = added([p[half:] for p in parts])
        for part in parts:
            away = part[:half] / plane_count - center
            spread = spread + plane_count * (away * away)
        self.out[:half] = center
        self.out[half:] = spread / total_count
        self.drain()

    def drain(self):
        gather_wait(PLANE, self.slots1, self.send.at[0])
        gather_wait(LINE, self.slots2, self.send.at[1])

    def rows(self):
        out = self.out[...]
        first = [out[k : k + 1] for k in range(self.half)]
        second = [out[self.half + k : self.half + k + 1] for k in range(self.half)]
        return jnp.concatenate(first, axis=1), jnp.concatenate(second, axis=1)


class Halo:
    scratch = [pltpu.SemaphoreType.DMA((5,)), pltpu.SemaphoreType.DMA((5,))]

    def __init__(self, pad, reach, tile, window, sems, image=None):
        if image is not None:
            tile, window = (ref.at[pl.ds(image, 1)] for ref in (tile, window))
        self.row, self.rows, col, pair, above, below = halo_peers()
        self.pad, self.reach, self.tile, self.window = pad, reach, tile, window
        self.tile_rows, self.tile_cols = tile.shape[1], tile.shape[2]
        self.own = own = pl.ds(pl.multiple_of(HALF * col, HALF), self.tile_cols)
        spot = pl.ds(pl.multiple_of(2 * HALF * col, HALF), HALF)
        side = pl.ds(pl.multiple_of(HALF * (1 - col), HALF), HALF)
        mid = pl.ds(HALF, HALF)
        upper = pl.ds(pad - reach, reach)
        lower = pl.ds(pad + self.tile_rows, reach)
        send, recv = sems

        def copy(src, dst, k, device):
            return pltpu.make_async_remote_copy(
                src_ref=src,
                dst_ref=dst,
                send_sem=send.at[k],
                recv_sem=recv.at[k],
                device_id=device,
                device_id_type=MESH,
            )

        w = window
        self.to_pair = copy(
            tile.at[:, :, side], w.at[:, pl.ds(pad, self.tile_rows), spot], 0, pair
        )
        self.up = copy(tile.at[:, pl.ds(0, reach)], w.at[:, lower, own], 1, above)
        self.down = copy(
            tile.at[:, pl.ds(self.tile_rows - reach, reach)], w.at[:, upper, own], 2, below
        )
        self.from_below = copy(w.at[:, lower, mid], w.at[:, lower, spot], 3, pair)
        self.from_above = copy(w.at[:, upper, mid], w.at[:, upper, spot], 4, pair)

    def blank(self):
        window, pad, reach, tile_rows = self.window, self.pad, self.reach, self.tile_rows
        zero = jnp.zeros((window.shape[0],) + window.shape[2:], window.dtype)

        def fill(first, last):
            for k in range(first, last):
                window[:, k] = zero

        fill(0, pad - reach)
        fill(pad + tile_rows + reach, 2 * pad + tile_rows)

        @pl.when(self.row == 0)
        def _():
            fill(pad - reach, pad)

        @pl.when(self.row == self.rows - 1)
        def _():
            fill(pad + tile_rows, pad + tile_rows + reach)

    def start(self):
        @pl.when(self.row > 0)
        def _():
            self.up.start()

        @pl.when(self.row < self.rows - 1)
        def _():
            self.down.start()

        self.to_pair.start()
        for n in range(self.tile.shape[0]):
            self.window[n, pl.ds(self.pad, self.tile_rows), self.own, :] = self.tile[n]

    def middle(self):
        @pl.when(self.row < self.rows - 1)
        def _():
            self.up.wait_recv()
            self.from_below.start()

        @pl.when(self.row > 0)
        def _():
            self.down.wait_recv()
            self.from_above.start()

    def finish(self):
        self.to_pair.wait()

        @pl.when(self.row < self.rows - 1)
        def _():
            self.down.wait_send()
            self.from_below.wait()

        @pl.when(self.row > 0)
        def _():
            self.up.wait_send()
            self.from_above.wait()


def gauss(x):
    bell = jnp.exp2(x * (x * -0.7213475204444817))
    d = 1.0 + (0.3275911 * 0.7071067811865476) * jnp.abs(x)
    t = pl.reciprocal(d, approx=True)
    t = t * (2.0 - d * t)
    poly = 0.5307027145 * t - 0.7265760135
    poly = poly * t + 0.7107068705
    poly = poly * t - 0.142248368
    poly = poly * t + 0.127414796
    tail = poly * (t * bell)
    return jnp.where(x < 0, tail, 1.0 - tail), bell * 0.3989422804014327


def wide(mask, width):
    return jnp.concatenate([mask] * (width // 128), axis=1)


def place(ref, i, lanes):
    if len(ref.shape) == 4:
        return (i // ref.shape[1], lax.rem(i, ref.shape[1]), slice(None), lanes)
    return (pl.ds(pl.multiple_of(i * STEP, STEP), STEP), lanes)


def by_rows(pixels, width, work, sums=0):
    pieces = [slice(l, l + PIECE) for l in range(0, width, PIECE)]

    def one(i, carry):
        out = []
        for k, lanes in enumerate(pieces):
            got = work(i, lanes)
            for j in range(sums):
                folded = jnp.sum(got[j].reshape(STEP // 8, 8, PIECE), axis=0)
                out.append(carry[k * sums + j] + folded)
        return tuple(out)

    start = tuple(jnp.zeros((8, PIECE), F32) for _ in range(sums * len(pieces)))
    final = lax.fori_loop(0, pixels // STEP, one, start)
    rows = []
    for j in range(sums):
        parts = [jnp.sum(final[k * sums + j], axis=0, keepdims=True) for k in range(len(pieces))]
        rows.append(jnp.concatenate(parts, axis=1))
    return rows


NORM_ROWS = 8


def norm_table(exchange, gain_ref, shift_ref, out_ref, first):
    mean, var = exchange.rows()
    lanes = slice(first, first + mean.shape[1])
    inv = lax.rsqrt(var + EPSILON)
    out_ref[...] = jnp.zeros_like(out_ref)
    out_ref[0:1, :] = mean
    out_ref[1:2, :] = inv
    out_ref[2:3, :] = inv * gain_ref[:, lanes]
    out_ref[3:4, :] = shift_ref[:, lanes]
    out_ref[4:5, :] = var


def normed(u_ref, norm, i, lanes):
    away = u_ref[place(u_ref, i, lanes)].astype(F32) - norm[0:1, lanes]
    return away * norm[2:3, lanes] + norm[3:4, lanes], away


def activate(u_ref, norm, mask, h_ref, residual=None, slope=None, keep=None):
    def work(i, lanes):
        x, _ = normed(u_ref, norm, i, lanes)
        if residual is not None:
            x = x + residual[place(residual, i, lanes)].astype(F32)
        below, bell = gauss(x)
        m = wide(mask[place(mask, i, slice(None))], PIECE)
        h_ref[place(h_ref, i, lanes)] = (x * below * m).astype(BF16)
        if slope is not None:
            slope[place(slope, i, lanes)] = ((below + x * bell) * m).astype(BF16)
        if keep is not None:
            keep[place(keep, i, lanes)] = u_ref[place(u_ref, i, lanes)].astype(BF16)

    by_rows(mask.shape[0], norm.shape[1], work)


def device_stats(u_ref, mask, count):
    pixels, width = u_ref.shape

    def total_of(i, lanes):
        m = wide(mask[place(mask, i, slice(None))], PIECE)
        return (u_ref[place(u_ref, i, lanes)] * m,)

    (total,) = by_rows(pixels, width, total_of, 1)
    center = total / jnp.maximum(wide(count, width), 1.0)

    def spread_of(i, lanes):
        m = wide(mask[place(mask, i, slice(None))], PIECE)
        away = u_ref[place(u_ref, i, lanes)] - center[:, lanes]
        return (away * away * m,)

    (spread,) = by_rows(pixels, width, spread_of, 1)
    return total, spread


def product(a_ref, w_ref, o_ref, turned=False):
    dims = (((1,), (1 if turned else 0,)), ((), ()))

    def one(i, carry):
        rows = pl.ds(pl.multiple_of(i * CHUNK, CHUNK), CHUNK)
        o_ref[rows, :] = lax.dot_general(
            a_ref[rows, :], w_ref[...], dims, preferred_element_type=F32
        )
        return carry

    lax.fori_loop(0, a_ref.shape[0] // CHUNK, one, 0)


def turn(a_ref, t_ref):
    def one(i, carry):
        rows = pl.ds(pl.multiple_of(i * CHUNK, CHUNK), CHUNK)
        t_ref[:, rows] = a_ref[rows, :].T
        return carry

    lax.fori_loop(0, a_ref.shape[0] // CHUNK, one, 0)


def put_lanes(ref, first, value):
    width = ref.shape[-1]
    at, stop = first, first + value.shape[1]
    while at < stop:
        cut = at // width
        until = min(stop, (cut + 1) * width)
        part = value[:, at - first : until - first].astype(ref.dtype)
        lanes = slice(at - cut * width, until - cut * width)
        if len(ref.shape) == 4:
            ref[cut, :, :, lanes] = part.reshape(ref.shape[1:3] + part.shape[1:])
        else:
            ref[cut, :, lanes] = part
        at = until


def weight_product(t_ref, b_ref, gw_ref):
    channels = b_ref.shape[1]
    for first in range(0, channels, 512):
        value = jnp.dot(t_ref[...], b_ref[:, first : first + 512], preferred_element_type=F32)
        if len(gw_ref.shape) == 4 and gw_ref.shape[-1] == channels:
            part = value.astype(gw_ref.dtype).reshape(gw_ref.shape[:3] + (512,))
            gw_ref[:, :, :, first : first + 512] = part
        else:
            put_lanes(gw_ref, first, value)


def put_rows(ref, first, value):
    if len(ref.shape) == 3:
        ref[0, first : first + value.shape[0], :] = value.astype(ref.dtype)
        return
    rows = ref.shape[2]
    at, stop = first, first + value.shape[0]
    while at < stop:
        eighth = at // rows
        until = min(stop, (eighth + 1) * rows)
        low, high = at - eighth * rows, until - eighth * rows
        part = value[at - first : until - first].astype(ref.dtype)
        ref[eighth // 8, eighth % 8, low:high, :] = part
        at = until


def norm_back(e_ref, u_ref, norm, sums, pixel_count, mask, out_ref):
    sum_grad, sum_unit = (s * (1.0 / pixel_count) for s in sums)

    def work(i, lanes):
        away = u_ref[place(u_ref, i, lanes)].astype(F32) - norm[0:1, lanes]
        unit = away * norm[1:2, lanes]
        e = e_ref[place(e_ref, i, lanes)].astype(F32)
        m = wide(mask[place(mask, i, slice(None))], PIECE)
        grad = norm[2:3, lanes] * (e - sum_grad[:, lanes] - unit * sum_unit[:, lanes]) * m
        out_ref[place(out_ref, i, lanes)] = grad.astype(BF16)

    by_rows(mask.shape[0], norm.shape[1], work)


def gelu_grad(e_ref, u_ref, norm, mask):
    def work(i, lanes):
        x, away = normed(u_ref, norm, i, lanes)
        below, bell = gauss(x)
        m = wide(mask[place(mask, i, slice(None))], PIECE)
        e = e_ref[place(e_ref, i, lanes)] * (below + x * bell) * m
        e_ref[place(e_ref, i, lanes)] = e
        return e, e * (away * norm[1:2, lanes])

    return by_rows(mask.shape[0], norm.shape[1], work, 2)


def put_sums(exchange, out_ref):
    first, second = exchange.rows()
    out_ref[...] = jnp.zeros_like(out_ref)
    out_ref[0:1, :] = first
    out_ref[1:2, :] = second
    return first, second


def order_taps(rows, width):
    to = lax.broadcasted_iota(jnp.int32, (rows, width), 0)
    at = lax.broadcasted_iota(jnp.int32, (rows, width), 1)
    picked = jnp.where(to < 16, 2 * to, 2 * (to - 16) + 1)
    real = lax.rem(to, 16) < 9
    return jnp.where(jnp.logical_and(at == picked, real), 1.0, 0.0)


def make_mask(r, tile_cols):
    row, col = lax.axis_index(ROW), lax.axis_index(COL)
    rows, cols = lax.axis_size(ROW), lax.axis_size(COL)
    images = r.orientation.shape[0]
    tile_rows = r.mask.shape[0] // images // tile_cols
    tall = [r.orientation[n].astype(F32) for n in range(images)]
    for n in range(images):

        def fill(i, carry, n=n):
            column = lax.broadcasted_iota(jnp.int32, (tile_cols, 128), 0) + col * tile_cols
            portrait = jnp.where(column < SHORT, 1.0, 0.0)
            line = jnp.zeros((tile_cols, 128), jnp.int32) + (row * tile_rows + i)
            landscape = jnp.where(line < SHORT, 1.0, 0.0)
            at = (n * tile_rows + i) * tile_cols
            r.mask[pl.ds(pl.multiple_of(at, tile_cols), tile_cols), :] = (
                landscape * (1.0 - tall[n]) + portrait * tall[n]
            )
            return carry

        lax.fori_loop(0, tile_rows, fill, 0)

    def count(row, col):
        return (
            jnp.clip(SHORT - row * tile_rows, 0, tile_rows) * tile_cols,
            jnp.clip(SHORT - col * tile_cols, 0, tile_cols) * tile_rows,
        )

    def fill_count(at, row, col):
        flat, upright = (c.astype(F32) for c in count(row, col))
        total = added([flat * (1.0 - t) + upright * t for t in tall])
        r.counts[at : at + 1, :] = jnp.zeros((1, 128), F32) + total

    r.counts[...] = jnp.zeros_like(r.counts)
    for k in range(rows * cols):
        fill_count(k, jnp.int32(k // cols), jnp.int32(k % cols))
    fill_count(8, row, col)


def make_corners(r, cols):
    images, _, pixels = r.up.shape
    tile_cols = cols - HALF
    order = order_taps(32, r.base.shape[1]).astype(BF16)
    tap = lax.broadcasted_iota(jnp.int32, (16, pixels), 0)
    pixel = lax.broadcasted_iota(jnp.int32, (16, pixels), 1)
    up0 = pixel // tile_cols + PAD + 2 * (tap // 3 - 1)
    left0 = lax.rem(pixel, tile_cols) + HALF * lax.axis_index(COL) + 2 * (lax.rem(tap, 3) - 1)
    for n in range(images):
        base = r.base[n * pixels : (n + 1) * pixels, :].astype(F32).astype(BF16)
        moved = lax.dot_general(
            order, base, (((1,), (1,)), ((), ())), preferred_element_type=F32
        ).astype(jnp.int32)
        r.up[n] = moved[:16] + up0
        r.left[n] = moved[16:] + left0


def first(plane_count, r):
    ex, ex2 = Exchange(r.ex1), Exchange(r.ex2)
    images, all_rows, cols, width = r.rim.shape
    halos = [Halo(PAD, REACH, r.tile, r.rim, r.halo[2 * n : 2 * n + 2], n) for n in range(images)]
    make_mask(r, cols - HALF)
    r.ready(r.feature, r.w_reduce)
    product(r.feature, r.w_reduce, r.u_a1)
    r.push(r.u_a1)
    total, spread = device_stats(r.u_a1, r.mask, r.counts[8:9, :])
    wait_all()
    ex.put(total, spread)
    make_corners(r, cols)
    ex.middle_stats(r.counts, plane_count)
    for halo in halos:
        halo.blank()
    order = order_taps(32, r.w_offset.shape[0]).astype(BF16)
    for tap in range(9):
        columns = r.w_offset[:, tap * width : (tap + 1) * width]
        r.w_off[32 * tap : 32 * tap + 32, :] = jnp.dot(
            order, columns, preferred_element_type=F32
        ).astype(BF16)
    ex.finish_stats(plane_count)
    norm_table(ex, r.scale, r.shift, r.norm_a1, 0)
    activate(r.u_a1, r.norm_a1, r.mask, r.tile)
    for halo in halos:
        halo.start()
    select_cells(r, cols)
    r.push(r.select)
    r.ready(r.w_deform)
    turn(r.w_deform, r.w_turned)
    for n, halo in enumerate(halos):
        if n == 0:
            halo.middle()
        halo.finish()
        for k in range(0, all_rows, 8):
            lines = r.rim[n, k : k + 8].reshape(8 * cols, width)
            r.rim_t[n, :, k * cols : (k + 8) * cols] = lines.T
        offset_fractions(r, cols, n)
        sample_units(r, cols, n, 0)
        if n + 1 < images:
            halos[n + 1].middle()
        sample_units(r, cols, n, 1)
    r.push(r.rim, r.fr, r.fc, r.samples, r.u_a2)
    total, spread = device_stats(r.u_a2, r.mask, r.counts[8:9, :])
    ex2.put(total, spread)
    ex2.middle_stats(r.counts, plane_count)
    ex2.finish_stats(plane_count)
    norm_table(ex2, r.scale, r.shift, r.norm_a2, width)


def offset_fractions(r, cols, n):
    _, width, cells = r.rim_t.shape
    column = lax.rem(lax.broadcasted_iota(jnp.int32, (32, cells), 1), cols)
    r.spread[...] = jnp.dot(r.w_off[...], r.rim_t[n], preferred_element_type=F32)
    total = None
    for tap in range(9):
        i, j = 2 * (tap // 3 - 1), 2 * (tap % 3 - 1)
        term = r.spread[32 * tap : 32 * tap + 32, :]
        shift = -(i * cols + j) % cells
        if shift:
            term = pltpu.roll(term, shift, axis=1)
        if j < 0:
            term = jnp.where(column >= -j, term, 0.0)
        if j > 0:
            term = jnp.where(column < cols - j, term, 0.0)
        total = term if total is None else total + term
    parts = []
    for _ in range(3):
        parts.append(total.astype(BF16))
        total = total - parts[-1].astype(F32)
    on_tile = lax.dot_general(
        jnp.concatenate(parts, axis=0),
        r.select[...],
        (((1,), (1,)), ((), ())),
        preferred_element_type=F32,
    )
    offsets = on_tile[:32] + on_tile[32:64] + on_tile[64:]
    fraction = 1.0 / (1.0 + jnp.exp(-offsets))
    r.fr[n] = fraction[:16]
    r.fc[n] = fraction[16:]


def sample_units(r, cols, n, b):
    block = r.table.shape[1]
    width = r.rim_t.shape[1]
    lanes = slice(b * block, (b + 1) * block)
    mine = slice((2 * n + b) * block, (2 * n + b + 1) * block)
    base = b * (BLOCK_ROWS * cols)
    for tap in range(9):
        row_w, _, col_w, _ = tap_weights(tap, b, cols, r.up, r.left, r.fr, r.fc, n, lanes)
        write_table(r.table, 0, row_w, col_w, tap // 3, cols)
        _, start, stop = tap_span(tap // 3, cols)
        cells = r.rim_t[n, :, base + start : base + stop]
        value = jnp.dot(cells, r.table[start:stop, :], preferred_element_type=F32)
        r.samples[tap * width : (tap + 1) * width, mine] = value.astype(BF16)
    deformed = jnp.dot(r.w_turned[...], r.samples[:, mine], preferred_element_type=F32)
    r.u_a2[mine, :] = deformed.T


def finish_kernel(unbias, count, *refs):
    ins, outs, rest = refs[:count], refs[count : count + 17], refs[count + 17 :]
    bufs, out_bufs, sems, out_sems = rest[:count], rest[count : count + 15], rest[-2], rest[-1]
    loads = [pltpu.make_async_copy(ins[k], bufs[k], sems.at[k]) for k in range(count)]
    stores = [pltpu.make_async_copy(out_bufs[k], outs[k], out_sems.at[k]) for k in range(15)]
    stores += [
        pltpu.make_async_copy(bufs[count - 2 + k], outs[15 + k], out_sems.at[15 + k]) for k in range(2)
    ]
    for load in loads:
        load.start()
    conv_b, reduce_b, reduce_a, expand_b, expand_a, deform, off = bufs[:7]
    tables = bufs[7:19]
    for load in loads[:7]:
        load.wait()
    for k, src in enumerate((expand_b, expand_a, deform)):
        rows = src.shape[1]
        for s in range(8):
            out_bufs[3 + k][s * rows : (s + 1) * rows, :] = src[s].astype(F32)
        stores[3 + k].start()
    for k, src in enumerate((conv_b, reduce_b, reduce_a)):
        eighth = src.shape[1]
        for s in range(0, 8, 2):
            rows = jnp.concatenate([src[s], src[s + 1]], axis=0).astype(F32)
            out_bufs[k][:, s * eighth : (s + 2) * eighth] = rows.T
        stores[k].start()
    for k in range(2):
        loads[count - 2 + k].wait()
        stores[15 + k].start()
    rest, total = off[...], None
    order = order_taps(32, 18).astype(BF16)
    for _ in range(3):
        part = rest.astype(BF16)
        rest = rest - part.astype(F32)
        term = lax.dot_general(order, part, (((0,), (0,)), ((), ())), preferred_element_type=F32)
        total = term if total is None else total + term
    out_bufs[6][...] = total
    for load in loads[7 : count - 2]:
        load.wait()
    for k in range(4):
        group, which = tables[3 * k : 3 * k + 3], out_bufs[7 + 2 * k : 9 + 2 * k]
        norms = k >= 2
        for out, row in zip(which, (0, 4) if norms else (1, 0)):
            at = 0
            for table in group:
                for first_lane in range(0, table.shape[1], 128):
                    value = table[row : row + 1, first_lane : first_lane + 128]
                    out[at : at + 1, :] = value * unbias if norms and row == 4 else value
                    at += 1
    for store in stores[6:15]:
        store.start()
    for store in stores:
        store.wait()


def forward(plane_count, r):
    ex_a3, ex_b1, ex_b2 = Exchange(r.ex_a3), Exchange(r.ex_b1), Exchange(r.ex_b2)
    ex_b3, ex_sums = Exchange(r.ex_b3), Exchange(r.ex_sums)
    halo = Halo(2, 2, r.tile, r.rim_b, r.halo)
    halo.blank()
    width = r.h2_a.shape[1]
    count = r.counts[8:9, :]

    def exchange(ex, u_ref):
        ex.put(*device_stats(u_ref, r.mask, count))
        ex.middle_stats(r.counts, plane_count)

    r.ready(r.u_a2)
    activate(r.u_a2, r.norm_a2, r.mask, r.h2_a)
    r.push(r.h2_a)
    r.ready(r.w_expand_a)
    product(r.h2_a, r.w_expand_a, r.wide)
    wait_all()
    exchange(ex_a3, r.wide)
    r.ready(r.feature, r.w_reduce)
    ex_a3.finish_stats(plane_count)
    norm_table(ex_a3, r.scale_a, r.shift_a, r.norm_a3, 2 * width)
    activate(r.wide, r.norm_a3, r.mask, r.middle, r.feature, r.slope_a, r.u_a3)
    r.push(r.middle, r.slope_a, r.u_a3)
    cotangent = pltpu.make_async_copy(r.cotangent, r.feature, r.far_sems.at[0])
    cotangent.start()
    product(r.middle, r.w_reduce, r.u_b1)
    r.push(r.u_b1)
    exchange(ex_b1, r.u_b1)
    ex_b1.finish_stats(plane_count)
    norm_table(ex_b1, r.scale_b, r.shift_b, r.norm_b1, 0)
    activate(r.u_b1, r.norm_b1, r.mask, r.tile)
    halo.start()
    halo.middle()
    halo.finish()
    r.push(r.rim_b)
    build_shifted(r.rim_b, r.shifted)
    r.ready(r.w_conv)
    conv_product(r.shifted, r.w_conv, r.u_b2)
    r.push(r.u_b2)
    exchange(ex_b2, r.u_b2)
    ex_b2.finish_stats(plane_count)
    norm_table(ex_b2, r.scale_b, r.shift_b, r.norm_b2, width)
    activate(r.u_b2, r.norm_b2, r.mask, r.h2_b)
    r.push(r.h2_b)
    r.ready(r.w_expand_b)
    product(r.h2_b, r.w_expand_b, r.wide)
    exchange(ex_b3, r.wide)
    cotangent.wait()
    r.pushed(r.slope_a, r.u_a3)
    e_b3, u_b3, norm = r.slope_a, r.u_a3, r.norm_b3
    ex_b3.finish_stats(plane_count)
    norm_table(ex_b3, r.scale_b, r.shift_b, norm, 2 * width)

    def work(i, lanes):
        x, away = normed(r.wide, norm, i, lanes)
        at = place(r.wide, i, lanes)
        u_b3[at] = r.wide[at].astype(BF16)
        x = x + r.middle[at].astype(F32)
        below, bell = gauss(x)
        m = wide(r.mask[place(r.mask, i, slice(None))], PIECE)
        r.feature_out[at] = (x * below * m).astype(BF16)
        e = (below + x * bell) * r.feature[at].astype(F32) * m
        e_b3[at] = e.astype(BF16)
        return e, e * (away * norm[1:2, lanes])

    sums = by_rows(r.wide.shape[0], r.wide.shape[1], work, 2)
    ex_sums.put(*sums)
    far = [
        pltpu.make_async_copy(e_b3, r.e_b3, r.far_sems.at[1]),
        pltpu.make_async_copy(u_b3, r.u_b3, r.far_sems.at[2]),
    ]
    for copy in far:
        copy.start()
    r.push(r.feature_out)
    ex_sums.middle_sums()
    ex_sums.finish_sums()
    put_sums(ex_sums, r.sums_b3)
    for copy in far:
        copy.wait()


def backward_b(pixel_count, direct, r):
    ex2, ex1 = Exchange(r.ex2), Exchange(r.ex1)
    halo = Halo(2, 2, r.tile, r.back_rim, r.halo)
    halo.blank()
    r.ready(r.e_b3, r.u_b3)
    sums = (r.sums_b3[0:1, :], r.sums_b3[1:2, :])
    norm_back(r.e_b3, r.u_b3, r.norm_b3, sums, pixel_count, r.mask, r.geo)
    r.ready(r.w_expand)
    product(r.geo, r.w_expand, r.grad, turned=True)
    r.ready(r.u_b2)
    sums = gelu_grad(r.grad, r.u_b2, r.norm_b2, r.mask)
    wait_all()
    ex2.put(*sums)
    r.ready(r.h2_b)
    turn(r.h2_b, r.turned)
    ex2.middle_sums()
    weight_product(r.turned, r.geo, r.gw_expand)
    jobs = Jobs()
    if direct:
        jobs.add(*plane_jobs(r.gw_expand, r.eighth_expand_b, r.plane_expand_b))
    else:
        r.push(r.gw_expand)
    jobs.tick(2)
    ex2.finish_sums()
    sums = put_sums(ex2, r.sums_b2)
    norm_back(r.grad, r.u_b2, r.norm_b2, sums, pixel_count, r.mask, r.tile)
    halo.start()
    tile_rows, tile_cols, width = r.tile.shape[1:]
    pixels = tile_rows * tile_cols
    for n in range(r.tile.shape[0]):
        for k in range(0, tile_rows, 8):
            at = n * pixels + k * tile_cols
            block = r.tile[n, k : k + 8].reshape(8 * tile_cols, width)
            r.turned[:, at : at + 8 * tile_cols] = block.T
    r.ready(r.rim_b)
    build_shifted(r.rim_b, r.shifted)
    conv_weight_product(r.turned, r.shifted, r.gw_conv, 0)
    halo.middle()
    jobs.tick(2)
    conv_weight_product(r.turned, r.shifted, r.gw_conv, 1)
    halo.finish()
    build_shifted(r.back_rim, r.back_shifted)
    r.ready(r.w_conv)
    unconv_product(r.back_shifted, r.w_conv, r.grad)
    r.ready(r.u_b1)
    sums = gelu_grad(r.grad, r.u_b1, r.norm_b1, r.mask)
    ex1.put(*sums)
    jobs.tick(2)
    ex1.middle_sums()
    conv_weight_product(r.turned, r.shifted, r.gw_conv, 2)
    r.push(r.gw_conv)
    jobs.finish()
    if direct:
        r.push(r.eighth_expand_b)
    ex1.finish_sums()
    sums = put_sums(ex1, r.sums_b1)
    norm_back(r.grad, r.u_b1, r.norm_b1, sums, pixel_count, r.mask, r.gro_b)


def backward_a(pixel_count, direct, r):
    ex3, ex2 = Exchange(r.ex3), Exchange(r.ex2)
    conv, line = Jobs(), Jobs()
    r.ready(r.gro_b, r.w_reduce)
    product(r.gro_b, r.w_reduce, r.wide, turned=True)
    wait_all()
    if direct:
        r.ready(r.src_conv_b, r.eighth_expand_b)
        conv.add(*plane_jobs(r.src_conv_b, r.eighth_conv_b, r.plane_conv_b))
        line.add(*line_jobs(r.eighth_expand_b, r.sum_expand_b, r.line_expand_b))
    conv.tick(2)
    line.tick(2)
    r.ready(r.e_b3, r.slope_a, r.u_a3)
    norm = r.norm_a3

    def work(i, lanes):
        at = place(r.wide, i, lanes)
        e = (r.wide[at] + r.e_b3[at].astype(F32)) * r.slope_a[at].astype(F32)
        r.e_a3[at] = e.astype(BF16)
        away = r.u_a3[at].astype(F32) - norm[0:1, lanes]
        return e, e * (away * norm[1:2, lanes])

    sums = by_rows(r.wide.shape[0], r.wide.shape[1], work, 2)
    ex3.put(*sums)
    conv.tick(2)
    r.push(r.e_a3)
    turn(r.gro_b, r.turned)
    ex3.middle_sums()
    r.ready(r.middle)
    weight_product(r.turned, r.middle, r.gw_reduce)
    r.push(r.gw_reduce)
    line.tick(2)
    ex3.finish_sums()
    sums = put_sums(ex3, r.sums_a3)
    norm_back(r.e_a3, r.u_a3, norm, sums, pixel_count, r.mask, r.e_b3)
    r.ready(r.w_expand)
    product(r.e_b3, r.w_expand, r.grad, turned=True)
    r.ready(r.u_a2)
    sums = gelu_grad(r.grad, r.u_a2, r.norm_a2, r.mask)
    ex2.put(*sums)
    conv.tick(2)
    line.tick(2)
    r.ready(r.h2_a)
    turn(r.h2_a, r.turned)
    ex2.middle_sums()
    weight_product(r.turned, r.e_b3, r.gw_expand)
    r.push(r.gw_expand)
    ex2.finish_sums()
    sums = put_sums(ex2, r.sums_a2)
    norm_back(r.grad, r.u_a2, r.norm_a2, sums, pixel_count, r.mask, r.gd)
    conv.finish()
    line.finish()
    if direct:
        r.push(r.eighth_conv_b, r.sum_expand_b)


def unsample(r, plan):
    width = r.rim.shape[2]
    cols = r.table.shape[0] // WINDOW
    pixels = r.up.shape[2] // 2
    r.spill[...] = jnp.zeros_like(r.spill)
    r.grad_row[...] = jnp.zeros_like(r.grad_row)
    r.grad_col[...] = jnp.zeros_like(r.grad_col)

    def unit(step, carry):
        n, block = step // 2, lax.rem(step, 2)
        lanes = pl.ds(pl.multiple_of(block * pixels, pixels), pixels)
        base = block * (BLOCK_ROWS * cols)
        grad_in = r.turned[:, pl.ds(pl.multiple_of(step * pixels, pixels), pixels)]
        for group in range(3):
            first, start, stop = tap_span(group, cols)
            cells = pl.ds(pl.multiple_of(base + start, 128), stop - start)
            for j in range(3):
                tap = 3 * group + j
                spot = slice(j * pixels, (j + 1) * pixels)
                row_w, row_s, col_w, col_s = tap_weights(
                    tap, block, cols, r.up, r.left, r.fr, r.fc, n, lanes
                )
                write_table(r.table, j * pixels, row_w, col_w, group, cols)
                grad = jnp.dot(
                    r.w_deform[tap * width : (tap + 1) * width, :],
                    grad_in,
                    preferred_element_type=F32,
                ).astype(BF16)
                r.grads[:, spot] = grad
                scores = jnp.dot(r.rim[n, cells, :], grad, preferred_element_type=F32)
                by_value = jnp.zeros((cols, pixels), F32)
                by_slope = jnp.zeros((cols, pixels), F32)
                for k in range(first, first + SPAN):
                    line = scores[k * cols - start : (k + 1) * cols - start]
                    by_value = by_value + line * row_w[k : k + 1, :]
                    by_slope = by_slope + line * row_s[k : k + 1, :]
                r.grad_row[n, tap : tap + 1, lanes] = jnp.sum(
                    by_slope * col_w, axis=0, keepdims=True
                )
                r.grad_col[n, tap : tap + 1, lanes] = jnp.sum(
                    by_value * col_s, axis=0, keepdims=True
                )
            r.spill[n, cells, :] += lax.dot_general(
                r.table[start:stop, :],
                r.grads[...],
                (((1,), (1,)), ((), ())),
                preferred_element_type=F32,
            )
            for turn_at in range(4):
                if 3 * turn_at + group in plan:

                    @pl.when(step == turn_at)
                    def _(slot=3 * turn_at + group):
                        plan[slot]()

        return carry

    lax.fori_loop(0, 4, unit, 0)


def select_cells(r, cols):
    off = HALF * lax.axis_index(COL)
    cells = r.select.shape[1]

    def fill(i, carry):
        ids = lax.broadcasted_iota(jnp.int32, (STEP, cells), 1)
        pixel = lax.broadcasted_iota(jnp.int32, (STEP, cells), 0)
        hit = ids == pixel + (i + PAD) * cols + off
        r.select[pl.ds(pl.multiple_of(i * STEP, STEP), STEP), :] = jnp.where(hit, 1.0, 0.0).astype(
            BF16
        )
        return carry

    lax.fori_loop(0, r.select.shape[0] // STEP, fill, 0)


def unoffset(r, n):
    images, cells, width = r.rim.shape
    cols = r.table.shape[0] // WINDOW
    column = lax.rem(lax.broadcasted_iota(jnp.int32, (32, cells), 1), cols)
    parts = []
    for grad, frac in ((r.grad_row, r.fr), (r.grad_col, r.fc)):
        f = frac[n]
        parts.append(grad[n] * f * (1.0 - f))
    go = jnp.concatenate(parts, axis=0).astype(BF16)
    on_tile = jnp.dot(go, r.select[...], preferred_element_type=F32)
    for tap in range(9):
        i, j = 2 * (tap // 3 - 1), 2 * (tap % 3 - 1)
        kept = on_tile
        if j < 0:
            kept = jnp.where(column >= -j, on_tile, 0.0)
        if j > 0:
            kept = jnp.where(column < cols - j, on_tile, 0.0)
        shift = (i * cols + j) % cells
        if shift:
            kept = pltpu.roll(kept, shift, axis=1)
        r.on_cells[32 * tap : 32 * tap + 32, :] = kept.astype(BF16)
    grad = jnp.dot(r.on_cells[...], r.rim[n], preferred_element_type=F32)
    if n == 0:
        r.gw_off_sum[...] = grad
    else:
        r.gw_off_sum[...] += grad
    for first in range(0, cells, 512):
        r.spill[n, first : first + 512, :] += lax.dot_general(
            r.on_cells[:, first : first + 512],
            r.w_off[...],
            (((0,), (0,)), ((), ())),
            preferred_element_type=F32,
        )
    if n == images - 1:
        for tap in range(9):
            put_lanes(r.gw_off, tap * width, r.gw_off_sum[32 * tap : 32 * tap + 32, :])


class Spill:
    @staticmethod
    def scratch(images, tile_rows, tile_cols, width):
        side = pltpu.VMEM((images, tile_rows + 2 * PAD, HALF, width), BF16)
        strip = pltpu.VMEM((images, REACH, tile_cols, width), BF16)
        sems = pltpu.SemaphoreType.DMA((3,))
        return [side, side, strip, strip, strip, strip, sems, sems]

    def __init__(self, spill, grad, cols, refs, image):
        self.spill, self.grad, self.cols = spill.at[pl.ds(image, 1)], grad, cols
        self.image = image
        self.side_out, self.side_in, self.up_out, self.down_out, self.up_in, self.down_in = refs[:6]
        send, recv = refs[6:]
        self.row, self.rows, col, pair, above, below = halo_peers()
        self.images, self.all_rows = self.side_out.shape[:2]
        self.tile_rows, self.tile_cols = self.all_rows - 2 * PAD, self.up_out.shape[2]
        self.off, self.away, self.near = HALF * col, 2 * HALF * (1 - col), HALF * (1 - col)
        self.side = remote(self.side_out, self.side_in, send.at[0], recv.at[0], pair)
        self.up = remote(self.up_out, self.down_in, send.at[1], recv.at[1], above)
        self.down = remote(self.down_out, self.up_in, send.at[2], recv.at[2], below)

    def cells(self, k, first, count):
        return pl.ds(pl.multiple_of(k * self.cols + first, HALF), count)

    def start(self):
        def cast(k, carry):
            for n in range(self.images):
                self.side_out[n, k] = self.spill[n, self.cells(k, self.away, HALF), :].astype(BF16)
            return carry

        lax.fori_loop(0, self.all_rows, cast, 0)
        self.side.start()

    def edge(self, buffer, first):
        near = pl.ds(pl.multiple_of(self.near, HALF), HALF)

        def one(k, carry):
            for n in range(self.images):
                at = first + k
                buffer[n, k] = self.spill[n, self.cells(at, self.off, self.tile_cols), :].astype(BF16)
                part = self.spill[n, self.cells(at, HALF, HALF), :]
                buffer[n, k, near, :] = (part + self.side_in[n, at].astype(F32)).astype(BF16)
            return carry

        lax.fori_loop(0, REACH, one, 0)

    def middle(self):
        self.side.wait_recv()

        @pl.when(self.row > 0)
        def _():
            self.edge(self.up_out, PAD - REACH)
            self.up.start()

        @pl.when(self.row < self.rows - 1)
        def _():
            self.edge(self.down_out, PAD + self.tile_rows)
            self.down.start()

    def pixels(self, n, k, first, count):
        at = ((self.image + n) * self.tile_rows + k) * self.tile_cols + first
        return pl.ds(pl.multiple_of(at, HALF), count)

    def own(self):
        def fill(k, carry):
            for n in range(self.images):
                home = self.spill[n, self.cells(PAD + k, self.off, self.tile_cols), :]
                self.grad[self.pixels(n, k, 0, self.tile_cols), :] = home
                self.grad[self.pixels(n, k, self.near, HALF), :] += self.side_in[n, PAD + k].astype(F32)
            return carry

        lax.fori_loop(0, self.tile_rows, fill, 0)

    def finish(self):
        def arrive(buffer, first):
            def one(k, carry):
                for n in range(self.images):
                    at = self.pixels(n, first + k, 0, self.tile_cols)
                    self.grad[at, :] += buffer[n, k].astype(F32)
                return carry

            lax.fori_loop(0, REACH, one, 0)

        @pl.when(self.row > 0)
        def _():
            self.down.wait_recv()
            arrive(self.up_in, 0)
            self.up.wait_send()

        @pl.when(self.row < self.rows - 1)
        def _():
            self.up.wait_recv()
            arrive(self.down_in, self.tile_rows - REACH)
            self.down.wait_send()

        self.side.wait_send()


def backward_s(pixel_count, direct, r):
    ex = Exchange(r.ex1)
    cols = r.table.shape[0] // WINDOW
    spills = [Spill(r.spill, r.grad, cols, r.strips[8 * n : 8 * n + 8], n) for n in range(2)]

    mid, late, end = Jobs(), Jobs(), Jobs()
    deform_weight_product(r)
    wait_all()
    if direct:
        line, planes, deform = Jobs(), Jobs(), Jobs()
        line.add(*line_jobs(r.eighth_conv_b, r.sum_conv_b, r.line_conv_b))
        planes.add(
            *plane_jobs(r.src_reduce_b, r.eighth_reduce_b, r.plane_reduce_b),
            *plane_jobs(r.src_expand_a, r.eighth_expand_a, r.plane_expand_a),
        )
        deform.add(*plane_jobs(r.gw_deform, r.eighth_deform, r.plane_deform))
        deform.tick(2)
        r.ready(r.eighth_conv_b)
        line.tick(2)
        r.ready(r.src_reduce_b, r.src_expand_a)
        sums = [
            part_jobs(LineSum, r.eighth_reduce_b, r.own_reduce_b, r.line_reduce_b),
            part_jobs(LineSum, r.eighth_expand_a, r.own_expand_a, r.line_expand_a),
            part_jobs(LineSum, r.eighth_deform, r.own_deform, r.line_deform),
        ]
        early, final = Jobs(), Jobs()
        early.add(*sums[0], *sums[1])
        final.add(*sums[2])
        q1, q2, q3, q4, q5 = planes.queue, line.queue, deform.queue, early.queue, final.queue
        slots = {
            1: q3[0:2] + q1[0:4],
            4: q1[4:8],
            7: q3[2:4],
            10: q3[4:6] + q5[0:2],
            11: q1[8:12] + q2[0:2],
        }
        mid.queue = q2[2:4]
        late.queue = q1[12:16] + q4[0:4] + q2[4:6]
        end.queue = q5[2:4] + q4[4:8]
    else:
        slots = {}
        r.push(r.gw_deform)
    slots[5] = [functools.partial(unoffset, r, 0), spills[0].start] + slots.get(5, [])
    slots[8] = [spills[0].middle] + slots.get(8, [])

    def run(queue):
        def call():
            for step in queue:
                step()

        return call

    plan = {slot: run(queue) for slot, queue in slots.items()}
    r.ready(r.w_deform, r.rim, r.w_off, r.select)
    turn(r.gd, r.turned)
    unsample(r, plan)
    unoffset(r, 1)
    spills[1].start()
    r.push(r.gw_off)
    spills[1].middle()
    mid.finish()
    for spill in spills:
        spill.own()
    spills[0].finish()
    late.finish()
    if direct:
        r.push(r.sum_conv_b)
    r.ready(r.u_a1)
    spills[1].finish()
    sums = gelu_grad(r.grad, r.u_a1, r.norm_a1, r.mask)
    ex.put(*sums)
    ex.middle_sums()
    ex.finish_sums()
    sums = put_sums(ex, r.sums_a1)
    norm_back(r.grad, r.u_a1, r.norm_a1, sums, pixel_count, r.mask, r.gr_a)
    end.finish()
    if direct:
        r.push(r.own_reduce_b, r.own_expand_a, r.own_deform)


def deform_weight_product(r):
    width = r.gd.shape[1]
    slots = r.sample_slots.shape[0]

    def load(tap):
        rows, slot = pl.ds(tap * width, width), tap % slots
        return pltpu.make_async_copy(
            r.samples.at[rows], r.sample_slots.at[slot], r.sample_sems.at[slot]
        )

    for tap in range(slots):
        load(tap).start()
    r.ready(r.gd)
    for tap in range(9):
        load(tap).wait()
        value = jnp.dot(r.sample_slots[tap % slots], r.gd[...], preferred_element_type=F32)
        put_rows(r.gw_deform, tap * width, value)
        if tap + slots < 9:
            load(tap + slots).start()


def last(direct, r):
    jobs, more, plane = Jobs(), Jobs(), Jobs()
    r.ready(r.gr_a, r.feature)
    wait_all()
    if direct:
        r.ready(r.own_deform, r.gw_off)
        jobs.add(
            *part_jobs(Gather, r.own_deform, r.sum_deform, r.gather_deform),
            SmallSum(r.gw_off, r.sum_off, r.small),
        )
        more.add(
            *part_jobs(Gather, r.own_reduce_b, r.sum_reduce_b, r.gather_reduce_b),
            *part_jobs(Gather, r.own_expand_a, r.sum_expand_a, r.gather_expand_a),
        )
    jobs.tick(3)
    turn(r.gr_a, r.turned)
    weight_product(r.turned, r.feature, r.gw_reduce)
    if direct:
        plane.add(*plane_jobs(r.gw_reduce, r.eighth_reduce_a, r.plane_reduce_a))
        plane.add(*line_jobs(r.eighth_reduce_a, r.sum_reduce_a, r.line_reduce_a))
    else:
        r.push(r.gw_reduce)
    plane.tick(2)
    if direct:
        r.ready(r.own_reduce_b, r.own_expand_a)
    r.ready(r.w_reduce, r.e_a3)

    def chunk(i, carry):
        rows = pl.ds(pl.multiple_of(i * CHUNK, CHUNK), CHUNK)
        for first in range(0, r.feature.shape[1], 512):
            lanes = slice(first, first + 512)
            grad = lax.dot_general(
                r.gr_a[rows, :],
                r.w_reduce[lanes, :],
                (((1,), (1,)), ((), ())),
                preferred_element_type=F32,
            )
            r.grad_in[rows, lanes] = (grad + r.e_a3[rows, lanes].astype(F32)).astype(BF16)
        return carry

    half = r.feature.shape[0] // CHUNK // 2
    lax.fori_loop(0, half, chunk, 0)
    plane.tick(2)
    lax.fori_loop(half, 2 * half, chunk, 0)
    r.push(r.grad_in)
    jobs.tick(3)
    plane.tick(2)
    more.tick(4)
    plane.tick(4)
    jobs.finish()
    more.tick(4)
    plane.tick(2)
    more.finish()
    if direct:
        r.push(r.sum_reduce_b, r.sum_expand_a, r.sum_deform)
    plane.finish()
    if direct:
        r.push(r.sum_reduce_a)


def body(
    feature_in,
    orientation,
    offset_base,
    w_reduce_a,
    w_offset_a,
    w_deform_a,
    w_expand_a,
    scale_a,
    shift_a,
    w_reduce_b,
    w_conv_b,
    w_expand_b,
    scale_b,
    shift_b,
    cotangent,
):
    images, tile_rows, tile_cols, channels = feature_in.shape
    inner_width = w_reduce_a.shape[1]
    tile_pixels = tile_rows * tile_cols
    pixels = images * tile_pixels
    win_cols = tile_cols + HALF
    win_rows = tile_rows + 2 * PAD
    cells = win_rows * win_cols
    plane_count = 1.0 * images * LONG * SHORT
    pixel_count = plane_count * lax.axis_size(IMG)
    unbias = pixel_count / (pixel_count - 1.0)

    def array(*shape, dtype=BF16):
        return jax.ShapeDtypeStruct(shape, dtype)

    def table(width):
        return array(NORM_ROWS, width, dtype=F32)

    small = (pixels, inner_width)
    big = (pixels, channels)
    window_b = (images, tile_rows + 4, win_cols, inner_width)
    shifted = pltpu.VMEM((images, tile_rows + 4, tile_cols, 3 * inner_width), BF16)
    tile = pltpu.VMEM((images, tile_rows, tile_cols, inner_width), BF16)
    turned = pltpu.VMEM((inner_width, pixels), BF16)
    images_axis = lax.axis_size(IMG)
    direct = inner_width % (images_axis * 8 * 16) == 0
    cuts = images_axis if direct else 1
    feature = feature_in.reshape(big)
    scale_a, shift_a, scale_b, shift_b = (v[None] for v in (scale_a, shift_a, scale_b, shift_b))
    taps_shape = (images, 16, tile_pixels)
    start = fused(
        functools.partial(first, plane_count),
        FIRST_CID,
        ins=dict(
            base=offset_base.reshape(pixels, 18),
            w_offset=w_offset_a.T,
            scale=scale_a,
            shift=shift_a,
        ),
        smem=dict(orientation=orientation),
        staged=dict(feature=feature, w_reduce=w_reduce_a, w_deform=w_deform_a),
        outs=dict(
            mask=array(pixels, 128, dtype=F32),
            counts=array(16, 128, dtype=F32),
            up=array(*taps_shape, dtype=jnp.int32),
            left=array(*taps_shape, dtype=jnp.int32),
            w_off=array(288, inner_width),
            norm_a1=table(inner_width),
            norm_a2=table(inner_width),
        ),
        pushed=dict(
            u_a1=array(*small, dtype=F32),
            rim=array(images, win_rows, win_cols, inner_width),
            select=array(tile_pixels, cells),
            fr=array(*taps_shape, dtype=F32),
            fc=array(*taps_shape, dtype=F32),
            samples=array(9 * inner_width, pixels),
            u_a2=array(*small, dtype=F32),
        ),
        scratch=dict(
            ex1=Exchange.scratch(inner_width),
            ex2=Exchange.scratch(inner_width),
            halo=Halo.scratch * images,
            tile=tile,
            w_turned=pltpu.VMEM((inner_width, 9 * inner_width), BF16),
            rim_t=pltpu.VMEM((images, inner_width, cells), BF16),
            spread=pltpu.VMEM((288, cells), F32),
            table=pltpu.VMEM((WINDOW * win_cols, tile_pixels // 2), BF16),
        ),
    )
    mask, count_rows, norm_a1 = start.mask, start.counts, start.norm_a1
    rim_flat = start.rim.reshape(images, cells, inner_width)
    norm_a2, deformed = start.norm_a2, start.u_a2
    fwd = fused(
        functools.partial(forward, plane_count),
        FORWARD_CID,
        ins=dict(
            norm_a2=norm_a2,
            mask=mask,
            counts=count_rows,
            scale_a=scale_a,
            shift_a=shift_a,
            scale_b=scale_b,
            shift_b=shift_b,
        ),
        far=dict(cotangent=cotangent.reshape(big)),
        staged=dict(
            u_a2=deformed,
            w_expand_a=w_expand_a,
            feature=feature,
            w_reduce=w_reduce_b,
            w_conv=w_conv_b,
            w_expand_b=w_expand_b,
        ),
        outs=dict(
            norm_a3=table(channels),
            norm_b1=table(inner_width),
            norm_b2=table(inner_width),
            norm_b3=table(channels),
            sums_b3=table(channels),
        ),
        pushed=dict(
            h2_a=array(*small),
            middle=array(*big),
            slope_a=array(*big),
            u_a3=array(*big),
            u_b1=array(*small, dtype=F32),
            rim_b=array(*window_b),
            u_b2=array(*small, dtype=F32),
            h2_b=array(*small),
            feature_out=array(*big),
        ),
        far_outs=dict(e_b3=array(*big), u_b3=array(*big)),
        scratch=dict(
            ex_a3=Exchange.scratch(channels),
            ex_b1=Exchange.scratch(inner_width),
            ex_b2=Exchange.scratch(inner_width),
            ex_b3=Exchange.scratch(channels),
            ex_sums=Exchange.scratch(channels),
            halo=Halo.scratch,
            wide=pltpu.VMEM(big, F32),
            tile=tile,
            shifted=shifted,
            far_sems=pltpu.SemaphoreType.DMA((3,)),
        ),
    )
    def eighths(grad):
        return grad.reshape(images_axis, 8, -1, grad.shape[-1])

    def eighth_of(src):
        return array(images_axis, *src.shape[2:])

    def own_of(src):
        return array(*src.shape[2:])

    def sum_of(src):
        return array(*src.shape[1:])

    def vmem(struct):
        return pltpu.VMEM(struct.shape, struct.dtype)

    natural = array(1, inner_width, channels)
    pushed_b, scratch_b = dict(gw_expand=natural), {}
    if direct:
        expand_b = array(images_axis, 8, inner_width // images_axis // 8, channels)
        pushed_b = dict(eighth_expand_b=eighth_of(expand_b))
        scratch_b = dict(gw_expand=vmem(expand_b), plane_expand_b=Plane.scratch(expand_b.shape))
    bwd_b = fused(
        functools.partial(backward_b, pixel_count, direct),
        BACKWARD_B_CID,
        ins=dict(
            mask=mask,
            norm_b3=fwd.norm_b3,
            sums_b3=fwd.sums_b3,
            norm_b2=fwd.norm_b2,
            norm_b1=fwd.norm_b1,
        ),
        staged=dict(
            e_b3=fwd.e_b3,
            u_b3=fwd.u_b3,
            w_expand=w_expand_b,
            u_b2=fwd.u_b2,
            h2_b=fwd.h2_b,
            rim_b=fwd.rim_b,
            w_conv=w_conv_b,
            u_b1=fwd.u_b1,
        ),
        outs=dict(gro_b=array(*small), sums_b2=table(inner_width), sums_b1=table(inner_width)),
        pushed=dict(
            **pushed_b,
            gw_conv=array(cuts, inner_width, 9 * inner_width // cuts),
        ),
        scratch=dict(
            **scratch_b,
            ex2=Exchange.scratch(inner_width),
            ex1=Exchange.scratch(inner_width),
            halo=Halo.scratch,
            geo=pltpu.VMEM(big, BF16),
            grad=pltpu.VMEM(small, F32),
            tile=tile,
            turned=turned,
            back_rim=pltpu.VMEM(window_b, BF16),
            shifted=shifted,
            back_shifted=shifted,
        ),
    )

    staged_a, pushed_a, scratch_a = {}, {}, {}
    if direct:
        conv_b = eighths(bwd_b.gw_conv)
        staged_a = dict(src_conv_b=conv_b, eighth_expand_b=bwd_b.eighth_expand_b)
        pushed_a = dict(eighth_conv_b=eighth_of(conv_b), sum_expand_b=sum_of(expand_b))
        scratch_a = dict(
            plane_conv_b=Plane.scratch(conv_b.shape),
            line_expand_b=Line.scratch(bwd_b.eighth_expand_b.shape),
        )
    bwd_a = fused(
        functools.partial(backward_a, pixel_count, direct),
        BACKWARD_A_CID,
        ins=dict(mask=mask, norm_a3=fwd.norm_a3, norm_a2=norm_a2),
        staged=dict(
            gro_b=bwd_b.gro_b,
            w_reduce=w_reduce_b,
            **staged_a,
            e_b3=fwd.e_b3,
            slope_a=fwd.slope_a,
            u_a3=fwd.u_a3,
            middle=fwd.middle,
            w_expand=w_expand_a,
            u_a2=deformed,
            h2_a=fwd.h2_a,
        ),
        outs=dict(gd=array(*small), sums_a3=table(channels), sums_a2=table(inner_width)),
        pushed=dict(
            **pushed_a,
            gw_reduce=array(cuts, inner_width, channels // cuts),
            gw_expand=natural,
            e_a3=array(*big),
        ),
        scratch=dict(
            **scratch_a,
            ex3=Exchange.scratch(channels),
            ex2=Exchange.scratch(inner_width),
            wide=pltpu.VMEM(big, F32),
            grad=pltpu.VMEM(small, F32),
            turned=turned,
        ),
    )
    staged_s, scratch_s = {}, {}
    pushed_s = dict(gw_deform=array(1, 9 * inner_width, inner_width))
    if direct:
        reduce_b, expand_a = eighths(bwd_a.gw_reduce), eighths(bwd_a.gw_expand)
        deform = array(images_axis, 8, 9 * inner_width // images_axis // 8, inner_width)
        staged_s = dict(
            src_reduce_b=reduce_b,
            src_expand_a=expand_a,
            eighth_conv_b=bwd_a.eighth_conv_b,
        )
        pushed_s = dict(
            sum_conv_b=sum_of(conv_b),
            own_reduce_b=own_of(reduce_b),
            own_expand_a=own_of(expand_a),
            own_deform=own_of(deform),
        )
        scratch_s = dict(
            gw_deform=vmem(deform),
            line_conv_b=Line.scratch(bwd_a.eighth_conv_b.shape),
            plane_reduce_b=Plane.scratch(reduce_b.shape),
            plane_expand_a=Plane.scratch(expand_a.shape),
            plane_deform=Plane.scratch(deform.shape),
            eighth_reduce_b=vmem(eighth_of(reduce_b)),
            eighth_expand_a=vmem(eighth_of(expand_a)),
            eighth_deform=vmem(eighth_of(deform)),
            line_reduce_b=LineSum.scratch(eighth_of(reduce_b).shape),
            line_expand_a=LineSum.scratch(eighth_of(expand_a).shape),
            line_deform=LineSum.scratch(eighth_of(deform).shape),
        )
    block = tile_pixels // 2
    bwd_s = fused(
        functools.partial(backward_s, pixel_count, direct),
        BACKWARD_S_CID,
        ins=dict(
            mask=mask,
            norm_a1=norm_a1,
            up=start.up,
            left=start.left,
            fr=start.fr,
            fc=start.fc,
        ),
        far=dict(samples=start.samples),
        staged=dict(
            gd=bwd_a.gd,
            **staged_s,
            w_deform=w_deform_a,
            rim=rim_flat,
            w_off=start.w_off,
            select=start.select,
            u_a1=start.u_a1,
        ),
        outs=dict(gr_a=array(*small), sums_a1=table(inner_width)),
        pushed=dict(**pushed_s, gw_off=array(cuts, 32, 9 * inner_width // cuts)),
        scratch=dict(
            **scratch_s,
            ex1=Exchange.scratch(inner_width),
            strips=Spill.scratch(1, tile_rows, tile_cols, inner_width) * images,
            spill=pltpu.VMEM((images, cells, inner_width), F32),
            table=pltpu.VMEM((WINDOW * win_cols, 3 * block), BF16),
            grads=pltpu.VMEM((inner_width, 3 * block), BF16),
            turned=turned,
            grad_row=pltpu.VMEM(taps_shape, F32),
            grad_col=pltpu.VMEM(taps_shape, F32),
            on_cells=pltpu.VMEM((288, cells), BF16),
            gw_off_sum=pltpu.VMEM((288, inner_width), F32),
            sample_slots=pltpu.VMEM((3, inner_width, pixels), BF16),
            sample_sems=pltpu.SemaphoreType.DMA((3,)),
            grad=pltpu.VMEM(small, F32),
        ),
    )
    staged_l, pushed_l, scratch_l = {}, {}, {}
    if direct:
        reduce_a = array(images_axis, 8, inner_width // 8, channels // cuts)
        staged_l = dict(
            own_deform=bwd_s.own_deform,
            gw_off=bwd_s.gw_off,
            own_reduce_b=bwd_s.own_reduce_b,
            own_expand_a=bwd_s.own_expand_a,
        )
        pushed_l = dict(
            sum_reduce_b=sum_of(reduce_b),
            sum_expand_a=sum_of(expand_a),
            sum_deform=sum_of(deform),
            sum_reduce_a=sum_of(reduce_a),
        )
        scratch_l = dict(
            gw_reduce=vmem(reduce_a),
            small=SmallSum.scratch(bwd_s.gw_off.shape),
            gather_reduce_b=Gather.scratch(reduce_b.shape),
            gather_expand_a=Gather.scratch(expand_a.shape),
            gather_deform=Gather.scratch(deform.shape),
            plane_reduce_a=Plane.scratch(reduce_a.shape),
            eighth_reduce_a=vmem(eighth_of(reduce_a)),
            line_reduce_a=Line.scratch(eighth_of(reduce_a).shape),
        )
        outs_l = dict(sum_off=array(*bwd_s.gw_off.shape[1:], dtype=F32))
    else:
        pushed_l = dict(gw_reduce=array(cuts, inner_width, channels // cuts))
        outs_l = {}
    end = fused(
        functools.partial(last, direct),
        LAST_CID,
        ins={},
        staged=dict(
            gr_a=bwd_s.gr_a, feature=feature, **staged_l, w_reduce=w_reduce_a, e_a3=bwd_a.e_a3
        ),
        outs=outs_l,
        pushed=dict(**pushed_l, grad_in=array(*big)),
        scratch=dict(**scratch_l, turned=turned),
    )
    sums_a = [bwd_s.sums_a1, bwd_a.sums_a2, bwd_a.sums_a3]
    sums_b = [bwd_b.sums_b1, bwd_b.sums_b2, fwd.sums_b3]
    norms_a = [norm_a1, norm_a2, fwd.norm_a3]
    norms_b = [fwd.norm_b1, fwd.norm_b2, fwd.norm_b3]
    if direct:
        sums = [
            bwd_s.sum_conv_b,
            end.sum_reduce_b,
            end.sum_reduce_a,
            bwd_a.sum_expand_b,
            end.sum_expand_a,
            end.sum_deform,
            end.sum_off,
        ]
    else:

        def over_devices(grad, dim):
            part = lax.psum_scatter(grad, IMG, scatter_dimension=dim, tiled=True)
            return lax.psum(part, (ROW, COL))

        turned_grads = (bwd_b.gw_conv, bwd_a.gw_reduce, end.gw_reduce)
        sums = [over_devices(g[0], 1) for g in turned_grads]
        sums += [over_devices(g[0], 0) for g in (bwd_b.gw_expand, bwd_a.gw_expand)]
        sums.append(over_devices(bwd_s.gw_deform[0], 0))
        sums = [g.reshape(8, -1, g.shape[1]) for g in sums]
        sums.append(over_devices(bwd_s.gw_off[0], 1).astype(F32))
    share = inner_width // images_axis
    long_share, wide_share = 9 * share, channels // images_axis
    shapes = [
        (long_share, inner_width),
        (wide_share, inner_width),
        (wide_share, inner_width),
        (share, channels),
        (share, channels),
        (long_share, inner_width),
        (18, long_share),
    ]
    vectors = ((2 * inner_width + channels) // 128, 128)
    shapes += [vectors] * 8
    operands = sums + sums_a + sums_b + norms_a + norms_b + [fwd.feature_out, end.grad_in]
    results = [array(*shape, dtype=F32) for shape in shapes]
    anywhere = pl.BlockSpec(memory_space=pl.ANY)
    results = pl.pallas_call(
        functools.partial(finish_kernel, unbias, len(operands)),
        out_shape=results + [array(*big)] * 2,
        in_specs=[anywhere] * len(operands),
        out_specs=[anywhere] * (len(shapes) + 2),
        scratch_shapes=[vmem(v) for v in operands + results]
        + [pltpu.SemaphoreType.DMA((len(operands),)), pltpu.SemaphoreType.DMA((17,))],
        compiler_params=pltpu.CompilerParams(vmem_limit_bytes=VMEM_LIMIT),
    )(*operands)
    conv_b, reduce_b, reduce_a, expand_b, expand_a, deform_a, offset_a = results[:7]
    scale_sums_a, shift_sums_a, scale_sums_b, shift_sums_b, mean_a, var_a, mean_b, var_b = (
        v.reshape(-1) for v in results[7:15]
    )
    return (
        results[15].reshape(feature_in.shape),
        results[16].reshape(feature_in.shape),
        reduce_a,
        offset_a.T,
        deform_a,
        expand_a,
        scale_sums_a,
        shift_sums_a,
        mean_a,
        var_a,
        reduce_b,
        conv_b,
        expand_b,
        scale_sums_b,
        shift_sums_b,
        mean_b,
        var_b,
    )


def solution(mesh):
    tiles = P(IMG, ROW, COL, None)
    in_specs = (tiles, P(IMG), tiles) + (P(),) * 11 + (tiles,)
    shares = P(IMG, None)
    out_specs = (tiles, tiles) + (shares,) * 4 + (P(),) * 4 + (shares,) * 3 + (P(),) * 4
    return jax.shard_map(body, mesh=mesh, in_specs=in_specs, out_specs=out_specs, check_vma=False)
```

```python
import functools
import types

import jax
import jax.numpy as jnp
import numpy as np
from jax import lax
from jax.experimental import pallas as pl
from jax.experimental.pallas import tpu as pltpu
from jax.sharding import PartitionSpec as P

LONG = 64
SHORT = 44
BOUND = 4
EPSILON = 1e-05
IMG, ROW, COL = "img", "row", "col"
MESH = pl.DeviceIdType.MESH
VMEM = pl.BlockSpec(memory_space=pltpu.VMEM)
VMEM_LIMIT = 60 * 1024 * 1024
F32 = jnp.float32
BF16 = jnp.bfloat16
REACH = BOUND + 3
PAD = 8
HALF = 16
FIRST_CID, FORWARD_CID, BACKWARD_B_CID, BACKWARD_A_CID, BACKWARD_S_CID, LAST_CID = range(6)


def group_of(axes):
    sizes = [lax.axis_size(a) for a in axes]
    total = int(np.prod(sizes))
    place = lax.axis_index(axes[0])
    for axis, size in zip(axes[1:], sizes[1:]):
        place = place * size + lax.axis_index(axis)

    def device(step):
        spot = lax.rem(place + step, total)
        coords = {}
        for axis, size in zip(reversed(axes), reversed(sizes)):
            coords[axis] = lax.rem(spot, size)
            spot = spot // size
        return coords

    return place, total, device


PLANE = (ROW, COL)
LINE = (IMG,)


def gather_start(axes, slots, send_sem, recv_sem):
    _, total, device = group_of(axes)
    for step in range(1, total):
        pltpu.make_async_remote_copy(
            src_ref=slots.at[0],
            dst_ref=slots.at[step],
            send_sem=send_sem,
            recv_sem=recv_sem,
            device_id=device(step),
            device_id_type=MESH,
        ).start()


def gather_wait(axes, slots, sem):
    _, total, _ = group_of(axes)
    others = slots.at[pl.ds(1, total - 1)]
    pltpu.make_async_copy(others, others, sem).wait()


def in_order(axes, slots):
    place, total, _ = group_of(axes)
    return [slots[lax.rem(place - spot + total, total)] for spot in range(total)]


def halo_peers():
    row, rows, col = lax.axis_index(ROW), lax.axis_size(ROW), lax.axis_index(COL)
    return row, rows, col, {COL: 1 - col}, {ROW: row - 1}, {ROW: row + 1}


BLOCK_ROWS = 8
SPAN = 17
WINDOW = 3 * BLOCK_ROWS


def tap_span(group, cols):
    first = 2 + 2 * group
    start = first * cols // 128 * 128
    stop = -(-(first + SPAN) * cols // 128) * 128
    return first, start, stop


def tap_weights(tap, block, cols, up_ref, left_ref, fr_ref, fc_ref, image=0, lanes=slice(None)):
    up, left, fr, fc = (
        ref[image, tap : tap + 1, lanes] for ref in (up_ref, left_ref, fr_ref, fc_ref)
    )
    up = up - block * BLOCK_ROWS
    pixels = up.shape[1]

    def pair(size, at, frac):
        ids = lax.broadcasted_iota(jnp.int32, (size, pixels), 0)
        first, second = ids == at, ids == at + 1
        value = jnp.where(first, 1.0 - frac, jnp.where(second, frac, 0.0))
        slope = jnp.where(second, 1.0, jnp.where(first, -1.0, 0.0))
        return value, slope

    return pair(WINDOW, up, fr) + pair(cols, left, fc)


def write_table(table, lane, row_w, col_w, group, cols):
    first, start, stop = tap_span(group, cols)
    pixels = row_w.shape[1]
    low = start // cols
    high = -(-stop // cols)
    for r in range(low, min(high, WINDOW)):
        table[r * cols : (r + 1) * cols, lane : lane + pixels] = (
            row_w[r : r + 1, :] * col_w
        ).astype(BF16)


def build_shifted(rim_ref, shifted):
    images, rows, cols, width = rim_ref.shape
    col = lax.axis_index(COL)
    tile = cols - HALF

    def fill(first):
        def one_row(k, carry):
            for n in range(images):
                line = rim_ref[n, k].astype(F32)
                none = jnp.zeros((2, width), F32)
                for d in range(3):
                    at = first + 2 * (d - 1)
                    if at < 0:
                        part = jnp.concatenate([none, line[: tile - 2]], axis=0)
                    elif at + tile > cols:
                        part = jnp.concatenate([line[at:], none], axis=0)
                    else:
                        part = line[at : at + tile]
                    shifted[n, k, :, d * width : (d + 1) * width] = part.astype(BF16)
            return carry

        lax.fori_loop(0, rows, one_row, 0)

    @pl.when(col == 0)
    def _():
        fill(0)

    @pl.when(col == 1)
    def _():
        fill(HALF)


def conv_product(shifted, w_ref, o_ref):
    images, rows, cols, width3 = shifted.shape
    tile_rows = rows - 4
    pixels = tile_rows * cols
    for n in range(images):
        total = None
        for i in range(3):
            taps = shifted[n, 2 * i : 2 * i + tile_rows].reshape(pixels, width3)
            term = jnp.dot(taps, w_ref[i * width3 : (i + 1) * width3, :], preferred_element_type=F32)
            total = term if total is None else total + term
        o_ref[n * pixels : (n + 1) * pixels, :] = total


def conv_weight_product(turned, shifted, gw_ref, i):
    images, rows, cols, width3 = shifted.shape
    tile_rows = rows - 4
    pixels = tile_rows * cols
    total = None
    for n in range(images):
        taps = shifted[n, 2 * i : 2 * i + tile_rows].reshape(pixels, width3)
        term = jnp.dot(turned[:, n * pixels : (n + 1) * pixels], taps, preferred_element_type=F32)
        total = term if total is None else total + term
    put_lanes(gw_ref, i * width3, total)


def unconv_product(shifted, w_ref, o_ref):
    images, rows, cols, width3 = shifted.shape
    width = width3 // 3
    tile_rows = rows - 4
    pixels = tile_rows * cols
    for n in range(images):
        total = None
        for tap in range(9):
            i, d = 2 - tap // 3, 2 - tap % 3
            grads = shifted[n, 2 * i : 2 * i + tile_rows, :, d * width : (d + 1) * width]
            term = lax.dot_general(
                grads.reshape(pixels, width),
                w_ref[tap * width : (tap + 1) * width, :],
                (((1,), (1,)), ((), ())),
                preferred_element_type=F32,
            )
            total = term if total is None else total + term
        o_ref[n * pixels : (n + 1) * pixels, :] = total


def halves(width):
    first = -(-width // 256) * 128
    return ((0, first), (first, width - first)) if first < width else ((0, width),)


def remote(src, dst, send, recv, device):
    return pltpu.make_async_remote_copy(
        src_ref=src, dst_ref=dst, send_sem=send, recv_sem=recv, device_id=device, device_id_type=MESH
    )


def arrival(ref, sem):
    return pltpu.make_async_copy(ref, ref, sem)


class Plane:
    @staticmethod
    def scratch(shape):
        images, _, rows, width = shape
        count = len(halves(width))
        return [
            pltpu.VMEM((images, 4, rows, width), BF16),
            pltpu.VMEM((images, 2, rows, width), BF16),
            pltpu.SemaphoreType.DMA((count, 3)),
            pltpu.SemaphoreType.DMA((count, 3)),
        ]

    def __init__(self, src, eighth, refs, part):
        half, quarter, send, recv = refs
        lanes = pl.ds(*halves(src.shape[-1])[part])
        self.src, self.half, self.quarter = (
            ref.at[:, :, :, lanes] for ref in (src, half, quarter)
        )
        self.eighth = eighth.at[:, :, lanes]
        self.images = src.shape[0]
        self.send, self.recv = [send.at[part, k] for k in range(3)], [recv.at[part, k] for k in range(3)]
        self.a, self.b, self.spot, self.first, self.second = self.peers(part == 0)
        col = lax.axis_index(COL)
        self.mine, self.pair, self.other = 4 * col, {COL: 1 - col}, 4 * (1 - col)

    @staticmethod
    def peers(x_first):
        row = lax.axis_index(ROW)
        x, y = lax.rem(row, 2), row // 2
        to_x, to_y = {ROW: row + 1 - 2 * x}, {ROW: row + 2 - 4 * y}
        if x_first:
            return x, y, lambda bit, free: bit + 2 * free, to_x, to_y
        return y, x, lambda bit, free: 2 * bit + free, to_y, to_x

    def steps(self):
        return [self.to_pair, self.to_first, self.to_second, self.done]

    def to_pair(self):
        src = self.src.at[:, pl.ds(self.other, 4)]
        remote(src, self.half, self.send[0], self.recv[0], self.pair).start()

    def to_first(self):
        arrival(self.half, self.recv[0]).wait()

        def add(i, carry):
            for s in range(4):
                self.half[i, s] = self.src[i, self.mine + s] + self.half[i, s]
            return carry

        lax.fori_loop(0, self.images, add, 0)
        for k in range(2):
            src = self.half.at[:, self.spot(1 - self.a, k)]
            remote(src, self.quarter.at[:, k], self.send[1], self.recv[1], self.first).start()

    def to_second(self):
        arrival(self.quarter, self.recv[1]).wait()

        def add(i, carry):
            for k in range(2):
                self.quarter[i, k] = self.half[i, self.spot(self.a, k)] + self.quarter[i, k]
            return carry

        lax.fori_loop(0, self.images, add, 0)
        src = self.quarter.at[:, 1 - self.b]
        remote(src, self.eighth, self.send[2], self.recv[2], self.second).start()

    def done(self):
        arrival(self.eighth, self.recv[2]).wait()

        def add(i, carry):
            self.eighth[i] = self.quarter[i, self.b] + self.eighth[i]
            return carry

        lax.fori_loop(0, self.images, add, 0)
        arrival(self.half, self.send[0]).wait()
        arrival(self.quarter, self.send[1]).wait()
        arrival(self.eighth, self.send[2]).wait()


class LinePlane:
    @staticmethod
    def scratch(shape):
        images, _, rows, width = shape
        sems = pltpu.SemaphoreType.DMA((len(halves(width)), 4))
        return [
            pltpu.VMEM((images, 4, rows, width), BF16),
            pltpu.VMEM((images, 4, rows, width), BF16),
            pltpu.VMEM((2, rows, width), BF16),
            pltpu.VMEM((rows, width), BF16),
            sems,
            sems,
        ]

    def __init__(self, src, own, refs, part):
        half, line, quarter, eighth, send, recv = refs
        lanes = pl.ds(*halves(src.shape[-1])[part])
        self.src, self.half, self.line = (ref.at[:, :, :, lanes] for ref in (src, half, line))
        self.quarter = quarter.at[:, :, lanes]
        self.eighth, self.own = eighth.at[:, lanes], own.at[:, lanes]
        self.images, self.img = src.shape[0], lax.axis_index(IMG)
        self.send, self.recv = [send.at[part, k] for k in range(4)], [recv.at[part, k] for k in range(4)]
        self.plane = Plane.peers(part == 0)
        col = lax.axis_index(COL)
        self.mine, self.pair, self.other = 4 * col, {COL: 1 - col}, 4 * (1 - col)

    def steps(self):
        return [self.to_pair, self.to_line, self.to_first, self.to_second, self.done]

    def to_pair(self):
        src = self.src.at[:, pl.ds(self.other, 4)]
        remote(src, self.half, self.send[0], self.recv[0], self.pair).start()

    def to_line(self):
        arrival(self.half, self.recv[0]).wait()

        def add(i, carry):
            for s in range(4):
                self.half[i, s] = self.src[i, self.mine + s] + self.half[i, s]
            return carry

        lax.fori_loop(0, self.images, add, 0)
        for j in range(1, self.images):
            there = lax.rem(self.img + j, self.images)
            src = self.half.at[there]
            remote(src, self.line.at[j], self.send[1], self.recv[1], {IMG: there}).start()

    def to_first(self):
        arrival(self.line.at[pl.ds(1, self.images - 1)], self.recv[1]).wait()
        for s in range(4):
            total = self.half[self.img, s].astype(F32)
            for j in range(1, self.images):
                total = total + self.line[j, s].astype(F32)
            self.line[0, s] = total.astype(BF16)
        a, _, spot, first, _ = self.plane
        for k in range(2):
            src = self.line.at[0, spot(1 - a, k)]
            remote(src, self.quarter.at[k], self.send[2], self.recv[2], first).start()

    def to_second(self):
        a, b, spot, _, second = self.plane
        arrival(self.quarter, self.recv[2]).wait()
        for k in range(2):
            self.quarter[k] = self.line[0, spot(a, k)] + self.quarter[k]
        remote(self.quarter.at[1 - b], self.eighth, self.send[3], self.recv[3], second).start()

    def done(self):
        _, b, _, _, _ = self.plane
        arrival(self.eighth, self.recv[3]).wait()
        self.own[...] = self.quarter[b] + self.eighth[...]
        arrival(self.half, self.send[0]).wait()
        arrival(self.line.at[pl.ds(1, self.images - 1)], self.send[1]).wait()
        arrival(self.quarter, self.send[2]).wait()
        arrival(self.eighth, self.send[3]).wait()


class LineSum:
    @staticmethod
    def scratch(shape):
        sems = pltpu.SemaphoreType.DMA((len(halves(shape[-1])),))
        return [pltpu.VMEM(shape, BF16), sems, sems]

    def __init__(self, eighth, own, refs, part):
        line, send, recv = refs
        lanes = pl.ds(*halves(eighth.shape[-1])[part])
        self.eighth, self.line, self.own = eighth.at[:, :, lanes], line.at[:, :, lanes], own.at[:, lanes]
        self.images, self.img = eighth.shape[0], lax.axis_index(IMG)
        self.send, self.recv = send.at[part], recv.at[part]

    def steps(self):
        return [self.to_line, self.done]

    def to_line(self):
        for j in range(1, self.images):
            there = lax.rem(self.img + j, self.images)
            src = self.eighth.at[there]
            remote(src, self.line.at[j], self.send, self.recv, {IMG: there}).start()

    def done(self):
        arrived = self.line.at[pl.ds(1, self.images - 1)]
        arrival(arrived, self.recv).wait()
        total = self.eighth[self.img].astype(F32)
        for j in range(1, self.images):
            total = total + self.line[j].astype(F32)
        self.own[...] = total.astype(BF16)
        arrival(arrived, self.send).wait()


class Gather:
    @staticmethod
    def scratch(shape):
        sems = pltpu.SemaphoreType.DMA((len(halves(shape[-1])), 2))
        return [sems, sems]

    def __init__(self, own, out, refs, part):
        send, recv = refs
        lanes = pl.ds(*halves(out.shape[-1])[part])
        self.own, self.out = own.at[:, lanes], out.at[:, :, lanes]
        self.send, self.recv = [send.at[part, k] for k in range(2)], [recv.at[part, k] for k in range(2)]
        self.row, col = lax.axis_index(ROW), lax.axis_index(COL)
        self.mine, self.pair = 4 * col, {COL: 1 - col}

    def steps(self):
        return [self.to_rows, self.to_pair, self.done]

    def to_rows(self):
        spot = self.out.at[self.mine + self.row]
        self.out[self.mine + self.row] = self.own[...]
        for j in range(1, 4):
            there = lax.rem(self.row + j, 4)
            remote(spot, spot, self.send[0], self.recv[0], {ROW: there}).start()

    def to_pair(self):
        arrival(self.out.at[pl.ds(0, 3)], self.recv[0]).wait()
        four = self.out.at[pl.ds(self.mine, 4)]
        remote(four, four, self.send[1], self.recv[1], self.pair).start()

    def done(self):
        four = self.out.at[pl.ds(0, 4)]
        arrival(four, self.recv[1]).wait()
        arrival(self.out.at[pl.ds(0, 3)], self.send[0]).wait()
        arrival(four, self.send[1]).wait()


class Line:
    @staticmethod
    def scratch(shape):
        return [pltpu.VMEM(shape[1:], BF16)] + LineSum.scratch(shape) + Gather.scratch(shape)

    def __init__(self, eighth, out, refs, part):
        own = refs[0]
        self.sum = LineSum(eighth, own, refs[1:4], part)
        self.gather = Gather(own, out, refs[4:], part)

    def steps(self):
        return [self.sum.to_line, self.to_rows, self.gather.to_pair, self.gather.done]

    def to_rows(self):
        self.sum.done()
        self.gather.to_rows()


class SmallSum:
    @staticmethod
    def scratch(shape):
        sizes = [lax.axis_size(IMG), lax.axis_size(ROW) * lax.axis_size(COL)]
        return [pltpu.VMEM((size,) + shape[1:], BF16) for size in sizes] + [
            pltpu.SemaphoreType.DMA((2,)),
            pltpu.SemaphoreType.DMA((2,)),
        ]

    def __init__(self, src, out, refs):
        self.src, self.out = src, out
        self.slots1, self.slots2, self.send, self.recv = refs

    def steps(self):
        return [self.to_line, self.to_plane, self.done]

    def to_line(self):
        here, total, _ = group_of(LINE)
        self.slots1[0] = self.src[here]
        for j in range(1, total):
            there = lax.rem(here + j, total)
            remote(
                self.src.at[there], self.slots1.at[j], self.send.at[0], self.recv.at[0], {IMG: there}
            ).start()

    def to_plane(self):
        gather_wait(LINE, self.slots1, self.recv.at[0])
        total = added([p.astype(F32) for p in in_order(LINE, self.slots1)])
        self.slots2[0] = total.astype(BF16)
        gather_start(PLANE, self.slots2, self.send.at[1], self.recv.at[1])

    def done(self):
        gather_wait(PLANE, self.slots2, self.recv.at[1])
        self.out[...] = added([p.astype(F32) for p in in_order(PLANE, self.slots2)])
        gather_wait(LINE, self.slots1, self.send.at[0])
        gather_wait(PLANE, self.slots2, self.send.at[1])


class Jobs:
    def __init__(self):
        self.queue = []

    def add(self, *jobs):
        lists = [job.steps() for job in jobs]
        for k in range(max(len(steps) for steps in lists)):
            self.queue += [steps[k] for steps in lists if k < len(steps)]

    def tick(self, count=1):
        for _ in range(min(count, len(self.queue))):
            self.queue.pop(0)()

    def finish(self):
        self.tick(len(self.queue))


def plane_jobs(src, eighth, refs):
    return [Plane(src, eighth, refs, part) for part in range(len(halves(src.shape[-1])))]


def part_jobs(kind, first, second, refs):
    return [kind(first, second, refs, part) for part in range(len(halves(first.shape[-1])))]


def line_jobs(eighth, out, refs):
    return [Line(eighth, out, refs, part) for part in range(len(halves(out.shape[-1])))]


STEP = 32
PIECE = 256
CHUNK = 256


class Refs:
    FLYING = 6 * 1024 * 1024

    def __init__(self):
        self.loads, self.stores, self.queue, self.flying = {}, {}, [], {}

    def load(self, ref, copy):
        self.loads[id(ref)] = copy
        self.queue.append((id(ref), int(np.prod(ref.shape)) * ref.dtype.itemsize))

    def start_loads(self, until=None):
        while self.queue:
            if until is None and sum(self.flying.values()) >= self.FLYING:
                return
            if until is not None and until in self.flying:
                return
            key, size = self.queue.pop(0)
            self.loads[key].start()
            self.flying[key] = size

    def ready(self, *refs):
        for ref in refs:
            self.start_loads(id(ref))
            self.loads.pop(id(ref)).wait()
            self.flying.pop(id(ref))
            self.start_loads()

    def push(self, *refs):
        for ref in refs:
            self.stores[id(ref)].start()

    def pushed(self, *refs):
        for ref in refs:
            self.stores.pop(id(ref)).wait()

    def flush(self):
        for copy in self.stores.values():
            copy.wait()


def fused(work, cid, ins, staged, outs, pushed, scratch, smem={}, far={}, far_outs={}):
    loaded, stored = {**ins, **staged}, {**outs, **pushed}
    sizes = (len(loaded), len(stored))

    def kernel(*refs):
        r = Refs()
        refs = list(refs)

        def take(count):
            taken = refs[:count]
            del refs[:count]
            return taken

        for key, ref in zip((*smem, *far), take(len(smem) + len(far))):
            setattr(r, key, ref)
        in_raw, out_raw = (take(count) for count in sizes)
        for key, ref in zip(far_outs, take(len(far_outs))):
            setattr(r, key, ref)
        for key, shape in scratch.items():
            setattr(r, key, take(len(shape)) if isinstance(shape, list) else take(1)[0])
        in_bufs, out_bufs = (take(count) for count in sizes)
        in_sems, out_sems = take(2)
        for keys, bufs in ((loaded, in_bufs), (stored, out_bufs)):
            for key, buf in zip(keys, bufs):
                setattr(r, key, buf)
        for k, (raw, buf) in enumerate(zip(in_raw, in_bufs)):
            r.load(buf, pltpu.make_async_copy(raw, buf, in_sems.at[k]))
        for k, (raw, buf) in enumerate(zip(out_raw, out_bufs)):
            r.stores[id(buf)] = pltpu.make_async_copy(buf, raw, out_sems.at[k])
        r.start_loads()
        signal_all()
        r.ready(*in_bufs[: len(ins)])
        work(r)
        r.push(*out_bufs[: len(outs)])
        r.flush()

    flat = []
    for shape in scratch.values():
        flat += shape if isinstance(shape, list) else [shape]
    flat += [pltpu.VMEM(a.shape, a.dtype) for a in (*loaded.values(), *stored.values())]
    flat += [pltpu.SemaphoreType.DMA((count,)) for count in sizes]
    anywhere, scalars = pl.BlockSpec(memory_space=pl.ANY), pl.BlockSpec(memory_space=pltpu.SMEM)
    result = pl.pallas_call(
        kernel,
        out_shape=[*stored.values(), *far_outs.values()],
        in_specs=[scalars] * len(smem) + [anywhere] * (len(far) + sizes[0]),
        out_specs=[anywhere] * (sizes[1] + len(far_outs)),
        scratch_shapes=flat,
        compiler_params=pltpu.CompilerParams(
            collective_id=cid, has_side_effects=True, vmem_limit_bytes=VMEM_LIMIT
        ),
    )(*smem.values(), *far.values(), *loaded.values())
    return types.SimpleNamespace(**dict(zip((*stored, *far_outs), result)))


def signal_all():
    barrier = pltpu.get_barrier_semaphore()
    for axes in (PLANE, LINE):
        _, total, device = group_of(axes)
        for step in range(1, total):
            pl.semaphore_signal(barrier, inc=1, device_id=device(step), device_id_type=MESH)


def wait_all():
    count = sum(group_of(axes)[1] - 1 for axes in (PLANE, LINE))
    pl.semaphore_wait(pltpu.get_barrier_semaphore(), count)


def added(parts):
    return functools.reduce(lambda a, b: a + b, parts)


class Exchange:
    @staticmethod
    def scratch(width):
        rows = 2 * width // 128
        sizes = [int(np.prod([lax.axis_size(a) for a in axes])) for axes in (PLANE, LINE)]
        return [
            pltpu.VMEM((sizes[0], rows, 128), F32),
            pltpu.VMEM((sizes[1], rows, 128), F32),
            pltpu.VMEM((rows, 128), F32),
            pltpu.SemaphoreType.DMA((2,)),
            pltpu.SemaphoreType.DMA((2,)),
        ]

    def __init__(self, refs):
        self.slots1, self.slots2, self.out, self.send, self.recv = refs
        self.half = self.out.shape[0] // 2

    def put(self, first, second):
        for k in range(self.half):
            self.slots1[0, k : k + 1, :] = first[:, 128 * k : 128 * (k + 1)]
            self.slots1[0, self.half + k : self.half + k + 1, :] = second[:, 128 * k : 128 * (k + 1)]
        gather_start(PLANE, self.slots1, self.send.at[0], self.recv.at[0])

    def line(self):
        gather_start(LINE, self.slots2, self.send.at[1], self.recv.at[1])

    def middle_sums(self):
        gather_wait(PLANE, self.slots1, self.recv.at[0])
        self.slots2[0] = added(in_order(PLANE, self.slots1))
        self.line()

    def finish_sums(self):
        gather_wait(LINE, self.slots2, self.recv.at[1])
        self.out[...] = added(in_order(LINE, self.slots2))
        self.drain()

    def middle_stats(self, count_ref, plane_count):
        half = self.half
        gather_wait(PLANE, self.slots1, self.recv.at[0])
        parts = in_order(PLANE, self.slots1)
        total = added([p[:half] for p in parts])
        center = total / plane_count
        spread = added([p[half:] for p in parts])
        for spot, part in enumerate(parts):
            count = count_ref[spot : spot + 1, :]
            away = part[:half] / jnp.maximum(count, 1.0) - center
            spread = spread + count * (away * away)
        self.slots2[0, :half] = total
        self.slots2[0, half:] = spread
        self.line()

    def finish_stats(self, plane_count):
        half = self.half
        total_count = plane_count * lax.axis_size(IMG)
        gather_wait(LINE, self.slots2, self.recv.at[1])
        parts = in_order(LINE, self.slots2)
        center = added([p[:half] for p in parts]) / total_count
        spread = added([p[half:] for p in parts])
        for part in parts:
            away = part[:half] / plane_count - center
            spread = spread + plane_count * (away * away)
        self.out[:half] = center
        self.out[half:] = spread / total_count
        self.drain()

    def drain(self):
        gather_wait(PLANE, self.slots1, self.send.at[0])
        gather_wait(LINE, self.slots2, self.send.at[1])

    def rows(self):
        out = self.out[...]
        first = [out[k : k + 1] for k in range(self.half)]
        second = [out[self.half + k : self.half + k + 1] for k in range(self.half)]
        return jnp.concatenate(first, axis=1), jnp.concatenate(second, axis=1)


class Halo:
    scratch = [pltpu.SemaphoreType.DMA((5,)), pltpu.SemaphoreType.DMA((5,))]

    def __init__(self, pad, reach, tile, window, sems, image=None):
        if image is not None:
            tile, window = (ref.at[pl.ds(image, 1)] for ref in (tile, window))
        self.row, self.rows, col, pair, above, below = halo_peers()
        self.pad, self.reach, self.tile, self.window = pad, reach, tile, window
        self.tile_rows, self.tile_cols = tile.shape[1], tile.shape[2]
        self.own = own = pl.ds(pl.multiple_of(HALF * col, HALF), self.tile_cols)
        spot = pl.ds(pl.multiple_of(2 * HALF * col, HALF), HALF)
        side = pl.ds(pl.multiple_of(HALF * (1 - col), HALF), HALF)
        mid = pl.ds(HALF, HALF)
        upper = pl.ds(pad - reach, reach)
        lower = pl.ds(pad + self.tile_rows, reach)
        send, recv = sems

        def copy(src, dst, k, device):
            return pltpu.make_async_remote_copy(
                src_ref=src,
                dst_ref=dst,
                send_sem=send.at[k],
                recv_sem=recv.at[k],
                device_id=device,
                device_id_type=MESH,
            )

        w = window
        self.to_pair = copy(
            tile.at[:, :, side], w.at[:, pl.ds(pad, self.tile_rows), spot], 0, pair
        )
        self.up = copy(tile.at[:, pl.ds(0, reach)], w.at[:, lower, own], 1, above)
        self.down = copy(
            tile.at[:, pl.ds(self.tile_rows - reach, reach)], w.at[:, upper, own], 2, below
        )
        self.from_below = copy(w.at[:, lower, mid], w.at[:, lower, spot], 3, pair)
        self.from_above = copy(w.at[:, upper, mid], w.at[:, upper, spot], 4, pair)

    def blank(self):
        window, pad, reach, tile_rows = self.window, self.pad, self.reach, self.tile_rows
        zero = jnp.zeros((window.shape[0],) + window.shape[2:], window.dtype)

        def fill(first, last):
            for k in range(first, last):
                window[:, k] = zero

        fill(0, pad - reach)
        fill(pad + tile_rows + reach, 2 * pad + tile_rows)

        @pl.when(self.row == 0)
        def _():
            fill(pad - reach, pad)

        @pl.when(self.row == self.rows - 1)
        def _():
            fill(pad + tile_rows, pad + tile_rows + reach)

    def start(self):
        @pl.when(self.row > 0)
        def _():
            self.up.start()

        @pl.when(self.row < self.rows - 1)
        def _():
            self.down.start()

        self.to_pair.start()
        for n in range(self.tile.shape[0]):
            self.window[n, pl.ds(self.pad, self.tile_rows), self.own, :] = self.tile[n]

    def middle(self):
        @pl.when(self.row < self.rows - 1)
        def _():
            self.up.wait_recv()
            self.from_below.start()

        @pl.when(self.row > 0)
        def _():
            self.down.wait_recv()
            self.from_above.start()

    def finish(self):
        self.to_pair.wait()

        @pl.when(self.row < self.rows - 1)
        def _():
            self.down.wait_send()
            self.from_below.wait()

        @pl.when(self.row > 0)
        def _():
            self.up.wait_send()
            self.from_above.wait()


def gauss(x):
    bell = jnp.exp2(x * (x * -0.7213475204444817))
    d = 1.0 + (0.3275911 * 0.7071067811865476) * jnp.abs(x)
    t = pl.reciprocal(d, approx=True)
    t = t * (2.0 - d * t)
    poly = 0.5307027145 * t - 0.7265760135
    poly = poly * t + 0.7107068705
    poly = poly * t - 0.142248368
    poly = poly * t + 0.127414796
    tail = poly * (t * bell)
    return jnp.where(x < 0, tail, 1.0 - tail), bell * 0.3989422804014327


def wide(mask, width):
    return jnp.concatenate([mask] * (width // 128), axis=1)


def place(ref, i, lanes):
    if len(ref.shape) == 4:
        return (i // ref.shape[1], lax.rem(i, ref.shape[1]), slice(None), lanes)
    return (pl.ds(pl.multiple_of(i * STEP, STEP), STEP), lanes)


def by_rows(pixels, width, work, sums=0):
    pieces = [slice(l, l + PIECE) for l in range(0, width, PIECE)]

    def one(i, carry):
        out = []
        for k, lanes in enumerate(pieces):
            got = work(i, lanes)
            for j in range(sums):
                folded = jnp.sum(got[j].reshape(STEP // 8, 8, PIECE), axis=0)
                out.append(carry[k * sums + j] + folded)
        return tuple(out)

    start = tuple(jnp.zeros((8, PIECE), F32) for _ in range(sums * len(pieces)))
    final = lax.fori_loop(0, pixels // STEP, one, start)
    rows = []
    for j in range(sums):
        parts = [jnp.sum(final[k * sums + j], axis=0, keepdims=True) for k in range(len(pieces))]
        rows.append(jnp.concatenate(parts, axis=1))
    return rows


NORM_ROWS = 8


def norm_table(exchange, gain_ref, shift_ref, out_ref, first):
    mean, var = exchange.rows()
    lanes = slice(first, first + mean.shape[1])
    inv = lax.rsqrt(var + EPSILON)
    out_ref[...] = jnp.zeros_like(out_ref)
    out_ref[0:1, :] = mean
    out_ref[1:2, :] = inv
    out_ref[2:3, :] = inv * gain_ref[:, lanes]
    out_ref[3:4, :] = shift_ref[:, lanes]
    out_ref[4:5, :] = var


def normed(u_ref, norm, i, lanes):
    away = u_ref[place(u_ref, i, lanes)].astype(F32) - norm[0:1, lanes]
    return away * norm[2:3, lanes] + norm[3:4, lanes], away


def activate(u_ref, norm, mask, h_ref, residual=None, slope=None, keep=None):
    def work(i, lanes):
        x, _ = normed(u_ref, norm, i, lanes)
        if residual is not None:
            x = x + residual[place(residual, i, lanes)].astype(F32)
        below, bell = gauss(x)
        m = wide(mask[place(mask, i, slice(None))], PIECE)
        h_ref[place(h_ref, i, lanes)] = (x * below * m).astype(BF16)
        if slope is not None:
            slope[place(slope, i, lanes)] = ((below + x * bell) * m).astype(BF16)
        if keep is not None:
            keep[place(keep, i, lanes)] = u_ref[place(u_ref, i, lanes)].astype(BF16)

    by_rows(mask.shape[0], norm.shape[1], work)


def device_stats(u_ref, mask, count):
    pixels, width = u_ref.shape

    def total_of(i, lanes):
        m = wide(mask[place(mask, i, slice(None))], PIECE)
        return (u_ref[place(u_ref, i, lanes)] * m,)

    (total,) = by_rows(pixels, width, total_of, 1)
    center = total / jnp.maximum(wide(count, width), 1.0)

    def spread_of(i, lanes):
        m = wide(mask[place(mask, i, slice(None))], PIECE)
        away = u_ref[place(u_ref, i, lanes)] - center[:, lanes]
        return (away * away * m,)

    (spread,) = by_rows(pixels, width, spread_of, 1)
    return total, spread


def product(a_ref, w_ref, o_ref, turned=False):
    dims = (((1,), (1 if turned else 0,)), ((), ()))

    def one(i, carry):
        rows = pl.ds(pl.multiple_of(i * CHUNK, CHUNK), CHUNK)
        o_ref[rows, :] = lax.dot_general(
            a_ref[rows, :], w_ref[...], dims, preferred_element_type=F32
        )
        return carry

    lax.fori_loop(0, a_ref.shape[0] // CHUNK, one, 0)


def turn(a_ref, t_ref):
    def one(i, carry):
        rows = pl.ds(pl.multiple_of(i * CHUNK, CHUNK), CHUNK)
        t_ref[:, rows] = a_ref[rows, :].T
        return carry

    lax.fori_loop(0, a_ref.shape[0] // CHUNK, one, 0)


def put_lanes(ref, first, value):
    width = ref.shape[-1]
    at, stop = first, first + value.shape[1]
    while at < stop:
        cut = at // width
        until = min(stop, (cut + 1) * width)
        part = value[:, at - first : until - first].astype(ref.dtype)
        lanes = slice(at - cut * width, until - cut * width)
        if len(ref.shape) == 4:
            ref[cut, :, :, lanes] = part.reshape(ref.shape[1:3] + part.shape[1:])
        else:
            ref[cut, :, lanes] = part
        at = until


def weight_product(t_ref, b_ref, gw_ref):
    channels = b_ref.shape[1]
    for first in range(0, channels, 512):
        value = jnp.dot(t_ref[...], b_ref[:, first : first + 512], preferred_element_type=F32)
        if len(gw_ref.shape) == 4 and gw_ref.shape[-1] == channels:
            part = value.astype(gw_ref.dtype).reshape(gw_ref.shape[:3] + (512,))
            gw_ref[:, :, :, first : first + 512] = part
        else:
            put_lanes(gw_ref, first, value)


def put_rows(ref, first, value):
    if len(ref.shape) == 3:
        ref[0, first : first + value.shape[0], :] = value.astype(ref.dtype)
        return
    rows = ref.shape[2]
    at, stop = first, first + value.shape[0]
    while at < stop:
        eighth = at // rows
        until = min(stop, (eighth + 1) * rows)
        low, high = at - eighth * rows, until - eighth * rows
        part = value[at - first : until - first].astype(ref.dtype)
        ref[eighth // 8, eighth % 8, low:high, :] = part
        at = until


def norm_back(e_ref, u_ref, norm, sums, pixel_count, mask, out_ref):
    sum_grad, sum_unit = (s * (1.0 / pixel_count) for s in sums)

    def work(i, lanes):
        away = u_ref[place(u_ref, i, lanes)].astype(F32) - norm[0:1, lanes]
        unit = away * norm[1:2, lanes]
        e = e_ref[place(e_ref, i, lanes)].astype(F32)
        m = wide(mask[place(mask, i, slice(None))], PIECE)
        grad = norm[2:3, lanes] * (e - sum_grad[:, lanes] - unit * sum_unit[:, lanes]) * m
        out_ref[place(out_ref, i, lanes)] = grad.astype(BF16)

    by_rows(mask.shape[0], norm.shape[1], work)


def gelu_grad(e_ref, u_ref, norm, mask):
    def work(i, lanes):
        x, away = normed(u_ref, norm, i, lanes)
        below, bell = gauss(x)
        m = wide(mask[place(mask, i, slice(None))], PIECE)
        e = e_ref[place(e_ref, i, lanes)] * (below + x * bell) * m
        e_ref[place(e_ref, i, lanes)] = e
        return e, e * (away * norm[1:2, lanes])

    return by_rows(mask.shape[0], norm.shape[1], work, 2)


def put_sums(exchange, out_ref):
    first, second = exchange.rows()
    out_ref[...] = jnp.zeros_like(out_ref)
    out_ref[0:1, :] = first
    out_ref[1:2, :] = second
    return first, second


def order_taps(rows, width):
    to = lax.broadcasted_iota(jnp.int32, (rows, width), 0)
    at = lax.broadcasted_iota(jnp.int32, (rows, width), 1)
    picked = jnp.where(to < 16, 2 * to, 2 * (to - 16) + 1)
    real = lax.rem(to, 16) < 9
    return jnp.where(jnp.logical_and(at == picked, real), 1.0, 0.0)


def make_mask(r, tile_cols):
    row, col = lax.axis_index(ROW), lax.axis_index(COL)
    rows, cols = lax.axis_size(ROW), lax.axis_size(COL)
    images = r.orientation.shape[0]
    tile_rows = r.mask.shape[0] // images // tile_cols
    tall = [r.orientation[n].astype(F32) for n in range(images)]
    for n in range(images):

        def fill(i, carry, n=n):
            column = lax.broadcasted_iota(jnp.int32, (tile_cols, 128), 0) + col * tile_cols
            portrait = jnp.where(column < SHORT, 1.0, 0.0)
            line = jnp.zeros((tile_cols, 128), jnp.int32) + (row * tile_rows + i)
            landscape = jnp.where(line < SHORT, 1.0, 0.0)
            at = (n * tile_rows + i) * tile_cols
            r.mask[pl.ds(pl.multiple_of(at, tile_cols), tile_cols), :] = (
                landscape * (1.0 - tall[n]) + portrait * tall[n]
            )
            return carry

        lax.fori_loop(0, tile_rows, fill, 0)

    def count(row, col):
        return (
            jnp.clip(SHORT - row * tile_rows, 0, tile_rows) * tile_cols,
            jnp.clip(SHORT - col * tile_cols, 0, tile_cols) * tile_rows,
        )

    def fill_count(at, row, col):
        flat, upright = (c.astype(F32) for c in count(row, col))
        total = added([flat * (1.0 - t) + upright * t for t in tall])
        r.counts[at : at + 1, :] = jnp.zeros((1, 128), F32) + total

    r.counts[...] = jnp.zeros_like(r.counts)
    for k in range(rows * cols):
        fill_count(k, jnp.int32(k // cols), jnp.int32(k % cols))
    fill_count(8, row, col)


def make_corners(r, cols):
    images, _, pixels = r.up.shape
    tile_cols = cols - HALF
    order = order_taps(32, r.base.shape[1]).astype(BF16)
    tap = lax.broadcasted_iota(jnp.int32, (16, pixels), 0)
    pixel = lax.broadcasted_iota(jnp.int32, (16, pixels), 1)
    up0 = pixel // tile_cols + PAD + 2 * (tap // 3 - 1)
    left0 = lax.rem(pixel, tile_cols) + HALF * lax.axis_index(COL) + 2 * (lax.rem(tap, 3) - 1)
    for n in range(images):
        base = r.base[n * pixels : (n + 1) * pixels, :].astype(F32).astype(BF16)
        moved = lax.dot_general(
            order, base, (((1,), (1,)), ((), ())), preferred_element_type=F32
        ).astype(jnp.int32)
        r.up[n] = moved[:16] + up0
        r.left[n] = moved[16:] + left0


def first(plane_count, r):
    ex, ex2 = Exchange(r.ex1), Exchange(r.ex2)
    images, all_rows, cols, width = r.rim.shape
    halos = [Halo(PAD, REACH, r.tile, r.rim, r.halo[2 * n : 2 * n + 2], n) for n in range(images)]
    make_mask(r, cols - HALF)
    r.ready(r.feature, r.w_reduce)
    product(r.feature, r.w_reduce, r.u_a1)
    r.push(r.u_a1)
    total, spread = device_stats(r.u_a1, r.mask, r.counts[8:9, :])
    wait_all()
    ex.put(total, spread)
    make_corners(r, cols)
    ex.middle_stats(r.counts, plane_count)
    for halo in halos:
        halo.blank()
    order = order_taps(32, r.w_offset.shape[0]).astype(BF16)
    for tap in range(9):
        columns = r.w_offset[:, tap * width : (tap + 1) * width]
        r.w_off[32 * tap : 32 * tap + 32, :] = jnp.dot(
            order, columns, preferred_element_type=F32
        ).astype(BF16)
    ex.finish_stats(plane_count)
    norm_table(ex, r.scale, r.shift, r.norm_a1, 0)
    activate(r.u_a1, r.norm_a1, r.mask, r.tile)
    halos[0].start()
    select_cells(r, cols)
    r.push(r.select)
    r.ready(r.w_deform)
    turn(r.w_deform, r.w_turned)
    for n, halo in enumerate(halos):
        if n == 0:
            halo.middle()
            halos[1].start()
        halo.finish()
        for k in range(0, all_rows, 8):
            lines = r.rim[n, k : k + 8].reshape(8 * cols, width)
            r.rim_t[n, :, k * cols : (k + 8) * cols] = lines.T
        offset_fractions(r, cols, n)
        sample_units(r, cols, n, 0)
        if n + 1 < images:
            halos[n + 1].middle()
        sample_units(r, cols, n, 1)
    r.push(r.rim, r.fr, r.fc, r.samples, r.u_a2)
    total, spread = device_stats(r.u_a2, r.mask, r.counts[8:9, :])
    ex2.put(total, spread)
    ex2.middle_stats(r.counts, plane_count)
    ex2.finish_stats(plane_count)
    norm_table(ex2, r.scale, r.shift, r.norm_a2, width)


def offset_fractions(r, cols, n):
    _, width, cells = r.rim_t.shape
    column = lax.rem(lax.broadcasted_iota(jnp.int32, (32, cells), 1), cols)
    r.spread[...] = jnp.dot(r.w_off[...], r.rim_t[n], preferred_element_type=F32)
    total = None
    for tap in range(9):
        i, j = 2 * (tap // 3 - 1), 2 * (tap % 3 - 1)
        term = r.spread[32 * tap : 32 * tap + 32, :]
        shift = -(i * cols + j) % cells
        if shift:
            term = pltpu.roll(term, shift, axis=1)
        if j < 0:
            term = jnp.where(column >= -j, term, 0.0)
        if j > 0:
            term = jnp.where(column < cols - j, term, 0.0)
        total = term if total is None else total + term
    parts = []
    for _ in range(3):
        parts.append(total.astype(BF16))
        total = total - parts[-1].astype(F32)
    on_tile = lax.dot_general(
        jnp.concatenate(parts, axis=0),
        r.select[...],
        (((1,), (1,)), ((), ())),
        preferred_element_type=F32,
    )
    offsets = on_tile[:32] + on_tile[32:64] + on_tile[64:]
    fraction = 1.0 / (1.0 + jnp.exp(-offsets))
    r.fr[n] = fraction[:16]
    r.fc[n] = fraction[16:]


def sample_units(r, cols, n, b):
    block = r.table.shape[1]
    width = r.rim_t.shape[1]
    lanes = slice(b * block, (b + 1) * block)
    mine = slice((2 * n + b) * block, (2 * n + b + 1) * block)
    base = b * (BLOCK_ROWS * cols)
    for tap in range(9):
        row_w, _, col_w, _ = tap_weights(tap, b, cols, r.up, r.left, r.fr, r.fc, n, lanes)
        write_table(r.table, 0, row_w, col_w, tap // 3, cols)
        _, start, stop = tap_span(tap // 3, cols)
        cells = r.rim_t[n, :, base + start : base + stop]
        value = jnp.dot(cells, r.table[start:stop, :], preferred_element_type=F32)
        r.samples[tap * width : (tap + 1) * width, mine] = value.astype(BF16)
    deformed = jnp.dot(r.w_turned[...], r.samples[:, mine], preferred_element_type=F32)
    r.u_a2[mine, :] = deformed.T


def finish_kernel(unbias, count, *refs):
    ins, outs, rest = refs[:count], refs[count : count + 17], refs[count + 17 :]
    bufs, out_bufs, sems, out_sems = rest[:count], rest[count : count + 15], rest[-2], rest[-1]
    loads = [pltpu.make_async_copy(ins[k], bufs[k], sems.at[k]) for k in range(count)]
    stores = [pltpu.make_async_copy(out_bufs[k], outs[k], out_sems.at[k]) for k in range(15)]
    stores += [
        pltpu.make_async_copy(bufs[count - 2 + k], outs[15 + k], out_sems.at[15 + k]) for k in range(2)
    ]
    for load in loads:
        load.start()
    conv_b, reduce_b, reduce_a, expand_b, expand_a, deform, off = bufs[:7]
    tables = bufs[7:19]
    for load in loads[:7]:
        load.wait()
    for k, src in enumerate((expand_b, expand_a, deform)):
        rows = src.shape[1]
        for s in range(8):
            out_bufs[3 + k][s * rows : (s + 1) * rows, :] = src[s].astype(F32)
        stores[3 + k].start()
    for k, src in enumerate((conv_b, reduce_b, reduce_a)):
        eighth = src.shape[1]
        for s in range(0, 8, 2):
            rows = jnp.concatenate([src[s], src[s + 1]], axis=0).astype(F32)
            out_bufs[k][:, s * eighth : (s + 2) * eighth] = rows.T
        stores[k].start()
    for k in range(2):
        loads[count - 2 + k].wait()
        stores[15 + k].start()
    rest, total = off[...], None
    order = order_taps(32, 18).astype(BF16)
    for _ in range(3):
        part = rest.astype(BF16)
        rest = rest - part.astype(F32)
        term = lax.dot_general(order, part, (((0,), (0,)), ((), ())), preferred_element_type=F32)
        total = term if total is None else total + term
    out_bufs[6][...] = total
    for load in loads[7 : count - 2]:
        load.wait()
    for k in range(4):
        group, which = tables[3 * k : 3 * k + 3], out_bufs[7 + 2 * k : 9 + 2 * k]
        norms = k >= 2
        for out, row in zip(which, (0, 4) if norms else (1, 0)):
            at = 0
            for table in group:
                for first_lane in range(0, table.shape[1], 128):
                    value = table[row : row + 1, first_lane : first_lane + 128]
                    out[at : at + 1, :] = value * unbias if norms and row == 4 else value
                    at += 1
    for store in stores[6:15]:
        store.start()
    for store in stores:
        store.wait()


def forward(plane_count, r):
    ex_a3, ex_b1, ex_b2 = Exchange(r.ex_a3), Exchange(r.ex_b1), Exchange(r.ex_b2)
    ex_b3, ex_sums = Exchange(r.ex_b3), Exchange(r.ex_sums)
    halo = Halo(2, 2, r.tile, r.rim_b, r.halo)
    halo.blank()
    width = r.h2_a.shape[1]
    count = r.counts[8:9, :]

    def exchange(ex, u_ref):
        ex.put(*device_stats(u_ref, r.mask, count))
        ex.middle_stats(r.counts, plane_count)

    r.ready(r.u_a2)
    activate(r.u_a2, r.norm_a2, r.mask, r.h2_a)
    r.push(r.h2_a)
    r.ready(r.w_expand_a)
    product(r.h2_a, r.w_expand_a, r.wide)
    wait_all()
    exchange(ex_a3, r.wide)
    r.ready(r.feature, r.w_reduce)
    ex_a3.finish_stats(plane_count)
    norm_table(ex_a3, r.scale_a, r.shift_a, r.norm_a3, 2 * width)
    activate(r.wide, r.norm_a3, r.mask, r.middle, r.feature, r.slope_a, r.u_a3)
    r.push(r.middle, r.slope_a, r.u_a3)
    cotangent = pltpu.make_async_copy(r.cotangent, r.feature, r.far_sems.at[0])
    cotangent.start()
    product(r.middle, r.w_reduce, r.u_b1)
    r.push(r.u_b1)
    exchange(ex_b1, r.u_b1)
    ex_b1.finish_stats(plane_count)
    norm_table(ex_b1, r.scale_b, r.shift_b, r.norm_b1, 0)
    activate(r.u_b1, r.norm_b1, r.mask, r.tile)
    halo.start()
    halo.middle()
    halo.finish()
    r.push(r.rim_b)
    build_shifted(r.rim_b, r.shifted)
    r.ready(r.w_conv)
    conv_product(r.shifted, r.w_conv, r.u_b2)
    r.push(r.u_b2)
    exchange(ex_b2, r.u_b2)
    ex_b2.finish_stats(plane_count)
    norm_table(ex_b2, r.scale_b, r.shift_b, r.norm_b2, width)
    activate(r.u_b2, r.norm_b2, r.mask, r.h2_b)
    r.push(r.h2_b)
    r.ready(r.w_expand_b)
    product(r.h2_b, r.w_expand_b, r.wide)
    exchange(ex_b3, r.wide)
    cotangent.wait()
    r.pushed(r.slope_a, r.u_a3)
    e_b3, u_b3, norm = r.slope_a, r.u_a3, r.norm_b3
    ex_b3.finish_stats(plane_count)
    norm_table(ex_b3, r.scale_b, r.shift_b, norm, 2 * width)

    def work(i, lanes):
        x, away = normed(r.wide, norm, i, lanes)
        at = place(r.wide, i, lanes)
        u_b3[at] = r.wide[at].astype(BF16)
        x = x + r.middle[at].astype(F32)
        below, bell = gauss(x)
        m = wide(r.mask[place(r.mask, i, slice(None))], PIECE)
        r.feature_out[at] = (x * below * m).astype(BF16)
        e = (below + x * bell) * r.feature[at].astype(F32) * m
        e_b3[at] = e.astype(BF16)
        return e, e * (away * norm[1:2, lanes])

    sums = by_rows(r.wide.shape[0], r.wide.shape[1], work, 2)
    ex_sums.put(*sums)
    far = [
        pltpu.make_async_copy(e_b3, r.e_b3, r.far_sems.at[1]),
        pltpu.make_async_copy(u_b3, r.u_b3, r.far_sems.at[2]),
    ]
    for copy in far:
        copy.start()
    r.push(r.feature_out)
    ex_sums.middle_sums()
    ex_sums.finish_sums()
    put_sums(ex_sums, r.sums_b3)
    for copy in far:
        copy.wait()


def backward_b(pixel_count, direct, r):
    ex2, ex1 = Exchange(r.ex2), Exchange(r.ex1)
    halo = Halo(2, 2, r.tile, r.back_rim, r.halo)
    halo.blank()
    r.ready(r.e_b3, r.u_b3)
    sums = (r.sums_b3[0:1, :], r.sums_b3[1:2, :])
    norm_back(r.e_b3, r.u_b3, r.norm_b3, sums, pixel_count, r.mask, r.geo)
    r.ready(r.w_expand)
    product(r.geo, r.w_expand, r.grad, turned=True)
    r.ready(r.u_b2)
    sums = gelu_grad(r.grad, r.u_b2, r.norm_b2, r.mask)
    wait_all()
    ex2.put(*sums)
    r.ready(r.h2_b)
    turn(r.h2_b, r.turned)
    ex2.middle_sums()
    weight_product(r.turned, r.geo, r.gw_expand)
    jobs = Jobs()
    if direct:
        jobs.add(*plane_jobs(r.gw_expand, r.eighth_expand_b, r.plane_expand_b))
    else:
        r.push(r.gw_expand)
    jobs.tick(2)
    ex2.finish_sums()
    sums = put_sums(ex2, r.sums_b2)
    norm_back(r.grad, r.u_b2, r.norm_b2, sums, pixel_count, r.mask, r.tile)
    halo.start()
    tile_rows, tile_cols, width = r.tile.shape[1:]
    pixels = tile_rows * tile_cols
    for n in range(r.tile.shape[0]):
        for k in range(0, tile_rows, 8):
            at = n * pixels + k * tile_cols
            block = r.tile[n, k : k + 8].reshape(8 * tile_cols, width)
            r.turned[:, at : at + 8 * tile_cols] = block.T
    r.ready(r.rim_b)
    build_shifted(r.rim_b, r.shifted)
    conv_weight_product(r.turned, r.shifted, r.gw_conv, 0)
    halo.middle()
    jobs.tick(2)
    conv_weight_product(r.turned, r.shifted, r.gw_conv, 1)
    halo.finish()
    build_shifted(r.back_rim, r.back_shifted)
    r.ready(r.w_conv)
    unconv_product(r.back_shifted, r.w_conv, r.grad)
    r.ready(r.u_b1)
    sums = gelu_grad(r.grad, r.u_b1, r.norm_b1, r.mask)
    ex1.put(*sums)
    jobs.tick(2)
    ex1.middle_sums()
    conv_weight_product(r.turned, r.shifted, r.gw_conv, 2)
    r.push(r.gw_conv)
    jobs.finish()
    if direct:
        r.push(r.eighth_expand_b)
    ex1.finish_sums()
    sums = put_sums(ex1, r.sums_b1)
    norm_back(r.grad, r.u_b1, r.norm_b1, sums, pixel_count, r.mask, r.gro_b)


def backward_a(pixel_count, direct, r):
    ex3, ex2 = Exchange(r.ex3), Exchange(r.ex2)
    conv, line = Jobs(), Jobs()
    r.ready(r.gro_b, r.w_reduce)
    product(r.gro_b, r.w_reduce, r.wide, turned=True)
    wait_all()
    if direct:
        r.ready(r.src_conv_b, r.eighth_expand_b)
        conv.add(*plane_jobs(r.src_conv_b, r.eighth_conv_b, r.plane_conv_b))
        line.add(*line_jobs(r.eighth_expand_b, r.sum_expand_b, r.line_expand_b))
    conv.tick(2)
    line.tick(2)
    r.ready(r.e_b3, r.slope_a, r.u_a3)
    norm = r.norm_a3

    def work(i, lanes):
        at = place(r.wide, i, lanes)
        e = (r.wide[at] + r.e_b3[at].astype(F32)) * r.slope_a[at].astype(F32)
        r.e_a3[at] = e.astype(BF16)
        away = r.u_a3[at].astype(F32) - norm[0:1, lanes]
        return e, e * (away * norm[1:2, lanes])

    sums = by_rows(r.wide.shape[0], r.wide.shape[1], work, 2)
    ex3.put(*sums)
    conv.tick(2)
    r.push(r.e_a3)
    turn(r.gro_b, r.turned)
    ex3.middle_sums()
    r.ready(r.middle)
    weight_product(r.turned, r.middle, r.gw_reduce)
    r.push(r.gw_reduce)
    line.tick(2)
    ex3.finish_sums()
    sums = put_sums(ex3, r.sums_a3)
    norm_back(r.e_a3, r.u_a3, norm, sums, pixel_count, r.mask, r.e_b3)
    r.ready(r.w_expand)
    product(r.e_b3, r.w_expand, r.grad, turned=True)
    r.ready(r.u_a2)
    sums = gelu_grad(r.grad, r.u_a2, r.norm_a2, r.mask)
    ex2.put(*sums)
    conv.tick(2)
    line.tick(2)
    r.ready(r.h2_a)
    turn(r.h2_a, r.turned)
    ex2.middle_sums()
    weight_product(r.turned, r.e_b3, r.gw_expand)
    r.push(r.gw_expand)
    ex2.finish_sums()
    sums = put_sums(ex2, r.sums_a2)
    norm_back(r.grad, r.u_a2, r.norm_a2, sums, pixel_count, r.mask, r.gd)
    conv.finish()
    line.finish()
    if direct:
        r.push(r.eighth_conv_b, r.sum_expand_b)


def unsample(r, plan):
    width = r.rim.shape[2]
    cols = r.table.shape[0] // WINDOW
    pixels = r.up.shape[2] // 2
    r.spill[...] = jnp.zeros_like(r.spill)
    r.grad_row[...] = jnp.zeros_like(r.grad_row)
    r.grad_col[...] = jnp.zeros_like(r.grad_col)

    def unit(step, carry):
        n, block = step // 2, lax.rem(step, 2)
        lanes = pl.ds(pl.multiple_of(block * pixels, pixels), pixels)
        base = block * (BLOCK_ROWS * cols)
        grad_in = r.turned[:, pl.ds(pl.multiple_of(step * pixels, pixels), pixels)]
        for group in range(3):
            first, start, stop = tap_span(group, cols)
            cells = pl.ds(pl.multiple_of(base + start, 128), stop - start)
            for j in range(3):
                tap = 3 * group + j
                spot = slice(j * pixels, (j + 1) * pixels)
                row_w, row_s, col_w, col_s = tap_weights(
                    tap, block, cols, r.up, r.left, r.fr, r.fc, n, lanes
                )
                write_table(r.table, j * pixels, row_w, col_w, group, cols)
                grad = jnp.dot(
                    r.w_deform[tap * width : (tap + 1) * width, :],
                    grad_in,
                    preferred_element_type=F32,
                ).astype(BF16)
                r.grads[:, spot] = grad
                scores = jnp.dot(r.rim[n, cells, :], grad, preferred_element_type=F32)
                by_value = jnp.zeros((cols, pixels), F32)
                by_slope = jnp.zeros((cols, pixels), F32)
                for k in range(first, first + SPAN):
                    line = scores[k * cols - start : (k + 1) * cols - start]
                    by_value = by_value + line * row_w[k : k + 1, :]
                    by_slope = by_slope + line * row_s[k : k + 1, :]
                r.grad_row[n, tap : tap + 1, lanes] = jnp.sum(
                    by_slope * col_w, axis=0, keepdims=True
                )
                r.grad_col[n, tap : tap + 1, lanes] = jnp.sum(
                    by_value * col_s, axis=0, keepdims=True
                )
            r.spill[n, cells, :] += lax.dot_general(
                r.table[start:stop, :],
                r.grads[...],
                (((1,), (1,)), ((), ())),
                preferred_element_type=F32,
            )
            for turn_at in range(4):
                if 3 * turn_at + group in plan:

                    @pl.when(step == turn_at)
                    def _(slot=3 * turn_at + group):
                        plan[slot]()

        return carry

    lax.fori_loop(0, 4, unit, 0)


def select_cells(r, cols):
    off = HALF * lax.axis_index(COL)
    cells = r.select.shape[1]

    def fill(i, carry):
        ids = lax.broadcasted_iota(jnp.int32, (STEP, cells), 1)
        pixel = lax.broadcasted_iota(jnp.int32, (STEP, cells), 0)
        hit = ids == pixel + (i + PAD) * cols + off
        r.select[pl.ds(pl.multiple_of(i * STEP, STEP), STEP), :] = jnp.where(hit, 1.0, 0.0).astype(
            BF16
        )
        return carry

    lax.fori_loop(0, r.select.shape[0] // STEP, fill, 0)


def unoffset(r, n):
    images, cells, width = r.rim.shape
    cols = r.table.shape[0] // WINDOW
    column = lax.rem(lax.broadcasted_iota(jnp.int32, (32, cells), 1), cols)
    parts = []
    for grad, frac in ((r.grad_row, r.fr), (r.grad_col, r.fc)):
        f = frac[n]
        parts.append(grad[n] * f * (1.0 - f))
    go = jnp.concatenate(parts, axis=0).astype(BF16)
    on_tile = jnp.dot(go, r.select[...], preferred_element_type=F32)
    for tap in range(9):
        i, j = 2 * (tap // 3 - 1), 2 * (tap % 3 - 1)
        kept = on_tile
        if j < 0:
            kept = jnp.where(column >= -j, on_tile, 0.0)
        if j > 0:
            kept = jnp.where(column < cols - j, on_tile, 0.0)
        shift = (i * cols + j) % cells
        if shift:
            kept = pltpu.roll(kept, shift, axis=1)
        r.on_cells[32 * tap : 32 * tap + 32, :] = kept.astype(BF16)
    grad = jnp.dot(r.on_cells[...], r.rim[n], preferred_element_type=F32)
    if n == 0:
        r.gw_off_sum[...] = grad
    else:
        r.gw_off_sum[...] += grad
    for first in range(0, cells, 512):
        r.spill[n, first : first + 512, :] += lax.dot_general(
            r.on_cells[:, first : first + 512],
            r.w_off[...],
            (((0,), (0,)), ((), ())),
            preferred_element_type=F32,
        )
    if n == images - 1:
        for tap in range(9):
            put_lanes(r.gw_off, tap * width, r.gw_off_sum[32 * tap : 32 * tap + 32, :])


class Spill:
    @staticmethod
    def scratch(images, tile_rows, tile_cols, width):
        side = pltpu.VMEM((images, tile_rows + 2 * PAD, HALF, width), BF16)
        strip = pltpu.VMEM((images, REACH, tile_cols, width), BF16)
        sems = pltpu.SemaphoreType.DMA((3,))
        return [side, side, strip, strip, strip, strip, sems, sems]

    def __init__(self, spill, grad, cols, refs, image):
        self.spill, self.grad, self.cols = spill.at[pl.ds(image, 1)], grad, cols
        self.image = image
        self.side_out, self.side_in, self.up_out, self.down_out, self.up_in, self.down_in = refs[:6]
        send, recv = refs[6:]
        self.row, self.rows, col, pair, above, below = halo_peers()
        self.images, self.all_rows = self.side_out.shape[:2]
        self.tile_rows, self.tile_cols = self.all_rows - 2 * PAD, self.up_out.shape[2]
        self.off, self.away, self.near = HALF * col, 2 * HALF * (1 - col), HALF * (1 - col)
        self.side = remote(self.side_out, self.side_in, send.at[0], recv.at[0], pair)
        self.up = remote(self.up_out, self.down_in, send.at[1], recv.at[1], above)
        self.down = remote(self.down_out, self.up_in, send.at[2], recv.at[2], below)

    def cells(self, k, first, count):
        return pl.ds(pl.multiple_of(k * self.cols + first, HALF), count)

    def start(self):
        def cast(k, carry):
            for n in range(self.images):
                self.side_out[n, k] = self.spill[n, self.cells(k, self.away, HALF), :].astype(BF16)
            return carry

        lax.fori_loop(0, self.all_rows, cast, 0)
        self.side.start()

    def edge(self, buffer, first):
        near = pl.ds(pl.multiple_of(self.near, HALF), HALF)

        def one(k, carry):
            for n in range(self.images):
                at = first + k
                buffer[n, k] = self.spill[n, self.cells(at, self.off, self.tile_cols), :].astype(BF16)
                part = self.spill[n, self.cells(at, HALF, HALF), :]
                buffer[n, k, near, :] = (part + self.side_in[n, at].astype(F32)).astype(BF16)
            return carry

        lax.fori_loop(0, REACH, one, 0)

    def middle(self):
        self.side.wait_recv()

        @pl.when(self.row > 0)
        def _():
            self.edge(self.up_out, PAD - REACH)
            self.up.start()

        @pl.when(self.row < self.rows - 1)
        def _():
            self.edge(self.down_out, PAD + self.tile_rows)
            self.down.start()

    def pixels(self, n, k, first, count):
        at = ((self.image + n) * self.tile_rows + k) * self.tile_cols + first
        return pl.ds(pl.multiple_of(at, HALF), count)

    def own(self):
        def fill(k, carry):
            for n in range(self.images):
                home = self.spill[n, self.cells(PAD + k, self.off, self.tile_cols), :]
                self.grad[self.pixels(n, k, 0, self.tile_cols), :] = home
                self.grad[self.pixels(n, k, self.near, HALF), :] += self.side_in[n, PAD + k].astype(F32)
            return carry

        lax.fori_loop(0, self.tile_rows, fill, 0)

    def finish(self):
        def arrive(buffer, first):
            def one(k, carry):
                for n in range(self.images):
                    at = self.pixels(n, first + k, 0, self.tile_cols)
                    self.grad[at, :] += buffer[n, k].astype(F32)
                return carry

            lax.fori_loop(0, REACH, one, 0)

        @pl.when(self.row > 0)
        def _():
            self.down.wait_recv()
            arrive(self.up_in, 0)
            self.up.wait_send()

        @pl.when(self.row < self.rows - 1)
        def _():
            self.up.wait_recv()
            arrive(self.down_in, self.tile_rows - REACH)
            self.down.wait_send()

        self.side.wait_send()


def backward_s(pixel_count, direct, r):
    ex = Exchange(r.ex1)
    cols = r.table.shape[0] // WINDOW
    spills = [Spill(r.spill, r.grad, cols, r.strips[8 * n : 8 * n + 8], n) for n in range(2)]

    mid, late, end = Jobs(), Jobs(), Jobs()
    deform_weight_product(r)
    wait_all()
    if direct:
        line, reduce, expand, deform = Jobs(), Jobs(), Jobs(), Jobs()
        line.add(*part_jobs(LineSum, r.eighth_conv_b, r.own_conv_b, r.line_conv_b))
        reduce.add(*plane_jobs(r.src_reduce_b, r.eighth_reduce_b, r.plane_reduce_b))
        reduce.add(*part_jobs(LineSum, r.eighth_reduce_b, r.own_reduce_b, r.line_reduce_b))
        expand.add(*part_jobs(LinePlane, r.src_expand_a, r.own_expand_a, r.plane_expand_a))
        deform.add(*plane_jobs(r.gw_deform, r.eighth_deform, r.plane_deform))
        deform.add(*part_jobs(LineSum, r.eighth_deform, r.own_deform, r.line_deform))
        deform.tick(2)
        r.ready(r.eighth_conv_b)
        line.tick(2)
        r.ready(r.src_expand_a, r.src_reduce_b)
        q1, q2, q3, q4 = line.queue, reduce.queue, expand.queue, deform.queue
        slots = {
            1: q4[0:2] + q3[0:2],
            3: q3[2:4] + q2[0:2],
            6: q4[2:4],
            7: q2[2:4] + q1[0:2],
            9: q4[4:8],
            10: q2[4:6],
        }
        mid.queue = q2[6:10] + q3[4:6]
        late.queue = q3[6:8]
        end.queue = q4[8:10] + q2[10:12] + q3[8:10]
    else:
        slots = {}
        r.push(r.gw_deform)
    slots[5] = [functools.partial(unoffset, r, 0), spills[0].start] + slots.get(5, [])
    slots[8] = [spills[0].middle] + slots.get(8, [])

    def run(queue):
        def call():
            for step in queue:
                step()

        return call

    plan = {slot: run(queue) for slot, queue in slots.items()}
    r.ready(r.w_deform, r.rim, r.w_off, r.select)
    turn(r.gd, r.turned)
    unsample(r, plan)
    unoffset(r, 1)
    spills[1].start()
    r.push(r.gw_off)
    spills[1].middle()
    mid.finish()
    for spill in spills:
        spill.own()
    spills[0].finish()
    late.finish()
    if direct:
        r.push(r.own_conv_b)
    r.ready(r.u_a1)
    spills[1].finish()
    sums = gelu_grad(r.grad, r.u_a1, r.norm_a1, r.mask)
    ex.put(*sums)
    ex.middle_sums()
    ex.finish_sums()
    sums = put_sums(ex, r.sums_a1)
    norm_back(r.grad, r.u_a1, r.norm_a1, sums, pixel_count, r.mask, r.gr_a)
    end.finish()
    if direct:
        r.push(r.own_reduce_b, r.own_expand_a, r.own_deform)


def deform_weight_product(r):
    width = r.gd.shape[1]
    slots = r.sample_slots.shape[0]

    def load(tap):
        rows, slot = pl.ds(tap * width, width), tap % slots
        return pltpu.make_async_copy(
            r.samples.at[rows], r.sample_slots.at[slot], r.sample_sems.at[slot]
        )

    for tap in range(slots):
        load(tap).start()
    r.ready(r.gd)
    for tap in range(9):
        load(tap).wait()
        value = jnp.dot(r.sample_slots[tap % slots], r.gd[...], preferred_element_type=F32)
        put_rows(r.gw_deform, tap * width, value)
        if tap + slots < 9:
            load(tap + slots).start()


def last(direct, r):
    jobs, more, plane = Jobs(), Jobs(), Jobs()
    r.ready(r.gr_a, r.feature)
    wait_all()
    if direct:
        r.ready(r.own_deform, r.gw_off)
        jobs.add(
            *part_jobs(Gather, r.own_deform, r.sum_deform, r.gather_deform),
            SmallSum(r.gw_off, r.sum_off, r.small),
        )
        more.add(
            *part_jobs(Gather, r.own_conv_b, r.sum_conv_b, r.gather_conv_b),
            *part_jobs(Gather, r.own_reduce_b, r.sum_reduce_b, r.gather_reduce_b),
            *part_jobs(Gather, r.own_expand_a, r.sum_expand_a, r.gather_expand_a),
        )
    jobs.tick(3)
    turn(r.gr_a, r.turned)
    weight_product(r.turned, r.feature, r.gw_reduce)
    if direct:
        plane.add(*plane_jobs(r.gw_reduce, r.eighth_reduce_a, r.plane_reduce_a))
        plane.add(*line_jobs(r.eighth_reduce_a, r.sum_reduce_a, r.line_reduce_a))
    else:
        r.push(r.gw_reduce)
    plane.tick(2)
    if direct:
        r.ready(r.own_conv_b, r.own_reduce_b, r.own_expand_a)
    r.ready(r.w_reduce, r.e_a3)

    def chunk(i, carry):
        rows = pl.ds(pl.multiple_of(i * CHUNK, CHUNK), CHUNK)
        for first in range(0, r.feature.shape[1], 512):
            lanes = slice(first, first + 512)
            grad = lax.dot_general(
                r.gr_a[rows, :],
                r.w_reduce[lanes, :],
                (((1,), (1,)), ((), ())),
                preferred_element_type=F32,
            )
            r.grad_in[rows, lanes] = (grad + r.e_a3[rows, lanes].astype(F32)).astype(BF16)
        return carry

    half = r.feature.shape[0] // CHUNK // 2
    lax.fori_loop(0, half, chunk, 0)
    plane.tick(2)
    lax.fori_loop(half, 2 * half, chunk, 0)
    r.push(r.grad_in)
    jobs.tick(3)
    plane.tick(2)
    more.tick(6)
    plane.tick(4)
    jobs.finish()
    more.tick(6)
    plane.tick(2)
    more.finish()
    if direct:
        r.push(r.sum_conv_b, r.sum_reduce_b, r.sum_expand_a, r.sum_deform)
    plane.finish()
    if direct:
        r.push(r.sum_reduce_a)


def body(
    feature_in,
    orientation,
    offset_base,
    w_reduce_a,
    w_offset_a,
    w_deform_a,
    w_expand_a,
    scale_a,
    shift_a,
    w_reduce_b,
    w_conv_b,
    w_expand_b,
    scale_b,
    shift_b,
    cotangent,
):
    images, tile_rows, tile_cols, channels = feature_in.shape
    inner_width = w_reduce_a.shape[1]
    tile_pixels = tile_rows * tile_cols
    pixels = images * tile_pixels
    win_cols = tile_cols + HALF
    win_rows = tile_rows + 2 * PAD
    cells = win_rows * win_cols
    plane_count = 1.0 * images * LONG * SHORT
    pixel_count = plane_count * lax.axis_size(IMG)
    unbias = pixel_count / (pixel_count - 1.0)

    def array(*shape, dtype=BF16):
        return jax.ShapeDtypeStruct(shape, dtype)

    def table(width):
        return array(NORM_ROWS, width, dtype=F32)

    small = (pixels, inner_width)
    big = (pixels, channels)
    window_b = (images, tile_rows + 4, win_cols, inner_width)
    shifted = pltpu.VMEM((images, tile_rows + 4, tile_cols, 3 * inner_width), BF16)
    tile = pltpu.VMEM((images, tile_rows, tile_cols, inner_width), BF16)
    turned = pltpu.VMEM((inner_width, pixels), BF16)
    images_axis = lax.axis_size(IMG)
    direct = inner_width % (images_axis * 8 * 16) == 0
    cuts = images_axis if direct else 1
    feature = feature_in.reshape(big)
    scale_a, shift_a, scale_b, shift_b = (v[None] for v in (scale_a, shift_a, scale_b, shift_b))
    taps_shape = (images, 16, tile_pixels)
    start = fused(
        functools.partial(first, plane_count),
        FIRST_CID,
        ins=dict(
            base=offset_base.reshape(pixels, 18),
            w_offset=w_offset_a.T,
            scale=scale_a,
            shift=shift_a,
        ),
        smem=dict(orientation=orientation),
        staged=dict(feature=feature, w_reduce=w_reduce_a, w_deform=w_deform_a),
        outs=dict(
            mask=array(pixels, 128, dtype=F32),
            counts=array(16, 128, dtype=F32),
            up=array(*taps_shape, dtype=jnp.int32),
            left=array(*taps_shape, dtype=jnp.int32),
            w_off=array(288, inner_width),
            norm_a1=table(inner_width),
            norm_a2=table(inner_width),
        ),
        pushed=dict(
            u_a1=array(*small, dtype=F32),
            rim=array(images, win_rows, win_cols, inner_width),
            select=array(tile_pixels, cells),
            fr=array(*taps_shape, dtype=F32),
            fc=array(*taps_shape, dtype=F32),
            samples=array(9 * inner_width, pixels),
            u_a2=array(*small, dtype=F32),
        ),
        scratch=dict(
            ex1=Exchange.scratch(inner_width),
            ex2=Exchange.scratch(inner_width),
            halo=Halo.scratch * images,
            tile=tile,
            w_turned=pltpu.VMEM((inner_width, 9 * inner_width), BF16),
            rim_t=pltpu.VMEM((images, inner_width, cells), BF16),
            spread=pltpu.VMEM((288, cells), F32),
            table=pltpu.VMEM((WINDOW * win_cols, tile_pixels // 2), BF16),
        ),
    )
    mask, count_rows, norm_a1 = start.mask, start.counts, start.norm_a1
    rim_flat = start.rim.reshape(images, cells, inner_width)
    norm_a2, deformed = start.norm_a2, start.u_a2
    fwd = fused(
        functools.partial(forward, plane_count),
        FORWARD_CID,
        ins=dict(
            norm_a2=norm_a2,
            mask=mask,
            counts=count_rows,
            scale_a=scale_a,
            shift_a=shift_a,
            scale_b=scale_b,
            shift_b=shift_b,
        ),
        far=dict(cotangent=cotangent.reshape(big)),
        staged=dict(
            u_a2=deformed,
            w_expand_a=w_expand_a,
            feature=feature,
            w_reduce=w_reduce_b,
            w_conv=w_conv_b,
            w_expand_b=w_expand_b,
        ),
        outs=dict(
            norm_a3=table(channels),
            norm_b1=table(inner_width),
            norm_b2=table(inner_width),
            norm_b3=table(channels),
            sums_b3=table(channels),
        ),
        pushed=dict(
            h2_a=array(*small),
            middle=array(*big),
            slope_a=array(*big),
            u_a3=array(*big),
            u_b1=array(*small, dtype=F32),
            rim_b=array(*window_b),
            u_b2=array(*small, dtype=F32),
            h2_b=array(*small),
            feature_out=array(*big),
        ),
        far_outs=dict(e_b3=array(*big), u_b3=array(*big)),
        scratch=dict(
            ex_a3=Exchange.scratch(channels),
            ex_b1=Exchange.scratch(inner_width),
            ex_b2=Exchange.scratch(inner_width),
            ex_b3=Exchange.scratch(channels),
            ex_sums=Exchange.scratch(channels),
            halo=Halo.scratch,
            wide=pltpu.VMEM(big, F32),
            tile=tile,
            shifted=shifted,
            far_sems=pltpu.SemaphoreType.DMA((3,)),
        ),
    )
    def eighths(grad):
        return grad.reshape(images_axis, 8, -1, grad.shape[-1])

    def eighth_of(src):
        return array(images_axis, *src.shape[2:])

    def own_of(src):
        return array(*src.shape[2:])

    def sum_of(src):
        return array(*src.shape[1:])

    def vmem(struct):
        return pltpu.VMEM(struct.shape, struct.dtype)

    natural = array(1, inner_width, channels)
    pushed_b, scratch_b = dict(gw_expand=natural), {}
    if direct:
        expand_b = array(images_axis, 8, inner_width // images_axis // 8, channels)
        pushed_b = dict(eighth_expand_b=eighth_of(expand_b))
        scratch_b = dict(gw_expand=vmem(expand_b), plane_expand_b=Plane.scratch(expand_b.shape))
    bwd_b = fused(
        functools.partial(backward_b, pixel_count, direct),
        BACKWARD_B_CID,
        ins=dict(
            mask=mask,
            norm_b3=fwd.norm_b3,
            sums_b3=fwd.sums_b3,
            norm_b2=fwd.norm_b2,
            norm_b1=fwd.norm_b1,
        ),
        staged=dict(
            e_b3=fwd.e_b3,
            u_b3=fwd.u_b3,
            w_expand=w_expand_b,
            u_b2=fwd.u_b2,
            h2_b=fwd.h2_b,
            rim_b=fwd.rim_b,
            w_conv=w_conv_b,
            u_b1=fwd.u_b1,
        ),
        outs=dict(gro_b=array(*small), sums_b2=table(inner_width), sums_b1=table(inner_width)),
        pushed=dict(
            **pushed_b,
            gw_conv=array(cuts, inner_width, 9 * inner_width // cuts),
        ),
        scratch=dict(
            **scratch_b,
            ex2=Exchange.scratch(inner_width),
            ex1=Exchange.scratch(inner_width),
            halo=Halo.scratch,
            geo=pltpu.VMEM(big, BF16),
            grad=pltpu.VMEM(small, F32),
            tile=tile,
            turned=turned,
            back_rim=pltpu.VMEM(window_b, BF16),
            shifted=shifted,
            back_shifted=shifted,
        ),
    )

    staged_a, pushed_a, scratch_a = {}, {}, {}
    if direct:
        conv_b = eighths(bwd_b.gw_conv)
        staged_a = dict(src_conv_b=conv_b, eighth_expand_b=bwd_b.eighth_expand_b)
        pushed_a = dict(eighth_conv_b=eighth_of(conv_b), sum_expand_b=sum_of(expand_b))
        scratch_a = dict(
            plane_conv_b=Plane.scratch(conv_b.shape),
            line_expand_b=Line.scratch(bwd_b.eighth_expand_b.shape),
        )
    bwd_a = fused(
        functools.partial(backward_a, pixel_count, direct),
        BACKWARD_A_CID,
        ins=dict(mask=mask, norm_a3=fwd.norm_a3, norm_a2=norm_a2),
        staged=dict(
            gro_b=bwd_b.gro_b,
            w_reduce=w_reduce_b,
            **staged_a,
            e_b3=fwd.e_b3,
            slope_a=fwd.slope_a,
            u_a3=fwd.u_a3,
            middle=fwd.middle,
            w_expand=w_expand_a,
            u_a2=deformed,
            h2_a=fwd.h2_a,
        ),
        outs=dict(gd=array(*small), sums_a3=table(channels), sums_a2=table(inner_width)),
        pushed=dict(
            **pushed_a,
            gw_reduce=array(cuts, inner_width, channels // cuts),
            gw_expand=natural,
            e_a3=array(*big),
        ),
        scratch=dict(
            **scratch_a,
            ex3=Exchange.scratch(channels),
            ex2=Exchange.scratch(inner_width),
            wide=pltpu.VMEM(big, F32),
            grad=pltpu.VMEM(small, F32),
            turned=turned,
        ),
    )
    staged_s, scratch_s = {}, {}
    pushed_s = dict(gw_deform=array(1, 9 * inner_width, inner_width))
    if direct:
        reduce_b, expand_a = eighths(bwd_a.gw_reduce), eighths(bwd_a.gw_expand)
        deform = array(images_axis, 8, 9 * inner_width // images_axis // 8, inner_width)
        staged_s = dict(
            src_reduce_b=reduce_b,
            src_expand_a=expand_a,
            eighth_conv_b=bwd_a.eighth_conv_b,
        )
        pushed_s = dict(
            own_conv_b=own_of(conv_b),
            own_reduce_b=own_of(reduce_b),
            own_expand_a=own_of(expand_a),
            own_deform=own_of(deform),
        )
        scratch_s = dict(
            gw_deform=vmem(deform),
            line_conv_b=LineSum.scratch(bwd_a.eighth_conv_b.shape),
            plane_reduce_b=Plane.scratch(reduce_b.shape),
            plane_expand_a=LinePlane.scratch(expand_a.shape),
            plane_deform=Plane.scratch(deform.shape),
            eighth_reduce_b=vmem(eighth_of(reduce_b)),
            eighth_deform=vmem(eighth_of(deform)),
            line_reduce_b=LineSum.scratch(eighth_of(reduce_b).shape),
            line_deform=LineSum.scratch(eighth_of(deform).shape),
        )
    block = tile_pixels // 2
    bwd_s = fused(
        functools.partial(backward_s, pixel_count, direct),
        BACKWARD_S_CID,
        ins=dict(
            mask=mask,
            norm_a1=norm_a1,
            up=start.up,
            left=start.left,
            fr=start.fr,
            fc=start.fc,
        ),
        far=dict(samples=start.samples),
        staged=dict(
            gd=bwd_a.gd,
            **staged_s,
            w_deform=w_deform_a,
            rim=rim_flat,
            w_off=start.w_off,
            select=start.select,
            u_a1=start.u_a1,
        ),
        outs=dict(gr_a=array(*small), sums_a1=table(inner_width)),
        pushed=dict(**pushed_s, gw_off=array(cuts, 32, 9 * inner_width // cuts)),
        scratch=dict(
            **scratch_s,
            ex1=Exchange.scratch(inner_width),
            strips=Spill.scratch(1, tile_rows, tile_cols, inner_width) * images,
            spill=pltpu.VMEM((images, cells, inner_width), F32),
            table=pltpu.VMEM((WINDOW * win_cols, 3 * block), BF16),
            grads=pltpu.VMEM((inner_width, 3 * block), BF16),
            turned=turned,
            grad_row=pltpu.VMEM(taps_shape, F32),
            grad_col=pltpu.VMEM(taps_shape, F32),
            on_cells=pltpu.VMEM((288, cells), BF16),
            gw_off_sum=pltpu.VMEM((288, inner_width), F32),
            sample_slots=pltpu.VMEM((3, inner_width, pixels), BF16),
            sample_sems=pltpu.SemaphoreType.DMA((3,)),
            grad=pltpu.VMEM(small, F32),
        ),
    )
    staged_l, pushed_l, scratch_l = {}, {}, {}
    if direct:
        reduce_a = array(images_axis, 8, inner_width // 8, channels // cuts)
        staged_l = dict(
            own_deform=bwd_s.own_deform,
            gw_off=bwd_s.gw_off,
            own_conv_b=bwd_s.own_conv_b,
            own_reduce_b=bwd_s.own_reduce_b,
            own_expand_a=bwd_s.own_expand_a,
        )
        pushed_l = dict(
            sum_conv_b=sum_of(conv_b),
            sum_reduce_b=sum_of(reduce_b),
            sum_expand_a=sum_of(expand_a),
            sum_deform=sum_of(deform),
            sum_reduce_a=sum_of(reduce_a),
        )
        scratch_l = dict(
            gw_reduce=vmem(reduce_a),
            small=SmallSum.scratch(bwd_s.gw_off.shape),
            gather_conv_b=Gather.scratch(conv_b.shape),
            gather_reduce_b=Gather.scratch(reduce_b.shape),
            gather_expand_a=Gather.scratch(expand_a.shape),
            gather_deform=Gather.scratch(deform.shape),
            plane_reduce_a=Plane.scratch(reduce_a.shape),
            eighth_reduce_a=vmem(eighth_of(reduce_a)),
            line_reduce_a=Line.scratch(eighth_of(reduce_a).shape),
        )
        outs_l = dict(sum_off=array(*bwd_s.gw_off.shape[1:], dtype=F32))
    else:
        pushed_l = dict(gw_reduce=array(cuts, inner_width, channels // cuts))
        outs_l = {}
    end = fused(
        functools.partial(last, direct),
        LAST_CID,
        ins={},
        staged=dict(
            gr_a=bwd_s.gr_a, feature=feature, **staged_l, w_reduce=w_reduce_a, e_a3=bwd_a.e_a3
        ),
        outs=outs_l,
        pushed=dict(**pushed_l, grad_in=array(*big)),
        scratch=dict(**scratch_l, turned=turned),
    )
    sums_a = [bwd_s.sums_a1, bwd_a.sums_a2, bwd_a.sums_a3]
    sums_b = [bwd_b.sums_b1, bwd_b.sums_b2, fwd.sums_b3]
    norms_a = [norm_a1, norm_a2, fwd.norm_a3]
    norms_b = [fwd.norm_b1, fwd.norm_b2, fwd.norm_b3]
    if direct:
        sums = [
            end.sum_conv_b,
            end.sum_reduce_b,
            end.sum_reduce_a,
            bwd_a.sum_expand_b,
            end.sum_expand_a,
            end.sum_deform,
            end.sum_off,
        ]
    else:

        def over_devices(grad, dim):
            part = lax.psum_scatter(grad, IMG, scatter_dimension=dim, tiled=True)
            return lax.psum(part, (ROW, COL))

        turned_grads = (bwd_b.gw_conv, bwd_a.gw_reduce, end.gw_reduce)
        sums = [over_devices(g[0], 1) for g in turned_grads]
        sums += [over_devices(g[0], 0) for g in (bwd_b.gw_expand, bwd_a.gw_expand)]
        sums.append(over_devices(bwd_s.gw_deform[0], 0))
        sums = [g.reshape(8, -1, g.shape[1]) for g in sums]
        sums.append(over_devices(bwd_s.gw_off[0], 1).astype(F32))
    share = inner_width // images_axis
    long_share, wide_share = 9 * share, channels // images_axis
    shapes = [
        (long_share, inner_width),
        (wide_share, inner_width),
        (wide_share, inner_width),
        (share, channels),
        (share, channels),
        (long_share, inner_width),
        (18, long_share),
    ]
    vectors = ((2 * inner_width + channels) // 128, 128)
    shapes += [vectors] * 8
    operands = sums + sums_a + sums_b + norms_a + norms_b + [fwd.feature_out, end.grad_in]
    results = [array(*shape, dtype=F32) for shape in shapes]
    anywhere = pl.BlockSpec(memory_space=pl.ANY)
    results = pl.pallas_call(
        functools.partial(finish_kernel, unbias, len(operands)),
        out_shape=results + [array(*big)] * 2,
        in_specs=[anywhere] * len(operands),
        out_specs=[anywhere] * (len(shapes) + 2),
        scratch_shapes=[vmem(v) for v in operands + results]
        + [pltpu.SemaphoreType.DMA((len(operands),)), pltpu.SemaphoreType.DMA((17,))],
        compiler_params=pltpu.CompilerParams(vmem_limit_bytes=VMEM_LIMIT),
    )(*operands)
    conv_b, reduce_b, reduce_a, expand_b, expand_a, deform_a, offset_a = results[:7]
    scale_sums_a, shift_sums_a, scale_sums_b, shift_sums_b, mean_a, var_a, mean_b, var_b = (
        v.reshape(-1) for v in results[7:15]
    )
    return (
        results[15].reshape(feature_in.shape),
        results[16].reshape(feature_in.shape),
        reduce_a,
        offset_a.T,
        deform_a,
        expand_a,
        scale_sums_a,
        shift_sums_a,
        mean_a,
        var_a,
        reduce_b,
        conv_b,
        expand_b,
        scale_sums_b,
        shift_sums_b,
        mean_b,
        var_b,
    )


def solution(mesh):
    tiles = P(IMG, ROW, COL, None)
    in_specs = (tiles, P(IMG), tiles) + (P(),) * 11 + (tiles,)
    shares = P(IMG, None)
    out_specs = (tiles, tiles) + (shares,) * 4 + (P(),) * 4 + (shares,) * 3 + (P(),) * 4
    return jax.shard_map(body, mesh=mesh, in_specs=in_specs, out_specs=out_specs, check_vma=False)
```

```python
import functools
import types

import jax
import jax.numpy as jnp
import numpy as np
from jax import lax
from jax.experimental import pallas as pl
from jax.experimental.pallas import tpu as pltpu
from jax.sharding import PartitionSpec as P

LONG = 64
SHORT = 44
BOUND = 4
EPSILON = 1e-05
IMG, ROW, COL = "img", "row", "col"
MESH = pl.DeviceIdType.MESH
VMEM = pl.BlockSpec(memory_space=pltpu.VMEM)
VMEM_LIMIT = 60 * 1024 * 1024
F32 = jnp.float32
BF16 = jnp.bfloat16
REACH = BOUND + 3
PAD = 8
HALF = 16
FIRST_CID, FORWARD_CID, BACKWARD_B_CID, BACKWARD_A_CID, BACKWARD_S_CID, LAST_CID = range(6)


def group_of(axes):
    sizes = [lax.axis_size(a) for a in axes]
    total = int(np.prod(sizes))
    place = lax.axis_index(axes[0])
    for axis, size in zip(axes[1:], sizes[1:]):
        place = place * size + lax.axis_index(axis)

    def device(step):
        spot = lax.rem(place + step, total)
        coords = {}
        for axis, size in zip(reversed(axes), reversed(sizes)):
            coords[axis] = lax.rem(spot, size)
            spot = spot // size
        return coords

    return place, total, device


PLANE = (ROW, COL)
LINE = (IMG,)


def gather_start(axes, slots, send_sem, recv_sem):
    _, total, device = group_of(axes)
    for step in range(1, total):
        pltpu.make_async_remote_copy(
            src_ref=slots.at[0],
            dst_ref=slots.at[step],
            send_sem=send_sem,
            recv_sem=recv_sem,
            device_id=device(step),
            device_id_type=MESH,
        ).start()


def gather_wait(axes, slots, sem):
    _, total, _ = group_of(axes)
    others = slots.at[pl.ds(1, total - 1)]
    pltpu.make_async_copy(others, others, sem).wait()


def in_order(axes, slots):
    place, total, _ = group_of(axes)
    return [slots[lax.rem(place - spot + total, total)] for spot in range(total)]


def halo_peers():
    row, rows, col = lax.axis_index(ROW), lax.axis_size(ROW), lax.axis_index(COL)
    return row, rows, col, {COL: 1 - col}, {ROW: row - 1}, {ROW: row + 1}


BLOCK_ROWS = 8
SPAN = 17
WINDOW = 3 * BLOCK_ROWS


def tap_span(group, cols):
    first = 2 + 2 * group
    start = first * cols // 128 * 128
    stop = -(-(first + SPAN) * cols // 128) * 128
    return first, start, stop


def tap_weights(tap, block, cols, up_ref, left_ref, fr_ref, fc_ref, image=0, lanes=slice(None)):
    up, left, fr, fc = (
        ref[image, tap : tap + 1, lanes] for ref in (up_ref, left_ref, fr_ref, fc_ref)
    )
    up = up - block * BLOCK_ROWS
    pixels = up.shape[1]

    def pair(size, at, frac):
        ids = lax.broadcasted_iota(jnp.int32, (size, pixels), 0)
        first, second = ids == at, ids == at + 1
        value = jnp.where(first, 1.0 - frac, jnp.where(second, frac, 0.0))
        slope = jnp.where(second, 1.0, jnp.where(first, -1.0, 0.0))
        return value, slope

    return pair(WINDOW, up, fr) + pair(cols, left, fc)


def write_table(table, lane, row_w, col_w, group, cols):
    first, start, stop = tap_span(group, cols)
    pixels = row_w.shape[1]
    low = start // cols
    high = -(-stop // cols)
    for r in range(low, min(high, WINDOW)):
        table[r * cols : (r + 1) * cols, lane : lane + pixels] = (
            row_w[r : r + 1, :] * col_w
        ).astype(BF16)


def build_shifted(rim_ref, shifted):
    images, rows, cols, width = rim_ref.shape
    col = lax.axis_index(COL)
    tile = cols - HALF

    def fill(first):
        def one_row(k, carry):
            for n in range(images):
                line = rim_ref[n, k].astype(F32)
                none = jnp.zeros((2, width), F32)
                for d in range(3):
                    at = first + 2 * (d - 1)
                    if at < 0:
                        part = jnp.concatenate([none, line[: tile - 2]], axis=0)
                    elif at + tile > cols:
                        part = jnp.concatenate([line[at:], none], axis=0)
                    else:
                        part = line[at : at + tile]
                    shifted[n, k, :, d * width : (d + 1) * width] = part.astype(BF16)
            return carry

        lax.fori_loop(0, rows, one_row, 0)

    @pl.when(col == 0)
    def _():
        fill(0)

    @pl.when(col == 1)
    def _():
        fill(HALF)


def conv_product(shifted, w_ref, o_ref):
    images, rows, cols, width3 = shifted.shape
    tile_rows = rows - 4
    pixels = tile_rows * cols
    for n in range(images):
        total = None
        for i in range(3):
            taps = shifted[n, 2 * i : 2 * i + tile_rows].reshape(pixels, width3)
            term = jnp.dot(taps, w_ref[i * width3 : (i + 1) * width3, :], preferred_element_type=F32)
            total = term if total is None else total + term
        o_ref[n * pixels : (n + 1) * pixels, :] = total


def conv_weight_product(turned, shifted, gw_ref, i):
    images, rows, cols, width3 = shifted.shape
    tile_rows = rows - 4
    pixels = tile_rows * cols
    total = None
    for n in range(images):
        taps = shifted[n, 2 * i : 2 * i + tile_rows].reshape(pixels, width3)
        term = jnp.dot(turned[:, n * pixels : (n + 1) * pixels], taps, preferred_element_type=F32)
        total = term if total is None else total + term
    put_lanes(gw_ref, i * width3, total)


def unconv_product(shifted, w_ref, o_ref):
    images, rows, cols, width3 = shifted.shape
    width = width3 // 3
    tile_rows = rows - 4
    pixels = tile_rows * cols
    for n in range(images):
        total = None
        for tap in range(9):
            i, d = 2 - tap // 3, 2 - tap % 3
            grads = shifted[n, 2 * i : 2 * i + tile_rows, :, d * width : (d + 1) * width]
            term = lax.dot_general(
                grads.reshape(pixels, width),
                w_ref[tap * width : (tap + 1) * width, :],
                (((1,), (1,)), ((), ())),
                preferred_element_type=F32,
            )
            total = term if total is None else total + term
        o_ref[n * pixels : (n + 1) * pixels, :] = total


def halves(width):
    first = -(-width // 256) * 128
    return ((0, first), (first, width - first)) if first < width else ((0, width),)


def remote(src, dst, send, recv, device):
    return pltpu.make_async_remote_copy(
        src_ref=src, dst_ref=dst, send_sem=send, recv_sem=recv, device_id=device, device_id_type=MESH
    )


def arrival(ref, sem):
    return pltpu.make_async_copy(ref, ref, sem)


class Plane:
    @staticmethod
    def scratch(shape):
        images, _, rows, width = shape
        count = len(halves(width))
        return [
            pltpu.VMEM((images, 4, rows, width), BF16),
            pltpu.VMEM((images, 2, rows, width), BF16),
            pltpu.SemaphoreType.DMA((count, 3)),
            pltpu.SemaphoreType.DMA((count, 3)),
        ]

    def __init__(self, src, eighth, refs, part):
        half, quarter, send, recv = refs
        lanes = pl.ds(*halves(src.shape[-1])[part])
        self.src, self.half, self.quarter = (
            ref.at[:, :, :, lanes] for ref in (src, half, quarter)
        )
        self.eighth = eighth.at[:, :, lanes]
        self.images = src.shape[0]
        self.send, self.recv = [send.at[part, k] for k in range(3)], [recv.at[part, k] for k in range(3)]
        self.a, self.b, self.spot, self.first, self.second = self.peers(part == 0)
        col = lax.axis_index(COL)
        self.mine, self.pair, self.other = 4 * col, {COL: 1 - col}, 4 * (1 - col)

    @staticmethod
    def peers(x_first):
        row = lax.axis_index(ROW)
        x, y = lax.rem(row, 2), row // 2
        to_x, to_y = {ROW: row + 1 - 2 * x}, {ROW: row + 2 - 4 * y}
        if x_first:
            return x, y, lambda bit, free: bit + 2 * free, to_x, to_y
        return y, x, lambda bit, free: 2 * bit + free, to_y, to_x

    def steps(self):
        return [self.to_pair, self.to_first, self.to_second, self.done]

    def to_pair(self):
        src = self.src.at[:, pl.ds(self.other, 4)]
        remote(src, self.half, self.send[0], self.recv[0], self.pair).start()

    def to_first(self):
        arrival(self.half, self.recv[0]).wait()

        def add(i, carry):
            for s in range(4):
                self.half[i, s] = self.src[i, self.mine + s] + self.half[i, s]
            return carry

        lax.fori_loop(0, self.images, add, 0)
        for k in range(2):
            src = self.half.at[:, self.spot(1 - self.a, k)]
            remote(src, self.quarter.at[:, k], self.send[1], self.recv[1], self.first).start()

    def to_second(self):
        arrival(self.quarter, self.recv[1]).wait()

        def add(i, carry):
            for k in range(2):
                self.quarter[i, k] = self.half[i, self.spot(self.a, k)] + self.quarter[i, k]
            return carry

        lax.fori_loop(0, self.images, add, 0)
        src = self.quarter.at[:, 1 - self.b]
        remote(src, self.eighth, self.send[2], self.recv[2], self.second).start()

    def done(self):
        arrival(self.eighth, self.recv[2]).wait()

        def add(i, carry):
            self.eighth[i] = self.quarter[i, self.b] + self.eighth[i]
            return carry

        lax.fori_loop(0, self.images, add, 0)
        arrival(self.half, self.send[0]).wait()
        arrival(self.quarter, self.send[1]).wait()
        arrival(self.eighth, self.send[2]).wait()


class LinePlane:
    @staticmethod
    def scratch(shape):
        images, _, rows, width = shape
        sems = pltpu.SemaphoreType.DMA((len(halves(width)), 4))
        return [
            pltpu.VMEM((images, 4, rows, width), BF16),
            pltpu.VMEM((images, 4, rows, width), BF16),
            pltpu.VMEM((2, rows, width), BF16),
            pltpu.VMEM((rows, width), BF16),
            sems,
            sems,
        ]

    def __init__(self, src, own, refs, part):
        half, line, quarter, eighth, send, recv = refs
        lanes = pl.ds(*halves(src.shape[-1])[part])
        self.src, self.half, self.line = (ref.at[:, :, :, lanes] for ref in (src, half, line))
        self.quarter = quarter.at[:, :, lanes]
        self.eighth, self.own = eighth.at[:, lanes], own.at[:, lanes]
        self.images, self.img = src.shape[0], lax.axis_index(IMG)
        self.send, self.recv = [send.at[part, k] for k in range(4)], [recv.at[part, k] for k in range(4)]
        self.plane = Plane.peers(part == 0)
        col = lax.axis_index(COL)
        self.mine, self.pair, self.other = 4 * col, {COL: 1 - col}, 4 * (1 - col)

    def steps(self):
        return [self.to_pair, self.to_line, self.to_first, self.to_second, self.done]

    def to_pair(self):
        src = self.src.at[:, pl.ds(self.other, 4)]
        remote(src, self.half, self.send[0], self.recv[0], self.pair).start()

    def to_line(self):
        arrival(self.half, self.recv[0]).wait()

        def add(i, carry):
            for s in range(4):
                self.half[i, s] = self.src[i, self.mine + s] + self.half[i, s]
            return carry

        lax.fori_loop(0, self.images, add, 0)
        for j in range(1, self.images):
            there = lax.rem(self.img + j, self.images)
            src = self.half.at[there]
            remote(src, self.line.at[j], self.send[1], self.recv[1], {IMG: there}).start()

    def to_first(self):
        arrival(self.line.at[pl.ds(1, self.images - 1)], self.recv[1]).wait()
        for s in range(4):
            total = self.half[self.img, s].astype(F32)
            for j in range(1, self.images):
                total = total + self.line[j, s].astype(F32)
            self.line[0, s] = total.astype(BF16)
        a, _, spot, first, _ = self.plane
        for k in range(2):
            src = self.line.at[0, spot(1 - a, k)]
            remote(src, self.quarter.at[k], self.send[2], self.recv[2], first).start()

    def to_second(self):
        a, b, spot, _, second = self.plane
        arrival(self.quarter, self.recv[2]).wait()
        for k in range(2):
            self.quarter[k] = self.line[0, spot(a, k)] + self.quarter[k]
        remote(self.quarter.at[1 - b], self.eighth, self.send[3], self.recv[3], second).start()

    def done(self):
        _, b, _, _, _ = self.plane
        arrival(self.eighth, self.recv[3]).wait()
        self.own[...] = self.quarter[b] + self.eighth[...]
        arrival(self.half, self.send[0]).wait()
        arrival(self.line.at[pl.ds(1, self.images - 1)], self.send[1]).wait()
        arrival(self.quarter, self.send[2]).wait()
        arrival(self.eighth, self.send[3]).wait()


class LineSum:
    @staticmethod
    def scratch(shape):
        sems = pltpu.SemaphoreType.DMA((len(halves(shape[-1])),))
        return [pltpu.VMEM(shape, BF16), sems, sems]

    def __init__(self, eighth, own, refs, part):
        line, send, recv = refs
        lanes = pl.ds(*halves(eighth.shape[-1])[part])
        self.eighth, self.line, self.own = eighth.at[:, :, lanes], line.at[:, :, lanes], own.at[:, lanes]
        self.images, self.img = eighth.shape[0], lax.axis_index(IMG)
        self.send, self.recv = send.at[part], recv.at[part]

    def steps(self):
        return [self.to_line, self.done]

    def to_line(self):
        for j in range(1, self.images):
            there = lax.rem(self.img + j, self.images)
            src = self.eighth.at[there]
            remote(src, self.line.at[j], self.send, self.recv, {IMG: there}).start()

    def done(self):
        arrived = self.line.at[pl.ds(1, self.images - 1)]
        arrival(arrived, self.recv).wait()
        total = self.eighth[self.img].astype(F32)
        for j in range(1, self.images):
            total = total + self.line[j].astype(F32)
        self.own[...] = total.astype(BF16)
        arrival(arrived, self.send).wait()


class Gather:
    @staticmethod
    def scratch(shape):
        sems = pltpu.SemaphoreType.DMA((len(halves(shape[-1])), 3))
        return [sems, sems]

    def __init__(self, own, out, refs, part):
        send, recv = refs
        lanes = pl.ds(*halves(out.shape[-1])[part])
        self.own, self.out = own.at[:, lanes], out.at[:, :, lanes]
        self.send, self.recv = [send.at[part, k] for k in range(3)], [recv.at[part, k] for k in range(3)]
        row, col = lax.axis_index(ROW), lax.axis_index(COL)
        x, y = lax.rem(row, 2), row // 2
        self.pair, mine = {COL: 1 - col}, 4 * col
        _, _, _, self.first, self.second = Plane.peers(part == 0)
        self.spot, self.four = mine + row, pl.ds(mine, 4)
        if part == 0:
            self.two = [pl.ds(mine + 2 * y, 2)]
        else:
            self.two = [pl.ds(mine + x, 1), pl.ds(mine + x + 2, 1)]

    def steps(self):
        return [self.to_first, self.to_second, self.to_pair, self.done]

    def of(self, count):
        return self.out.at[pl.ds(0, count)]

    def to_first(self):
        self.out[self.spot] = self.own[...]
        one = self.out.at[pl.ds(self.spot, 1)]
        remote(one, one, self.send[0], self.recv[0], self.first).start()

    def to_second(self):
        arrival(self.of(1), self.recv[0]).wait()
        for pieces in self.two:
            ref = self.out.at[pieces]
            remote(ref, ref, self.send[1], self.recv[1], self.second).start()

    def to_pair(self):
        arrival(self.of(2), self.recv[1]).wait()
        four = self.out.at[self.four]
        remote(four, four, self.send[2], self.recv[2], self.pair).start()

    def done(self):
        arrival(self.of(4), self.recv[2]).wait()
        arrival(self.of(1), self.send[0]).wait()
        arrival(self.of(2), self.send[1]).wait()
        arrival(self.of(4), self.send[2]).wait()


class Line:
    @staticmethod
    def scratch(shape):
        return [pltpu.VMEM(shape[1:], BF16)] + LineSum.scratch(shape) + Gather.scratch(shape)

    def __init__(self, eighth, out, refs, part):
        own = refs[0]
        self.sum = LineSum(eighth, own, refs[1:4], part)
        self.gather = Gather(own, out, refs[4:], part)

    def steps(self):
        gather = self.gather
        return [self.sum.to_line, self.to_first, gather.to_second, gather.to_pair, gather.done]

    def to_first(self):
        self.sum.done()
        self.gather.to_first()


class SmallSum:
    @staticmethod
    def scratch(shape):
        sizes = [lax.axis_size(IMG), lax.axis_size(ROW) * lax.axis_size(COL)]
        return [pltpu.VMEM((size,) + shape[1:], BF16) for size in sizes] + [
            pltpu.SemaphoreType.DMA((2,)),
            pltpu.SemaphoreType.DMA((2,)),
        ]

    def __init__(self, src, out, refs):
        self.src, self.out = src, out
        self.slots1, self.slots2, self.send, self.recv = refs

    def steps(self):
        return [self.to_line, self.to_plane, self.done]

    def to_line(self):
        here, total, _ = group_of(LINE)
        self.slots1[0] = self.src[here]
        for j in range(1, total):
            there = lax.rem(here + j, total)
            remote(
                self.src.at[there], self.slots1.at[j], self.send.at[0], self.recv.at[0], {IMG: there}
            ).start()

    def to_plane(self):
        gather_wait(LINE, self.slots1, self.recv.at[0])
        total = added([p.astype(F32) for p in in_order(LINE, self.slots1)])
        self.slots2[0] = total.astype(BF16)
        gather_start(PLANE, self.slots2, self.send.at[1], self.recv.at[1])

    def done(self):
        gather_wait(PLANE, self.slots2, self.recv.at[1])
        self.out[...] = added([p.astype(F32) for p in in_order(PLANE, self.slots2)])
        gather_wait(LINE, self.slots1, self.send.at[0])
        gather_wait(PLANE, self.slots2, self.send.at[1])


class Jobs:
    def __init__(self):
        self.queue = []

    def add(self, *jobs):
        lists = [job.steps() for job in jobs]
        for k in range(max(len(steps) for steps in lists)):
            self.queue += [steps[k] for steps in lists if k < len(steps)]

    def tick(self, count=1):
        for _ in range(min(count, len(self.queue))):
            self.queue.pop(0)()

    def finish(self):
        self.tick(len(self.queue))


def plane_jobs(src, eighth, refs):
    return [Plane(src, eighth, refs, part) for part in range(len(halves(src.shape[-1])))]


def part_jobs(kind, first, second, refs):
    return [kind(first, second, refs, part) for part in range(len(halves(first.shape[-1])))]


def line_jobs(eighth, out, refs):
    return [Line(eighth, out, refs, part) for part in range(len(halves(out.shape[-1])))]


STEP = 32
PIECE = 256
CHUNK = 256


class Refs:
    FLYING = 6 * 1024 * 1024

    def __init__(self):
        self.loads, self.stores, self.queue, self.flying = {}, {}, [], {}

    def load(self, ref, copy):
        self.loads[id(ref)] = copy
        self.queue.append((id(ref), int(np.prod(ref.shape)) * ref.dtype.itemsize))

    def start_loads(self, until=None):
        while self.queue:
            if until is None and sum(self.flying.values()) >= self.FLYING:
                return
            if until is not None and until in self.flying:
                return
            key, size = self.queue.pop(0)
            self.loads[key].start()
            self.flying[key] = size

    def ready(self, *refs):
        for ref in refs:
            self.start_loads(id(ref))
            self.loads.pop(id(ref)).wait()
            self.flying.pop(id(ref))
            self.start_loads()

    def push(self, *refs):
        for ref in refs:
            self.stores[id(ref)].start()

    def pushed(self, *refs):
        for ref in refs:
            self.stores.pop(id(ref)).wait()

    def flush(self):
        for copy in self.stores.values():
            copy.wait()


def fused(work, cid, ins, staged, outs, pushed, scratch, smem={}, far={}, far_outs={}):
    loaded, stored = {**ins, **staged}, {**outs, **pushed}
    sizes = (len(loaded), len(stored))

    def kernel(*refs):
        r = Refs()
        refs = list(refs)

        def take(count):
            taken = refs[:count]
            del refs[:count]
            return taken

        for key, ref in zip((*smem, *far), take(len(smem) + len(far))):
            setattr(r, key, ref)
        in_raw, out_raw = (take(count) for count in sizes)
        for key, ref in zip(far_outs, take(len(far_outs))):
            setattr(r, key, ref)
        for key, shape in scratch.items():
            setattr(r, key, take(len(shape)) if isinstance(shape, list) else take(1)[0])
        in_bufs, out_bufs = (take(count) for count in sizes)
        in_sems, out_sems = take(2)
        for keys, bufs in ((loaded, in_bufs), (stored, out_bufs)):
            for key, buf in zip(keys, bufs):
                setattr(r, key, buf)
        for k, (raw, buf) in enumerate(zip(in_raw, in_bufs)):
            r.load(buf, pltpu.make_async_copy(raw, buf, in_sems.at[k]))
        for k, (raw, buf) in enumerate(zip(out_raw, out_bufs)):
            r.stores[id(buf)] = pltpu.make_async_copy(buf, raw, out_sems.at[k])
        r.start_loads()
        signal_all()
        r.ready(*in_bufs[: len(ins)])
        work(r)
        r.push(*out_bufs[: len(outs)])
        r.flush()

    flat = []
    for shape in scratch.values():
        flat += shape if isinstance(shape, list) else [shape]
    flat += [pltpu.VMEM(a.shape, a.dtype) for a in (*loaded.values(), *stored.values())]
    flat += [pltpu.SemaphoreType.DMA((count,)) for count in sizes]
    anywhere, scalars = pl.BlockSpec(memory_space=pl.ANY), pl.BlockSpec(memory_space=pltpu.SMEM)
    result = pl.pallas_call(
        kernel,
        out_shape=[*stored.values(), *far_outs.values()],
        in_specs=[scalars] * len(smem) + [anywhere] * (len(far) + sizes[0]),
        out_specs=[anywhere] * (sizes[1] + len(far_outs)),
        scratch_shapes=flat,
        compiler_params=pltpu.CompilerParams(
            collective_id=cid, has_side_effects=True, vmem_limit_bytes=VMEM_LIMIT
        ),
    )(*smem.values(), *far.values(), *loaded.values())
    return types.SimpleNamespace(**dict(zip((*stored, *far_outs), result)))


def signal_all():
    barrier = pltpu.get_barrier_semaphore()
    for axes in (PLANE, LINE):
        _, total, device = group_of(axes)
        for step in range(1, total):
            pl.semaphore_signal(barrier, inc=1, device_id=device(step), device_id_type=MESH)


def wait_all():
    count = sum(group_of(axes)[1] - 1 for axes in (PLANE, LINE))
    pl.semaphore_wait(pltpu.get_barrier_semaphore(), count)


def added(parts):
    return functools.reduce(lambda a, b: a + b, parts)


class Exchange:
    @staticmethod
    def scratch(width):
        rows = 2 * width // 128
        sizes = [int(np.prod([lax.axis_size(a) for a in axes])) for axes in (PLANE, LINE)]
        return [
            pltpu.VMEM((sizes[0], rows, 128), F32),
            pltpu.VMEM((sizes[1], rows, 128), F32),
            pltpu.VMEM((rows, 128), F32),
            pltpu.SemaphoreType.DMA((2,)),
            pltpu.SemaphoreType.DMA((2,)),
        ]

    def __init__(self, refs):
        self.slots1, self.slots2, self.out, self.send, self.recv = refs
        self.half = self.out.shape[0] // 2

    def put(self, first, second):
        for k in range(self.half):
            self.slots1[0, k : k + 1, :] = first[:, 128 * k : 128 * (k + 1)]
            self.slots1[0, self.half + k : self.half + k + 1, :] = second[:, 128 * k : 128 * (k + 1)]
        gather_start(PLANE, self.slots1, self.send.at[0], self.recv.at[0])

    def line(self):
        gather_start(LINE, self.slots2, self.send.at[1], self.recv.at[1])

    def middle_sums(self):
        gather_wait(PLANE, self.slots1, self.recv.at[0])
        self.slots2[0] = added(in_order(PLANE, self.slots1))
        self.line()

    def finish_sums(self):
        gather_wait(LINE, self.slots2, self.recv.at[1])
        self.out[...] = added(in_order(LINE, self.slots2))
        self.drain()

    def middle_stats(self, count_ref, plane_count):
        half = self.half
        gather_wait(PLANE, self.slots1, self.recv.at[0])
        parts = in_order(PLANE, self.slots1)
        total = added([p[:half] for p in parts])
        center = total / plane_count
        spread = added([p[half:] for p in parts])
        for spot, part in enumerate(parts):
            count = count_ref[spot : spot + 1, :]
            away = part[:half] / jnp.maximum(count, 1.0) - center
            spread = spread + count * (away * away)
        self.slots2[0, :half] = total
        self.slots2[0, half:] = spread
        self.line()

    def finish_stats(self, plane_count):
        half = self.half
        total_count = plane_count * lax.axis_size(IMG)
        gather_wait(LINE, self.slots2, self.recv.at[1])
        parts = in_order(LINE, self.slots2)
        center = added([p[:half] for p in parts]) / total_count
        spread = added([p[half:] for p in parts])
        for part in parts:
            away = part[:half] / plane_count - center
            spread = spread + plane_count * (away * away)
        self.out[:half] = center
        self.out[half:] = spread / total_count
        self.drain()

    def drain(self):
        gather_wait(PLANE, self.slots1, self.send.at[0])
        gather_wait(LINE, self.slots2, self.send.at[1])

    def rows(self):
        out = self.out[...]
        first = [out[k : k + 1] for k in range(self.half)]
        second = [out[self.half + k : self.half + k + 1] for k in range(self.half)]
        return jnp.concatenate(first, axis=1), jnp.concatenate(second, axis=1)


class Halo:
    scratch = [pltpu.SemaphoreType.DMA((5,)), pltpu.SemaphoreType.DMA((5,))]

    def __init__(self, pad, reach, tile, window, sems, image=None):
        if image is not None:
            tile, window = (ref.at[pl.ds(image, 1)] for ref in (tile, window))
        self.row, self.rows, col, pair, above, below = halo_peers()
        self.pad, self.reach, self.tile, self.window = pad, reach, tile, window
        self.tile_rows, self.tile_cols = tile.shape[1], tile.shape[2]
        self.own = own = pl.ds(pl.multiple_of(HALF * col, HALF), self.tile_cols)
        spot = pl.ds(pl.multiple_of(2 * HALF * col, HALF), HALF)
        side = pl.ds(pl.multiple_of(HALF * (1 - col), HALF), HALF)
        mid = pl.ds(HALF, HALF)
        upper = pl.ds(pad - reach, reach)
        lower = pl.ds(pad + self.tile_rows, reach)
        send, recv = sems

        def copy(src, dst, k, device):
            return pltpu.make_async_remote_copy(
                src_ref=src,
                dst_ref=dst,
                send_sem=send.at[k],
                recv_sem=recv.at[k],
                device_id=device,
                device_id_type=MESH,
            )

        w = window
        self.to_pair = copy(
            tile.at[:, :, side], w.at[:, pl.ds(pad, self.tile_rows), spot], 0, pair
        )
        self.up = copy(tile.at[:, pl.ds(0, reach)], w.at[:, lower, own], 1, above)
        self.down = copy(
            tile.at[:, pl.ds(self.tile_rows - reach, reach)], w.at[:, upper, own], 2, below
        )
        self.from_below = copy(w.at[:, lower, mid], w.at[:, lower, spot], 3, pair)
        self.from_above = copy(w.at[:, upper, mid], w.at[:, upper, spot], 4, pair)

    def blank(self):
        window, pad, reach, tile_rows = self.window, self.pad, self.reach, self.tile_rows
        zero = jnp.zeros((window.shape[0],) + window.shape[2:], window.dtype)

        def fill(first, last):
            for k in range(first, last):
                window[:, k] = zero

        fill(0, pad - reach)
        fill(pad + tile_rows + reach, 2 * pad + tile_rows)

        @pl.when(self.row == 0)
        def _():
            fill(pad - reach, pad)

        @pl.when(self.row == self.rows - 1)
        def _():
            fill(pad + tile_rows, pad + tile_rows + reach)

    def start(self):
        @pl.when(self.row > 0)
        def _():
            self.up.start()

        @pl.when(self.row < self.rows - 1)
        def _():
            self.down.start()

        self.to_pair.start()
        for n in range(self.tile.shape[0]):
            self.window[n, pl.ds(self.pad, self.tile_rows), self.own, :] = self.tile[n]

    def middle(self):
        @pl.when(self.row < self.rows - 1)
        def _():
            self.up.wait_recv()
            self.from_below.start()

        @pl.when(self.row > 0)
        def _():
            self.down.wait_recv()
            self.from_above.start()

    def finish(self):
        self.to_pair.wait()

        @pl.when(self.row < self.rows - 1)
        def _():
            self.down.wait_send()
            self.from_below.wait()

        @pl.when(self.row > 0)
        def _():
            self.up.wait_send()
            self.from_above.wait()


def gauss(x):
    bell = jnp.exp2(x * (x * -0.7213475204444817))
    d = 1.0 + (0.3275911 * 0.7071067811865476) * jnp.abs(x)
    t = pl.reciprocal(d, approx=True)
    t = t * (2.0 - d * t)
    poly = 0.5307027145 * t - 0.7265760135
    poly = poly * t + 0.7107068705
    poly = poly * t - 0.142248368
    poly = poly * t + 0.127414796
    tail = poly * (t * bell)
    return jnp.where(x < 0, tail, 1.0 - tail), bell * 0.3989422804014327


def wide(mask, width):
    return jnp.concatenate([mask] * (width // 128), axis=1)


def place(ref, i, lanes):
    if len(ref.shape) == 4:
        return (i // ref.shape[1], lax.rem(i, ref.shape[1]), slice(None), lanes)
    return (pl.ds(pl.multiple_of(i * STEP, STEP), STEP), lanes)


def by_rows(pixels, width, work, sums=0):
    pieces = [slice(l, l + PIECE) for l in range(0, width, PIECE)]

    def one(i, carry):
        out = []
        for k, lanes in enumerate(pieces):
            got = work(i, lanes)
            for j in range(sums):
                folded = jnp.sum(got[j].reshape(STEP // 8, 8, PIECE), axis=0)
                out.append(carry[k * sums + j] + folded)
        return tuple(out)

    start = tuple(jnp.zeros((8, PIECE), F32) for _ in range(sums * len(pieces)))
    final = lax.fori_loop(0, pixels // STEP, one, start)
    rows = []
    for j in range(sums):
        parts = [jnp.sum(final[k * sums + j], axis=0, keepdims=True) for k in range(len(pieces))]
        rows.append(jnp.concatenate(parts, axis=1))
    return rows


NORM_ROWS = 8


def norm_table(exchange, gain_ref, shift_ref, out_ref, first):
    mean, var = exchange.rows()
    lanes = slice(first, first + mean.shape[1])
    inv = lax.rsqrt(var + EPSILON)
    out_ref[...] = jnp.zeros_like(out_ref)
    out_ref[0:1, :] = mean
    out_ref[1:2, :] = inv
    out_ref[2:3, :] = inv * gain_ref[:, lanes]
    out_ref[3:4, :] = shift_ref[:, lanes]
    out_ref[4:5, :] = var


def normed(u_ref, norm, i, lanes):
    away = u_ref[place(u_ref, i, lanes)].astype(F32) - norm[0:1, lanes]
    return away * norm[2:3, lanes] + norm[3:4, lanes], away


def activate(u_ref, norm, mask, h_ref, residual=None, slope=None, keep=None):
    def work(i, lanes):
        x, _ = normed(u_ref, norm, i, lanes)
        if residual is not None:
            x = x + residual[place(residual, i, lanes)].astype(F32)
        below, bell = gauss(x)
        m = wide(mask[place(mask, i, slice(None))], PIECE)
        h_ref[place(h_ref, i, lanes)] = (x * below * m).astype(BF16)
        if slope is not None:
            slope[place(slope, i, lanes)] = ((below + x * bell) * m).astype(BF16)
        if keep is not None:
            keep[place(keep, i, lanes)] = u_ref[place(u_ref, i, lanes)].astype(BF16)

    by_rows(mask.shape[0], norm.shape[1], work)


def device_stats(u_ref, mask, count):
    pixels, width = u_ref.shape

    def total_of(i, lanes):
        m = wide(mask[place(mask, i, slice(None))], PIECE)
        return (u_ref[place(u_ref, i, lanes)] * m,)

    (total,) = by_rows(pixels, width, total_of, 1)
    center = total / jnp.maximum(wide(count, width), 1.0)

    def spread_of(i, lanes):
        m = wide(mask[place(mask, i, slice(None))], PIECE)
        away = u_ref[place(u_ref, i, lanes)] - center[:, lanes]
        return (away * away * m,)

    (spread,) = by_rows(pixels, width, spread_of, 1)
    return total, spread


def product(a_ref, w_ref, o_ref, turned=False):
    dims = (((1,), (1 if turned else 0,)), ((), ()))

    def one(i, carry):
        rows = pl.ds(pl.multiple_of(i * CHUNK, CHUNK), CHUNK)
        o_ref[rows, :] = lax.dot_general(
            a_ref[rows, :], w_ref[...], dims, preferred_element_type=F32
        )
        return carry

    lax.fori_loop(0, a_ref.shape[0] // CHUNK, one, 0)


def turn(a_ref, t_ref):
    def one(i, carry):
        rows = pl.ds(pl.multiple_of(i * CHUNK, CHUNK), CHUNK)
        t_ref[:, rows] = a_ref[rows, :].T
        return carry

    lax.fori_loop(0, a_ref.shape[0] // CHUNK, one, 0)


def put_lanes(ref, first, value):
    width = ref.shape[-1]
    at, stop = first, first + value.shape[1]
    while at < stop:
        cut = at // width
        until = min(stop, (cut + 1) * width)
        part = value[:, at - first : until - first].astype(ref.dtype)
        lanes = slice(at - cut * width, until - cut * width)
        if len(ref.shape) == 4:
            ref[cut, :, :, lanes] = part.reshape(ref.shape[1:3] + part.shape[1:])
        else:
            ref[cut, :, lanes] = part
        at = until


def weight_product(t_ref, b_ref, gw_ref):
    channels = b_ref.shape[1]
    for first in range(0, channels, 512):
        value = jnp.dot(t_ref[...], b_ref[:, first : first + 512], preferred_element_type=F32)
        if len(gw_ref.shape) == 4 and gw_ref.shape[-1] == channels:
            part = value.astype(gw_ref.dtype).reshape(gw_ref.shape[:3] + (512,))
            gw_ref[:, :, :, first : first + 512] = part
        else:
            put_lanes(gw_ref, first, value)


def put_rows(ref, first, value):
    if len(ref.shape) == 3:
        ref[0, first : first + value.shape[0], :] = value.astype(ref.dtype)
        return
    rows = ref.shape[2]
    at, stop = first, first + value.shape[0]
    while at < stop:
        eighth = at // rows
        until = min(stop, (eighth + 1) * rows)
        low, high = at - eighth * rows, until - eighth * rows
        part = value[at - first : until - first].astype(ref.dtype)
        ref[eighth // 8, eighth % 8, low:high, :] = part
        at = until


def norm_back(e_ref, u_ref, norm, sums, pixel_count, mask, out_ref):
    sum_grad, sum_unit = (s * (1.0 / pixel_count) for s in sums)

    def work(i, lanes):
        away = u_ref[place(u_ref, i, lanes)].astype(F32) - norm[0:1, lanes]
        unit = away * norm[1:2, lanes]
        e = e_ref[place(e_ref, i, lanes)].astype(F32)
        m = wide(mask[place(mask, i, slice(None))], PIECE)
        grad = norm[2:3, lanes] * (e - sum_grad[:, lanes] - unit * sum_unit[:, lanes]) * m
        out_ref[place(out_ref, i, lanes)] = grad.astype(BF16)

    by_rows(mask.shape[0], norm.shape[1], work)


def gelu_grad(e_ref, u_ref, norm, mask):
    def work(i, lanes):
        x, away = normed(u_ref, norm, i, lanes)
        below, bell = gauss(x)
        m = wide(mask[place(mask, i, slice(None))], PIECE)
        e = e_ref[place(e_ref, i, lanes)] * (below + x * bell) * m
        e_ref[place(e_ref, i, lanes)] = e
        return e, e * (away * norm[1:2, lanes])

    return by_rows(mask.shape[0], norm.shape[1], work, 2)


def put_sums(exchange, out_ref):
    first, second = exchange.rows()
    out_ref[...] = jnp.zeros_like(out_ref)
    out_ref[0:1, :] = first
    out_ref[1:2, :] = second
    return first, second


def order_taps(rows, width):
    to = lax.broadcasted_iota(jnp.int32, (rows, width), 0)
    at = lax.broadcasted_iota(jnp.int32, (rows, width), 1)
    picked = jnp.where(to < 16, 2 * to, 2 * (to - 16) + 1)
    real = lax.rem(to, 16) < 9
    return jnp.where(jnp.logical_and(at == picked, real), 1.0, 0.0)


def make_mask(r, tile_cols):
    row, col = lax.axis_index(ROW), lax.axis_index(COL)
    rows, cols = lax.axis_size(ROW), lax.axis_size(COL)
    images = r.orientation.shape[0]
    tile_rows = r.mask.shape[0] // images // tile_cols
    tall = [r.orientation[n].astype(F32) for n in range(images)]
    for n in range(images):

        def fill(i, carry, n=n):
            column = lax.broadcasted_iota(jnp.int32, (tile_cols, 128), 0) + col * tile_cols
            portrait = jnp.where(column < SHORT, 1.0, 0.0)
            line = jnp.zeros((tile_cols, 128), jnp.int32) + (row * tile_rows + i)
            landscape = jnp.where(line < SHORT, 1.0, 0.0)
            at = (n * tile_rows + i) * tile_cols
            r.mask[pl.ds(pl.multiple_of(at, tile_cols), tile_cols), :] = (
                landscape * (1.0 - tall[n]) + portrait * tall[n]
            )
            return carry

        lax.fori_loop(0, tile_rows, fill, 0)

    def count(row, col):
        return (
            jnp.clip(SHORT - row * tile_rows, 0, tile_rows) * tile_cols,
            jnp.clip(SHORT - col * tile_cols, 0, tile_cols) * tile_rows,
        )

    def fill_count(at, row, col):
        flat, upright = (c.astype(F32) for c in count(row, col))
        total = added([flat * (1.0 - t) + upright * t for t in tall])
        r.counts[at : at + 1, :] = jnp.zeros((1, 128), F32) + total

    r.counts[...] = jnp.zeros_like(r.counts)
    for k in range(rows * cols):
        fill_count(k, jnp.int32(k // cols), jnp.int32(k % cols))
    fill_count(8, row, col)


def make_corners(r, cols):
    images, _, pixels = r.up.shape
    tile_cols = cols - HALF
    order = order_taps(32, r.base.shape[1]).astype(BF16)
    tap = lax.broadcasted_iota(jnp.int32, (16, pixels), 0)
    pixel = lax.broadcasted_iota(jnp.int32, (16, pixels), 1)
    up0 = pixel // tile_cols + PAD + 2 * (tap // 3 - 1)
    left0 = lax.rem(pixel, tile_cols) + HALF * lax.axis_index(COL) + 2 * (lax.rem(tap, 3) - 1)
    for n in range(images):
        base = r.base[n * pixels : (n + 1) * pixels, :].astype(F32).astype(BF16)
        moved = lax.dot_general(
            order, base, (((1,), (1,)), ((), ())), preferred_element_type=F32
        ).astype(jnp.int32)
        r.up[n] = moved[:16] + up0
        r.left[n] = moved[16:] + left0


def first(plane_count, r):
    ex, ex2 = Exchange(r.ex1), Exchange(r.ex2)
    images, all_rows, cols, width = r.rim.shape
    halos = [Halo(PAD, REACH, r.tile, r.rim, r.halo[2 * n : 2 * n + 2], n) for n in range(images)]
    make_mask(r, cols - HALF)
    r.ready(r.feature, r.w_reduce)
    product(r.feature, r.w_reduce, r.u_a1)
    r.push(r.u_a1)
    total, spread = device_stats(r.u_a1, r.mask, r.counts[8:9, :])
    wait_all()
    ex.put(total, spread)
    make_corners(r, cols)
    ex.middle_stats(r.counts, plane_count)
    for halo in halos:
        halo.blank()
    order = order_taps(32, r.w_offset.shape[0]).astype(BF16)
    for tap in range(9):
        columns = r.w_offset[:, tap * width : (tap + 1) * width]
        r.w_off[32 * tap : 32 * tap + 32, :] = jnp.dot(
            order, columns, preferred_element_type=F32
        ).astype(BF16)
    ex.finish_stats(plane_count)
    norm_table(ex, r.scale, r.shift, r.norm_a1, 0)
    activate(r.u_a1, r.norm_a1, r.mask, r.tile)
    halos[0].start()
    select_cells(r, cols)
    r.push(r.select)
    r.ready(r.w_deform)
    turn(r.w_deform, r.w_turned)
    for n, halo in enumerate(halos):
        if n == 0:
            halo.middle()
            halos[1].start()
        halo.finish()
        for k in range(0, all_rows, 8):
            lines = r.rim[n, k : k + 8].reshape(8 * cols, width)
            r.rim_t[n, :, k * cols : (k + 8) * cols] = lines.T
        offset_fractions(r, cols, n)
        sample_units(r, cols, n, 0)
        if n + 1 < images:
            halos[n + 1].middle()
        sample_units(r, cols, n, 1)
    r.push(r.rim, r.fr, r.fc, r.samples, r.u_a2)
    total, spread = device_stats(r.u_a2, r.mask, r.counts[8:9, :])
    ex2.put(total, spread)
    ex2.middle_stats(r.counts, plane_count)
    ex2.finish_stats(plane_count)
    norm_table(ex2, r.scale, r.shift, r.norm_a2, width)


def offset_fractions(r, cols, n):
    _, width, cells = r.rim_t.shape
    column = lax.rem(lax.broadcasted_iota(jnp.int32, (32, cells), 1), cols)
    r.spread[...] = jnp.dot(r.w_off[...], r.rim_t[n], preferred_element_type=F32)
    total = None
    for tap in range(9):
        i, j = 2 * (tap // 3 - 1), 2 * (tap % 3 - 1)
        term = r.spread[32 * tap : 32 * tap + 32, :]
        shift = -(i * cols + j) % cells
        if shift:
            term = pltpu.roll(term, shift, axis=1)
        if j < 0:
            term = jnp.where(column >= -j, term, 0.0)
        if j > 0:
            term = jnp.where(column < cols - j, term, 0.0)
        total = term if total is None else total + term
    parts = []
    for _ in range(3):
        parts.append(total.astype(BF16))
        total = total - parts[-1].astype(F32)
    on_tile = lax.dot_general(
        jnp.concatenate(parts, axis=0),
        r.select[...],
        (((1,), (1,)), ((), ())),
        preferred_element_type=F32,
    )
    offsets = on_tile[:32] + on_tile[32:64] + on_tile[64:]
    fraction = 1.0 / (1.0 + jnp.exp(-offsets))
    r.fr[n] = fraction[:16]
    r.fc[n] = fraction[16:]


def sample_units(r, cols, n, b):
    block = r.table.shape[1]
    width = r.rim_t.shape[1]
    lanes = slice(b * block, (b + 1) * block)
    mine = slice((2 * n + b) * block, (2 * n + b + 1) * block)
    base = b * (BLOCK_ROWS * cols)
    for tap in range(9):
        row_w, _, col_w, _ = tap_weights(tap, b, cols, r.up, r.left, r.fr, r.fc, n, lanes)
        write_table(r.table, 0, row_w, col_w, tap // 3, cols)
        _, start, stop = tap_span(tap // 3, cols)
        cells = r.rim_t[n, :, base + start : base + stop]
        value = jnp.dot(cells, r.table[start:stop, :], preferred_element_type=F32)
        r.samples[tap * width : (tap + 1) * width, mine] = value.astype(BF16)
    deformed = jnp.dot(r.w_turned[...], r.samples[:, mine], preferred_element_type=F32)
    r.u_a2[mine, :] = deformed.T


def finish_kernel(unbias, count, *refs):
    ins, outs, rest = refs[:count], refs[count : count + 17], refs[count + 17 :]
    bufs, out_bufs, sems, out_sems = rest[:count], rest[count : count + 15], rest[-2], rest[-1]
    loads = [pltpu.make_async_copy(ins[k], bufs[k], sems.at[k]) for k in range(count)]
    stores = [pltpu.make_async_copy(out_bufs[k], outs[k], out_sems.at[k]) for k in range(15)]
    stores += [
        pltpu.make_async_copy(bufs[count - 2 + k], outs[15 + k], out_sems.at[15 + k]) for k in range(2)
    ]
    for load in loads:
        load.start()
    conv_b, reduce_b, reduce_a, expand_b, expand_a, deform, off = bufs[:7]
    tables = bufs[7:19]
    for load in loads[:7]:
        load.wait()
    for k, src in enumerate((expand_b, expand_a, deform)):
        rows = src.shape[1]
        for s in range(8):
            out_bufs[3 + k][s * rows : (s + 1) * rows, :] = src[s].astype(F32)
        stores[3 + k].start()
    for k, src in enumerate((conv_b, reduce_b, reduce_a)):
        eighth = src.shape[1]
        for s in range(0, 8, 2):
            rows = jnp.concatenate([src[s], src[s + 1]], axis=0).astype(F32)
            out_bufs[k][:, s * eighth : (s + 2) * eighth] = rows.T
        stores[k].start()
    for k in range(2):
        loads[count - 2 + k].wait()
        stores[15 + k].start()
    rest, total = off[...], None
    order = order_taps(32, 18).astype(BF16)
    for _ in range(3):
        part = rest.astype(BF16)
        rest = rest - part.astype(F32)
        term = lax.dot_general(order, part, (((0,), (0,)), ((), ())), preferred_element_type=F32)
        total = term if total is None else total + term
    out_bufs[6][...] = total
    for load in loads[7 : count - 2]:
        load.wait()
    for k in range(4):
        group, which = tables[3 * k : 3 * k + 3], out_bufs[7 + 2 * k : 9 + 2 * k]
        norms = k >= 2
        for out, row in zip(which, (0, 4) if norms else (1, 0)):
            at = 0
            for table in group:
                for first_lane in range(0, table.shape[1], 128):
                    value = table[row : row + 1, first_lane : first_lane + 128]
                    out[at : at + 1, :] = value * unbias if norms and row == 4 else value
                    at += 1
    for store in stores[6:15]:
        store.start()
    for store in stores:
        store.wait()


def forward(plane_count, r):
    ex_a3, ex_b1, ex_b2 = Exchange(r.ex_a3), Exchange(r.ex_b1), Exchange(r.ex_b2)
    ex_b3, ex_sums = Exchange(r.ex_b3), Exchange(r.ex_sums)
    halo = Halo(2, 2, r.tile, r.rim_b, r.halo)
    halo.blank()
    width = r.h2_a.shape[1]
    count = r.counts[8:9, :]

    def exchange(ex, u_ref):
        ex.put(*device_stats(u_ref, r.mask, count))
        ex.middle_stats(r.counts, plane_count)

    r.ready(r.u_a2)
    activate(r.u_a2, r.norm_a2, r.mask, r.h2_a)
    r.push(r.h2_a)
    r.ready(r.w_expand_a)
    product(r.h2_a, r.w_expand_a, r.wide)
    wait_all()
    exchange(ex_a3, r.wide)
    r.ready(r.feature, r.w_reduce)
    ex_a3.finish_stats(plane_count)
    norm_table(ex_a3, r.scale_a, r.shift_a, r.norm_a3, 2 * width)
    activate(r.wide, r.norm_a3, r.mask, r.middle, r.feature, r.slope_a, r.u_a3)
    r.push(r.middle, r.slope_a, r.u_a3)
    cotangent = pltpu.make_async_copy(r.cotangent, r.feature, r.far_sems.at[0])
    cotangent.start()
    product(r.middle, r.w_reduce, r.u_b1)
    r.push(r.u_b1)
    exchange(ex_b1, r.u_b1)
    ex_b1.finish_stats(plane_count)
    norm_table(ex_b1, r.scale_b, r.shift_b, r.norm_b1, 0)
    activate(r.u_b1, r.norm_b1, r.mask, r.tile)
    halo.start()
    halo.middle()
    halo.finish()
    r.push(r.rim_b)
    build_shifted(r.rim_b, r.shifted)
    r.ready(r.w_conv)
    conv_product(r.shifted, r.w_conv, r.u_b2)
    r.push(r.u_b2)
    exchange(ex_b2, r.u_b2)
    ex_b2.finish_stats(plane_count)
    norm_table(ex_b2, r.scale_b, r.shift_b, r.norm_b2, width)
    activate(r.u_b2, r.norm_b2, r.mask, r.h2_b)
    r.push(r.h2_b)
    r.ready(r.w_expand_b)
    product(r.h2_b, r.w_expand_b, r.wide)
    exchange(ex_b3, r.wide)
    cotangent.wait()
    r.pushed(r.slope_a, r.u_a3)
    e_b3, u_b3, norm = r.slope_a, r.u_a3, r.norm_b3
    ex_b3.finish_stats(plane_count)
    norm_table(ex_b3, r.scale_b, r.shift_b, norm, 2 * width)

    def work(i, lanes):
        x, away = normed(r.wide, norm, i, lanes)
        at = place(r.wide, i, lanes)
        u_b3[at] = r.wide[at].astype(BF16)
        x = x + r.middle[at].astype(F32)
        below, bell = gauss(x)
        m = wide(r.mask[place(r.mask, i, slice(None))], PIECE)
        r.feature_out[at] = (x * below * m).astype(BF16)
        e = (below + x * bell) * r.feature[at].astype(F32) * m
        e_b3[at] = e.astype(BF16)
        return e, e * (away * norm[1:2, lanes])

    sums = by_rows(r.wide.shape[0], r.wide.shape[1], work, 2)
    ex_sums.put(*sums)
    far = [
        pltpu.make_async_copy(e_b3, r.e_b3, r.far_sems.at[1]),
        pltpu.make_async_copy(u_b3, r.u_b3, r.far_sems.at[2]),
    ]
    for copy in far:
        copy.start()
    r.push(r.feature_out)
    ex_sums.middle_sums()
    ex_sums.finish_sums()
    put_sums(ex_sums, r.sums_b3)
    for copy in far:
        copy.wait()


def backward_b(pixel_count, direct, r):
    ex2, ex1 = Exchange(r.ex2), Exchange(r.ex1)
    halo = Halo(2, 2, r.tile, r.back_rim, r.halo)
    halo.blank()
    r.ready(r.e_b3, r.u_b3)
    sums = (r.sums_b3[0:1, :], r.sums_b3[1:2, :])
    norm_back(r.e_b3, r.u_b3, r.norm_b3, sums, pixel_count, r.mask, r.geo)
    r.ready(r.w_expand)
    product(r.geo, r.w_expand, r.grad, turned=True)
    r.ready(r.u_b2)
    sums = gelu_grad(r.grad, r.u_b2, r.norm_b2, r.mask)
    wait_all()
    ex2.put(*sums)
    r.ready(r.h2_b)
    turn(r.h2_b, r.turned)
    ex2.middle_sums()
    weight_product(r.turned, r.geo, r.gw_expand)
    jobs = Jobs()
    if direct:
        jobs.add(*plane_jobs(r.gw_expand, r.eighth_expand_b, r.plane_expand_b))
    else:
        r.push(r.gw_expand)
    jobs.tick(2)
    ex2.finish_sums()
    sums = put_sums(ex2, r.sums_b2)
    norm_back(r.grad, r.u_b2, r.norm_b2, sums, pixel_count, r.mask, r.tile)
    halo.start()
    tile_rows, tile_cols, width = r.tile.shape[1:]
    pixels = tile_rows * tile_cols
    for n in range(r.tile.shape[0]):
        for k in range(0, tile_rows, 8):
            at = n * pixels + k * tile_cols
            block = r.tile[n, k : k + 8].reshape(8 * tile_cols, width)
            r.turned[:, at : at + 8 * tile_cols] = block.T
    r.ready(r.rim_b)
    build_shifted(r.rim_b, r.shifted)
    conv_weight_product(r.turned, r.shifted, r.gw_conv, 0)
    halo.middle()
    jobs.tick(2)
    conv_weight_product(r.turned, r.shifted, r.gw_conv, 1)
    halo.finish()
    build_shifted(r.back_rim, r.back_shifted)
    r.ready(r.w_conv)
    unconv_product(r.back_shifted, r.w_conv, r.grad)
    r.ready(r.u_b1)
    sums = gelu_grad(r.grad, r.u_b1, r.norm_b1, r.mask)
    ex1.put(*sums)
    jobs.tick(2)
    ex1.middle_sums()
    conv_weight_product(r.turned, r.shifted, r.gw_conv, 2)
    r.push(r.gw_conv)
    jobs.finish()
    if direct:
        r.push(r.eighth_expand_b)
    ex1.finish_sums()
    sums = put_sums(ex1, r.sums_b1)
    norm_back(r.grad, r.u_b1, r.norm_b1, sums, pixel_count, r.mask, r.gro_b)


def backward_a(pixel_count, direct, r):
    ex3, ex2 = Exchange(r.ex3), Exchange(r.ex2)
    conv, line = Jobs(), Jobs()
    r.ready(r.gro_b, r.w_reduce)
    product(r.gro_b, r.w_reduce, r.wide, turned=True)
    wait_all()
    if direct:
        r.ready(r.src_conv_b, r.eighth_expand_b)
        conv.add(*plane_jobs(r.src_conv_b, r.eighth_conv_b, r.plane_conv_b))
        line.add(*line_jobs(r.eighth_expand_b, r.sum_expand_b, r.line_expand_b))
    conv.tick(2)
    line.tick(2)
    r.ready(r.e_b3, r.slope_a, r.u_a3)
    norm = r.norm_a3

    def work(i, lanes):
        at = place(r.wide, i, lanes)
        e = (r.wide[at] + r.e_b3[at].astype(F32)) * r.slope_a[at].astype(F32)
        r.e_a3[at] = e.astype(BF16)
        away = r.u_a3[at].astype(F32) - norm[0:1, lanes]
        return e, e * (away * norm[1:2, lanes])

    sums = by_rows(r.wide.shape[0], r.wide.shape[1], work, 2)
    ex3.put(*sums)
    conv.tick(2)
    r.push(r.e_a3)
    turn(r.gro_b, r.turned)
    ex3.middle_sums()
    r.ready(r.middle)
    weight_product(r.turned, r.middle, r.gw_reduce)
    r.push(r.gw_reduce)
    line.tick(2)
    ex3.finish_sums()
    sums = put_sums(ex3, r.sums_a3)
    norm_back(r.e_a3, r.u_a3, norm, sums, pixel_count, r.mask, r.e_b3)
    r.ready(r.w_expand)
    product(r.e_b3, r.w_expand, r.grad, turned=True)
    r.ready(r.u_a2)
    sums = gelu_grad(r.grad, r.u_a2, r.norm_a2, r.mask)
    ex2.put(*sums)
    conv.tick(2)
    line.tick(2)
    r.ready(r.h2_a)
    turn(r.h2_a, r.turned)
    ex2.middle_sums()
    weight_product(r.turned, r.e_b3, r.gw_expand)
    r.push(r.gw_expand)
    line.tick(2)
    ex2.finish_sums()
    sums = put_sums(ex2, r.sums_a2)
    norm_back(r.grad, r.u_a2, r.norm_a2, sums, pixel_count, r.mask, r.gd)
    conv.finish()
    line.finish()
    if direct:
        r.push(r.eighth_conv_b, r.sum_expand_b)


def unsample(r, plan):
    width = r.rim.shape[2]
    cols = r.table.shape[0] // WINDOW
    pixels = r.up.shape[2] // 2
    r.spill[...] = jnp.zeros_like(r.spill)
    r.grad_row[...] = jnp.zeros_like(r.grad_row)
    r.grad_col[...] = jnp.zeros_like(r.grad_col)

    def unit(step, carry):
        n, block = step // 2, lax.rem(step, 2)
        lanes = pl.ds(pl.multiple_of(block * pixels, pixels), pixels)
        base = block * (BLOCK_ROWS * cols)
        grad_in = r.turned[:, pl.ds(pl.multiple_of(step * pixels, pixels), pixels)]
        for group in range(3):
            first, start, stop = tap_span(group, cols)
            cells = pl.ds(pl.multiple_of(base + start, 128), stop - start)
            for j in range(3):
                tap = 3 * group + j
                spot = slice(j * pixels, (j + 1) * pixels)
                row_w, row_s, col_w, col_s = tap_weights(
                    tap, block, cols, r.up, r.left, r.fr, r.fc, n, lanes
                )
                write_table(r.table, j * pixels, row_w, col_w, group, cols)
                grad = jnp.dot(
                    r.w_deform[tap * width : (tap + 1) * width, :],
                    grad_in,
                    preferred_element_type=F32,
                ).astype(BF16)
                r.grads[:, spot] = grad
                scores = jnp.dot(r.rim[n, cells, :], grad, preferred_element_type=F32)
                by_value = jnp.zeros((cols, pixels), F32)
                by_slope = jnp.zeros((cols, pixels), F32)
                for k in range(first, first + SPAN):
                    line = scores[k * cols - start : (k + 1) * cols - start]
                    by_value = by_value + line * row_w[k : k + 1, :]
                    by_slope = by_slope + line * row_s[k : k + 1, :]
                r.grad_row[n, tap : tap + 1, lanes] = jnp.sum(
                    by_slope * col_w, axis=0, keepdims=True
                )
                r.grad_col[n, tap : tap + 1, lanes] = jnp.sum(
                    by_value * col_s, axis=0, keepdims=True
                )
            r.spill[n, cells, :] += lax.dot_general(
                r.table[start:stop, :],
                r.grads[...],
                (((1,), (1,)), ((), ())),
                preferred_element_type=F32,
            )
            for turn_at in range(4):
                if 3 * turn_at + group in plan:

                    @pl.when(step == turn_at)
                    def _(slot=3 * turn_at + group):
                        plan[slot]()

        return carry

    lax.fori_loop(0, 4, unit, 0)


def select_cells(r, cols):
    off = HALF * lax.axis_index(COL)
    cells = r.select.shape[1]

    def fill(i, carry):
        ids = lax.broadcasted_iota(jnp.int32, (STEP, cells), 1)
        pixel = lax.broadcasted_iota(jnp.int32, (STEP, cells), 0)
        hit = ids == pixel + (i + PAD) * cols + off
        r.select[pl.ds(pl.multiple_of(i * STEP, STEP), STEP), :] = jnp.where(hit, 1.0, 0.0).astype(
            BF16
        )
        return carry

    lax.fori_loop(0, r.select.shape[0] // STEP, fill, 0)


def unoffset(r, n):
    images, cells, width = r.rim.shape
    cols = r.table.shape[0] // WINDOW
    column = lax.rem(lax.broadcasted_iota(jnp.int32, (32, cells), 1), cols)
    parts = []
    for grad, frac in ((r.grad_row, r.fr), (r.grad_col, r.fc)):
        f = frac[n]
        parts.append(grad[n] * f * (1.0 - f))
    go = jnp.concatenate(parts, axis=0).astype(BF16)
    on_tile = jnp.dot(go, r.select[...], preferred_element_type=F32)
    for tap in range(9):
        i, j = 2 * (tap // 3 - 1), 2 * (tap % 3 - 1)
        kept = on_tile
        if j < 0:
            kept = jnp.where(column >= -j, on_tile, 0.0)
        if j > 0:
            kept = jnp.where(column < cols - j, on_tile, 0.0)
        shift = (i * cols + j) % cells
        if shift:
            kept = pltpu.roll(kept, shift, axis=1)
        r.on_cells[32 * tap : 32 * tap + 32, :] = kept.astype(BF16)
    grad = jnp.dot(r.on_cells[...], r.rim[n], preferred_element_type=F32)
    if n == 0:
        r.gw_off_sum[...] = grad
    else:
        r.gw_off_sum[...] += grad
    for first in range(0, cells, 512):
        r.spill[n, first : first + 512, :] += lax.dot_general(
            r.on_cells[:, first : first + 512],
            r.w_off[...],
            (((0,), (0,)), ((), ())),
            preferred_element_type=F32,
        )
    if n == images - 1:
        for tap in range(9):
            put_lanes(r.gw_off, tap * width, r.gw_off_sum[32 * tap : 32 * tap + 32, :])


class Spill:
    @staticmethod
    def scratch(images, tile_rows, tile_cols, width):
        side = pltpu.VMEM((images, tile_rows + 2 * PAD, HALF, width), BF16)
        strip = pltpu.VMEM((images, REACH, tile_cols, width), BF16)
        sems = pltpu.SemaphoreType.DMA((3,))
        return [side, side, strip, strip, strip, strip, sems, sems]

    def __init__(self, spill, grad, cols, refs, image):
        self.spill, self.grad, self.cols = spill.at[pl.ds(image, 1)], grad, cols
        self.image = image
        self.side_out, self.side_in, self.up_out, self.down_out, self.up_in, self.down_in = refs[:6]
        send, recv = refs[6:]
        self.row, self.rows, col, pair, above, below = halo_peers()
        self.images, self.all_rows = self.side_out.shape[:2]
        self.tile_rows, self.tile_cols = self.all_rows - 2 * PAD, self.up_out.shape[2]
        self.off, self.away, self.near = HALF * col, 2 * HALF * (1 - col), HALF * (1 - col)
        self.side = remote(self.side_out, self.side_in, send.at[0], recv.at[0], pair)
        self.up = remote(self.up_out, self.down_in, send.at[1], recv.at[1], above)
        self.down = remote(self.down_out, self.up_in, send.at[2], recv.at[2], below)

    def cells(self, k, first, count):
        return pl.ds(pl.multiple_of(k * self.cols + first, HALF), count)

    def start(self):
        def cast(k, carry):
            for n in range(self.images):
                self.side_out[n, k] = self.spill[n, self.cells(k, self.away, HALF), :].astype(BF16)
            return carry

        lax.fori_loop(0, self.all_rows, cast, 0)
        self.side.start()

    def edge(self, buffer, first):
        near = pl.ds(pl.multiple_of(self.near, HALF), HALF)

        def one(k, carry):
            for n in range(self.images):
                at = first + k
                buffer[n, k] = self.spill[n, self.cells(at, self.off, self.tile_cols), :].astype(BF16)
                part = self.spill[n, self.cells(at, HALF, HALF), :]
                buffer[n, k, near, :] = (part + self.side_in[n, at].astype(F32)).astype(BF16)
            return carry

        lax.fori_loop(0, REACH, one, 0)

    def middle(self):
        self.side.wait_recv()

        @pl.when(self.row > 0)
        def _():
            self.edge(self.up_out, PAD - REACH)
            self.up.start()

        @pl.when(self.row < self.rows - 1)
        def _():
            self.edge(self.down_out, PAD + self.tile_rows)
            self.down.start()

    def pixels(self, n, k, first, count):
        at = ((self.image + n) * self.tile_rows + k) * self.tile_cols + first
        return pl.ds(pl.multiple_of(at, HALF), count)

    def own(self):
        def fill(k, carry):
            for n in range(self.images):
                home = self.spill[n, self.cells(PAD + k, self.off, self.tile_cols), :]
                self.grad[self.pixels(n, k, 0, self.tile_cols), :] = home
                self.grad[self.pixels(n, k, self.near, HALF), :] += self.side_in[n, PAD + k].astype(F32)
            return carry

        lax.fori_loop(0, self.tile_rows, fill, 0)

    def finish(self):
        def arrive(buffer, first):
            def one(k, carry):
                for n in range(self.images):
                    at = self.pixels(n, first + k, 0, self.tile_cols)
                    self.grad[at, :] += buffer[n, k].astype(F32)
                return carry

            lax.fori_loop(0, REACH, one, 0)

        @pl.when(self.row > 0)
        def _():
            self.down.wait_recv()
            arrive(self.up_in, 0)
            self.up.wait_send()

        @pl.when(self.row < self.rows - 1)
        def _():
            self.up.wait_recv()
            arrive(self.down_in, self.tile_rows - REACH)
            self.down.wait_send()

        self.side.wait_send()


def backward_s(pixel_count, direct, r):
    ex = Exchange(r.ex1)
    cols = r.table.shape[0] // WINDOW
    spills = [Spill(r.spill, r.grad, cols, r.strips[8 * n : 8 * n + 8], n) for n in range(2)]

    mid, late, end = Jobs(), Jobs(), Jobs()
    deform_weight_product(r)
    wait_all()
    if direct:
        line, reduce, expand, deform = Jobs(), Jobs(), Jobs(), Jobs()
        line.add(*part_jobs(LineSum, r.eighth_conv_b, r.own_conv_b, r.line_conv_b))
        reduce.add(*plane_jobs(r.src_reduce_b, r.eighth_reduce_b, r.plane_reduce_b))
        reduce.add(*part_jobs(LineSum, r.eighth_reduce_b, r.own_reduce_b, r.line_reduce_b))
        expand.add(*part_jobs(LinePlane, r.src_expand_a, r.own_expand_a, r.plane_expand_a))
        deform.add(*plane_jobs(r.gw_deform, r.eighth_deform, r.plane_deform))
        deform.add(*part_jobs(LineSum, r.eighth_deform, r.own_deform, r.line_deform))
        deform.tick(2)
        r.ready(r.eighth_conv_b)
        line.tick(2)
        r.ready(r.src_expand_a, r.src_reduce_b)
        q1, q2, q3, q4 = line.queue, reduce.queue, expand.queue, deform.queue
        slots = {
            1: q4[0:2] + q3[0:2],
            3: q3[2:4] + q2[0:2],
            6: q4[2:4],
            7: q2[2:4] + q1[0:2],
            9: q4[4:8],
            10: q2[4:6],
        }
        mid.queue = q2[6:10] + q3[4:6]
        late.queue = q3[6:8]
        end.queue = q4[8:10] + q2[10:12] + q3[8:10]
    else:
        slots = {}
        r.push(r.gw_deform)
    slots[5] = [functools.partial(unoffset, r, 0), spills[0].start] + slots.get(5, [])
    slots[8] = [spills[0].middle] + slots.get(8, [])

    def run(queue):
        def call():
            for step in queue:
                step()

        return call

    plan = {slot: run(queue) for slot, queue in slots.items()}
    r.ready(r.w_deform, r.rim, r.w_off, r.select)
    turn(r.gd, r.turned)
    unsample(r, plan)
    unoffset(r, 1)
    spills[1].start()
    r.push(r.gw_off)
    spills[1].middle()
    mid.finish()
    for spill in spills:
        spill.own()
    spills[0].finish()
    late.finish()
    if direct:
        r.push(r.own_conv_b)
    r.ready(r.u_a1)
    spills[1].finish()
    sums = gelu_grad(r.grad, r.u_a1, r.norm_a1, r.mask)
    ex.put(*sums)
    ex.middle_sums()
    ex.finish_sums()
    sums = put_sums(ex, r.sums_a1)
    norm_back(r.grad, r.u_a1, r.norm_a1, sums, pixel_count, r.mask, r.gr_a)
    end.finish()
    if direct:
        r.push(r.own_reduce_b, r.own_expand_a, r.own_deform)


def deform_weight_product(r):
    width = r.gd.shape[1]
    slots = r.sample_slots.shape[0]

    def load(tap):
        rows, slot = pl.ds(tap * width, width), tap % slots
        return pltpu.make_async_copy(
            r.samples.at[rows], r.sample_slots.at[slot], r.sample_sems.at[slot]
        )

    for tap in range(slots):
        load(tap).start()
    r.ready(r.gd)
    for tap in range(9):
        load(tap).wait()
        value = jnp.dot(r.sample_slots[tap % slots], r.gd[...], preferred_element_type=F32)
        put_rows(r.gw_deform, tap * width, value)
        if tap + slots < 9:
            load(tap + slots).start()


def last(direct, r):
    jobs, more, plane = Jobs(), Jobs(), Jobs()
    r.ready(r.gr_a, r.feature)
    wait_all()
    if direct:
        r.ready(r.own_deform, r.gw_off)
        jobs.add(
            *part_jobs(Gather, r.own_deform, r.sum_deform, r.gather_deform),
            SmallSum(r.gw_off, r.sum_off, r.small),
        )
        more.add(
            *part_jobs(Gather, r.own_conv_b, r.sum_conv_b, r.gather_conv_b),
            *part_jobs(Gather, r.own_reduce_b, r.sum_reduce_b, r.gather_reduce_b),
            *part_jobs(Gather, r.own_expand_a, r.sum_expand_a, r.gather_expand_a),
        )
    jobs.tick(3)
    turn(r.gr_a, r.turned)
    weight_product(r.turned, r.feature, r.gw_reduce)
    if direct:
        plane.add(*plane_jobs(r.gw_reduce, r.eighth_reduce_a, r.plane_reduce_a))
        plane.add(*line_jobs(r.eighth_reduce_a, r.sum_reduce_a, r.line_reduce_a))
    else:
        r.push(r.gw_reduce)
    plane.tick(2)
    jobs.tick(3)
    if direct:
        r.ready(r.own_conv_b, r.own_reduce_b, r.own_expand_a)
    r.ready(r.w_reduce, r.e_a3)

    def chunk(i, carry):
        rows = pl.ds(pl.multiple_of(i * CHUNK, CHUNK), CHUNK)
        for first in range(0, r.feature.shape[1], 512):
            lanes = slice(first, first + 512)
            grad = lax.dot_general(
                r.gr_a[rows, :],
                r.w_reduce[lanes, :],
                (((1,), (1,)), ((), ())),
                preferred_element_type=F32,
            )
            r.grad_in[rows, lanes] = (grad + r.e_a3[rows, lanes].astype(F32)).astype(BF16)
        return carry

    half = r.feature.shape[0] // CHUNK // 2
    lax.fori_loop(0, half, chunk, 0)
    plane.tick(2)
    lax.fori_loop(half, 2 * half, chunk, 0)
    r.push(r.grad_in)
    more.tick(6)
    plane.tick(2)
    more.tick(6)
    jobs.tick(3)
    plane.tick(4)
    more.tick(6)
    jobs.finish()
    more.finish()
    if direct:
        r.push(r.sum_conv_b, r.sum_reduce_b, r.sum_expand_a, r.sum_deform)
    plane.finish()
    if direct:
        r.push(r.sum_reduce_a)


def body(
    feature_in,
    orientation,
    offset_base,
    w_reduce_a,
    w_offset_a,
    w_deform_a,
    w_expand_a,
    scale_a,
    shift_a,
    w_reduce_b,
    w_conv_b,
    w_expand_b,
    scale_b,
    shift_b,
    cotangent,
):
    images, tile_rows, tile_cols, channels = feature_in.shape
    inner_width = w_reduce_a.shape[1]
    tile_pixels = tile_rows * tile_cols
    pixels = images * tile_pixels
    win_cols = tile_cols + HALF
    win_rows = tile_rows + 2 * PAD
    cells = win_rows * win_cols
    plane_count = 1.0 * images * LONG * SHORT
    pixel_count = plane_count * lax.axis_size(IMG)
    unbias = pixel_count / (pixel_count - 1.0)

    def array(*shape, dtype=BF16):
        return jax.ShapeDtypeStruct(shape, dtype)

    def table(width):
        return array(NORM_ROWS, width, dtype=F32)

    small = (pixels, inner_width)
    big = (pixels, channels)
    window_b = (images, tile_rows + 4, win_cols, inner_width)
    shifted = pltpu.VMEM((images, tile_rows + 4, tile_cols, 3 * inner_width), BF16)
    tile = pltpu.VMEM((images, tile_rows, tile_cols, inner_width), BF16)
    turned = pltpu.VMEM((inner_width, pixels), BF16)
    images_axis = lax.axis_size(IMG)
    direct = inner_width % (images_axis * 8 * 16) == 0
    cuts = images_axis if direct else 1
    feature = feature_in.reshape(big)
    scale_a, shift_a, scale_b, shift_b = (v[None] for v in (scale_a, shift_a, scale_b, shift_b))
    taps_shape = (images, 16, tile_pixels)
    start = fused(
        functools.partial(first, plane_count),
        FIRST_CID,
        ins=dict(
            base=offset_base.reshape(pixels, 18),
            w_offset=w_offset_a.T,
            scale=scale_a,
            shift=shift_a,
        ),
        smem=dict(orientation=orientation),
        staged=dict(feature=feature, w_reduce=w_reduce_a, w_deform=w_deform_a),
        outs=dict(
            mask=array(pixels, 128, dtype=F32),
            counts=array(16, 128, dtype=F32),
            up=array(*taps_shape, dtype=jnp.int32),
            left=array(*taps_shape, dtype=jnp.int32),
            w_off=array(288, inner_width),
            norm_a1=table(inner_width),
            norm_a2=table(inner_width),
        ),
        pushed=dict(
            u_a1=array(*small, dtype=F32),
            rim=array(images, win_rows, win_cols, inner_width),
            select=array(tile_pixels, cells),
            fr=array(*taps_shape, dtype=F32),
            fc=array(*taps_shape, dtype=F32),
            samples=array(9 * inner_width, pixels),
            u_a2=array(*small, dtype=F32),
        ),
        scratch=dict(
            ex1=Exchange.scratch(inner_width),
            ex2=Exchange.scratch(inner_width),
            halo=Halo.scratch * images,
            tile=tile,
            w_turned=pltpu.VMEM((inner_width, 9 * inner_width), BF16),
            rim_t=pltpu.VMEM((images, inner_width, cells), BF16),
            spread=pltpu.VMEM((288, cells), F32),
            table=pltpu.VMEM((WINDOW * win_cols, tile_pixels // 2), BF16),
        ),
    )
    mask, count_rows, norm_a1 = start.mask, start.counts, start.norm_a1
    rim_flat = start.rim.reshape(images, cells, inner_width)
    norm_a2, deformed = start.norm_a2, start.u_a2
    fwd = fused(
        functools.partial(forward, plane_count),
        FORWARD_CID,
        ins=dict(
            norm_a2=norm_a2,
            mask=mask,
            counts=count_rows,
            scale_a=scale_a,
            shift_a=shift_a,
            scale_b=scale_b,
            shift_b=shift_b,
        ),
        far=dict(cotangent=cotangent.reshape(big)),
        staged=dict(
            u_a2=deformed,
            w_expand_a=w_expand_a,
            feature=feature,
            w_reduce=w_reduce_b,
            w_conv=w_conv_b,
            w_expand_b=w_expand_b,
        ),
        outs=dict(
            norm_a3=table(channels),
            norm_b1=table(inner_width),
            norm_b2=table(inner_width),
            norm_b3=table(channels),
            sums_b3=table(channels),
        ),
        pushed=dict(
            h2_a=array(*small),
            middle=array(*big),
            slope_a=array(*big),
            u_a3=array(*big),
            u_b1=array(*small, dtype=F32),
            rim_b=array(*window_b),
            u_b2=array(*small, dtype=F32),
            h2_b=array(*small),
            feature_out=array(*big),
        ),
        far_outs=dict(e_b3=array(*big), u_b3=array(*big)),
        scratch=dict(
            ex_a3=Exchange.scratch(channels),
            ex_b1=Exchange.scratch(inner_width),
            ex_b2=Exchange.scratch(inner_width),
            ex_b3=Exchange.scratch(channels),
            ex_sums=Exchange.scratch(channels),
            halo=Halo.scratch,
            wide=pltpu.VMEM(big, F32),
            tile=tile,
            shifted=shifted,
            far_sems=pltpu.SemaphoreType.DMA((3,)),
        ),
    )
    def eighths(grad):
        return grad.reshape(images_axis, 8, -1, grad.shape[-1])

    def eighth_of(src):
        return array(images_axis, *src.shape[2:])

    def own_of(src):
        return array(*src.shape[2:])

    def sum_of(src):
        return array(*src.shape[1:])

    def vmem(struct):
        return pltpu.VMEM(struct.shape, struct.dtype)

    natural = array(1, inner_width, channels)
    pushed_b, scratch_b = dict(gw_expand=natural), {}
    if direct:
        expand_b = array(images_axis, 8, inner_width // images_axis // 8, channels)
        pushed_b = dict(eighth_expand_b=eighth_of(expand_b))
        scratch_b = dict(gw_expand=vmem(expand_b), plane_expand_b=Plane.scratch(expand_b.shape))
    bwd_b = fused(
        functools.partial(backward_b, pixel_count, direct),
        BACKWARD_B_CID,
        ins=dict(
            mask=mask,
            norm_b3=fwd.norm_b3,
            sums_b3=fwd.sums_b3,
            norm_b2=fwd.norm_b2,
            norm_b1=fwd.norm_b1,
        ),
        staged=dict(
            e_b3=fwd.e_b3,
            u_b3=fwd.u_b3,
            w_expand=w_expand_b,
            u_b2=fwd.u_b2,
            h2_b=fwd.h2_b,
            rim_b=fwd.rim_b,
            w_conv=w_conv_b,
            u_b1=fwd.u_b1,
        ),
        outs=dict(gro_b=array(*small), sums_b2=table(inner_width), sums_b1=table(inner_width)),
        pushed=dict(
            **pushed_b,
            gw_conv=array(cuts, inner_width, 9 * inner_width // cuts),
        ),
        scratch=dict(
            **scratch_b,
            ex2=Exchange.scratch(inner_width),
            ex1=Exchange.scratch(inner_width),
            halo=Halo.scratch,
            geo=pltpu.VMEM(big, BF16),
            grad=pltpu.VMEM(small, F32),
            tile=tile,
            turned=turned,
            back_rim=pltpu.VMEM(window_b, BF16),
            shifted=shifted,
            back_shifted=shifted,
        ),
    )

    staged_a, pushed_a, scratch_a = {}, {}, {}
    if direct:
        conv_b = eighths(bwd_b.gw_conv)
        staged_a = dict(src_conv_b=conv_b, eighth_expand_b=bwd_b.eighth_expand_b)
        pushed_a = dict(eighth_conv_b=eighth_of(conv_b), sum_expand_b=sum_of(expand_b))
        scratch_a = dict(
            plane_conv_b=Plane.scratch(conv_b.shape),
            line_expand_b=Line.scratch(bwd_b.eighth_expand_b.shape),
        )
    bwd_a = fused(
        functools.partial(backward_a, pixel_count, direct),
        BACKWARD_A_CID,
        ins=dict(mask=mask, norm_a3=fwd.norm_a3, norm_a2=norm_a2),
        staged=dict(
            gro_b=bwd_b.gro_b,
            w_reduce=w_reduce_b,
            **staged_a,
            e_b3=fwd.e_b3,
            slope_a=fwd.slope_a,
            u_a3=fwd.u_a3,
            middle=fwd.middle,
            w_expand=w_expand_a,
            u_a2=deformed,
            h2_a=fwd.h2_a,
        ),
        outs=dict(gd=array(*small), sums_a3=table(channels), sums_a2=table(inner_width)),
        pushed=dict(
            **pushed_a,
            gw_reduce=array(cuts, inner_width, channels // cuts),
            gw_expand=natural,
            e_a3=array(*big),
        ),
        scratch=dict(
            **scratch_a,
            ex3=Exchange.scratch(channels),
            ex2=Exchange.scratch(inner_width),
            wide=pltpu.VMEM(big, F32),
            grad=pltpu.VMEM(small, F32),
            turned=turned,
        ),
    )
    staged_s, scratch_s = {}, {}
    pushed_s = dict(gw_deform=array(1, 9 * inner_width, inner_width))
    if direct:
        reduce_b, expand_a = eighths(bwd_a.gw_reduce), eighths(bwd_a.gw_expand)
        deform = array(images_axis, 8, 9 * inner_width // images_axis // 8, inner_width)
        staged_s = dict(
            src_reduce_b=reduce_b,
            src_expand_a=expand_a,
            eighth_conv_b=bwd_a.eighth_conv_b,
        )
        pushed_s = dict(
            own_conv_b=own_of(conv_b),
            own_reduce_b=own_of(reduce_b),
            own_expand_a=own_of(expand_a),
            own_deform=own_of(deform),
        )
        scratch_s = dict(
            gw_deform=vmem(deform),
            line_conv_b=LineSum.scratch(bwd_a.eighth_conv_b.shape),
            plane_reduce_b=Plane.scratch(reduce_b.shape),
            plane_expand_a=LinePlane.scratch(expand_a.shape),
            plane_deform=Plane.scratch(deform.shape),
            eighth_reduce_b=vmem(eighth_of(reduce_b)),
            eighth_deform=vmem(eighth_of(deform)),
            line_reduce_b=LineSum.scratch(eighth_of(reduce_b).shape),
            line_deform=LineSum.scratch(eighth_of(deform).shape),
        )
    block = tile_pixels // 2
    bwd_s = fused(
        functools.partial(backward_s, pixel_count, direct),
        BACKWARD_S_CID,
        ins=dict(
            mask=mask,
            norm_a1=norm_a1,
            up=start.up,
            left=start.left,
            fr=start.fr,
            fc=start.fc,
        ),
        far=dict(samples=start.samples),
        staged=dict(
            gd=bwd_a.gd,
            **staged_s,
            w_deform=w_deform_a,
            rim=rim_flat,
            w_off=start.w_off,
            select=start.select,
            u_a1=start.u_a1,
        ),
        outs=dict(gr_a=array(*small), sums_a1=table(inner_width)),
        pushed=dict(**pushed_s, gw_off=array(cuts, 32, 9 * inner_width // cuts)),
        scratch=dict(
            **scratch_s,
            ex1=Exchange.scratch(inner_width),
            strips=Spill.scratch(1, tile_rows, tile_cols, inner_width) * images,
            spill=pltpu.VMEM((images, cells, inner_width), F32),
            table=pltpu.VMEM((WINDOW * win_cols, 3 * block), BF16),
            grads=pltpu.VMEM((inner_width, 3 * block), BF16),
            turned=turned,
            grad_row=pltpu.VMEM(taps_shape, F32),
            grad_col=pltpu.VMEM(taps_shape, F32),
            on_cells=pltpu.VMEM((288, cells), BF16),
            gw_off_sum=pltpu.VMEM((288, inner_width), F32),
            sample_slots=pltpu.VMEM((3, inner_width, pixels), BF16),
            sample_sems=pltpu.SemaphoreType.DMA((3,)),
            grad=pltpu.VMEM(small, F32),
        ),
    )
    staged_l, pushed_l, scratch_l = {}, {}, {}
    if direct:
        reduce_a = array(images_axis, 8, inner_width // 8, channels // cuts)
        staged_l = dict(
            own_deform=bwd_s.own_deform,
            gw_off=bwd_s.gw_off,
            own_conv_b=bwd_s.own_conv_b,
            own_reduce_b=bwd_s.own_reduce_b,
            own_expand_a=bwd_s.own_expand_a,
        )
        pushed_l = dict(
            sum_conv_b=sum_of(conv_b),
            sum_reduce_b=sum_of(reduce_b),
            sum_expand_a=sum_of(expand_a),
            sum_deform=sum_of(deform),
            sum_reduce_a=sum_of(reduce_a),
        )
        scratch_l = dict(
            gw_reduce=vmem(reduce_a),
            small=SmallSum.scratch(bwd_s.gw_off.shape),
            gather_conv_b=Gather.scratch(conv_b.shape),
            gather_reduce_b=Gather.scratch(reduce_b.shape),
            gather_expand_a=Gather.scratch(expand_a.shape),
            gather_deform=Gather.scratch(deform.shape),
            plane_reduce_a=Plane.scratch(reduce_a.shape),
            eighth_reduce_a=vmem(eighth_of(reduce_a)),
            line_reduce_a=Line.scratch(eighth_of(reduce_a).shape),
        )
        outs_l = dict(sum_off=array(*bwd_s.gw_off.shape[1:], dtype=F32))
    else:
        pushed_l = dict(gw_reduce=array(cuts, inner_width, channels // cuts))
        outs_l = {}
    end = fused(
        functools.partial(last, direct),
        LAST_CID,
        ins={},
        staged=dict(
            gr_a=bwd_s.gr_a, feature=feature, **staged_l, w_reduce=w_reduce_a, e_a3=bwd_a.e_a3
        ),
        outs=outs_l,
        pushed=dict(**pushed_l, grad_in=array(*big)),
        scratch=dict(**scratch_l, turned=turned),
    )
    sums_a = [bwd_s.sums_a1, bwd_a.sums_a2, bwd_a.sums_a3]
    sums_b = [bwd_b.sums_b1, bwd_b.sums_b2, fwd.sums_b3]
    norms_a = [norm_a1, norm_a2, fwd.norm_a3]
    norms_b = [fwd.norm_b1, fwd.norm_b2, fwd.norm_b3]
    if direct:
        sums = [
            end.sum_conv_b,
            end.sum_reduce_b,
            end.sum_reduce_a,
            bwd_a.sum_expand_b,
            end.sum_expand_a,
            end.sum_deform,
            end.sum_off,
        ]
    else:

        def over_devices(grad, dim):
            part = lax.psum_scatter(grad, IMG, scatter_dimension=dim, tiled=True)
            return lax.psum(part, (ROW, COL))

        turned_grads = (bwd_b.gw_conv, bwd_a.gw_reduce, end.gw_reduce)
        sums = [over_devices(g[0], 1) for g in turned_grads]
        sums += [over_devices(g[0], 0) for g in (bwd_b.gw_expand, bwd_a.gw_expand)]
        sums.append(over_devices(bwd_s.gw_deform[0], 0))
        sums = [g.reshape(8, -1, g.shape[1]) for g in sums]
        sums.append(over_devices(bwd_s.gw_off[0], 1).astype(F32))
    share = inner_width // images_axis
    long_share, wide_share = 9 * share, channels // images_axis
    shapes = [
        (long_share, inner_width),
        (wide_share, inner_width),
        (wide_share, inner_width),
        (share, channels),
        (share, channels),
        (long_share, inner_width),
        (18, long_share),
    ]
    vectors = ((2 * inner_width + channels) // 128, 128)
    shapes += [vectors] * 8
    operands = sums + sums_a + sums_b + norms_a + norms_b + [fwd.feature_out, end.grad_in]
    results = [array(*shape, dtype=F32) for shape in shapes]
    anywhere = pl.BlockSpec(memory_space=pl.ANY)
    results = pl.pallas_call(
        functools.partial(finish_kernel, unbias, len(operands)),
        out_shape=results + [array(*big)] * 2,
        in_specs=[anywhere] * len(operands),
        out_specs=[anywhere] * (len(shapes) + 2),
        scratch_shapes=[vmem(v) for v in operands + results]
        + [pltpu.SemaphoreType.DMA((len(operands),)), pltpu.SemaphoreType.DMA((17,))],
        compiler_params=pltpu.CompilerParams(vmem_limit_bytes=VMEM_LIMIT),
    )(*operands)
    conv_b, reduce_b, reduce_a, expand_b, expand_a, deform_a, offset_a = results[:7]
    scale_sums_a, shift_sums_a, scale_sums_b, shift_sums_b, mean_a, var_a, mean_b, var_b = (
        v.reshape(-1) for v in results[7:15]
    )
    return (
        results[15].reshape(feature_in.shape),
        results[16].reshape(feature_in.shape),
        reduce_a,
        offset_a.T,
        deform_a,
        expand_a,
        scale_sums_a,
        shift_sums_a,
        mean_a,
        var_a,
        reduce_b,
        conv_b,
        expand_b,
        scale_sums_b,
        shift_sums_b,
        mean_b,
        var_b,
    )


def solution(mesh):
    tiles = P(IMG, ROW, COL, None)
    in_specs = (tiles, P(IMG), tiles) + (P(),) * 11 + (tiles,)
    shares = P(IMG, None)
    out_specs = (tiles, tiles) + (shares,) * 4 + (P(),) * 4 + (shares,) * 3 + (P(),) * 4
    return jax.shard_map(body, mesh=mesh, in_specs=in_specs, out_specs=out_specs, check_vma=False)
```

```python
import functools
import types

import jax
import jax.numpy as jnp
import numpy as np
from jax import lax
from jax.experimental import pallas as pl
from jax.experimental.pallas import tpu as pltpu
from jax.sharding import PartitionSpec as P

LONG = 64
SHORT = 44
BOUND = 4
EPSILON = 1e-05
IMG, ROW, COL = "img", "row", "col"
MESH = pl.DeviceIdType.MESH
VMEM = pl.BlockSpec(memory_space=pltpu.VMEM)
VMEM_LIMIT = 60 * 1024 * 1024
F32 = jnp.float32
BF16 = jnp.bfloat16
REACH = BOUND + 3
PAD = 8
HALF = 16
FIRST_CID, FORWARD_CID, BACKWARD_B_CID, BACKWARD_A_CID, BACKWARD_S_CID, LAST_CID = range(6)


def group_of(axes):
    sizes = [lax.axis_size(a) for a in axes]
    total = int(np.prod(sizes))
    place = lax.axis_index(axes[0])
    for axis, size in zip(axes[1:], sizes[1:]):
        place = place * size + lax.axis_index(axis)

    def device(step):
        spot = lax.rem(place + step, total)
        coords = {}
        for axis, size in zip(reversed(axes), reversed(sizes)):
            coords[axis] = lax.rem(spot, size)
            spot = spot // size
        return coords

    return place, total, device


PLANE = (ROW, COL)
LINE = (IMG,)


def gather_start(axes, slots, send_sem, recv_sem):
    _, total, device = group_of(axes)
    for step in range(1, total):
        pltpu.make_async_remote_copy(
            src_ref=slots.at[0],
            dst_ref=slots.at[step],
            send_sem=send_sem,
            recv_sem=recv_sem,
            device_id=device(step),
            device_id_type=MESH,
        ).start()


def gather_wait(axes, slots, sem):
    _, total, _ = group_of(axes)
    others = slots.at[pl.ds(1, total - 1)]
    pltpu.make_async_copy(others, others, sem).wait()


def in_order(axes, slots):
    place, total, _ = group_of(axes)
    return [slots[lax.rem(place - spot + total, total)] for spot in range(total)]


def halo_peers():
    row, rows, col = lax.axis_index(ROW), lax.axis_size(ROW), lax.axis_index(COL)
    return row, rows, col, {COL: 1 - col}, {ROW: row - 1}, {ROW: row + 1}


BLOCK_ROWS = 8
SPAN = 17
WINDOW = 3 * BLOCK_ROWS


def tap_span(group, cols):
    first = 2 + 2 * group
    start = first * cols // 128 * 128
    stop = -(-(first + SPAN) * cols // 128) * 128
    return first, start, stop


def tap_weights(tap, block, cols, up_ref, left_ref, fr_ref, fc_ref, image=0, lanes=slice(None)):
    up, left, fr, fc = (
        ref[image, tap : tap + 1, lanes] for ref in (up_ref, left_ref, fr_ref, fc_ref)
    )
    up = up - block * BLOCK_ROWS
    pixels = up.shape[1]

    def pair(size, at, frac):
        ids = lax.broadcasted_iota(jnp.int32, (size, pixels), 0)
        first, second = ids == at, ids == at + 1
        value = jnp.where(first, 1.0 - frac, jnp.where(second, frac, 0.0))
        slope = jnp.where(second, 1.0, jnp.where(first, -1.0, 0.0))
        return value, slope

    return pair(WINDOW, up, fr) + pair(cols, left, fc)


def write_table(table, lane, row_w, col_w, group, cols):
    first, start, stop = tap_span(group, cols)
    pixels = row_w.shape[1]
    low = start // cols
    high = -(-stop // cols)
    for r in range(low, min(high, WINDOW)):
        table[r * cols : (r + 1) * cols, lane : lane + pixels] = (
            row_w[r : r + 1, :] * col_w
        ).astype(BF16)


def build_shifted(rim_ref, shifted):
    images, rows, cols, width = rim_ref.shape
    col = lax.axis_index(COL)
    tile = cols - HALF

    def fill(first):
        def one_row(k, carry):
            for n in range(images):
                line = rim_ref[n, k].astype(F32)
                none = jnp.zeros((2, width), F32)
                for d in range(3):
                    at = first + 2 * (d - 1)
                    if at < 0:
                        part = jnp.concatenate([none, line[: tile - 2]], axis=0)
                    elif at + tile > cols:
                        part = jnp.concatenate([line[at:], none], axis=0)
                    else:
                        part = line[at : at + tile]
                    shifted[n, k, :, d * width : (d + 1) * width] = part.astype(BF16)
            return carry

        lax.fori_loop(0, rows, one_row, 0)

    @pl.when(col == 0)
    def _():
        fill(0)

    @pl.when(col == 1)
    def _():
        fill(HALF)


def conv_product(shifted, w_ref, o_ref):
    images, rows, cols, width3 = shifted.shape
    tile_rows = rows - 4
    pixels = tile_rows * cols
    for n in range(images):
        total = None
        for i in range(3):
            taps = shifted[n, 2 * i : 2 * i + tile_rows].reshape(pixels, width3)
            term = jnp.dot(taps, w_ref[i * width3 : (i + 1) * width3, :], preferred_element_type=F32)
            total = term if total is None else total + term
        o_ref[n * pixels : (n + 1) * pixels, :] = total


def conv_weight_product(turned, shifted, gw_ref, i):
    images, rows, cols, width3 = shifted.shape
    tile_rows = rows - 4
    pixels = tile_rows * cols
    total = None
    for n in range(images):
        taps = shifted[n, 2 * i : 2 * i + tile_rows].reshape(pixels, width3)
        term = jnp.dot(turned[:, n * pixels : (n + 1) * pixels], taps, preferred_element_type=F32)
        total = term if total is None else total + term
    put_lanes(gw_ref, i * width3, total)


def unconv_product(shifted, w_ref, o_ref):
    images, rows, cols, width3 = shifted.shape
    width = width3 // 3
    tile_rows = rows - 4
    pixels = tile_rows * cols
    for n in range(images):
        total = None
        for tap in range(9):
            i, d = 2 - tap // 3, 2 - tap % 3
            grads = shifted[n, 2 * i : 2 * i + tile_rows, :, d * width : (d + 1) * width]
            term = lax.dot_general(
                grads.reshape(pixels, width),
                w_ref[tap * width : (tap + 1) * width, :],
                (((1,), (1,)), ((), ())),
                preferred_element_type=F32,
            )
            total = term if total is None else total + term
        o_ref[n * pixels : (n + 1) * pixels, :] = total


def halves(width):
    first = -(-width // 256) * 128
    return ((0, first), (first, width - first)) if first < width else ((0, width),)


def remote(src, dst, send, recv, device):
    return pltpu.make_async_remote_copy(
        src_ref=src, dst_ref=dst, send_sem=send, recv_sem=recv, device_id=device, device_id_type=MESH
    )


def arrival(ref, sem):
    return pltpu.make_async_copy(ref, ref, sem)


class Plane:
    @staticmethod
    def scratch(shape):
        images, _, rows, width = shape
        count = len(halves(width))
        return [
            pltpu.VMEM((images, 4, rows, width), BF16),
            pltpu.VMEM((images, 2, rows, width), BF16),
            pltpu.SemaphoreType.DMA((count, 3)),
            pltpu.SemaphoreType.DMA((count, 3)),
        ]

    def __init__(self, src, eighth, refs, part):
        half, quarter, send, recv = refs
        lanes = pl.ds(*halves(src.shape[-1])[part])
        self.src, self.half, self.quarter = (
            ref.at[:, :, :, lanes] for ref in (src, half, quarter)
        )
        self.eighth = eighth.at[:, :, lanes]
        self.images = src.shape[0]
        self.send, self.recv = [send.at[part, k] for k in range(3)], [recv.at[part, k] for k in range(3)]
        self.a, self.b, self.spot, self.first, self.second = self.peers(part == 0)
        col = lax.axis_index(COL)
        self.mine, self.pair, self.other = 4 * col, {COL: 1 - col}, 4 * (1 - col)

    @staticmethod
    def peers(x_first):
        row = lax.axis_index(ROW)
        x, y = lax.rem(row, 2), row // 2
        to_x, to_y = {ROW: row + 1 - 2 * x}, {ROW: row + 2 - 4 * y}
        if x_first:
            return x, y, lambda bit, free: bit + 2 * free, to_x, to_y
        return y, x, lambda bit, free: 2 * bit + free, to_y, to_x

    def steps(self):
        return [self.to_pair, self.to_first, self.to_second, self.done]

    def to_pair(self):
        src = self.src.at[:, pl.ds(self.other, 4)]
        remote(src, self.half, self.send[0], self.recv[0], self.pair).start()

    def to_first(self):
        arrival(self.half, self.recv[0]).wait()

        def add(i, carry):
            for s in range(4):
                self.half[i, s] = self.src[i, self.mine + s] + self.half[i, s]
            return carry

        lax.fori_loop(0, self.images, add, 0)
        for k in range(2):
            src = self.half.at[:, self.spot(1 - self.a, k)]
            remote(src, self.quarter.at[:, k], self.send[1], self.recv[1], self.first).start()

    def to_second(self):
        arrival(self.quarter, self.recv[1]).wait()

        def add(i, carry):
            for k in range(2):
                self.quarter[i, k] = self.half[i, self.spot(self.a, k)] + self.quarter[i, k]
            return carry

        lax.fori_loop(0, self.images, add, 0)
        src = self.quarter.at[:, 1 - self.b]
        remote(src, self.eighth, self.send[2], self.recv[2], self.second).start()

    def done(self):
        arrival(self.eighth, self.recv[2]).wait()

        def add(i, carry):
            self.eighth[i] = self.quarter[i, self.b] + self.eighth[i]
            return carry

        lax.fori_loop(0, self.images, add, 0)
        arrival(self.half, self.send[0]).wait()
        arrival(self.quarter, self.send[1]).wait()
        arrival(self.eighth, self.send[2]).wait()


class LinePlane:
    @staticmethod
    def scratch(shape):
        images, _, rows, width = shape
        sems = pltpu.SemaphoreType.DMA((len(halves(width)), 4))
        return [
            pltpu.VMEM((images, 4, rows, width), BF16),
            pltpu.VMEM((images, 4, rows, width), BF16),
            pltpu.VMEM((2, rows, width), BF16),
            pltpu.VMEM((rows, width), BF16),
            sems,
            sems,
        ]

    def __init__(self, src, own, refs, part):
        half, line, quarter, eighth, send, recv = refs
        lanes = pl.ds(*halves(src.shape[-1])[part])
        self.src, self.half, self.line = (ref.at[:, :, :, lanes] for ref in (src, half, line))
        self.quarter = quarter.at[:, :, lanes]
        self.eighth, self.own = eighth.at[:, lanes], own.at[:, lanes]
        self.images, self.img = src.shape[0], lax.axis_index(IMG)
        self.send, self.recv = [send.at[part, k] for k in range(4)], [recv.at[part, k] for k in range(4)]
        self.plane = Plane.peers(part == 0)
        col = lax.axis_index(COL)
        self.mine, self.pair, self.other = 4 * col, {COL: 1 - col}, 4 * (1 - col)

    def steps(self):
        return [self.to_pair, self.to_line, self.to_first, self.to_second, self.done]

    def to_pair(self):
        src = self.src.at[:, pl.ds(self.other, 4)]
        remote(src, self.half, self.send[0], self.recv[0], self.pair).start()

    def to_line(self):
        arrival(self.half, self.recv[0]).wait()

        def add(i, carry):
            for s in range(4):
                self.half[i, s] = self.src[i, self.mine + s] + self.half[i, s]
            return carry

        lax.fori_loop(0, self.images, add, 0)
        for j in range(1, self.images):
            there = lax.rem(self.img + j, self.images)
            src = self.half.at[there]
            remote(src, self.line.at[j], self.send[1], self.recv[1], {IMG: there}).start()

    def to_first(self):
        arrival(self.line.at[pl.ds(1, self.images - 1)], self.recv[1]).wait()
        for s in range(4):
            total = self.half[self.img, s].astype(F32)
            for j in range(1, self.images):
                total = total + self.line[j, s].astype(F32)
            self.line[0, s] = total.astype(BF16)
        a, _, spot, first, _ = self.plane
        for k in range(2):
            src = self.line.at[0, spot(1 - a, k)]
            remote(src, self.quarter.at[k], self.send[2], self.recv[2], first).start()

    def to_second(self):
        a, b, spot, _, second = self.plane
        arrival(self.quarter, self.recv[2]).wait()
        for k in range(2):
            self.quarter[k] = self.line[0, spot(a, k)] + self.quarter[k]
        remote(self.quarter.at[1 - b], self.eighth, self.send[3], self.recv[3], second).start()

    def done(self):
        _, b, _, _, _ = self.plane
        arrival(self.eighth, self.recv[3]).wait()
        self.own[...] = self.quarter[b] + self.eighth[...]
        arrival(self.half, self.send[0]).wait()
        arrival(self.line.at[pl.ds(1, self.images - 1)], self.send[1]).wait()
        arrival(self.quarter, self.send[2]).wait()
        arrival(self.eighth, self.send[3]).wait()


class LineSum:
    @staticmethod
    def scratch(shape):
        sems = pltpu.SemaphoreType.DMA((len(halves(shape[-1])),))
        return [pltpu.VMEM(shape, BF16), sems, sems]

    def __init__(self, eighth, own, refs, part):
        line, send, recv = refs
        lanes = pl.ds(*halves(eighth.shape[-1])[part])
        self.eighth, self.line, self.own = eighth.at[:, :, lanes], line.at[:, :, lanes], own.at[:, lanes]
        self.images, self.img = eighth.shape[0], lax.axis_index(IMG)
        self.send, self.recv = send.at[part], recv.at[part]

    def steps(self):
        return [self.to_line, self.done]

    def to_line(self):
        for j in range(1, self.images):
            there = lax.rem(self.img + j, self.images)
            src = self.eighth.at[there]
            remote(src, self.line.at[j], self.send, self.recv, {IMG: there}).start()

    def done(self):
        arrived = self.line.at[pl.ds(1, self.images - 1)]
        arrival(arrived, self.recv).wait()
        total = self.eighth[self.img].astype(F32)
        for j in range(1, self.images):
            total = total + self.line[j].astype(F32)
        self.own[...] = total.astype(BF16)
        arrival(arrived, self.send).wait()


class Gather:
    @staticmethod
    def scratch(shape):
        sems = pltpu.SemaphoreType.DMA((len(halves(shape[-1])), 2))
        return [sems, sems]

    def __init__(self, own, out, refs, part):
        send, recv = refs
        lanes = pl.ds(*halves(out.shape[-1])[part])
        self.own, self.out = own.at[:, lanes], out.at[:, :, lanes]
        self.send, self.recv = [send.at[part, k] for k in range(2)], [recv.at[part, k] for k in range(2)]
        self.row, col = lax.axis_index(ROW), lax.axis_index(COL)
        self.mine, self.pair = 4 * col, {COL: 1 - col}

    def steps(self):
        return [self.to_rows, self.to_pair, self.done]

    def to_rows(self):
        spot = self.out.at[self.mine + self.row]
        self.out[self.mine + self.row] = self.own[...]
        for j in range(1, 4):
            there = lax.rem(self.row + j, 4)
            remote(spot, spot, self.send[0], self.recv[0], {ROW: there}).start()

    def to_pair(self):
        arrival(self.out.at[pl.ds(0, 3)], self.recv[0]).wait()
        four = self.out.at[pl.ds(self.mine, 4)]
        remote(four, four, self.send[1], self.recv[1], self.pair).start()

    def done(self):
        four = self.out.at[pl.ds(0, 4)]
        arrival(four, self.recv[1]).wait()
        arrival(self.out.at[pl.ds(0, 3)], self.send[0]).wait()
        arrival(four, self.send[1]).wait()


class Line:
    @staticmethod
    def scratch(shape):
        return [pltpu.VMEM(shape[1:], BF16)] + LineSum.scratch(shape) + Gather.scratch(shape)

    def __init__(self, eighth, out, refs, part):
        own = refs[0]
        self.sum = LineSum(eighth, own, refs[1:4], part)
        self.gather = Gather(own, out, refs[4:], part)

    def steps(self):
        return [self.sum.to_line, self.to_rows, self.gather.to_pair, self.gather.done]

    def to_rows(self):
        self.sum.done()
        self.gather.to_rows()


class SmallSum:
    @staticmethod
    def scratch(shape):
        sizes = [lax.axis_size(IMG), lax.axis_size(ROW) * lax.axis_size(COL)]
        return [pltpu.VMEM((size,) + shape[1:], BF16) for size in sizes] + [
            pltpu.SemaphoreType.DMA((2,)),
            pltpu.SemaphoreType.DMA((2,)),
        ]

    def __init__(self, src, out, refs):
        self.src, self.out = src, out
        self.slots1, self.slots2, self.send, self.recv = refs

    def steps(self):
        return [self.to_line, self.to_plane, self.done]

    def to_line(self):
        here, total, _ = group_of(LINE)
        self.slots1[0] = self.src[here]
        for j in range(1, total):
            there = lax.rem(here + j, total)
            remote(
                self.src.at[there], self.slots1.at[j], self.send.at[0], self.recv.at[0], {IMG: there}
            ).start()

    def to_plane(self):
        gather_wait(LINE, self.slots1, self.recv.at[0])
        total = added([p.astype(F32) for p in in_order(LINE, self.slots1)])
        self.slots2[0] = total.astype(BF16)
        gather_start(PLANE, self.slots2, self.send.at[1], self.recv.at[1])

    def done(self):
        gather_wait(PLANE, self.slots2, self.recv.at[1])
        self.out[...] = added([p.astype(F32) for p in in_order(PLANE, self.slots2)])
        gather_wait(LINE, self.slots1, self.send.at[0])
        gather_wait(PLANE, self.slots2, self.send.at[1])


class Jobs:
    def __init__(self):
        self.queue = []

    def add(self, *jobs):
        lists = [job.steps() for job in jobs]
        for k in range(max(len(steps) for steps in lists)):
            self.queue += [steps[k] for steps in lists if k < len(steps)]

    def tick(self, count=1):
        for _ in range(min(count, len(self.queue))):
            self.queue.pop(0)()

    def finish(self):
        self.tick(len(self.queue))


def plane_jobs(src, eighth, refs):
    return [Plane(src, eighth, refs, part) for part in range(len(halves(src.shape[-1])))]


def part_jobs(kind, first, second, refs):
    return [kind(first, second, refs, part) for part in range(len(halves(first.shape[-1])))]


def line_jobs(eighth, out, refs):
    return [Line(eighth, out, refs, part) for part in range(len(halves(out.shape[-1])))]


STEP = 32
PIECE = 256
CHUNK = 256


class Refs:
    FLYING = 6 * 1024 * 1024

    def __init__(self):
        self.loads, self.stores, self.queue, self.flying = {}, {}, [], {}

    def load(self, ref, copy):
        self.loads[id(ref)] = copy
        self.queue.append((id(ref), int(np.prod(ref.shape)) * ref.dtype.itemsize))

    def start_loads(self, until=None):
        while self.queue:
            if until is None and sum(self.flying.values()) >= self.FLYING:
                return
            if until is not None and until in self.flying:
                return
            key, size = self.queue.pop(0)
            self.loads[key].start()
            self.flying[key] = size

    def ready(self, *refs):
        for ref in refs:
            self.start_loads(id(ref))
            self.loads.pop(id(ref)).wait()
            self.flying.pop(id(ref))
            self.start_loads()

    def push(self, *refs):
        for ref in refs:
            self.stores[id(ref)].start()

    def pushed(self, *refs):
        for ref in refs:
            self.stores.pop(id(ref)).wait()

    def flush(self):
        for copy in self.stores.values():
            copy.wait()


def fused(work, cid, ins, staged, outs, pushed, scratch, smem={}, far={}, far_outs={}):
    loaded, stored = {**ins, **staged}, {**outs, **pushed}
    sizes = (len(loaded), len(stored))

    def kernel(*refs):
        r = Refs()
        refs = list(refs)

        def take(count):
            taken = refs[:count]
            del refs[:count]
            return taken

        for key, ref in zip((*smem, *far), take(len(smem) + len(far))):
            setattr(r, key, ref)
        in_raw, out_raw = (take(count) for count in sizes)
        for key, ref in zip(far_outs, take(len(far_outs))):
            setattr(r, key, ref)
        for key, shape in scratch.items():
            setattr(r, key, take(len(shape)) if isinstance(shape, list) else take(1)[0])
        in_bufs, out_bufs = (take(count) for count in sizes)
        in_sems, out_sems = take(2)
        for keys, bufs in ((loaded, in_bufs), (stored, out_bufs)):
            for key, buf in zip(keys, bufs):
                setattr(r, key, buf)
        for k, (raw, buf) in enumerate(zip(in_raw, in_bufs)):
            r.load(buf, pltpu.make_async_copy(raw, buf, in_sems.at[k]))
        for k, (raw, buf) in enumerate(zip(out_raw, out_bufs)):
            r.stores[id(buf)] = pltpu.make_async_copy(buf, raw, out_sems.at[k])
        r.start_loads()
        signal_all()
        r.ready(*in_bufs[: len(ins)])
        work(r)
        r.push(*out_bufs[: len(outs)])
        r.flush()

    flat = []
    for shape in scratch.values():
        flat += shape if isinstance(shape, list) else [shape]
    flat += [pltpu.VMEM(a.shape, a.dtype) for a in (*loaded.values(), *stored.values())]
    flat += [pltpu.SemaphoreType.DMA((count,)) for count in sizes]
    anywhere, scalars = pl.BlockSpec(memory_space=pl.ANY), pl.BlockSpec(memory_space=pltpu.SMEM)
    result = pl.pallas_call(
        kernel,
        out_shape=[*stored.values(), *far_outs.values()],
        in_specs=[scalars] * len(smem) + [anywhere] * (len(far) + sizes[0]),
        out_specs=[anywhere] * (sizes[1] + len(far_outs)),
        scratch_shapes=flat,
        compiler_params=pltpu.CompilerParams(
            collective_id=cid, has_side_effects=True, vmem_limit_bytes=VMEM_LIMIT
        ),
    )(*smem.values(), *far.values(), *loaded.values())
    return types.SimpleNamespace(**dict(zip((*stored, *far_outs), result)))


def signal_all():
    barrier = pltpu.get_barrier_semaphore()
    for axes in (PLANE, LINE):
        _, total, device = group_of(axes)
        for step in range(1, total):
            pl.semaphore_signal(barrier, inc=1, device_id=device(step), device_id_type=MESH)


def wait_all():
    count = sum(group_of(axes)[1] - 1 for axes in (PLANE, LINE))
    pl.semaphore_wait(pltpu.get_barrier_semaphore(), count)


def added(parts):
    return functools.reduce(lambda a, b: a + b, parts)


class Exchange:
    @staticmethod
    def scratch(width):
        rows = 2 * width // 128
        sizes = [int(np.prod([lax.axis_size(a) for a in axes])) for axes in (PLANE, LINE)]
        return [
            pltpu.VMEM((sizes[0], rows, 128), F32),
            pltpu.VMEM((sizes[1], rows, 128), F32),
            pltpu.VMEM((rows, 128), F32),
            pltpu.SemaphoreType.DMA((2,)),
            pltpu.SemaphoreType.DMA((2,)),
        ]

    def __init__(self, refs):
        self.slots1, self.slots2, self.out, self.send, self.recv = refs
        self.half = self.out.shape[0] // 2

    def put(self, first, second):
        for k in range(self.half):
            self.slots1[0, k : k + 1, :] = first[:, 128 * k : 128 * (k + 1)]
            self.slots1[0, self.half + k : self.half + k + 1, :] = second[:, 128 * k : 128 * (k + 1)]
        gather_start(PLANE, self.slots1, self.send.at[0], self.recv.at[0])

    def line(self):
        gather_start(LINE, self.slots2, self.send.at[1], self.recv.at[1])

    def middle_sums(self):
        gather_wait(PLANE, self.slots1, self.recv.at[0])
        self.slots2[0] = added(in_order(PLANE, self.slots1))
        self.line()

    def finish_sums(self):
        gather_wait(LINE, self.slots2, self.recv.at[1])
        self.out[...] = added(in_order(LINE, self.slots2))
        self.drain()

    def middle_stats(self, count_ref, plane_count):
        half = self.half
        gather_wait(PLANE, self.slots1, self.recv.at[0])
        parts = in_order(PLANE, self.slots1)
        total = added([p[:half] for p in parts])
        center = total / plane_count
        spread = added([p[half:] for p in parts])
        for spot, part in enumerate(parts):
            count = count_ref[spot : spot + 1, :]
            away = part[:half] / jnp.maximum(count, 1.0) - center
            spread = spread + count * (away * away)
        self.slots2[0, :half] = total
        self.slots2[0, half:] = spread
        self.line()

    def finish_stats(self, plane_count):
        half = self.half
        total_count = plane_count * lax.axis_size(IMG)
        gather_wait(LINE, self.slots2, self.recv.at[1])
        parts = in_order(LINE, self.slots2)
        center = added([p[:half] for p in parts]) / total_count
        spread = added([p[half:] for p in parts])
        for part in parts:
            away = part[:half] / plane_count - center
            spread = spread + plane_count * (away * away)
        self.out[:half] = center
        self.out[half:] = spread / total_count
        self.drain()

    def drain(self):
        gather_wait(PLANE, self.slots1, self.send.at[0])
        gather_wait(LINE, self.slots2, self.send.at[1])

    def rows(self):
        out = self.out[...]
        first = [out[k : k + 1] for k in range(self.half)]
        second = [out[self.half + k : self.half + k + 1] for k in range(self.half)]
        return jnp.concatenate(first, axis=1), jnp.concatenate(second, axis=1)


class Halo:
    scratch = [pltpu.SemaphoreType.DMA((5,)), pltpu.SemaphoreType.DMA((5,))]

    def __init__(self, pad, reach, tile, window, sems, image=None):
        if image is not None:
            tile, window = (ref.at[pl.ds(image, 1)] for ref in (tile, window))
        self.row, self.rows, col, pair, above, below = halo_peers()
        self.pad, self.reach, self.tile, self.window = pad, reach, tile, window
        self.tile_rows, self.tile_cols = tile.shape[1], tile.shape[2]
        self.own = own = pl.ds(pl.multiple_of(HALF * col, HALF), self.tile_cols)
        spot = pl.ds(pl.multiple_of(2 * HALF * col, HALF), HALF)
        side = pl.ds(pl.multiple_of(HALF * (1 - col), HALF), HALF)
        mid = pl.ds(HALF, HALF)
        upper = pl.ds(pad - reach, reach)
        lower = pl.ds(pad + self.tile_rows, reach)
        send, recv = sems

        def copy(src, dst, k, device):
            return pltpu.make_async_remote_copy(
                src_ref=src,
                dst_ref=dst,
                send_sem=send.at[k],
                recv_sem=recv.at[k],
                device_id=device,
                device_id_type=MESH,
            )

        w = window
        self.to_pair = copy(
            tile.at[:, :, side], w.at[:, pl.ds(pad, self.tile_rows), spot], 0, pair
        )
        self.up = copy(tile.at[:, pl.ds(0, reach)], w.at[:, lower, own], 1, above)
        self.down = copy(
            tile.at[:, pl.ds(self.tile_rows - reach, reach)], w.at[:, upper, own], 2, below
        )
        self.from_below = copy(w.at[:, lower, mid], w.at[:, lower, spot], 3, pair)
        self.from_above = copy(w.at[:, upper, mid], w.at[:, upper, spot], 4, pair)

    def blank(self):
        window, pad, reach, tile_rows = self.window, self.pad, self.reach, self.tile_rows
        zero = jnp.zeros((window.shape[0],) + window.shape[2:], window.dtype)

        def fill(first, last):
            for k in range(first, last):
                window[:, k] = zero

        fill(0, pad - reach)
        fill(pad + tile_rows + reach, 2 * pad + tile_rows)

        @pl.when(self.row == 0)
        def _():
            fill(pad - reach, pad)

        @pl.when(self.row == self.rows - 1)
        def _():
            fill(pad + tile_rows, pad + tile_rows + reach)

    def start(self):
        @pl.when(self.row > 0)
        def _():
            self.up.start()

        @pl.when(self.row < self.rows - 1)
        def _():
            self.down.start()

        self.to_pair.start()
        for n in range(self.tile.shape[0]):
            self.window[n, pl.ds(self.pad, self.tile_rows), self.own, :] = self.tile[n]

    def middle(self):
        @pl.when(self.row < self.rows - 1)
        def _():
            self.up.wait_recv()
            self.from_below.start()

        @pl.when(self.row > 0)
        def _():
            self.down.wait_recv()
            self.from_above.start()

    def finish(self):
        self.to_pair.wait()

        @pl.when(self.row < self.rows - 1)
        def _():
            self.down.wait_send()
            self.from_below.wait()

        @pl.when(self.row > 0)
        def _():
            self.up.wait_send()
            self.from_above.wait()


def gauss(x):
    bell = jnp.exp2(x * (x * -0.7213475204444817))
    d = 1.0 + (0.3275911 * 0.7071067811865476) * jnp.abs(x)
    t = pl.reciprocal(d, approx=True)
    t = t * (2.0 - d * t)
    poly = 0.5307027145 * t - 0.7265760135
    poly = poly * t + 0.7107068705
    poly = poly * t - 0.142248368
    poly = poly * t + 0.127414796
    tail = poly * (t * bell)
    return jnp.where(x < 0, tail, 1.0 - tail), bell * 0.3989422804014327


def wide(mask, width):
    return jnp.concatenate([mask] * (width // 128), axis=1)


def place(ref, i, lanes):
    if len(ref.shape) == 4:
        return (i // ref.shape[1], lax.rem(i, ref.shape[1]), slice(None), lanes)
    return (pl.ds(pl.multiple_of(i * STEP, STEP), STEP), lanes)


def by_rows(pixels, width, work, sums=0):
    pieces = [slice(l, l + PIECE) for l in range(0, width, PIECE)]

    def one(i, carry):
        out = []
        for k, lanes in enumerate(pieces):
            got = work(i, lanes)
            for j in range(sums):
                folded = jnp.sum(got[j].reshape(STEP // 8, 8, PIECE), axis=0)
                out.append(carry[k * sums + j] + folded)
        return tuple(out)

    start = tuple(jnp.zeros((8, PIECE), F32) for _ in range(sums * len(pieces)))
    final = lax.fori_loop(0, pixels // STEP, one, start)
    rows = []
    for j in range(sums):
        parts = [jnp.sum(final[k * sums + j], axis=0, keepdims=True) for k in range(len(pieces))]
        rows.append(jnp.concatenate(parts, axis=1))
    return rows


NORM_ROWS = 8


def norm_table(exchange, gain_ref, shift_ref, out_ref, first):
    mean, var = exchange.rows()
    lanes = slice(first, first + mean.shape[1])
    inv = lax.rsqrt(var + EPSILON)
    out_ref[...] = jnp.zeros_like(out_ref)
    out_ref[0:1, :] = mean
    out_ref[1:2, :] = inv
    out_ref[2:3, :] = inv * gain_ref[:, lanes]
    out_ref[3:4, :] = shift_ref[:, lanes]
    out_ref[4:5, :] = var


def normed(u_ref, norm, i, lanes):
    away = u_ref[place(u_ref, i, lanes)].astype(F32) - norm[0:1, lanes]
    return away * norm[2:3, lanes] + norm[3:4, lanes], away


def activate(u_ref, norm, mask, h_ref, residual=None, slope=None, keep=None):
    def work(i, lanes):
        x, _ = normed(u_ref, norm, i, lanes)
        if residual is not None:
            x = x + residual[place(residual, i, lanes)].astype(F32)
        below, bell = gauss(x)
        m = wide(mask[place(mask, i, slice(None))], PIECE)
        h_ref[place(h_ref, i, lanes)] = (x * below * m).astype(BF16)
        if slope is not None:
            slope[place(slope, i, lanes)] = ((below + x * bell) * m).astype(BF16)
        if keep is not None:
            keep[place(keep, i, lanes)] = u_ref[place(u_ref, i, lanes)].astype(BF16)

    by_rows(mask.shape[0], norm.shape[1], work)


def device_stats(u_ref, mask, count):
    pixels, width = u_ref.shape

    def total_of(i, lanes):
        m = wide(mask[place(mask, i, slice(None))], PIECE)
        return (u_ref[place(u_ref, i, lanes)] * m,)

    (total,) = by_rows(pixels, width, total_of, 1)
    center = total / jnp.maximum(wide(count, width), 1.0)

    def spread_of(i, lanes):
        m = wide(mask[place(mask, i, slice(None))], PIECE)
        away = u_ref[place(u_ref, i, lanes)] - center[:, lanes]
        return (away * away * m,)

    (spread,) = by_rows(pixels, width, spread_of, 1)
    return total, spread


def product(a_ref, w_ref, o_ref, turned=False):
    dims = (((1,), (1 if turned else 0,)), ((), ()))

    def one(i, carry):
        rows = pl.ds(pl.multiple_of(i * CHUNK, CHUNK), CHUNK)
        o_ref[rows, :] = lax.dot_general(
            a_ref[rows, :], w_ref[...], dims, preferred_element_type=F32
        )
        return carry

    lax.fori_loop(0, a_ref.shape[0] // CHUNK, one, 0)


def turn(a_ref, t_ref):
    def one(i, carry):
        rows = pl.ds(pl.multiple_of(i * CHUNK, CHUNK), CHUNK)
        t_ref[:, rows] = a_ref[rows, :].T
        return carry

    lax.fori_loop(0, a_ref.shape[0] // CHUNK, one, 0)


def put_lanes(ref, first, value):
    width = ref.shape[-1]
    at, stop = first, first + value.shape[1]
    while at < stop:
        cut = at // width
        until = min(stop, (cut + 1) * width)
        part = value[:, at - first : until - first].astype(ref.dtype)
        lanes = slice(at - cut * width, until - cut * width)
        if len(ref.shape) == 4:
            ref[cut, :, :, lanes] = part.reshape(ref.shape[1:3] + part.shape[1:])
        else:
            ref[cut, :, lanes] = part
        at = until


def weight_product(t_ref, b_ref, gw_ref):
    channels = b_ref.shape[1]
    for first in range(0, channels, 512):
        value = jnp.dot(t_ref[...], b_ref[:, first : first + 512], preferred_element_type=F32)
        if len(gw_ref.shape) == 4 and gw_ref.shape[-1] == channels:
            part = value.astype(gw_ref.dtype).reshape(gw_ref.shape[:3] + (512,))
            gw_ref[:, :, :, first : first + 512] = part
        else:
            put_lanes(gw_ref, first, value)


def put_rows(ref, first, value):
    if len(ref.shape) == 3:
        ref[0, first : first + value.shape[0], :] = value.astype(ref.dtype)
        return
    rows = ref.shape[2]
    at, stop = first, first + value.shape[0]
    while at < stop:
        eighth = at // rows
        until = min(stop, (eighth + 1) * rows)
        low, high = at - eighth * rows, until - eighth * rows
        part = value[at - first : until - first].astype(ref.dtype)
        ref[eighth // 8, eighth % 8, low:high, :] = part
        at = until


def norm_back(e_ref, u_ref, norm, sums, pixel_count, mask, out_ref):
    sum_grad, sum_unit = (s * (1.0 / pixel_count) for s in sums)

    def work(i, lanes):
        away = u_ref[place(u_ref, i, lanes)].astype(F32) - norm[0:1, lanes]
        unit = away * norm[1:2, lanes]
        e = e_ref[place(e_ref, i, lanes)].astype(F32)
        m = wide(mask[place(mask, i, slice(None))], PIECE)
        grad = norm[2:3, lanes] * (e - sum_grad[:, lanes] - unit * sum_unit[:, lanes]) * m
        out_ref[place(out_ref, i, lanes)] = grad.astype(BF16)

    by_rows(mask.shape[0], norm.shape[1], work)


def gelu_grad(e_ref, u_ref, norm, mask):
    def work(i, lanes):
        x, away = normed(u_ref, norm, i, lanes)
        below, bell = gauss(x)
        m = wide(mask[place(mask, i, slice(None))], PIECE)
        e = e_ref[place(e_ref, i, lanes)] * (below + x * bell) * m
        e_ref[place(e_ref, i, lanes)] = e
        return e, e * (away * norm[1:2, lanes])

    return by_rows(mask.shape[0], norm.shape[1], work, 2)


def put_sums(exchange, out_ref):
    first, second = exchange.rows()
    out_ref[...] = jnp.zeros_like(out_ref)
    out_ref[0:1, :] = first
    out_ref[1:2, :] = second
    return first, second


def order_taps(rows, width):
    to = lax.broadcasted_iota(jnp.int32, (rows, width), 0)
    at = lax.broadcasted_iota(jnp.int32, (rows, width), 1)
    picked = jnp.where(to < 16, 2 * to, 2 * (to - 16) + 1)
    real = lax.rem(to, 16) < 9
    return jnp.where(jnp.logical_and(at == picked, real), 1.0, 0.0)


def make_mask(r, tile_cols):
    row, col = lax.axis_index(ROW), lax.axis_index(COL)
    rows, cols = lax.axis_size(ROW), lax.axis_size(COL)
    images = r.orientation.shape[0]
    tile_rows = r.mask.shape[0] // images // tile_cols
    tall = [r.orientation[n].astype(F32) for n in range(images)]
    for n in range(images):

        def fill(i, carry, n=n):
            column = lax.broadcasted_iota(jnp.int32, (tile_cols, 128), 0) + col * tile_cols
            portrait = jnp.where(column < SHORT, 1.0, 0.0)
            line = jnp.zeros((tile_cols, 128), jnp.int32) + (row * tile_rows + i)
            landscape = jnp.where(line < SHORT, 1.0, 0.0)
            at = (n * tile_rows + i) * tile_cols
            r.mask[pl.ds(pl.multiple_of(at, tile_cols), tile_cols), :] = (
                landscape * (1.0 - tall[n]) + portrait * tall[n]
            )
            return carry

        lax.fori_loop(0, tile_rows, fill, 0)

    def count(row, col):
        return (
            jnp.clip(SHORT - row * tile_rows, 0, tile_rows) * tile_cols,
            jnp.clip(SHORT - col * tile_cols, 0, tile_cols) * tile_rows,
        )

    def fill_count(at, row, col):
        flat, upright = (c.astype(F32) for c in count(row, col))
        total = added([flat * (1.0 - t) + upright * t for t in tall])
        r.counts[at : at + 1, :] = jnp.zeros((1, 128), F32) + total

    r.counts[...] = jnp.zeros_like(r.counts)
    for k in range(rows * cols):
        fill_count(k, jnp.int32(k // cols), jnp.int32(k % cols))
    fill_count(8, row, col)


def make_corners(r, cols):
    images, _, pixels = r.up.shape
    tile_cols = cols - HALF
    order = order_taps(32, r.base.shape[1]).astype(BF16)
    tap = lax.broadcasted_iota(jnp.int32, (16, pixels), 0)
    pixel = lax.broadcasted_iota(jnp.int32, (16, pixels), 1)
    up0 = pixel // tile_cols + PAD + 2 * (tap // 3 - 1)
    left0 = lax.rem(pixel, tile_cols) + HALF * lax.axis_index(COL) + 2 * (lax.rem(tap, 3) - 1)
    for n in range(images):
        base = r.base[n * pixels : (n + 1) * pixels, :].astype(F32).astype(BF16)
        moved = lax.dot_general(
            order, base, (((1,), (1,)), ((), ())), preferred_element_type=F32
        ).astype(jnp.int32)
        r.up[n] = moved[:16] + up0
        r.left[n] = moved[16:] + left0


def first(plane_count, r):
    ex, ex2 = Exchange(r.ex1), Exchange(r.ex2)
    images, all_rows, cols, width = r.rim.shape
    halos = [Halo(PAD, REACH, r.tile, r.rim, r.halo[2 * n : 2 * n + 2], n) for n in range(images)]
    make_mask(r, cols - HALF)
    r.ready(r.feature, r.w_reduce)
    product(r.feature, r.w_reduce, r.u_a1)
    r.push(r.u_a1)
    total, spread = device_stats(r.u_a1, r.mask, r.counts[8:9, :])
    wait_all()
    ex.put(total, spread)
    make_corners(r, cols)
    ex.middle_stats(r.counts, plane_count)
    for halo in halos:
        halo.blank()
    order = order_taps(32, r.w_offset.shape[0]).astype(BF16)
    for tap in range(9):
        columns = r.w_offset[:, tap * width : (tap + 1) * width]
        r.w_off[32 * tap : 32 * tap + 32, :] = jnp.dot(
            order, columns, preferred_element_type=F32
        ).astype(BF16)
    ex.finish_stats(plane_count)
    norm_table(ex, r.scale, r.shift, r.norm_a1, 0)
    activate(r.u_a1, r.norm_a1, r.mask, r.tile)
    for halo in halos:
        halo.start()
    select_cells(r, cols)
    r.push(r.select)
    r.ready(r.w_deform)
    turn(r.w_deform, r.w_turned)
    for n, halo in enumerate(halos):
        if n == 0:
            halo.middle()
        halo.finish()
        for k in range(0, all_rows, 8):
            lines = r.rim[n, k : k + 8].reshape(8 * cols, width)
            r.rim_t[n, :, k * cols : (k + 8) * cols] = lines.T
        offset_fractions(r, cols, n)
        sample_units(r, cols, n, 0)
        if n + 1 < images:
            halos[n + 1].middle()
        sample_units(r, cols, n, 1)
    r.push(r.rim, r.fr, r.fc, r.samples, r.u_a2)
    total, spread = device_stats(r.u_a2, r.mask, r.counts[8:9, :])
    ex2.put(total, spread)
    ex2.middle_stats(r.counts, plane_count)
    ex2.finish_stats(plane_count)
    norm_table(ex2, r.scale, r.shift, r.norm_a2, width)


def offset_fractions(r, cols, n):
    _, width, cells = r.rim_t.shape
    column = lax.rem(lax.broadcasted_iota(jnp.int32, (32, cells), 1), cols)
    r.spread[...] = jnp.dot(r.w_off[...], r.rim_t[n], preferred_element_type=F32)
    total = None
    for tap in range(9):
        i, j = 2 * (tap // 3 - 1), 2 * (tap % 3 - 1)
        term = r.spread[32 * tap : 32 * tap + 32, :]
        shift = -(i * cols + j) % cells
        if shift:
            term = pltpu.roll(term, shift, axis=1)
        if j < 0:
            term = jnp.where(column >= -j, term, 0.0)
        if j > 0:
            term = jnp.where(column < cols - j, term, 0.0)
        total = term if total is None else total + term
    parts = []
    for _ in range(3):
        parts.append(total.astype(BF16))
        total = total - parts[-1].astype(F32)
    on_tile = lax.dot_general(
        jnp.concatenate(parts, axis=0),
        r.select[...],
        (((1,), (1,)), ((), ())),
        preferred_element_type=F32,
    )
    offsets = on_tile[:32] + on_tile[32:64] + on_tile[64:]
    fraction = 1.0 / (1.0 + jnp.exp(-offsets))
    r.fr[n] = fraction[:16]
    r.fc[n] = fraction[16:]


def sample_units(r, cols, n, b):
    block = r.table.shape[1]
    width = r.rim_t.shape[1]
    lanes = slice(b * block, (b + 1) * block)
    mine = slice((2 * n + b) * block, (2 * n + b + 1) * block)
    base = b * (BLOCK_ROWS * cols)
    for tap in range(9):
        row_w, _, col_w, _ = tap_weights(tap, b, cols, r.up, r.left, r.fr, r.fc, n, lanes)
        write_table(r.table, 0, row_w, col_w, tap // 3, cols)
        _, start, stop = tap_span(tap // 3, cols)
        cells = r.rim_t[n, :, base + start : base + stop]
        value = jnp.dot(cells, r.table[start:stop, :], preferred_element_type=F32)
        r.samples[tap * width : (tap + 1) * width, mine] = value.astype(BF16)
    deformed = jnp.dot(r.w_turned[...], r.samples[:, mine], preferred_element_type=F32)
    r.u_a2[mine, :] = deformed.T


def finish_kernel(unbias, count, *refs):
    ins, outs, rest = refs[:count], refs[count : count + 17], refs[count + 17 :]
    bufs, out_bufs, sems, out_sems = rest[:count], rest[count : count + 15], rest[-2], rest[-1]
    loads = [pltpu.make_async_copy(ins[k], bufs[k], sems.at[k]) for k in range(count)]
    stores = [pltpu.make_async_copy(out_bufs[k], outs[k], out_sems.at[k]) for k in range(15)]
    stores += [
        pltpu.make_async_copy(bufs[count - 2 + k], outs[15 + k], out_sems.at[15 + k]) for k in range(2)
    ]
    for load in loads:
        load.start()
    conv_b, reduce_b, reduce_a, expand_b, expand_a, deform, off = bufs[:7]
    tables = bufs[7:19]
    for load in loads[:7]:
        load.wait()
    for k, src in enumerate((expand_b, expand_a, deform)):
        rows = src.shape[1]
        for s in range(8):
            out_bufs[3 + k][s * rows : (s + 1) * rows, :] = src[s].astype(F32)
        stores[3 + k].start()
    for k, src in enumerate((conv_b, reduce_b, reduce_a)):
        eighth = src.shape[1]
        for s in range(0, 8, 2):
            rows = jnp.concatenate([src[s], src[s + 1]], axis=0).astype(F32)
            out_bufs[k][:, s * eighth : (s + 2) * eighth] = rows.T
        stores[k].start()
    for k in range(2):
        loads[count - 2 + k].wait()
        stores[15 + k].start()
    rest, total = off[...], None
    order = order_taps(32, 18).astype(BF16)
    for _ in range(3):
        part = rest.astype(BF16)
        rest = rest - part.astype(F32)
        term = lax.dot_general(order, part, (((0,), (0,)), ((), ())), preferred_element_type=F32)
        total = term if total is None else total + term
    out_bufs[6][...] = total
    for load in loads[7 : count - 2]:
        load.wait()
    for k in range(4):
        group, which = tables[3 * k : 3 * k + 3], out_bufs[7 + 2 * k : 9 + 2 * k]
        norms = k >= 2
        for out, row in zip(which, (0, 4) if norms else (1, 0)):
            at = 0
            for table in group:
                for first_lane in range(0, table.shape[1], 128):
                    value = table[row : row + 1, first_lane : first_lane + 128]
                    out[at : at + 1, :] = value * unbias if norms and row == 4 else value
                    at += 1
    for store in stores[6:15]:
        store.start()
    for store in stores:
        store.wait()


def forward(plane_count, r):
    ex_a3, ex_b1, ex_b2 = Exchange(r.ex_a3), Exchange(r.ex_b1), Exchange(r.ex_b2)
    ex_b3, ex_sums = Exchange(r.ex_b3), Exchange(r.ex_sums)
    halo = Halo(2, 2, r.tile, r.rim_b, r.halo)
    halo.blank()
    width = r.h2_a.shape[1]
    count = r.counts[8:9, :]

    def exchange(ex, u_ref):
        ex.put(*device_stats(u_ref, r.mask, count))
        ex.middle_stats(r.counts, plane_count)

    r.ready(r.u_a2)
    activate(r.u_a2, r.norm_a2, r.mask, r.h2_a)
    r.push(r.h2_a)
    r.ready(r.w_expand_a)
    product(r.h2_a, r.w_expand_a, r.wide)
    wait_all()
    exchange(ex_a3, r.wide)
    r.ready(r.feature, r.w_reduce)
    ex_a3.finish_stats(plane_count)
    norm_table(ex_a3, r.scale_a, r.shift_a, r.norm_a3, 2 * width)
    activate(r.wide, r.norm_a3, r.mask, r.middle, r.feature, r.slope_a, r.u_a3)
    r.push(r.middle, r.slope_a, r.u_a3)
    cotangent = pltpu.make_async_copy(r.cotangent, r.feature, r.far_sems.at[0])
    cotangent.start()
    product(r.middle, r.w_reduce, r.u_b1)
    r.push(r.u_b1)
    exchange(ex_b1, r.u_b1)
    ex_b1.finish_stats(plane_count)
    norm_table(ex_b1, r.scale_b, r.shift_b, r.norm_b1, 0)
    activate(r.u_b1, r.norm_b1, r.mask, r.tile)
    halo.start()
    halo.middle()
    halo.finish()
    r.push(r.rim_b)
    build_shifted(r.rim_b, r.shifted)
    r.ready(r.w_conv)
    conv_product(r.shifted, r.w_conv, r.u_b2)
    r.push(r.u_b2)
    exchange(ex_b2, r.u_b2)
    ex_b2.finish_stats(plane_count)
    norm_table(ex_b2, r.scale_b, r.shift_b, r.norm_b2, width)
    activate(r.u_b2, r.norm_b2, r.mask, r.h2_b)
    r.push(r.h2_b)
    r.ready(r.w_expand_b)
    product(r.h2_b, r.w_expand_b, r.wide)
    exchange(ex_b3, r.wide)
    cotangent.wait()
    r.pushed(r.slope_a, r.u_a3)
    e_b3, u_b3, norm = r.slope_a, r.u_a3, r.norm_b3
    ex_b3.finish_stats(plane_count)
    norm_table(ex_b3, r.scale_b, r.shift_b, norm, 2 * width)

    def work(i, lanes):
        x, away = normed(r.wide, norm, i, lanes)
        at = place(r.wide, i, lanes)
        u_b3[at] = r.wide[at].astype(BF16)
        x = x + r.middle[at].astype(F32)
        below, bell = gauss(x)
        m = wide(r.mask[place(r.mask, i, slice(None))], PIECE)
        r.feature_out[at] = (x * below * m).astype(BF16)
        e = (below + x * bell) * r.feature[at].astype(F32) * m
        e_b3[at] = e.astype(BF16)
        return e, e * (away * norm[1:2, lanes])

    sums = by_rows(r.wide.shape[0], r.wide.shape[1], work, 2)
    ex_sums.put(*sums)
    far = [
        pltpu.make_async_copy(e_b3, r.e_b3, r.far_sems.at[1]),
        pltpu.make_async_copy(u_b3, r.u_b3, r.far_sems.at[2]),
    ]
    for copy in far:
        copy.start()
    r.push(r.feature_out)
    ex_sums.middle_sums()
    ex_sums.finish_sums()
    put_sums(ex_sums, r.sums_b3)
    for copy in far:
        copy.wait()


def backward_b(pixel_count, direct, r):
    ex2, ex1 = Exchange(r.ex2), Exchange(r.ex1)
    halo = Halo(2, 2, r.tile, r.back_rim, r.halo)
    halo.blank()
    r.ready(r.e_b3, r.u_b3)
    sums = (r.sums_b3[0:1, :], r.sums_b3[1:2, :])
    norm_back(r.e_b3, r.u_b3, r.norm_b3, sums, pixel_count, r.mask, r.geo)
    r.ready(r.w_expand)
    product(r.geo, r.w_expand, r.grad, turned=True)
    r.ready(r.u_b2)
    sums = gelu_grad(r.grad, r.u_b2, r.norm_b2, r.mask)
    wait_all()
    ex2.put(*sums)
    r.ready(r.h2_b)
    turn(r.h2_b, r.turned)
    ex2.middle_sums()
    weight_product(r.turned, r.geo, r.gw_expand)
    jobs = Jobs()
    if direct:
        jobs.add(*plane_jobs(r.gw_expand, r.eighth_expand_b, r.plane_expand_b))
    else:
        r.push(r.gw_expand)
    jobs.tick(2)
    ex2.finish_sums()
    sums = put_sums(ex2, r.sums_b2)
    norm_back(r.grad, r.u_b2, r.norm_b2, sums, pixel_count, r.mask, r.tile)
    halo.start()
    tile_rows, tile_cols, width = r.tile.shape[1:]
    pixels = tile_rows * tile_cols
    for n in range(r.tile.shape[0]):
        for k in range(0, tile_rows, 8):
            at = n * pixels + k * tile_cols
            block = r.tile[n, k : k + 8].reshape(8 * tile_cols, width)
            r.turned[:, at : at + 8 * tile_cols] = block.T
    r.ready(r.rim_b)
    build_shifted(r.rim_b, r.shifted)
    conv_weight_product(r.turned, r.shifted, r.gw_conv, 0)
    halo.middle()
    jobs.tick(2)
    conv_weight_product(r.turned, r.shifted, r.gw_conv, 1)
    halo.finish()
    build_shifted(r.back_rim, r.back_shifted)
    r.ready(r.w_conv)
    unconv_product(r.back_shifted, r.w_conv, r.grad)
    r.ready(r.u_b1)
    sums = gelu_grad(r.grad, r.u_b1, r.norm_b1, r.mask)
    ex1.put(*sums)
    jobs.tick(2)
    ex1.middle_sums()
    conv_weight_product(r.turned, r.shifted, r.gw_conv, 2)
    r.push(r.gw_conv)
    jobs.finish()
    if direct:
        r.push(r.eighth_expand_b)
    ex1.finish_sums()
    sums = put_sums(ex1, r.sums_b1)
    norm_back(r.grad, r.u_b1, r.norm_b1, sums, pixel_count, r.mask, r.gro_b)


def backward_a(pixel_count, direct, r):
    ex3, ex2 = Exchange(r.ex3), Exchange(r.ex2)
    conv, line = Jobs(), Jobs()
    r.ready(r.gro_b, r.w_reduce)
    product(r.gro_b, r.w_reduce, r.wide, turned=True)
    wait_all()
    if direct:
        r.ready(r.src_conv_b, r.eighth_expand_b)
        conv.add(*plane_jobs(r.src_conv_b, r.eighth_conv_b, r.plane_conv_b))
        line.add(*line_jobs(r.eighth_expand_b, r.sum_expand_b, r.line_expand_b))
    conv.tick(2)
    line.tick(2)
    r.ready(r.e_b3, r.slope_a, r.u_a3)
    norm = r.norm_a3

    def work(i, lanes):
        at = place(r.wide, i, lanes)
        e = (r.wide[at] + r.e_b3[at].astype(F32)) * r.slope_a[at].astype(F32)
        r.e_a3[at] = e.astype(BF16)
        away = r.u_a3[at].astype(F32) - norm[0:1, lanes]
        return e, e * (away * norm[1:2, lanes])

    sums = by_rows(r.wide.shape[0], r.wide.shape[1], work, 2)
    ex3.put(*sums)
    conv.tick(2)
    r.push(r.e_a3)
    turn(r.gro_b, r.turned)
    ex3.middle_sums()
    r.ready(r.middle)
    weight_product(r.turned, r.middle, r.gw_reduce)
    r.push(r.gw_reduce)
    line.tick(2)
    ex3.finish_sums()
    sums = put_sums(ex3, r.sums_a3)
    norm_back(r.e_a3, r.u_a3, norm, sums, pixel_count, r.mask, r.e_b3)
    r.ready(r.w_expand)
    product(r.e_b3, r.w_expand, r.grad, turned=True)
    r.ready(r.u_a2)
    sums = gelu_grad(r.grad, r.u_a2, r.norm_a2, r.mask)
    ex2.put(*sums)
    conv.tick(2)
    line.tick(2)
    r.ready(r.h2_a)
    turn(r.h2_a, r.turned)
    ex2.middle_sums()
    weight_product(r.turned, r.e_b3, r.gw_expand)
    r.push(r.gw_expand)
    ex2.finish_sums()
    sums = put_sums(ex2, r.sums_a2)
    norm_back(r.grad, r.u_a2, r.norm_a2, sums, pixel_count, r.mask, r.gd)
    conv.finish()
    line.finish()
    if direct:
        r.push(r.eighth_conv_b, r.sum_expand_b)


def unsample(r, plan):
    width = r.rim.shape[2]
    cols = r.table.shape[0] // WINDOW
    pixels = r.up.shape[2] // 2
    r.spill[...] = jnp.zeros_like(r.spill)
    r.grad_row[...] = jnp.zeros_like(r.grad_row)
    r.grad_col[...] = jnp.zeros_like(r.grad_col)

    def unit(step, carry):
        n, block = step // 2, lax.rem(step, 2)
        lanes = pl.ds(pl.multiple_of(block * pixels, pixels), pixels)
        base = block * (BLOCK_ROWS * cols)
        grad_in = r.turned[:, pl.ds(pl.multiple_of(step * pixels, pixels), pixels)]
        for group in range(3):
            first, start, stop = tap_span(group, cols)
            cells = pl.ds(pl.multiple_of(base + start, 128), stop - start)
            for j in range(3):
                tap = 3 * group + j
                spot = slice(j * pixels, (j + 1) * pixels)
                row_w, row_s, col_w, col_s = tap_weights(
                    tap, block, cols, r.up, r.left, r.fr, r.fc, n, lanes
                )
                write_table(r.table, j * pixels, row_w, col_w, group, cols)
                grad = jnp.dot(
                    r.w_deform[tap * width : (tap + 1) * width, :],
                    grad_in,
                    preferred_element_type=F32,
                ).astype(BF16)
                r.grads[:, spot] = grad
                scores = jnp.dot(r.rim[n, cells, :], grad, preferred_element_type=F32)
                by_value = jnp.zeros((cols, pixels), F32)
                by_slope = jnp.zeros((cols, pixels), F32)
                for k in range(first, first + SPAN):
                    line = scores[k * cols - start : (k + 1) * cols - start]
                    by_value = by_value + line * row_w[k : k + 1, :]
                    by_slope = by_slope + line * row_s[k : k + 1, :]
                r.grad_row[n, tap : tap + 1, lanes] = jnp.sum(
                    by_slope * col_w, axis=0, keepdims=True
                )
                r.grad_col[n, tap : tap + 1, lanes] = jnp.sum(
                    by_value * col_s, axis=0, keepdims=True
                )
            r.spill[n, cells, :] += lax.dot_general(
                r.table[start:stop, :],
                r.grads[...],
                (((1,), (1,)), ((), ())),
                preferred_element_type=F32,
            )
            for turn_at in range(4):
                if 3 * turn_at + group in plan:

                    @pl.when(step == turn_at)
                    def _(slot=3 * turn_at + group):
                        plan[slot]()

        return carry

    lax.fori_loop(0, 4, unit, 0)


def select_cells(r, cols):
    off = HALF * lax.axis_index(COL)
    cells = r.select.shape[1]

    def fill(i, carry):
        ids = lax.broadcasted_iota(jnp.int32, (STEP, cells), 1)
        pixel = lax.broadcasted_iota(jnp.int32, (STEP, cells), 0)
        hit = ids == pixel + (i + PAD) * cols + off
        r.select[pl.ds(pl.multiple_of(i * STEP, STEP), STEP), :] = jnp.where(hit, 1.0, 0.0).astype(
            BF16
        )
        return carry

    lax.fori_loop(0, r.select.shape[0] // STEP, fill, 0)


def unoffset(r, n):
    images, cells, width = r.rim.shape
    cols = r.table.shape[0] // WINDOW
    column = lax.rem(lax.broadcasted_iota(jnp.int32, (32, cells), 1), cols)
    parts = []
    for grad, frac in ((r.grad_row, r.fr), (r.grad_col, r.fc)):
        f = frac[n]
        parts.append(grad[n] * f * (1.0 - f))
    go = jnp.concatenate(parts, axis=0).astype(BF16)
    on_tile = jnp.dot(go, r.select[...], preferred_element_type=F32)
    for tap in range(9):
        i, j = 2 * (tap // 3 - 1), 2 * (tap % 3 - 1)
        kept = on_tile
        if j < 0:
            kept = jnp.where(column >= -j, on_tile, 0.0)
        if j > 0:
            kept = jnp.where(column < cols - j, on_tile, 0.0)
        shift = (i * cols + j) % cells
        if shift:
            kept = pltpu.roll(kept, shift, axis=1)
        r.on_cells[32 * tap : 32 * tap + 32, :] = kept.astype(BF16)
    grad = jnp.dot(r.on_cells[...], r.rim[n], preferred_element_type=F32)
    if n == 0:
        r.gw_off_sum[...] = grad
    else:
        r.gw_off_sum[...] += grad
    for first in range(0, cells, 512):
        r.spill[n, first : first + 512, :] += lax.dot_general(
            r.on_cells[:, first : first + 512],
            r.w_off[...],
            (((0,), (0,)), ((), ())),
            preferred_element_type=F32,
        )
    if n == images - 1:
        for tap in range(9):
            put_lanes(r.gw_off, tap * width, r.gw_off_sum[32 * tap : 32 * tap + 32, :])


class Spill:
    @staticmethod
    def scratch(images, tile_rows, tile_cols, width):
        side = pltpu.VMEM((images, tile_rows + 2 * PAD, HALF, width), BF16)
        strip = pltpu.VMEM((images, REACH, tile_cols, width), BF16)
        sems = pltpu.SemaphoreType.DMA((3,))
        return [side, side, strip, strip, strip, strip, sems, sems]

    def __init__(self, spill, grad, cols, refs, image):
        self.spill, self.grad, self.cols = spill.at[pl.ds(image, 1)], grad, cols
        self.image = image
        self.side_out, self.side_in, self.up_out, self.down_out, self.up_in, self.down_in = refs[:6]
        send, recv = refs[6:]
        self.row, self.rows, col, pair, above, below = halo_peers()
        self.images, self.all_rows = self.side_out.shape[:2]
        self.tile_rows, self.tile_cols = self.all_rows - 2 * PAD, self.up_out.shape[2]
        self.off, self.away, self.near = HALF * col, 2 * HALF * (1 - col), HALF * (1 - col)
        self.side = remote(self.side_out, self.side_in, send.at[0], recv.at[0], pair)
        self.up = remote(self.up_out, self.down_in, send.at[1], recv.at[1], above)
        self.down = remote(self.down_out, self.up_in, send.at[2], recv.at[2], below)

    def cells(self, k, first, count):
        return pl.ds(pl.multiple_of(k * self.cols + first, HALF), count)

    def start(self):
        def cast(k, carry):
            for n in range(self.images):
                self.side_out[n, k] = self.spill[n, self.cells(k, self.away, HALF), :].astype(BF16)
            return carry

        lax.fori_loop(0, self.all_rows, cast, 0)
        self.side.start()

    def edge(self, buffer, first):
        near = pl.ds(pl.multiple_of(self.near, HALF), HALF)

        def one(k, carry):
            for n in range(self.images):
                at = first + k
                buffer[n, k] = self.spill[n, self.cells(at, self.off, self.tile_cols), :].astype(BF16)
                part = self.spill[n, self.cells(at, HALF, HALF), :]
                buffer[n, k, near, :] = (part + self.side_in[n, at].astype(F32)).astype(BF16)
            return carry

        lax.fori_loop(0, REACH, one, 0)

    def middle(self):
        self.side.wait_recv()

        @pl.when(self.row > 0)
        def _():
            self.edge(self.up_out, PAD - REACH)
            self.up.start()

        @pl.when(self.row < self.rows - 1)
        def _():
            self.edge(self.down_out, PAD + self.tile_rows)
            self.down.start()

    def pixels(self, n, k, first, count):
        at = ((self.image + n) * self.tile_rows + k) * self.tile_cols + first
        return pl.ds(pl.multiple_of(at, HALF), count)

    def own(self):
        def fill(k, carry):
            for n in range(self.images):
                home = self.spill[n, self.cells(PAD + k, self.off, self.tile_cols), :]
                self.grad[self.pixels(n, k, 0, self.tile_cols), :] = home
                self.grad[self.pixels(n, k, self.near, HALF), :] += self.side_in[n, PAD + k].astype(F32)
            return carry

        lax.fori_loop(0, self.tile_rows, fill, 0)

    def finish(self):
        def arrive(buffer, first):
            def one(k, carry):
                for n in range(self.images):
                    at = self.pixels(n, first + k, 0, self.tile_cols)
                    self.grad[at, :] += buffer[n, k].astype(F32)
                return carry

            lax.fori_loop(0, REACH, one, 0)

        @pl.when(self.row > 0)
        def _():
            self.down.wait_recv()
            arrive(self.up_in, 0)
            self.up.wait_send()

        @pl.when(self.row < self.rows - 1)
        def _():
            self.up.wait_recv()
            arrive(self.down_in, self.tile_rows - REACH)
            self.down.wait_send()

        self.side.wait_send()


def backward_s(pixel_count, direct, r):
    ex = Exchange(r.ex1)
    cols = r.table.shape[0] // WINDOW
    spills = [Spill(r.spill, r.grad, cols, r.strips[8 * n : 8 * n + 8], n) for n in range(2)]

    mid, late, end, line = Jobs(), Jobs(), Jobs(), Jobs()
    deform_weight_product(r)
    wait_all()
    if direct:
        reduce, expand, deform = Jobs(), Jobs(), Jobs()
        line.add(*line_jobs(r.eighth_conv_b, r.sum_conv_b, r.line_conv_b))
        reduce.add(*plane_jobs(r.src_reduce_b, r.eighth_reduce_b, r.plane_reduce_b))
        reduce.add(*part_jobs(LineSum, r.eighth_reduce_b, r.own_reduce_b, r.line_reduce_b))
        expand.add(*part_jobs(LinePlane, r.src_expand_a, r.own_expand_a, r.plane_expand_a))
        deform.add(*plane_jobs(r.gw_deform, r.eighth_deform, r.plane_deform))
        deform.add(*part_jobs(LineSum, r.eighth_deform, r.own_deform, r.line_deform))
        deform.tick(2)
        r.ready(r.eighth_conv_b)
        line.tick(2)
        r.ready(r.src_expand_a, r.src_reduce_b)
        q2, q3, q4 = reduce.queue, expand.queue, deform.queue
        slots = {
            1: q4[0:2] + q3[0:2],
            3: q3[2:4] + q2[0:2],
            6: q4[2:4],
            7: q2[2:4],
            9: q4[4:8],
            10: q2[4:6],
        }
        mid.queue = q2[6:10] + q3[4:6]
        late.queue = q3[6:8]
        end.queue = q4[8:10] + q2[10:12] + q3[8:10]
    else:
        slots = {}
        r.push(r.gw_deform)
    slots[5] = [functools.partial(unoffset, r, 0), spills[0].start] + slots.get(5, [])
    slots[8] = [spills[0].middle] + slots.get(8, [])

    def run(queue):
        def call():
            for step in queue:
                step()

        return call

    plan = {slot: run(queue) for slot, queue in slots.items()}
    r.ready(r.w_deform, r.rim, r.w_off, r.select)
    turn(r.gd, r.turned)
    unsample(r, plan)
    unoffset(r, 1)
    spills[1].start()
    r.push(r.gw_off)
    spills[1].middle()
    mid.finish()
    for spill in spills:
        spill.own()
    spills[0].finish()
    late.finish()
    r.ready(r.u_a1)
    spills[1].finish()
    line.tick(2)
    sums = gelu_grad(r.grad, r.u_a1, r.norm_a1, r.mask)
    ex.put(*sums)
    ex.middle_sums()
    ex.finish_sums()
    sums = put_sums(ex, r.sums_a1)
    line.tick(2)
    norm_back(r.grad, r.u_a1, r.norm_a1, sums, pixel_count, r.mask, r.gr_a)
    end.finish()
    line.finish()
    if direct:
        r.push(r.sum_conv_b, r.own_reduce_b, r.own_expand_a, r.own_deform)


def deform_weight_product(r):
    width = r.gd.shape[1]
    slots = r.sample_slots.shape[0]

    def load(tap):
        rows, slot = pl.ds(tap * width, width), tap % slots
        return pltpu.make_async_copy(
            r.samples.at[rows], r.sample_slots.at[slot], r.sample_sems.at[slot]
        )

    for tap in range(slots):
        load(tap).start()
    r.ready(r.gd)
    for tap in range(9):
        load(tap).wait()
        value = jnp.dot(r.sample_slots[tap % slots], r.gd[...], preferred_element_type=F32)
        put_rows(r.gw_deform, tap * width, value)
        if tap + slots < 9:
            load(tap + slots).start()


def last(direct, r):
    jobs, more, plane = Jobs(), Jobs(), Jobs()
    r.ready(r.gr_a, r.feature)
    wait_all()
    if direct:
        r.ready(r.own_deform, r.gw_off)
        jobs.add(
            *part_jobs(Gather, r.own_deform, r.sum_deform, r.gather_deform),
            SmallSum(r.gw_off, r.sum_off, r.small),
        )
        more.add(
            *part_jobs(Gather, r.own_reduce_b, r.sum_reduce_b, r.gather_reduce_b),
            *part_jobs(Gather, r.own_expand_a, r.sum_expand_a, r.gather_expand_a),
        )
    jobs.tick(3)
    turn(r.gr_a, r.turned)
    weight_product(r.turned, r.feature, r.gw_reduce)
    if direct:
        plane.add(*plane_jobs(r.gw_reduce, r.eighth_reduce_a, r.plane_reduce_a))
        plane.add(*line_jobs(r.eighth_reduce_a, r.sum_reduce_a, r.line_reduce_a))
    else:
        r.push(r.gw_reduce)
    plane.tick(2)
    if direct:
        r.ready(r.own_reduce_b, r.own_expand_a)
    r.ready(r.w_reduce, r.e_a3)

    def chunk(i, carry):
        rows = pl.ds(pl.multiple_of(i * CHUNK, CHUNK), CHUNK)
        for first in range(0, r.feature.shape[1], 512):
            lanes = slice(first, first + 512)
            grad = lax.dot_general(
                r.gr_a[rows, :],
                r.w_reduce[lanes, :],
                (((1,), (1,)), ((), ())),
                preferred_element_type=F32,
            )
            r.grad_in[rows, lanes] = (grad + r.e_a3[rows, lanes].astype(F32)).astype(BF16)
        return carry

    half = r.feature.shape[0] // CHUNK // 2
    lax.fori_loop(0, half, chunk, 0)
    plane.tick(2)
    lax.fori_loop(half, 2 * half, chunk, 0)
    r.push(r.grad_in)
    jobs.tick(3)
    plane.tick(2)
    more.tick(4)
    plane.tick(4)
    jobs.finish()
    more.tick(4)
    plane.tick(2)
    more.finish()
    if direct:
        r.push(r.sum_reduce_b, r.sum_expand_a, r.sum_deform)
    plane.finish()
    if direct:
        r.push(r.sum_reduce_a)


def body(
    feature_in,
    orientation,
    offset_base,
    w_reduce_a,
    w_offset_a,
    w_deform_a,
    w_expand_a,
    scale_a,
    shift_a,
    w_reduce_b,
    w_conv_b,
    w_expand_b,
    scale_b,
    shift_b,
    cotangent,
):
    images, tile_rows, tile_cols, channels = feature_in.shape
    inner_width = w_reduce_a.shape[1]
    tile_pixels = tile_rows * tile_cols
    pixels = images * tile_pixels
    win_cols = tile_cols + HALF
    win_rows = tile_rows + 2 * PAD
    cells = win_rows * win_cols
    plane_count = 1.0 * images * LONG * SHORT
    pixel_count = plane_count * lax.axis_size(IMG)
    unbias = pixel_count / (pixel_count - 1.0)

    def array(*shape, dtype=BF16):
        return jax.ShapeDtypeStruct(shape, dtype)

    def table(width):
        return array(NORM_ROWS, width, dtype=F32)

    small = (pixels, inner_width)
    big = (pixels, channels)
    window_b = (images, tile_rows + 4, win_cols, inner_width)
    shifted = pltpu.VMEM((images, tile_rows + 4, tile_cols, 3 * inner_width), BF16)
    tile = pltpu.VMEM((images, tile_rows, tile_cols, inner_width), BF16)
    turned = pltpu.VMEM((inner_width, pixels), BF16)
    images_axis = lax.axis_size(IMG)
    direct = inner_width % (images_axis * 8 * 16) == 0
    cuts = images_axis if direct else 1
    feature = feature_in.reshape(big)
    scale_a, shift_a, scale_b, shift_b = (v[None] for v in (scale_a, shift_a, scale_b, shift_b))
    taps_shape = (images, 16, tile_pixels)
    start = fused(
        functools.partial(first, plane_count),
        FIRST_CID,
        ins=dict(
            base=offset_base.reshape(pixels, 18),
            w_offset=w_offset_a.T,
            scale=scale_a,
            shift=shift_a,
        ),
        smem=dict(orientation=orientation),
        staged=dict(feature=feature, w_reduce=w_reduce_a, w_deform=w_deform_a),
        outs=dict(
            mask=array(pixels, 128, dtype=F32),
            counts=array(16, 128, dtype=F32),
            up=array(*taps_shape, dtype=jnp.int32),
            left=array(*taps_shape, dtype=jnp.int32),
            w_off=array(288, inner_width),
            norm_a1=table(inner_width),
            norm_a2=table(inner_width),
        ),
        pushed=dict(
            u_a1=array(*small, dtype=F32),
            rim=array(images, win_rows, win_cols, inner_width),
            select=array(tile_pixels, cells),
            fr=array(*taps_shape, dtype=F32),
            fc=array(*taps_shape, dtype=F32),
            samples=array(9 * inner_width, pixels),
            u_a2=array(*small, dtype=F32),
        ),
        scratch=dict(
            ex1=Exchange.scratch(inner_width),
            ex2=Exchange.scratch(inner_width),
            halo=Halo.scratch * images,
            tile=tile,
            w_turned=pltpu.VMEM((inner_width, 9 * inner_width), BF16),
            rim_t=pltpu.VMEM((images, inner_width, cells), BF16),
            spread=pltpu.VMEM((288, cells), F32),
            table=pltpu.VMEM((WINDOW * win_cols, tile_pixels // 2), BF16),
        ),
    )
    mask, count_rows, norm_a1 = start.mask, start.counts, start.norm_a1
    rim_flat = start.rim.reshape(images, cells, inner_width)
    norm_a2, deformed = start.norm_a2, start.u_a2
    fwd = fused(
        functools.partial(forward, plane_count),
        FORWARD_CID,
        ins=dict(
            norm_a2=norm_a2,
            mask=mask,
            counts=count_rows,
            scale_a=scale_a,
            shift_a=shift_a,
            scale_b=scale_b,
            shift_b=shift_b,
        ),
        far=dict(cotangent=cotangent.reshape(big)),
        staged=dict(
            u_a2=deformed,
            w_expand_a=w_expand_a,
            feature=feature,
            w_reduce=w_reduce_b,
            w_conv=w_conv_b,
            w_expand_b=w_expand_b,
        ),
        outs=dict(
            norm_a3=table(channels),
            norm_b1=table(inner_width),
            norm_b2=table(inner_width),
            norm_b3=table(channels),
            sums_b3=table(channels),
        ),
        pushed=dict(
            h2_a=array(*small),
            middle=array(*big),
            slope_a=array(*big),
            u_a3=array(*big),
            u_b1=array(*small, dtype=F32),
            rim_b=array(*window_b),
            u_b2=array(*small, dtype=F32),
            h2_b=array(*small),
            feature_out=array(*big),
        ),
        far_outs=dict(e_b3=array(*big), u_b3=array(*big)),
        scratch=dict(
            ex_a3=Exchange.scratch(channels),
            ex_b1=Exchange.scratch(inner_width),
            ex_b2=Exchange.scratch(inner_width),
            ex_b3=Exchange.scratch(channels),
            ex_sums=Exchange.scratch(channels),
            halo=Halo.scratch,
            wide=pltpu.VMEM(big, F32),
            tile=tile,
            shifted=shifted,
            far_sems=pltpu.SemaphoreType.DMA((3,)),
        ),
    )
    def eighths(grad):
        return grad.reshape(images_axis, 8, -1, grad.shape[-1])

    def eighth_of(src):
        return array(images_axis, *src.shape[2:])

    def own_of(src):
        return array(*src.shape[2:])

    def sum_of(src):
        return array(*src.shape[1:])

    def vmem(struct):
        return pltpu.VMEM(struct.shape, struct.dtype)

    natural = array(1, inner_width, channels)
    pushed_b, scratch_b = dict(gw_expand=natural), {}
    if direct:
        expand_b = array(images_axis, 8, inner_width // images_axis // 8, channels)
        pushed_b = dict(eighth_expand_b=eighth_of(expand_b))
        scratch_b = dict(gw_expand=vmem(expand_b), plane_expand_b=Plane.scratch(expand_b.shape))
    bwd_b = fused(
        functools.partial(backward_b, pixel_count, direct),
        BACKWARD_B_CID,
        ins=dict(
            mask=mask,
            norm_b3=fwd.norm_b3,
            sums_b3=fwd.sums_b3,
            norm_b2=fwd.norm_b2,
            norm_b1=fwd.norm_b1,
        ),
        staged=dict(
            e_b3=fwd.e_b3,
            u_b3=fwd.u_b3,
            w_expand=w_expand_b,
            u_b2=fwd.u_b2,
            h2_b=fwd.h2_b,
            rim_b=fwd.rim_b,
            w_conv=w_conv_b,
            u_b1=fwd.u_b1,
        ),
        outs=dict(gro_b=array(*small), sums_b2=table(inner_width), sums_b1=table(inner_width)),
        pushed=dict(
            **pushed_b,
            gw_conv=array(cuts, inner_width, 9 * inner_width // cuts),
        ),
        scratch=dict(
            **scratch_b,
            ex2=Exchange.scratch(inner_width),
            ex1=Exchange.scratch(inner_width),
            halo=Halo.scratch,
            geo=pltpu.VMEM(big, BF16),
            grad=pltpu.VMEM(small, F32),
            tile=tile,
            turned=turned,
            back_rim=pltpu.VMEM(window_b, BF16),
            shifted=shifted,
            back_shifted=shifted,
        ),
    )

    staged_a, pushed_a, scratch_a = {}, {}, {}
    if direct:
        conv_b = eighths(bwd_b.gw_conv)
        staged_a = dict(src_conv_b=conv_b, eighth_expand_b=bwd_b.eighth_expand_b)
        pushed_a = dict(eighth_conv_b=eighth_of(conv_b), sum_expand_b=sum_of(expand_b))
        scratch_a = dict(
            plane_conv_b=Plane.scratch(conv_b.shape),
            line_expand_b=Line.scratch(bwd_b.eighth_expand_b.shape),
        )
    bwd_a = fused(
        functools.partial(backward_a, pixel_count, direct),
        BACKWARD_A_CID,
        ins=dict(mask=mask, norm_a3=fwd.norm_a3, norm_a2=norm_a2),
        staged=dict(
            gro_b=bwd_b.gro_b,
            w_reduce=w_reduce_b,
            **staged_a,
            e_b3=fwd.e_b3,
            slope_a=fwd.slope_a,
            u_a3=fwd.u_a3,
            middle=fwd.middle,
            w_expand=w_expand_a,
            u_a2=deformed,
            h2_a=fwd.h2_a,
        ),
        outs=dict(gd=array(*small), sums_a3=table(channels), sums_a2=table(inner_width)),
        pushed=dict(
            **pushed_a,
            gw_reduce=array(cuts, inner_width, channels // cuts),
            gw_expand=natural,
            e_a3=array(*big),
        ),
        scratch=dict(
            **scratch_a,
            ex3=Exchange.scratch(channels),
            ex2=Exchange.scratch(inner_width),
            wide=pltpu.VMEM(big, F32),
            grad=pltpu.VMEM(small, F32),
            turned=turned,
        ),
    )
    staged_s, scratch_s = {}, {}
    pushed_s = dict(gw_deform=array(1, 9 * inner_width, inner_width))
    if direct:
        reduce_b, expand_a = eighths(bwd_a.gw_reduce), eighths(bwd_a.gw_expand)
        deform = array(images_axis, 8, 9 * inner_width // images_axis // 8, inner_width)
        staged_s = dict(
            src_reduce_b=reduce_b,
            src_expand_a=expand_a,
            eighth_conv_b=bwd_a.eighth_conv_b,
        )
        pushed_s = dict(
            sum_conv_b=sum_of(conv_b),
            own_reduce_b=own_of(reduce_b),
            own_expand_a=own_of(expand_a),
            own_deform=own_of(deform),
        )
        scratch_s = dict(
            gw_deform=vmem(deform),
            line_conv_b=Line.scratch(bwd_a.eighth_conv_b.shape),
            plane_reduce_b=Plane.scratch(reduce_b.shape),
            plane_expand_a=LinePlane.scratch(expand_a.shape),
            plane_deform=Plane.scratch(deform.shape),
            eighth_reduce_b=vmem(eighth_of(reduce_b)),
            eighth_deform=vmem(eighth_of(deform)),
            line_reduce_b=LineSum.scratch(eighth_of(reduce_b).shape),
            line_deform=LineSum.scratch(eighth_of(deform).shape),
        )
    block = tile_pixels // 2
    bwd_s = fused(
        functools.partial(backward_s, pixel_count, direct),
        BACKWARD_S_CID,
        ins=dict(
            mask=mask,
            norm_a1=norm_a1,
            up=start.up,
            left=start.left,
            fr=start.fr,
            fc=start.fc,
        ),
        far=dict(samples=start.samples),
        staged=dict(
            gd=bwd_a.gd,
            **staged_s,
            w_deform=w_deform_a,
            rim=rim_flat,
            w_off=start.w_off,
            select=start.select,
            u_a1=start.u_a1,
        ),
        outs=dict(gr_a=array(*small), sums_a1=table(inner_width)),
        pushed=dict(**pushed_s, gw_off=array(cuts, 32, 9 * inner_width // cuts)),
        scratch=dict(
            **scratch_s,
            ex1=Exchange.scratch(inner_width),
            strips=Spill.scratch(1, tile_rows, tile_cols, inner_width) * images,
            spill=pltpu.VMEM((images, cells, inner_width), F32),
            table=pltpu.VMEM((WINDOW * win_cols, 3 * block), BF16),
            grads=pltpu.VMEM((inner_width, 3 * block), BF16),
            turned=turned,
            grad_row=pltpu.VMEM(taps_shape, F32),
            grad_col=pltpu.VMEM(taps_shape, F32),
            on_cells=pltpu.VMEM((288, cells), BF16),
            gw_off_sum=pltpu.VMEM((288, inner_width), F32),
            sample_slots=pltpu.VMEM((3, inner_width, pixels), BF16),
            sample_sems=pltpu.SemaphoreType.DMA((3,)),
            grad=pltpu.VMEM(small, F32),
        ),
    )
    staged_l, pushed_l, scratch_l = {}, {}, {}
    if direct:
        reduce_a = array(images_axis, 8, inner_width // 8, channels // cuts)
        staged_l = dict(
            own_deform=bwd_s.own_deform,
            gw_off=bwd_s.gw_off,
            own_reduce_b=bwd_s.own_reduce_b,
            own_expand_a=bwd_s.own_expand_a,
        )
        pushed_l = dict(
            sum_reduce_b=sum_of(reduce_b),
            sum_expand_a=sum_of(expand_a),
            sum_deform=sum_of(deform),
            sum_reduce_a=sum_of(reduce_a),
        )
        scratch_l = dict(
            gw_reduce=vmem(reduce_a),
            small=SmallSum.scratch(bwd_s.gw_off.shape),
            gather_reduce_b=Gather.scratch(reduce_b.shape),
            gather_expand_a=Gather.scratch(expand_a.shape),
            gather_deform=Gather.scratch(deform.shape),
            plane_reduce_a=Plane.scratch(reduce_a.shape),
            eighth_reduce_a=vmem(eighth_of(reduce_a)),
            line_reduce_a=Line.scratch(eighth_of(reduce_a).shape),
        )
        outs_l = dict(sum_off=array(*bwd_s.gw_off.shape[1:], dtype=F32))
    else:
        pushed_l = dict(gw_reduce=array(cuts, inner_width, channels // cuts))
        outs_l = {}
    end = fused(
        functools.partial(last, direct),
        LAST_CID,
        ins={},
        staged=dict(
            gr_a=bwd_s.gr_a, feature=feature, **staged_l, w_reduce=w_reduce_a, e_a3=bwd_a.e_a3
        ),
        outs=outs_l,
        pushed=dict(**pushed_l, grad_in=array(*big)),
        scratch=dict(**scratch_l, turned=turned),
    )
    sums_a = [bwd_s.sums_a1, bwd_a.sums_a2, bwd_a.sums_a3]
    sums_b = [bwd_b.sums_b1, bwd_b.sums_b2, fwd.sums_b3]
    norms_a = [norm_a1, norm_a2, fwd.norm_a3]
    norms_b = [fwd.norm_b1, fwd.norm_b2, fwd.norm_b3]
    if direct:
        sums = [
            bwd_s.sum_conv_b,
            end.sum_reduce_b,
            end.sum_reduce_a,
            bwd_a.sum_expand_b,
            end.sum_expand_a,
            end.sum_deform,
            end.sum_off,
        ]
    else:

        def over_devices(grad, dim):
            part = lax.psum_scatter(grad, IMG, scatter_dimension=dim, tiled=True)
            return lax.psum(part, (ROW, COL))

        turned_grads = (bwd_b.gw_conv, bwd_a.gw_reduce, end.gw_reduce)
        sums = [over_devices(g[0], 1) for g in turned_grads]
        sums += [over_devices(g[0], 0) for g in (bwd_b.gw_expand, bwd_a.gw_expand)]
        sums.append(over_devices(bwd_s.gw_deform[0], 0))
        sums = [g.reshape(8, -1, g.shape[1]) for g in sums]
        sums.append(over_devices(bwd_s.gw_off[0], 1).astype(F32))
    share = inner_width // images_axis
    long_share, wide_share = 9 * share, channels // images_axis
    shapes = [
        (long_share, inner_width),
        (wide_share, inner_width),
        (wide_share, inner_width),
        (share, channels),
        (share, channels),
        (long_share, inner_width),
        (18, long_share),
    ]
    vectors = ((2 * inner_width + channels) // 128, 128)
    shapes += [vectors] * 8
    operands = sums + sums_a + sums_b + norms_a + norms_b + [fwd.feature_out, end.grad_in]
    results = [array(*shape, dtype=F32) for shape in shapes]
    anywhere = pl.BlockSpec(memory_space=pl.ANY)
    results = pl.pallas_call(
        functools.partial(finish_kernel, unbias, len(operands)),
        out_shape=results + [array(*big)] * 2,
        in_specs=[anywhere] * len(operands),
        out_specs=[anywhere] * (len(shapes) + 2),
        scratch_shapes=[vmem(v) for v in operands + results]
        + [pltpu.SemaphoreType.DMA((len(operands),)), pltpu.SemaphoreType.DMA((17,))],
        compiler_params=pltpu.CompilerParams(vmem_limit_bytes=VMEM_LIMIT),
    )(*operands)
    conv_b, reduce_b, reduce_a, expand_b, expand_a, deform_a, offset_a = results[:7]
    scale_sums_a, shift_sums_a, scale_sums_b, shift_sums_b, mean_a, var_a, mean_b, var_b = (
        v.reshape(-1) for v in results[7:15]
    )
    return (
        results[15].reshape(feature_in.shape),
        results[16].reshape(feature_in.shape),
        reduce_a,
        offset_a.T,
        deform_a,
        expand_a,
        scale_sums_a,
        shift_sums_a,
        mean_a,
        var_a,
        reduce_b,
        conv_b,
        expand_b,
        scale_sums_b,
        shift_sums_b,
        mean_b,
        var_b,
    )


def solution(mesh):
    tiles = P(IMG, ROW, COL, None)
    in_specs = (tiles, P(IMG), tiles) + (P(),) * 11 + (tiles,)
    shares = P(IMG, None)
    out_specs = (tiles, tiles) + (shares,) * 4 + (P(),) * 4 + (shares,) * 3 + (P(),) * 4
    return jax.shard_map(body, mesh=mesh, in_specs=in_specs, out_specs=out_specs, check_vma=False)
```

```python
import functools
import types

import jax
import jax.numpy as jnp
import numpy as np
from jax import lax
from jax.experimental import pallas as pl
from jax.experimental.pallas import tpu as pltpu
from jax.sharding import PartitionSpec as P

LONG = 64
SHORT = 44
BOUND = 4
EPSILON = 1e-05
IMG, ROW, COL = "img", "row", "col"
MESH = pl.DeviceIdType.MESH
VMEM = pl.BlockSpec(memory_space=pltpu.VMEM)
VMEM_LIMIT = 60 * 1024 * 1024
F32 = jnp.float32
BF16 = jnp.bfloat16
REACH = BOUND + 3
PAD = 8
HALF = 16
FIRST_CID, FORWARD_CID, BACKWARD_B_CID, BACKWARD_A_CID, BACKWARD_S_CID, LAST_CID = range(6)


def group_of(axes):
    sizes = [lax.axis_size(a) for a in axes]
    total = int(np.prod(sizes))
    place = lax.axis_index(axes[0])
    for axis, size in zip(axes[1:], sizes[1:]):
        place = place * size + lax.axis_index(axis)

    def device(step):
        spot = lax.rem(place + step, total)
        coords = {}
        for axis, size in zip(reversed(axes), reversed(sizes)):
            coords[axis] = lax.rem(spot, size)
            spot = spot // size
        return coords

    return place, total, device


PLANE = (ROW, COL)
LINE = (IMG,)


def gather_start(axes, slots, send_sem, recv_sem):
    _, total, device = group_of(axes)
    for step in range(1, total):
        pltpu.make_async_remote_copy(
            src_ref=slots.at[0],
            dst_ref=slots.at[step],
            send_sem=send_sem,
            recv_sem=recv_sem,
            device_id=device(step),
            device_id_type=MESH,
        ).start()


def gather_wait(axes, slots, sem):
    _, total, _ = group_of(axes)
    others = slots.at[pl.ds(1, total - 1)]
    pltpu.make_async_copy(others, others, sem).wait()


def in_order(axes, slots):
    place, total, _ = group_of(axes)
    return [slots[lax.rem(place - spot + total, total)] for spot in range(total)]


def halo_peers():
    row, rows, col = lax.axis_index(ROW), lax.axis_size(ROW), lax.axis_index(COL)
    return row, rows, col, {COL: 1 - col}, {ROW: row - 1}, {ROW: row + 1}


BLOCK_ROWS = 8
SPAN = 17
WINDOW = 3 * BLOCK_ROWS


def tap_span(group, cols):
    first = 2 + 2 * group
    start = first * cols // 128 * 128
    stop = -(-(first + SPAN) * cols // 128) * 128
    return first, start, stop


def tap_weights(tap, block, cols, up_ref, left_ref, fr_ref, fc_ref, image=0, lanes=slice(None)):
    up, left, fr, fc = (
        ref[image, tap : tap + 1, lanes] for ref in (up_ref, left_ref, fr_ref, fc_ref)
    )
    up = up - block * BLOCK_ROWS
    pixels = up.shape[1]

    def pair(size, at, frac):
        ids = lax.broadcasted_iota(jnp.int32, (size, pixels), 0)
        first, second = ids == at, ids == at + 1
        value = jnp.where(first, 1.0 - frac, jnp.where(second, frac, 0.0))
        slope = jnp.where(second, 1.0, jnp.where(first, -1.0, 0.0))
        return value, slope

    return pair(WINDOW, up, fr) + pair(cols, left, fc)


def write_table(table, lane, row_w, col_w, group, cols):
    first, start, stop = tap_span(group, cols)
    pixels = row_w.shape[1]
    low = start // cols
    high = -(-stop // cols)
    for r in range(low, min(high, WINDOW)):
        table[r * cols : (r + 1) * cols, lane : lane + pixels] = (
            row_w[r : r + 1, :] * col_w
        ).astype(BF16)


def build_shifted(rim_ref, shifted):
    images, rows, cols, width = rim_ref.shape
    col = lax.axis_index(COL)
    tile = cols - HALF

    def fill(first):
        def one_row(k, carry):
            for n in range(images):
                line = rim_ref[n, k].astype(F32)
                none = jnp.zeros((2, width), F32)
                for d in range(3):
                    at = first + 2 * (d - 1)
                    if at < 0:
                        part = jnp.concatenate([none, line[: tile - 2]], axis=0)
                    elif at + tile > cols:
                        part = jnp.concatenate([line[at:], none], axis=0)
                    else:
                        part = line[at : at + tile]
                    shifted[n, k, :, d * width : (d + 1) * width] = part.astype(BF16)
            return carry

        lax.fori_loop(0, rows, one_row, 0)

    @pl.when(col == 0)
    def _():
        fill(0)

    @pl.when(col == 1)
    def _():
        fill(HALF)


def conv_product(shifted, w_ref, o_ref):
    images, rows, cols, width3 = shifted.shape
    tile_rows = rows - 4
    pixels = tile_rows * cols
    for n in range(images):
        total = None
        for i in range(3):
            taps = shifted[n, 2 * i : 2 * i + tile_rows].reshape(pixels, width3)
            term = jnp.dot(taps, w_ref[i * width3 : (i + 1) * width3, :], preferred_element_type=F32)
            total = term if total is None else total + term
        o_ref[n * pixels : (n + 1) * pixels, :] = total


def conv_weight_product(turned, shifted, gw_ref, i):
    images, rows, cols, width3 = shifted.shape
    tile_rows = rows - 4
    pixels = tile_rows * cols
    total = None
    for n in range(images):
        taps = shifted[n, 2 * i : 2 * i + tile_rows].reshape(pixels, width3)
        term = jnp.dot(turned[:, n * pixels : (n + 1) * pixels], taps, preferred_element_type=F32)
        total = term if total is None else total + term
    put_lanes(gw_ref, i * width3, total)


def unconv_product(shifted, w_ref, o_ref):
    images, rows, cols, width3 = shifted.shape
    width = width3 // 3
    tile_rows = rows - 4
    pixels = tile_rows * cols
    for n in range(images):
        total = None
        for tap in range(9):
            i, d = 2 - tap // 3, 2 - tap % 3
            grads = shifted[n, 2 * i : 2 * i + tile_rows, :, d * width : (d + 1) * width]
            term = lax.dot_general(
                grads.reshape(pixels, width),
                w_ref[tap * width : (tap + 1) * width, :],
                (((1,), (1,)), ((), ())),
                preferred_element_type=F32,
            )
            total = term if total is None else total + term
        o_ref[n * pixels : (n + 1) * pixels, :] = total


def halves(width):
    first = -(-width // 256) * 128
    return ((0, first), (first, width - first)) if first < width else ((0, width),)


def remote(src, dst, send, recv, device):
    return pltpu.make_async_remote_copy(
        src_ref=src, dst_ref=dst, send_sem=send, recv_sem=recv, device_id=device, device_id_type=MESH
    )


def arrival(ref, sem):
    return pltpu.make_async_copy(ref, ref, sem)


class Plane:
    @staticmethod
    def scratch(shape):
        images, _, rows, width = shape
        count = len(halves(width))
        return [
            pltpu.VMEM((images, 4, rows, width), BF16),
            pltpu.VMEM((images, 2, rows, width), BF16),
            pltpu.SemaphoreType.DMA((count, 3)),
            pltpu.SemaphoreType.DMA((count, 3)),
        ]

    def __init__(self, src, eighth, refs, part):
        half, quarter, send, recv = refs
        lanes = pl.ds(*halves(src.shape[-1])[part])
        self.src, self.half, self.quarter = (
            ref.at[:, :, :, lanes] for ref in (src, half, quarter)
        )
        self.eighth = eighth.at[:, :, lanes]
        self.images = src.shape[0]
        self.send, self.recv = [send.at[part, k] for k in range(3)], [recv.at[part, k] for k in range(3)]
        self.a, self.b, self.spot, self.first, self.second = self.peers(part == 0)
        col = lax.axis_index(COL)
        self.mine, self.pair, self.other = 4 * col, {COL: 1 - col}, 4 * (1 - col)

    @staticmethod
    def peers(x_first):
        row = lax.axis_index(ROW)
        x, y = lax.rem(row, 2), row // 2
        to_x, to_y = {ROW: row + 1 - 2 * x}, {ROW: row + 2 - 4 * y}
        if x_first:
            return x, y, lambda bit, free: bit + 2 * free, to_x, to_y
        return y, x, lambda bit, free: 2 * bit + free, to_y, to_x

    def steps(self):
        return [self.to_pair, self.to_first, self.to_second, self.done]

    def to_pair(self):
        src = self.src.at[:, pl.ds(self.other, 4)]
        remote(src, self.half, self.send[0], self.recv[0], self.pair).start()

    def to_first(self):
        arrival(self.half, self.recv[0]).wait()

        def add(i, carry):
            for s in range(4):
                self.half[i, s] = self.src[i, self.mine + s] + self.half[i, s]
            return carry

        lax.fori_loop(0, self.images, add, 0)
        for k in range(2):
            src = self.half.at[:, self.spot(1 - self.a, k)]
            remote(src, self.quarter.at[:, k], self.send[1], self.recv[1], self.first).start()

    def to_second(self):
        arrival(self.quarter, self.recv[1]).wait()

        def add(i, carry):
            for k in range(2):
                self.quarter[i, k] = self.half[i, self.spot(self.a, k)] + self.quarter[i, k]
            return carry

        lax.fori_loop(0, self.images, add, 0)
        src = self.quarter.at[:, 1 - self.b]
        remote(src, self.eighth, self.send[2], self.recv[2], self.second).start()

    def done(self):
        arrival(self.eighth, self.recv[2]).wait()

        def add(i, carry):
            self.eighth[i] = self.quarter[i, self.b] + self.eighth[i]
            return carry

        lax.fori_loop(0, self.images, add, 0)
        arrival(self.half, self.send[0]).wait()
        arrival(self.quarter, self.send[1]).wait()
        arrival(self.eighth, self.send[2]).wait()


class LinePlane:
    @staticmethod
    def scratch(shape):
        images, _, rows, width = shape
        sems = pltpu.SemaphoreType.DMA((len(halves(width)), 4))
        return [
            pltpu.VMEM((images, 4, rows, width), BF16),
            pltpu.VMEM((images, 4, rows, width), BF16),
            pltpu.VMEM((2, rows, width), BF16),
            pltpu.VMEM((rows, width), BF16),
            sems,
            sems,
        ]

    def __init__(self, src, own, refs, part):
        half, line, quarter, eighth, send, recv = refs
        lanes = pl.ds(*halves(src.shape[-1])[part])
        self.src, self.half, self.line = (ref.at[:, :, :, lanes] for ref in (src, half, line))
        self.quarter = quarter.at[:, :, lanes]
        self.eighth, self.own = eighth.at[:, lanes], own.at[:, lanes]
        self.images, self.img = src.shape[0], lax.axis_index(IMG)
        self.send, self.recv = [send.at[part, k] for k in range(4)], [recv.at[part, k] for k in range(4)]
        self.plane = Plane.peers(part == 0)
        col = lax.axis_index(COL)
        self.mine, self.pair, self.other = 4 * col, {COL: 1 - col}, 4 * (1 - col)

    def steps(self):
        return [self.to_pair, self.to_line, self.to_first, self.to_second, self.done]

    def to_pair(self):
        src = self.src.at[:, pl.ds(self.other, 4)]
        remote(src, self.half, self.send[0], self.recv[0], self.pair).start()

    def to_line(self):
        arrival(self.half, self.recv[0]).wait()

        def add(i, carry):
            for s in range(4):
                self.half[i, s] = self.src[i, self.mine + s] + self.half[i, s]
            return carry

        lax.fori_loop(0, self.images, add, 0)
        for j in range(1, self.images):
            there = lax.rem(self.img + j, self.images)
            src = self.half.at[there]
            remote(src, self.line.at[j], self.send[1], self.recv[1], {IMG: there}).start()

    def to_first(self):
        arrival(self.line.at[pl.ds(1, self.images - 1)], self.recv[1]).wait()
        for s in range(4):
            total = self.half[self.img, s].astype(F32)
            for j in range(1, self.images):
                total = total + self.line[j, s].astype(F32)
            self.line[0, s] = total.astype(BF16)
        a, _, spot, first, _ = self.plane
        for k in range(2):
            src = self.line.at[0, spot(1 - a, k)]
            remote(src, self.quarter.at[k], self.send[2], self.recv[2], first).start()

    def to_second(self):
        a, b, spot, _, second = self.plane
        arrival(self.quarter, self.recv[2]).wait()
        for k in range(2):
            self.quarter[k] = self.line[0, spot(a, k)] + self.quarter[k]
        remote(self.quarter.at[1 - b], self.eighth, self.send[3], self.recv[3], second).start()

    def done(self):
        _, b, _, _, _ = self.plane
        arrival(self.eighth, self.recv[3]).wait()
        self.own[...] = self.quarter[b] + self.eighth[...]
        arrival(self.half, self.send[0]).wait()
        arrival(self.line.at[pl.ds(1, self.images - 1)], self.send[1]).wait()
        arrival(self.quarter, self.send[2]).wait()
        arrival(self.eighth, self.send[3]).wait()


class LineSum:
    @staticmethod
    def scratch(shape):
        sems = pltpu.SemaphoreType.DMA((len(halves(shape[-1])),))
        return [pltpu.VMEM(shape, BF16), sems, sems]

    def __init__(self, eighth, own, refs, part):
        line, send, recv = refs
        lanes = pl.ds(*halves(eighth.shape[-1])[part])
        self.eighth, self.line, self.own = eighth.at[:, :, lanes], line.at[:, :, lanes], own.at[:, lanes]
        self.images, self.img = eighth.shape[0], lax.axis_index(IMG)
        self.send, self.recv = send.at[part], recv.at[part]

    def steps(self):
        return [self.to_line, self.done]

    def to_line(self):
        for j in range(1, self.images):
            there = lax.rem(self.img + j, self.images)
            src = self.eighth.at[there]
            remote(src, self.line.at[j], self.send, self.recv, {IMG: there}).start()

    def done(self):
        arrived = self.line.at[pl.ds(1, self.images - 1)]
        arrival(arrived, self.recv).wait()
        total = self.eighth[self.img].astype(F32)
        for j in range(1, self.images):
            total = total + self.line[j].astype(F32)
        self.own[...] = total.astype(BF16)
        arrival(arrived, self.send).wait()


class Gather:
    @staticmethod
    def scratch(shape):
        sems = pltpu.SemaphoreType.DMA((len(halves(shape[-1])), 2))
        return [sems, sems]

    def __init__(self, own, out, refs, part):
        send, recv = refs
        lanes = pl.ds(*halves(out.shape[-1])[part])
        self.own, self.out = own.at[:, lanes], out.at[:, :, lanes]
        self.send, self.recv = [send.at[part, k] for k in range(2)], [recv.at[part, k] for k in range(2)]
        self.row, col = lax.axis_index(ROW), lax.axis_index(COL)
        self.mine, self.pair = 4 * col, {COL: 1 - col}

    def steps(self):
        return [self.to_rows, self.to_pair, self.done]

    def to_rows(self):
        spot = self.out.at[self.mine + self.row]
        self.out[self.mine + self.row] = self.own[...]
        for j in range(1, 4):
            there = lax.rem(self.row + j, 4)
            remote(spot, spot, self.send[0], self.recv[0], {ROW: there}).start()

    def to_pair(self):
        arrival(self.out.at[pl.ds(0, 3)], self.recv[0]).wait()
        four = self.out.at[pl.ds(self.mine, 4)]
        remote(four, four, self.send[1], self.recv[1], self.pair).start()

    def done(self):
        four = self.out.at[pl.ds(0, 4)]
        arrival(four, self.recv[1]).wait()
        arrival(self.out.at[pl.ds(0, 3)], self.send[0]).wait()
        arrival(four, self.send[1]).wait()


class Line:
    @staticmethod
    def scratch(shape):
        return [pltpu.VMEM(shape[1:], BF16)] + LineSum.scratch(shape) + Gather.scratch(shape)

    def __init__(self, eighth, out, refs, part):
        own = refs[0]
        self.sum = LineSum(eighth, own, refs[1:4], part)
        self.gather = Gather(own, out, refs[4:], part)

    def steps(self):
        return [self.sum.to_line, self.to_rows, self.gather.to_pair, self.gather.done]

    def to_rows(self):
        self.sum.done()
        self.gather.to_rows()


class SmallSum:
    @staticmethod
    def scratch(shape):
        sizes = [lax.axis_size(IMG), lax.axis_size(ROW) * lax.axis_size(COL)]
        return [pltpu.VMEM((size,) + shape[1:], BF16) for size in sizes] + [
            pltpu.SemaphoreType.DMA((2,)),
            pltpu.SemaphoreType.DMA((2,)),
        ]

    def __init__(self, src, out, refs):
        self.src, self.out = src, out
        self.slots1, self.slots2, self.send, self.recv = refs

    def steps(self):
        return [self.to_line, self.to_plane, self.done]

    def to_line(self):
        here, total, _ = group_of(LINE)
        self.slots1[0] = self.src[here]
        for j in range(1, total):
            there = lax.rem(here + j, total)
            remote(
                self.src.at[there], self.slots1.at[j], self.send.at[0], self.recv.at[0], {IMG: there}
            ).start()

    def to_plane(self):
        gather_wait(LINE, self.slots1, self.recv.at[0])
        total = added([p.astype(F32) for p in in_order(LINE, self.slots1)])
        self.slots2[0] = total.astype(BF16)
        gather_start(PLANE, self.slots2, self.send.at[1], self.recv.at[1])

    def done(self):
        gather_wait(PLANE, self.slots2, self.recv.at[1])
        self.out[...] = added([p.astype(F32) for p in in_order(PLANE, self.slots2)])
        gather_wait(LINE, self.slots1, self.send.at[0])
        gather_wait(PLANE, self.slots2, self.send.at[1])


class Jobs:
    def __init__(self):
        self.queue = []

    def add(self, *jobs):
        lists = [job.steps() for job in jobs]
        for k in range(max(len(steps) for steps in lists)):
            self.queue += [steps[k] for steps in lists if k < len(steps)]

    def tick(self, count=1):
        for _ in range(min(count, len(self.queue))):
            self.queue.pop(0)()

    def finish(self):
        self.tick(len(self.queue))


def plane_jobs(src, eighth, refs):
    return [Plane(src, eighth, refs, part) for part in range(len(halves(src.shape[-1])))]


def part_jobs(kind, first, second, refs):
    return [kind(first, second, refs, part) for part in range(len(halves(first.shape[-1])))]


def line_jobs(eighth, out, refs):
    return [Line(eighth, out, refs, part) for part in range(len(halves(out.shape[-1])))]


STEP = 32
PIECE = 256
CHUNK = 256


class Refs:
    FLYING = 6 * 1024 * 1024

    def __init__(self):
        self.loads, self.stores, self.queue, self.flying = {}, {}, [], {}

    def load(self, ref, copy):
        self.loads[id(ref)] = copy
        self.queue.append((id(ref), int(np.prod(ref.shape)) * ref.dtype.itemsize))

    def start_loads(self, until=None):
        while self.queue:
            if until is None and sum(self.flying.values()) >= self.FLYING:
                return
            if until is not None and until in self.flying:
                return
            key, size = self.queue.pop(0)
            self.loads[key].start()
            self.flying[key] = size

    def ready(self, *refs):
        for ref in refs:
            self.start_loads(id(ref))
            self.loads.pop(id(ref)).wait()
            self.flying.pop(id(ref))
            self.start_loads()

    def push(self, *refs):
        for ref in refs:
            self.stores[id(ref)].start()

    def pushed(self, *refs):
        for ref in refs:
            self.stores.pop(id(ref)).wait()

    def flush(self):
        for copy in self.stores.values():
            copy.wait()


def fused(work, cid, ins, staged, outs, pushed, scratch, smem={}, far={}, far_outs={}):
    loaded, stored = {**ins, **staged}, {**outs, **pushed}
    sizes = (len(loaded), len(stored))

    def kernel(*refs):
        r = Refs()
        refs = list(refs)

        def take(count):
            taken = refs[:count]
            del refs[:count]
            return taken

        for key, ref in zip((*smem, *far), take(len(smem) + len(far))):
            setattr(r, key, ref)
        in_raw, out_raw = (take(count) for count in sizes)
        for key, ref in zip(far_outs, take(len(far_outs))):
            setattr(r, key, ref)
        for key, shape in scratch.items():
            setattr(r, key, take(len(shape)) if isinstance(shape, list) else take(1)[0])
        in_bufs, out_bufs = (take(count) for count in sizes)
        in_sems, out_sems = take(2)
        for keys, bufs in ((loaded, in_bufs), (stored, out_bufs)):
            for key, buf in zip(keys, bufs):
                setattr(r, key, buf)
        for k, (raw, buf) in enumerate(zip(in_raw, in_bufs)):
            r.load(buf, pltpu.make_async_copy(raw, buf, in_sems.at[k]))
        for k, (raw, buf) in enumerate(zip(out_raw, out_bufs)):
            r.stores[id(buf)] = pltpu.make_async_copy(buf, raw, out_sems.at[k])
        r.start_loads()
        signal_all()
        r.ready(*in_bufs[: len(ins)])
        work(r)
        r.push(*out_bufs[: len(outs)])
        r.flush()

    flat = []
    for shape in scratch.values():
        flat += shape if isinstance(shape, list) else [shape]
    flat += [pltpu.VMEM(a.shape, a.dtype) for a in (*loaded.values(), *stored.values())]
    flat += [pltpu.SemaphoreType.DMA((count,)) for count in sizes]
    anywhere, scalars = pl.BlockSpec(memory_space=pl.ANY), pl.BlockSpec(memory_space=pltpu.SMEM)
    result = pl.pallas_call(
        kernel,
        out_shape=[*stored.values(), *far_outs.values()],
        in_specs=[scalars] * len(smem) + [anywhere] * (len(far) + sizes[0]),
        out_specs=[anywhere] * (sizes[1] + len(far_outs)),
        scratch_shapes=flat,
        compiler_params=pltpu.CompilerParams(
            collective_id=cid, has_side_effects=True, vmem_limit_bytes=VMEM_LIMIT
        ),
    )(*smem.values(), *far.values(), *loaded.values())
    return types.SimpleNamespace(**dict(zip((*stored, *far_outs), result)))


def signal_all():
    barrier = pltpu.get_barrier_semaphore()
    for axes in (PLANE, LINE):
        _, total, device = group_of(axes)
        for step in range(1, total):
            pl.semaphore_signal(barrier, inc=1, device_id=device(step), device_id_type=MESH)


def wait_all():
    count = sum(group_of(axes)[1] - 1 for axes in (PLANE, LINE))
    pl.semaphore_wait(pltpu.get_barrier_semaphore(), count)


def added(parts):
    return functools.reduce(lambda a, b: a + b, parts)


class Exchange:
    @staticmethod
    def scratch(width):
        rows = 2 * width // 128
        sizes = [int(np.prod([lax.axis_size(a) for a in axes])) for axes in (PLANE, LINE)]
        return [
            pltpu.VMEM((sizes[0], rows, 128), F32),
            pltpu.VMEM((sizes[1], rows, 128), F32),
            pltpu.VMEM((rows, 128), F32),
            pltpu.SemaphoreType.DMA((2,)),
            pltpu.SemaphoreType.DMA((2,)),
        ]

    def __init__(self, refs):
        self.slots1, self.slots2, self.out, self.send, self.recv = refs
        self.half = self.out.shape[0] // 2

    def put(self, first, second):
        for k in range(self.half):
            self.slots1[0, k : k + 1, :] = first[:, 128 * k : 128 * (k + 1)]
            self.slots1[0, self.half + k : self.half + k + 1, :] = second[:, 128 * k : 128 * (k + 1)]
        gather_start(PLANE, self.slots1, self.send.at[0], self.recv.at[0])

    def line(self):
        gather_start(LINE, self.slots2, self.send.at[1], self.recv.at[1])

    def middle_sums(self):
        gather_wait(PLANE, self.slots1, self.recv.at[0])
        self.slots2[0] = added(in_order(PLANE, self.slots1))
        self.line()

    def finish_sums(self):
        gather_wait(LINE, self.slots2, self.recv.at[1])
        self.out[...] = added(in_order(LINE, self.slots2))
        self.drain()

    def middle_stats(self, count_ref, plane_count):
        half = self.half
        gather_wait(PLANE, self.slots1, self.recv.at[0])
        parts = in_order(PLANE, self.slots1)
        total = added([p[:half] for p in parts])
        center = total / plane_count
        spread = added([p[half:] for p in parts])
        for spot, part in enumerate(parts):
            count = count_ref[spot : spot + 1, :]
            away = part[:half] / jnp.maximum(count, 1.0) - center
            spread = spread + count * (away * away)
        self.slots2[0, :half] = total
        self.slots2[0, half:] = spread
        self.line()

    def finish_stats(self, plane_count):
        half = self.half
        total_count = plane_count * lax.axis_size(IMG)
        gather_wait(LINE, self.slots2, self.recv.at[1])
        parts = in_order(LINE, self.slots2)
        center = added([p[:half] for p in parts]) / total_count
        spread = added([p[half:] for p in parts])
        for part in parts:
            away = part[:half] / plane_count - center
            spread = spread + plane_count * (away * away)
        self.out[:half] = center
        self.out[half:] = spread / total_count
        self.drain()

    def drain(self):
        gather_wait(PLANE, self.slots1, self.send.at[0])
        gather_wait(LINE, self.slots2, self.send.at[1])

    def rows(self):
        out = self.out[...]
        first = [out[k : k + 1] for k in range(self.half)]
        second = [out[self.half + k : self.half + k + 1] for k in range(self.half)]
        return jnp.concatenate(first, axis=1), jnp.concatenate(second, axis=1)


class Halo:
    scratch = [pltpu.SemaphoreType.DMA((5,)), pltpu.SemaphoreType.DMA((5,))]

    def __init__(self, pad, reach, tile, window, sems, image=None):
        if image is not None:
            tile, window = (ref.at[pl.ds(image, 1)] for ref in (tile, window))
        self.row, self.rows, col, pair, above, below = halo_peers()
        self.pad, self.reach, self.tile, self.window = pad, reach, tile, window
        self.tile_rows, self.tile_cols = tile.shape[1], tile.shape[2]
        self.own = own = pl.ds(pl.multiple_of(HALF * col, HALF), self.tile_cols)
        spot = pl.ds(pl.multiple_of(2 * HALF * col, HALF), HALF)
        side = pl.ds(pl.multiple_of(HALF * (1 - col), HALF), HALF)
        mid = pl.ds(HALF, HALF)
        upper = pl.ds(pad - reach, reach)
        lower = pl.ds(pad + self.tile_rows, reach)
        send, recv = sems

        def copy(src, dst, k, device):
            return pltpu.make_async_remote_copy(
                src_ref=src,
                dst_ref=dst,
                send_sem=send.at[k],
                recv_sem=recv.at[k],
                device_id=device,
                device_id_type=MESH,
            )

        w = window
        self.to_pair = copy(
            tile.at[:, :, side], w.at[:, pl.ds(pad, self.tile_rows), spot], 0, pair
        )
        self.up = copy(tile.at[:, pl.ds(0, reach)], w.at[:, lower, own], 1, above)
        self.down = copy(
            tile.at[:, pl.ds(self.tile_rows - reach, reach)], w.at[:, upper, own], 2, below
        )
        self.from_below = copy(w.at[:, lower, mid], w.at[:, lower, spot], 3, pair)
        self.from_above = copy(w.at[:, upper, mid], w.at[:, upper, spot], 4, pair)

    def blank(self):
        window, pad, reach, tile_rows = self.window, self.pad, self.reach, self.tile_rows
        zero = jnp.zeros((window.shape[0],) + window.shape[2:], window.dtype)

        def fill(first, last):
            for k in range(first, last):
                window[:, k] = zero

        fill(0, pad - reach)
        fill(pad + tile_rows + reach, 2 * pad + tile_rows)

        @pl.when(self.row == 0)
        def _():
            fill(pad - reach, pad)

        @pl.when(self.row == self.rows - 1)
        def _():
            fill(pad + tile_rows, pad + tile_rows + reach)

    def start(self):
        @pl.when(self.row > 0)
        def _():
            self.up.start()

        @pl.when(self.row < self.rows - 1)
        def _():
            self.down.start()

        self.to_pair.start()
        for n in range(self.tile.shape[0]):
            self.window[n, pl.ds(self.pad, self.tile_rows), self.own, :] = self.tile[n]

    def middle(self):
        @pl.when(self.row < self.rows - 1)
        def _():
            self.up.wait_recv()
            self.from_below.start()

        @pl.when(self.row > 0)
        def _():
            self.down.wait_recv()
            self.from_above.start()

    def finish(self):
        self.to_pair.wait()

        @pl.when(self.row < self.rows - 1)
        def _():
            self.down.wait_send()
            self.from_below.wait()

        @pl.when(self.row > 0)
        def _():
            self.up.wait_send()
            self.from_above.wait()


def gauss(x):
    bell = jnp.exp2(x * (x * -0.7213475204444817))
    d = 1.0 + (0.3275911 * 0.7071067811865476) * jnp.abs(x)
    t = pl.reciprocal(d, approx=True)
    t = t * (2.0 - d * t)
    poly = 0.5307027145 * t - 0.7265760135
    poly = poly * t + 0.7107068705
    poly = poly * t - 0.142248368
    poly = poly * t + 0.127414796
    tail = poly * (t * bell)
    return jnp.where(x < 0, tail, 1.0 - tail), bell * 0.3989422804014327


def wide(mask, width):
    return jnp.concatenate([mask] * (width // 128), axis=1)


def place(ref, i, lanes):
    if len(ref.shape) == 4:
        return (i // ref.shape[1], lax.rem(i, ref.shape[1]), slice(None), lanes)
    return (pl.ds(pl.multiple_of(i * STEP, STEP), STEP), lanes)


def by_rows(pixels, width, work, sums=0):
    pieces = [slice(l, l + PIECE) for l in range(0, width, PIECE)]

    def one(i, carry):
        out = []
        for k, lanes in enumerate(pieces):
            got = work(i, lanes)
            for j in range(sums):
                folded = jnp.sum(got[j].reshape(STEP // 8, 8, PIECE), axis=0)
                out.append(carry[k * sums + j] + folded)
        return tuple(out)

    start = tuple(jnp.zeros((8, PIECE), F32) for _ in range(sums * len(pieces)))
    final = lax.fori_loop(0, pixels // STEP, one, start)
    rows = []
    for j in range(sums):
        parts = [jnp.sum(final[k * sums + j], axis=0, keepdims=True) for k in range(len(pieces))]
        rows.append(jnp.concatenate(parts, axis=1))
    return rows


NORM_ROWS = 8


def norm_table(exchange, gain_ref, shift_ref, out_ref, first):
    mean, var = exchange.rows()
    lanes = slice(first, first + mean.shape[1])
    inv = lax.rsqrt(var + EPSILON)
    out_ref[...] = jnp.zeros_like(out_ref)
    out_ref[0:1, :] = mean
    out_ref[1:2, :] = inv
    out_ref[2:3, :] = inv * gain_ref[:, lanes]
    out_ref[3:4, :] = shift_ref[:, lanes]
    out_ref[4:5, :] = var


def normed(u_ref, norm, i, lanes):
    away = u_ref[place(u_ref, i, lanes)].astype(F32) - norm[0:1, lanes]
    return away * norm[2:3, lanes] + norm[3:4, lanes], away


def activate(u_ref, norm, mask, h_ref, residual=None, slope=None, keep=None):
    def work(i, lanes):
        x, _ = normed(u_ref, norm, i, lanes)
        if residual is not None:
            x = x + residual[place(residual, i, lanes)].astype(F32)
        below, bell = gauss(x)
        m = wide(mask[place(mask, i, slice(None))], PIECE)
        h_ref[place(h_ref, i, lanes)] = (x * below * m).astype(BF16)
        if slope is not None:
            slope[place(slope, i, lanes)] = ((below + x * bell) * m).astype(BF16)
        if keep is not None:
            keep[place(keep, i, lanes)] = u_ref[place(u_ref, i, lanes)].astype(BF16)

    by_rows(mask.shape[0], norm.shape[1], work)


def device_stats(u_ref, mask, count):
    pixels, width = u_ref.shape

    def total_of(i, lanes):
        m = wide(mask[place(mask, i, slice(None))], PIECE)
        return (u_ref[place(u_ref, i, lanes)] * m,)

    (total,) = by_rows(pixels, width, total_of, 1)
    center = total / jnp.maximum(wide(count, width), 1.0)

    def spread_of(i, lanes):
        m = wide(mask[place(mask, i, slice(None))], PIECE)
        away = u_ref[place(u_ref, i, lanes)] - center[:, lanes]
        return (away * away * m,)

    (spread,) = by_rows(pixels, width, spread_of, 1)
    return total, spread


def product(a_ref, w_ref, o_ref, turned=False):
    dims = (((1,), (1 if turned else 0,)), ((), ()))

    def one(i, carry):
        rows = pl.ds(pl.multiple_of(i * CHUNK, CHUNK), CHUNK)
        o_ref[rows, :] = lax.dot_general(
            a_ref[rows, :], w_ref[...], dims, preferred_element_type=F32
        )
        return carry

    lax.fori_loop(0, a_ref.shape[0] // CHUNK, one, 0)


def turn(a_ref, t_ref):
    def one(i, carry):
        rows = pl.ds(pl.multiple_of(i * CHUNK, CHUNK), CHUNK)
        t_ref[:, rows] = a_ref[rows, :].T
        return carry

    lax.fori_loop(0, a_ref.shape[0] // CHUNK, one, 0)


def put_lanes(ref, first, value):
    width = ref.shape[-1]
    at, stop = first, first + value.shape[1]
    while at < stop:
        cut = at // width
        until = min(stop, (cut + 1) * width)
        part = value[:, at - first : until - first].astype(ref.dtype)
        lanes = slice(at - cut * width, until - cut * width)
        if len(ref.shape) == 4:
            ref[cut, :, :, lanes] = part.reshape(ref.shape[1:3] + part.shape[1:])
        else:
            ref[cut, :, lanes] = part
        at = until


def weight_product(t_ref, b_ref, gw_ref):
    channels = b_ref.shape[1]
    for first in range(0, channels, 512):
        value = jnp.dot(t_ref[...], b_ref[:, first : first + 512], preferred_element_type=F32)
        if len(gw_ref.shape) == 4 and gw_ref.shape[-1] == channels:
            part = value.astype(gw_ref.dtype).reshape(gw_ref.shape[:3] + (512,))
            gw_ref[:, :, :, first : first + 512] = part
        else:
            put_lanes(gw_ref, first, value)


def put_rows(ref, first, value):
    if len(ref.shape) == 3:
        ref[0, first : first + value.shape[0], :] = value.astype(ref.dtype)
        return
    rows = ref.shape[2]
    at, stop = first, first + value.shape[0]
    while at < stop:
        eighth = at // rows
        until = min(stop, (eighth + 1) * rows)
        low, high = at - eighth * rows, until - eighth * rows
        part = value[at - first : until - first].astype(ref.dtype)
        ref[eighth // 8, eighth % 8, low:high, :] = part
        at = until


def norm_back(e_ref, u_ref, norm, sums, pixel_count, mask, out_ref):
    sum_grad, sum_unit = (s * (1.0 / pixel_count) for s in sums)

    def work(i, lanes):
        away = u_ref[place(u_ref, i, lanes)].astype(F32) - norm[0:1, lanes]
        unit = away * norm[1:2, lanes]
        e = e_ref[place(e_ref, i, lanes)].astype(F32)
        m = wide(mask[place(mask, i, slice(None))], PIECE)
        grad = norm[2:3, lanes] * (e - sum_grad[:, lanes] - unit * sum_unit[:, lanes]) * m
        out_ref[place(out_ref, i, lanes)] = grad.astype(BF16)

    by_rows(mask.shape[0], norm.shape[1], work)


def gelu_grad(e_ref, u_ref, norm, mask):
    def work(i, lanes):
        x, away = normed(u_ref, norm, i, lanes)
        below, bell = gauss(x)
        m = wide(mask[place(mask, i, slice(None))], PIECE)
        e = e_ref[place(e_ref, i, lanes)] * (below + x * bell) * m
        e_ref[place(e_ref, i, lanes)] = e
        return e, e * (away * norm[1:2, lanes])

    return by_rows(mask.shape[0], norm.shape[1], work, 2)


def put_sums(exchange, out_ref):
    first, second = exchange.rows()
    out_ref[...] = jnp.zeros_like(out_ref)
    out_ref[0:1, :] = first
    out_ref[1:2, :] = second
    return first, second


def order_taps(rows, width):
    to = lax.broadcasted_iota(jnp.int32, (rows, width), 0)
    at = lax.broadcasted_iota(jnp.int32, (rows, width), 1)
    picked = jnp.where(to < 16, 2 * to, 2 * (to - 16) + 1)
    real = lax.rem(to, 16) < 9
    return jnp.where(jnp.logical_and(at == picked, real), 1.0, 0.0)


def make_mask(r, tile_cols):
    row, col = lax.axis_index(ROW), lax.axis_index(COL)
    rows, cols = lax.axis_size(ROW), lax.axis_size(COL)
    images = r.orientation.shape[0]
    tile_rows = r.mask.shape[0] // images // tile_cols
    tall = [r.orientation[n].astype(F32) for n in range(images)]
    for n in range(images):

        def fill(i, carry, n=n):
            column = lax.broadcasted_iota(jnp.int32, (tile_cols, 128), 0) + col * tile_cols
            portrait = jnp.where(column < SHORT, 1.0, 0.0)
            line = jnp.zeros((tile_cols, 128), jnp.int32) + (row * tile_rows + i)
            landscape = jnp.where(line < SHORT, 1.0, 0.0)
            at = (n * tile_rows + i) * tile_cols
            r.mask[pl.ds(pl.multiple_of(at, tile_cols), tile_cols), :] = (
                landscape * (1.0 - tall[n]) + portrait * tall[n]
            )
            return carry

        lax.fori_loop(0, tile_rows, fill, 0)

    def count(row, col):
        return (
            jnp.clip(SHORT - row * tile_rows, 0, tile_rows) * tile_cols,
            jnp.clip(SHORT - col * tile_cols, 0, tile_cols) * tile_rows,
        )

    def fill_count(at, row, col):
        flat, upright = (c.astype(F32) for c in count(row, col))
        total = added([flat * (1.0 - t) + upright * t for t in tall])
        r.counts[at : at + 1, :] = jnp.zeros((1, 128), F32) + total

    r.counts[...] = jnp.zeros_like(r.counts)
    for k in range(rows * cols):
        fill_count(k, jnp.int32(k // cols), jnp.int32(k % cols))
    fill_count(8, row, col)


def make_corners(r, cols):
    images, _, pixels = r.up.shape
    tile_cols = cols - HALF
    order = order_taps(32, r.base.shape[1]).astype(BF16)
    tap = lax.broadcasted_iota(jnp.int32, (16, pixels), 0)
    pixel = lax.broadcasted_iota(jnp.int32, (16, pixels), 1)
    up0 = pixel // tile_cols + PAD + 2 * (tap // 3 - 1)
    left0 = lax.rem(pixel, tile_cols) + HALF * lax.axis_index(COL) + 2 * (lax.rem(tap, 3) - 1)
    for n in range(images):
        base = r.base[n * pixels : (n + 1) * pixels, :].astype(F32).astype(BF16)
        moved = lax.dot_general(
            order, base, (((1,), (1,)), ((), ())), preferred_element_type=F32
        ).astype(jnp.int32)
        r.up[n] = moved[:16] + up0
        r.left[n] = moved[16:] + left0


def first(plane_count, r):
    ex, ex2 = Exchange(r.ex1), Exchange(r.ex2)
    images, all_rows, cols, width = r.rim.shape
    halos = [Halo(PAD, REACH, r.tile, r.rim, r.halo[2 * n : 2 * n + 2], n) for n in range(images)]
    make_mask(r, cols - HALF)
    r.ready(r.feature, r.w_reduce)
    product(r.feature, r.w_reduce, r.u_a1)
    r.push(r.u_a1)
    total, spread = device_stats(r.u_a1, r.mask, r.counts[8:9, :])
    wait_all()
    ex.put(total, spread)
    make_corners(r, cols)
    ex.middle_stats(r.counts, plane_count)
    for halo in halos:
        halo.blank()
    order = order_taps(32, r.w_offset.shape[0]).astype(BF16)
    for tap in range(9):
        columns = r.w_offset[:, tap * width : (tap + 1) * width]
        r.w_off[32 * tap : 32 * tap + 32, :] = jnp.dot(
            order, columns, preferred_element_type=F32
        ).astype(BF16)
    ex.finish_stats(plane_count)
    norm_table(ex, r.scale, r.shift, r.norm_a1, 0)
    activate(r.u_a1, r.norm_a1, r.mask, r.tile)
    for halo in halos:
        halo.start()
    select_cells(r, cols)
    r.push(r.select)
    r.ready(r.w_deform)
    turn(r.w_deform, r.w_turned)
    for n, halo in enumerate(halos):
        if n == 0:
            halo.middle()
        halo.finish()
        for k in range(0, all_rows, 8):
            lines = r.rim[n, k : k + 8].reshape(8 * cols, width)
            r.rim_t[n, :, k * cols : (k + 8) * cols] = lines.T
        offset_fractions(r, cols, n)
        sample_units(r, cols, n, 0)
        if n + 1 < images:
            halos[n + 1].middle()
        sample_units(r, cols, n, 1)
    r.push(r.rim, r.fr, r.fc, r.samples, r.u_a2)
    total, spread = device_stats(r.u_a2, r.mask, r.counts[8:9, :])
    ex2.put(total, spread)
    ex2.middle_stats(r.counts, plane_count)
    ex2.finish_stats(plane_count)
    norm_table(ex2, r.scale, r.shift, r.norm_a2, width)


def offset_fractions(r, cols, n):
    _, width, cells = r.rim_t.shape
    column = lax.rem(lax.broadcasted_iota(jnp.int32, (32, cells), 1), cols)
    r.spread[...] = jnp.dot(r.w_off[...], r.rim_t[n], preferred_element_type=F32)
    total = None
    for tap in range(9):
        i, j = 2 * (tap // 3 - 1), 2 * (tap % 3 - 1)
        term = r.spread[32 * tap : 32 * tap + 32, :]
        shift = -(i * cols + j) % cells
        if shift:
            term = pltpu.roll(term, shift, axis=1)
        if j < 0:
            term = jnp.where(column >= -j, term, 0.0)
        if j > 0:
            term = jnp.where(column < cols - j, term, 0.0)
        total = term if total is None else total + term
    parts = []
    for _ in range(3):
        parts.append(total.astype(BF16))
        total = total - parts[-1].astype(F32)
    on_tile = lax.dot_general(
        jnp.concatenate(parts, axis=0),
        r.select[...],
        (((1,), (1,)), ((), ())),
        preferred_element_type=F32,
    )
    offsets = on_tile[:32] + on_tile[32:64] + on_tile[64:]
    fraction = 1.0 / (1.0 + jnp.exp(-offsets))
    r.fr[n] = fraction[:16]
    r.fc[n] = fraction[16:]


def sample_units(r, cols, n, b):
    block = r.table.shape[1]
    width = r.rim_t.shape[1]
    lanes = slice(b * block, (b + 1) * block)
    mine = slice((2 * n + b) * block, (2 * n + b + 1) * block)
    base = b * (BLOCK_ROWS * cols)
    for tap in range(9):
        row_w, _, col_w, _ = tap_weights(tap, b, cols, r.up, r.left, r.fr, r.fc, n, lanes)
        write_table(r.table, 0, row_w, col_w, tap // 3, cols)
        _, start, stop = tap_span(tap // 3, cols)
        cells = r.rim_t[n, :, base + start : base + stop]
        value = jnp.dot(cells, r.table[start:stop, :], preferred_element_type=F32)
        r.samples[tap * width : (tap + 1) * width, mine] = value.astype(BF16)
    deformed = jnp.dot(r.w_turned[...], r.samples[:, mine], preferred_element_type=F32)
    r.u_a2[mine, :] = deformed.T


def finish_kernel(unbias, count, *refs):
    ins, outs, rest = refs[:count], refs[count : count + 17], refs[count + 17 :]
    bufs, out_bufs, sems, out_sems = rest[:count], rest[count : count + 15], rest[-2], rest[-1]
    loads = [pltpu.make_async_copy(ins[k], bufs[k], sems.at[k]) for k in range(count)]
    stores = [pltpu.make_async_copy(out_bufs[k], outs[k], out_sems.at[k]) for k in range(15)]
    stores += [
        pltpu.make_async_copy(bufs[count - 2 + k], outs[15 + k], out_sems.at[15 + k]) for k in range(2)
    ]
    for load in loads:
        load.start()
    conv_b, reduce_b, reduce_a, expand_b, expand_a, deform, off = bufs[:7]
    tables = bufs[7:19]
    for load in loads[:7]:
        load.wait()
    for k, src in enumerate((expand_b, expand_a, deform)):
        rows = src.shape[1]
        for s in range(8):
            out_bufs[3 + k][s * rows : (s + 1) * rows, :] = src[s].astype(F32)
        stores[3 + k].start()
    for k, src in enumerate((conv_b, reduce_b, reduce_a)):
        eighth = src.shape[1]
        for s in range(0, 8, 2):
            rows = jnp.concatenate([src[s], src[s + 1]], axis=0).astype(F32)
            out_bufs[k][:, s * eighth : (s + 2) * eighth] = rows.T
        stores[k].start()
    for k in range(2):
        loads[count - 2 + k].wait()
        stores[15 + k].start()
    rest, total = off[...], None
    order = order_taps(32, 18).astype(BF16)
    for _ in range(3):
        part = rest.astype(BF16)
        rest = rest - part.astype(F32)
        term = lax.dot_general(order, part, (((0,), (0,)), ((), ())), preferred_element_type=F32)
        total = term if total is None else total + term
    out_bufs[6][...] = total
    for load in loads[7 : count - 2]:
        load.wait()
    for k in range(4):
        group, which = tables[3 * k : 3 * k + 3], out_bufs[7 + 2 * k : 9 + 2 * k]
        norms = k >= 2
        for out, row in zip(which, (0, 4) if norms else (1, 0)):
            at = 0
            for table in group:
                for first_lane in range(0, table.shape[1], 128):
                    value = table[row : row + 1, first_lane : first_lane + 128]
                    out[at : at + 1, :] = value * unbias if norms and row == 4 else value
                    at += 1
    for store in stores[6:15]:
        store.start()
    for store in stores:
        store.wait()


def forward(plane_count, r):
    ex_a3, ex_b1, ex_b2 = Exchange(r.ex_a3), Exchange(r.ex_b1), Exchange(r.ex_b2)
    ex_b3, ex_sums = Exchange(r.ex_b3), Exchange(r.ex_sums)
    halo = Halo(2, 2, r.tile, r.rim_b, r.halo)
    halo.blank()
    width = r.h2_a.shape[1]
    count = r.counts[8:9, :]

    def exchange(ex, u_ref):
        ex.put(*device_stats(u_ref, r.mask, count))
        ex.middle_stats(r.counts, plane_count)

    r.ready(r.u_a2)
    activate(r.u_a2, r.norm_a2, r.mask, r.h2_a)
    r.push(r.h2_a)
    r.ready(r.w_expand_a)
    product(r.h2_a, r.w_expand_a, r.wide)
    wait_all()
    exchange(ex_a3, r.wide)
    r.ready(r.feature, r.w_reduce)
    ex_a3.finish_stats(plane_count)
    norm_table(ex_a3, r.scale_a, r.shift_a, r.norm_a3, 2 * width)
    activate(r.wide, r.norm_a3, r.mask, r.middle, r.feature, r.slope_a, r.u_a3)
    r.push(r.middle, r.slope_a, r.u_a3)
    cotangent = pltpu.make_async_copy(r.cotangent, r.feature, r.far_sems.at[0])
    cotangent.start()
    product(r.middle, r.w_reduce, r.u_b1)
    r.push(r.u_b1)
    exchange(ex_b1, r.u_b1)
    ex_b1.finish_stats(plane_count)
    norm_table(ex_b1, r.scale_b, r.shift_b, r.norm_b1, 0)
    activate(r.u_b1, r.norm_b1, r.mask, r.tile)
    halo.start()
    halo.middle()
    halo.finish()
    r.push(r.rim_b)
    build_shifted(r.rim_b, r.shifted)
    r.ready(r.w_conv)
    conv_product(r.shifted, r.w_conv, r.u_b2)
    r.push(r.u_b2)
    exchange(ex_b2, r.u_b2)
    ex_b2.finish_stats(plane_count)
    norm_table(ex_b2, r.scale_b, r.shift_b, r.norm_b2, width)
    activate(r.u_b2, r.norm_b2, r.mask, r.h2_b)
    r.push(r.h2_b)
    r.ready(r.w_expand_b)
    product(r.h2_b, r.w_expand_b, r.wide)
    exchange(ex_b3, r.wide)
    cotangent.wait()
    r.pushed(r.slope_a, r.u_a3)
    e_b3, u_b3, norm = r.slope_a, r.u_a3, r.norm_b3
    ex_b3.finish_stats(plane_count)
    norm_table(ex_b3, r.scale_b, r.shift_b, norm, 2 * width)

    def work(i, lanes):
        x, away = normed(r.wide, norm, i, lanes)
        at = place(r.wide, i, lanes)
        u_b3[at] = r.wide[at].astype(BF16)
        x = x + r.middle[at].astype(F32)
        below, bell = gauss(x)
        m = wide(r.mask[place(r.mask, i, slice(None))], PIECE)
        r.feature_out[at] = (x * below * m).astype(BF16)
        e = (below + x * bell) * r.feature[at].astype(F32) * m
        e_b3[at] = e.astype(BF16)
        return e, e * (away * norm[1:2, lanes])

    sums = by_rows(r.wide.shape[0], r.wide.shape[1], work, 2)
    ex_sums.put(*sums)
    far = [
        pltpu.make_async_copy(e_b3, r.e_b3, r.far_sems.at[1]),
        pltpu.make_async_copy(u_b3, r.u_b3, r.far_sems.at[2]),
    ]
    for copy in far:
        copy.start()
    r.push(r.feature_out)
    ex_sums.middle_sums()
    ex_sums.finish_sums()
    put_sums(ex_sums, r.sums_b3)
    for copy in far:
        copy.wait()


def backward_b(pixel_count, direct, r):
    ex2, ex1 = Exchange(r.ex2), Exchange(r.ex1)
    halo = Halo(2, 2, r.tile, r.back_rim, r.halo)
    halo.blank()
    r.ready(r.e_b3, r.u_b3)
    sums = (r.sums_b3[0:1, :], r.sums_b3[1:2, :])
    norm_back(r.e_b3, r.u_b3, r.norm_b3, sums, pixel_count, r.mask, r.geo)
    r.ready(r.w_expand)
    product(r.geo, r.w_expand, r.grad, turned=True)
    r.ready(r.u_b2)
    sums = gelu_grad(r.grad, r.u_b2, r.norm_b2, r.mask)
    wait_all()
    ex2.put(*sums)
    r.ready(r.h2_b)
    turn(r.h2_b, r.turned)
    ex2.middle_sums()
    weight_product(r.turned, r.geo, r.gw_expand)
    jobs = Jobs()
    if direct:
        jobs.add(*plane_jobs(r.gw_expand, r.eighth_expand_b, r.plane_expand_b))
    else:
        r.push(r.gw_expand)
    jobs.tick(2)
    ex2.finish_sums()
    sums = put_sums(ex2, r.sums_b2)
    norm_back(r.grad, r.u_b2, r.norm_b2, sums, pixel_count, r.mask, r.tile)
    halo.start()
    tile_rows, tile_cols, width = r.tile.shape[1:]
    pixels = tile_rows * tile_cols
    for n in range(r.tile.shape[0]):
        for k in range(0, tile_rows, 8):
            at = n * pixels + k * tile_cols
            block = r.tile[n, k : k + 8].reshape(8 * tile_cols, width)
            r.turned[:, at : at + 8 * tile_cols] = block.T
    r.ready(r.rim_b)
    build_shifted(r.rim_b, r.shifted)
    conv_weight_product(r.turned, r.shifted, r.gw_conv, 0)
    halo.middle()
    jobs.tick(2)
    conv_weight_product(r.turned, r.shifted, r.gw_conv, 1)
    halo.finish()
    build_shifted(r.back_rim, r.back_shifted)
    r.ready(r.w_conv)
    unconv_product(r.back_shifted, r.w_conv, r.grad)
    r.ready(r.u_b1)
    sums = gelu_grad(r.grad, r.u_b1, r.norm_b1, r.mask)
    ex1.put(*sums)
    jobs.tick(2)
    ex1.middle_sums()
    conv_weight_product(r.turned, r.shifted, r.gw_conv, 2)
    r.push(r.gw_conv)
    jobs.finish()
    if direct:
        r.push(r.eighth_expand_b)
    ex1.finish_sums()
    sums = put_sums(ex1, r.sums_b1)
    norm_back(r.grad, r.u_b1, r.norm_b1, sums, pixel_count, r.mask, r.gro_b)


def backward_a(pixel_count, direct, r):
    ex3, ex2 = Exchange(r.ex3), Exchange(r.ex2)
    conv, line = Jobs(), Jobs()
    r.ready(r.gro_b, r.w_reduce)
    product(r.gro_b, r.w_reduce, r.wide, turned=True)
    wait_all()
    if direct:
        r.ready(r.src_conv_b, r.eighth_expand_b)
        conv.add(*plane_jobs(r.src_conv_b, r.eighth_conv_b, r.plane_conv_b))
        line.add(*line_jobs(r.eighth_expand_b, r.sum_expand_b, r.line_expand_b))
    conv.tick(2)
    line.tick(2)
    r.ready(r.e_b3, r.slope_a, r.u_a3)
    norm = r.norm_a3

    def work(i, lanes):
        at = place(r.wide, i, lanes)
        e = (r.wide[at] + r.e_b3[at].astype(F32)) * r.slope_a[at].astype(F32)
        r.e_a3[at] = e.astype(BF16)
        away = r.u_a3[at].astype(F32) - norm[0:1, lanes]
        return e, e * (away * norm[1:2, lanes])

    sums = by_rows(r.wide.shape[0], r.wide.shape[1], work, 2)
    ex3.put(*sums)
    conv.tick(2)
    r.push(r.e_a3)
    turn(r.gro_b, r.turned)
    ex3.middle_sums()
    r.ready(r.middle)
    weight_product(r.turned, r.middle, r.gw_reduce)
    r.push(r.gw_reduce)
    line.tick(2)
    ex3.finish_sums()
    sums = put_sums(ex3, r.sums_a3)
    norm_back(r.e_a3, r.u_a3, norm, sums, pixel_count, r.mask, r.e_b3)
    r.ready(r.w_expand)
    product(r.e_b3, r.w_expand, r.grad, turned=True)
    r.ready(r.u_a2)
    sums = gelu_grad(r.grad, r.u_a2, r.norm_a2, r.mask)
    ex2.put(*sums)
    conv.tick(2)
    line.tick(2)
    r.ready(r.h2_a)
    turn(r.h2_a, r.turned)
    ex2.middle_sums()
    weight_product(r.turned, r.e_b3, r.gw_expand)
    r.push(r.gw_expand)
    ex2.finish_sums()
    sums = put_sums(ex2, r.sums_a2)
    norm_back(r.grad, r.u_a2, r.norm_a2, sums, pixel_count, r.mask, r.gd)
    conv.finish()
    line.finish()
    if direct:
        r.push(r.eighth_conv_b, r.sum_expand_b)


def unsample(r, plan):
    width = r.rim.shape[2]
    cols = r.table.shape[0] // WINDOW
    pixels = r.up.shape[2] // 2
    r.spill[...] = jnp.zeros_like(r.spill)
    r.grad_row[...] = jnp.zeros_like(r.grad_row)
    r.grad_col[...] = jnp.zeros_like(r.grad_col)

    def unit(step, carry):
        n, block = step // 2, lax.rem(step, 2)
        lanes = pl.ds(pl.multiple_of(block * pixels, pixels), pixels)
        base = block * (BLOCK_ROWS * cols)
        grad_in = r.turned[:, pl.ds(pl.multiple_of(step * pixels, pixels), pixels)]
        for group in range(3):
            first, start, stop = tap_span(group, cols)
            cells = pl.ds(pl.multiple_of(base + start, 128), stop - start)
            for j in range(3):
                tap = 3 * group + j
                spot = slice(j * pixels, (j + 1) * pixels)
                row_w, row_s, col_w, col_s = tap_weights(
                    tap, block, cols, r.up, r.left, r.fr, r.fc, n, lanes
                )
                write_table(r.table, j * pixels, row_w, col_w, group, cols)
                grad = jnp.dot(
                    r.w_deform[tap * width : (tap + 1) * width, :],
                    grad_in,
                    preferred_element_type=F32,
                ).astype(BF16)
                r.grads[:, spot] = grad
                scores = jnp.dot(r.rim[n, cells, :], grad, preferred_element_type=F32)
                by_value = jnp.zeros((cols, pixels), F32)
                by_slope = jnp.zeros((cols, pixels), F32)
                for k in range(first, first + SPAN):
                    line = scores[k * cols - start : (k + 1) * cols - start]
                    by_value = by_value + line * row_w[k : k + 1, :]
                    by_slope = by_slope + line * row_s[k : k + 1, :]
                r.grad_row[n, tap : tap + 1, lanes] = jnp.sum(
                    by_slope * col_w, axis=0, keepdims=True
                )
                r.grad_col[n, tap : tap + 1, lanes] = jnp.sum(
                    by_value * col_s, axis=0, keepdims=True
                )
            r.spill[n, cells, :] += lax.dot_general(
                r.table[start:stop, :],
                r.grads[...],
                (((1,), (1,)), ((), ())),
                preferred_element_type=F32,
            )
            for turn_at in range(4):
                if 3 * turn_at + group in plan:

                    @pl.when(step == turn_at)
                    def _(slot=3 * turn_at + group):
                        plan[slot]()

        return carry

    lax.fori_loop(0, 4, unit, 0)


def select_cells(r, cols):
    off = HALF * lax.axis_index(COL)
    cells = r.select.shape[1]

    def fill(i, carry):
        ids = lax.broadcasted_iota(jnp.int32, (STEP, cells), 1)
        pixel = lax.broadcasted_iota(jnp.int32, (STEP, cells), 0)
        hit = ids == pixel + (i + PAD) * cols + off
        r.select[pl.ds(pl.multiple_of(i * STEP, STEP), STEP), :] = jnp.where(hit, 1.0, 0.0).astype(
            BF16
        )
        return carry

    lax.fori_loop(0, r.select.shape[0] // STEP, fill, 0)


def unoffset(r, n):
    images, cells, width = r.rim.shape
    cols = r.table.shape[0] // WINDOW
    column = lax.rem(lax.broadcasted_iota(jnp.int32, (32, cells), 1), cols)
    parts = []
    for grad, frac in ((r.grad_row, r.fr), (r.grad_col, r.fc)):
        f = frac[n]
        parts.append(grad[n] * f * (1.0 - f))
    go = jnp.concatenate(parts, axis=0).astype(BF16)
    on_tile = jnp.dot(go, r.select[...], preferred_element_type=F32)
    for tap in range(9):
        i, j = 2 * (tap // 3 - 1), 2 * (tap % 3 - 1)
        kept = on_tile
        if j < 0:
            kept = jnp.where(column >= -j, on_tile, 0.0)
        if j > 0:
            kept = jnp.where(column < cols - j, on_tile, 0.0)
        shift = (i * cols + j) % cells
        if shift:
            kept = pltpu.roll(kept, shift, axis=1)
        r.on_cells[32 * tap : 32 * tap + 32, :] = kept.astype(BF16)
    grad = jnp.dot(r.on_cells[...], r.rim[n], preferred_element_type=F32)
    if n == 0:
        r.gw_off_sum[...] = grad
    else:
        r.gw_off_sum[...] += grad
    for first in range(0, cells, 512):
        r.spill[n, first : first + 512, :] += lax.dot_general(
            r.on_cells[:, first : first + 512],
            r.w_off[...],
            (((0,), (0,)), ((), ())),
            preferred_element_type=F32,
        )
    if n == images - 1:
        for tap in range(9):
            put_lanes(r.gw_off, tap * width, r.gw_off_sum[32 * tap : 32 * tap + 32, :])


class Spill:
    @staticmethod
    def scratch(images, tile_rows, tile_cols, width):
        side = pltpu.VMEM((images, tile_rows + 2 * PAD, HALF, width), BF16)
        strip = pltpu.VMEM((images, REACH, tile_cols, width), BF16)
        sems = pltpu.SemaphoreType.DMA((3,))
        return [side, side, strip, strip, strip, strip, sems, sems]

    def __init__(self, spill, grad, cols, refs, image):
        self.spill, self.grad, self.cols = spill.at[pl.ds(image, 1)], grad, cols
        self.image = image
        self.side_out, self.side_in, self.up_out, self.down_out, self.up_in, self.down_in = refs[:6]
        send, recv = refs[6:]
        self.row, self.rows, col, pair, above, below = halo_peers()
        self.images, self.all_rows = self.side_out.shape[:2]
        self.tile_rows, self.tile_cols = self.all_rows - 2 * PAD, self.up_out.shape[2]
        self.off, self.away, self.near = HALF * col, 2 * HALF * (1 - col), HALF * (1 - col)
        self.side = remote(self.side_out, self.side_in, send.at[0], recv.at[0], pair)
        self.up = remote(self.up_out, self.down_in, send.at[1], recv.at[1], above)
        self.down = remote(self.down_out, self.up_in, send.at[2], recv.at[2], below)

    def cells(self, k, first, count):
        return pl.ds(pl.multiple_of(k * self.cols + first, HALF), count)

    def start(self):
        def cast(k, carry):
            for n in range(self.images):
                self.side_out[n, k] = self.spill[n, self.cells(k, self.away, HALF), :].astype(BF16)
            return carry

        lax.fori_loop(0, self.all_rows, cast, 0)
        self.side.start()

    def edge(self, buffer, first):
        near = pl.ds(pl.multiple_of(self.near, HALF), HALF)

        def one(k, carry):
            for n in range(self.images):
                at = first + k
                buffer[n, k] = self.spill[n, self.cells(at, self.off, self.tile_cols), :].astype(BF16)
                part = self.spill[n, self.cells(at, HALF, HALF), :]
                buffer[n, k, near, :] = (part + self.side_in[n, at].astype(F32)).astype(BF16)
            return carry

        lax.fori_loop(0, REACH, one, 0)

    def middle(self):
        self.side.wait_recv()

        @pl.when(self.row > 0)
        def _():
            self.edge(self.up_out, PAD - REACH)
            self.up.start()

        @pl.when(self.row < self.rows - 1)
        def _():
            self.edge(self.down_out, PAD + self.tile_rows)
            self.down.start()

    def pixels(self, n, k, first, count):
        at = ((self.image + n) * self.tile_rows + k) * self.tile_cols + first
        return pl.ds(pl.multiple_of(at, HALF), count)

    def own(self):
        def fill(k, carry):
            for n in range(self.images):
                home = self.spill[n, self.cells(PAD + k, self.off, self.tile_cols), :]
                self.grad[self.pixels(n, k, 0, self.tile_cols), :] = home
                self.grad[self.pixels(n, k, self.near, HALF), :] += self.side_in[n, PAD + k].astype(F32)
            return carry

        lax.fori_loop(0, self.tile_rows, fill, 0)

    def finish(self):
        def arrive(buffer, first):
            def one(k, carry):
                for n in range(self.images):
                    at = self.pixels(n, first + k, 0, self.tile_cols)
                    self.grad[at, :] += buffer[n, k].astype(F32)
                return carry

            lax.fori_loop(0, REACH, one, 0)

        @pl.when(self.row > 0)
        def _():
            self.down.wait_recv()
            arrive(self.up_in, 0)
            self.up.wait_send()

        @pl.when(self.row < self.rows - 1)
        def _():
            self.up.wait_recv()
            arrive(self.down_in, self.tile_rows - REACH)
            self.down.wait_send()

        self.side.wait_send()


def backward_s(pixel_count, direct, r):
    ex = Exchange(r.ex1)
    cols = r.table.shape[0] // WINDOW
    spills = [Spill(r.spill, r.grad, cols, r.strips[8 * n : 8 * n + 8], n) for n in range(2)]

    mid, late, end, line = Jobs(), Jobs(), Jobs(), Jobs()
    deform_weight_product(r)
    wait_all()
    if direct:
        reduce, expand, deform = Jobs(), Jobs(), Jobs()
        line.add(*line_jobs(r.eighth_conv_b, r.sum_conv_b, r.line_conv_b))
        reduce.add(*plane_jobs(r.src_reduce_b, r.eighth_reduce_b, r.plane_reduce_b))
        reduce.add(*part_jobs(LineSum, r.eighth_reduce_b, r.own_reduce_b, r.line_reduce_b))
        expand.add(*part_jobs(LinePlane, r.src_expand_a, r.own_expand_a, r.plane_expand_a))
        deform.add(*plane_jobs(r.gw_deform, r.eighth_deform, r.plane_deform))
        deform.add(*part_jobs(LineSum, r.eighth_deform, r.own_deform, r.line_deform))
        deform.tick(2)
        r.ready(r.eighth_conv_b)
        line.tick(2)
        r.ready(r.src_expand_a, r.src_reduce_b)
        q2, q3, q4 = reduce.queue, expand.queue, deform.queue
        slots = {
            1: q4[0:2] + q3[0:2],
            3: q3[2:4] + q2[0:2],
            6: q4[2:4],
            7: q2[2:4],
            9: q4[4:8],
            10: q2[4:6],
        }
        mid.queue = q2[6:10] + q3[4:6]
        late.queue = q3[6:8]
        end.queue = q4[8:10] + q2[10:12] + q3[8:10]
    else:
        slots = {}
        r.push(r.gw_deform)
    slots[5] = [functools.partial(unoffset, r, 0), spills[0].start] + slots.get(5, [])
    slots[8] = [spills[0].middle] + slots.get(8, [])

    def run(queue):
        def call():
            for step in queue:
                step()

        return call

    plan = {slot: run(queue) for slot, queue in slots.items()}
    r.ready(r.w_deform, r.rim, r.w_off, r.select)
    turn(r.gd, r.turned)
    unsample(r, plan)
    unoffset(r, 1)
    spills[1].start()
    r.push(r.gw_off)
    spills[1].middle()
    mid.finish()
    for spill in spills:
        spill.own()
    spills[0].finish()
    late.finish()
    r.ready(r.u_a1)
    spills[1].finish()
    line.tick(2)
    sums = gelu_grad(r.grad, r.u_a1, r.norm_a1, r.mask)
    ex.put(*sums)
    ex.middle_sums()
    ex.finish_sums()
    sums = put_sums(ex, r.sums_a1)
    line.tick(2)
    norm_back(r.grad, r.u_a1, r.norm_a1, sums, pixel_count, r.mask, r.gr_a)
    end.finish()
    line.finish()
    if direct:
        r.push(r.sum_conv_b, r.own_reduce_b, r.own_expand_a, r.own_deform)


def deform_weight_product(r):
    width = r.gd.shape[1]
    slots = r.sample_slots.shape[0]

    def load(tap):
        rows, slot = pl.ds(tap * width, width), tap % slots
        return pltpu.make_async_copy(
            r.samples.at[rows], r.sample_slots.at[slot], r.sample_sems.at[slot]
        )

    for tap in range(slots):
        load(tap).start()
    r.ready(r.gd)
    for tap in range(9):
        load(tap).wait()
        value = jnp.dot(r.sample_slots[tap % slots], r.gd[...], preferred_element_type=F32)
        put_rows(r.gw_deform, tap * width, value)
        if tap + slots < 9:
            load(tap + slots).start()


def last(direct, r):
    jobs, more, plane = Jobs(), Jobs(), Jobs()
    r.ready(r.gr_a, r.feature)
    wait_all()
    if direct:
        r.ready(r.own_deform, r.gw_off)
        jobs.add(
            *part_jobs(Gather, r.own_deform, r.sum_deform, r.gather_deform),
            SmallSum(r.gw_off, r.sum_off, r.small),
        )
        more.add(
            *part_jobs(Gather, r.own_reduce_b, r.sum_reduce_b, r.gather_reduce_b),
            *part_jobs(Gather, r.own_expand_a, r.sum_expand_a, r.gather_expand_a),
        )
    jobs.tick(3)
    turn(r.gr_a, r.turned)
    weight_product(r.turned, r.feature, r.gw_reduce)
    if direct:
        plane.add(*plane_jobs(r.gw_reduce, r.eighth_reduce_a, r.plane_reduce_a))
        plane.add(*line_jobs(r.eighth_reduce_a, r.sum_reduce_a, r.line_reduce_a))
    else:
        r.push(r.gw_reduce)
    plane.tick(2)
    if direct:
        r.ready(r.own_reduce_b, r.own_expand_a)
    r.ready(r.w_reduce, r.e_a3)

    def chunk(i, carry):
        rows = pl.ds(pl.multiple_of(i * CHUNK, CHUNK), CHUNK)
        for first in range(0, r.feature.shape[1], 512):
            lanes = slice(first, first + 512)
            grad = lax.dot_general(
                r.gr_a[rows, :],
                r.w_reduce[lanes, :],
                (((1,), (1,)), ((), ())),
                preferred_element_type=F32,
            )
            r.grad_in[rows, lanes] = (grad + r.e_a3[rows, lanes].astype(F32)).astype(BF16)
        return carry

    half = r.feature.shape[0] // CHUNK // 2
    lax.fori_loop(0, half, chunk, 0)
    plane.tick(2)
    lax.fori_loop(half, 2 * half, chunk, 0)
    r.push(r.grad_in)
    jobs.tick(3)
    plane.tick(2)
    more.tick(4)
    plane.tick(4)
    jobs.finish()
    more.tick(4)
    plane.tick(2)
    more.finish()
    if direct:
        r.push(r.sum_reduce_b, r.sum_expand_a, r.sum_deform)
    plane.finish()
    if direct:
        r.push(r.sum_reduce_a)


def body(
    feature_in,
    orientation,
    offset_base,
    w_reduce_a,
    w_offset_a,
    w_deform_a,
    w_expand_a,
    scale_a,
    shift_a,
    w_reduce_b,
    w_conv_b,
    w_expand_b,
    scale_b,
    shift_b,
    cotangent,
):
    images, tile_rows, tile_cols, channels = feature_in.shape
    inner_width = w_reduce_a.shape[1]
    tile_pixels = tile_rows * tile_cols
    pixels = images * tile_pixels
    win_cols = tile_cols + HALF
    win_rows = tile_rows + 2 * PAD
    cells = win_rows * win_cols
    plane_count = 1.0 * images * LONG * SHORT
    pixel_count = plane_count * lax.axis_size(IMG)
    unbias = pixel_count / (pixel_count - 1.0)

    def array(*shape, dtype=BF16):
        return jax.ShapeDtypeStruct(shape, dtype)

    def table(width):
        return array(NORM_ROWS, width, dtype=F32)

    small = (pixels, inner_width)
    big = (pixels, channels)
    window_b = (images, tile_rows + 4, win_cols, inner_width)
    shifted = pltpu.VMEM((images, tile_rows + 4, tile_cols, 3 * inner_width), BF16)
    tile = pltpu.VMEM((images, tile_rows, tile_cols, inner_width), BF16)
    turned = pltpu.VMEM((inner_width, pixels), BF16)
    images_axis = lax.axis_size(IMG)
    direct = inner_width % (images_axis * 8 * 16) == 0
    cuts = images_axis if direct else 1
    feature = feature_in.reshape(big)
    scale_a, shift_a, scale_b, shift_b = (v[None] for v in (scale_a, shift_a, scale_b, shift_b))
    taps_shape = (images, 16, tile_pixels)
    start = fused(
        functools.partial(first, plane_count),
        FIRST_CID,
        ins=dict(
            base=offset_base.reshape(pixels, 18),
            w_offset=jnp.pad(w_offset_a.T, ((0, 14), (0, 0))),
            scale=scale_a,
            shift=shift_a,
        ),
        smem=dict(orientation=orientation),
        staged=dict(feature=feature, w_reduce=w_reduce_a, w_deform=w_deform_a),
        outs=dict(
            mask=array(pixels, 128, dtype=F32),
            counts=array(16, 128, dtype=F32),
            up=array(*taps_shape, dtype=jnp.int32),
            left=array(*taps_shape, dtype=jnp.int32),
            w_off=array(288, inner_width),
            norm_a1=table(inner_width),
            norm_a2=table(inner_width),
        ),
        pushed=dict(
            u_a1=array(*small, dtype=F32),
            rim=array(images, win_rows, win_cols, inner_width),
            select=array(tile_pixels, cells),
            fr=array(*taps_shape, dtype=F32),
            fc=array(*taps_shape, dtype=F32),
            samples=array(9 * inner_width, pixels),
            u_a2=array(*small, dtype=F32),
        ),
        scratch=dict(
            ex1=Exchange.scratch(inner_width),
            ex2=Exchange.scratch(inner_width),
            halo=Halo.scratch * images,
            tile=tile,
            w_turned=pltpu.VMEM((inner_width, 9 * inner_width), BF16),
            rim_t=pltpu.VMEM((images, inner_width, cells), BF16),
            spread=pltpu.VMEM((288, cells), F32),
            table=pltpu.VMEM((WINDOW * win_cols, tile_pixels // 2), BF16),
        ),
    )
    mask, count_rows, norm_a1 = start.mask, start.counts, start.norm_a1
    rim_flat = start.rim.reshape(images, cells, inner_width)
    norm_a2, deformed = start.norm_a2, start.u_a2
    fwd = fused(
        functools.partial(forward, plane_count),
        FORWARD_CID,
        ins=dict(
            norm_a2=norm_a2,
            mask=mask,
            counts=count_rows,
            scale_a=scale_a,
            shift_a=shift_a,
            scale_b=scale_b,
            shift_b=shift_b,
        ),
        far=dict(cotangent=cotangent.reshape(big)),
        staged=dict(
            u_a2=deformed,
            w_expand_a=w_expand_a,
            feature=feature,
            w_reduce=w_reduce_b,
            w_conv=w_conv_b,
            w_expand_b=w_expand_b,
        ),
        outs=dict(
            norm_a3=table(channels),
            norm_b1=table(inner_width),
            norm_b2=table(inner_width),
            norm_b3=table(channels),
            sums_b3=table(channels),
        ),
        pushed=dict(
            h2_a=array(*small),
            middle=array(*big),
            slope_a=array(*big),
            u_a3=array(*big),
            u_b1=array(*small, dtype=F32),
            rim_b=array(*window_b),
            u_b2=array(*small, dtype=F32),
            h2_b=array(*small),
            feature_out=array(*big),
        ),
        far_outs=dict(e_b3=array(*big), u_b3=array(*big)),
        scratch=dict(
            ex_a3=Exchange.scratch(channels),
            ex_b1=Exchange.scratch(inner_width),
            ex_b2=Exchange.scratch(inner_width),
            ex_b3=Exchange.scratch(channels),
            ex_sums=Exchange.scratch(channels),
            halo=Halo.scratch,
            wide=pltpu.VMEM(big, F32),
            tile=tile,
            shifted=shifted,
            far_sems=pltpu.SemaphoreType.DMA((3,)),
        ),
    )
    def eighths(grad):
        return grad.reshape(images_axis, 8, -1, grad.shape[-1])

    def eighth_of(src):
        return array(images_axis, *src.shape[2:])

    def own_of(src):
        return array(*src.shape[2:])

    def sum_of(src):
        return array(*src.shape[1:])

    def vmem(struct):
        return pltpu.VMEM(struct.shape, struct.dtype)

    natural = array(1, inner_width, channels)
    pushed_b, scratch_b = dict(gw_expand=natural), {}
    if direct:
        expand_b = array(images_axis, 8, inner_width // images_axis // 8, channels)
        pushed_b = dict(eighth_expand_b=eighth_of(expand_b))
        scratch_b = dict(gw_expand=vmem(expand_b), plane_expand_b=Plane.scratch(expand_b.shape))
    bwd_b = fused(
        functools.partial(backward_b, pixel_count, direct),
        BACKWARD_B_CID,
        ins=dict(
            mask=mask,
            norm_b3=fwd.norm_b3,
            sums_b3=fwd.sums_b3,
            norm_b2=fwd.norm_b2,
            norm_b1=fwd.norm_b1,
        ),
        staged=dict(
            e_b3=fwd.e_b3,
            u_b3=fwd.u_b3,
            w_expand=w_expand_b,
            u_b2=fwd.u_b2,
            h2_b=fwd.h2_b,
            rim_b=fwd.rim_b,
            w_conv=w_conv_b,
            u_b1=fwd.u_b1,
        ),
        outs=dict(gro_b=array(*small), sums_b2=table(inner_width), sums_b1=table(inner_width)),
        pushed=dict(
            **pushed_b,
            gw_conv=array(cuts, inner_width, 9 * inner_width // cuts),
        ),
        scratch=dict(
            **scratch_b,
            ex2=Exchange.scratch(inner_width),
            ex1=Exchange.scratch(inner_width),
            halo=Halo.scratch,
            geo=pltpu.VMEM(big, BF16),
            grad=pltpu.VMEM(small, F32),
            tile=tile,
            turned=turned,
            back_rim=pltpu.VMEM(window_b, BF16),
            shifted=shifted,
            back_shifted=shifted,
        ),
    )

    staged_a, pushed_a, scratch_a = {}, {}, {}
    if direct:
        conv_b = eighths(bwd_b.gw_conv)
        staged_a = dict(src_conv_b=conv_b, eighth_expand_b=bwd_b.eighth_expand_b)
        pushed_a = dict(eighth_conv_b=eighth_of(conv_b), sum_expand_b=sum_of(expand_b))
        scratch_a = dict(
            plane_conv_b=Plane.scratch(conv_b.shape),
            line_expand_b=Line.scratch(bwd_b.eighth_expand_b.shape),
        )
    bwd_a = fused(
        functools.partial(backward_a, pixel_count, direct),
        BACKWARD_A_CID,
        ins=dict(mask=mask, norm_a3=fwd.norm_a3, norm_a2=norm_a2),
        staged=dict(
            gro_b=bwd_b.gro_b,
            w_reduce=w_reduce_b,
            **staged_a,
            e_b3=fwd.e_b3,
            slope_a=fwd.slope_a,
            u_a3=fwd.u_a3,
            middle=fwd.middle,
            w_expand=w_expand_a,
            u_a2=deformed,
            h2_a=fwd.h2_a,
        ),
        outs=dict(gd=array(*small), sums_a3=table(channels), sums_a2=table(inner_width)),
        pushed=dict(
            **pushed_a,
            gw_reduce=array(cuts, inner_width, channels // cuts),
            gw_expand=natural,
            e_a3=array(*big),
        ),
        scratch=dict(
            **scratch_a,
            ex3=Exchange.scratch(channels),
            ex2=Exchange.scratch(inner_width),
            wide=pltpu.VMEM(big, F32),
            grad=pltpu.VMEM(small, F32),
            turned=turned,
        ),
    )
    staged_s, scratch_s = {}, {}
    pushed_s = dict(gw_deform=array(1, 9 * inner_width, inner_width))
    if direct:
        reduce_b, expand_a = eighths(bwd_a.gw_reduce), eighths(bwd_a.gw_expand)
        deform = array(images_axis, 8, 9 * inner_width // images_axis // 8, inner_width)
        staged_s = dict(
            src_reduce_b=reduce_b,
            src_expand_a=expand_a,
            eighth_conv_b=bwd_a.eighth_conv_b,
        )
        pushed_s = dict(
            sum_conv_b=sum_of(conv_b),
            own_reduce_b=own_of(reduce_b),
            own_expand_a=own_of(expand_a),
            own_deform=own_of(deform),
        )
        scratch_s = dict(
            gw_deform=vmem(deform),
            line_conv_b=Line.scratch(bwd_a.eighth_conv_b.shape),
            plane_reduce_b=Plane.scratch(reduce_b.shape),
            plane_expand_a=LinePlane.scratch(expand_a.shape),
            plane_deform=Plane.scratch(deform.shape),
            eighth_reduce_b=vmem(eighth_of(reduce_b)),
            eighth_deform=vmem(eighth_of(deform)),
            line_reduce_b=LineSum.scratch(eighth_of(reduce_b).shape),
            line_deform=LineSum.scratch(eighth_of(deform).shape),
        )
    block = tile_pixels // 2
    bwd_s = fused(
        functools.partial(backward_s, pixel_count, direct),
        BACKWARD_S_CID,
        ins=dict(
            mask=mask,
            norm_a1=norm_a1,
            up=start.up,
            left=start.left,
            fr=start.fr,
            fc=start.fc,
        ),
        far=dict(samples=start.samples),
        staged=dict(
            gd=bwd_a.gd,
            **staged_s,
            w_deform=w_deform_a,
            rim=rim_flat,
            w_off=start.w_off,
            select=start.select,
            u_a1=start.u_a1,
        ),
        outs=dict(gr_a=array(*small), sums_a1=table(inner_width)),
        pushed=dict(**pushed_s, gw_off=array(cuts, 32, 9 * inner_width // cuts)),
        scratch=dict(
            **scratch_s,
            ex1=Exchange.scratch(inner_width),
            strips=Spill.scratch(1, tile_rows, tile_cols, inner_width) * images,
            spill=pltpu.VMEM((images, cells, inner_width), F32),
            table=pltpu.VMEM((WINDOW * win_cols, 3 * block), BF16),
            grads=pltpu.VMEM((inner_width, 3 * block), BF16),
            turned=turned,
            grad_row=pltpu.VMEM(taps_shape, F32),
            grad_col=pltpu.VMEM(taps_shape, F32),
            on_cells=pltpu.VMEM((288, cells), BF16),
            gw_off_sum=pltpu.VMEM((288, inner_width), F32),
            sample_slots=pltpu.VMEM((3, inner_width, pixels), BF16),
            sample_sems=pltpu.SemaphoreType.DMA((3,)),
            grad=pltpu.VMEM(small, F32),
        ),
    )
    staged_l, pushed_l, scratch_l = {}, {}, {}
    if direct:
        reduce_a = array(images_axis, 8, inner_width // 8, channels // cuts)
        staged_l = dict(
            own_deform=bwd_s.own_deform,
            gw_off=bwd_s.gw_off,
            own_reduce_b=bwd_s.own_reduce_b,
            own_expand_a=bwd_s.own_expand_a,
        )
        pushed_l = dict(
            sum_reduce_b=sum_of(reduce_b),
            sum_expand_a=sum_of(expand_a),
            sum_deform=sum_of(deform),
            sum_reduce_a=sum_of(reduce_a),
        )
        scratch_l = dict(
            gw_reduce=vmem(reduce_a),
            small=SmallSum.scratch(bwd_s.gw_off.shape),
            gather_reduce_b=Gather.scratch(reduce_b.shape),
            gather_expand_a=Gather.scratch(expand_a.shape),
            gather_deform=Gather.scratch(deform.shape),
            plane_reduce_a=Plane.scratch(reduce_a.shape),
            eighth_reduce_a=vmem(eighth_of(reduce_a)),
            line_reduce_a=Line.scratch(eighth_of(reduce_a).shape),
        )
        outs_l = dict(sum_off=array(*bwd_s.gw_off.shape[1:], dtype=F32))
    else:
        pushed_l = dict(gw_reduce=array(cuts, inner_width, channels // cuts))
        outs_l = {}
    end = fused(
        functools.partial(last, direct),
        LAST_CID,
        ins={},
        staged=dict(
            gr_a=bwd_s.gr_a, feature=feature, **staged_l, w_reduce=w_reduce_a, e_a3=bwd_a.e_a3
        ),
        outs=outs_l,
        pushed=dict(**pushed_l, grad_in=array(*big)),
        scratch=dict(**scratch_l, turned=turned),
    )
    sums_a = [bwd_s.sums_a1, bwd_a.sums_a2, bwd_a.sums_a3]
    sums_b = [bwd_b.sums_b1, bwd_b.sums_b2, fwd.sums_b3]
    norms_a = [norm_a1, norm_a2, fwd.norm_a3]
    norms_b = [fwd.norm_b1, fwd.norm_b2, fwd.norm_b3]
    if direct:
        sums = [
            bwd_s.sum_conv_b,
            end.sum_reduce_b,
            end.sum_reduce_a,
            bwd_a.sum_expand_b,
            end.sum_expand_a,
            end.sum_deform,
            end.sum_off,
        ]
    else:

        def over_devices(grad, dim):
            part = lax.psum_scatter(grad, IMG, scatter_dimension=dim, tiled=True)
            return lax.psum(part, (ROW, COL))

        turned_grads = (bwd_b.gw_conv, bwd_a.gw_reduce, end.gw_reduce)
        sums = [over_devices(g[0], 1) for g in turned_grads]
        sums += [over_devices(g[0], 0) for g in (bwd_b.gw_expand, bwd_a.gw_expand)]
        sums.append(over_devices(bwd_s.gw_deform[0], 0))
        sums = [g.reshape(8, -1, g.shape[1]) for g in sums]
        sums.append(over_devices(bwd_s.gw_off[0], 1).astype(F32))
    share = inner_width // images_axis
    long_share, wide_share = 9 * share, channels // images_axis
    shapes = [
        (long_share, inner_width),
        (wide_share, inner_width),
        (wide_share, inner_width),
        (share, channels),
        (share, channels),
        (long_share, inner_width),
        (18, long_share),
    ]
    vectors = ((2 * inner_width + channels) // 128, 128)
    shapes += [vectors] * 8
    operands = sums + sums_a + sums_b + norms_a + norms_b + [fwd.feature_out, end.grad_in]
    results = [array(*shape, dtype=F32) for shape in shapes]
    anywhere = pl.BlockSpec(memory_space=pl.ANY)
    results = pl.pallas_call(
        functools.partial(finish_kernel, unbias, len(operands)),
        out_shape=results + [array(*big)] * 2,
        in_specs=[anywhere] * len(operands),
        out_specs=[anywhere] * (len(shapes) + 2),
        scratch_shapes=[vmem(v) for v in operands + results]
        + [pltpu.SemaphoreType.DMA((len(operands),)), pltpu.SemaphoreType.DMA((17,))],
        compiler_params=pltpu.CompilerParams(vmem_limit_bytes=VMEM_LIMIT),
    )(*operands)
    conv_b, reduce_b, reduce_a, expand_b, expand_a, deform_a, offset_a = results[:7]
    scale_sums_a, shift_sums_a, scale_sums_b, shift_sums_b, mean_a, var_a, mean_b, var_b = (
        v.reshape(-1) for v in results[7:15]
    )
    return (
        results[15].reshape(feature_in.shape),
        results[16].reshape(feature_in.shape),
        reduce_a,
        offset_a.T,
        deform_a,
        expand_a,
        scale_sums_a,
        shift_sums_a,
        mean_a,
        var_a,
        reduce_b,
        conv_b,
        expand_b,
        scale_sums_b,
        shift_sums_b,
        mean_b,
        var_b,
    )


def solution(mesh):
    tiles = P(IMG, ROW, COL, None)
    in_specs = (tiles, P(IMG), tiles) + (P(),) * 11 + (tiles,)
    shares = P(IMG, None)
    out_specs = (tiles, tiles) + (shares,) * 4 + (P(),) * 4 + (shares,) * 3 + (P(),) * 4
    return jax.shard_map(body, mesh=mesh, in_specs=in_specs, out_specs=out_specs, check_vma=False)
```
